32 devices in a mesh: section: 2 (over core), dp: 4 (over y, x), expert: 4 (over z).
Axes of the slice: x: 2, y: 2, z: 4, core: 2. Of those that a mesh axis runs over, the one named last changes fastest.
Arguments:
- tokens: bfloat16 [3072, 1536], P(('dp', 'expert')), may hold values from -6 to 6
- cotangent: bfloat16 [3072, 1536], P(('dp', 'expert')), may hold values from -6 to 6
- segments: int32 [32, 96], P(('dp', 'expert')), may hold values from 0 to 3, never falling along the last dimension, each value on 1 to 48 neighbouring positions
- routes: int32 [2, 3072, 8], P('section', ('dp', 'expert')), may hold values from 0 to 15, as said below
- gain_attn: bfloat16 [2, 1536], P('section'), may hold values from 0.5 to 1.5
- w_query: bfloat16 [2, 1536, 1536], P('section'), may hold values from -0.15625 to 0.15625
- w_key: bfloat16 [2, 1536, 512], P('section'), may hold values from -0.15625 to 0.15625
- w_value: bfloat16 [2, 1536, 512], P('section'), may hold values from -0.15625 to 0.15625
- w_out: bfloat16 [2, 1536, 1536], P('section'), may hold values from -0.4375 to 0.4375
- gain_moe: bfloat16 [2, 1536], P('section'), may hold values from 0.5 to 1.5
- w_router: bfloat16 [2, 1536, 16], P('section'), may hold values from -0.078125 to 0.078125
- w_gate: bfloat16 [2, 16, 1536, 512], P('section', 'expert'), may hold values from -0.15625 to 0.15625
- w_up: bfloat16 [2, 16, 1536, 512], P('section', 'expert'), may hold values from -0.15625 to 0.15625
- w_down: bfloat16 [2, 16, 512, 1536], P('section', 'expert'), may hold values from -1 to 1
Outputs:
- layer_out: bfloat16 [2, 3072, 1536], P('section', ('dp', 'expert'))
- input_grad: float32 [2, 3072, 1536], P('section', ('dp', 'expert'))
- grad_gain_attn: float32 [2, 1536], P('section', ('dp', 'expert'))
- grad_w_query: float32 [2, 1536, 1536], P('section', ('dp', 'expert'))
- grad_w_key: float32 [2, 1536, 512], P('section', ('dp', 'expert'))
- grad_w_value: float32 [2, 1536, 512], P('section', ('dp', 'expert'))
- grad_w_out: float32 [2, 1536, 1536], P('section', ('dp', 'expert'))
- grad_gain_moe: float32 [2, 1536], P('section', ('dp', 'expert'))
- grad_w_router: float32 [2, 1536, 16], P('section', ('dp', 'expert'))
- grad_w_gate: float32 [2, 16, 1536, 512], P('section', 'expert', 'dp')
- grad_w_up: float32 [2, 16, 1536, 512], P('section', 'expert', 'dp')
- grad_w_down: float32 [2, 16, 512, 1536], P('section', 'expert', 'dp')
- balance_loss: float32 [2, 16], P('section')
The draws below stay inside these ranges and needn't reach their ends.
Inputs may be any that keep to these rules, and one draw needn't show every extreme that they name: `routes`: each row names 8 different experts. In each aligned block of 96 rows (the rows of one micro-batch of one device in one layer) every expert is named, none by more than 64 rows, and some by exactly 64 rows. `segments`: ids never fall along a sequence; each document has 1 to 48 positions, and some has exactly 48.
All inputs are finite; a program needn't handle non-finite values.
Results may differ from the reference program's by a relative error of at most 0.025.
Values may be sent and summed in bfloat16 or wider, within the bound.
A program may use at most 256 MiB of HBM per device.

```python
import math
import jax
import jax.numpy as jnp
import numpy as np
from jax import lax

D = 1536
H = 24
KVH = 8
HD = 64
FF = 512
TOPK = 8
MB = 2
SEQ = 96
EXPERTS = 16
TOKENS = 3072
SEQS = 32


def draw_routes(key, part):
    key = jax.random.fold_in(key, 11)
    perm_key, shift_key = jax.random.split(key)
    block_count = TOKENS // SEQ
    device_count = block_count // MB
    block_keys = jax.random.split(perm_key, 2 * block_count)
    orders = jax.vmap(lambda one_key: jax.random.permutation(one_key, SEQ))(block_keys)
    offsets = (orders % 12).reshape(2, block_count, SEQ).astype(jnp.int32)
    device_place = jnp.arange(block_count, dtype=jnp.int32) // MB * EXPERTS // device_count
    jitter = jax.random.randint(shift_key, (2, block_count), 0, 2).astype(jnp.int32)
    layer_shift = 3 * jnp.arange(2, dtype=jnp.int32)[:, None]
    shift = (device_place[None, :] + jitter + layer_shift) % EXPERTS
    chosen = (shift[:, :, None, None] + offsets[:, :, :, None] + jnp.arange(TOPK, dtype=jnp.int32)[None, None, None, :]) % EXPERTS
    return chosen.reshape(2, TOKENS, TOPK).astype(jnp.int32)


def block_scale(key, extent, shards, low, high):
    gain, own = 1.0, jax.random.fold_in(key, 6)
    for dim, blocks in shards:
        heights = jnp.exp(jax.random.uniform(jax.random.fold_in(own, dim), (blocks,), jnp.float32, low / len(shards), high / len(shards)))
        gain = gain * jnp.repeat(heights, extent[dim] // blocks).reshape([-1 if axis == dim else 1 for axis in range(len(extent))])
    return gain


def length_profile(amount, total, bound, lean):
    portions = [(1 << 20) // math.isqrt(grade ** lean) + 1 for grade in range(2, amount + 1)]
    surplus, given = total - bound - (amount - 1), [1] * (amount - 1)
    while surplus > 0:
        movable = [i for i in range(amount - 1) if given[i] < bound]
        whole, left = sum([portions[i] for i in movable]), surplus
        for i in movable:
            extra = min(bound - given[i], max(1, left * portions[i] // whole), surplus)
            given[i] = given[i] + extra
            surplus = surplus - extra
    return np.array([bound] + given)


def ragged_sizes(stream_key, count, total, bound, slope):
    if count == 2:
        one = jax.random.randint(stream_key, (), max(1, total - bound), min(bound, total - 1) + 1)
        return jnp.stack([one, total - one])
    sizes = jnp.asarray(length_profile(count, total, bound, slope), jnp.int32)
    twos = (count - 1) // 2
    giver, taker = sizes[1:1 + 2 * twos:2], sizes[2:2 + 2 * twos:2]
    margin = jnp.minimum(giver - 1, bound - taker)
    moved = jax.random.randint(jax.random.fold_in(stream_key, 1), (twos,), 0, 1 << 20) % (margin + 1)
    sizes = sizes.at[1:1 + 2 * twos:2].set(giver - moved).at[2:2 + 2 * twos:2].set(taker + moved)
    return sizes[jax.random.permutation(jax.random.fold_in(stream_key, 2), count)]


def bell_draw(key, extent, scale, reach, cuts=(), kind=jnp.bfloat16):
    drawn = scale * jax.random.normal(key, extent, jnp.float32)
    if cuts:
        drawn = drawn * block_scale(key, extent, cuts, -0.22, 0.18)
    return jnp.clip(drawn, -reach, reach).astype(kind)


def setup_inputs(seed: int = 0) -> dict:
    key_of = jax.random.split(jax.random.key(seed), 15)
    return {
        "tokens": bell_draw(key_of[0], (TOKENS, D), 1.0, 6.0, ((0, 16),)),
        "cotangent": bell_draw(key_of[1], (TOKENS, D), 1.0, 6.0, ((0, 16),)),
        "segments": jax.vmap(lambda own: jnp.searchsorted(jnp.cumsum(ragged_sizes(own, 4, SEQ, SEQ // 2, 0)), jnp.arange(SEQ), side="right"))(jax.random.split(key_of[2], SEQS)).reshape((SEQS, SEQ)).astype(jnp.int32),
        "routes": draw_routes(jax.random.fold_in(key_of[14], 71), 0),
        "gain_attn": jnp.clip(1.0 + 0.1 * jax.random.normal(key_of[4], (2, D), jnp.float32), 0.5, 1.5).astype(jnp.bfloat16),
        "w_query": bell_draw(key_of[5], (2, D, H * HD), D ** -0.5, 0.15625, ((0, 2),)),
        "w_key": bell_draw(key_of[6], (2, D, KVH * HD), D ** -0.5, 0.15625, ((0, 2),)),
        "w_value": bell_draw(key_of[7], (2, D, KVH * HD), D ** -0.5, 0.15625, ((0, 2),)),
        "w_out": bell_draw(key_of[8], (2, H * HD, D), (D // 9) ** -0.5, 0.4375, ((0, 2),)),
        "gain_moe": jnp.clip(1.0 + 0.1 * jax.random.normal(key_of[9], (2, D), jnp.float32), 0.5, 1.5).astype(jnp.bfloat16),
        "w_router": bell_draw(key_of[10], (2, D, EXPERTS), (4 * D) ** -0.5, 0.078125, ((0, 2),)),
        "w_gate": bell_draw(key_of[11], (2, EXPERTS, D, FF), D ** -0.5, 0.15625, ((0, 2), (1, 4))),
        "w_up": bell_draw(key_of[12], (2, EXPERTS, D, FF), D ** -0.5, 0.15625, ((0, 2), (1, 4))),
        "w_down": bell_draw(key_of[13], (2, EXPERTS, FF, D), (FF // 16) ** -0.5, 1.0, ((0, 2), (1, 4))),
    }


EPSILON = 1e-05
THETA = 10000.0
MASKED = -1e+30
PRECISE = lax.Precision.HIGHEST

@jax.custom_vjp
def low(v):
    return lax.optimization_barrier(v.astype(jnp.bfloat16)).astype(jnp.float32)

@jax.custom_vjp
def low_back(v):
    return v

def low_keep(v):
    return (low(v), None)

def low_pass(kept, grad):
    return (grad,)

def back_keep(v):
    return (v, None)

def back_low(kept, grad):
    return (low(grad),)
low.defvjp(low_keep, low_pass)
low_back.defvjp(back_keep, back_low)

def matmul(left_side, right_side):
    return jnp.dot(left_side, right_side, precision=PRECISE, preferred_element_type=jnp.float32)

def rms_scale(tensor, gain_vector):
    return tensor * lax.rsqrt(lax.optimization_barrier(jnp.mean(tensor * tensor, axis=-1, keepdims=True)) + EPSILON) * gain_vector

def rotary(tensor):
    length = tensor.shape[-3]
    half_width = tensor.shape[-1] // 2
    position = jnp.arange(length, dtype=jnp.float32)[:, None]
    freq_rate = THETA ** (-jnp.arange(half_width, dtype=jnp.float32) / half_width)
    angles = position * freq_rate[None, :]
    cosine_table = jnp.cos(angles)[:, None, :]
    sine_table = jnp.sin(angles)[:, None, :]
    first_half = tensor[..., :half_width]
    second_half = tensor[..., half_width:]
    return jnp.concatenate([first_half * cosine_table - second_half * sine_table, second_half * cosine_table + first_half * sine_table], axis=-1)

def attend(pieces):
    queries, key_rows, values, segment_row = pieces
    length = queries.shape[0]
    grouped = queries.reshape(length, KVH, H // KVH, HD)
    scores = jnp.einsum('qkgd,skd->kgqs', grouped, key_rows, precision=PRECISE) * HD ** (-0.5)
    scores = low_back(scores)
    position = jnp.arange(length)
    allowed = (position[None, :] <= position[:, None]) & (segment_row[:, None] == segment_row[None, :])
    scores = jnp.where(allowed[None, None], scores, MASKED)
    weight = jax.nn.softmax(scores, axis=-1)
    mixture = jnp.einsum('kgqs,skd->qkgd', low(weight), values, precision=PRECISE)
    return mixture.reshape(length, H * HD)

def layer(inputs, gain_attn, w_query, w_key, w_value, w_out, gain_moe, w_router, w_gate, w_up, w_down, segments, route_rows):
    seq_count, length = segments.shape
    normed_one = low(rms_scale(inputs, gain_attn))
    query_pre = low_back(matmul(normed_one, w_query)).reshape(seq_count, length, H, HD)
    key_pre = low_back(matmul(normed_one, w_key)).reshape(seq_count, length, KVH, HD)
    values = low_back(low(matmul(normed_one, w_value))).reshape(seq_count, length, KVH, HD)
    queries = low(rotary(query_pre))
    key_rows = low(rotary(key_pre))
    mixture = lax.map(jax.checkpoint(attend), (queries, key_rows, values, segments))
    attended = low_back(low(mixture.reshape(seq_count * length, H * HD)))
    hidden = inputs + low_back(matmul(attended, w_out))
    normed_two = low(rms_scale(hidden, gain_moe))
    logits = low_back(matmul(normed_two, w_router))
    experts = w_router.shape[1]
    one_hot = (route_rows[:, :, None] == jnp.arange(experts, dtype=jnp.int32)[None, None, :]).astype(jnp.float32)
    chosen = lax.optimization_barrier(jnp.sum(one_hot * logits[:, None, :], axis=-1))
    gate_weights = jax.nn.softmax(chosen, axis=-1)
    dense_gates = lax.optimization_barrier(jnp.sum(gate_weights[:, :, None] * one_hot, axis=1))

    def expert(running, pieces):
        gate_matrix, up_matrix, down_matrix, column = pieces
        token_rows = low_back(normed_two)
        gate_pre = low_back(matmul(token_rows, gate_matrix))
        up_pre = low_back(matmul(token_rows, up_matrix))
        active = low(jax.nn.silu(gate_pre) * up_pre)
        result = low_back(low(matmul(active, down_matrix)))
        return (running + column[:, None] * result, None)
    moe_sum, unused = lax.scan(jax.checkpoint(expert), jnp.zeros_like(hidden), (w_gate, w_up, w_down, dense_gates.T))
    outputs = low(hidden + moe_sum)
    probabilities = lax.optimization_barrier(jnp.mean(jax.nn.softmax(logits, axis=-1), axis=0))
    return (outputs, probabilities)

def reference(tokens, cotangent, segments, routes, gain_attn, w_query, w_key, w_value, w_out, gain_moe, w_router, w_gate, w_up, w_down):
    float_params = [weight_array.astype(jnp.float32) for weight_array in (gain_attn, w_query, w_key, w_value, w_out, gain_moe, w_router, w_gate, w_up, w_down)]

    def section_layer(section_index):

        def run_layer(inputs, *section_weights):
            return layer(inputs, *section_weights, segments, routes[section_index])
        return run_layer
    first_out, first_back, first_probs = jax.vjp(section_layer(0), tokens.astype(jnp.float32), *[weight_array[0] for weight_array in float_params], has_aux=True)
    second_out, second_back, second_probs = jax.vjp(section_layer(1), first_out, *[weight_array[1] for weight_array in float_params], has_aux=True)
    second_grads = second_back(cotangent.astype(jnp.float32))
    sent_back = low(second_grads[0])
    first_grads = first_back(sent_back)
    token_total = routes.shape[1]

    def balance(section_index, probabilities):
        one_hot = (routes[section_index][:, :, None] == jnp.arange(EXPERTS, dtype=jnp.int32)[None, None, :]).astype(jnp.float32)
        counts = lax.optimization_barrier(jnp.sum(one_hot, axis=(0, 1)))
        return EXPERTS * (counts / (token_total * TOPK) * probabilities)

    def paired(position_index):
        return jnp.stack([first_grads[position_index], second_grads[position_index]])
    layer_out = jnp.stack([first_out, second_out]).astype(jnp.bfloat16)
    input_grad = jnp.stack([first_grads[0], sent_back])
    balance_loss = jnp.stack([balance(0, first_probs), balance(1, second_probs)])
    return (layer_out, input_grad, paired(1), paired(2), paired(3), paired(4), paired(5), paired(6), paired(7), paired(8), paired(9), paired(10), balance_loss)
```

```python
import jax
import jax.numpy as jnp
from jax import lax
from jax.sharding import PartitionSpec as P

D = 1536
H = 24
KVH = 8
HD = 64
TOPK = 8
SEQ = 96


EPSILON = 1e-05
THETA = 10000.0
MASKED = -1e30


def matmul(left_side, right_side):
    return jnp.dot(left_side, right_side, preferred_element_type=jnp.float32)


def rotary_tables(length):
    half_width = HD // 2
    position = jnp.arange(length, dtype=jnp.float32)[:, None]
    freq_rate = THETA ** (-jnp.arange(half_width, dtype=jnp.float32) / half_width)
    angles = position * freq_rate[None, :]
    return (jnp.cos(angles)[:, None, :], jnp.sin(angles)[:, None, :])


def rotate(tensor, cosine_table, sine_table):
    half_width = HD // 2
    first_half = tensor[..., :half_width]
    second_half = tensor[..., half_width:]
    return jnp.concatenate(
        [
            first_half * cosine_table - second_half * sine_table,
            second_half * cosine_table + first_half * sine_table,
        ],
        axis=-1,
    )


def unrotate(gradient, cosine_table, sine_table):
    half_width = HD // 2
    first_half = gradient[..., :half_width]
    second_half = gradient[..., half_width:]
    return jnp.concatenate(
        [
            first_half * cosine_table + second_half * sine_table,
            second_half * cosine_table - first_half * sine_table,
        ],
        axis=-1,
    )


def norm_back(grad_normed, tensor, inverse, gain_vector):
    scaled = grad_normed * gain_vector
    grad_gain = jnp.sum(grad_normed * tensor * inverse, axis=0)
    grad_tensor = inverse * scaled - tensor * inverse**3 * jnp.mean(
        scaled * tensor, axis=-1, keepdims=True
    )
    return (grad_tensor, grad_gain)


def attention_scores(queries, key_rows, segment_row):
    length = queries.shape[0]
    grouped = queries.reshape(length, KVH, H // KVH, HD)
    scores = jnp.einsum(
        "qkgd,skd->kgqs", grouped, key_rows, preferred_element_type=jnp.float32
    ) * HD ** (-0.5)
    position = jnp.arange(length)
    allowed = (position[None, :] <= position[:, None]) & (
        segment_row[:, None] == segment_row[None, :]
    )
    return jnp.where(allowed[None, None], scores, MASKED)


def masked_softmax(logits, mask):
    highest = jnp.max(jnp.where(mask > 0, logits, MASKED), axis=-1, keepdims=True)
    exponent = jnp.where(mask > 0, jnp.exp(logits - highest), 0.0)
    return exponent / jnp.sum(exponent, axis=-1, keepdims=True)


def multi_hot(route_rows, experts):
    columns = jnp.arange(experts, dtype=jnp.int32)
    return jnp.sum(
        (route_rows[..., None] == columns).astype(jnp.float32), axis=-2
    )


def swapped(array):
    return lax.ppermute(array, "section", [(0, 1), (1, 0)])


def halved_over(arrays, axis, bit):
    count = lax.axis_size(axis)
    mine = (lax.axis_index(axis) >> bit) & 1
    pairs = [(i, i ^ (1 << bit)) for i in range(count)]
    results = []
    for array in arrays:
        keep = lax.dynamic_index_in_dim(array, mine, 0, keepdims=False)
        send = lax.dynamic_index_in_dim(array, 1 - mine, 0, keepdims=False)
        got = lax.ppermute(send, axis, pairs)
        results.append((keep.astype(jnp.float32) + got.astype(jnp.float32)).astype(jnp.bfloat16))
    return results


def scattered(array, steps):
    bits = len(steps)
    shape = array.shape[1:]
    array = array.reshape((2,) * bits + shape)
    left = sorted((place for _, _, place in steps))
    for axis, bit, place in steps:
        at = left.index(place)
        (array,) = halved_over([jnp.moveaxis(array, at, 0)], axis, bit)
        left.remove(place)
    return array.astype(jnp.float32)


def bits_of(count):
    return count.bit_length() - 1


def orders(axes):
    steps, place = [], 0
    per_axis = []
    for axis in axes:
        count = bits_of(lax.axis_size(axis))
        own = []
        for bit in range(count - 1, -1, -1):
            own.append((axis, bit, place))
            place += 1
        per_axis.append(own)
    first = [s for own in per_axis for s in own]
    second = [s for own in per_axis for s in reversed(own)]
    return second, first


def attention_forward(inputs, weights, segment_row):
    gain_attn, w_query, w_key, w_value, w_out, gain_moe = weights[:6]
    length = inputs.shape[0]
    cosine_table, sine_table = rotary_tables(length)
    inverse_one = lax.rsqrt(jnp.mean(inputs * inputs, axis=-1, keepdims=True) + EPSILON)
    normed_one = (inputs * inverse_one * gain_attn).astype(jnp.bfloat16)
    queries = rotate(
        matmul(normed_one, w_query).reshape(length, H, HD), cosine_table, sine_table
    ).astype(jnp.bfloat16)
    key_rows = rotate(
        matmul(normed_one, w_key).reshape(length, KVH, HD), cosine_table, sine_table
    ).astype(jnp.bfloat16)
    values = matmul(normed_one, w_value).astype(jnp.bfloat16).reshape(length, KVH, HD)
    scores = attention_scores(queries, key_rows, segment_row)
    highest = jnp.max(scores, axis=-1, keepdims=True)
    exponent = jnp.exp(scores - highest)
    denominator = jnp.sum(exponent, axis=-1, keepdims=True)
    weight = exponent / denominator
    attended = jnp.einsum(
        "kgqs,skd->qkgd", weight.astype(jnp.bfloat16), values, preferred_element_type=jnp.float32
    )
    attended = attended.reshape(length, H * HD).astype(jnp.bfloat16)
    hidden = inputs + matmul(attended, w_out)
    inverse_two = lax.rsqrt(jnp.mean(hidden * hidden, axis=-1, keepdims=True) + EPSILON)
    normed_two = (hidden * inverse_two * gain_moe).astype(jnp.bfloat16)
    state = (inverse_one, normed_one, queries, key_rows, values, weight, attended, hidden, inverse_two, normed_two)
    return state


def experts_forward(rows, mask, weights):
    w_router, w_gate, w_up, w_down = weights[6:]
    held = w_gate.shape[0]
    gates = masked_softmax(matmul(rows, w_router), mask)
    local = lax.dynamic_slice_in_dim(gates, lax.axis_index("expert") * held, held, 1)
    local = local.T[:, :, None]
    gate_pre = jnp.einsum("td,edf->etf", rows, w_gate, preferred_element_type=jnp.float32)
    up_pre = jnp.einsum("td,edf->etf", rows, w_up, preferred_element_type=jnp.float32)
    gated = (local * (jax.nn.silu(gate_pre) * up_pre)).astype(jnp.bfloat16)
    partial = jnp.einsum("etf,efd->td", gated, w_down, preferred_element_type=jnp.float32)
    return partial.astype(jnp.bfloat16), (rows, local, gate_pre, up_pre, gated)


def experts_backward(grad_rows, state, weights):
    w_router, w_gate, w_up, w_down = weights[6:]
    rows, local, gate_pre, up_pre, gated = state
    experts = w_router.shape[1]
    held = w_gate.shape[0]
    raw = jnp.einsum("td,efd->etf", grad_rows, w_down, preferred_element_type=jnp.float32)
    sigmoid = jax.nn.sigmoid(gate_pre)
    silu_gate = gate_pre * sigmoid
    grad_gates = jnp.sum(raw * (silu_gate * up_pre), axis=-1).T
    grad_gates = lax.dynamic_update_slice_in_dim(
        jnp.zeros((grad_gates.shape[0], experts), jnp.float32),
        grad_gates,
        lax.axis_index("expert") * held,
        1,
    )
    grad_active = local * raw
    grad_gate_pre = (grad_active * up_pre * sigmoid * (1.0 + gate_pre * (1.0 - sigmoid))).astype(
        jnp.bfloat16
    )
    grad_up_pre = (grad_active * silu_gate).astype(jnp.bfloat16)
    partial = jnp.einsum(
        "etf,edf->td", grad_gate_pre, w_gate, preferred_element_type=jnp.float32
    ) + jnp.einsum("etf,edf->td", grad_up_pre, w_up, preferred_element_type=jnp.float32)
    return partial.astype(jnp.bfloat16), grad_gates, grad_gate_pre, grad_up_pre


def attention_backward(grad_hidden, inputs, state, weights):
    gain_attn, w_query, w_key, w_value, w_out, gain_moe = weights[:6]
    (inverse_one, normed_one, queries, key_rows, values, weight, attended, hidden, inverse_two, normed_two) = state
    length = inputs.shape[0]
    grad_branch = grad_hidden.astype(jnp.bfloat16)
    grad_attended = jnp.einsum("td,cd->tc", grad_branch, w_out, preferred_element_type=jnp.float32)
    grad_attended = grad_attended.astype(jnp.bfloat16).reshape(length, KVH, H // KVH, HD)
    grad_weight = jnp.einsum(
        "qkgd,skd->kgqs", grad_attended, values, preferred_element_type=jnp.float32
    )
    grad_values = jnp.einsum(
        "kgqs,qkgd->skd",
        weight.astype(jnp.bfloat16),
        grad_attended,
        preferred_element_type=jnp.float32,
    )
    grad_values = grad_values.astype(jnp.bfloat16).reshape(length, KVH * HD)
    grad_scores = (
        weight * (grad_weight - jnp.sum(weight * grad_weight, axis=-1, keepdims=True))
    ).astype(jnp.bfloat16)
    score_scale = HD ** (-0.5)
    grouped = queries.reshape(length, KVH, H // KVH, HD)
    grad_queries = jnp.einsum(
        "kgqs,skd->qkgd", grad_scores, key_rows, preferred_element_type=jnp.float32
    )
    grad_queries = grad_queries.reshape(length, H, HD) * score_scale
    grad_keys = (
        jnp.einsum("kgqs,qkgd->skd", grad_scores, grouped, preferred_element_type=jnp.float32)
        * score_scale
    )
    cosine_table, sine_table = rotary_tables(length)
    grad_query_pre = (
        unrotate(grad_queries, cosine_table, sine_table)
        .reshape(length, H * HD)
        .astype(jnp.bfloat16)
    )
    grad_key_pre = (
        unrotate(grad_keys, cosine_table, sine_table).reshape(length, KVH * HD).astype(jnp.bfloat16)
    )
    grad_normed_one = (
        jnp.einsum("tq,cq->tc", grad_query_pre, w_query, preferred_element_type=jnp.float32)
        + jnp.einsum("tq,cq->tc", grad_key_pre, w_key, preferred_element_type=jnp.float32)
        + jnp.einsum("tq,cq->tc", grad_values, w_value, preferred_element_type=jnp.float32)
    )
    grad_norm_one, grad_gain_attn = norm_back(grad_normed_one, inputs, inverse_one, gain_attn)
    grad_inputs = grad_hidden + grad_norm_one
    grad_qkv = jnp.concatenate([grad_query_pre, grad_key_pre, grad_values], axis=1)
    return grad_inputs, grad_gain_attn, grad_qkv, grad_branch


def gather_rows(rows):
    return lax.all_gather(rows, "expert", axis=0, tiled=True)


def sum_rows(partial):
    return lax.psum_scatter(
        partial, "expert", scatter_dimension=0, tiled=True
    ).astype(jnp.float32)


def turned(left, right):
    return jnp.einsum("tc,tq->cq", left, right, preferred_element_type=jnp.float32)


def body(tokens, cotangent, segments, routes, *weight_arrays):
    core = lax.axis_index("section")
    first = core == 0
    experts = weight_arrays[6].shape[2]
    held = weight_arrays[7].shape[1]
    own = [array[0] for array in weight_arrays]
    other = [swapped(array) for array in own]
    weights = [
        [jnp.where(first, a, b) for a, b in zip(own, other)],
        [jnp.where(first, b, a) for a, b in zip(own, other)],
    ]
    inputs_low = lax.dynamic_slice_in_dim(tokens, core * SEQ, SEQ, 0)
    grad_low = lax.dynamic_slice_in_dim(cotangent, core * SEQ, SEQ, 0)
    segment_row = lax.dynamic_index_in_dim(segments, core, 0, keepdims=False)
    mine = lax.dynamic_slice_in_dim(routes[0], core * SEQ, SEQ, 0)
    got = swapped(lax.dynamic_slice_in_dim(routes[0], (1 - core) * SEQ, SEQ, 0))
    routes_here = jnp.stack([jnp.where(first, mine, got), jnp.where(first, got, mine)])
    routes_all = lax.all_gather(routes_here, "expert", axis=1, tiled=True)
    masks_here = multi_hot(routes_here, experts)
    masks_all = multi_hot(routes_all, experts)

    saved, outs, probabilities = [], [], []
    for s in range(2):
        inputs = inputs_low.astype(jnp.float32)
        state = attention_forward(inputs, weights[s], segment_row)
        hidden, normed_two = state[7], state[9]
        logits = matmul(normed_two, weights[s][6])
        gates = masked_softmax(logits, masks_here[s])
        probabilities.append(jnp.sum(jax.nn.softmax(logits, axis=-1), axis=0))
        partial, expert_state = experts_forward(gather_rows(normed_two), masks_all[s], weights[s])
        inputs_low = (hidden + sum_rows(partial)).astype(jnp.bfloat16)
        outs.append(inputs_low)
        saved.append((inputs, state, gates, expert_state))

    counts = jnp.sum(masks_here, axis=1)
    axes = ("section", "dp", "expert")
    count_all, prob_all = lax.psum((counts, jnp.stack(probabilities)), axes)
    token_total = SEQ * lax.axis_size(axes)
    balance = experts * (count_all / (token_total * TOPK) * prob_all / token_total)
    balance = lax.dynamic_index_in_dim(balance, core, 0)

    grads = [None, None]
    input_grads = [None, None]
    for s in (1, 0):
        inputs, state, gates, expert_state = saved[s]
        (inverse_one, normed_one, _, _, _, _, attended, hidden, inverse_two, normed_two) = state
        gain_moe, w_router = weights[s][5], weights[s][6]
        grad_all = gather_rows(grad_low)
        partial, grad_gates, grad_gate_pre, grad_up_pre = experts_backward(
            grad_all, expert_state, weights[s]
        )
        grad_gates = lax.psum_scatter(grad_gates, "expert", scatter_dimension=0, tiled=True)
        grad_chosen = gates * (grad_gates - jnp.sum(gates * grad_gates, axis=-1, keepdims=True))
        grad_logits = grad_chosen.astype(jnp.bfloat16)
        grad_normed_two = sum_rows(partial) + jnp.einsum(
            "te,de->td", grad_logits, w_router, preferred_element_type=jnp.float32
        )
        grad_norm_two, grad_gain_moe = norm_back(grad_normed_two, hidden, inverse_two, gain_moe)
        grad_hidden = grad_low.astype(jnp.float32) + grad_norm_two
        half = held // 2
        stacked = jnp.stack([expert_state[4], grad_gate_pre, grad_up_pre])
        keep = lax.dynamic_slice_in_dim(stacked, core * half, half, 1)
        send = lax.dynamic_slice_in_dim(stacked, (1 - core) * half, half, 1)
        arrived = swapped(send)
        both = jnp.concatenate([keep, arrived], axis=2)
        rows_both = jnp.concatenate([expert_state[0], swapped(expert_state[0])], axis=0)
        grad_both = jnp.concatenate([grad_all, swapped(grad_all)], axis=0)
        w_down_grad = jnp.einsum(
            "etf,td->efd", both[0], grad_both, preferred_element_type=jnp.float32
        ).astype(jnp.bfloat16)
        w_gate_grad = jnp.einsum(
            "td,etf->edf", rows_both, both[1], preferred_element_type=jnp.float32
        ).astype(jnp.bfloat16)
        w_up_grad = jnp.einsum(
            "td,etf->edf", rows_both, both[2], preferred_element_type=jnp.float32
        ).astype(jnp.bfloat16)

        grad_inputs, grad_gain_attn, grad_qkv, grad_branch = attention_backward(
            grad_hidden, inputs, state, weights[s]
        )
        def halves(array):
            width = array.shape[1] // 2
            return (
                lax.dynamic_slice_in_dim(array, core * width, width, 1),
                lax.dynamic_slice_in_dim(array, (1 - core) * width, width, 1),
            )
        qkv_keep, qkv_send = halves(grad_qkv)
        branch_keep, branch_send = halves(grad_branch)
        packed = swapped(jnp.concatenate([normed_one, attended, qkv_send, branch_send], axis=1))
        normed_got, attended_got = packed[:, :D], packed[:, D : 2 * D]
        qkv_got = packed[:, 2 * D : 2 * D + qkv_send.shape[1]]
        branch_got = packed[:, 2 * D + qkv_send.shape[1] :]
        grad_w_qkv = turned(
            jnp.concatenate([normed_one, normed_got]), jnp.concatenate([qkv_keep, qkv_got])
        ).astype(jnp.bfloat16)
        grad_w_out = turned(
            jnp.concatenate([attended, attended_got]), jnp.concatenate([branch_keep, branch_got])
        ).astype(jnp.bfloat16)
        grad_w_router = turned(normed_two, grad_logits)
        small = jnp.concatenate(
            [grad_gain_attn[:, None], grad_gain_moe[:, None], grad_w_router], axis=1
        ).astype(jnp.bfloat16)
        grads[s] = (w_gate_grad, w_up_grad, w_down_grad, grad_w_qkv, grad_w_out, small)
        input_grads[s] = grad_inputs
        grad_low = grad_inputs.astype(jnp.bfloat16)

    order_a, order_b = orders(("dp",))
    order_all_a, order_all_b = orders(("dp", "expert"))
    dp = lax.axis_size("dp")
    devices = dp * lax.axis_size("expert")
    reduced = []
    for s in (0, 1):
        w_gate_grad, w_up_grad, w_down_grad, grad_w_qkv, grad_w_out, small = grads[s]

        def by_dp(array):
            return jnp.moveaxis(
                array.reshape(array.shape[0], dp, array.shape[1] // dp, array.shape[2]), 1, 0
            )

        def by_all(array):
            return array.reshape(devices, array.shape[0] // devices, array.shape[1])

        reduced.append(
            (
                scattered(by_dp(w_gate_grad), order_a),
                scattered(by_dp(w_up_grad), order_b),
                scattered(by_dp(w_down_grad), order_a),
                scattered(by_all(grad_w_qkv), order_all_a),
                scattered(by_all(grad_w_out), order_all_b),
                scattered(by_all(small), order_all_a),
            )
        )
    final = []
    for a, b, dim in zip(reduced[0], reduced[1], (0, 0, 0, 1, 1, None)):
        keep = jnp.where(first, a, b)
        got = swapped(jnp.where(first, b, a).astype(jnp.bfloat16)).astype(jnp.float32)
        if dim is None:
            final.append(keep + got)
        else:
            final.append(
                jnp.concatenate(
                    [jnp.where(first, keep, got), jnp.where(first, got, keep)], axis=dim
                )
            )
    w_gate_grad, w_up_grad, w_down_grad, grad_w_qkv, grad_w_out, small = final
    heads, kv = H * HD, KVH * HD
    out_keep = jnp.where(first, outs[0], outs[1])
    out_got = swapped(jnp.where(first, outs[1], outs[0]))
    layer_out = jnp.where(
        first, jnp.concatenate([out_keep, out_got]), jnp.concatenate([out_got, out_keep])
    )
    low_one = input_grads[1].astype(jnp.bfloat16).astype(jnp.float32)
    grad_keep = jnp.where(first, input_grads[0], low_one)
    grad_got = swapped(jnp.where(first, low_one, input_grads[0]))
    input_grad = jnp.where(
        first, jnp.concatenate([grad_keep, grad_got]), jnp.concatenate([grad_got, grad_keep])
    )
    results = (
        layer_out,
        input_grad,
        small[:, 0],
        grad_w_qkv[:, :heads],
        grad_w_qkv[:, heads : heads + kv],
        grad_w_qkv[:, heads + kv :],
        grad_w_out,
        small[:, 1],
        small[:, 2:],
        w_gate_grad,
        w_up_grad,
        w_down_grad,
    )
    return tuple(result[None] for result in results) + (balance,)


def solution(mesh):
    return jax.shard_map(
        body,
        mesh=mesh,
        in_specs=(
            P(("dp", "expert"), None),
            P(("dp", "expert"), None),
            P(("dp", "expert"), None),
            P("section", ("dp", "expert"), None),
            P("section", None),
            P("section", None, None),
            P("section", None, None),
            P("section", None, None),
            P("section", None, None),
            P("section", None),
            P("section", None, None),
            P("section", "expert", None, None),
            P("section", "expert", None, None),
            P("section", "expert", None, None),
        ),
        out_specs=(
            P("section", ("dp", "expert"), None),
            P("section", ("dp", "expert"), None),
            P("section", ("dp", "expert")),
            P("section", ("dp", "expert"), None),
            P("section", ("dp", "expert"), None),
            P("section", ("dp", "expert"), None),
            P("section", ("dp", "expert"), None),
            P("section", ("dp", "expert")),
            P("section", ("dp", "expert"), None),
            P("section", "expert", "dp", None),
            P("section", "expert", "dp", None),
            P("section", "expert", "dp", None),
            P("section", None),
        ),
        check_vma=False,
    )
```

```python
import functools
import itertools

import jax
import jax.numpy as jnp
from jax import lax
from jax.experimental import pallas as pl
from jax.experimental.pallas import tpu as pltpu
from jax.sharding import PartitionSpec as P

D = 1536
H = 24
KVH = 8
HD = 64
TOPK = 8
SEQ = 96


EPSILON = 1e-05
THETA = 10000.0
MASKED = -1e30


def matmul(left_side, right_side):
    return jnp.dot(left_side, right_side, preferred_element_type=jnp.float32)


def rotary_tables(length):
    half_width = HD // 2
    position = jnp.arange(length, dtype=jnp.float32)[:, None]
    freq_rate = THETA ** (-jnp.arange(half_width, dtype=jnp.float32) / half_width)
    angles = position * freq_rate[None, :]
    return (jnp.cos(angles)[:, None, :], jnp.sin(angles)[:, None, :])


def rotate(tensor, cosine_table, sine_table):
    half_width = HD // 2
    first_half = tensor[..., :half_width]
    second_half = tensor[..., half_width:]
    return jnp.concatenate(
        [
            first_half * cosine_table - second_half * sine_table,
            second_half * cosine_table + first_half * sine_table,
        ],
        axis=-1,
    )


def unrotate(gradient, cosine_table, sine_table):
    half_width = HD // 2
    first_half = gradient[..., :half_width]
    second_half = gradient[..., half_width:]
    return jnp.concatenate(
        [
            first_half * cosine_table + second_half * sine_table,
            second_half * cosine_table - first_half * sine_table,
        ],
        axis=-1,
    )


def norm_back(grad_normed, tensor, inverse, gain_vector):
    scaled = grad_normed * gain_vector
    grad_gain = jnp.sum(grad_normed * tensor * inverse, axis=0)
    grad_tensor = inverse * scaled - tensor * inverse**3 * jnp.mean(
        scaled * tensor, axis=-1, keepdims=True
    )
    return (grad_tensor, grad_gain)


def attention_scores(queries, key_rows, segment_row):
    length = queries.shape[0]
    grouped = queries.reshape(length, KVH, H // KVH, HD)
    scores = jnp.einsum(
        "qkgd,skd->kgqs", grouped, key_rows, preferred_element_type=jnp.float32
    ) * HD ** (-0.5)
    position = jnp.arange(length)
    allowed = (position[None, :] <= position[:, None]) & (
        segment_row[:, None] == segment_row[None, :]
    )
    return jnp.where(allowed[None, None], scores, MASKED)


def masked_softmax(logits, mask):
    highest = jnp.max(jnp.where(mask > 0, logits, MASKED), axis=-1, keepdims=True)
    exponent = jnp.where(mask > 0, jnp.exp(logits - highest), 0.0)
    return exponent / jnp.sum(exponent, axis=-1, keepdims=True)


def multi_hot(route_rows, experts):
    columns = jnp.arange(experts, dtype=jnp.int32)
    return jnp.sum(
        (route_rows[..., None] == columns).astype(jnp.float32), axis=-2
    )


def swapped(array):
    return lax.ppermute(array, "section", [(0, 1), (1, 0)])


def add_slab(total, arrived):
    *lead, rows, _ = total.shape
    step = 16 if rows % 16 == 0 else rows
    for where in itertools.product(*(range(n) for n in lead)):

        def add(i, carry):
            at = (*where, pl.ds(pl.multiple_of(i * step, step), step), slice(None))
            both = total[at].astype(jnp.float32) + arrived[at].astype(jnp.float32)
            total[at] = both.astype(jnp.bfloat16)
            return carry

        lax.fori_loop(0, rows // step, add, 0)


def sum_scatter_kernel(plan, *refs):
    lanes, ins, copies = plan
    sources = refs[:ins]
    outs = refs[ins : ins + len(lanes)]
    scratch = list(refs[ins + len(lanes) :])
    send_sem, recv_sem, local_sem = scratch[-3:]
    partners = []
    for lane in lanes:
        for axis, bits in lane["phases"]:
            partners += [(axis, bit) for bit in bits if (axis, bit) not in partners]
    index = {axis: lax.axis_index(axis) for axis, _ in partners}
    mine = {(axis, bit): (index[axis] >> bit) & 1 for axis, bit in partners}
    far = {key: index[key[0]] + (1 - 2 * mine[key]) * (1 << key[1]) for key in partners}
    barrier = pltpu.get_barrier_semaphore()
    for axis, bit in partners:
        pl.semaphore_signal(
            barrier, inc=1, device_id={axis: far[axis, bit]}, device_id_type=pl.DeviceIdType.MESH
        )
    pl.semaphore_wait(barrier, len(partners))

    counter = itertools.count()

    def send(source, target, key):
        number = next(counter)
        copy = pltpu.make_async_remote_copy(
            src_ref=source,
            dst_ref=target,
            send_sem=send_sem.at[number],
            recv_sem=recv_sem.at[number],
            device_id={key[0]: far[key]},
            device_id_type=pl.DeviceIdType.MESH,
        )
        copy.start()
        return copy

    def place(axis, values):
        total = 0
        for bit, value in values.items():
            total = total + value * (1 << bit)
        return total

    started = []
    states = []
    for number, lane in enumerate(lanes):
        count = len(lane["buffers"])
        buffers, scratch = scratch[:count], scratch[count:]
        source = sources[lane["source"]]
        if lane["prefix"] is not None:
            source = source.at[lane["prefix"]]
        axis, bits = lane["phases"][0]
        total, arrived = buffers[0], buffers[1:]
        rest = [bit for bit in bits[1:]]
        pending = []
        for choice in itertools.product((0, 1), repeat=len(rest)):
            values = dict(zip(rest, choice))
            slot = sum(value << i for i, value in enumerate(choice))
            far_at = place(axis, {**values, bits[0]: 1 - mine[axis, bits[0]]})
            here_at = place(axis, {**values, bits[0]: mine[axis, bits[0]]})
            copy = send(source.at[far_at], arrived[0].at[slot], (axis, bits[0]))
            pending.append((copy, slot))
            started.append(copy)
            states.append((number, here_at, slot, source, total))
        lane_state = {"total": total, "arrived": arrived, "pending": pending, "rest": rest}
        lane["state"] = lane_state
    locals_ = {}
    for at, (number, here_at, slot, source, total) in enumerate(states):
        copy = pltpu.make_async_copy(source.at[here_at], total.at[slot], local_sem.at[at])
        copy.start()
        locals_[number, slot] = copy
    longest = max(sum(len(bits) for _, bits in lane["phases"]) for lane in lanes)
    for step in range(1, longest + 1):
        for number, lane in enumerate(lanes):
            state = lane["state"]
            sizes = [len(bits) for _, bits in lane["phases"]]
            if step > sum(sizes):
                continue
            if step <= sizes[0]:
                axis, bits = lane["phases"][0]
                resolved, rest = bits[:step], bits[step:]

                def slot_of(values):
                    found = 0
                    for i, bit in enumerate(bits[1:]):
                        found = found + values.get(bit, mine[axis, bit]) * (1 << i)
                    return found

                for copy, slot in state["pending"]:
                    copy.wait_recv()
                    if step == 1:
                        locals_[number, slot].wait()
                state["pending_next"] = []
                for choice in itertools.product((0, 1), repeat=len(rest)):
                    values = dict(zip(rest, choice))
                    got = sum(value << i for i, value in enumerate(choice))
                    add_slab(
                        state["total"].at[slot_of(values)], state["arrived"][step - 1].at[got]
                    )
                if rest:
                    following = rest[1:]
                    for choice in itertools.product((0, 1), repeat=len(following)):
                        values = dict(zip(following, choice))
                        got = sum(value << i for i, value in enumerate(choice))
                        values[rest[0]] = 1 - mine[axis, rest[0]]
                        copy = send(
                            state["total"].at[slot_of(values)],
                            state["arrived"][step].at[got],
                            (axis, rest[0]),
                        )
                        state["pending_next"].append((copy, got))
                        started.append(copy)
                final = state["total"].at[slot_of({})] if not rest else None
            else:
                axis, bits = lane["phases"][1]
                done = step - sizes[0]
                rest = bits[done:]
                final = state["final"]
                for copy, _ in state["pending"]:
                    copy.wait_recv()
                state["pending_next"] = []
                for choice in itertools.product((0, 1), repeat=len(rest)):
                    values = dict(zip(rest, choice))
                    got = sum(value << i for i, value in enumerate(choice))
                    at = place(axis, {bit: values.get(bit, mine[axis, bit]) for bit in bits})
                    add_slab(final.at[at], state["arrived"][step - 1].at[got])
                if not rest:
                    at = place(axis, {bit: mine[axis, bit] for bit in bits})
                    final = final.at[at]
            if final is not None and step >= sizes[0]:
                state["final"] = final
                if step == sum(sizes):
                    outs[number][...] = final[...]
                elif step < sum(sizes):
                    axis, bits = lane["phases"][1]
                    done = step - sizes[0]
                    bit, following = bits[done], bits[done + 1 :]
                    for choice in itertools.product((0, 1), repeat=len(following)):
                        values = dict(zip(following, choice))
                        got = sum(value << i for i, value in enumerate(choice))
                        at = place(
                            axis,
                            {
                                b: values.get(b, 1 - mine[axis, b] if b == bit else mine[axis, b])
                                for b in bits
                            },
                        )
                        copy = send(final.at[at], state["arrived"][step].at[got], (axis, bit))
                        state["pending_next"].append((copy, got))
                        started.append(copy)
            state["pending"] = state["pending_next"]
    for copy in started:
        copy.wait_send()


def sum_scatter(arrays, lanes, collective):
    plans, scratch, shapes, copies, locals_ = [], [], [], 0, 0
    for source, prefix, phases in lanes:
        shape = arrays[source].shape
        if prefix is not None:
            shape = shape[1:]
        buffers = [(shape[0] // 2, *shape[1:])]
        for step in range(1, len(phases[0][1]) + 1):
            buffers.append((shape[0] >> step, *shape[1:]))
            copies += shape[0] >> step
        locals_ += shape[0] // 2
        if len(phases) > 1:
            for step in range(1, len(phases[1][1]) + 1):
                buffers.append((shape[1] >> step, *shape[2:]))
                copies += shape[1] >> step
        plans.append({"source": source, "prefix": prefix, "phases": phases, "buffers": buffers})
        scratch += [pltpu.VMEM(buffer, jnp.bfloat16) for buffer in buffers]
        shapes.append(jax.ShapeDtypeStruct(shape[-2:], jnp.bfloat16))
    scratch += [
        pltpu.SemaphoreType.DMA((copies,)),
        pltpu.SemaphoreType.DMA((copies,)),
        pltpu.SemaphoreType.DMA((locals_,)),
    ]
    return pl.pallas_call(
        functools.partial(sum_scatter_kernel, (plans, len(arrays), copies)),
        out_shape=shapes,
        in_specs=[pl.BlockSpec(memory_space=pl.ANY)] * len(arrays),
        out_specs=[pl.BlockSpec(memory_space=pltpu.VMEM)] * len(lanes),
        scratch_shapes=scratch,
        compiler_params=pltpu.CompilerParams(
            collective_id=collective, has_side_effects=True, vmem_limit_bytes=60 * 2**20
        ),
    )(*arrays)


def bits_of(axis):
    return list(range(lax.axis_size(axis).bit_length() - 1))


def layer_lanes(first):
    up, down, deep = bits_of("dp"), bits_of("dp")[::-1], bits_of("expert")
    one, two = [("dp", up)], [("dp", down)]
    return [
        (first, 0, one),
        (first + 1, 0, two),
        (first, 1, one),
        (first + 1, 1, two),
        (first + 2, 0, one),
        (first + 2, 1, two),
        (first + 3, None, [("expert", deep), ("dp", up)]),
        (first + 4, None, [("dp", down), ("expert", deep)]),
        (first + 5, None, [("dp", up), ("expert", deep)]),
    ]


def attention_forward(inputs, weights, segment_row):
    gain_attn, w_query, w_key, w_value, w_out, gain_moe = weights[:6]
    length = inputs.shape[0]
    cosine_table, sine_table = rotary_tables(length)
    inverse_one = lax.rsqrt(jnp.mean(inputs * inputs, axis=-1, keepdims=True) + EPSILON)
    normed_one = (inputs * inverse_one * gain_attn).astype(jnp.bfloat16)
    queries = rotate(
        matmul(normed_one, w_query).reshape(length, H, HD), cosine_table, sine_table
    ).astype(jnp.bfloat16)
    key_rows = rotate(
        matmul(normed_one, w_key).reshape(length, KVH, HD), cosine_table, sine_table
    ).astype(jnp.bfloat16)
    values = matmul(normed_one, w_value).astype(jnp.bfloat16).reshape(length, KVH, HD)
    scores = attention_scores(queries, key_rows, segment_row)
    highest = jnp.max(scores, axis=-1, keepdims=True)
    exponent = jnp.exp(scores - highest)
    denominator = jnp.sum(exponent, axis=-1, keepdims=True)
    weight = exponent / denominator
    attended = jnp.einsum(
        "kgqs,skd->qkgd", weight.astype(jnp.bfloat16), values, preferred_element_type=jnp.float32
    )
    attended = attended.reshape(length, H * HD).astype(jnp.bfloat16)
    hidden = inputs + matmul(attended, w_out)
    inverse_two = lax.rsqrt(jnp.mean(hidden * hidden, axis=-1, keepdims=True) + EPSILON)
    normed_two = (hidden * inverse_two * gain_moe).astype(jnp.bfloat16)
    state = (inverse_one, normed_one, queries, key_rows, values, weight, attended, hidden, inverse_two, normed_two)
    return state


def experts_forward(rows, mask, weights):
    w_router, w_gate, w_up, w_down = weights[6:]
    held = w_gate.shape[0]
    gates = masked_softmax(matmul(rows, w_router), mask)
    local = lax.dynamic_slice_in_dim(gates, lax.axis_index("expert") * held, held, 1)
    local = local.T[:, :, None]
    gate_pre = jnp.einsum("td,edf->etf", rows, w_gate, preferred_element_type=jnp.float32)
    up_pre = jnp.einsum("td,edf->etf", rows, w_up, preferred_element_type=jnp.float32)
    gated = (local * (jax.nn.silu(gate_pre) * up_pre)).astype(jnp.bfloat16)
    partial = jnp.einsum("etf,efd->td", gated, w_down, preferred_element_type=jnp.float32)
    return partial.astype(jnp.bfloat16), (rows, local, gate_pre, up_pre, gated)


def experts_backward(grad_rows, state, weights):
    w_router, w_gate, w_up, w_down = weights[6:]
    rows, local, gate_pre, up_pre, gated = state
    experts = w_router.shape[1]
    held = w_gate.shape[0]
    raw = jnp.einsum("td,efd->etf", grad_rows, w_down, preferred_element_type=jnp.float32)
    sigmoid = jax.nn.sigmoid(gate_pre)
    silu_gate = gate_pre * sigmoid
    grad_gates = jnp.sum(raw * (silu_gate * up_pre), axis=-1).T
    grad_gates = lax.dynamic_update_slice_in_dim(
        jnp.zeros((grad_gates.shape[0], experts), jnp.float32),
        grad_gates,
        lax.axis_index("expert") * held,
        1,
    )
    grad_active = local * raw
    grad_gate_pre = (grad_active * up_pre * sigmoid * (1.0 + gate_pre * (1.0 - sigmoid))).astype(
        jnp.bfloat16
    )
    grad_up_pre = (grad_active * silu_gate).astype(jnp.bfloat16)
    partial = jnp.einsum(
        "etf,edf->td", grad_gate_pre, w_gate, preferred_element_type=jnp.float32
    ) + jnp.einsum("etf,edf->td", grad_up_pre, w_up, preferred_element_type=jnp.float32)
    return partial.astype(jnp.bfloat16), grad_gates, grad_gate_pre, grad_up_pre


def attention_backward(grad_hidden, inputs, state, weights):
    gain_attn, w_query, w_key, w_value, w_out, gain_moe = weights[:6]
    (inverse_one, normed_one, queries, key_rows, values, weight, attended, hidden, inverse_two, normed_two) = state
    length = inputs.shape[0]
    grad_branch = grad_hidden.astype(jnp.bfloat16)
    grad_attended = jnp.einsum("td,cd->tc", grad_branch, w_out, preferred_element_type=jnp.float32)
    grad_attended = grad_attended.astype(jnp.bfloat16).reshape(length, KVH, H // KVH, HD)
    grad_weight = jnp.einsum(
        "qkgd,skd->kgqs", grad_attended, values, preferred_element_type=jnp.float32
    )
    grad_values = jnp.einsum(
        "kgqs,qkgd->skd",
        weight.astype(jnp.bfloat16),
        grad_attended,
        preferred_element_type=jnp.float32,
    )
    grad_values = grad_values.astype(jnp.bfloat16).reshape(length, KVH * HD)
    grad_scores = (
        weight * (grad_weight - jnp.sum(weight * grad_weight, axis=-1, keepdims=True))
    ).astype(jnp.bfloat16)
    score_scale = HD ** (-0.5)
    grouped = queries.reshape(length, KVH, H // KVH, HD)
    grad_queries = jnp.einsum(
        "kgqs,skd->qkgd", grad_scores, key_rows, preferred_element_type=jnp.float32
    )
    grad_queries = grad_queries.reshape(length, H, HD) * score_scale
    grad_keys = (
        jnp.einsum("kgqs,qkgd->skd", grad_scores, grouped, preferred_element_type=jnp.float32)
        * score_scale
    )
    cosine_table, sine_table = rotary_tables(length)
    grad_query_pre = (
        unrotate(grad_queries, cosine_table, sine_table)
        .reshape(length, H * HD)
        .astype(jnp.bfloat16)
    )
    grad_key_pre = (
        unrotate(grad_keys, cosine_table, sine_table).reshape(length, KVH * HD).astype(jnp.bfloat16)
    )
    grad_normed_one = (
        jnp.einsum("tq,cq->tc", grad_query_pre, w_query, preferred_element_type=jnp.float32)
        + jnp.einsum("tq,cq->tc", grad_key_pre, w_key, preferred_element_type=jnp.float32)
        + jnp.einsum("tq,cq->tc", grad_values, w_value, preferred_element_type=jnp.float32)
    )
    grad_norm_one, grad_gain_attn = norm_back(grad_normed_one, inputs, inverse_one, gain_attn)
    grad_inputs = grad_hidden + grad_norm_one
    grad_qkv = jnp.concatenate([grad_query_pre, grad_key_pre, grad_values], axis=1)
    return grad_inputs, grad_gain_attn, grad_qkv, grad_branch


def gather_rows(rows):
    return lax.all_gather(rows, "expert", axis=0, tiled=True)


def sum_rows(partial):
    return lax.psum_scatter(
        partial, "expert", scatter_dimension=0, tiled=True
    ).astype(jnp.float32)


def turned(left, right):
    return jnp.einsum("tc,tq->cq", left, right, preferred_element_type=jnp.float32)


def body(tokens, cotangent, segments, routes, *weight_arrays):
    core = lax.axis_index("section")
    first = core == 0
    experts = weight_arrays[6].shape[2]
    held = weight_arrays[7].shape[1]
    own = [array[0] for array in weight_arrays]
    other = [swapped(array) for array in own]
    weights = [
        [jnp.where(first, a, b) for a, b in zip(own, other)],
        [jnp.where(first, b, a) for a, b in zip(own, other)],
    ]
    inputs_low = lax.dynamic_slice_in_dim(tokens, core * SEQ, SEQ, 0)
    grad_low = lax.dynamic_slice_in_dim(cotangent, core * SEQ, SEQ, 0)
    segment_row = lax.dynamic_index_in_dim(segments, core, 0, keepdims=False)
    mine = lax.dynamic_slice_in_dim(routes[0], core * SEQ, SEQ, 0)
    got = swapped(lax.dynamic_slice_in_dim(routes[0], (1 - core) * SEQ, SEQ, 0))
    routes_here = jnp.stack([jnp.where(first, mine, got), jnp.where(first, got, mine)])
    routes_all = lax.all_gather(routes_here, "expert", axis=1, tiled=True)
    masks_here = multi_hot(routes_here, experts)
    masks_all = multi_hot(routes_all, experts)

    saved, outs, probabilities = [], [], []
    for s in range(2):
        inputs = inputs_low.astype(jnp.float32)
        state = attention_forward(inputs, weights[s], segment_row)
        hidden, normed_two = state[7], state[9]
        logits = matmul(normed_two, weights[s][6])
        gates = masked_softmax(logits, masks_here[s])
        probabilities.append(jnp.sum(jax.nn.softmax(logits, axis=-1), axis=0))
        partial, expert_state = experts_forward(gather_rows(normed_two), masks_all[s], weights[s])
        inputs_low = (hidden + sum_rows(partial)).astype(jnp.bfloat16)
        outs.append(inputs_low)
        saved.append((inputs, state, gates, expert_state))

    counts = jnp.sum(masks_here, axis=1)
    axes = ("section", "dp", "expert")
    count_all, prob_all = lax.psum((counts, jnp.stack(probabilities)), axes)
    token_total = SEQ * lax.axis_size(axes)
    balance = experts * (count_all / (token_total * TOPK) * prob_all / token_total)
    balance = lax.dynamic_index_in_dim(balance, core, 0)

    grads = [None, None]
    input_grads = [None, None]
    for s in (1, 0):
        inputs, state, gates, expert_state = saved[s]
        (inverse_one, normed_one, _, _, _, _, attended, hidden, inverse_two, normed_two) = state
        gain_moe, w_router = weights[s][5], weights[s][6]
        grad_all = gather_rows(grad_low)
        partial, grad_gates, grad_gate_pre, grad_up_pre = experts_backward(
            grad_all, expert_state, weights[s]
        )
        grad_gates = lax.psum_scatter(grad_gates, "expert", scatter_dimension=0, tiled=True)
        grad_chosen = gates * (grad_gates - jnp.sum(gates * grad_gates, axis=-1, keepdims=True))
        grad_logits = grad_chosen.astype(jnp.bfloat16)
        grad_normed_two = sum_rows(partial) + jnp.einsum(
            "te,de->td", grad_logits, w_router, preferred_element_type=jnp.float32
        )
        grad_norm_two, grad_gain_moe = norm_back(grad_normed_two, hidden, inverse_two, gain_moe)
        grad_hidden = grad_low.astype(jnp.float32) + grad_norm_two
        half = held // 2
        stacked = jnp.stack([expert_state[4], grad_gate_pre, grad_up_pre])
        keep = lax.dynamic_slice_in_dim(stacked, core * half, half, 1)
        send = lax.dynamic_slice_in_dim(stacked, (1 - core) * half, half, 1)
        arrived = swapped(send)
        both = jnp.concatenate([keep, arrived], axis=2)
        rows_both = jnp.concatenate([expert_state[0], swapped(expert_state[0])], axis=0)
        grad_both = jnp.concatenate([grad_all, swapped(grad_all)], axis=0)
        w_down_grad = jnp.einsum(
            "etf,td->efd", both[0], grad_both, preferred_element_type=jnp.float32
        ).astype(jnp.bfloat16)
        w_gate_grad = jnp.einsum(
            "td,etf->edf", rows_both, both[1], preferred_element_type=jnp.float32
        ).astype(jnp.bfloat16)
        w_up_grad = jnp.einsum(
            "td,etf->edf", rows_both, both[2], preferred_element_type=jnp.float32
        ).astype(jnp.bfloat16)

        grad_inputs, grad_gain_attn, grad_qkv, grad_branch = attention_backward(
            grad_hidden, inputs, state, weights[s]
        )
        def halves(array):
            width = array.shape[1] // 2
            return (
                lax.dynamic_slice_in_dim(array, core * width, width, 1),
                lax.dynamic_slice_in_dim(array, (1 - core) * width, width, 1),
            )
        qkv_keep, qkv_send = halves(grad_qkv)
        branch_keep, branch_send = halves(grad_branch)
        packed = swapped(jnp.concatenate([normed_one, attended, qkv_send, branch_send], axis=1))
        normed_got, attended_got = packed[:, :D], packed[:, D : 2 * D]
        qkv_got = packed[:, 2 * D : 2 * D + qkv_send.shape[1]]
        branch_got = packed[:, 2 * D + qkv_send.shape[1] :]
        grad_w_qkv = turned(
            jnp.concatenate([normed_one, normed_got]), jnp.concatenate([qkv_keep, qkv_got])
        ).astype(jnp.bfloat16)
        grad_w_out = turned(
            jnp.concatenate([attended, attended_got]), jnp.concatenate([branch_keep, branch_got])
        ).astype(jnp.bfloat16)
        grad_w_router = turned(normed_two, grad_logits)
        small = jnp.concatenate(
            [grad_gain_attn[:, None], grad_gain_moe[:, None], grad_w_router], axis=1
        ).astype(jnp.bfloat16)
        grads[s] = (w_gate_grad, w_up_grad, w_down_grad, grad_w_qkv, grad_w_out, small)
        input_grads[s] = grad_inputs
        grad_low = grad_inputs.astype(jnp.bfloat16)

    dp, deep = lax.axis_size("dp"), lax.axis_size("expert")
    arrays, lanes = [], []
    for s in (1, 0):
        w_gate_grad, w_up_grad, w_down_grad, grad_w_qkv, grad_w_out, small = grads[s]
        lanes += layer_lanes(len(arrays))
        for array in (w_gate_grad, w_up_grad, w_down_grad):
            arrays.append(array.reshape(array.shape[0], dp, array.shape[1] // dp, array.shape[2]))
        small = jnp.pad(small, ((0, 0), (0, 128 - small.shape[1])))
        for array in (grad_w_qkv, grad_w_out, small):
            arrays.append(array.reshape(dp, deep, array.shape[0] // (dp * deep), array.shape[1]))
        arrays[-3] = jnp.swapaxes(arrays[-3], 0, 1)
    sums = sum_scatter(arrays, lanes, 0)
    reduced = []
    for piece in (sums[9:], sums[:9]):
        reduced.append(
            (
                jnp.stack([piece[0], piece[2]]),
                jnp.stack([piece[1], piece[3]]),
                jnp.stack([piece[4], piece[5]]),
                *piece[6:],
            )
        )
    final = []
    for a, b, dim in zip(reduced[0], reduced[1], (0, 0, 0, 1, 1, None)):
        keep = jnp.where(first, a, b)
        got = swapped(jnp.where(first, b, a))
        keep, got = keep.astype(jnp.float32), got.astype(jnp.float32)
        if dim is None:
            final.append(keep + got)
        else:
            final.append(
                jnp.concatenate(
                    [jnp.where(first, keep, got), jnp.where(first, got, keep)], axis=dim
                )
            )
    w_gate_grad, w_up_grad, w_down_grad, grad_w_qkv, grad_w_out, small = final
    heads, kv = H * HD, KVH * HD
    out_keep = jnp.where(first, outs[0], outs[1])
    out_got = swapped(jnp.where(first, outs[1], outs[0]))
    layer_out = jnp.where(
        first, jnp.concatenate([out_keep, out_got]), jnp.concatenate([out_got, out_keep])
    )
    low_one = input_grads[1].astype(jnp.bfloat16).astype(jnp.float32)
    grad_keep = jnp.where(first, input_grads[0], low_one)
    grad_got = swapped(jnp.where(first, low_one, input_grads[0]))
    input_grad = jnp.where(
        first, jnp.concatenate([grad_keep, grad_got]), jnp.concatenate([grad_got, grad_keep])
    )
    results = (
        layer_out,
        input_grad,
        small[:, 0],
        grad_w_qkv[:, :heads],
        grad_w_qkv[:, heads : heads + kv],
        grad_w_qkv[:, heads + kv :],
        grad_w_out,
        small[:, 1],
        small[:, 2 : 2 + experts],
        w_gate_grad,
        w_up_grad,
        w_down_grad,
    )
    return tuple(result[None] for result in results) + (balance,)


def solution(mesh):
    return jax.shard_map(
        body,
        mesh=mesh,
        in_specs=(
            P(("dp", "expert"), None),
            P(("dp", "expert"), None),
            P(("dp", "expert"), None),
            P("section", ("dp", "expert"), None),
            P("section", None),
            P("section", None, None),
            P("section", None, None),
            P("section", None, None),
            P("section", None, None),
            P("section", None),
            P("section", None, None),
            P("section", "expert", None, None),
            P("section", "expert", None, None),
            P("section", "expert", None, None),
        ),
        out_specs=(
            P("section", ("dp", "expert"), None),
            P("section", ("dp", "expert"), None),
            P("section", ("dp", "expert")),
            P("section", ("dp", "expert"), None),
            P("section", ("dp", "expert"), None),
            P("section", ("dp", "expert"), None),
            P("section", ("dp", "expert"), None),
            P("section", ("dp", "expert")),
            P("section", ("dp", "expert"), None),
            P("section", "expert", "dp", None),
            P("section", "expert", "dp", None),
            P("section", "expert", "dp", None),
            P("section", None),
        ),
        check_vma=False,
    )
```

```python
import functools
import itertools

import jax
import jax.numpy as jnp
from jax import lax
from jax.experimental import pallas as pl
from jax.experimental.pallas import tpu as pltpu
from jax.sharding import PartitionSpec as P

D = 1536
H = 24
KVH = 8
HD = 64
TOPK = 8
SEQ = 96


EPSILON = 1e-05
THETA = 10000.0
MASKED = -1e30


def matmul(left_side, right_side):
    return jnp.dot(left_side, right_side, preferred_element_type=jnp.float32)


def rotary_tables(length):
    half_width = HD // 2
    position = jnp.arange(length, dtype=jnp.float32)[:, None]
    freq_rate = THETA ** (-jnp.arange(half_width, dtype=jnp.float32) / half_width)
    angles = position * freq_rate[None, :]
    return (jnp.cos(angles)[:, None, :], jnp.sin(angles)[:, None, :])


def rotate(tensor, cosine_table, sine_table):
    half_width = HD // 2
    first_half = tensor[..., :half_width]
    second_half = tensor[..., half_width:]
    return jnp.concatenate(
        [
            first_half * cosine_table - second_half * sine_table,
            second_half * cosine_table + first_half * sine_table,
        ],
        axis=-1,
    )


def unrotate(gradient, cosine_table, sine_table):
    half_width = HD // 2
    first_half = gradient[..., :half_width]
    second_half = gradient[..., half_width:]
    return jnp.concatenate(
        [
            first_half * cosine_table + second_half * sine_table,
            second_half * cosine_table - first_half * sine_table,
        ],
        axis=-1,
    )


def norm_back(grad_normed, tensor, inverse, gain_vector):
    scaled = grad_normed * gain_vector
    grad_gain = jnp.sum(grad_normed * tensor * inverse, axis=0)
    grad_tensor = inverse * scaled - tensor * inverse**3 * jnp.mean(
        scaled * tensor, axis=-1, keepdims=True
    )
    return (grad_tensor, grad_gain)


def attention_scores(queries, key_rows, segment_row):
    length = queries.shape[0]
    grouped = queries.reshape(length, KVH, H // KVH, HD)
    scores = jnp.einsum(
        "qkgd,skd->kgqs", grouped, key_rows, preferred_element_type=jnp.float32
    ) * HD ** (-0.5)
    position = jnp.arange(length)
    allowed = (position[None, :] <= position[:, None]) & (
        segment_row[:, None] == segment_row[None, :]
    )
    return jnp.where(allowed[None, None], scores, MASKED)


def multi_hot(route_rows, experts):
    columns = jnp.arange(experts, dtype=jnp.int32)
    return jnp.sum(
        (route_rows[..., None] == columns).astype(jnp.float32), axis=-2
    )


def swapped(array):
    return lax.ppermute(array, "section", [(0, 1), (1, 0)])


def add_slab(total, arrived):
    *lead, rows, _ = total.shape
    step = 16 if rows % 16 == 0 else rows
    for where in itertools.product(*(range(n) for n in lead)):

        def add(i, carry):
            at = (*where, pl.ds(pl.multiple_of(i * step, step), step), slice(None))
            both = total[at].astype(jnp.float32) + arrived[at].astype(jnp.float32)
            total[at] = both.astype(jnp.bfloat16)
            return carry

        lax.fori_loop(0, rows // step, add, 0)


def sum_scatter_kernel(plan, *refs):
    lanes, ins, copies = plan
    sources = refs[:ins]
    stats_in = refs[ins]
    outs = refs[ins + 1 : ins + 1 + len(lanes)]
    stats = refs[ins + 1 + len(lanes)]
    scratch = list(refs[ins + 2 + len(lanes) :])
    send_sem, recv_sem, local_sem, stats_got, stats_send, stats_recv = scratch[-6:]
    partners = []
    for lane in lanes:
        for axis, bits in lane["phases"]:
            partners += [(axis, bit) for bit in bits if (axis, bit) not in partners]
    partners.append(("section", 0))
    index = {axis: lax.axis_index(axis) for axis, _ in partners}
    mine = {(axis, bit): (index[axis] >> bit) & 1 for axis, bit in partners}
    far = {key: index[key[0]] + (1 - 2 * mine[key]) * (1 << key[1]) for key in partners}
    barrier = pltpu.get_barrier_semaphore()
    for axis, bit in partners:
        pl.semaphore_signal(
            barrier, inc=1, device_id={axis: far[axis, bit]}, device_id_type=pl.DeviceIdType.MESH
        )
    pl.semaphore_wait(barrier, len(partners))

    counter = itertools.count()

    def send(source, target, key):
        number = next(counter)
        copy = pltpu.make_async_remote_copy(
            src_ref=source,
            dst_ref=target,
            send_sem=send_sem.at[number],
            recv_sem=recv_sem.at[number],
            device_id={key[0]: far[key]},
            device_id_type=pl.DeviceIdType.MESH,
        )
        copy.start()
        return copy

    def place(axis, values):
        total = 0
        for bit, value in values.items():
            total = total + value * (1 << bit)
        return total

    stats[...] = stats_in[...]

    def sum_stats():
        for at, key in enumerate(partners):
            copy = pltpu.make_async_remote_copy(
                src_ref=stats,
                dst_ref=stats_got.at[at],
                send_sem=stats_send.at[at],
                recv_sem=stats_recv.at[at],
                device_id={key[0]: far[key]},
                device_id_type=pl.DeviceIdType.MESH,
            )
            copy.start()
            yield
            copy.wait()
            stats[...] += stats_got[at]

    summing = sum_stats()
    started = []
    states = []
    for number, lane in enumerate(lanes):
        count = len(lane["buffers"])
        buffers, scratch = scratch[:count], scratch[count:]
        source = sources[lane["source"]]
        if lane["prefix"] is not None:
            source = source.at[lane["prefix"]]
        axis, bits = lane["phases"][0]
        total, arrived = buffers[0], buffers[1:]
        rest = [bit for bit in bits[1:]]
        pending = []
        for choice in itertools.product((0, 1), repeat=len(rest)):
            values = dict(zip(rest, choice))
            slot = sum(value << i for i, value in enumerate(choice))
            far_at = place(axis, {**values, bits[0]: 1 - mine[axis, bits[0]]})
            here_at = place(axis, {**values, bits[0]: mine[axis, bits[0]]})
            copy = send(source.at[far_at], arrived[0].at[slot], (axis, bits[0]))
            pending.append((copy, slot))
            started.append(copy)
            states.append((number, here_at, slot, source, total))
        lane_state = {"total": total, "arrived": arrived, "pending": pending, "rest": rest}
        lane["state"] = lane_state
    locals_ = {}
    for at, (number, here_at, slot, source, total) in enumerate(states):
        copy = pltpu.make_async_copy(source.at[here_at], total.at[slot], local_sem.at[at])
        copy.start()
        locals_[number, slot] = copy
    longest = max(sum(len(bits) for _, bits in lane["phases"]) for lane in lanes)
    for step in range(1, longest + 1):
        for number, lane in enumerate(lanes):
            next(summing, None)
            state = lane["state"]
            sizes = [len(bits) for _, bits in lane["phases"]]
            if step > sum(sizes):
                continue
            if step <= sizes[0]:
                axis, bits = lane["phases"][0]
                resolved, rest = bits[:step], bits[step:]

                def slot_of(values):
                    found = 0
                    for i, bit in enumerate(bits[1:]):
                        found = found + values.get(bit, mine[axis, bit]) * (1 << i)
                    return found

                for copy, slot in state["pending"]:
                    copy.wait_recv()
                    if step == 1:
                        locals_[number, slot].wait()
                state["pending_next"] = []
                for choice in itertools.product((0, 1), repeat=len(rest)):
                    values = dict(zip(rest, choice))
                    got = sum(value << i for i, value in enumerate(choice))
                    add_slab(
                        state["total"].at[slot_of(values)], state["arrived"][step - 1].at[got]
                    )
                if rest:
                    following = rest[1:]
                    for choice in itertools.product((0, 1), repeat=len(following)):
                        values = dict(zip(following, choice))
                        got = sum(value << i for i, value in enumerate(choice))
                        values[rest[0]] = 1 - mine[axis, rest[0]]
                        copy = send(
                            state["total"].at[slot_of(values)],
                            state["arrived"][step].at[got],
                            (axis, rest[0]),
                        )
                        state["pending_next"].append((copy, got))
                        started.append(copy)
                final = state["total"].at[slot_of({})] if not rest else None
            else:
                axis, bits = lane["phases"][1]
                done = step - sizes[0]
                rest = bits[done:]
                final = state["final"]
                for copy, _ in state["pending"]:
                    copy.wait_recv()
                state["pending_next"] = []
                for choice in itertools.product((0, 1), repeat=len(rest)):
                    values = dict(zip(rest, choice))
                    got = sum(value << i for i, value in enumerate(choice))
                    at = place(axis, {bit: values.get(bit, mine[axis, bit]) for bit in bits})
                    add_slab(final.at[at], state["arrived"][step - 1].at[got])
                if not rest:
                    at = place(axis, {bit: mine[axis, bit] for bit in bits})
                    final = final.at[at]
            if final is not None and step >= sizes[0]:
                state["final"] = final
                if step == sum(sizes):
                    outs[number][...] = final[...]
                elif step < sum(sizes):
                    axis, bits = lane["phases"][1]
                    done = step - sizes[0]
                    bit, following = bits[done], bits[done + 1 :]
                    for choice in itertools.product((0, 1), repeat=len(following)):
                        values = dict(zip(following, choice))
                        got = sum(value << i for i, value in enumerate(choice))
                        at = place(
                            axis,
                            {
                                b: values.get(b, 1 - mine[axis, b] if b == bit else mine[axis, b])
                                for b in bits
                            },
                        )
                        copy = send(final.at[at], state["arrived"][step].at[got], (axis, bit))
                        state["pending_next"].append((copy, got))
                        started.append(copy)
            state["pending"] = state["pending_next"]
    for _ in summing:
        pass
    for copy in started:
        copy.wait_send()


def sum_scatter(arrays, lanes, stats, collective):
    plans, scratch, shapes, copies, locals_ = [], [], [], 0, 0
    for source, prefix, phases in lanes:
        shape = arrays[source].shape
        if prefix is not None:
            shape = shape[1:]
        buffers = [(shape[0] // 2, *shape[1:])]
        for step in range(1, len(phases[0][1]) + 1):
            buffers.append((shape[0] >> step, *shape[1:]))
            copies += shape[0] >> step
        locals_ += shape[0] // 2
        if len(phases) > 1:
            for step in range(1, len(phases[1][1]) + 1):
                buffers.append((shape[1] >> step, *shape[2:]))
                copies += shape[1] >> step
        plans.append({"source": source, "prefix": prefix, "phases": phases, "buffers": buffers})
        scratch += [pltpu.VMEM(buffer, jnp.bfloat16) for buffer in buffers]
        shapes.append(jax.ShapeDtypeStruct(shape[-2:], jnp.bfloat16))
    scratch += [
        pltpu.SemaphoreType.DMA((copies,)),
        pltpu.SemaphoreType.DMA((copies,)),
        pltpu.SemaphoreType.DMA((locals_,)),
    ]
    hops = 1 + len(bits_of("dp")) + len(bits_of("expert"))
    scratch += [
        pltpu.VMEM((hops, *stats.shape), jnp.float32),
        pltpu.SemaphoreType.DMA((hops,)),
        pltpu.SemaphoreType.DMA((hops,)),
    ]
    shapes.append(jax.ShapeDtypeStruct(stats.shape, jnp.float32))
    return pl.pallas_call(
        functools.partial(sum_scatter_kernel, (plans, len(arrays), copies)),
        out_shape=shapes,
        in_specs=[pl.BlockSpec(memory_space=pl.ANY)] * len(arrays)
        + [pl.BlockSpec(memory_space=pltpu.VMEM)],
        out_specs=[pl.BlockSpec(memory_space=pltpu.VMEM)] * (len(lanes) + 1),
        scratch_shapes=scratch,
        compiler_params=pltpu.CompilerParams(
            collective_id=collective, has_side_effects=True, vmem_limit_bytes=60 * 2**20
        ),
    )(*arrays, stats)


def bits_of(axis):
    return list(range(lax.axis_size(axis).bit_length() - 1))


def layer_lanes(first):
    up, down, deep = bits_of("dp"), bits_of("dp")[::-1], bits_of("expert")
    one, two = [("dp", up)], [("dp", down)]
    return [
        (first, 0, one),
        (first + 1, 0, two),
        (first, 1, one),
        (first + 1, 1, two),
        (first + 2, 0, one),
        (first + 2, 1, two),
        (first + 3, None, [("expert", deep), ("dp", up)]),
        (first + 4, None, [("dp", down), ("expert", deep)]),
        (first + 5, None, [("dp", up), ("expert", deep)]),
    ]


def attention_forward(inputs, weights, segment_row):
    gain_attn, w_query, w_key, w_value, w_out, gain_moe = weights[:6]
    length = inputs.shape[0]
    cosine_table, sine_table = rotary_tables(length)
    inverse_one = lax.rsqrt(jnp.mean(inputs * inputs, axis=-1, keepdims=True) + EPSILON)
    normed_one = (inputs * inverse_one * gain_attn).astype(jnp.bfloat16)
    queries = rotate(
        matmul(normed_one, w_query).reshape(length, H, HD), cosine_table, sine_table
    ).astype(jnp.bfloat16)
    key_rows = rotate(
        matmul(normed_one, w_key).reshape(length, KVH, HD), cosine_table, sine_table
    ).astype(jnp.bfloat16)
    values = matmul(normed_one, w_value).astype(jnp.bfloat16).reshape(length, KVH, HD)
    scores = attention_scores(queries, key_rows, segment_row)
    highest = jnp.max(scores, axis=-1, keepdims=True)
    exponent = jnp.exp(scores - highest)
    denominator = jnp.sum(exponent, axis=-1, keepdims=True)
    weight = exponent / denominator
    attended = jnp.einsum(
        "kgqs,skd->qkgd", weight.astype(jnp.bfloat16), values, preferred_element_type=jnp.float32
    )
    attended = attended.reshape(length, H * HD).astype(jnp.bfloat16)
    hidden = inputs + matmul(attended, w_out)
    inverse_two = lax.rsqrt(jnp.mean(hidden * hidden, axis=-1, keepdims=True) + EPSILON)
    normed_two = (hidden * inverse_two * gain_moe).astype(jnp.bfloat16)
    state = (inverse_one, normed_one, queries, key_rows, values, weight, attended, hidden, inverse_two, normed_two)
    return state


MESH = pl.DeviceIdType.MESH
COLUMNS = 128


def move_rows(refs, compute, z, n):
    sources, held, sums, returned, sems = refs
    row_send, row_recv, sum_send, sum_recv = sems
    barrier = pltpu.get_barrier_semaphore()
    for k in range(1, n):
        peer = lax.rem(z + k, n)
        pl.semaphore_signal(barrier, inc=1, device_id={"expert": peer}, device_id_type=MESH)
    pl.semaphore_wait(barrier, n - 1)

    def row_copy(kind, way, hop, source=None):
        step = 1 - 2 * way
        block = jnp.clip(z - step * hop, 0, n - 1)
        peer = jnp.clip(z + step, 0, n - 1)
        return pltpu.make_async_remote_copy(
            src_ref=held[kind].at[block] if source is None else source,
            dst_ref=held[kind].at[block],
            send_sem=row_send.at[kind, way, hop],
            recv_sem=row_recv.at[kind, way, hop],
            device_id={"expert": peer},
            device_id_type=MESH,
        )

    def sends(way, hop):
        step = 1 - 2 * way
        block, peer = z - step * hop, z + step
        return (block >= 0) & (block < n) & (peer >= 0) & (peer < n)

    def arrives(way, hop):
        block = z - (1 - 2 * way) * (hop + 1)
        return (block >= 0) & (block < n)

    def start(kind):
        for way in range(2):
            @pl.when(sends(way, 0))
            def _():
                row_copy(kind, way, 0, sources[kind]).start()

    def take(hop):
        for kind in range(len(held)):
            for way in range(2):
                @pl.when(arrives(way, hop))
                def _():
                    row_copy(kind, way, hop).wait_recv()

                @pl.when(sends(way, hop + 1) & (hop + 1 < n - 1))
                def _():
                    row_copy(kind, way, hop + 1).start()

    def sum_copy(kind, peer):
        return pltpu.make_async_remote_copy(
            src_ref=sums[kind].at[peer],
            dst_ref=returned[kind].at[z],
            send_sem=sum_send.at[kind, peer],
            recv_sem=sum_recv.at[kind, z],
            device_id={"expert": peer},
            device_id_type=MESH,
        )

    def came_back(kind, peer):
        return pltpu.make_async_remote_copy(
            src_ref=sums[kind].at[peer],
            dst_ref=returned[kind].at[peer],
            send_sem=sum_send.at[kind, peer],
            recv_sem=sum_recv.at[kind, peer],
            device_id={"expert": peer},
            device_id_type=MESH,
        )

    def run():
        def turn(k, carry):
            hop = lax.div(k + 1, 2) - 1
            block = z + (1 + hop) * (1 - 2 * lax.rem(k, 2))

            @pl.when(lax.rem(k, 2) == 1)
            def _():
                take(hop)

            @pl.when((block >= 0) & (block < n))
            def _():
                compute(block)

                @pl.when(block != z)
                def _():
                    for kind in range(len(sums)):
                        sum_copy(kind, block).start()

            return carry

        lax.fori_loop(0, 2 * n - 1, turn, 0)

    def finish():
        for kind in range(len(held)):
            for way in range(2):
                for hop in range(n - 1):
                    @pl.when(sends(way, hop))
                    def _():
                        row_copy(kind, way, hop).wait_send()
        for kind in range(len(sums)):
            for k in range(1, n):
                sum_copy(kind, lax.rem(z + k, n)).wait_send()

    def collect(kind, k):
        peer = lax.rem(z + k, n)
        came_back(kind, peer).wait_recv()
        return peer

    return start, run, collect, finish


def fetch_weights(layer, own, other, places, sem):
    count = places[0].shape[0]
    mine = lax.axis_index("section") == layer

    def copy(group, kind, e):
        return pltpu.make_async_copy(
            group[kind].at[e], places[kind].at[e], sem.at[kind * count + e]
        )

    for kind in range(len(places)):
        for e in range(count):
            @pl.when(mine)
            def _():
                copy(own, kind, e).start()

            @pl.when(jnp.logical_not(mine))
            def _():
                copy(other, kind, e).start()

    def wait():
        for kind in range(len(places)):
            for e in range(count):
                copy(own, kind, e).wait()

    return wait


def sigmoid_of(value):
    return 1.0 / (1.0 + jnp.exp(-value))


def column_of(block, column):
    here = lax.broadcasted_iota(jnp.int32, block.shape, 1) == column
    return jnp.sum(jnp.where(here, block, 0.0), axis=1, keepdims=True)


def experts_forward_kernel(
    layer, experts, x, mask, hidden, router, *refs
):
    own, other, refs = refs[:3], refs[3:6], refs[6:]
    out, rows, gates, gate_keep, up_keep, gated, stats = refs[:7]
    w_gate, w_up, w_down, sums, returned, mixed, total = refs[7:14]
    weight_sem, *sems = refs[14:]
    n, held = rows.shape[0], w_gate.shape[0]
    z = lax.axis_index("expert")

    def compute(block):
        picked = rows[block]
        gate_block = gates[block]

        def one(e, carry):
            gate_pre = jnp.dot(picked, w_gate[e], preferred_element_type=jnp.float32)
            up_pre = jnp.dot(picked, w_up[e], preferred_element_type=jnp.float32)
            gate_keep[e, block] = gate_pre.astype(jnp.bfloat16)
            up_keep[e, block] = up_pre.astype(jnp.bfloat16)
            active = gate_pre * sigmoid_of(gate_pre) * up_pre
            share = (column_of(gate_block, z * held + e) * active).astype(jnp.bfloat16)
            gated[e, block] = share
            mixed[e] = share
            return carry

        lax.fori_loop(0, held, one, 0)
        width = out.shape[1] // 3
        for part in range(3):
            at = pl.ds(part * width, width)
            result = jnp.zeros((out.shape[0], width), jnp.float32)
            for e in range(held):
                result += jnp.dot(mixed[e], w_down[e, :, at], preferred_element_type=jnp.float32)

            @pl.when(block == z)
            def _():
                total[:, at] = hidden[:, at] + result

            @pl.when(block != z)
            def _():
                sums[block, :, at] = result.astype(jnp.bfloat16)

    own_gates = gates.at[z]
    start, run, collect, finish = move_rows(
        ((x, own_gates), (rows, gates), (sums,), (returned,), sems), compute, z, n
    )
    start(0)
    wait_weights = fetch_weights(layer, own, other, (w_gate, w_up, w_down), weight_sem)
    logits = jnp.dot(x[...], router[...], preferred_element_type=jnp.float32)
    chosen = mask[...] > 0
    highest = jnp.max(jnp.where(chosen, logits, MASKED), axis=1, keepdims=True)
    exponent = jnp.where(chosen, jnp.exp(logits - highest), 0.0)
    own_gates[...] = exponent / jnp.sum(exponent, axis=1, keepdims=True)
    start(1)
    real = lax.broadcasted_iota(jnp.int32, logits.shape, 1) < experts
    highest = jnp.max(jnp.where(real, logits, MASKED), axis=1, keepdims=True)
    exponent = jnp.where(real, jnp.exp(logits - highest), 0.0)
    chance = exponent / jnp.sum(exponent, axis=1, keepdims=True)
    line = lax.broadcasted_iota(jnp.int32, stats.shape, 0)
    stats[...] = jnp.where(
        line == 0,
        jnp.sum(chance, axis=0, keepdims=True),
        jnp.where(line == 1, jnp.sum(mask[...], axis=0, keepdims=True), 0.0),
    )
    rows[z] = x[...]
    wait_weights()
    run()
    for k in range(1, n):
        peer = collect(0, k)
        total[...] += returned[peer].astype(jnp.float32)
    out[...] = total[...].astype(jnp.bfloat16)
    finish()


def experts_backward_kernel(layer, grad, gates, gate_keep, up_keep, *refs):
    own, other, refs = refs[:3], refs[3:6], refs[6:]
    out, out_gates, rows, grad_gate, grad_up = refs[:5]
    w_gate, w_up, w_down, sums, sum_gates, returned, returned_gates = refs[5:12]
    weight_sem, *sems = refs[12:]
    n, held = rows.shape[0], w_gate.shape[0]
    z = lax.axis_index("expert")
    turned_dims = (((1,), (1,)), ((), ()))

    def compute(block):
        picked = rows[block]
        gate_block = gates[block]
        sum_gates[block] = jnp.zeros(sum_gates.shape[1:], jnp.float32)

        def one(e, carry):
            raw = lax.dot_general(
                picked, w_down[e], turned_dims, preferred_element_type=jnp.float32
            )
            gate_pre = gate_keep[e, block].astype(jnp.float32)
            up_pre = up_keep[e, block].astype(jnp.float32)
            sigmoid = sigmoid_of(gate_pre)
            silu = gate_pre * sigmoid
            column = z * held + e
            dot = jnp.sum(raw * (silu * up_pre), axis=1, keepdims=True)
            here = lax.broadcasted_iota(jnp.int32, sum_gates.shape[1:], 1) == column
            sum_gates[block] += jnp.where(here, dot, 0.0)
            active = column_of(gate_block, column) * raw
            grad_gate[e, block] = (
                active * up_pre * sigmoid * (1.0 + gate_pre * (1.0 - sigmoid))
            ).astype(jnp.bfloat16)
            grad_up[e, block] = (active * silu).astype(jnp.bfloat16)
            return carry

        lax.fori_loop(0, held, one, 0)
        width = out.shape[1] // 3
        for part in range(3):
            at = pl.ds(part * width, width)
            result = jnp.zeros((out.shape[0], width), jnp.float32)
            for e in range(held):
                for left, right in ((grad_gate, w_gate), (grad_up, w_up)):
                    result += lax.dot_general(
                        left[e, block],
                        right[e, at, :],
                        turned_dims,
                        preferred_element_type=jnp.float32,
                    )

            @pl.when(block == z)
            def _():
                out[:, at] = result

            @pl.when(block != z)
            def _():
                sums[block, :, at] = result.astype(jnp.bfloat16)

    start, run, collect, finish = move_rows(
        ((grad,), (rows,), (sums, sum_gates), (returned, returned_gates), sems), compute, z, n
    )
    start(0)
    wait_weights = fetch_weights(layer, own, other, (w_gate, w_up, w_down), weight_sem)
    rows[z] = grad[...]
    wait_weights()
    run()
    out_gates[...] = sum_gates[z]
    for k in range(1, n):
        peer = collect(0, k)
        out[...] += returned[peer].astype(jnp.float32)
        peer = collect(1, k)
        out_gates[...] += returned_gates[peer]
    finish()


def exchange_scratch(n, kinds_out, kinds_back):
    return [
        pltpu.SemaphoreType.DMA((kinds_out, 2, n)),
        pltpu.SemaphoreType.DMA((kinds_out, 2, n)),
        pltpu.SemaphoreType.DMA((kinds_back, n)),
        pltpu.SemaphoreType.DMA((kinds_back, n)),
    ]


def expert_call(kernel, operands, own, other, shapes, scratch, collective):
    vmem, free = pl.BlockSpec(memory_space=pltpu.VMEM), pl.BlockSpec(memory_space=pl.ANY)
    weights = [pltpu.VMEM(array.shape, jnp.bfloat16) for array in own]
    return pl.pallas_call(
        kernel,
        out_shape=shapes,
        in_specs=[vmem] * len(operands) + [free] * 6,
        out_specs=[vmem] * len(shapes),
        scratch_shapes=weights + scratch,
        compiler_params=pltpu.CompilerParams(
            collective_id=collective, has_side_effects=True, vmem_limit_bytes=50 * 2**20
        ),
    )(*operands, *own, *other)


def experts_forward(layer, normed_two, mask, hidden, router, own, other, experts):
    n, held = lax.axis_size("expert"), own[0].shape[0]
    length, width = normed_two.shape
    inner = own[0].shape[2]
    low, full = jnp.bfloat16, jnp.float32
    kept = jax.ShapeDtypeStruct((held, n, length, inner), low)
    shapes = [
        jax.ShapeDtypeStruct((length, width), low),
        jax.ShapeDtypeStruct((n, length, width), low),
        jax.ShapeDtypeStruct((n, length, COLUMNS), full),
        kept,
        kept,
        kept,
        jax.ShapeDtypeStruct((8, COLUMNS), full),
    ]
    scratch = [
        pltpu.VMEM((n, length, width), low),
        pltpu.VMEM((n, length, width), low),
        pltpu.VMEM((held, length, inner), low),
        pltpu.VMEM((length, width), full),
        pltpu.SemaphoreType.DMA((3 * held,)),
    ] + exchange_scratch(n, 2, 1)
    kernel = functools.partial(experts_forward_kernel, layer, experts)
    return expert_call(
        kernel, (normed_two, mask, hidden, router), own, other, shapes, scratch, 1 + layer
    )


def experts_backward(layer, grad_low, gates, gate_keep, up_keep, own, other):
    held, n, length, inner = gate_keep.shape
    width = grad_low.shape[1]
    low, full = jnp.bfloat16, jnp.float32
    kept = jax.ShapeDtypeStruct((held, n, length, inner), low)
    shapes = [
        jax.ShapeDtypeStruct((length, width), full),
        jax.ShapeDtypeStruct((length, COLUMNS), full),
        jax.ShapeDtypeStruct((n, length, width), low),
        kept,
        kept,
    ]
    scratch = [
        pltpu.VMEM((n, length, width), low),
        pltpu.VMEM((n, length, COLUMNS), full),
        pltpu.VMEM((n, length, width), low),
        pltpu.VMEM((n, length, COLUMNS), full),
        pltpu.SemaphoreType.DMA((3 * held,)),
    ] + exchange_scratch(n, 1, 2)
    kernel = functools.partial(experts_backward_kernel, layer)
    return expert_call(
        kernel, (grad_low, gates, gate_keep, up_keep), own, other, shapes, scratch, 3 + layer
    )


def attention_backward(grad_hidden, inputs, state, weights):
    gain_attn, w_query, w_key, w_value, w_out, gain_moe = weights[:6]
    (inverse_one, normed_one, queries, key_rows, values, weight, attended, hidden, inverse_two, normed_two) = state
    length = inputs.shape[0]
    grad_branch = grad_hidden.astype(jnp.bfloat16)
    grad_attended = jnp.einsum("td,cd->tc", grad_branch, w_out, preferred_element_type=jnp.float32)
    grad_attended = grad_attended.astype(jnp.bfloat16).reshape(length, KVH, H // KVH, HD)
    grad_weight = jnp.einsum(
        "qkgd,skd->kgqs", grad_attended, values, preferred_element_type=jnp.float32
    )
    grad_values = jnp.einsum(
        "kgqs,qkgd->skd",
        weight.astype(jnp.bfloat16),
        grad_attended,
        preferred_element_type=jnp.float32,
    )
    grad_values = grad_values.astype(jnp.bfloat16).reshape(length, KVH * HD)
    grad_scores = (
        weight * (grad_weight - jnp.sum(weight * grad_weight, axis=-1, keepdims=True))
    ).astype(jnp.bfloat16)
    score_scale = HD ** (-0.5)
    grouped = queries.reshape(length, KVH, H // KVH, HD)
    grad_queries = jnp.einsum(
        "kgqs,skd->qkgd", grad_scores, key_rows, preferred_element_type=jnp.float32
    )
    grad_queries = grad_queries.reshape(length, H, HD) * score_scale
    grad_keys = (
        jnp.einsum("kgqs,qkgd->skd", grad_scores, grouped, preferred_element_type=jnp.float32)
        * score_scale
    )
    cosine_table, sine_table = rotary_tables(length)
    grad_query_pre = (
        unrotate(grad_queries, cosine_table, sine_table)
        .reshape(length, H * HD)
        .astype(jnp.bfloat16)
    )
    grad_key_pre = (
        unrotate(grad_keys, cosine_table, sine_table).reshape(length, KVH * HD).astype(jnp.bfloat16)
    )
    grad_normed_one = (
        jnp.einsum("tq,cq->tc", grad_query_pre, w_query, preferred_element_type=jnp.float32)
        + jnp.einsum("tq,cq->tc", grad_key_pre, w_key, preferred_element_type=jnp.float32)
        + jnp.einsum("tq,cq->tc", grad_values, w_value, preferred_element_type=jnp.float32)
    )
    grad_norm_one, grad_gain_attn = norm_back(grad_normed_one, inputs, inverse_one, gain_attn)
    grad_inputs = grad_hidden + grad_norm_one
    grad_qkv = jnp.concatenate([grad_query_pre, grad_key_pre, grad_values], axis=1)
    return grad_inputs, grad_gain_attn, grad_qkv, grad_branch


def turned(left, right):
    return jnp.einsum("tc,tq->cq", left, right, preferred_element_type=jnp.float32)


def body(tokens, cotangent, segments, routes, *weight_arrays):
    core = lax.axis_index("section")
    first = core == 0
    experts = weight_arrays[6].shape[2]
    held = weight_arrays[7].shape[1]
    own = [array[0] for array in weight_arrays]
    other = [swapped(array) for array in own]
    weights = [
        [jnp.where(first, a, b) for a, b in zip(own[:7], other[:7])],
        [jnp.where(first, b, a) for a, b in zip(own[:7], other[:7])],
    ]
    inputs_low = lax.dynamic_slice_in_dim(tokens, core * SEQ, SEQ, 0)
    grad_low = lax.dynamic_slice_in_dim(cotangent, core * SEQ, SEQ, 0)
    segment_row = lax.dynamic_index_in_dim(segments, core, 0, keepdims=False)
    mine = lax.dynamic_slice_in_dim(routes[0], core * SEQ, SEQ, 0)
    got = swapped(lax.dynamic_slice_in_dim(routes[0], (1 - core) * SEQ, SEQ, 0))
    routes_here = jnp.stack([jnp.where(first, mine, got), jnp.where(first, got, mine)])
    masks = multi_hot(routes_here, COLUMNS)
    own_experts, other_experts = own[7:], other[7:]

    saved, outs, stats = [], [], []
    for s in range(2):
        inputs = inputs_low.astype(jnp.float32)
        state = attention_forward(inputs, weights[s], segment_row)
        hidden, normed_two = state[7], state[9]
        router = jnp.pad(weights[s][6], ((0, 0), (0, COLUMNS - experts)))
        inputs_low, *expert_state, stat = experts_forward(
            s, normed_two, masks[s], hidden, router, own_experts, other_experts, experts
        )
        outs.append(inputs_low)
        stats.append(stat)
        saved.append((inputs, state, expert_state))

    grads = [None, None]
    input_grads = [None, None]
    for s in (1, 0):
        inputs, state, expert_state = saved[s]
        (inverse_one, normed_one, _, _, _, _, attended, hidden, inverse_two, normed_two) = state
        rows_all, gates_all, gate_keep, up_keep, gated = expert_state
        gain_moe, w_router = weights[s][5], weights[s][6]
        grad_sum, grad_gates, grad_all, grad_gate_pre, grad_up_pre = experts_backward(
            s, grad_low, gates_all, gate_keep, up_keep, own_experts, other_experts
        )
        gates = lax.dynamic_index_in_dim(gates_all, lax.axis_index("expert"), 0, keepdims=False)
        gates, grad_gates = gates[:, :experts], grad_gates[:, :experts]
        grad_chosen = gates * (grad_gates - jnp.sum(gates * grad_gates, axis=-1, keepdims=True))
        grad_logits = grad_chosen.astype(jnp.bfloat16)
        grad_normed_two = grad_sum + jnp.einsum(
            "te,de->td", grad_logits, w_router, preferred_element_type=jnp.float32
        )
        grad_norm_two, grad_gain_moe = norm_back(grad_normed_two, hidden, inverse_two, gain_moe)
        grad_hidden = grad_low.astype(jnp.float32) + grad_norm_two
        half = held // 2
        inner = gated.shape[3]
        flat = [a.reshape(held, -1, inner) for a in (gated, grad_gate_pre, grad_up_pre)]
        rows_all, grad_all = rows_all.reshape(-1, D), grad_all.reshape(-1, D)
        stacked = jnp.stack(flat)
        keep = lax.dynamic_slice_in_dim(stacked, core * half, half, 1)
        send = lax.dynamic_slice_in_dim(stacked, (1 - core) * half, half, 1)
        arrived = swapped(send)
        both = jnp.concatenate([keep, arrived], axis=2)
        rows_both = jnp.concatenate([rows_all, swapped(rows_all)], axis=0)
        grad_both = jnp.concatenate([grad_all, swapped(grad_all)], axis=0)
        w_down_grad = jnp.einsum(
            "etf,td->efd", both[0], grad_both, preferred_element_type=jnp.float32
        ).astype(jnp.bfloat16)
        w_gate_grad = jnp.einsum(
            "td,etf->edf", rows_both, both[1], preferred_element_type=jnp.float32
        ).astype(jnp.bfloat16)
        w_up_grad = jnp.einsum(
            "td,etf->edf", rows_both, both[2], preferred_element_type=jnp.float32
        ).astype(jnp.bfloat16)

        grad_inputs, grad_gain_attn, grad_qkv, grad_branch = attention_backward(
            grad_hidden, inputs, state, weights[s]
        )
        def halves(array):
            width = array.shape[1] // 2
            return (
                lax.dynamic_slice_in_dim(array, core * width, width, 1),
                lax.dynamic_slice_in_dim(array, (1 - core) * width, width, 1),
            )
        qkv_keep, qkv_send = halves(grad_qkv)
        branch_keep, branch_send = halves(grad_branch)
        packed = swapped(jnp.concatenate([normed_one, attended, qkv_send, branch_send], axis=1))
        normed_got, attended_got = packed[:, :D], packed[:, D : 2 * D]
        qkv_got = packed[:, 2 * D : 2 * D + qkv_send.shape[1]]
        branch_got = packed[:, 2 * D + qkv_send.shape[1] :]
        grad_w_qkv = turned(
            jnp.concatenate([normed_one, normed_got]), jnp.concatenate([qkv_keep, qkv_got])
        ).astype(jnp.bfloat16)
        grad_w_out = turned(
            jnp.concatenate([attended, attended_got]), jnp.concatenate([branch_keep, branch_got])
        ).astype(jnp.bfloat16)
        grad_w_router = turned(normed_two, grad_logits)
        small = jnp.concatenate(
            [grad_gain_attn[:, None], grad_gain_moe[:, None], grad_w_router], axis=1
        ).astype(jnp.bfloat16)
        grads[s] = (w_gate_grad, w_up_grad, w_down_grad, grad_w_qkv, grad_w_out, small)
        input_grads[s] = grad_inputs
        grad_low = grad_inputs.astype(jnp.bfloat16)

    dp, deep = lax.axis_size("dp"), lax.axis_size("expert")
    arrays, lanes = [], []
    for s in (1, 0):
        w_gate_grad, w_up_grad, w_down_grad, grad_w_qkv, grad_w_out, small = grads[s]
        lanes += layer_lanes(len(arrays))
        for array in (w_gate_grad, w_up_grad, w_down_grad):
            arrays.append(array.reshape(array.shape[0], dp, array.shape[1] // dp, array.shape[2]))
        small = jnp.pad(small, ((0, 0), (0, 128 - small.shape[1])))
        for array in (grad_w_qkv, grad_w_out, small):
            arrays.append(array.reshape(dp, deep, array.shape[0] // (dp * deep), array.shape[1]))
        arrays[-3] = jnp.swapaxes(arrays[-3], 0, 1)
    *sums, stats = sum_scatter(arrays, lanes, jnp.concatenate(stats, axis=0), 0)
    stats = lax.dynamic_index_in_dim(stats.reshape(2, 8, COLUMNS), core, 0)
    token_total = SEQ * lax.axis_size(("section", "dp", "expert"))
    counts, chances = stats[:, 1, :experts], stats[:, 0, :experts]
    balance = experts * (counts / (token_total * TOPK) * chances / token_total)
    reduced = []
    for piece in (sums[9:], sums[:9]):
        reduced.append(
            (
                jnp.stack([piece[0], piece[2]]),
                jnp.stack([piece[1], piece[3]]),
                jnp.stack([piece[4], piece[5]]),
                *piece[6:],
            )
        )
    final = []
    for a, b, dim in zip(reduced[0], reduced[1], (0, 0, 0, 1, 1, None)):
        keep = jnp.where(first, a, b)
        got = swapped(jnp.where(first, b, a))
        keep, got = keep.astype(jnp.float32), got.astype(jnp.float32)
        if dim is None:
            final.append(keep + got)
        else:
            final.append(
                jnp.concatenate(
                    [jnp.where(first, keep, got), jnp.where(first, got, keep)], axis=dim
                )
            )
    w_gate_grad, w_up_grad, w_down_grad, grad_w_qkv, grad_w_out, small = final
    heads, kv = H * HD, KVH * HD
    out_keep = jnp.where(first, outs[0], outs[1])
    out_got = swapped(jnp.where(first, outs[1], outs[0]))
    layer_out = jnp.where(
        first, jnp.concatenate([out_keep, out_got]), jnp.concatenate([out_got, out_keep])
    )
    low_one = input_grads[1].astype(jnp.bfloat16).astype(jnp.float32)
    grad_keep = jnp.where(first, input_grads[0], low_one)
    grad_got = swapped(jnp.where(first, low_one, input_grads[0]))
    input_grad = jnp.where(
        first, jnp.concatenate([grad_keep, grad_got]), jnp.concatenate([grad_got, grad_keep])
    )
    results = (
        layer_out,
        input_grad,
        small[:, 0],
        grad_w_qkv[:, :heads],
        grad_w_qkv[:, heads : heads + kv],
        grad_w_qkv[:, heads + kv :],
        grad_w_out,
        small[:, 1],
        small[:, 2 : 2 + experts],
        w_gate_grad,
        w_up_grad,
        w_down_grad,
    )
    return tuple(result[None] for result in results) + (balance,)


def solution(mesh):
    return jax.shard_map(
        body,
        mesh=mesh,
        in_specs=(
            P(("dp", "expert"), None),
            P(("dp", "expert"), None),
            P(("dp", "expert"), None),
            P("section", ("dp", "expert"), None),
            P("section", None),
            P("section", None, None),
            P("section", None, None),
            P("section", None, None),
            P("section", None, None),
            P("section", None),
            P("section", None, None),
            P("section", "expert", None, None),
            P("section", "expert", None, None),
            P("section", "expert", None, None),
        ),
        out_specs=(
            P("section", ("dp", "expert"), None),
            P("section", ("dp", "expert"), None),
            P("section", ("dp", "expert")),
            P("section", ("dp", "expert"), None),
            P("section", ("dp", "expert"), None),
            P("section", ("dp", "expert"), None),
            P("section", ("dp", "expert"), None),
            P("section", ("dp", "expert")),
            P("section", ("dp", "expert"), None),
            P("section", "expert", "dp", None),
            P("section", "expert", "dp", None),
            P("section", "expert", "dp", None),
            P("section", None),
        ),
        check_vma=False,
    )
```

```python
import functools
import itertools

import jax
import jax.numpy as jnp
from jax import lax
from jax.experimental import pallas as pl
from jax.experimental.pallas import tpu as pltpu
from jax.sharding import PartitionSpec as P

D = 1536
H = 24
KVH = 8
HD = 64
TOPK = 8
SEQ = 96


EPSILON = 1e-05
THETA = 10000.0
MASKED = -1e30


def matmul(left_side, right_side):
    return jnp.dot(left_side, right_side, preferred_element_type=jnp.float32)


def rotary_tables(length):
    half_width = HD // 2
    position = jnp.arange(length, dtype=jnp.float32)[:, None]
    freq_rate = THETA ** (-jnp.arange(half_width, dtype=jnp.float32) / half_width)
    angles = position * freq_rate[None, :]
    return (jnp.cos(angles)[:, None, :], jnp.sin(angles)[:, None, :])


def rotate(tensor, cosine_table, sine_table):
    half_width = HD // 2
    first_half = tensor[..., :half_width]
    second_half = tensor[..., half_width:]
    return jnp.concatenate(
        [
            first_half * cosine_table - second_half * sine_table,
            second_half * cosine_table + first_half * sine_table,
        ],
        axis=-1,
    )


def unrotate(gradient, cosine_table, sine_table):
    half_width = HD // 2
    first_half = gradient[..., :half_width]
    second_half = gradient[..., half_width:]
    return jnp.concatenate(
        [
            first_half * cosine_table + second_half * sine_table,
            second_half * cosine_table - first_half * sine_table,
        ],
        axis=-1,
    )


def norm_back(grad_normed, tensor, inverse, gain_vector):
    scaled = grad_normed * gain_vector
    grad_gain = jnp.sum(grad_normed * tensor * inverse, axis=0)
    grad_tensor = inverse * scaled - tensor * inverse**3 * jnp.mean(
        scaled * tensor, axis=-1, keepdims=True
    )
    return (grad_tensor, grad_gain)


def attention_scores(queries, key_rows, segment_row):
    length = queries.shape[0]
    grouped = queries.reshape(length, KVH, H // KVH, HD)
    scores = jnp.einsum(
        "qkgd,skd->kgqs", grouped, key_rows, preferred_element_type=jnp.float32
    ) * HD ** (-0.5)
    position = jnp.arange(length)
    allowed = (position[None, :] <= position[:, None]) & (
        segment_row[:, None] == segment_row[None, :]
    )
    return jnp.where(allowed[None, None], scores, MASKED)


def multi_hot(route_rows, experts):
    columns = jnp.arange(experts, dtype=jnp.int32)
    return jnp.sum(
        (route_rows[..., None] == columns).astype(jnp.float32), axis=-2
    )


def swapped(array):
    return lax.ppermute(array, "section", [(0, 1), (1, 0)])


def add_slab(total, arrived):
    *lead, rows, _ = total.shape
    step = 16 if rows % 16 == 0 else rows
    for where in itertools.product(*(range(n) for n in lead)):

        def add(i, carry):
            at = (*where, pl.ds(pl.multiple_of(i * step, step), step), slice(None))
            both = total[at].astype(jnp.float32) + arrived[at].astype(jnp.float32)
            total[at] = both.astype(jnp.bfloat16)
            return carry

        lax.fori_loop(0, rows // step, add, 0)


def sum_scatter_kernel(plan, *refs):
    lanes, ins, copies = plan
    sources = refs[:ins]
    stats_in = refs[ins]
    outs = refs[ins + 1 : ins + 1 + len(lanes)]
    stats = refs[ins + 1 + len(lanes)]
    scratch = list(refs[ins + 2 + len(lanes) :])
    send_sem, recv_sem, local_sem, stats_got, stats_send, stats_recv = scratch[-6:]
    partners = []
    for lane in lanes:
        for axis, bits in lane["phases"]:
            partners += [(axis, bit) for bit in bits if (axis, bit) not in partners]
    partners.append(("section", 0))
    index = {axis: lax.axis_index(axis) for axis, _ in partners}
    mine = {(axis, bit): (index[axis] >> bit) & 1 for axis, bit in partners}
    far = {key: index[key[0]] + (1 - 2 * mine[key]) * (1 << key[1]) for key in partners}
    barrier = pltpu.get_barrier_semaphore()
    peers = [{axis: far[axis, bit]} for axis, bit in partners if axis != "dp"]
    groups = lax.axis_size("dp")
    peers += [{"dp": lax.rem(lax.axis_index("dp") + k, groups)} for k in range(1, groups)]
    for peer in peers:
        pl.semaphore_signal(
            barrier, inc=1, device_id=peer, device_id_type=pl.DeviceIdType.MESH
        )
    pl.semaphore_wait(barrier, len(peers))

    counter = itertools.count()

    def send(source, target, key):
        number = next(counter)
        copy = pltpu.make_async_remote_copy(
            src_ref=source,
            dst_ref=target,
            send_sem=send_sem.at[number],
            recv_sem=recv_sem.at[number],
            device_id={key[0]: far[key]},
            device_id_type=pl.DeviceIdType.MESH,
        )
        copy.start()
        return copy

    def place(axis, values):
        total = 0
        for bit, value in values.items():
            total = total + value * (1 << bit)
        return total

    def sum_stats():
        count = lax.axis_size("dp")
        me = lax.axis_index("dp")

        def copy(at, source, slot, target):
            return pltpu.make_async_remote_copy(
                src_ref=source,
                dst_ref=stats_got.at[slot],
                send_sem=stats_send.at[at],
                recv_sem=stats_recv.at[slot],
                device_id=target,
                device_id_type=pl.DeviceIdType.MESH,
            )

        for k in range(1, count):
            copy(k, stats_in, me, {"dp": lax.rem(me + k, count)}).start()
        yield
        stats[...] = stats_in[...]
        for k in range(1, count):
            peer = lax.rem(me + k, count)
            copy(k, stats_in, peer, {"dp": peer}).wait_recv()
            stats[...] += stats_got[peer]
        both = copy(0, stats, count, {"section": far["section", 0]})
        both.start()
        yield
        both.wait()
        stats[...] += stats_got[count]
        for k in range(1, count):
            copy(k, stats_in, me, {"dp": lax.rem(me + k, count)}).wait_send()

    summing = sum_stats()
    next(summing)
    started = []
    states = []
    for number, lane in enumerate(lanes):
        count = len(lane["buffers"])
        buffers, scratch = scratch[:count], scratch[count:]
        source = sources[lane["source"]]
        prefix = lane["prefix"]
        if isinstance(prefix, int):
            source = source.at[prefix]

        def part(at, source=source, prefix=prefix):
            if isinstance(prefix, tuple):
                return source.at[at, :, pl.ds(*prefix)]
            return source.at[at]

        axis, bits = lane["phases"][0]
        total, arrived = buffers[0], buffers[1:]
        rest = [bit for bit in bits[1:]]
        pending = []
        for choice in itertools.product((0, 1), repeat=len(rest)):
            values = dict(zip(rest, choice))
            slot = sum(value << i for i, value in enumerate(choice))
            far_at = place(axis, {**values, bits[0]: 1 - mine[axis, bits[0]]})
            here_at = place(axis, {**values, bits[0]: mine[axis, bits[0]]})
            copy = send(part(far_at), arrived[0].at[slot], (axis, bits[0]))
            pending.append((copy, slot))
            started.append(copy)
            states.append((number, part(here_at), slot, total))
        lane_state = {"total": total, "arrived": arrived, "pending": pending, "rest": rest}
        lane["state"] = lane_state
    locals_ = {}
    for at, (number, here, slot, total) in enumerate(states):
        copy = pltpu.make_async_copy(here, total.at[slot], local_sem.at[at])
        copy.start()
        locals_[number, slot] = copy
    longest = max(sum(len(bits) for _, bits in lane["phases"]) for lane in lanes)
    for step in range(1, longest + 1):
        if step == 2:
            next(summing)
        for number, lane in enumerate(lanes):
            state = lane["state"]
            sizes = [len(bits) for _, bits in lane["phases"]]
            if step > sum(sizes):
                continue
            if step <= sizes[0]:
                axis, bits = lane["phases"][0]
                resolved, rest = bits[:step], bits[step:]

                def slot_of(values):
                    found = 0
                    for i, bit in enumerate(bits[1:]):
                        found = found + values.get(bit, mine[axis, bit]) * (1 << i)
                    return found

                for copy, slot in state["pending"]:
                    copy.wait_recv()
                    if step == 1:
                        locals_[number, slot].wait()
                state["pending_next"] = []
                for choice in itertools.product((0, 1), repeat=len(rest)):
                    values = dict(zip(rest, choice))
                    got = sum(value << i for i, value in enumerate(choice))
                    add_slab(
                        state["total"].at[slot_of(values)], state["arrived"][step - 1].at[got]
                    )
                if rest:
                    following = rest[1:]
                    for choice in itertools.product((0, 1), repeat=len(following)):
                        values = dict(zip(following, choice))
                        got = sum(value << i for i, value in enumerate(choice))
                        values[rest[0]] = 1 - mine[axis, rest[0]]
                        copy = send(
                            state["total"].at[slot_of(values)],
                            state["arrived"][step].at[got],
                            (axis, rest[0]),
                        )
                        state["pending_next"].append((copy, got))
                        started.append(copy)
                final = state["total"].at[slot_of({})] if not rest else None
            else:
                axis, bits = lane["phases"][1]
                done = step - sizes[0]
                rest = bits[done:]
                final = state["final"]
                for copy, _ in state["pending"]:
                    copy.wait_recv()
                state["pending_next"] = []
                for choice in itertools.product((0, 1), repeat=len(rest)):
                    values = dict(zip(rest, choice))
                    got = sum(value << i for i, value in enumerate(choice))
                    at = place(axis, {bit: values.get(bit, mine[axis, bit]) for bit in bits})
                    add_slab(final.at[at], state["arrived"][step - 1].at[got])
                if not rest:
                    at = place(axis, {bit: mine[axis, bit] for bit in bits})
                    final = final.at[at]
            if final is not None and step >= sizes[0]:
                state["final"] = final
                if step == sum(sizes):
                    outs[number][...] = final[...]
                elif step < sum(sizes):
                    axis, bits = lane["phases"][1]
                    done = step - sizes[0]
                    bit, following = bits[done], bits[done + 1 :]
                    for choice in itertools.product((0, 1), repeat=len(following)):
                        values = dict(zip(following, choice))
                        got = sum(value << i for i, value in enumerate(choice))
                        at = place(
                            axis,
                            {
                                b: values.get(b, 1 - mine[axis, b] if b == bit else mine[axis, b])
                                for b in bits
                            },
                        )
                        copy = send(final.at[at], state["arrived"][step].at[got], (axis, bit))
                        state["pending_next"].append((copy, got))
                        started.append(copy)
            state["pending"] = state["pending_next"]
    for _ in summing:
        pass
    for copy in started:
        copy.wait_send()


def sum_scatter(arrays, lanes, stats, collective):
    plans, scratch, shapes, copies, locals_ = [], [], [], 0, 0
    for source, prefix, phases in lanes:
        shape = arrays[source].shape
        if isinstance(prefix, int):
            shape = shape[1:]
        elif prefix is not None:
            shape = (*shape[:-1], prefix[1])
        buffers = [(shape[0] // 2, *shape[1:])]
        for step in range(1, len(phases[0][1]) + 1):
            buffers.append((shape[0] >> step, *shape[1:]))
            copies += shape[0] >> step
        locals_ += shape[0] // 2
        if len(phases) > 1:
            for step in range(1, len(phases[1][1]) + 1):
                buffers.append((shape[1] >> step, *shape[2:]))
                copies += shape[1] >> step
        plans.append({"source": source, "prefix": prefix, "phases": phases, "buffers": buffers})
        scratch += [pltpu.VMEM(buffer, jnp.bfloat16) for buffer in buffers]
        shapes.append(jax.ShapeDtypeStruct(shape[-2:], jnp.bfloat16))
    scratch += [
        pltpu.SemaphoreType.DMA((copies,)),
        pltpu.SemaphoreType.DMA((copies,)),
        pltpu.SemaphoreType.DMA((locals_,)),
    ]
    hops = lax.axis_size("dp") + 1
    scratch += [
        pltpu.VMEM((hops, *stats.shape), jnp.float32),
        pltpu.SemaphoreType.DMA((hops,)),
        pltpu.SemaphoreType.DMA((hops,)),
    ]
    shapes.append(jax.ShapeDtypeStruct(stats.shape, jnp.float32))
    return pl.pallas_call(
        functools.partial(sum_scatter_kernel, (plans, len(arrays), copies)),
        out_shape=shapes,
        in_specs=[pl.BlockSpec(memory_space=pl.ANY)] * len(arrays)
        + [pl.BlockSpec(memory_space=pltpu.VMEM)],
        out_specs=[pl.BlockSpec(memory_space=pltpu.VMEM)] * (len(lanes) + 1),
        scratch_shapes=scratch,
        compiler_params=pltpu.CompilerParams(
            collective_id=collective, has_side_effects=True, vmem_limit_bytes=60 * 2**20
        ),
    )(*arrays, stats)


def bits_of(axis):
    return list(range(lax.axis_size(axis).bit_length() - 1))


def expert_lanes(first, inner):
    up, down = bits_of("dp"), bits_of("dp")[::-1]
    one, two = [("dp", up)], [("dp", down)]
    return [
        (first, (0, inner), one),
        (first, (2 * inner, inner), two),
        (first, (inner, inner), one),
        (first, (3 * inner, inner), two),
        (first + 1, 0, one),
        (first + 1, 1, two),
    ]


def dense_lanes(first):
    up, down, deep = bits_of("dp"), bits_of("dp")[::-1], bits_of("expert")
    return [
        (first, None, [("expert", deep), ("dp", up)]),
        (first + 1, None, [("dp", down), ("expert", deep)]),
        (first + 2, None, [("dp", up), ("expert", deep)]),
    ]


def attention_forward(inputs, weights, segment_row):
    gain_attn, w_query, w_key, w_value, w_out, gain_moe = weights[:6]
    length = inputs.shape[0]
    cosine_table, sine_table = rotary_tables(length)
    inverse_one = lax.rsqrt(jnp.mean(inputs * inputs, axis=-1, keepdims=True) + EPSILON)
    normed_one = (inputs * inverse_one * gain_attn).astype(jnp.bfloat16)
    queries = rotate(
        matmul(normed_one, w_query).reshape(length, H, HD), cosine_table, sine_table
    ).astype(jnp.bfloat16)
    key_rows = rotate(
        matmul(normed_one, w_key).reshape(length, KVH, HD), cosine_table, sine_table
    ).astype(jnp.bfloat16)
    values = matmul(normed_one, w_value).astype(jnp.bfloat16).reshape(length, KVH, HD)
    scores = attention_scores(queries, key_rows, segment_row)
    highest = jnp.max(scores, axis=-1, keepdims=True)
    exponent = jnp.exp(scores - highest)
    denominator = jnp.sum(exponent, axis=-1, keepdims=True)
    weight = exponent / denominator
    attended = jnp.einsum(
        "kgqs,skd->qkgd", weight.astype(jnp.bfloat16), values, preferred_element_type=jnp.float32
    )
    attended = attended.reshape(length, H * HD).astype(jnp.bfloat16)
    hidden = inputs + matmul(attended, w_out)
    inverse_two = lax.rsqrt(jnp.mean(hidden * hidden, axis=-1, keepdims=True) + EPSILON)
    normed_two = (hidden * inverse_two * gain_moe).astype(jnp.bfloat16)
    state = (inverse_one, normed_one, queries, key_rows, values, weight, attended, hidden, inverse_two, normed_two)
    return state


MESH = pl.DeviceIdType.MESH
COLUMNS = 128


def move_rows(refs, compute, z, n, others):
    sources, held, sums, returned, sems = refs
    row_send, row_recv, sum_send, sum_recv = sems
    barrier = pltpu.get_barrier_semaphore()
    for k in range(1, n):
        peer = lax.rem(z + k, n)
        pl.semaphore_signal(barrier, inc=1, device_id={"expert": peer}, device_id_type=MESH)
    for peer in others:
        pl.semaphore_signal(barrier, inc=1, device_id=peer, device_id_type=MESH)
    pl.semaphore_wait(barrier, n - 1 + len(others))

    def row_copy(kind, way, hop, source=None):
        step = 1 - 2 * way
        block = jnp.clip(z - step * hop, 0, n - 1)
        peer = jnp.clip(z + step, 0, n - 1)
        return pltpu.make_async_remote_copy(
            src_ref=held[kind].at[block] if source is None else source,
            dst_ref=held[kind].at[block],
            send_sem=row_send.at[kind, way, hop],
            recv_sem=row_recv.at[kind, way, hop],
            device_id={"expert": peer},
            device_id_type=MESH,
        )

    def sends(way, hop):
        step = 1 - 2 * way
        block, peer = z - step * hop, z + step
        return (block >= 0) & (block < n) & (peer >= 0) & (peer < n)

    def arrives(way, hop):
        block = z - (1 - 2 * way) * (hop + 1)
        return (block >= 0) & (block < n)

    def start(kind):
        for way in range(2):
            @pl.when(sends(way, 0))
            def _():
                row_copy(kind, way, 0, sources[kind]).start()

    def take(hop):
        for kind in range(len(held)):
            for way in range(2):
                @pl.when(arrives(way, hop))
                def _():
                    row_copy(kind, way, hop).wait_recv()

                @pl.when(sends(way, hop + 1) & (hop + 1 < n - 1))
                def _():
                    row_copy(kind, way, hop + 1).start()

    def sum_copy(kind, peer):
        return pltpu.make_async_remote_copy(
            src_ref=sums[kind].at[peer],
            dst_ref=returned[kind].at[z],
            send_sem=sum_send.at[kind, peer],
            recv_sem=sum_recv.at[kind, z],
            device_id={"expert": peer},
            device_id_type=MESH,
        )

    def came_back(kind, peer):
        return pltpu.make_async_remote_copy(
            src_ref=sums[kind].at[peer],
            dst_ref=returned[kind].at[peer],
            send_sem=sum_send.at[kind, peer],
            recv_sem=sum_recv.at[kind, peer],
            device_id={"expert": peer},
            device_id_type=MESH,
        )

    def run():
        def turn(k, carry):
            hop = lax.div(k + 1, 2) - 1
            block = z + (1 + hop) * (1 - 2 * lax.rem(k, 2))

            @pl.when(lax.rem(k, 2) == 1)
            def _():
                take(hop)

            @pl.when((block >= 0) & (block < n))
            def _():
                compute(block)

                @pl.when(block != z)
                def _():
                    for kind in range(len(sums)):
                        sum_copy(kind, block).start()

            return carry

        lax.fori_loop(0, 2 * n - 1, turn, 0)

    def finish():
        for kind in range(len(held)):
            for way in range(2):
                for hop in range(n - 1):
                    @pl.when(sends(way, hop))
                    def _():
                        row_copy(kind, way, hop).wait_send()
        for kind in range(len(sums)):
            for k in range(1, n):
                sum_copy(kind, lax.rem(z + k, n)).wait_send()

    def collect(kind, k):
        peer = lax.rem(z + k, n)
        came_back(kind, peer).wait_recv()
        return peer

    return start, run, collect, finish


def fetch_weights(layer, own, other, places, sem):
    count = places[0].shape[0]
    mine = lax.axis_index("section") == layer

    def copy(group, kind, e):
        return pltpu.make_async_copy(
            group[kind].at[e], places[kind].at[e], sem.at[kind * count + e]
        )

    for kind in range(len(places)):
        for e in range(count):
            @pl.when(mine)
            def _():
                copy(own, kind, e).start()

            @pl.when(jnp.logical_not(mine))
            def _():
                copy(other, kind, e).start()

    def wait():
        for kind in range(len(places)):
            for e in range(count):
                copy(own, kind, e).wait()

    return wait


def sigmoid_of(value):
    return 1.0 / (1.0 + jnp.exp(-value))


def column_of(block, column):
    here = lax.broadcasted_iota(jnp.int32, block.shape, 1) == column
    return jnp.sum(jnp.where(here, block, 0.0), axis=1, keepdims=True)


def experts_forward_kernel(
    layer, experts, x, mask, hidden, router, *refs
):
    own, other, refs = refs[:3], refs[3:6], refs[6:]
    out, rows, gates, gate_keep, up_keep, gated, stats = refs[:7]
    w_gate, w_up, w_down, sums, returned, mixed, total, stats_all = refs[7:15]
    weight_sem, *sems = refs[15:]
    n, held = rows.shape[0], w_gate.shape[0]
    z = lax.axis_index("expert")

    def compute(block):
        picked = rows[block]
        gate_block = gates[block]

        def one(e, carry):
            gate_pre = jnp.dot(picked, w_gate[e], preferred_element_type=jnp.float32)
            up_pre = jnp.dot(picked, w_up[e], preferred_element_type=jnp.float32)
            gate_keep[e, block] = gate_pre.astype(jnp.bfloat16)
            up_keep[e, block] = up_pre.astype(jnp.bfloat16)
            active = gate_pre * sigmoid_of(gate_pre) * up_pre
            share = (column_of(gate_block, z * held + e) * active).astype(jnp.bfloat16)
            inner = share.shape[1]
            gated[block, :, pl.ds(pl.multiple_of(e * inner, inner), inner)] = share
            mixed[e] = share
            return carry

        lax.fori_loop(0, held, one, 0)
        width = out.shape[1] // 3
        for part in range(3):
            at = pl.ds(part * width, width)
            result = jnp.zeros((out.shape[0], width), jnp.float32)
            for e in range(held):
                result += jnp.dot(mixed[e], w_down[e, :, at], preferred_element_type=jnp.float32)

            @pl.when(block == z)
            def _():
                total[:, at] = hidden[:, at] + result

            @pl.when(block != z)
            def _():
                sums[block, :, at] = result.astype(jnp.bfloat16)

    own_gates = gates.at[z]
    start, run, collect, finish = move_rows(
        ((x, own_gates, stats_all.at[z]), (rows, gates, stats_all), (sums,), (returned,), sems),
        compute,
        z,
        n,
        [],
    )
    start(0)
    wait_weights = fetch_weights(layer, own, other, (w_gate, w_up, w_down), weight_sem)
    logits = jnp.dot(x[...], router[...], preferred_element_type=jnp.float32)
    chosen = mask[...] > 0
    highest = jnp.max(jnp.where(chosen, logits, MASKED), axis=1, keepdims=True)
    exponent = jnp.where(chosen, jnp.exp(logits - highest), 0.0)
    own_gates[...] = exponent / jnp.sum(exponent, axis=1, keepdims=True)
    start(1)
    real = lax.broadcasted_iota(jnp.int32, logits.shape, 1) < experts
    highest = jnp.max(jnp.where(real, logits, MASKED), axis=1, keepdims=True)
    exponent = jnp.where(real, jnp.exp(logits - highest), 0.0)
    chance = exponent / jnp.sum(exponent, axis=1, keepdims=True)
    line = lax.broadcasted_iota(jnp.int32, stats.shape, 0)
    stats_all[z] = jnp.where(
        line == 0,
        jnp.sum(chance, axis=0, keepdims=True),
        jnp.where(line == 1, jnp.sum(mask[...], axis=0, keepdims=True), 0.0),
    )
    start(2)
    rows[z] = x[...]
    wait_weights()
    run()
    stats[...] = jnp.sum(stats_all[...], axis=0)
    for k in range(1, n):
        peer = collect(0, k)
        total[...] += returned[peer].astype(jnp.float32)
    out[...] = total[...].astype(jnp.bfloat16)
    finish()


def experts_backward_kernel(layer, grad, gates, gate_keep, up_keep, *refs):
    own, other, saved_rows, saved_gated, refs = refs[:3], refs[3:6], refs[6], refs[7], refs[8:]
    out, out_gates, rows_both, gated_both, grad_both, pre_both = refs[:6]
    w_gate, w_up, w_down, sums, sum_gates, returned, returned_gates, away = refs[6:14]
    weight_sem, core_send, core_recv, core_local, *sems = refs[14:]
    n, held = gates.shape[0], w_gate.shape[0]
    half, inner = held // 2, w_gate.shape[2]
    core = lax.axis_index("section")
    z = lax.axis_index("expert")
    turned_dims = (((1,), (1,)), ((), ()))
    rows = grad_both.at[core]

    def to_core(number, source, target):
        return pltpu.make_async_remote_copy(
            src_ref=source,
            dst_ref=target,
            send_sem=core_send.at[number],
            recv_sem=core_recv.at[number],
            device_id={"section": 1 - core},
            device_id_type=MESH,
        )

    def block_copies(block):
        return (
            to_core(2 + block, rows.at[block], rows.at[block]),
            to_core(2 + n + block, away.at[block], pre_both.at[core, block]),
        )

    def columns(at):
        return pl.ds(pl.multiple_of(at * half * inner, half * inner), half * inner)

    def whole_copies():
        return (
            to_core(0, saved_rows, rows_both.at[core]),
            to_core(1, saved_gated.at[:, :, columns(1 - core)], gated_both.at[core]),
        )

    def local_copies():
        return (
            pltpu.make_async_copy(saved_rows, rows_both.at[core], core_local.at[0]),
            pltpu.make_async_copy(
                saved_gated.at[:, :, columns(core)], gated_both.at[core], core_local.at[1]
            ),
        )

    def compute(block):
        picked = rows[block]
        gate_block = gates[block]
        sum_gates[block] = jnp.zeros(sum_gates.shape[1:], jnp.float32)

        def one(e, place, j):
            raw = lax.dot_general(
                picked, w_down[e], turned_dims, preferred_element_type=jnp.float32
            )
            gate_pre = gate_keep[e, block].astype(jnp.float32)
            up_pre = up_keep[e, block].astype(jnp.float32)
            sigmoid = sigmoid_of(gate_pre)
            silu = gate_pre * sigmoid
            column = z * held + e
            dot = jnp.sum(raw * (silu * up_pre), axis=1, keepdims=True)
            here = lax.broadcasted_iota(jnp.int32, sum_gates.shape[1:], 1) == column
            sum_gates[block] += jnp.where(here, dot, 0.0)
            active = column_of(gate_block, column) * raw
            place[:, pl.ds(pl.multiple_of(j * inner, inner), inner)] = (
                active * up_pre * sigmoid * (1.0 + gate_pre * (1.0 - sigmoid))
            ).astype(jnp.bfloat16)
            place[:, pl.ds(pl.multiple_of((half + j) * inner, inner), inner)] = (
                active * silu
            ).astype(jnp.bfloat16)

        def own_half(j, carry):
            one(core * half + j, pre_both.at[core, block], j)
            return carry

        def other_half(j, carry):
            one((1 - core) * half + j, away.at[block], j)
            return carry

        lax.fori_loop(0, half, other_half, 0)
        for copy in block_copies(block):
            copy.start()
        lax.fori_loop(0, half, own_half, 0)
        width = out.shape[1] // 3
        for part in range(3):
            at = pl.ds(part * width, width)
            result = jnp.zeros((out.shape[0], width), jnp.float32)
            for place, side in ((away.at[block], 1 - core), (pre_both.at[core, block], core)):
                for kind, right in enumerate((w_gate, w_up)):
                    for j in range(half):
                        left = place[:, pl.ds((kind * half + j) * inner, inner)]
                        result += lax.dot_general(
                            left,
                            right[side * half + j, at, :],
                            turned_dims,
                            preferred_element_type=jnp.float32,
                        )

            @pl.when(block == z)
            def _():
                out[:, at] = result

            @pl.when(block != z)
            def _():
                sums[block, :, at] = result.astype(jnp.bfloat16)

    start, run, collect, finish = move_rows(
        ((grad,), (rows,), (sums, sum_gates), (returned, returned_gates), sems),
        compute,
        z,
        n,
        [{"section": 1 - core}],
    )
    start(0)
    wait_weights = fetch_weights(layer, own, other, (w_gate, w_up, w_down), weight_sem)
    for copy in whole_copies() + local_copies():
        copy.start()
    rows[z] = grad[...]
    wait_weights()
    run()
    out_gates[...] = sum_gates[z]
    for k in range(1, n):
        peer = collect(0, k)
        out[...] += returned[peer].astype(jnp.float32)
        peer = collect(1, k)
        out_gates[...] += returned_gates[peer]
    finish()
    for copy in local_copies():
        copy.wait()
    for copy in whole_copies():
        copy.wait()
    for block in range(n):
        for copy in block_copies(block):
            copy.wait()


def exchange_scratch(n, kinds_out, kinds_back):
    return [
        pltpu.SemaphoreType.DMA((kinds_out, 2, n)),
        pltpu.SemaphoreType.DMA((kinds_out, 2, n)),
        pltpu.SemaphoreType.DMA((kinds_back, n)),
        pltpu.SemaphoreType.DMA((kinds_back, n)),
    ]


def expert_call(kernel, operands, own, other, extra, shapes, scratch, collective):
    vmem, free = pl.BlockSpec(memory_space=pltpu.VMEM), pl.BlockSpec(memory_space=pl.ANY)
    weights = [pltpu.VMEM(array.shape, jnp.bfloat16) for array in own]
    return pl.pallas_call(
        kernel,
        out_shape=shapes,
        in_specs=[vmem] * len(operands) + [free] * (6 + len(extra)),
        out_specs=[vmem] * len(shapes),
        scratch_shapes=weights + scratch,
        compiler_params=pltpu.CompilerParams(
            collective_id=collective, has_side_effects=True, vmem_limit_bytes=50 * 2**20
        ),
        cost_estimate=pl.CostEstimate(
            flops=5 * 10**10, bytes_accessed=10**8, transcendentals=0
        ),
    )(*operands, *own, *other, *extra)


def experts_forward(layer, normed_two, mask, hidden, router, own, other, experts):
    n, held = lax.axis_size("expert"), own[0].shape[0]
    length, width = normed_two.shape
    inner = own[0].shape[2]
    low, full = jnp.bfloat16, jnp.float32
    kept = jax.ShapeDtypeStruct((held, n, length, inner), low)
    shapes = [
        jax.ShapeDtypeStruct((length, width), low),
        jax.ShapeDtypeStruct((n, length, width), low),
        jax.ShapeDtypeStruct((n, length, COLUMNS), full),
        kept,
        kept,
        jax.ShapeDtypeStruct((n, length, held * inner), low),
        jax.ShapeDtypeStruct((8, COLUMNS), full),
    ]
    scratch = [
        pltpu.VMEM((n, length, width), low),
        pltpu.VMEM((n, length, width), low),
        pltpu.VMEM((held, length, inner), low),
        pltpu.VMEM((length, width), full),
        pltpu.VMEM((n, 8, COLUMNS), full),
        pltpu.SemaphoreType.DMA((3 * held,)),
    ] + exchange_scratch(n, 3, 1)
    kernel = functools.partial(experts_forward_kernel, layer, experts)
    return expert_call(
        kernel, (normed_two, mask, hidden, router), own, other, (), shapes, scratch, 1 + layer
    )


def experts_backward(layer, grad_low, gates, gate_keep, up_keep, rows, gated, own, other):
    held, n, length, inner = gate_keep.shape
    width = grad_low.shape[1]
    low, full = jnp.bfloat16, jnp.float32
    shapes = [
        jax.ShapeDtypeStruct((length, width), full),
        jax.ShapeDtypeStruct((length, COLUMNS), full),
        jax.ShapeDtypeStruct((2, n, length, width), low),
        jax.ShapeDtypeStruct((2, n, length, held // 2 * inner), low),
        jax.ShapeDtypeStruct((2, n, length, width), low),
        jax.ShapeDtypeStruct((2, n, length, held * inner), low),
    ]
    scratch = [
        pltpu.VMEM((n, length, width), low),
        pltpu.VMEM((n, length, COLUMNS), full),
        pltpu.VMEM((n, length, width), low),
        pltpu.VMEM((n, length, COLUMNS), full),
        pltpu.VMEM((n, length, held * inner), low),
        pltpu.SemaphoreType.DMA((3 * held,)),
        pltpu.SemaphoreType.DMA((2 + 2 * n,)),
        pltpu.SemaphoreType.DMA((2 + 2 * n,)),
        pltpu.SemaphoreType.DMA((2,)),
    ] + exchange_scratch(n, 1, 2)
    kernel = functools.partial(experts_backward_kernel, layer)
    return expert_call(
        kernel,
        (grad_low, gates, gate_keep, up_keep),
        own,
        other,
        (rows, gated),
        shapes,
        scratch,
        3 + layer,
    )


def attention_backward(grad_hidden, inputs, state, weights):
    gain_attn, w_query, w_key, w_value, w_out, gain_moe = weights[:6]
    (inverse_one, normed_one, queries, key_rows, values, weight, attended, hidden, inverse_two, normed_two) = state
    length = inputs.shape[0]
    grad_branch = grad_hidden.astype(jnp.bfloat16)
    grad_attended = jnp.einsum("td,cd->tc", grad_branch, w_out, preferred_element_type=jnp.float32)
    grad_attended = grad_attended.astype(jnp.bfloat16).reshape(length, KVH, H // KVH, HD)
    grad_weight = jnp.einsum(
        "qkgd,skd->kgqs", grad_attended, values, preferred_element_type=jnp.float32
    )
    grad_values = jnp.einsum(
        "kgqs,qkgd->skd",
        weight.astype(jnp.bfloat16),
        grad_attended,
        preferred_element_type=jnp.float32,
    )
    grad_values = grad_values.astype(jnp.bfloat16).reshape(length, KVH * HD)
    grad_scores = (
        weight * (grad_weight - jnp.sum(weight * grad_weight, axis=-1, keepdims=True))
    ).astype(jnp.bfloat16)
    score_scale = HD ** (-0.5)
    grouped = queries.reshape(length, KVH, H // KVH, HD)
    grad_queries = jnp.einsum(
        "kgqs,skd->qkgd", grad_scores, key_rows, preferred_element_type=jnp.float32
    )
    grad_queries = grad_queries.reshape(length, H, HD) * score_scale
    grad_keys = (
        jnp.einsum("kgqs,qkgd->skd", grad_scores, grouped, preferred_element_type=jnp.float32)
        * score_scale
    )
    cosine_table, sine_table = rotary_tables(length)
    grad_query_pre = (
        unrotate(grad_queries, cosine_table, sine_table)
        .reshape(length, H * HD)
        .astype(jnp.bfloat16)
    )
    grad_key_pre = (
        unrotate(grad_keys, cosine_table, sine_table).reshape(length, KVH * HD).astype(jnp.bfloat16)
    )
    grad_normed_one = (
        jnp.einsum("tq,cq->tc", grad_query_pre, w_query, preferred_element_type=jnp.float32)
        + jnp.einsum("tq,cq->tc", grad_key_pre, w_key, preferred_element_type=jnp.float32)
        + jnp.einsum("tq,cq->tc", grad_values, w_value, preferred_element_type=jnp.float32)
    )
    grad_norm_one, grad_gain_attn = norm_back(grad_normed_one, inputs, inverse_one, gain_attn)
    grad_inputs = grad_hidden + grad_norm_one
    grad_qkv = jnp.concatenate([grad_query_pre, grad_key_pre, grad_values], axis=1)
    return grad_inputs, grad_gain_attn, grad_qkv, grad_branch


def turned(left, right):
    return jnp.einsum("tc,tq->cq", left, right, preferred_element_type=jnp.float32)


def body(tokens, cotangent, segments, routes, *weight_arrays):
    core = lax.axis_index("section")
    first = core == 0
    experts = weight_arrays[6].shape[2]
    w_gate = weight_arrays[7]
    held = w_gate.shape[1]
    own = [array[0] for array in weight_arrays]
    other = [swapped(array) for array in own]
    weights = [
        [jnp.where(first, a, b) for a, b in zip(own[:7], other[:7])],
        [jnp.where(first, b, a) for a, b in zip(own[:7], other[:7])],
    ]
    inputs_low = lax.dynamic_slice_in_dim(tokens, core * SEQ, SEQ, 0)
    grad_low = lax.dynamic_slice_in_dim(cotangent, core * SEQ, SEQ, 0)
    segment_row = lax.dynamic_index_in_dim(segments, core, 0, keepdims=False)
    mine = lax.dynamic_slice_in_dim(routes[0], core * SEQ, SEQ, 0)
    got = swapped(lax.dynamic_slice_in_dim(routes[0], (1 - core) * SEQ, SEQ, 0))
    routes_here = jnp.stack([jnp.where(first, mine, got), jnp.where(first, got, mine)])
    masks = multi_hot(routes_here, COLUMNS)
    own_experts, other_experts = own[7:], other[7:]

    saved, outs, stats = [], [], []
    for s in range(2):
        inputs = inputs_low.astype(jnp.float32)
        state = attention_forward(inputs, weights[s], segment_row)
        hidden, normed_two = state[7], state[9]
        router = jnp.pad(weights[s][6], ((0, 0), (0, COLUMNS - experts)))
        inputs_low, *expert_state, stat = experts_forward(
            s, normed_two, masks[s], hidden, router, own_experts, other_experts, experts
        )
        outs.append(inputs_low)
        stats.append(stat)
        saved.append((inputs, state, expert_state))

    grads = [None, None]
    input_grads = [None, None]
    for s in (1, 0):
        inputs, state, expert_state = saved[s]
        (inverse_one, normed_one, _, _, _, _, attended, hidden, inverse_two, normed_two) = state
        rows_all, gates_all, gate_keep, up_keep, gated = expert_state
        gain_moe, w_router = weights[s][5], weights[s][6]
        grad_sum, grad_gates, rows_both, gated_both, grad_both, pre_both = experts_backward(
            s,
            grad_low,
            gates_all,
            gate_keep,
            up_keep,
            rows_all,
            gated,
            own_experts,
            other_experts,
        )
        inner = w_gate.shape[3]
        grad_gate_up = turned(
            rows_both.reshape(-1, D), pre_both.reshape(-1, held * inner)
        ).astype(jnp.bfloat16)
        grad_down = turned(
            gated_both.reshape(-1, held // 2 * inner), grad_both.reshape(-1, D)
        ).astype(jnp.bfloat16)
        grad_sum, grad_gate_up, grad_down = lax.optimization_barrier(
            (grad_sum, grad_gate_up, grad_down)
        )
        gates = lax.dynamic_index_in_dim(gates_all, lax.axis_index("expert"), 0, keepdims=False)
        gates, grad_gates = gates[:, :experts], grad_gates[:, :experts]
        grad_chosen = gates * (grad_gates - jnp.sum(gates * grad_gates, axis=-1, keepdims=True))
        grad_logits = grad_chosen.astype(jnp.bfloat16)
        grad_normed_two = grad_sum + jnp.einsum(
            "te,de->td", grad_logits, w_router, preferred_element_type=jnp.float32
        )
        grad_norm_two, grad_gain_moe = norm_back(grad_normed_two, hidden, inverse_two, gain_moe)
        grad_hidden = grad_low.astype(jnp.float32) + grad_norm_two
        grad_inputs, grad_gain_attn, grad_qkv, grad_branch = attention_backward(
            grad_hidden, inputs, state, weights[s]
        )
        def halves(array):
            width = array.shape[1] // 2
            return (
                lax.dynamic_slice_in_dim(array, core * width, width, 1),
                lax.dynamic_slice_in_dim(array, (1 - core) * width, width, 1),
            )
        qkv_keep, qkv_send = halves(grad_qkv)
        branch_keep, branch_send = halves(grad_branch)
        packed = swapped(jnp.concatenate([normed_one, attended, qkv_send, branch_send], axis=1))
        normed_got, attended_got = packed[:, :D], packed[:, D : 2 * D]
        qkv_got = packed[:, 2 * D : 2 * D + qkv_send.shape[1]]
        branch_got = packed[:, 2 * D + qkv_send.shape[1] :]
        grad_w_qkv = turned(
            jnp.concatenate([normed_one, normed_got]), jnp.concatenate([qkv_keep, qkv_got])
        ).astype(jnp.bfloat16)
        grad_w_out = turned(
            jnp.concatenate([attended, attended_got]), jnp.concatenate([branch_keep, branch_got])
        ).astype(jnp.bfloat16)
        grad_w_router = turned(normed_two, grad_logits)
        small = jnp.concatenate(
            [grad_gain_attn[:, None], grad_gain_moe[:, None], grad_w_router], axis=1
        ).astype(jnp.bfloat16)
        grads[s] = (grad_gate_up, grad_down, grad_w_qkv, grad_w_out, small)
        input_grads[s] = grad_inputs
        grad_low = grad_inputs.astype(jnp.bfloat16)

    dp, deep = lax.axis_size("dp"), lax.axis_size("expert")
    half, inner = held // 2, w_gate.shape[3]
    grad_gate_up, grad_down = grads[1][:2]
    second_pre = lax.psum_scatter(grad_gate_up, "dp", scatter_dimension=0, tiled=True)
    second_down = [
        lax.psum_scatter(
            grad_down[j * inner : (j + 1) * inner], "dp", scatter_dimension=0, tiled=True
        )
        for j in range(half)
    ]
    arrays, lanes = [], []
    for s in (0, 1):
        grad_gate_up, grad_down, grad_w_qkv, grad_w_out, small = grads[s]
        if s == 0:
            lanes += expert_lanes(len(arrays), inner)
            arrays.append(grad_gate_up.reshape(dp, D // dp, held * inner))
            arrays.append(grad_down.reshape(half, dp, inner // dp, D))
        lanes += dense_lanes(len(arrays))
        small = jnp.pad(small, ((0, 0), (0, 128 - small.shape[1])))
        for array in (grad_w_qkv, grad_w_out, small):
            arrays.append(array.reshape(dp, deep, array.shape[0] // (dp * deep), array.shape[1]))
        arrays[-3] = jnp.swapaxes(arrays[-3], 0, 1)
    *sums, stats = sum_scatter(arrays, lanes, jnp.concatenate(stats, axis=0), 0)
    stats = lax.dynamic_index_in_dim(stats.reshape(2, 8, COLUMNS), core, 0)
    token_total = SEQ * lax.axis_size(("section", "dp", "expert"))
    counts, chances = stats[:, 1, :experts], stats[:, 0, :experts]
    balance = experts * (counts / (token_total * TOPK) * chances / token_total)
    first_experts = (
        jnp.stack([sums[0], sums[2]]),
        jnp.stack([sums[1], sums[3]]),
        jnp.stack([sums[4], sums[5]]),
    )
    columns = [second_pre[:, i * inner : (i + 1) * inner] for i in range(2 * half)]
    second_experts = (
        jnp.stack(columns[:half]), jnp.stack(columns[half:]), jnp.stack(second_down)
    )
    reduced = [(*first_experts, *sums[6:9]), (*second_experts, *sums[9:])]
    final = []
    for a, b, dim in zip(reduced[0], reduced[1], (0, 0, 0, 1, 1, None)):
        keep = jnp.where(first, a, b)
        got = swapped(jnp.where(first, b, a))
        keep, got = keep.astype(jnp.float32), got.astype(jnp.float32)
        if dim is None:
            final.append(keep + got)
        else:
            final.append(
                jnp.concatenate(
                    [jnp.where(first, keep, got), jnp.where(first, got, keep)], axis=dim
                )
            )
    w_gate_grad, w_up_grad, w_down_grad, grad_w_qkv, grad_w_out, small = final
    heads, kv = H * HD, KVH * HD
    out_keep = jnp.where(first, outs[0], outs[1])
    out_got = swapped(jnp.where(first, outs[1], outs[0]))
    layer_out = jnp.where(
        first, jnp.concatenate([out_keep, out_got]), jnp.concatenate([out_got, out_keep])
    )
    low_one = input_grads[1].astype(jnp.bfloat16).astype(jnp.float32)
    grad_keep = jnp.where(first, input_grads[0], low_one)
    grad_got = swapped(jnp.where(first, low_one, input_grads[0]))
    input_grad = jnp.where(
        first, jnp.concatenate([grad_keep, grad_got]), jnp.concatenate([grad_got, grad_keep])
    )
    results = (
        layer_out,
        input_grad,
        small[:, 0],
        grad_w_qkv[:, :heads],
        grad_w_qkv[:, heads : heads + kv],
        grad_w_qkv[:, heads + kv :],
        grad_w_out,
        small[:, 1],
        small[:, 2 : 2 + experts],
        w_gate_grad,
        w_up_grad,
        w_down_grad,
    )
    return tuple(result[None] for result in results) + (balance,)


def solution(mesh):
    return jax.shard_map(
        body,
        mesh=mesh,
        in_specs=(
            P(("dp", "expert"), None),
            P(("dp", "expert"), None),
            P(("dp", "expert"), None),
            P("section", ("dp", "expert"), None),
            P("section", None),
            P("section", None, None),
            P("section", None, None),
            P("section", None, None),
            P("section", None, None),
            P("section", None),
            P("section", None, None),
            P("section", "expert", None, None),
            P("section", "expert", None, None),
            P("section", "expert", None, None),
        ),
        out_specs=(
            P("section", ("dp", "expert"), None),
            P("section", ("dp", "expert"), None),
            P("section", ("dp", "expert")),
            P("section", ("dp", "expert"), None),
            P("section", ("dp", "expert"), None),
            P("section", ("dp", "expert"), None),
            P("section", ("dp", "expert"), None),
            P("section", ("dp", "expert")),
            P("section", ("dp", "expert"), None),
            P("section", "expert", "dp", None),
            P("section", "expert", "dp", None),
            P("section", "expert", "dp", None),
            P("section", None),
        ),
        check_vma=False,
    )
```

```python
import functools
import itertools

import jax
import jax.numpy as jnp
from jax import lax
from jax.experimental import pallas as pl
from jax.experimental.pallas import tpu as pltpu
from jax.sharding import PartitionSpec as P

D = 1536
H = 24
KVH = 8
HD = 64
TOPK = 8
SEQ = 96


EPSILON = 1e-05
THETA = 10000.0
MASKED = -1e30


def matmul(left_side, right_side):
    return jnp.dot(left_side, right_side, preferred_element_type=jnp.float32)


def rotary_tables(length):
    half_width = HD // 2
    position = jnp.arange(length, dtype=jnp.float32)[:, None]
    freq_rate = THETA ** (-jnp.arange(half_width, dtype=jnp.float32) / half_width)
    angles = position * freq_rate[None, :]
    return (jnp.cos(angles)[:, None, :], jnp.sin(angles)[:, None, :])


def rotate(tensor, cosine_table, sine_table):
    half_width = HD // 2
    first_half = tensor[..., :half_width]
    second_half = tensor[..., half_width:]
    return jnp.concatenate(
        [
            first_half * cosine_table - second_half * sine_table,
            second_half * cosine_table + first_half * sine_table,
        ],
        axis=-1,
    )


def unrotate(gradient, cosine_table, sine_table):
    half_width = HD // 2
    first_half = gradient[..., :half_width]
    second_half = gradient[..., half_width:]
    return jnp.concatenate(
        [
            first_half * cosine_table + second_half * sine_table,
            second_half * cosine_table - first_half * sine_table,
        ],
        axis=-1,
    )


def norm_back(grad_normed, tensor, inverse, gain_vector):
    scaled = grad_normed * gain_vector
    grad_gain = jnp.sum(grad_normed * tensor * inverse, axis=0)
    grad_tensor = inverse * scaled - tensor * inverse**3 * jnp.mean(
        scaled * tensor, axis=-1, keepdims=True
    )
    return (grad_tensor, grad_gain)


def attention_scores(queries, key_rows, segment_row):
    length = queries.shape[0]
    grouped = queries.reshape(length, KVH, H // KVH, HD)
    scores = jnp.einsum(
        "qkgd,skd->kgqs", grouped, key_rows, preferred_element_type=jnp.float32
    ) * HD ** (-0.5)
    position = jnp.arange(length)
    allowed = (position[None, :] <= position[:, None]) & (
        segment_row[:, None] == segment_row[None, :]
    )
    return jnp.where(allowed[None, None], scores, MASKED)


def multi_hot(route_rows, experts):
    columns = jnp.arange(experts, dtype=jnp.int32)
    return jnp.sum(
        (route_rows[..., None] == columns).astype(jnp.float32), axis=-2
    )


def swapped(array):
    return lax.ppermute(array, "section", [(0, 1), (1, 0)])


def add_slab(total, arrived):
    *lead, rows, _ = total.shape
    step = 16 if rows % 16 == 0 else rows
    for where in itertools.product(*(range(n) for n in lead)):

        def add(i, carry):
            at = (*where, pl.ds(pl.multiple_of(i * step, step), step), slice(None))
            both = total[at].astype(jnp.float32) + arrived[at].astype(jnp.float32)
            total[at] = both.astype(jnp.bfloat16)
            return carry

        lax.fori_loop(0, rows // step, add, 0)


def sum_scatter_kernel(plan, *refs):
    lanes, ins, copies = plan
    sources = refs[:ins]
    stats_in = refs[ins]
    outs = refs[ins + 1 : ins + 1 + len(lanes)]
    stats = refs[ins + 1 + len(lanes)]
    scratch = list(refs[ins + 2 + len(lanes) :])
    send_sem, recv_sem, local_sem, stats_got, stats_send, stats_recv = scratch[-6:]
    partners = []
    for lane in lanes:
        for axis, bits in lane["phases"]:
            partners += [(axis, bit) for bit in bits if (axis, bit) not in partners]
    partners.append(("section", 0))
    index = {axis: lax.axis_index(axis) for axis, _ in partners}
    mine = {(axis, bit): (index[axis] >> bit) & 1 for axis, bit in partners}
    far = {key: index[key[0]] + (1 - 2 * mine[key]) * (1 << key[1]) for key in partners}
    barrier = pltpu.get_barrier_semaphore()
    peers = [{axis: far[axis, bit]} for axis, bit in partners if axis != "dp"]
    groups = lax.axis_size("dp")
    peers += [{"dp": lax.rem(lax.axis_index("dp") + k, groups)} for k in range(1, groups)]
    for peer in peers:
        pl.semaphore_signal(
            barrier, inc=1, device_id=peer, device_id_type=pl.DeviceIdType.MESH
        )
    pl.semaphore_wait(barrier, len(peers))

    counter = itertools.count()

    def send(source, target, key):
        number = next(counter)
        copy = pltpu.make_async_remote_copy(
            src_ref=source,
            dst_ref=target,
            send_sem=send_sem.at[number],
            recv_sem=recv_sem.at[number],
            device_id={key[0]: far[key]},
            device_id_type=pl.DeviceIdType.MESH,
        )
        copy.start()
        return copy

    def place(axis, values):
        total = 0
        for bit, value in values.items():
            total = total + value * (1 << bit)
        return total

    def sum_stats():
        count = lax.axis_size("dp")
        me = lax.axis_index("dp")

        def copy(at, source, slot, target):
            return pltpu.make_async_remote_copy(
                src_ref=source,
                dst_ref=stats_got.at[slot],
                send_sem=stats_send.at[at],
                recv_sem=stats_recv.at[slot],
                device_id=target,
                device_id_type=pl.DeviceIdType.MESH,
            )

        for k in range(1, count):
            copy(k, stats_in, me, {"dp": lax.rem(me + k, count)}).start()
        yield
        stats[...] = stats_in[...]
        for k in range(1, count):
            peer = lax.rem(me + k, count)
            copy(k, stats_in, peer, {"dp": peer}).wait_recv()
            stats[...] += stats_got[peer]
        both = copy(0, stats, count, {"section": far["section", 0]})
        both.start()
        yield
        both.wait()
        stats[...] += stats_got[count]
        for k in range(1, count):
            copy(k, stats_in, me, {"dp": lax.rem(me + k, count)}).wait_send()

    summing = sum_stats()
    next(summing)
    started = []
    states = []
    for number, lane in enumerate(lanes):
        count = len(lane["buffers"])
        buffers, scratch = scratch[:count], scratch[count:]
        source = sources[lane["source"]]
        prefix = lane["prefix"]
        if isinstance(prefix, int):
            source = source.at[prefix]

        def part(at, source=source, prefix=prefix):
            if isinstance(prefix, tuple):
                return source.at[at, :, pl.ds(*prefix)]
            if prefix == "inner":
                return source.at[:, at]
            return source.at[at]

        axis, bits = lane["phases"][0]
        total, arrived = buffers[0], buffers[1:]
        rest = [bit for bit in bits[1:]]
        pending = []
        for choice in itertools.product((0, 1), repeat=len(rest)):
            values = dict(zip(rest, choice))
            slot = sum(value << i for i, value in enumerate(choice))
            far_at = place(axis, {**values, bits[0]: 1 - mine[axis, bits[0]]})
            here_at = place(axis, {**values, bits[0]: mine[axis, bits[0]]})
            copy = send(part(far_at), arrived[0].at[slot], (axis, bits[0]))
            pending.append((copy, slot))
            started.append(copy)
            states.append((number, part(here_at), slot, total))
        lane_state = {"total": total, "arrived": arrived, "pending": pending, "rest": rest}
        lane["state"] = lane_state
    locals_ = {}
    for at, (number, here, slot, total) in enumerate(states):
        copy = pltpu.make_async_copy(here, total.at[slot], local_sem.at[at])
        copy.start()
        locals_[number, slot] = copy
    longest = max(sum(len(bits) for _, bits in lane["phases"]) for lane in lanes)
    for step in range(1, longest + 1):
        if step == 2:
            next(summing)
        for number, lane in enumerate(lanes):
            state = lane["state"]
            sizes = [len(bits) for _, bits in lane["phases"]]
            if step > sum(sizes):
                continue
            if step <= sizes[0]:
                axis, bits = lane["phases"][0]
                resolved, rest = bits[:step], bits[step:]

                def slot_of(values):
                    found = 0
                    for i, bit in enumerate(bits[1:]):
                        found = found + values.get(bit, mine[axis, bit]) * (1 << i)
                    return found

                for copy, slot in state["pending"]:
                    copy.wait_recv()
                    if step == 1:
                        locals_[number, slot].wait()
                state["pending_next"] = []
                for choice in itertools.product((0, 1), repeat=len(rest)):
                    values = dict(zip(rest, choice))
                    got = sum(value << i for i, value in enumerate(choice))
                    add_slab(
                        state["total"].at[slot_of(values)], state["arrived"][step - 1].at[got]
                    )
                if rest:
                    following = rest[1:]
                    for choice in itertools.product((0, 1), repeat=len(following)):
                        values = dict(zip(following, choice))
                        got = sum(value << i for i, value in enumerate(choice))
                        values[rest[0]] = 1 - mine[axis, rest[0]]
                        copy = send(
                            state["total"].at[slot_of(values)],
                            state["arrived"][step].at[got],
                            (axis, rest[0]),
                        )
                        state["pending_next"].append((copy, got))
                        started.append(copy)
                final = state["total"].at[slot_of({})] if not rest else None
            else:
                axis, bits = lane["phases"][1]
                done = step - sizes[0]
                rest = bits[done:]
                final = state["final"]
                for copy, _ in state["pending"]:
                    copy.wait_recv()
                state["pending_next"] = []
                for choice in itertools.product((0, 1), repeat=len(rest)):
                    values = dict(zip(rest, choice))
                    got = sum(value << i for i, value in enumerate(choice))
                    at = place(axis, {bit: values.get(bit, mine[axis, bit]) for bit in bits})
                    add_slab(final.at[at], state["arrived"][step - 1].at[got])
                if not rest:
                    at = place(axis, {bit: mine[axis, bit] for bit in bits})
                    final = final.at[at]
            if final is not None and step >= sizes[0]:
                state["final"] = final
                if step == sum(sizes):
                    outs[number][...] = final[...]
                elif step < sum(sizes):
                    axis, bits = lane["phases"][1]
                    done = step - sizes[0]
                    bit, following = bits[done], bits[done + 1 :]
                    for choice in itertools.product((0, 1), repeat=len(following)):
                        values = dict(zip(following, choice))
                        got = sum(value << i for i, value in enumerate(choice))
                        at = place(
                            axis,
                            {
                                b: values.get(b, 1 - mine[axis, b] if b == bit else mine[axis, b])
                                for b in bits
                            },
                        )
                        copy = send(final.at[at], state["arrived"][step].at[got], (axis, bit))
                        state["pending_next"].append((copy, got))
                        started.append(copy)
            state["pending"] = state["pending_next"]
    for _ in summing:
        pass
    for copy in started:
        copy.wait_send()


def sum_scatter(arrays, lanes, stats, collective):
    plans, scratch, shapes, copies, locals_ = [], [], [], 0, 0
    for source, prefix, phases in lanes:
        shape = arrays[source].shape
        if isinstance(prefix, int):
            shape = shape[1:]
        elif prefix == "inner":
            shape = (shape[1], shape[0], *shape[2:])
        elif prefix is not None:
            shape = (*shape[:-1], prefix[1])
        buffers = [(shape[0] // 2, *shape[1:])]
        for step in range(1, len(phases[0][1]) + 1):
            buffers.append((shape[0] >> step, *shape[1:]))
            copies += shape[0] >> step
        locals_ += shape[0] // 2
        if len(phases) > 1:
            for step in range(1, len(phases[1][1]) + 1):
                buffers.append((shape[1] >> step, *shape[2:]))
                copies += shape[1] >> step
        plans.append({"source": source, "prefix": prefix, "phases": phases, "buffers": buffers})
        scratch += [pltpu.VMEM(buffer, jnp.bfloat16) for buffer in buffers]
        shapes.append(jax.ShapeDtypeStruct(shape[-2:], jnp.bfloat16))
    scratch += [
        pltpu.SemaphoreType.DMA((copies,)),
        pltpu.SemaphoreType.DMA((copies,)),
        pltpu.SemaphoreType.DMA((locals_,)),
    ]
    hops = lax.axis_size("dp") + 1
    scratch += [
        pltpu.VMEM((hops, *stats.shape), jnp.float32),
        pltpu.SemaphoreType.DMA((hops,)),
        pltpu.SemaphoreType.DMA((hops,)),
    ]
    shapes.append(jax.ShapeDtypeStruct(stats.shape, jnp.float32))
    return pl.pallas_call(
        functools.partial(sum_scatter_kernel, (plans, len(arrays), copies)),
        out_shape=shapes,
        in_specs=[pl.BlockSpec(memory_space=pl.ANY)] * len(arrays)
        + [pl.BlockSpec(memory_space=pltpu.VMEM)],
        out_specs=[pl.BlockSpec(memory_space=pltpu.VMEM)] * (len(lanes) + 1),
        scratch_shapes=scratch,
        compiler_params=pltpu.CompilerParams(
            collective_id=collective, has_side_effects=True, vmem_limit_bytes=60 * 2**20
        ),
    )(*arrays, stats)


def bits_of(axis):
    return list(range(lax.axis_size(axis).bit_length() - 1))


def expert_lanes(first, inner):
    up, down = bits_of("dp"), bits_of("dp")[::-1]
    one, two = [("dp", up)], [("dp", down)]
    return [
        (first, (0, inner), one),
        (first, (2 * inner, inner), two),
        (first, (inner, inner), one),
        (first, (3 * inner, inner), two),
        (first + 1, 0, one),
        (first + 1, 1, two),
    ]


def dense_lanes(first):
    up, down, deep = bits_of("dp"), bits_of("dp")[::-1], bits_of("expert")
    return [
        (first, "inner", [("expert", deep), ("dp", up)]),
        (first + 1, None, [("dp", down), ("expert", deep)]),
        (first + 2, None, [("dp", up), ("expert", deep)]),
    ]


def attention_forward(inputs, weights, segment_row):
    gain_attn, w_query, w_key, w_value, w_out, gain_moe = weights[:6]
    length = inputs.shape[0]
    cosine_table, sine_table = rotary_tables(length)
    inverse_one = lax.rsqrt(jnp.mean(inputs * inputs, axis=-1, keepdims=True) + EPSILON)
    normed_one = (inputs * inverse_one * gain_attn).astype(jnp.bfloat16)
    queries = rotate(
        matmul(normed_one, w_query).reshape(length, H, HD), cosine_table, sine_table
    ).astype(jnp.bfloat16)
    key_rows = rotate(
        matmul(normed_one, w_key).reshape(length, KVH, HD), cosine_table, sine_table
    ).astype(jnp.bfloat16)
    values = matmul(normed_one, w_value).astype(jnp.bfloat16).reshape(length, KVH, HD)
    scores = attention_scores(queries, key_rows, segment_row)
    highest = jnp.max(scores, axis=-1, keepdims=True)
    exponent = jnp.exp(scores - highest)
    denominator = jnp.sum(exponent, axis=-1, keepdims=True)
    weight = exponent / denominator
    attended = jnp.einsum(
        "kgqs,skd->qkgd", weight.astype(jnp.bfloat16), values, preferred_element_type=jnp.float32
    )
    attended = attended.reshape(length, H * HD).astype(jnp.bfloat16)
    hidden = inputs + matmul(attended, w_out)
    inverse_two = lax.rsqrt(jnp.mean(hidden * hidden, axis=-1, keepdims=True) + EPSILON)
    normed_two = (hidden * inverse_two * gain_moe).astype(jnp.bfloat16)
    state = (inverse_one, normed_one, queries, key_rows, values, weight, attended, hidden, inverse_two, normed_two)
    return state


MESH = pl.DeviceIdType.MESH
COLUMNS = 128


def move_rows(refs, compute, z, n, others):
    sources, held, sums, returned, sems = refs
    row_send, row_recv, sum_send, sum_recv = sems
    barrier = pltpu.get_barrier_semaphore()
    for k in range(1, n):
        peer = lax.rem(z + k, n)
        pl.semaphore_signal(barrier, inc=1, device_id={"expert": peer}, device_id_type=MESH)
    for peer in others:
        pl.semaphore_signal(barrier, inc=1, device_id=peer, device_id_type=MESH)
    pl.semaphore_wait(barrier, n - 1 + len(others))

    def row_copy(kind, way, hop, source=None):
        step = 1 - 2 * way
        block = jnp.clip(z - step * hop, 0, n - 1)
        peer = jnp.clip(z + step, 0, n - 1)
        return pltpu.make_async_remote_copy(
            src_ref=held[kind].at[block] if source is None else source,
            dst_ref=held[kind].at[block],
            send_sem=row_send.at[kind, way, hop],
            recv_sem=row_recv.at[kind, way, hop],
            device_id={"expert": peer},
            device_id_type=MESH,
        )

    def sends(way, hop):
        step = 1 - 2 * way
        block, peer = z - step * hop, z + step
        return (block >= 0) & (block < n) & (peer >= 0) & (peer < n)

    def arrives(way, hop):
        block = z - (1 - 2 * way) * (hop + 1)
        return (block >= 0) & (block < n)

    def start(kind):
        for way in range(2):
            @pl.when(sends(way, 0))
            def _():
                row_copy(kind, way, 0, sources[kind]).start()

    def take(hop):
        for kind in range(len(held)):
            for way in range(2):
                @pl.when(arrives(way, hop))
                def _():
                    row_copy(kind, way, hop).wait_recv()

                @pl.when(sends(way, hop + 1) & (hop + 1 < n - 1))
                def _():
                    row_copy(kind, way, hop + 1).start()

    def sum_copy(kind, peer):
        return pltpu.make_async_remote_copy(
            src_ref=sums[kind].at[peer],
            dst_ref=returned[kind].at[z],
            send_sem=sum_send.at[kind, peer],
            recv_sem=sum_recv.at[kind, z],
            device_id={"expert": peer},
            device_id_type=MESH,
        )

    def came_back(kind, peer):
        return pltpu.make_async_remote_copy(
            src_ref=sums[kind].at[peer],
            dst_ref=returned[kind].at[peer],
            send_sem=sum_send.at[kind, peer],
            recv_sem=sum_recv.at[kind, peer],
            device_id={"expert": peer},
            device_id_type=MESH,
        )

    def run():
        def turn(k, carry):
            hop = lax.div(k + 1, 2) - 1
            block = z + (1 + hop) * (1 - 2 * lax.rem(k, 2))

            @pl.when(lax.rem(k, 2) == 1)
            def _():
                take(hop)

            @pl.when((block >= 0) & (block < n))
            def _():
                compute(block)

                @pl.when(block != z)
                def _():
                    for kind in range(len(sums)):
                        sum_copy(kind, block).start()

            return carry

        lax.fori_loop(0, 2 * n - 1, turn, 0)

    def finish():
        for kind in range(len(held)):
            for way in range(2):
                for hop in range(n - 1):
                    @pl.when(sends(way, hop))
                    def _():
                        row_copy(kind, way, hop).wait_send()
        for kind in range(len(sums)):
            for k in range(1, n):
                sum_copy(kind, lax.rem(z + k, n)).wait_send()

    def collect(kind, k):
        peer = lax.rem(z + k, n)
        came_back(kind, peer).wait_recv()
        return peer

    return start, run, collect, finish


def fetch_weights(layer, own, other, places, sem):
    count = places[0].shape[0]
    mine = lax.axis_index("section") == layer

    def copy(group, kind, e):
        return pltpu.make_async_copy(
            group[kind].at[e], places[kind].at[e], sem.at[kind * count + e]
        )

    for kind in range(len(places)):
        for e in range(count):
            @pl.when(mine)
            def _():
                copy(own, kind, e).start()

            @pl.when(jnp.logical_not(mine))
            def _():
                copy(other, kind, e).start()

    def wait():
        for kind in range(len(places)):
            for e in range(count):
                copy(own, kind, e).wait()

    return wait


def sigmoid_of(value):
    return 1.0 / (1.0 + jnp.exp(-value))


def column_of(block, column):
    here = lax.broadcasted_iota(jnp.int32, block.shape, 1) == column
    return jnp.sum(jnp.where(here, block, 0.0), axis=1, keepdims=True)


def experts_forward_kernel(
    layer, experts, x, mask, hidden, router, *refs
):
    own, other, refs = refs[:3], refs[3:6], refs[6:]
    out, rows, gates, gate_keep, up_keep, gated, stats = refs[:7]
    w_gate, w_up, w_down, sums, returned, mixed, total, stats_all = refs[7:15]
    weight_sem, *sems = refs[15:]
    n, held = rows.shape[0], w_gate.shape[0]
    z = lax.axis_index("expert")

    def compute(block):
        picked = rows[block]
        gate_block = gates[block]

        def one(e, carry):
            gate_pre = jnp.dot(picked, w_gate[e], preferred_element_type=jnp.float32)
            up_pre = jnp.dot(picked, w_up[e], preferred_element_type=jnp.float32)
            gate_keep[e, block] = gate_pre.astype(jnp.bfloat16)
            up_keep[e, block] = up_pre.astype(jnp.bfloat16)
            active = gate_pre * sigmoid_of(gate_pre) * up_pre
            share = (column_of(gate_block, z * held + e) * active).astype(jnp.bfloat16)
            inner = share.shape[1]
            gated[block, :, pl.ds(pl.multiple_of(e * inner, inner), inner)] = share
            mixed[e] = share
            return carry

        lax.fori_loop(0, held, one, 0)
        width = out.shape[1] // 3
        for part in range(3):
            at = pl.ds(part * width, width)
            result = jnp.zeros((out.shape[0], width), jnp.float32)
            for e in range(held):
                result += jnp.dot(mixed[e], w_down[e, :, at], preferred_element_type=jnp.float32)

            @pl.when(block == z)
            def _():
                total[:, at] = hidden[:, at] + result

            @pl.when(block != z)
            def _():
                sums[block, :, at] = result.astype(jnp.bfloat16)

    own_gates = gates.at[z]
    start, run, collect, finish = move_rows(
        ((x, own_gates, stats_all.at[z]), (rows, gates, stats_all), (sums,), (returned,), sems),
        compute,
        z,
        n,
        [],
    )
    start(0)
    wait_weights = fetch_weights(layer, own, other, (w_gate, w_up, w_down), weight_sem)
    logits = jnp.dot(x[...], router[...], preferred_element_type=jnp.float32)
    chosen = mask[...] > 0
    highest = jnp.max(jnp.where(chosen, logits, MASKED), axis=1, keepdims=True)
    exponent = jnp.where(chosen, jnp.exp(logits - highest), 0.0)
    own_gates[...] = exponent / jnp.sum(exponent, axis=1, keepdims=True)
    start(1)
    real = lax.broadcasted_iota(jnp.int32, logits.shape, 1) < experts
    highest = jnp.max(jnp.where(real, logits, MASKED), axis=1, keepdims=True)
    exponent = jnp.where(real, jnp.exp(logits - highest), 0.0)
    chance = exponent / jnp.sum(exponent, axis=1, keepdims=True)
    line = lax.broadcasted_iota(jnp.int32, stats.shape, 0)
    stats_all[z] = jnp.where(
        line == 0,
        jnp.sum(chance, axis=0, keepdims=True),
        jnp.where(line == 1, jnp.sum(mask[...], axis=0, keepdims=True), 0.0),
    )
    start(2)
    rows[z] = x[...]
    wait_weights()
    run()
    stats[...] = jnp.sum(stats_all[...], axis=0)
    for k in range(1, n):
        peer = collect(0, k)
        total[...] += returned[peer].astype(jnp.float32)
    out[...] = total[...].astype(jnp.bfloat16)
    finish()


def experts_backward_kernel(layer, grad, gates, gate_keep, up_keep, *refs):
    own, other, saved_rows, saved_gated, refs = refs[:3], refs[3:6], refs[6], refs[7], refs[8:]
    out, out_gates, rows_both, gated_both, grad_both, pre_both = refs[:6]
    w_gate, w_up, w_down, sums, sum_gates, returned, returned_gates, away = refs[6:14]
    weight_sem, core_send, core_recv, core_local, *sems = refs[14:]
    n, held = gates.shape[0], w_gate.shape[0]
    half, inner = held // 2, w_gate.shape[2]
    core = lax.axis_index("section")
    z = lax.axis_index("expert")
    turned_dims = (((1,), (1,)), ((), ()))
    rows = grad_both.at[core]

    def to_core(number, source, target):
        return pltpu.make_async_remote_copy(
            src_ref=source,
            dst_ref=target,
            send_sem=core_send.at[number],
            recv_sem=core_recv.at[number],
            device_id={"section": 1 - core},
            device_id_type=MESH,
        )

    def block_copies(block):
        return (
            to_core(2 + block, rows.at[block], rows.at[block]),
            to_core(2 + n + block, away.at[block], pre_both.at[core, block]),
        )

    def columns(at):
        return pl.ds(pl.multiple_of(at * half * inner, half * inner), half * inner)

    def whole_copies():
        return (
            to_core(0, saved_rows, rows_both.at[core]),
            to_core(1, saved_gated.at[:, :, columns(1 - core)], gated_both.at[core]),
        )

    def local_copies():
        return (
            pltpu.make_async_copy(saved_rows, rows_both.at[core], core_local.at[0]),
            pltpu.make_async_copy(
                saved_gated.at[:, :, columns(core)], gated_both.at[core], core_local.at[1]
            ),
        )

    def compute(block):
        picked = rows[block]
        gate_block = gates[block]
        sum_gates[block] = jnp.zeros(sum_gates.shape[1:], jnp.float32)

        def one(e, place, j):
            raw = lax.dot_general(
                picked, w_down[e], turned_dims, preferred_element_type=jnp.float32
            )
            gate_pre = gate_keep[e, block].astype(jnp.float32)
            up_pre = up_keep[e, block].astype(jnp.float32)
            sigmoid = sigmoid_of(gate_pre)
            silu = gate_pre * sigmoid
            column = z * held + e
            dot = jnp.sum(raw * (silu * up_pre), axis=1, keepdims=True)
            here = lax.broadcasted_iota(jnp.int32, sum_gates.shape[1:], 1) == column
            sum_gates[block] += jnp.where(here, dot, 0.0)
            active = column_of(gate_block, column) * raw
            place[:, pl.ds(pl.multiple_of(j * inner, inner), inner)] = (
                active * up_pre * sigmoid * (1.0 + gate_pre * (1.0 - sigmoid))
            ).astype(jnp.bfloat16)
            place[:, pl.ds(pl.multiple_of((half + j) * inner, inner), inner)] = (
                active * silu
            ).astype(jnp.bfloat16)

        def own_half(j, carry):
            one(core * half + j, pre_both.at[core, block], j)
            return carry

        def other_half(j, carry):
            one((1 - core) * half + j, away.at[block], j)
            return carry

        lax.fori_loop(0, half, other_half, 0)
        for copy in block_copies(block):
            copy.start()
        lax.fori_loop(0, half, own_half, 0)
        width = out.shape[1] // 3
        for part in range(3):
            at = pl.ds(part * width, width)
            result = jnp.zeros((out.shape[0], width), jnp.float32)
            for place, side in ((away.at[block], 1 - core), (pre_both.at[core, block], core)):
                for kind, right in enumerate((w_gate, w_up)):
                    for j in range(half):
                        left = place[:, pl.ds((kind * half + j) * inner, inner)]
                        result += lax.dot_general(
                            left,
                            right[side * half + j, at, :],
                            turned_dims,
                            preferred_element_type=jnp.float32,
                        )

            @pl.when(block == z)
            def _():
                out[:, at] = result

            @pl.when(block != z)
            def _():
                sums[block, :, at] = result.astype(jnp.bfloat16)

    start, run, collect, finish = move_rows(
        ((grad,), (rows,), (sums, sum_gates), (returned, returned_gates), sems),
        compute,
        z,
        n,
        [{"section": 1 - core}],
    )
    start(0)
    wait_weights = fetch_weights(layer, own, other, (w_gate, w_up, w_down), weight_sem)
    for copy in whole_copies() + local_copies():
        copy.start()
    rows[z] = grad[...]
    wait_weights()
    run()
    out_gates[...] = sum_gates[z]
    for k in range(1, n):
        peer = collect(0, k)
        out[...] += returned[peer].astype(jnp.float32)
        peer = collect(1, k)
        out_gates[...] += returned_gates[peer]
    finish()
    for copy in local_copies():
        copy.wait()
    for copy in whole_copies():
        copy.wait()
    for block in range(n):
        for copy in block_copies(block):
            copy.wait()


def exchange_scratch(n, kinds_out, kinds_back):
    return [
        pltpu.SemaphoreType.DMA((kinds_out, 2, n)),
        pltpu.SemaphoreType.DMA((kinds_out, 2, n)),
        pltpu.SemaphoreType.DMA((kinds_back, n)),
        pltpu.SemaphoreType.DMA((kinds_back, n)),
    ]


def expert_call(kernel, operands, own, other, extra, shapes, scratch, collective):
    vmem, free = pl.BlockSpec(memory_space=pltpu.VMEM), pl.BlockSpec(memory_space=pl.ANY)
    weights = [pltpu.VMEM(array.shape, jnp.bfloat16) for array in own]
    return pl.pallas_call(
        kernel,
        out_shape=shapes,
        in_specs=[vmem] * len(operands) + [free] * (6 + len(extra)),
        out_specs=[vmem] * len(shapes),
        scratch_shapes=weights + scratch,
        compiler_params=pltpu.CompilerParams(
            collective_id=collective, has_side_effects=True, vmem_limit_bytes=50 * 2**20
        ),
        cost_estimate=pl.CostEstimate(
            flops=5 * 10**10, bytes_accessed=10**8, transcendentals=0
        ),
    )(*operands, *own, *other, *extra)


def experts_forward(layer, normed_two, mask, hidden, router, own, other, experts):
    n, held = lax.axis_size("expert"), own[0].shape[0]
    length, width = normed_two.shape
    inner = own[0].shape[2]
    low, full = jnp.bfloat16, jnp.float32
    kept = jax.ShapeDtypeStruct((held, n, length, inner), low)
    shapes = [
        jax.ShapeDtypeStruct((length, width), low),
        jax.ShapeDtypeStruct((n, length, width), low),
        jax.ShapeDtypeStruct((n, length, COLUMNS), full),
        kept,
        kept,
        jax.ShapeDtypeStruct((n, length, held * inner), low),
        jax.ShapeDtypeStruct((8, COLUMNS), full),
    ]
    scratch = [
        pltpu.VMEM((n, length, width), low),
        pltpu.VMEM((n, length, width), low),
        pltpu.VMEM((held, length, inner), low),
        pltpu.VMEM((length, width), full),
        pltpu.VMEM((n, 8, COLUMNS), full),
        pltpu.SemaphoreType.DMA((3 * held,)),
    ] + exchange_scratch(n, 3, 1)
    kernel = functools.partial(experts_forward_kernel, layer, experts)
    return expert_call(
        kernel, (normed_two, mask, hidden, router), own, other, (), shapes, scratch, 1 + layer
    )


def experts_backward(layer, grad_low, gates, gate_keep, up_keep, rows, gated, own, other):
    held, n, length, inner = gate_keep.shape
    width = grad_low.shape[1]
    low, full = jnp.bfloat16, jnp.float32
    shapes = [
        jax.ShapeDtypeStruct((length, width), full),
        jax.ShapeDtypeStruct((length, COLUMNS), full),
        jax.ShapeDtypeStruct((2, n, length, width), low),
        jax.ShapeDtypeStruct((2, n, length, held // 2 * inner), low),
        jax.ShapeDtypeStruct((2, n, length, width), low),
        jax.ShapeDtypeStruct((2, n, length, held * inner), low),
    ]
    scratch = [
        pltpu.VMEM((n, length, width), low),
        pltpu.VMEM((n, length, COLUMNS), full),
        pltpu.VMEM((n, length, width), low),
        pltpu.VMEM((n, length, COLUMNS), full),
        pltpu.VMEM((n, length, held * inner), low),
        pltpu.SemaphoreType.DMA((3 * held,)),
        pltpu.SemaphoreType.DMA((2 + 2 * n,)),
        pltpu.SemaphoreType.DMA((2 + 2 * n,)),
        pltpu.SemaphoreType.DMA((2,)),
    ] + exchange_scratch(n, 1, 2)
    kernel = functools.partial(experts_backward_kernel, layer)
    return expert_call(
        kernel,
        (grad_low, gates, gate_keep, up_keep),
        own,
        other,
        (rows, gated),
        shapes,
        scratch,
        3 + layer,
    )


def attention_backward(grad_hidden, inputs, state, weights):
    gain_attn, w_query, w_key, w_value, w_out, gain_moe = weights[:6]
    (inverse_one, normed_one, queries, key_rows, values, weight, attended, hidden, inverse_two, normed_two) = state
    length = inputs.shape[0]
    grad_branch = grad_hidden.astype(jnp.bfloat16)
    grad_attended = jnp.einsum("td,cd->tc", grad_branch, w_out, preferred_element_type=jnp.float32)
    grad_attended = grad_attended.astype(jnp.bfloat16).reshape(length, KVH, H // KVH, HD)
    grad_weight = jnp.einsum(
        "qkgd,skd->kgqs", grad_attended, values, preferred_element_type=jnp.float32
    )
    grad_values = jnp.einsum(
        "kgqs,qkgd->skd",
        weight.astype(jnp.bfloat16),
        grad_attended,
        preferred_element_type=jnp.float32,
    )
    grad_values = grad_values.astype(jnp.bfloat16).reshape(length, KVH * HD)
    grad_scores = (
        weight * (grad_weight - jnp.sum(weight * grad_weight, axis=-1, keepdims=True))
    ).astype(jnp.bfloat16)
    score_scale = HD ** (-0.5)
    grouped = queries.reshape(length, KVH, H // KVH, HD)
    grad_queries = jnp.einsum(
        "kgqs,skd->qkgd", grad_scores, key_rows, preferred_element_type=jnp.float32
    )
    grad_queries = grad_queries.reshape(length, H, HD) * score_scale
    grad_keys = (
        jnp.einsum("kgqs,qkgd->skd", grad_scores, grouped, preferred_element_type=jnp.float32)
        * score_scale
    )
    cosine_table, sine_table = rotary_tables(length)
    grad_query_pre = (
        unrotate(grad_queries, cosine_table, sine_table)
        .reshape(length, H * HD)
        .astype(jnp.bfloat16)
    )
    grad_key_pre = (
        unrotate(grad_keys, cosine_table, sine_table).reshape(length, KVH * HD).astype(jnp.bfloat16)
    )
    grad_normed_one = (
        jnp.einsum("tq,cq->tc", grad_query_pre, w_query, preferred_element_type=jnp.float32)
        + jnp.einsum("tq,cq->tc", grad_key_pre, w_key, preferred_element_type=jnp.float32)
        + jnp.einsum("tq,cq->tc", grad_values, w_value, preferred_element_type=jnp.float32)
    )
    grad_norm_one, grad_gain_attn = norm_back(grad_normed_one, inputs, inverse_one, gain_attn)
    grad_inputs = grad_hidden + grad_norm_one
    grad_qkv = jnp.concatenate([grad_query_pre, grad_key_pre, grad_values], axis=1)
    return grad_inputs, grad_gain_attn, grad_qkv, grad_branch


def turned(left, right):
    return jnp.einsum("tc,tq->cq", left, right, preferred_element_type=jnp.float32)


def body(tokens, cotangent, segments, routes, *weight_arrays):
    core = lax.axis_index("section")
    first = core == 0
    experts = weight_arrays[6].shape[2]
    w_gate = weight_arrays[7]
    held = w_gate.shape[1]
    own = [array[0] for array in weight_arrays]
    other = [swapped(array) for array in own]
    weights = [
        [jnp.where(first, a, b) for a, b in zip(own[:7], other[:7])],
        [jnp.where(first, b, a) for a, b in zip(own[:7], other[:7])],
    ]
    inputs_low = lax.dynamic_slice_in_dim(tokens, core * SEQ, SEQ, 0)
    grad_low = lax.dynamic_slice_in_dim(cotangent, core * SEQ, SEQ, 0)
    segment_row = lax.dynamic_index_in_dim(segments, core, 0, keepdims=False)
    mine = lax.dynamic_slice_in_dim(routes[0], core * SEQ, SEQ, 0)
    got = swapped(lax.dynamic_slice_in_dim(routes[0], (1 - core) * SEQ, SEQ, 0))
    routes_here = jnp.stack([jnp.where(first, mine, got), jnp.where(first, got, mine)])
    masks = multi_hot(routes_here, COLUMNS)
    own_experts, other_experts = own[7:], other[7:]

    saved, outs, stats = [], [], []
    for s in range(2):
        inputs = inputs_low.astype(jnp.float32)
        state = attention_forward(inputs, weights[s], segment_row)
        hidden, normed_two = state[7], state[9]
        router = jnp.pad(weights[s][6], ((0, 0), (0, COLUMNS - experts)))
        inputs_low, *expert_state, stat = experts_forward(
            s, normed_two, masks[s], hidden, router, own_experts, other_experts, experts
        )
        outs.append(inputs_low)
        stats.append(stat)
        saved.append((inputs, state, expert_state))

    grads = [None, None]
    input_grads = [None, None]
    for s in (1, 0):
        inputs, state, expert_state = saved[s]
        (inverse_one, normed_one, _, _, _, _, attended, hidden, inverse_two, normed_two) = state
        rows_all, gates_all, gate_keep, up_keep, gated = expert_state
        gain_moe, w_router = weights[s][5], weights[s][6]
        grad_sum, grad_gates, rows_both, gated_both, grad_both, pre_both = experts_backward(
            s,
            grad_low,
            gates_all,
            gate_keep,
            up_keep,
            rows_all,
            gated,
            own_experts,
            other_experts,
        )
        inner = w_gate.shape[3]
        grad_gate_up = turned(
            rows_both.reshape(-1, D), pre_both.reshape(-1, held * inner)
        ).astype(jnp.bfloat16)
        if s == 1:
            grad_sum, grad_gate_up = lax.optimization_barrier((grad_sum, grad_gate_up))
            second_pre = lax.psum_scatter(grad_gate_up, "dp", scatter_dimension=0, tiled=True)
        else:
            grad_sum, second_pre = lax.optimization_barrier((grad_sum, second_pre))
        gates = lax.dynamic_index_in_dim(gates_all, lax.axis_index("expert"), 0, keepdims=False)
        gates, grad_gates = gates[:, :experts], grad_gates[:, :experts]
        grad_chosen = gates * (grad_gates - jnp.sum(gates * grad_gates, axis=-1, keepdims=True))
        grad_logits = grad_chosen.astype(jnp.bfloat16)
        grad_normed_two = grad_sum + jnp.einsum(
            "te,de->td", grad_logits, w_router, preferred_element_type=jnp.float32
        )
        grad_norm_two, grad_gain_moe = norm_back(grad_normed_two, hidden, inverse_two, gain_moe)
        grad_hidden = grad_low.astype(jnp.float32) + grad_norm_two
        grad_inputs, grad_gain_attn, grad_qkv, grad_branch = attention_backward(
            grad_hidden, inputs, state, weights[s]
        )
        if s == 1:
            grad_inputs, gated_both = lax.optimization_barrier((grad_inputs, gated_both))
        grad_down = turned(
            gated_both.reshape(-1, held // 2 * inner), grad_both.reshape(-1, D)
        ).astype(jnp.bfloat16)

        def halves(array):
            width = array.shape[1] // 2
            return (
                lax.dynamic_slice_in_dim(array, core * width, width, 1),
                lax.dynamic_slice_in_dim(array, (1 - core) * width, width, 1),
            )
        qkv_keep, qkv_send = halves(grad_qkv)
        branch_keep, branch_send = halves(grad_branch)
        packed = swapped(jnp.concatenate([normed_one, attended, qkv_send, branch_send], axis=1))
        normed_got, attended_got = packed[:, :D], packed[:, D : 2 * D]
        qkv_got = packed[:, 2 * D : 2 * D + qkv_send.shape[1]]
        branch_got = packed[:, 2 * D + qkv_send.shape[1] :]
        grad_w_qkv = turned(
            jnp.concatenate([normed_one, normed_got]), jnp.concatenate([qkv_keep, qkv_got])
        ).astype(jnp.bfloat16)
        grad_w_out = turned(
            jnp.concatenate([attended, attended_got]), jnp.concatenate([branch_keep, branch_got])
        ).astype(jnp.bfloat16)
        grad_w_router = turned(normed_two, grad_logits)
        small = jnp.concatenate(
            [grad_gain_attn[:, None], grad_gain_moe[:, None], grad_w_router], axis=1
        ).astype(jnp.bfloat16)
        small = jnp.pad(small, ((0, 0), (0, COLUMNS - small.shape[1])))
        if s == 1:
            axes = ("dp", "expert")
            dp = lax.axis_size("dp")
            parts = grad_down.reshape(held // 2, dp, inner // dp, D)
            parts = jnp.moveaxis(parts, 1, 0).reshape(-1, D)
            dense = jnp.concatenate([grad_w_qkv, grad_w_out, small], axis=1)
            grad_inputs, parts, dense = lax.optimization_barrier((grad_inputs, parts, dense))
            second_down = lax.psum_scatter(parts, "dp", scatter_dimension=0, tiled=True)
            second_dense = lax.psum_scatter(dense, axes, scatter_dimension=0, tiled=True)
        grads[s] = (grad_gate_up, grad_down, grad_w_qkv, grad_w_out, small)
        input_grads[s] = grad_inputs
        grad_low = grad_inputs.astype(jnp.bfloat16)

    dp, deep = lax.axis_size("dp"), lax.axis_size("expert")
    half, inner = held // 2, w_gate.shape[3]
    arrays, lanes = [], []
    grad_gate_up, grad_down, grad_w_qkv, grad_w_out, small = grads[0]
    lanes += expert_lanes(len(arrays), inner)
    arrays.append(grad_gate_up.reshape(dp, D // dp, held * inner))
    arrays.append(grad_down.reshape(half, dp, inner // dp, D))
    lanes += dense_lanes(len(arrays))
    for array in (grad_w_qkv, grad_w_out, small):
        arrays.append(array.reshape(dp, deep, array.shape[0] // (dp * deep), array.shape[1]))
    *arrays, second_down = lax.optimization_barrier((*arrays, second_down))
    *sums, stats = sum_scatter(arrays, lanes, jnp.concatenate(stats, axis=0), 0)
    stats = lax.dynamic_index_in_dim(stats.reshape(2, 8, COLUMNS), core, 0)
    token_total = SEQ * lax.axis_size(("section", "dp", "expert"))
    counts, chances = stats[:, 1, :experts], stats[:, 0, :experts]
    balance = experts * (counts / (token_total * TOPK) * chances / token_total)
    first_experts = (
        jnp.stack([sums[0], sums[2]]),
        jnp.stack([sums[1], sums[3]]),
        jnp.stack([sums[4], sums[5]]),
    )
    columns = [second_pre[:, i * inner : (i + 1) * inner] for i in range(2 * half)]
    second_experts = (
        jnp.stack(columns[:half]),
        jnp.stack(columns[half:]),
        second_down.reshape(half, inner // dp, D),
    )
    qkv, out = grads[0][2].shape[1], grads[0][3].shape[1]
    second_dense = (
        second_dense[:, :qkv], second_dense[:, qkv : qkv + out], second_dense[:, qkv + out :]
    )
    reduced = [(*first_experts, *sums[6:9]), (*second_experts, *second_dense)]
    final = []
    for a, b, dim in zip(reduced[0], reduced[1], (0, 0, 0, 1, 1, None)):
        keep = jnp.where(first, a, b)
        got = swapped(jnp.where(first, b, a))
        keep, got = keep.astype(jnp.float32), got.astype(jnp.float32)
        if dim is None:
            final.append(keep + got)
        else:
            final.append(
                jnp.concatenate(
                    [jnp.where(first, keep, got), jnp.where(first, got, keep)], axis=dim
                )
            )
    w_gate_grad, w_up_grad, w_down_grad, grad_w_qkv, grad_w_out, small = final
    heads, kv = H * HD, KVH * HD
    out_keep = jnp.where(first, outs[0], outs[1])
    out_got = swapped(jnp.where(first, outs[1], outs[0]))
    layer_out = jnp.where(
        first, jnp.concatenate([out_keep, out_got]), jnp.concatenate([out_got, out_keep])
    )
    low_one = input_grads[1].astype(jnp.bfloat16).astype(jnp.float32)
    grad_keep = jnp.where(first, input_grads[0], low_one)
    grad_got = swapped(jnp.where(first, low_one, input_grads[0]))
    input_grad = jnp.where(
        first, jnp.concatenate([grad_keep, grad_got]), jnp.concatenate([grad_got, grad_keep])
    )
    results = (
        layer_out,
        input_grad,
        small[:, 0],
        grad_w_qkv[:, :heads],
        grad_w_qkv[:, heads : heads + kv],
        grad_w_qkv[:, heads + kv :],
        grad_w_out,
        small[:, 1],
        small[:, 2 : 2 + experts],
        w_gate_grad,
        w_up_grad,
        w_down_grad,
    )
    return tuple(result[None] for result in results) + (balance,)


def solution(mesh):
    return jax.shard_map(
        body,
        mesh=mesh,
        in_specs=(
            P(("dp", "expert"), None),
            P(("dp", "expert"), None),
            P(("dp", "expert"), None),
            P("section", ("dp", "expert"), None),
            P("section", None),
            P("section", None, None),
            P("section", None, None),
            P("section", None, None),
            P("section", None, None),
            P("section", None),
            P("section", None, None),
            P("section", "expert", None, None),
            P("section", "expert", None, None),
            P("section", "expert", None, None),
        ),
        out_specs=(
            P("section", ("dp", "expert"), None),
            P("section", ("dp", "expert"), None),
            P("section", ("dp", "expert")),
            P("section", ("dp", "expert"), None),
            P("section", ("dp", "expert"), None),
            P("section", ("dp", "expert"), None),
            P("section", ("dp", "expert"), None),
            P("section", ("dp", "expert")),
            P("section", ("dp", "expert"), None),
            P("section", "expert", "dp", None),
            P("section", "expert", "dp", None),
            P("section", "expert", "dp", None),
            P("section", None),
        ),
        check_vma=False,
    )
```

```python
import functools
import itertools

import jax
import jax.numpy as jnp
from jax import lax
from jax.experimental import pallas as pl
from jax.experimental.pallas import tpu as pltpu
from jax.sharding import PartitionSpec as P

D = 1536
H = 24
KVH = 8
HD = 64
TOPK = 8
SEQ = 96


EPSILON = 1e-05
THETA = 10000.0
MASKED = -1e30


def matmul(left_side, right_side):
    return jnp.dot(left_side, right_side, preferred_element_type=jnp.float32)


def rotary_tables(length):
    half_width = HD // 2
    position = jnp.arange(length, dtype=jnp.float32)[:, None]
    freq_rate = THETA ** (-jnp.arange(half_width, dtype=jnp.float32) / half_width)
    angles = position * freq_rate[None, :]
    return (jnp.cos(angles)[:, None, :], jnp.sin(angles)[:, None, :])


def rotate(tensor, cosine_table, sine_table):
    half_width = HD // 2
    first_half = tensor[..., :half_width]
    second_half = tensor[..., half_width:]
    return jnp.concatenate(
        [
            first_half * cosine_table - second_half * sine_table,
            second_half * cosine_table + first_half * sine_table,
        ],
        axis=-1,
    )


def unrotate(gradient, cosine_table, sine_table):
    half_width = HD // 2
    first_half = gradient[..., :half_width]
    second_half = gradient[..., half_width:]
    return jnp.concatenate(
        [
            first_half * cosine_table + second_half * sine_table,
            second_half * cosine_table - first_half * sine_table,
        ],
        axis=-1,
    )


def norm_back(grad_normed, tensor, inverse, gain_vector):
    scaled = grad_normed * gain_vector
    grad_gain = jnp.sum(grad_normed * tensor * inverse, axis=0)
    grad_tensor = inverse * scaled - tensor * inverse**3 * jnp.mean(
        scaled * tensor, axis=-1, keepdims=True
    )
    return (grad_tensor, grad_gain)


def attention_scores(queries, key_rows, segment_row):
    length = queries.shape[0]
    grouped = queries.reshape(length, KVH, H // KVH, HD)
    scores = jnp.einsum(
        "qkgd,skd->kgqs", grouped, key_rows, preferred_element_type=jnp.float32
    ) * HD ** (-0.5)
    position = jnp.arange(length)
    allowed = (position[None, :] <= position[:, None]) & (
        segment_row[:, None] == segment_row[None, :]
    )
    return jnp.where(allowed[None, None], scores, MASKED)


def multi_hot(route_rows, experts):
    columns = jnp.arange(experts, dtype=jnp.int32)
    return jnp.sum(
        (route_rows[..., None] == columns).astype(jnp.float32), axis=-2
    )


def swapped(array):
    return lax.ppermute(array, "section", [(0, 1), (1, 0)])


def add_slab(total, arrived):
    *lead, rows, _ = total.shape
    step = 16 if rows % 16 == 0 else rows
    for where in itertools.product(*(range(n) for n in lead)):

        def add(i, carry):
            at = (*where, pl.ds(pl.multiple_of(i * step, step), step), slice(None))
            both = total[at].astype(jnp.float32) + arrived[at].astype(jnp.float32)
            total[at] = both.astype(jnp.bfloat16)
            return carry

        lax.fori_loop(0, rows // step, add, 0)


def sum_scatter_kernel(plan, *refs):
    lanes, ins, copies = plan
    sources = refs[:ins]
    stats_in = refs[ins]
    outs = refs[ins + 1 : ins + 1 + len(lanes)]
    stats = refs[ins + 1 + len(lanes)]
    scratch = list(refs[ins + 2 + len(lanes) :])
    send_sem, recv_sem, local_sem, stats_got, stats_send, stats_recv = scratch[-6:]
    partners = []
    for lane in lanes:
        for axis, bits in lane["phases"]:
            partners += [(axis, bit) for bit in bits if (axis, bit) not in partners]
    partners.append(("section", 0))
    index = {axis: lax.axis_index(axis) for axis, _ in partners}
    mine = {(axis, bit): (index[axis] >> bit) & 1 for axis, bit in partners}
    far = {key: index[key[0]] + (1 - 2 * mine[key]) * (1 << key[1]) for key in partners}
    barrier = pltpu.get_barrier_semaphore()
    peers = [{axis: far[axis, bit]} for axis, bit in partners if axis != "dp"]
    groups = lax.axis_size("dp")
    peers += [{"dp": lax.rem(lax.axis_index("dp") + k, groups)} for k in range(1, groups)]
    for peer in peers:
        pl.semaphore_signal(
            barrier, inc=1, device_id=peer, device_id_type=pl.DeviceIdType.MESH
        )
    pl.semaphore_wait(barrier, len(peers))

    counter = itertools.count()

    def send(source, target, key):
        number = next(counter)
        copy = pltpu.make_async_remote_copy(
            src_ref=source,
            dst_ref=target,
            send_sem=send_sem.at[number],
            recv_sem=recv_sem.at[number],
            device_id={key[0]: far[key]},
            device_id_type=pl.DeviceIdType.MESH,
        )
        copy.start()
        return copy

    def place(axis, values):
        total = 0
        for bit, value in values.items():
            total = total + value * (1 << bit)
        return total

    def sum_stats():
        count = lax.axis_size("dp")
        me = lax.axis_index("dp")

        def copy(at, source, slot, target):
            return pltpu.make_async_remote_copy(
                src_ref=source,
                dst_ref=stats_got.at[slot],
                send_sem=stats_send.at[at],
                recv_sem=stats_recv.at[slot],
                device_id=target,
                device_id_type=pl.DeviceIdType.MESH,
            )

        for k in range(1, count):
            copy(k, stats_in, me, {"dp": lax.rem(me + k, count)}).start()
        yield
        stats[...] = stats_in[...]
        for k in range(1, count):
            peer = lax.rem(me + k, count)
            copy(k, stats_in, peer, {"dp": peer}).wait_recv()
            stats[...] += stats_got[peer]
        both = copy(0, stats, count, {"section": far["section", 0]})
        both.start()
        yield
        both.wait()
        stats[...] += stats_got[count]
        for k in range(1, count):
            copy(k, stats_in, me, {"dp": lax.rem(me + k, count)}).wait_send()

    summing = sum_stats()
    next(summing)
    started = []
    states = []
    for number, lane in enumerate(lanes):
        count = len(lane["buffers"])
        buffers, scratch = scratch[:count], scratch[count:]
        source = sources[lane["source"]]
        prefix = lane["prefix"]
        if isinstance(prefix, int):
            source = source.at[prefix]

        def part(at, source=source, prefix=prefix):
            if isinstance(prefix, tuple):
                return source.at[at, :, pl.ds(*prefix)]
            if prefix == "inner":
                return source.at[:, at]
            return source.at[at]

        axis, bits = lane["phases"][0]
        total, arrived = buffers[0], buffers[1:]
        rest = [bit for bit in bits[1:]]
        pending = []
        for choice in itertools.product((0, 1), repeat=len(rest)):
            values = dict(zip(rest, choice))
            slot = sum(value << i for i, value in enumerate(choice))
            far_at = place(axis, {**values, bits[0]: 1 - mine[axis, bits[0]]})
            here_at = place(axis, {**values, bits[0]: mine[axis, bits[0]]})
            copy = send(part(far_at), arrived[0].at[slot], (axis, bits[0]))
            pending.append((copy, slot))
            started.append(copy)
            states.append((number, part(here_at), slot, total))
        lane_state = {"total": total, "arrived": arrived, "pending": pending, "rest": rest}
        lane["state"] = lane_state
    locals_ = {}
    for at, (number, here, slot, total) in enumerate(states):
        copy = pltpu.make_async_copy(here, total.at[slot], local_sem.at[at])
        copy.start()
        locals_[number, slot] = copy
    longest = max(sum(len(bits) for _, bits in lane["phases"]) for lane in lanes)
    for step in range(1, longest + 1):
        if step == 2:
            next(summing)
        for number, lane in enumerate(lanes):
            state = lane["state"]
            sizes = [len(bits) for _, bits in lane["phases"]]
            if step > sum(sizes):
                continue
            if step <= sizes[0]:
                axis, bits = lane["phases"][0]
                resolved, rest = bits[:step], bits[step:]

                def slot_of(values):
                    found = 0
                    for i, bit in enumerate(bits[1:]):
                        found = found + values.get(bit, mine[axis, bit]) * (1 << i)
                    return found

                for copy, slot in state["pending"]:
                    copy.wait_recv()
                    if step == 1:
                        locals_[number, slot].wait()
                state["pending_next"] = []
                for choice in itertools.product((0, 1), repeat=len(rest)):
                    values = dict(zip(rest, choice))
                    got = sum(value << i for i, value in enumerate(choice))
                    add_slab(
                        state["total"].at[slot_of(values)], state["arrived"][step - 1].at[got]
                    )
                if rest:
                    following = rest[1:]
                    for choice in itertools.product((0, 1), repeat=len(following)):
                        values = dict(zip(following, choice))
                        got = sum(value << i for i, value in enumerate(choice))
                        values[rest[0]] = 1 - mine[axis, rest[0]]
                        copy = send(
                            state["total"].at[slot_of(values)],
                            state["arrived"][step].at[got],
                            (axis, rest[0]),
                        )
                        state["pending_next"].append((copy, got))
                        started.append(copy)
                final = state["total"].at[slot_of({})] if not rest else None
            else:
                axis, bits = lane["phases"][1]
                done = step - sizes[0]
                rest = bits[done:]
                final = state["final"]
                for copy, _ in state["pending"]:
                    copy.wait_recv()
                state["pending_next"] = []
                for choice in itertools.product((0, 1), repeat=len(rest)):
                    values = dict(zip(rest, choice))
                    got = sum(value << i for i, value in enumerate(choice))
                    at = place(axis, {bit: values.get(bit, mine[axis, bit]) for bit in bits})
                    add_slab(final.at[at], state["arrived"][step - 1].at[got])
                if not rest:
                    at = place(axis, {bit: mine[axis, bit] for bit in bits})
                    final = final.at[at]
            if final is not None and step >= sizes[0]:
                state["final"] = final
                if step == sum(sizes):
                    outs[number][...] = final[...]
                elif step < sum(sizes):
                    axis, bits = lane["phases"][1]
                    done = step - sizes[0]
                    bit, following = bits[done], bits[done + 1 :]
                    for choice in itertools.product((0, 1), repeat=len(following)):
                        values = dict(zip(following, choice))
                        got = sum(value << i for i, value in enumerate(choice))
                        at = place(
                            axis,
                            {
                                b: values.get(b, 1 - mine[axis, b] if b == bit else mine[axis, b])
                                for b in bits
                            },
                        )
                        copy = send(final.at[at], state["arrived"][step].at[got], (axis, bit))
                        state["pending_next"].append((copy, got))
                        started.append(copy)
            state["pending"] = state["pending_next"]
    for _ in summing:
        pass
    for copy in started:
        copy.wait_send()


def sum_scatter(arrays, lanes, stats, collective):
    plans, scratch, shapes, copies, locals_ = [], [], [], 0, 0
    for source, prefix, phases in lanes:
        shape = arrays[source].shape
        if isinstance(prefix, int):
            shape = shape[1:]
        elif prefix == "inner":
            shape = (shape[1], shape[0], *shape[2:])
        elif prefix is not None:
            shape = (*shape[:-1], prefix[1])
        buffers = [(shape[0] // 2, *shape[1:])]
        for step in range(1, len(phases[0][1]) + 1):
            buffers.append((shape[0] >> step, *shape[1:]))
            copies += shape[0] >> step
        locals_ += shape[0] // 2
        if len(phases) > 1:
            for step in range(1, len(phases[1][1]) + 1):
                buffers.append((shape[1] >> step, *shape[2:]))
                copies += shape[1] >> step
        plans.append({"source": source, "prefix": prefix, "phases": phases, "buffers": buffers})
        scratch += [pltpu.VMEM(buffer, jnp.bfloat16) for buffer in buffers]
        shapes.append(jax.ShapeDtypeStruct(shape[-2:], jnp.bfloat16))
    scratch += [
        pltpu.SemaphoreType.DMA((copies,)),
        pltpu.SemaphoreType.DMA((copies,)),
        pltpu.SemaphoreType.DMA((locals_,)),
    ]
    hops = lax.axis_size("dp") + 1
    scratch += [
        pltpu.VMEM((hops, *stats.shape), jnp.float32),
        pltpu.SemaphoreType.DMA((hops,)),
        pltpu.SemaphoreType.DMA((hops,)),
    ]
    shapes.append(jax.ShapeDtypeStruct(stats.shape, jnp.float32))
    return pl.pallas_call(
        functools.partial(sum_scatter_kernel, (plans, len(arrays), copies)),
        out_shape=shapes,
        in_specs=[pl.BlockSpec(memory_space=pl.ANY)] * len(arrays)
        + [pl.BlockSpec(memory_space=pltpu.VMEM)],
        out_specs=[pl.BlockSpec(memory_space=pltpu.VMEM)] * (len(lanes) + 1),
        scratch_shapes=scratch,
        compiler_params=pltpu.CompilerParams(
            collective_id=collective, has_side_effects=True, vmem_limit_bytes=60 * 2**20
        ),
    )(*arrays, stats)


def bits_of(axis):
    return list(range(lax.axis_size(axis).bit_length() - 1))


def expert_lanes(first, inner):
    up, down = bits_of("dp"), bits_of("dp")[::-1]
    one, two = [("dp", up)], [("dp", down)]
    return [
        (first, (0, inner), one),
        (first, (2 * inner, inner), two),
        (first, (inner, inner), one),
        (first, (3 * inner, inner), two),
        (first + 1, 0, one),
        (first + 1, 1, two),
    ]


def dense_lanes(first):
    up, down, deep = bits_of("dp"), bits_of("dp")[::-1], bits_of("expert")
    return [
        (first, "inner", [("expert", deep), ("dp", up)]),
        (first + 1, None, [("dp", down), ("expert", deep)]),
        (first + 2, None, [("dp", up), ("expert", deep)]),
    ]


def attention_forward(inputs, weights, segment_row):
    gain_attn, w_query, w_key, w_value, w_out, gain_moe = weights[:6]
    length = inputs.shape[0]
    cosine_table, sine_table = rotary_tables(length)
    inverse_one = lax.rsqrt(jnp.mean(inputs * inputs, axis=-1, keepdims=True) + EPSILON)
    normed_one = (inputs * inverse_one * gain_attn).astype(jnp.bfloat16)
    queries = rotate(
        matmul(normed_one, w_query).reshape(length, H, HD), cosine_table, sine_table
    ).astype(jnp.bfloat16)
    key_rows = rotate(
        matmul(normed_one, w_key).reshape(length, KVH, HD), cosine_table, sine_table
    ).astype(jnp.bfloat16)
    values = matmul(normed_one, w_value).astype(jnp.bfloat16).reshape(length, KVH, HD)
    scores = attention_scores(queries, key_rows, segment_row)
    highest = jnp.max(scores, axis=-1, keepdims=True)
    exponent = jnp.exp(scores - highest)
    denominator = jnp.sum(exponent, axis=-1, keepdims=True)
    weight = exponent / denominator
    attended = jnp.einsum(
        "kgqs,skd->qkgd", weight.astype(jnp.bfloat16), values, preferred_element_type=jnp.float32
    )
    attended = attended.reshape(length, H * HD).astype(jnp.bfloat16)
    hidden = inputs + matmul(attended, w_out)
    inverse_two = lax.rsqrt(jnp.mean(hidden * hidden, axis=-1, keepdims=True) + EPSILON)
    normed_two = (hidden * inverse_two * gain_moe).astype(jnp.bfloat16)
    state = (inverse_one, normed_one, queries, key_rows, values, weight, attended, hidden, inverse_two, normed_two)
    return state


MESH = pl.DeviceIdType.MESH
COLUMNS = 128
PARTS = 3


def move_rows(sources, held, pieces, sems, compute, z, n, others):
    row_send, row_recv, sum_send, sum_recv = sems
    barrier = pltpu.get_barrier_semaphore()
    for k in range(1, n):
        peer = lax.rem(z + k, n)
        pl.semaphore_signal(barrier, inc=1, device_id={"expert": peer}, device_id_type=MESH)
    for peer in others:
        pl.semaphore_signal(barrier, inc=1, device_id=peer, device_id_type=MESH)
    pl.semaphore_wait(barrier, n - 1 + len(others))

    def row_copy(kind, way, hop, source=None):
        step = 1 - 2 * way
        block = jnp.clip(z - step * hop, 0, n - 1)
        peer = jnp.clip(z + step, 0, n - 1)
        return pltpu.make_async_remote_copy(
            src_ref=held[kind].at[block] if source is None else source,
            dst_ref=held[kind].at[block],
            send_sem=row_send.at[kind, way, hop],
            recv_sem=row_recv.at[kind, way, hop],
            device_id={"expert": peer},
            device_id_type=MESH,
        )

    def sends(way, hop):
        step = 1 - 2 * way
        block, peer = z - step * hop, z + step
        return (block >= 0) & (block < n) & (peer >= 0) & (peer < n)

    def arrives(way, hop):
        block = z - (1 - 2 * way) * (hop + 1)
        return (block >= 0) & (block < n)

    def start(kind):
        for way in range(2):
            @pl.when(sends(way, 0))
            def _():
                row_copy(kind, way, 0, sources[kind]).start()

    def take(hop):
        for kind in range(len(held)):
            for way in range(2):
                @pl.when(arrives(way, hop))
                def _():
                    row_copy(kind, way, hop).wait_recv()

                @pl.when(sends(way, hop + 1) & (hop + 1 < n - 1))
                def _():
                    row_copy(kind, way, hop + 1).start()

    def behind(way):
        peer = z - (1 - 2 * way)
        return (peer >= 0) & (peer < n)

    def sum_copy(way, block, p):
        mine, arrived = pieces[p]
        return pltpu.make_async_remote_copy(
            src_ref=mine(block),
            dst_ref=arrived(way, block),
            send_sem=sum_send.at[block, p],
            recv_sem=sum_recv.at[way, block, p],
            device_id={"expert": jnp.clip(z + 1 - 2 * way, 0, n - 1)},
            device_id_type=MESH,
        )

    def sent(block, p):
        way = jnp.where(block > z, 0, 1)

        @pl.when((block != z) & jnp.logical_not(behind(way)))
        def _():
            sum_copy(way, block, p).start()

    def run():
        def both(hop):
            return (hop >= 0) & (z - 1 - hop >= 0) & (z + 1 + hop < n)

        def turn(k, carry):
            hop = lax.div(k + 1, 2) - 1
            block = z + (1 + hop) * (1 - 2 * lax.rem(k, 2))
            odd = lax.rem(k, 2) == 1

            @pl.when(odd & jnp.logical_not(both(hop - 1)))
            def _():
                take(hop)

            @pl.when(jnp.logical_not(odd) & both(hop) & (hop + 1 < n - 1))
            def _():
                take(hop + 1)

            @pl.when((block >= 0) & (block < n))
            def _():
                compute(block, sent)

            return carry

        lax.fori_loop(0, 2 * n - 1, turn, 0)

        first = jnp.where(2 * z < n, 0, 1)
        for way in (first, 1 - first):
            for k in range(1, n):
                block = z + (1 - 2 * way) * k

                @pl.when(behind(way) & (block >= 0) & (block < n))
                def _():
                    for p, (mine, arrived) in enumerate(pieces):
                        sum_copy(way, block, p).wait_recv()
                        own, other = mine(block), arrived(way, block)
                        own[...] = (
                            own[...].astype(jnp.float32) + other[...].astype(jnp.float32)
                        ).astype(jnp.bfloat16)
                        sum_copy(way, block, p).start()

    def collect(add):
        for way in range(2):
            @pl.when(behind(way))
            def _():
                for p, (_, arrived) in enumerate(pieces):
                    sum_copy(way, z, p).wait_recv()
                    add(p, arrived(way, z)[...].astype(jnp.float32))

    def finish():
        for kind in range(len(held)):
            for way in range(2):
                for hop in range(n - 1):
                    @pl.when(sends(way, hop))
                    def _():
                        row_copy(kind, way, hop).wait_send()
        for k in range(1, n):
            for p in range(len(pieces)):
                sum_copy(0, lax.rem(z + k, n), p).wait_send()

    return start, run, collect, finish


def row_pieces(sums, returned, parts):
    width = sums.shape[2] // parts

    def piece(p):
        at = pl.ds(p * width, width)
        return (
            lambda block: sums.at[block, :, at],
            lambda way, block: returned.at[way, block, :, at],
        )

    return [piece(p) for p in range(parts)]


def fetch_weights(layer, own, other, places, sem):
    count = places[0].shape[0]
    mine = lax.axis_index("section") == layer

    def copy(group, kind, e):
        return pltpu.make_async_copy(
            group[kind].at[e], places[kind].at[e], sem.at[kind * count + e]
        )

    for kind in range(len(places)):
        for e in range(count):
            @pl.when(mine)
            def _():
                copy(own, kind, e).start()

            @pl.when(jnp.logical_not(mine))
            def _():
                copy(other, kind, e).start()

    def wait():
        for kind in range(len(places)):
            for e in range(count):
                copy(own, kind, e).wait()

    return wait


def sigmoid_of(value):
    return 1.0 / (1.0 + jnp.exp(-value))


def column_of(block, column):
    here = lax.broadcasted_iota(jnp.int32, block.shape, 1) == column
    return jnp.sum(jnp.where(here, block, 0.0), axis=1, keepdims=True)


def experts_forward_kernel(
    layer, experts, x, mask, hidden, router, *refs
):
    own, other, refs = refs[:3], refs[3:6], refs[6:]
    out, rows, gates_all, gates, gate_keep, up_keep, gated, stats = refs[:8]
    w_gate, w_up, w_down, sums, returned, mixed, total, stats_all = refs[8:16]
    weight_sem, *sems = refs[16:]
    n, held = rows.shape[0], w_gate.shape[0]
    z = lax.axis_index("expert")

    def compute(block, sent):
        picked = rows[block]
        gate_block = gates_all[block].astype(jnp.float32)

        def one(e, carry):
            gate_pre = jnp.dot(picked, w_gate[e], preferred_element_type=jnp.float32)
            up_pre = jnp.dot(picked, w_up[e], preferred_element_type=jnp.float32)
            gate_keep[e, block] = gate_pre.astype(jnp.bfloat16)
            up_keep[e, block] = up_pre.astype(jnp.bfloat16)
            active = gate_pre * sigmoid_of(gate_pre) * up_pre
            share = (column_of(gate_block, z * held + e) * active).astype(jnp.bfloat16)
            inner = share.shape[1]
            gated[block, :, pl.ds(pl.multiple_of(e * inner, inner), inner)] = share
            mixed[e] = share
            return carry

        lax.fori_loop(0, held, one, 0)
        width = out.shape[1] // PARTS
        for part in range(PARTS):
            at = pl.ds(part * width, width)
            result = jnp.zeros((out.shape[0], width), jnp.float32)
            for e in range(held):
                result += jnp.dot(mixed[e], w_down[e, :, at], preferred_element_type=jnp.float32)

            @pl.when(block == z)
            def _():
                total[:, at] = hidden[:, at] + result

            @pl.when(block != z)
            def _():
                sums[block, :, at] = result.astype(jnp.bfloat16)

            sent(block, part)

    own_gates = gates_all.at[z]
    start, run, collect, finish = move_rows(
        (x, own_gates, stats_all.at[z]),
        (rows, gates_all, stats_all),
        row_pieces(sums, returned, PARTS),
        sems,
        compute,
        z,
        n,
        [],
    )
    start(0)
    wait_weights = fetch_weights(layer, own, other, (w_gate, w_up, w_down), weight_sem)
    logits = jnp.dot(x[...], router[...], preferred_element_type=jnp.float32)
    chosen = mask[...] > 0
    highest = jnp.max(jnp.where(chosen, logits, MASKED), axis=1, keepdims=True)
    exponent = jnp.where(chosen, jnp.exp(logits - highest), 0.0)
    gates[...] = exponent / jnp.sum(exponent, axis=1, keepdims=True)
    own_gates[...] = gates[...].astype(jnp.bfloat16)
    start(1)
    real = lax.broadcasted_iota(jnp.int32, logits.shape, 1) < experts
    highest = jnp.max(jnp.where(real, logits, MASKED), axis=1, keepdims=True)
    exponent = jnp.where(real, jnp.exp(logits - highest), 0.0)
    chance = exponent / jnp.sum(exponent, axis=1, keepdims=True)
    line = lax.broadcasted_iota(jnp.int32, stats.shape, 0)
    stats_all[z] = jnp.where(
        line == 0,
        jnp.sum(chance, axis=0, keepdims=True),
        jnp.where(line == 1, jnp.sum(mask[...], axis=0, keepdims=True), 0.0),
    )
    start(2)
    rows[z] = x[...]
    wait_weights()
    run()
    stats[...] = jnp.sum(stats_all[...], axis=0)
    width = out.shape[1] // PARTS

    def add(p, value):
        total[:, p * width : (p + 1) * width] += value

    collect(add)
    out[...] = total[...].astype(jnp.bfloat16)
    finish()


def experts_backward_kernel(layer, grad, gates, gate_keep, up_keep, *refs):
    own, other, saved_rows, saved_gated, refs = refs[:3], refs[3:6], refs[6], refs[7], refs[8:]
    out, out_gates, rows_both, gated_both, grad_both, pre_both = refs[:6]
    w_gate, w_up, w_down, sums, sum_gates, returned, returned_gates, away, dots = refs[6:15]
    weight_sem, core_send, core_recv, core_local, *sems = refs[15:]
    n, held = gates.shape[0], w_gate.shape[0]
    half, inner = held // 2, w_gate.shape[2]
    core = lax.axis_index("section")
    z = lax.axis_index("expert")
    turned_dims = (((1,), (1,)), ((), ()))
    rows = grad_both.at[core]

    def to_core(number, source, target):
        return pltpu.make_async_remote_copy(
            src_ref=source,
            dst_ref=target,
            send_sem=core_send.at[number],
            recv_sem=core_recv.at[number],
            device_id={"section": 1 - core},
            device_id_type=MESH,
        )

    def block_copies(block):
        return (
            to_core(2 + block, rows.at[block], rows.at[block]),
            to_core(2 + n + block, away.at[block], pre_both.at[core, block]),
        )

    def columns(at):
        return pl.ds(pl.multiple_of(at * half * inner, half * inner), half * inner)

    def whole_copies():
        return (
            to_core(0, saved_rows, rows_both.at[core]),
            to_core(1, saved_gated.at[:, :, columns(1 - core)], gated_both.at[core]),
        )

    def local_copies():
        return (
            pltpu.make_async_copy(saved_rows, rows_both.at[core], core_local.at[0]),
            pltpu.make_async_copy(
                saved_gated.at[:, :, columns(core)], gated_both.at[core], core_local.at[1]
            ),
        )

    def compute(block, sent):
        picked = rows[block]
        gate_block = gates[block].astype(jnp.float32)
        dots[...] = jnp.zeros(dots.shape, jnp.float32)

        def one(e, place, j):
            raw = lax.dot_general(
                picked, w_down[e], turned_dims, preferred_element_type=jnp.float32
            )
            gate_pre = gate_keep[e, block].astype(jnp.float32)
            up_pre = up_keep[e, block].astype(jnp.float32)
            sigmoid = sigmoid_of(gate_pre)
            silu = gate_pre * sigmoid
            column = z * held + e
            dot = jnp.sum(raw * (silu * up_pre), axis=1, keepdims=True)
            here = lax.broadcasted_iota(jnp.int32, dots.shape, 1) == column
            dots[...] += jnp.where(here, dot, 0.0)
            active = column_of(gate_block, column) * raw
            place[:, pl.ds(pl.multiple_of(j * inner, inner), inner)] = (
                active * up_pre * sigmoid * (1.0 + gate_pre * (1.0 - sigmoid))
            ).astype(jnp.bfloat16)
            place[:, pl.ds(pl.multiple_of((half + j) * inner, inner), inner)] = (
                active * silu
            ).astype(jnp.bfloat16)

        def own_half(j, carry):
            one(core * half + j, pre_both.at[core, block], j)
            return carry

        def other_half(j, carry):
            one((1 - core) * half + j, away.at[block], j)
            return carry

        lax.fori_loop(0, half, other_half, 0)
        for copy in block_copies(block):
            copy.start()
        lax.fori_loop(0, half, own_half, 0)
        sum_gates[block] = dots[...].astype(jnp.bfloat16)

        @pl.when(block == z)
        def _():
            out_gates[...] = dots[...]

        sent(block, PARTS)
        width = out.shape[1] // PARTS
        for part in range(PARTS):
            at = pl.ds(part * width, width)
            result = jnp.zeros((out.shape[0], width), jnp.float32)
            for place, side in ((away.at[block], 1 - core), (pre_both.at[core, block], core)):
                for kind, right in enumerate((w_gate, w_up)):
                    for j in range(half):
                        left = place[:, pl.ds((kind * half + j) * inner, inner)]
                        result += lax.dot_general(
                            left,
                            right[side * half + j, at, :],
                            turned_dims,
                            preferred_element_type=jnp.float32,
                        )

            @pl.when(block == z)
            def _():
                out[:, at] = result

            @pl.when(block != z)
            def _():
                sums[block, :, at] = result.astype(jnp.bfloat16)

            sent(block, part)

    gate_piece = (lambda block: sum_gates.at[block], lambda way, block: returned_gates.at[way, block])
    start, run, collect, finish = move_rows(
        (grad,),
        (rows,),
        row_pieces(sums, returned, PARTS) + [gate_piece],
        sems,
        compute,
        z,
        n,
        [{"section": 1 - core}],
    )
    start(0)
    wait_weights = fetch_weights(layer, own, other, (w_gate, w_up, w_down), weight_sem)
    for copy in whole_copies() + local_copies():
        copy.start()
    rows[z] = grad[...]
    wait_weights()
    run()
    width = out.shape[1] // PARTS

    def add(p, value):
        if p == PARTS:
            out_gates[...] += value
        else:
            out[:, p * width : (p + 1) * width] += value

    collect(add)
    finish()
    for copy in local_copies():
        copy.wait()
    for copy in whole_copies():
        copy.wait()
    for block in range(n):
        for copy in block_copies(block):
            copy.wait()


def exchange_scratch(n, kinds_out, kinds_back):
    return [
        pltpu.SemaphoreType.DMA((kinds_out, 2, n)),
        pltpu.SemaphoreType.DMA((kinds_out, 2, n)),
        pltpu.SemaphoreType.DMA((n, kinds_back)),
        pltpu.SemaphoreType.DMA((2, n, kinds_back)),
    ]


def expert_call(kernel, operands, own, other, extra, shapes, scratch, collective):
    vmem, free = pl.BlockSpec(memory_space=pltpu.VMEM), pl.BlockSpec(memory_space=pl.ANY)
    weights = [pltpu.VMEM(array.shape, jnp.bfloat16) for array in own]
    return pl.pallas_call(
        kernel,
        out_shape=shapes,
        in_specs=[vmem] * len(operands) + [free] * (6 + len(extra)),
        out_specs=[vmem] * len(shapes),
        scratch_shapes=weights + scratch,
        compiler_params=pltpu.CompilerParams(
            collective_id=collective, has_side_effects=True, vmem_limit_bytes=50 * 2**20
        ),
        cost_estimate=pl.CostEstimate(
            flops=5 * 10**10, bytes_accessed=10**8, transcendentals=0
        ),
    )(*operands, *own, *other, *extra)


def experts_forward(layer, normed_two, mask, hidden, router, own, other, experts):
    n, held = lax.axis_size("expert"), own[0].shape[0]
    length, width = normed_two.shape
    inner = own[0].shape[2]
    low, full = jnp.bfloat16, jnp.float32
    kept = jax.ShapeDtypeStruct((held, n, length, inner), low)
    shapes = [
        jax.ShapeDtypeStruct((length, width), low),
        jax.ShapeDtypeStruct((n, length, width), low),
        jax.ShapeDtypeStruct((n, length, COLUMNS), low),
        jax.ShapeDtypeStruct((length, COLUMNS), full),
        kept,
        kept,
        jax.ShapeDtypeStruct((n, length, held * inner), low),
        jax.ShapeDtypeStruct((8, COLUMNS), full),
    ]
    scratch = [
        pltpu.VMEM((n, length, width), low),
        pltpu.VMEM((2, n, length, width), low),
        pltpu.VMEM((held, length, inner), low),
        pltpu.VMEM((length, width), full),
        pltpu.VMEM((n, 8, COLUMNS), full),
        pltpu.SemaphoreType.DMA((3 * held,)),
    ] + exchange_scratch(n, 3, PARTS)
    kernel = functools.partial(experts_forward_kernel, layer, experts)
    return expert_call(
        kernel, (normed_two, mask, hidden, router), own, other, (), shapes, scratch, 1 + layer
    )


def experts_backward(layer, grad_low, gates, gate_keep, up_keep, rows, gated, own, other):
    held, n, length, inner = gate_keep.shape
    width = grad_low.shape[1]
    low, full = jnp.bfloat16, jnp.float32
    shapes = [
        jax.ShapeDtypeStruct((length, width), full),
        jax.ShapeDtypeStruct((length, COLUMNS), full),
        jax.ShapeDtypeStruct((2, n, length, width), low),
        jax.ShapeDtypeStruct((2, n, length, held // 2 * inner), low),
        jax.ShapeDtypeStruct((2, n, length, width), low),
        jax.ShapeDtypeStruct((2, n, length, held * inner), low),
    ]
    scratch = [
        pltpu.VMEM((n, length, width), low),
        pltpu.VMEM((n, length, COLUMNS), low),
        pltpu.VMEM((2, n, length, width), low),
        pltpu.VMEM((2, n, length, COLUMNS), low),
        pltpu.VMEM((n, length, held * inner), low),
        pltpu.VMEM((length, COLUMNS), full),
        pltpu.SemaphoreType.DMA((3 * held,)),
        pltpu.SemaphoreType.DMA((2 + 2 * n,)),
        pltpu.SemaphoreType.DMA((2 + 2 * n,)),
        pltpu.SemaphoreType.DMA((2,)),
    ] + exchange_scratch(n, 1, PARTS + 1)
    kernel = functools.partial(experts_backward_kernel, layer)
    return expert_call(
        kernel,
        (grad_low, gates, gate_keep, up_keep),
        own,
        other,
        (rows, gated),
        shapes,
        scratch,
        3 + layer,
    )


def attention_backward(grad_hidden, inputs, state, weights):
    gain_attn, w_query, w_key, w_value, w_out, gain_moe = weights[:6]
    (inverse_one, normed_one, queries, key_rows, values, weight, attended, hidden, inverse_two, normed_two) = state
    length = inputs.shape[0]
    grad_branch = grad_hidden.astype(jnp.bfloat16)
    grad_attended = jnp.einsum("td,cd->tc", grad_branch, w_out, preferred_element_type=jnp.float32)
    grad_attended = grad_attended.astype(jnp.bfloat16).reshape(length, KVH, H // KVH, HD)
    grad_weight = jnp.einsum(
        "qkgd,skd->kgqs", grad_attended, values, preferred_element_type=jnp.float32
    )
    grad_values = jnp.einsum(
        "kgqs,qkgd->skd",
        weight.astype(jnp.bfloat16),
        grad_attended,
        preferred_element_type=jnp.float32,
    )
    grad_values = grad_values.astype(jnp.bfloat16).reshape(length, KVH * HD)
    grad_scores = (
        weight * (grad_weight - jnp.sum(weight * grad_weight, axis=-1, keepdims=True))
    ).astype(jnp.bfloat16)
    score_scale = HD ** (-0.5)
    grouped = queries.reshape(length, KVH, H // KVH, HD)
    grad_queries = jnp.einsum(
        "kgqs,skd->qkgd", grad_scores, key_rows, preferred_element_type=jnp.float32
    )
    grad_queries = grad_queries.reshape(length, H, HD) * score_scale
    grad_keys = (
        jnp.einsum("kgqs,qkgd->skd", grad_scores, grouped, preferred_element_type=jnp.float32)
        * score_scale
    )
    cosine_table, sine_table = rotary_tables(length)
    grad_query_pre = (
        unrotate(grad_queries, cosine_table, sine_table)
        .reshape(length, H * HD)
        .astype(jnp.bfloat16)
    )
    grad_key_pre = (
        unrotate(grad_keys, cosine_table, sine_table).reshape(length, KVH * HD).astype(jnp.bfloat16)
    )
    grad_normed_one = (
        jnp.einsum("tq,cq->tc", grad_query_pre, w_query, preferred_element_type=jnp.float32)
        + jnp.einsum("tq,cq->tc", grad_key_pre, w_key, preferred_element_type=jnp.float32)
        + jnp.einsum("tq,cq->tc", grad_values, w_value, preferred_element_type=jnp.float32)
    )
    grad_norm_one, grad_gain_attn = norm_back(grad_normed_one, inputs, inverse_one, gain_attn)
    grad_inputs = grad_hidden + grad_norm_one
    grad_qkv = jnp.concatenate([grad_query_pre, grad_key_pre, grad_values], axis=1)
    return grad_inputs, grad_gain_attn, grad_qkv, grad_branch


def turned(left, right):
    return jnp.einsum("tc,tq->cq", left, right, preferred_element_type=jnp.float32)


def body(tokens, cotangent, segments, routes, *weight_arrays):
    core = lax.axis_index("section")
    first = core == 0
    experts = weight_arrays[6].shape[2]
    w_gate = weight_arrays[7]
    held = w_gate.shape[1]
    own = [array[0] for array in weight_arrays]
    other = [swapped(array) for array in own]
    weights = [
        [jnp.where(first, a, b) for a, b in zip(own[:7], other[:7])],
        [jnp.where(first, b, a) for a, b in zip(own[:7], other[:7])],
    ]
    inputs_low = lax.dynamic_slice_in_dim(tokens, core * SEQ, SEQ, 0)
    grad_low = lax.dynamic_slice_in_dim(cotangent, core * SEQ, SEQ, 0)
    segment_row = lax.dynamic_index_in_dim(segments, core, 0, keepdims=False)
    mine = lax.dynamic_slice_in_dim(routes[0], core * SEQ, SEQ, 0)
    got = swapped(lax.dynamic_slice_in_dim(routes[0], (1 - core) * SEQ, SEQ, 0))
    routes_here = jnp.stack([jnp.where(first, mine, got), jnp.where(first, got, mine)])
    masks = multi_hot(routes_here, COLUMNS)
    own_experts, other_experts = own[7:], other[7:]

    saved, outs, stats = [], [], []
    for s in range(2):
        inputs = inputs_low.astype(jnp.float32)
        state = attention_forward(inputs, weights[s], segment_row)
        hidden, normed_two = state[7], state[9]
        router = jnp.pad(weights[s][6], ((0, 0), (0, COLUMNS - experts)))
        inputs_low, *expert_state, stat = experts_forward(
            s, normed_two, masks[s], hidden, router, own_experts, other_experts, experts
        )
        outs.append(inputs_low)
        stats.append(stat)
        saved.append((inputs, state, expert_state))

    grads = [None, None]
    input_grads = [None, None]
    for s in (1, 0):
        inputs, state, expert_state = saved[s]
        (inverse_one, normed_one, _, _, _, _, attended, hidden, inverse_two, normed_two) = state
        rows_all, gates_all, gates, gate_keep, up_keep, gated = expert_state
        gain_moe, w_router = weights[s][5], weights[s][6]
        grad_sum, grad_gates, rows_both, gated_both, grad_both, pre_both = experts_backward(
            s,
            grad_low,
            gates_all,
            gate_keep,
            up_keep,
            rows_all,
            gated,
            own_experts,
            other_experts,
        )
        inner = w_gate.shape[3]
        grad_gate_up = turned(
            rows_both.reshape(-1, D), pre_both.reshape(-1, held * inner)
        ).astype(jnp.bfloat16)
        if s == 1:
            grad_sum, grad_gate_up = lax.optimization_barrier((grad_sum, grad_gate_up))
            second_pre = lax.psum_scatter(grad_gate_up, "dp", scatter_dimension=0, tiled=True)
        else:
            grad_sum, second_pre = lax.optimization_barrier((grad_sum, second_pre))
        gates, grad_gates = gates[:, :experts], grad_gates[:, :experts]
        grad_chosen = gates * (grad_gates - jnp.sum(gates * grad_gates, axis=-1, keepdims=True))
        grad_logits = grad_chosen.astype(jnp.bfloat16)
        grad_normed_two = grad_sum + jnp.einsum(
            "te,de->td", grad_logits, w_router, preferred_element_type=jnp.float32
        )
        grad_norm_two, grad_gain_moe = norm_back(grad_normed_two, hidden, inverse_two, gain_moe)
        grad_hidden = grad_low.astype(jnp.float32) + grad_norm_two
        grad_inputs, grad_gain_attn, grad_qkv, grad_branch = attention_backward(
            grad_hidden, inputs, state, weights[s]
        )
        if s == 1:
            grad_inputs, gated_both = lax.optimization_barrier((grad_inputs, gated_both))
        grad_down = turned(
            gated_both.reshape(-1, held // 2 * inner), grad_both.reshape(-1, D)
        ).astype(jnp.bfloat16)

        def halves(array):
            width = array.shape[1] // 2
            return (
                lax.dynamic_slice_in_dim(array, core * width, width, 1),
                lax.dynamic_slice_in_dim(array, (1 - core) * width, width, 1),
            )
        qkv_keep, qkv_send = halves(grad_qkv)
        branch_keep, branch_send = halves(grad_branch)
        packed = swapped(jnp.concatenate([normed_one, attended, qkv_send, branch_send], axis=1))
        normed_got, attended_got = packed[:, :D], packed[:, D : 2 * D]
        qkv_got = packed[:, 2 * D : 2 * D + qkv_send.shape[1]]
        branch_got = packed[:, 2 * D + qkv_send.shape[1] :]
        grad_w_qkv = turned(
            jnp.concatenate([normed_one, normed_got]), jnp.concatenate([qkv_keep, qkv_got])
        ).astype(jnp.bfloat16)
        grad_w_out = turned(
            jnp.concatenate([attended, attended_got]), jnp.concatenate([branch_keep, branch_got])
        ).astype(jnp.bfloat16)
        grad_w_router = turned(normed_two, grad_logits)
        small = jnp.concatenate(
            [grad_gain_attn[:, None], grad_gain_moe[:, None], grad_w_router], axis=1
        ).astype(jnp.bfloat16)
        small = jnp.pad(small, ((0, 0), (0, COLUMNS - small.shape[1])))
        if s == 1:
            dp = lax.axis_size("dp")
            parts = grad_down.reshape(held // 2, dp, inner // dp, D)
            parts = jnp.moveaxis(parts, 1, 0).reshape(-1, D)
            dense = jnp.concatenate([grad_w_qkv, grad_w_out, small], axis=1)
            grad_inputs, parts, dense = lax.optimization_barrier((grad_inputs, parts, dense))
            second_dense = lax.psum_scatter(dense, "dp", scatter_dimension=0, tiled=True)
            second_down = lax.psum_scatter(parts, "dp", scatter_dimension=0, tiled=True)
        grads[s] = (grad_gate_up, grad_down, grad_w_qkv, grad_w_out, small)
        input_grads[s] = grad_inputs
        grad_low = grad_inputs.astype(jnp.bfloat16)

    dp, deep = lax.axis_size("dp"), lax.axis_size("expert")
    half, inner = held // 2, w_gate.shape[3]
    arrays, lanes = [], []
    grad_gate_up, grad_down, grad_w_qkv, grad_w_out, small = grads[0]
    lanes += expert_lanes(len(arrays), inner)
    arrays.append(grad_gate_up.reshape(dp, D // dp, held * inner))
    arrays.append(grad_down.reshape(half, dp, inner // dp, D))
    lanes += dense_lanes(len(arrays))
    for array in (grad_w_qkv, grad_w_out, small):
        arrays.append(array.reshape(dp, deep, array.shape[0] // (dp * deep), array.shape[1]))
    lanes.append((len(arrays), None, [("expert", bits_of("expert"))]))
    rows_each = second_dense.shape[0] // deep
    arrays.append(second_dense.reshape(deep, rows_each, second_dense.shape[1]))
    *sums, stats = sum_scatter(arrays, lanes, jnp.concatenate(stats, axis=0), 0)
    stats = lax.dynamic_index_in_dim(stats.reshape(2, 8, COLUMNS), core, 0)
    token_total = SEQ * lax.axis_size(("section", "dp", "expert"))
    counts, chances = stats[:, 1, :experts], stats[:, 0, :experts]
    balance = experts * (counts / (token_total * TOPK) * chances / token_total)
    first_experts = (
        jnp.stack([sums[0], sums[2]]),
        jnp.stack([sums[1], sums[3]]),
        jnp.stack([sums[4], sums[5]]),
    )
    columns = [second_pre[:, i * inner : (i + 1) * inner] for i in range(2 * half)]
    second_experts = (
        jnp.stack(columns[:half]),
        jnp.stack(columns[half:]),
        second_down.reshape(half, inner // dp, D),
    )
    qkv, out = grads[0][2].shape[1], grads[0][3].shape[1]
    second_dense = sums[9]
    second_dense = (
        second_dense[:, :qkv], second_dense[:, qkv : qkv + out], second_dense[:, qkv + out :]
    )
    reduced = [(*first_experts, *sums[6:9]), (*second_experts, *second_dense)]
    final = []
    for a, b, dim in zip(reduced[0], reduced[1], (0, 0, 0, 1, 1, None)):
        keep = jnp.where(first, a, b)
        got = swapped(jnp.where(first, b, a))
        keep, got = keep.astype(jnp.float32), got.astype(jnp.float32)
        if dim is None:
            final.append(keep + got)
        else:
            final.append(
                jnp.concatenate(
                    [jnp.where(first, keep, got), jnp.where(first, got, keep)], axis=dim
                )
            )
    w_gate_grad, w_up_grad, w_down_grad, grad_w_qkv, grad_w_out, small = final
    heads, kv = H * HD, KVH * HD
    out_keep = jnp.where(first, outs[0], outs[1])
    out_got = swapped(jnp.where(first, outs[1], outs[0]))
    layer_out = jnp.where(
        first, jnp.concatenate([out_keep, out_got]), jnp.concatenate([out_got, out_keep])
    )
    low_one = input_grads[1].astype(jnp.bfloat16).astype(jnp.float32)
    grad_keep = jnp.where(first, input_grads[0], low_one)
    grad_got = swapped(jnp.where(first, low_one, input_grads[0]))
    input_grad = jnp.where(
        first, jnp.concatenate([grad_keep, grad_got]), jnp.concatenate([grad_got, grad_keep])
    )
    results = (
        layer_out,
        input_grad,
        small[:, 0],
        grad_w_qkv[:, :heads],
        grad_w_qkv[:, heads : heads + kv],
        grad_w_qkv[:, heads + kv :],
        grad_w_out,
        small[:, 1],
        small[:, 2 : 2 + experts],
        w_gate_grad,
        w_up_grad,
        w_down_grad,
    )
    return tuple(result[None] for result in results) + (balance,)


def solution(mesh):
    return jax.shard_map(
        body,
        mesh=mesh,
        in_specs=(
            P(("dp", "expert"), None),
            P(("dp", "expert"), None),
            P(("dp", "expert"), None),
            P("section", ("dp", "expert"), None),
            P("section", None),
            P("section", None, None),
            P("section", None, None),
            P("section", None, None),
            P("section", None, None),
            P("section", None),
            P("section", None, None),
            P("section", "expert", None, None),
            P("section", "expert", None, None),
            P("section", "expert", None, None),
        ),
        out_specs=(
            P("section", ("dp", "expert"), None),
            P("section", ("dp", "expert"), None),
            P("section", ("dp", "expert")),
            P("section", ("dp", "expert"), None),
            P("section", ("dp", "expert"), None),
            P("section", ("dp", "expert"), None),
            P("section", ("dp", "expert"), None),
            P("section", ("dp", "expert")),
            P("section", ("dp", "expert"), None),
            P("section", "expert", "dp", None),
            P("section", "expert", "dp", None),
            P("section", "expert", "dp", None),
            P("section", None),
        ),
        check_vma=False,
    )
```

```python
import functools
import itertools

import jax
import jax.numpy as jnp
from jax import lax
from jax.experimental import pallas as pl
from jax.experimental.pallas import tpu as pltpu
from jax.sharding import PartitionSpec as P

D = 1536
H = 24
KVH = 8
HD = 64
TOPK = 8
SEQ = 96


EPSILON = 1e-05
THETA = 10000.0
MASKED = -1e30


def matmul(left_side, right_side):
    return jnp.dot(left_side, right_side, preferred_element_type=jnp.float32)


def rotary_tables(length):
    half_width = HD // 2
    position = jnp.arange(length, dtype=jnp.float32)[:, None]
    freq_rate = THETA ** (-jnp.arange(half_width, dtype=jnp.float32) / half_width)
    angles = position * freq_rate[None, :]
    return (jnp.cos(angles)[:, None, :], jnp.sin(angles)[:, None, :])


def rotate(tensor, cosine_table, sine_table):
    half_width = HD // 2
    first_half = tensor[..., :half_width]
    second_half = tensor[..., half_width:]
    return jnp.concatenate(
        [
            first_half * cosine_table - second_half * sine_table,
            second_half * cosine_table + first_half * sine_table,
        ],
        axis=-1,
    )


def unrotate(gradient, cosine_table, sine_table):
    half_width = HD // 2
    first_half = gradient[..., :half_width]
    second_half = gradient[..., half_width:]
    return jnp.concatenate(
        [
            first_half * cosine_table + second_half * sine_table,
            second_half * cosine_table - first_half * sine_table,
        ],
        axis=-1,
    )


def norm_back(grad_normed, tensor, inverse, gain_vector):
    scaled = grad_normed * gain_vector
    grad_gain = jnp.sum(grad_normed * tensor * inverse, axis=0)
    grad_tensor = inverse * scaled - tensor * inverse**3 * jnp.mean(
        scaled * tensor, axis=-1, keepdims=True
    )
    return (grad_tensor, grad_gain)


def attention_scores(queries, key_rows, segment_row):
    length = queries.shape[0]
    grouped = queries.reshape(length, KVH, H // KVH, HD)
    scores = jnp.einsum(
        "qkgd,skd->kgqs", grouped, key_rows, preferred_element_type=jnp.float32
    ) * HD ** (-0.5)
    position = jnp.arange(length)
    allowed = (position[None, :] <= position[:, None]) & (
        segment_row[:, None] == segment_row[None, :]
    )
    return jnp.where(allowed[None, None], scores, MASKED)


def multi_hot(route_rows, experts):
    columns = jnp.arange(experts, dtype=jnp.int32)
    return jnp.sum(
        (route_rows[..., None] == columns).astype(jnp.float32), axis=-2
    )


def swapped(array):
    return lax.ppermute(array, "section", [(0, 1), (1, 0)])


def add_slab(total, arrived):
    *lead, rows, _ = total.shape
    step = 16 if rows % 16 == 0 else rows
    for where in itertools.product(*(range(n) for n in lead)):

        def add(i, carry):
            at = (*where, pl.ds(pl.multiple_of(i * step, step), step), slice(None))
            both = total[at].astype(jnp.float32) + arrived[at].astype(jnp.float32)
            total[at] = both.astype(jnp.bfloat16)
            return carry

        lax.fori_loop(0, rows // step, add, 0)


def sum_scatter_kernel(plan, *refs):
    lanes, ins, copies = plan
    sources = refs[:ins]
    stats_in = refs[ins]
    outs = refs[ins + 1 : ins + 1 + len(lanes)]
    stats = refs[ins + 1 + len(lanes)]
    scratch = list(refs[ins + 2 + len(lanes) :])
    send_sem, recv_sem, local_sem, stats_got, stats_send, stats_recv = scratch[-6:]
    partners = []
    for lane in lanes:
        for axis, bits in lane["phases"]:
            partners += [(axis, bit) for bit in bits if (axis, bit) not in partners]
    partners.append(("section", 0))
    index = {axis: lax.axis_index(axis) for axis, _ in partners}
    mine = {(axis, bit): (index[axis] >> bit) & 1 for axis, bit in partners}
    far = {key: index[key[0]] + (1 - 2 * mine[key]) * (1 << key[1]) for key in partners}
    barrier = pltpu.get_barrier_semaphore()
    peers = [{axis: far[axis, bit]} for axis, bit in partners if axis != "dp"]
    groups = lax.axis_size("dp")
    peers += [{"dp": lax.rem(lax.axis_index("dp") + k, groups)} for k in range(1, groups)]
    for peer in peers:
        pl.semaphore_signal(
            barrier, inc=1, device_id=peer, device_id_type=pl.DeviceIdType.MESH
        )
    pl.semaphore_wait(barrier, len(peers))

    counter = itertools.count()

    def send(source, target, key):
        number = next(counter)
        copy = pltpu.make_async_remote_copy(
            src_ref=source,
            dst_ref=target,
            send_sem=send_sem.at[number],
            recv_sem=recv_sem.at[number],
            device_id={key[0]: far[key]},
            device_id_type=pl.DeviceIdType.MESH,
        )
        copy.start()
        return copy

    def place(axis, values):
        total = 0
        for bit, value in values.items():
            total = total + value * (1 << bit)
        return total

    def sum_stats():
        count = lax.axis_size("dp")
        me = lax.axis_index("dp")

        def copy(at, source, slot, target):
            return pltpu.make_async_remote_copy(
                src_ref=source,
                dst_ref=stats_got.at[slot],
                send_sem=stats_send.at[at],
                recv_sem=stats_recv.at[slot],
                device_id=target,
                device_id_type=pl.DeviceIdType.MESH,
            )

        for k in range(1, count):
            copy(k, stats_in, me, {"dp": lax.rem(me + k, count)}).start()
        yield
        stats[...] = stats_in[...]
        for k in range(1, count):
            peer = lax.rem(me + k, count)
            copy(k, stats_in, peer, {"dp": peer}).wait_recv()
            stats[...] += stats_got[peer]
        both = copy(0, stats, count, {"section": far["section", 0]})
        both.start()
        yield
        both.wait()
        stats[...] += stats_got[count]
        for k in range(1, count):
            copy(k, stats_in, me, {"dp": lax.rem(me + k, count)}).wait_send()

    summing = sum_stats()
    next(summing)
    started = []
    states = []
    for number, lane in enumerate(lanes):
        count = len(lane["buffers"])
        buffers, scratch = scratch[:count], scratch[count:]
        source = sources[lane["source"]]
        prefix = lane["prefix"]
        if isinstance(prefix, int):
            source = source.at[prefix]

        def part(at, source=source, prefix=prefix):
            if isinstance(prefix, tuple):
                return source.at[at, :, pl.ds(*prefix)]
            if prefix == "inner":
                return source.at[:, at]
            return source.at[at]

        axis, bits = lane["phases"][0]
        total, arrived = buffers[0], buffers[1:]
        rest = [bit for bit in bits[1:]]
        pending = []
        for choice in itertools.product((0, 1), repeat=len(rest)):
            values = dict(zip(rest, choice))
            slot = sum(value << i for i, value in enumerate(choice))
            far_at = place(axis, {**values, bits[0]: 1 - mine[axis, bits[0]]})
            here_at = place(axis, {**values, bits[0]: mine[axis, bits[0]]})
            copy = send(part(far_at), arrived[0].at[slot], (axis, bits[0]))
            pending.append((copy, slot))
            started.append(copy)
            states.append((number, part(here_at), slot, total))
        lane_state = {"total": total, "arrived": arrived, "pending": pending, "rest": rest}
        lane["state"] = lane_state
    locals_ = {}
    for at, (number, here, slot, total) in enumerate(states):
        copy = pltpu.make_async_copy(here, total.at[slot], local_sem.at[at])
        copy.start()
        locals_[number, slot] = copy
    longest = max(sum(len(bits) for _, bits in lane["phases"]) for lane in lanes)
    for step in range(1, longest + 1):
        if step == 2:
            next(summing)
        for number, lane in enumerate(lanes):
            state = lane["state"]
            sizes = [len(bits) for _, bits in lane["phases"]]
            if step > sum(sizes):
                continue
            if step <= sizes[0]:
                axis, bits = lane["phases"][0]
                resolved, rest = bits[:step], bits[step:]

                def slot_of(values):
                    found = 0
                    for i, bit in enumerate(bits[1:]):
                        found = found + values.get(bit, mine[axis, bit]) * (1 << i)
                    return found

                for copy, slot in state["pending"]:
                    copy.wait_recv()
                    if step == 1:
                        locals_[number, slot].wait()
                state["pending_next"] = []
                for choice in itertools.product((0, 1), repeat=len(rest)):
                    values = dict(zip(rest, choice))
                    got = sum(value << i for i, value in enumerate(choice))
                    add_slab(
                        state["total"].at[slot_of(values)], state["arrived"][step - 1].at[got]
                    )
                if rest:
                    following = rest[1:]
                    for choice in itertools.product((0, 1), repeat=len(following)):
                        values = dict(zip(following, choice))
                        got = sum(value << i for i, value in enumerate(choice))
                        values[rest[0]] = 1 - mine[axis, rest[0]]
                        copy = send(
                            state["total"].at[slot_of(values)],
                            state["arrived"][step].at[got],
                            (axis, rest[0]),
                        )
                        state["pending_next"].append((copy, got))
                        started.append(copy)
                final = state["total"].at[slot_of({})] if not rest else None
            else:
                axis, bits = lane["phases"][1]
                done = step - sizes[0]
                rest = bits[done:]
                final = state["final"]
                for copy, _ in state["pending"]:
                    copy.wait_recv()
                state["pending_next"] = []
                for choice in itertools.product((0, 1), repeat=len(rest)):
                    values = dict(zip(rest, choice))
                    got = sum(value << i for i, value in enumerate(choice))
                    at = place(axis, {bit: values.get(bit, mine[axis, bit]) for bit in bits})
                    add_slab(final.at[at], state["arrived"][step - 1].at[got])
                if not rest:
                    at = place(axis, {bit: mine[axis, bit] for bit in bits})
                    final = final.at[at]
            if final is not None and step >= sizes[0]:
                state["final"] = final
                if step == sum(sizes):
                    outs[number][...] = final[...]
                elif step < sum(sizes):
                    axis, bits = lane["phases"][1]
                    done = step - sizes[0]
                    bit, following = bits[done], bits[done + 1 :]
                    for choice in itertools.product((0, 1), repeat=len(following)):
                        values = dict(zip(following, choice))
                        got = sum(value << i for i, value in enumerate(choice))
                        at = place(
                            axis,
                            {
                                b: values.get(b, 1 - mine[axis, b] if b == bit else mine[axis, b])
                                for b in bits
                            },
                        )
                        copy = send(final.at[at], state["arrived"][step].at[got], (axis, bit))
                        state["pending_next"].append((copy, got))
                        started.append(copy)
            state["pending"] = state["pending_next"]
    for _ in summing:
        pass
    for copy in started:
        copy.wait_send()


def sum_scatter(arrays, lanes, stats, collective):
    plans, scratch, shapes, copies, locals_ = [], [], [], 0, 0
    for source, prefix, phases in lanes:
        shape = arrays[source].shape
        if isinstance(prefix, int):
            shape = shape[1:]
        elif prefix == "inner":
            shape = (shape[1], shape[0], *shape[2:])
        elif prefix is not None:
            shape = (*shape[:-1], prefix[1])
        buffers = [(shape[0] // 2, *shape[1:])]
        for step in range(1, len(phases[0][1]) + 1):
            buffers.append((shape[0] >> step, *shape[1:]))
            copies += shape[0] >> step
        locals_ += shape[0] // 2
        if len(phases) > 1:
            for step in range(1, len(phases[1][1]) + 1):
                buffers.append((shape[1] >> step, *shape[2:]))
                copies += shape[1] >> step
        plans.append({"source": source, "prefix": prefix, "phases": phases, "buffers": buffers})
        scratch += [pltpu.VMEM(buffer, jnp.bfloat16) for buffer in buffers]
        shapes.append(jax.ShapeDtypeStruct(shape[-2:], jnp.bfloat16))
    scratch += [
        pltpu.SemaphoreType.DMA((copies,)),
        pltpu.SemaphoreType.DMA((copies,)),
        pltpu.SemaphoreType.DMA((locals_,)),
    ]
    hops = lax.axis_size("dp") + 1
    scratch += [
        pltpu.VMEM((hops, *stats.shape), jnp.float32),
        pltpu.SemaphoreType.DMA((hops,)),
        pltpu.SemaphoreType.DMA((hops,)),
    ]
    shapes.append(jax.ShapeDtypeStruct(stats.shape, jnp.float32))
    return pl.pallas_call(
        functools.partial(sum_scatter_kernel, (plans, len(arrays), copies)),
        out_shape=shapes,
        in_specs=[pl.BlockSpec(memory_space=pl.ANY)] * len(arrays)
        + [pl.BlockSpec(memory_space=pltpu.VMEM)],
        out_specs=[pl.BlockSpec(memory_space=pltpu.VMEM)] * (len(lanes) + 1),
        scratch_shapes=scratch,
        compiler_params=pltpu.CompilerParams(
            collective_id=collective, has_side_effects=True, vmem_limit_bytes=60 * 2**20
        ),
    )(*arrays, stats)


def bits_of(axis):
    return list(range(lax.axis_size(axis).bit_length() - 1))


def expert_lanes(first, inner):
    up, down = bits_of("dp"), bits_of("dp")[::-1]
    one, two = [("dp", up)], [("dp", down)]
    return [
        (first, (0, inner), one),
        (first, (2 * inner, inner), two),
        (first, (inner, inner), one),
        (first, (3 * inner, inner), two),
        (first + 1, 0, one),
        (first + 1, 1, two),
    ]


def dense_lanes(first):
    up, down, deep = bits_of("dp"), bits_of("dp")[::-1], bits_of("expert")
    return [
        (first, "inner", [("expert", deep), ("dp", up)]),
        (first + 1, None, [("dp", down), ("expert", deep)]),
        (first + 2, None, [("dp", up), ("expert", deep)]),
    ]


def attention_forward(inputs, weights, segment_row):
    gain_attn, w_query, w_key, w_value, w_out, gain_moe = weights[:6]
    length = inputs.shape[0]
    cosine_table, sine_table = rotary_tables(length)
    inverse_one = lax.rsqrt(jnp.mean(inputs * inputs, axis=-1, keepdims=True) + EPSILON)
    normed_one = (inputs * inverse_one * gain_attn).astype(jnp.bfloat16)
    queries = rotate(
        matmul(normed_one, w_query).reshape(length, H, HD), cosine_table, sine_table
    ).astype(jnp.bfloat16)
    key_rows = rotate(
        matmul(normed_one, w_key).reshape(length, KVH, HD), cosine_table, sine_table
    ).astype(jnp.bfloat16)
    values = matmul(normed_one, w_value).astype(jnp.bfloat16).reshape(length, KVH, HD)
    scores = attention_scores(queries, key_rows, segment_row)
    highest = jnp.max(scores, axis=-1, keepdims=True)
    exponent = jnp.exp(scores - highest)
    denominator = jnp.sum(exponent, axis=-1, keepdims=True)
    weight = exponent / denominator
    attended = jnp.einsum(
        "kgqs,skd->qkgd", weight.astype(jnp.bfloat16), values, preferred_element_type=jnp.float32
    )
    attended = attended.reshape(length, H * HD).astype(jnp.bfloat16)
    hidden = inputs + matmul(attended, w_out)
    inverse_two = lax.rsqrt(jnp.mean(hidden * hidden, axis=-1, keepdims=True) + EPSILON)
    normed_two = (hidden * inverse_two * gain_moe).astype(jnp.bfloat16)
    state = (inverse_one, normed_one, queries, key_rows, values, weight, attended, hidden, inverse_two, normed_two)
    return state


MESH = pl.DeviceIdType.MESH
COLUMNS = 128
PARTS = 3


def move_rows(sources, held, pieces, sems, compute, z, n, others):
    row_send, row_recv, sum_send, sum_recv = sems
    barrier = pltpu.get_barrier_semaphore()
    for k in range(1, n):
        peer = lax.rem(z + k, n)
        pl.semaphore_signal(barrier, inc=1, device_id={"expert": peer}, device_id_type=MESH)
    for peer in others:
        pl.semaphore_signal(barrier, inc=1, device_id=peer, device_id_type=MESH)
    pl.semaphore_wait(barrier, n - 1 + len(others))

    def row_copy(kind, way, hop, source=None):
        step = 1 - 2 * way
        block = jnp.clip(z - step * hop, 0, n - 1)
        peer = jnp.clip(z + step, 0, n - 1)
        return pltpu.make_async_remote_copy(
            src_ref=held[kind].at[block] if source is None else source,
            dst_ref=held[kind].at[block],
            send_sem=row_send.at[kind, way, hop],
            recv_sem=row_recv.at[kind, way, hop],
            device_id={"expert": peer},
            device_id_type=MESH,
        )

    def sends(way, hop):
        step = 1 - 2 * way
        block, peer = z - step * hop, z + step
        return (block >= 0) & (block < n) & (peer >= 0) & (peer < n)

    def arrives(way, hop):
        block = z - (1 - 2 * way) * (hop + 1)
        return (block >= 0) & (block < n)

    def start(kind):
        for way in range(2):
            @pl.when(sends(way, 0))
            def _():
                row_copy(kind, way, 0, sources[kind]).start()

    def take(hop):
        for kind in range(len(held)):
            for way in range(2):
                @pl.when(arrives(way, hop))
                def _():
                    row_copy(kind, way, hop).wait_recv()

                @pl.when(sends(way, hop + 1) & (hop + 1 < n - 1))
                def _():
                    row_copy(kind, way, hop + 1).start()

    def behind(way):
        peer = z - (1 - 2 * way)
        return (peer >= 0) & (peer < n)

    def sum_copy(way, block, p):
        mine, arrived = pieces[p]
        return pltpu.make_async_remote_copy(
            src_ref=mine(block),
            dst_ref=arrived(way, block),
            send_sem=sum_send.at[block, p],
            recv_sem=sum_recv.at[way, block, p],
            device_id={"expert": jnp.clip(z + 1 - 2 * way, 0, n - 1)},
            device_id_type=MESH,
        )

    def sent(block, p):
        way = jnp.where(block > z, 0, 1)

        @pl.when((block != z) & jnp.logical_not(behind(way)))
        def _():
            sum_copy(way, block, p).start()

    def run():
        inward = jnp.where(2 * z < n, 1, -1)
        outer = (z - inward >= 0) & (z - inward < n)
        take(0)
        compute(z, z + inward, True, sent)
        for hop in range(1, n - 1):
            take(hop)
        compute(
            jnp.where(outer, z - inward, z + 2 * inward),
            jnp.where(outer, z + 2 * inward, z + 3 * inward),
            False,
            sent,
        )

        first = jnp.where(2 * z < n, 0, 1)
        for way in (first, 1 - first):
            for k in range(1, n):
                block = z + (1 - 2 * way) * k

                @pl.when(behind(way) & (block >= 0) & (block < n))
                def _():
                    for p, (mine, arrived) in enumerate(pieces):
                        sum_copy(way, block, p).wait_recv()
                        own, other = mine(block), arrived(way, block)
                        own[...] = (
                            own[...].astype(jnp.float32) + other[...].astype(jnp.float32)
                        ).astype(jnp.bfloat16)
                        sum_copy(way, block, p).start()

    def collect(add):
        for way in range(2):
            @pl.when(behind(way))
            def _():
                for p, (_, arrived) in enumerate(pieces):
                    sum_copy(way, z, p).wait_recv()
                    add(p, arrived(way, z)[...].astype(jnp.float32))

    def finish():
        for kind in range(len(held)):
            for way in range(2):
                for hop in range(n - 1):
                    @pl.when(sends(way, hop))
                    def _():
                        row_copy(kind, way, hop).wait_send()
        for k in range(1, n):
            for p in range(len(pieces)):
                sum_copy(0, lax.rem(z + k, n), p).wait_send()

    return start, run, collect, finish


def row_pieces(sums, returned, parts):
    width = sums.shape[2] // parts

    def piece(p):
        at = pl.ds(p * width, width)
        return (
            lambda block: sums.at[block, :, at],
            lambda way, block: returned.at[way, block, :, at],
        )

    return [piece(p) for p in range(parts)]


def fetch_weights(layer, own, other, places, sem, order):
    count = places[0].shape[0]
    mine = lax.axis_index("section") == layer

    def copy(group, kind, e):
        return pltpu.make_async_copy(
            group[kind].at[e], places[kind].at[e], sem.at[kind * count + e]
        )

    for kinds in order:
        for e, kind in itertools.product(range(count), kinds):
            @pl.when(mine)
            def _():
                copy(own, kind, e).start()

            @pl.when(jnp.logical_not(mine))
            def _():
                copy(other, kind, e).start()

    def wait(kind, e):
        copy(own, kind, e).wait()

    return wait


def sigmoid_of(value):
    return 1.0 / (1.0 + jnp.exp(-value))


def column_of(block, column):
    here = lax.broadcasted_iota(jnp.int32, block.shape, 1) == column
    return jnp.sum(jnp.where(here, block, 0.0), axis=1, keepdims=True)


def experts_forward_kernel(
    layer, experts, x, mask, hidden, router, *refs
):
    own, other, refs = refs[:3], refs[3:6], refs[6:]
    out, rows, gates_all, gates, gate_keep, up_keep, gated, stats = refs[:8]
    w_gate, w_up, w_down, sums, returned, mixed, stacked, total, stats_all = refs[8:17]
    weight_sem, *sems = refs[17:]
    n, held = rows.shape[0], w_gate.shape[0]
    z = lax.axis_index("expert")

    length = x.shape[0]

    def compute(a, b, first, sent):
        stacked[:length] = rows[a]
        stacked[length:] = rows[b]
        gate_block = jnp.concatenate([gates_all[a], gates_all[b]], axis=0).astype(jnp.float32)

        def one(e, carry):
            if first:
                wait_weight(0, e)
                wait_weight(1, e)
            gate_pre = jnp.dot(stacked[...], w_gate[e], preferred_element_type=jnp.float32)
            up_pre = jnp.dot(stacked[...], w_up[e], preferred_element_type=jnp.float32)
            active = gate_pre * sigmoid_of(gate_pre) * up_pre
            share = (column_of(gate_block, z * held + e) * active).astype(jnp.bfloat16)
            mixed[e] = share
            inner = share.shape[1]
            at = pl.ds(pl.multiple_of(e * inner, inner), inner)
            for block, half in ((a, slice(0, length)), (b, slice(length, 2 * length))):
                gate_keep[e, block] = gate_pre[half].astype(jnp.bfloat16)
                up_keep[e, block] = up_pre[half].astype(jnp.bfloat16)
                gated[block, :, at] = share[half]
            return carry

        lax.fori_loop(0, held, one, 0)
        if first:
            for e in range(held):
                wait_weight(2, e)
        width = out.shape[1] // PARTS
        for part in range(PARTS):
            at = pl.ds(part * width, width)
            result = jnp.zeros((2 * length, width), jnp.float32)
            for e in range(held):
                result += jnp.dot(mixed[e], w_down[e, :, at], preferred_element_type=jnp.float32)
            sums[b, :, at] = result[length:].astype(jnp.bfloat16)
            sent(b, part)
            if first:
                total[:, at] = hidden[:, at] + result[:length]
            else:
                sums[a, :, at] = result[:length].astype(jnp.bfloat16)
                sent(a, part)

    own_gates = gates_all.at[z]
    start, run, collect, finish = move_rows(
        (x, own_gates, stats_all.at[z]),
        (rows, gates_all, stats_all),
        row_pieces(sums, returned, PARTS),
        sems,
        compute,
        z,
        n,
        [],
    )
    start(0)
    wait_weight = fetch_weights(
        layer, own, other, (w_gate, w_up, w_down), weight_sem, ((0, 1), (2,))
    )
    logits = jnp.dot(x[...], router[...], preferred_element_type=jnp.float32)
    chosen = mask[...] > 0
    highest = jnp.max(jnp.where(chosen, logits, MASKED), axis=1, keepdims=True)
    exponent = jnp.where(chosen, jnp.exp(logits - highest), 0.0)
    gates[...] = exponent / jnp.sum(exponent, axis=1, keepdims=True)
    own_gates[...] = gates[...].astype(jnp.bfloat16)
    start(1)
    real = lax.broadcasted_iota(jnp.int32, logits.shape, 1) < experts
    highest = jnp.max(jnp.where(real, logits, MASKED), axis=1, keepdims=True)
    exponent = jnp.where(real, jnp.exp(logits - highest), 0.0)
    chance = exponent / jnp.sum(exponent, axis=1, keepdims=True)
    line = lax.broadcasted_iota(jnp.int32, stats.shape, 0)
    stats_all[z] = jnp.where(
        line == 0,
        jnp.sum(chance, axis=0, keepdims=True),
        jnp.where(line == 1, jnp.sum(mask[...], axis=0, keepdims=True), 0.0),
    )
    start(2)
    rows[z] = x[...]
    run()
    stats[...] = jnp.sum(stats_all[...], axis=0)
    width = out.shape[1] // PARTS

    def add(p, value):
        total[:, p * width : (p + 1) * width] += value

    collect(add)
    out[...] = total[...].astype(jnp.bfloat16)
    finish()


def experts_backward_kernel(layer, grad, gates, gate_keep, up_keep, *refs):
    own, other, saved_rows, saved_gated, refs = refs[:3], refs[3:6], refs[6], refs[7], refs[8:]
    out, out_gates, rows_both, gated_both, grad_both, pre_both = refs[:6]
    w_gate, w_up, w_down, sums, sum_gates, returned, returned_gates, away, dots = refs[6:15]
    mixed, stacked, weight_sem, core_send, core_recv, core_local, *sems = refs[15:]
    n, held = gates.shape[0], w_gate.shape[0]
    half, inner = held // 2, w_gate.shape[2]
    core = lax.axis_index("section")
    z = lax.axis_index("expert")
    turned_dims = (((1,), (1,)), ((), ()))
    rows = grad_both.at[core]

    def to_core(number, source, target):
        return pltpu.make_async_remote_copy(
            src_ref=source,
            dst_ref=target,
            send_sem=core_send.at[number],
            recv_sem=core_recv.at[number],
            device_id={"section": 1 - core},
            device_id_type=MESH,
        )

    def block_copies(block):
        return (
            to_core(2 + block, rows.at[block], rows.at[block]),
            to_core(2 + n + block, away.at[block], pre_both.at[core, block]),
        )

    def columns(at):
        return pl.ds(pl.multiple_of(at * half * inner, half * inner), half * inner)

    def whole_copies():
        return (
            to_core(0, saved_rows, rows_both.at[core]),
            to_core(1, saved_gated.at[:, :, columns(1 - core)], gated_both.at[core]),
        )

    def local_copies():
        return (
            pltpu.make_async_copy(saved_rows, rows_both.at[core], core_local.at[0]),
            pltpu.make_async_copy(
                saved_gated.at[:, :, columns(core)], gated_both.at[core], core_local.at[1]
            ),
        )

    length = grad.shape[0]

    def compute(a, b, first, sent):
        stacked[:length] = rows[a]
        stacked[length:] = rows[b]
        gate_block = jnp.concatenate([gates[a], gates[b]], axis=0).astype(jnp.float32)
        dots[...] = jnp.zeros(dots.shape, jnp.float32)
        spans = ((a, slice(0, length)), (b, slice(length, 2 * length)))

        def both(ref, e):
            return jnp.concatenate([ref[e, a], ref[e, b]], axis=0).astype(jnp.float32)

        def one(e, place, j):
            if first:
                wait_weight(2, e)
            raw = lax.dot_general(
                stacked[...], w_down[e], turned_dims, preferred_element_type=jnp.float32
            )
            gate_pre, up_pre = both(gate_keep, e), both(up_keep, e)
            sigmoid = sigmoid_of(gate_pre)
            silu = gate_pre * sigmoid
            column = z * held + e
            dot = jnp.sum(raw * (silu * up_pre), axis=1, keepdims=True)
            here = lax.broadcasted_iota(jnp.int32, dots.shape, 1) == column
            dots[...] += jnp.where(here, dot, 0.0)
            active = column_of(gate_block, column) * raw
            grads = (
                (active * up_pre * sigmoid * (1.0 + gate_pre * (1.0 - sigmoid))).astype(
                    jnp.bfloat16
                ),
                (active * silu).astype(jnp.bfloat16),
            )
            for kind, value in enumerate(grads):
                mixed[kind, e] = value
                at = pl.ds(pl.multiple_of((kind * half + j) * inner, inner), inner)
                for block, span in spans:
                    place(block)[:, at] = value[span]

        def own_half(j, carry):
            one(core * half + j, lambda block: pre_both.at[core, block], j)
            return carry

        def other_half(j, carry):
            one((1 - core) * half + j, lambda block: away.at[block], j)
            return carry

        lax.fori_loop(0, half, other_half, 0)
        for block in (a, b):
            for copy in block_copies(block):
                copy.start()
        lax.fori_loop(0, half, own_half, 0)
        sum_gates[b] = dots[length:].astype(jnp.bfloat16)
        sent(b, PARTS)
        if first:
            out_gates[...] = dots[:length]
            for e in range(held):
                wait_weight(0, e)
                wait_weight(1, e)
        else:
            sum_gates[a] = dots[:length].astype(jnp.bfloat16)
            sent(a, PARTS)
        width = out.shape[1] // PARTS
        for part in range(PARTS):
            at = pl.ds(part * width, width)
            result = jnp.zeros((2 * length, width), jnp.float32)
            for kind, right in enumerate((w_gate, w_up)):
                for e in range(held):
                    result += lax.dot_general(
                        mixed[kind, e],
                        right[e, at, :],
                        turned_dims,
                        preferred_element_type=jnp.float32,
                    )
            sums[b, :, at] = result[length:].astype(jnp.bfloat16)
            sent(b, part)
            if first:
                out[:, at] = result[:length]
            else:
                sums[a, :, at] = result[:length].astype(jnp.bfloat16)
                sent(a, part)

    gate_piece = (lambda block: sum_gates.at[block], lambda way, block: returned_gates.at[way, block])
    start, run, collect, finish = move_rows(
        (grad,),
        (rows,),
        row_pieces(sums, returned, PARTS) + [gate_piece],
        sems,
        compute,
        z,
        n,
        [{"section": 1 - core}],
    )
    start(0)
    wait_weight = fetch_weights(
        layer, own, other, (w_gate, w_up, w_down), weight_sem, ((2,), (0, 1))
    )
    for copy in whole_copies() + local_copies():
        copy.start()
    rows[z] = grad[...]
    run()
    width = out.shape[1] // PARTS

    def add(p, value):
        if p == PARTS:
            out_gates[...] += value
        else:
            out[:, p * width : (p + 1) * width] += value

    collect(add)
    finish()
    for copy in local_copies():
        copy.wait()
    for copy in whole_copies():
        copy.wait()
    for block in range(n):
        for copy in block_copies(block):
            copy.wait()


def exchange_scratch(n, kinds_out, kinds_back):
    return [
        pltpu.SemaphoreType.DMA((kinds_out, 2, n)),
        pltpu.SemaphoreType.DMA((kinds_out, 2, n)),
        pltpu.SemaphoreType.DMA((n, kinds_back)),
        pltpu.SemaphoreType.DMA((2, n, kinds_back)),
    ]


def expert_call(kernel, operands, own, other, extra, shapes, scratch, collective):
    vmem, free = pl.BlockSpec(memory_space=pltpu.VMEM), pl.BlockSpec(memory_space=pl.ANY)
    weights = [pltpu.VMEM(array.shape, jnp.bfloat16) for array in own]
    return pl.pallas_call(
        kernel,
        out_shape=shapes,
        in_specs=[vmem] * len(operands) + [free] * (6 + len(extra)),
        out_specs=[vmem] * len(shapes),
        scratch_shapes=weights + scratch,
        compiler_params=pltpu.CompilerParams(
            collective_id=collective, has_side_effects=True, vmem_limit_bytes=50 * 2**20
        ),
        cost_estimate=pl.CostEstimate(
            flops=5 * 10**10, bytes_accessed=10**8, transcendentals=0
        ),
    )(*operands, *own, *other, *extra)


def experts_forward(layer, normed_two, mask, hidden, router, own, other, experts):
    n, held = lax.axis_size("expert"), own[0].shape[0]
    length, width = normed_two.shape
    inner = own[0].shape[2]
    low, full = jnp.bfloat16, jnp.float32
    kept = jax.ShapeDtypeStruct((held, n, length, inner), low)
    shapes = [
        jax.ShapeDtypeStruct((length, width), low),
        jax.ShapeDtypeStruct((n, length, width), low),
        jax.ShapeDtypeStruct((n, length, COLUMNS), low),
        jax.ShapeDtypeStruct((length, COLUMNS), full),
        kept,
        kept,
        jax.ShapeDtypeStruct((n, length, held * inner), low),
        jax.ShapeDtypeStruct((8, COLUMNS), full),
    ]
    scratch = [
        pltpu.VMEM((n, length, width), low),
        pltpu.VMEM((2, n, length, width), low),
        pltpu.VMEM((held, 2 * length, inner), low),
        pltpu.VMEM((2 * length, width), low),
        pltpu.VMEM((length, width), full),
        pltpu.VMEM((n, 8, COLUMNS), full),
        pltpu.SemaphoreType.DMA((3 * held,)),
    ] + exchange_scratch(n, 3, PARTS)
    kernel = functools.partial(experts_forward_kernel, layer, experts)
    return expert_call(
        kernel, (normed_two, mask, hidden, router), own, other, (), shapes, scratch, 1 + layer
    )


def experts_backward(layer, grad_low, gates, gate_keep, up_keep, rows, gated, own, other):
    held, n, length, inner = gate_keep.shape
    width = grad_low.shape[1]
    low, full = jnp.bfloat16, jnp.float32
    shapes = [
        jax.ShapeDtypeStruct((length, width), full),
        jax.ShapeDtypeStruct((length, COLUMNS), full),
        jax.ShapeDtypeStruct((2, n, length, width), low),
        jax.ShapeDtypeStruct((2, n, length, held // 2 * inner), low),
        jax.ShapeDtypeStruct((2, n, length, width), low),
        jax.ShapeDtypeStruct((2, n, length, held * inner), low),
    ]
    scratch = [
        pltpu.VMEM((n, length, width), low),
        pltpu.VMEM((n, length, COLUMNS), low),
        pltpu.VMEM((2, n, length, width), low),
        pltpu.VMEM((2, n, length, COLUMNS), low),
        pltpu.VMEM((n, length, held * inner), low),
        pltpu.VMEM((2 * length, COLUMNS), full),
        pltpu.VMEM((2, held, 2 * length, inner), low),
        pltpu.VMEM((2 * length, width), low),
        pltpu.SemaphoreType.DMA((3 * held,)),
        pltpu.SemaphoreType.DMA((2 + 2 * n,)),
        pltpu.SemaphoreType.DMA((2 + 2 * n,)),
        pltpu.SemaphoreType.DMA((2,)),
    ] + exchange_scratch(n, 1, PARTS + 1)
    kernel = functools.partial(experts_backward_kernel, layer)
    return expert_call(
        kernel,
        (grad_low, gates, gate_keep, up_keep),
        own,
        other,
        (rows, gated),
        shapes,
        scratch,
        3 + layer,
    )


def attention_backward(grad_hidden, inputs, state, weights):
    gain_attn, w_query, w_key, w_value, w_out, gain_moe = weights[:6]
    (inverse_one, normed_one, queries, key_rows, values, weight, attended, hidden, inverse_two, normed_two) = state
    length = inputs.shape[0]
    grad_branch = grad_hidden.astype(jnp.bfloat16)
    grad_attended = jnp.einsum("td,cd->tc", grad_branch, w_out, preferred_element_type=jnp.float32)
    grad_attended = grad_attended.astype(jnp.bfloat16).reshape(length, KVH, H // KVH, HD)
    grad_weight = jnp.einsum(
        "qkgd,skd->kgqs", grad_attended, values, preferred_element_type=jnp.float32
    )
    grad_values = jnp.einsum(
        "kgqs,qkgd->skd",
        weight.astype(jnp.bfloat16),
        grad_attended,
        preferred_element_type=jnp.float32,
    )
    grad_values = grad_values.astype(jnp.bfloat16).reshape(length, KVH * HD)
    grad_scores = (
        weight * (grad_weight - jnp.sum(weight * grad_weight, axis=-1, keepdims=True))
    ).astype(jnp.bfloat16)
    score_scale = HD ** (-0.5)
    grouped = queries.reshape(length, KVH, H // KVH, HD)
    grad_queries = jnp.einsum(
        "kgqs,skd->qkgd", grad_scores, key_rows, preferred_element_type=jnp.float32
    )
    grad_queries = grad_queries.reshape(length, H, HD) * score_scale
    grad_keys = (
        jnp.einsum("kgqs,qkgd->skd", grad_scores, grouped, preferred_element_type=jnp.float32)
        * score_scale
    )
    cosine_table, sine_table = rotary_tables(length)
    grad_query_pre = (
        unrotate(grad_queries, cosine_table, sine_table)
        .reshape(length, H * HD)
        .astype(jnp.bfloat16)
    )
    grad_key_pre = (
        unrotate(grad_keys, cosine_table, sine_table).reshape(length, KVH * HD).astype(jnp.bfloat16)
    )
    grad_normed_one = (
        jnp.einsum("tq,cq->tc", grad_query_pre, w_query, preferred_element_type=jnp.float32)
        + jnp.einsum("tq,cq->tc", grad_key_pre, w_key, preferred_element_type=jnp.float32)
        + jnp.einsum("tq,cq->tc", grad_values, w_value, preferred_element_type=jnp.float32)
    )
    grad_norm_one, grad_gain_attn = norm_back(grad_normed_one, inputs, inverse_one, gain_attn)
    grad_inputs = grad_hidden + grad_norm_one
    grad_qkv = jnp.concatenate([grad_query_pre, grad_key_pre, grad_values], axis=1)
    return grad_inputs, grad_gain_attn, grad_qkv, grad_branch


def turned(left, right):
    return jnp.einsum("tc,tq->cq", left, right, preferred_element_type=jnp.float32)


def body(tokens, cotangent, segments, routes, *weight_arrays):
    core = lax.axis_index("section")
    first = core == 0
    experts = weight_arrays[6].shape[2]
    w_gate = weight_arrays[7]
    held = w_gate.shape[1]
    own = [array[0] for array in weight_arrays]
    other = [swapped(array) for array in own]
    weights = [
        [jnp.where(first, a, b) for a, b in zip(own[:7], other[:7])],
        [jnp.where(first, b, a) for a, b in zip(own[:7], other[:7])],
    ]
    inputs_low = lax.dynamic_slice_in_dim(tokens, core * SEQ, SEQ, 0)
    grad_low = lax.dynamic_slice_in_dim(cotangent, core * SEQ, SEQ, 0)
    segment_row = lax.dynamic_index_in_dim(segments, core, 0, keepdims=False)
    mine = lax.dynamic_slice_in_dim(routes[0], core * SEQ, SEQ, 0)
    got = swapped(lax.dynamic_slice_in_dim(routes[0], (1 - core) * SEQ, SEQ, 0))
    routes_here = jnp.stack([jnp.where(first, mine, got), jnp.where(first, got, mine)])
    masks = multi_hot(routes_here, COLUMNS)
    own_experts, other_experts = own[7:], other[7:]

    saved, outs, stats = [], [], []
    for s in range(2):
        inputs = inputs_low.astype(jnp.float32)
        state = attention_forward(inputs, weights[s], segment_row)
        hidden, normed_two = state[7], state[9]
        router = jnp.pad(weights[s][6], ((0, 0), (0, COLUMNS - experts)))
        inputs_low, *expert_state, stat = experts_forward(
            s, normed_two, masks[s], hidden, router, own_experts, other_experts, experts
        )
        outs.append(inputs_low)
        stats.append(stat)
        saved.append((inputs, state, expert_state))

    grads = [None, None]
    input_grads = [None, None]
    for s in (1, 0):
        inputs, state, expert_state = saved[s]
        (inverse_one, normed_one, _, _, _, _, attended, hidden, inverse_two, normed_two) = state
        rows_all, gates_all, gates, gate_keep, up_keep, gated = expert_state
        gain_moe, w_router = weights[s][5], weights[s][6]
        grad_sum, grad_gates, rows_both, gated_both, grad_both, pre_both = experts_backward(
            s,
            grad_low,
            gates_all,
            gate_keep,
            up_keep,
            rows_all,
            gated,
            own_experts,
            other_experts,
        )
        inner = w_gate.shape[3]
        grad_gate_up = turned(
            rows_both.reshape(-1, D), pre_both.reshape(-1, held * inner)
        ).astype(jnp.bfloat16)
        grad_down = turned(
            gated_both.reshape(-1, held // 2 * inner), grad_both.reshape(-1, D)
        ).astype(jnp.bfloat16)
        if s == 1:
            dp = lax.axis_size("dp")
            parts = grad_down.reshape(held // 2, dp, inner // dp, D)
            parts = jnp.moveaxis(parts, 1, 0).reshape(-1, D)
            grad_sum, grad_gate_up, parts = lax.optimization_barrier(
                (grad_sum, grad_gate_up, parts)
            )
            second_pre = lax.psum_scatter(grad_gate_up, "dp", scatter_dimension=0, tiled=True)
            second_down = lax.psum_scatter(parts, "dp", scatter_dimension=0, tiled=True)
        else:
            grad_sum, second_pre = lax.optimization_barrier((grad_sum, second_pre))
        gates, grad_gates = gates[:, :experts], grad_gates[:, :experts]
        grad_chosen = gates * (grad_gates - jnp.sum(gates * grad_gates, axis=-1, keepdims=True))
        grad_logits = grad_chosen.astype(jnp.bfloat16)
        grad_normed_two = grad_sum + jnp.einsum(
            "te,de->td", grad_logits, w_router, preferred_element_type=jnp.float32
        )
        grad_norm_two, grad_gain_moe = norm_back(grad_normed_two, hidden, inverse_two, gain_moe)
        grad_hidden = grad_low.astype(jnp.float32) + grad_norm_two
        grad_inputs, grad_gain_attn, grad_qkv, grad_branch = attention_backward(
            grad_hidden, inputs, state, weights[s]
        )
        def halves(array):
            width = array.shape[1] // 2
            return (
                lax.dynamic_slice_in_dim(array, core * width, width, 1),
                lax.dynamic_slice_in_dim(array, (1 - core) * width, width, 1),
            )
        qkv_keep, qkv_send = halves(grad_qkv)
        branch_keep, branch_send = halves(grad_branch)
        packed = swapped(jnp.concatenate([normed_one, attended, qkv_send, branch_send], axis=1))
        normed_got, attended_got = packed[:, :D], packed[:, D : 2 * D]
        qkv_got = packed[:, 2 * D : 2 * D + qkv_send.shape[1]]
        branch_got = packed[:, 2 * D + qkv_send.shape[1] :]
        grad_w_qkv = turned(
            jnp.concatenate([normed_one, normed_got]), jnp.concatenate([qkv_keep, qkv_got])
        ).astype(jnp.bfloat16)
        grad_w_out = turned(
            jnp.concatenate([attended, attended_got]), jnp.concatenate([branch_keep, branch_got])
        ).astype(jnp.bfloat16)
        grad_w_router = turned(normed_two, grad_logits)
        small = jnp.concatenate(
            [grad_gain_attn[:, None], grad_gain_moe[:, None], grad_w_router], axis=1
        ).astype(jnp.bfloat16)
        small = jnp.pad(small, ((0, 0), (0, COLUMNS - small.shape[1])))
        if s == 1:
            grad_inputs, grad_w_qkv, grad_w_out = lax.optimization_barrier(
                (grad_inputs, grad_w_qkv, grad_w_out)
            )
            second_qkv = lax.psum_scatter(grad_w_qkv, "dp", scatter_dimension=0, tiled=True)
            second_out = lax.psum_scatter(grad_w_out, "dp", scatter_dimension=0, tiled=True)
        else:
            grad_w_qkv, second_down = lax.optimization_barrier((grad_w_qkv, second_down))
        grads[s] = (grad_gate_up, grad_down, grad_w_qkv, grad_w_out, small)
        input_grads[s] = grad_inputs
        grad_low = grad_inputs.astype(jnp.bfloat16)

    dp, deep = lax.axis_size("dp"), lax.axis_size("expert")
    half, inner = held // 2, w_gate.shape[3]
    arrays, lanes = [], []
    grad_gate_up, grad_down, grad_w_qkv, grad_w_out, small = grads[0]
    lanes += expert_lanes(len(arrays), inner)
    arrays.append(grad_gate_up.reshape(dp, D // dp, held * inner))
    arrays.append(grad_down.reshape(half, dp, inner // dp, D))
    lanes += dense_lanes(len(arrays))
    for array in (grad_w_qkv, grad_w_out, small):
        arrays.append(array.reshape(dp, deep, array.shape[0] // (dp * deep), array.shape[1]))
    for array in (second_qkv, second_out):
        lanes.append((len(arrays), None, [("expert", bits_of("expert"))]))
        arrays.append(array.reshape(deep, array.shape[0] // deep, array.shape[1]))
    lanes.append((len(arrays), None, dense_lanes(0)[2][2]))
    small = grads[1][4]
    arrays.append(small.reshape(dp, deep, small.shape[0] // (dp * deep), small.shape[1]))
    *sums, stats = sum_scatter(arrays, lanes, jnp.concatenate(stats, axis=0), 0)
    stats = lax.dynamic_index_in_dim(stats.reshape(2, 8, COLUMNS), core, 0)
    token_total = SEQ * lax.axis_size(("section", "dp", "expert"))
    counts, chances = stats[:, 1, :experts], stats[:, 0, :experts]
    balance = experts * (counts / (token_total * TOPK) * chances / token_total)
    first_experts = (
        jnp.stack([sums[0], sums[2]]),
        jnp.stack([sums[1], sums[3]]),
        jnp.stack([sums[4], sums[5]]),
    )
    columns = [second_pre[:, i * inner : (i + 1) * inner] for i in range(2 * half)]
    second_experts = (
        jnp.stack(columns[:half]),
        jnp.stack(columns[half:]),
        second_down.reshape(half, inner // dp, D),
    )
    reduced = [(*first_experts, *sums[6:9]), (*second_experts, *sums[9:12])]
    final = []
    for a, b, dim in zip(reduced[0], reduced[1], (0, 0, 0, 1, 1, None)):
        keep = jnp.where(first, a, b)
        got = swapped(jnp.where(first, b, a))
        keep, got = keep.astype(jnp.float32), got.astype(jnp.float32)
        if dim is None:
            final.append(keep + got)
        else:
            final.append(
                jnp.concatenate(
                    [jnp.where(first, keep, got), jnp.where(first, got, keep)], axis=dim
                )
            )
    w_gate_grad, w_up_grad, w_down_grad, grad_w_qkv, grad_w_out, small = final
    heads, kv = H * HD, KVH * HD
    out_keep = jnp.where(first, outs[0], outs[1])
    out_got = swapped(jnp.where(first, outs[1], outs[0]))
    layer_out = jnp.where(
        first, jnp.concatenate([out_keep, out_got]), jnp.concatenate([out_got, out_keep])
    )
    low_one = input_grads[1].astype(jnp.bfloat16).astype(jnp.float32)
    grad_keep = jnp.where(first, input_grads[0], low_one)
    grad_got = swapped(jnp.where(first, low_one, input_grads[0]))
    input_grad = jnp.where(
        first, jnp.concatenate([grad_keep, grad_got]), jnp.concatenate([grad_got, grad_keep])
    )
    results = (
        layer_out,
        input_grad,
        small[:, 0],
        grad_w_qkv[:, :heads],
        grad_w_qkv[:, heads : heads + kv],
        grad_w_qkv[:, heads + kv :],
        grad_w_out,
        small[:, 1],
        small[:, 2 : 2 + experts],
        w_gate_grad,
        w_up_grad,
        w_down_grad,
    )
    return tuple(result[None] for result in results) + (balance,)


def solution(mesh):
    return jax.shard_map(
        body,
        mesh=mesh,
        in_specs=(
            P(("dp", "expert"), None),
            P(("dp", "expert"), None),
            P(("dp", "expert"), None),
            P("section", ("dp", "expert"), None),
            P("section", None),
            P("section", None, None),
            P("section", None, None),
            P("section", None, None),
            P("section", None, None),
            P("section", None),
            P("section", None, None),
            P("section", "expert", None, None),
            P("section", "expert", None, None),
            P("section", "expert", None, None),
        ),
        out_specs=(
            P("section", ("dp", "expert"), None),
            P("section", ("dp", "expert"), None),
            P("section", ("dp", "expert")),
            P("section", ("dp", "expert"), None),
            P("section", ("dp", "expert"), None),
            P("section", ("dp", "expert"), None),
            P("section", ("dp", "expert"), None),
            P("section", ("dp", "expert")),
            P("section", ("dp", "expert"), None),
            P("section", "expert", "dp", None),
            P("section", "expert", "dp", None),
            P("section", "expert", "dp", None),
            P("section", None),
        ),
        check_vma=False,
    )
```

```python
import functools
import itertools

import jax
import jax.numpy as jnp
from jax import lax
from jax.experimental import pallas as pl
from jax.experimental.pallas import tpu as pltpu
from jax.sharding import PartitionSpec as P

D = 1536
H = 24
KVH = 8
HD = 64
TOPK = 8
SEQ = 96


EPSILON = 1e-05
THETA = 10000.0
MASKED = -1e30


def matmul(left_side, right_side):
    return jnp.dot(left_side, right_side, preferred_element_type=jnp.float32)


def rotary_tables(length):
    half_width = HD // 2
    position = jnp.arange(length, dtype=jnp.float32)[:, None]
    freq_rate = THETA ** (-jnp.arange(half_width, dtype=jnp.float32) / half_width)
    angles = position * freq_rate[None, :]
    return (jnp.cos(angles)[:, None, :], jnp.sin(angles)[:, None, :])


def rotate(tensor, cosine_table, sine_table):
    half_width = HD // 2
    first_half = tensor[..., :half_width]
    second_half = tensor[..., half_width:]
    return jnp.concatenate(
        [
            first_half * cosine_table - second_half * sine_table,
            second_half * cosine_table + first_half * sine_table,
        ],
        axis=-1,
    )


def unrotate(gradient, cosine_table, sine_table):
    half_width = HD // 2
    first_half = gradient[..., :half_width]
    second_half = gradient[..., half_width:]
    return jnp.concatenate(
        [
            first_half * cosine_table + second_half * sine_table,
            second_half * cosine_table - first_half * sine_table,
        ],
        axis=-1,
    )


def norm_back(grad_normed, tensor, inverse, gain_vector):
    scaled = grad_normed * gain_vector
    grad_gain = jnp.sum(grad_normed * tensor * inverse, axis=0)
    grad_tensor = inverse * scaled - tensor * inverse**3 * jnp.mean(
        scaled * tensor, axis=-1, keepdims=True
    )
    return (grad_tensor, grad_gain)


def attention_scores(queries, key_rows, segment_row):
    length = queries.shape[0]
    grouped = queries.reshape(length, KVH, H // KVH, HD)
    scores = jnp.einsum(
        "qkgd,skd->kgqs", grouped, key_rows, preferred_element_type=jnp.float32
    ) * HD ** (-0.5)
    position = jnp.arange(length)
    allowed = (position[None, :] <= position[:, None]) & (
        segment_row[:, None] == segment_row[None, :]
    )
    return jnp.where(allowed[None, None], scores, MASKED)


def multi_hot(route_rows, experts):
    columns = jnp.arange(experts, dtype=jnp.int32)
    return jnp.sum(
        (route_rows[..., None] == columns).astype(jnp.float32), axis=-2
    )


def swapped(array):
    return lax.ppermute(array, "section", [(0, 1), (1, 0)])


def add_slab(total, arrived):
    *lead, rows, _ = total.shape
    step = 16 if rows % 16 == 0 else rows
    for where in itertools.product(*(range(n) for n in lead)):

        def add(i, carry):
            at = (*where, pl.ds(pl.multiple_of(i * step, step), step), slice(None))
            both = total[at].astype(jnp.float32) + arrived[at].astype(jnp.float32)
            total[at] = both.astype(jnp.bfloat16)
            return carry

        lax.fori_loop(0, rows // step, add, 0)


def sum_scatter_kernel(plan, *refs):
    lanes, ins, copies = plan
    sources = refs[:ins]
    second_pre, stats_in = refs[ins : ins + 2]
    gate_out, up_out, down_out, query_out, key_out, value_out, out_out, small_out, stats = refs[
        ins + 2 : ins + 11
    ]
    scratch = list(refs[ins + 11 :])
    stage = dict(zip(("pre", "down", "qkv", "out", "small"), scratch[-13:-8]))
    send_sem, recv_sem, local_sem, stats_got, stats_send, stats_recv, core_send, core_recv = (
        scratch[-8:]
    )
    core = lax.axis_index("section")
    partners = []
    for lane in lanes:
        for axis, bits in lane["phases"]:
            partners += [(axis, bit) for bit in bits if (axis, bit) not in partners]
    partners.append(("section", 0))
    index = {axis: lax.axis_index(axis) for axis, _ in partners}
    mine = {(axis, bit): (index[axis] >> bit) & 1 for axis, bit in partners}
    far = {key: index[key[0]] + (1 - 2 * mine[key]) * (1 << key[1]) for key in partners}
    barrier = pltpu.get_barrier_semaphore()
    peers = [{axis: far[axis, bit]} for axis, bit in partners if axis != "dp"]
    groups = lax.axis_size("dp")
    peers += [{"dp": lax.rem(lax.axis_index("dp") + k, groups)} for k in range(1, groups)]
    for peer in peers:
        pl.semaphore_signal(
            barrier, inc=1, device_id=peer, device_id_type=pl.DeviceIdType.MESH
        )
    pl.semaphore_wait(barrier, len(peers))

    counter = itertools.count()

    def send(source, target, key):
        number = next(counter)
        copy = pltpu.make_async_remote_copy(
            src_ref=source,
            dst_ref=target,
            send_sem=send_sem.at[number],
            recv_sem=recv_sem.at[number],
            device_id={key[0]: far[key]},
            device_id_type=pl.DeviceIdType.MESH,
        )
        copy.start()
        return copy

    def place(axis, values):
        total = 0
        for bit, value in values.items():
            total = total + value * (1 << bit)
        return total

    def sum_stats():
        count = lax.axis_size("dp")
        me = lax.axis_index("dp")

        def copy(at, source, slot, target):
            return pltpu.make_async_remote_copy(
                src_ref=source,
                dst_ref=stats_got.at[slot],
                send_sem=stats_send.at[at],
                recv_sem=stats_recv.at[slot],
                device_id=target,
                device_id_type=pl.DeviceIdType.MESH,
            )

        for k in range(1, count):
            copy(k, stats_in, me, {"dp": lax.rem(me + k, count)}).start()
        yield
        stats[...] = stats_in[...]
        for k in range(1, count):
            peer = lax.rem(me + k, count)
            copy(k, stats_in, peer, {"dp": peer}).wait_recv()
            stats[...] += stats_got[peer]
        both = copy(0, stats, count, {"section": far["section", 0]})
        both.start()
        yield
        both.wait()
        stats[...] += stats_got[count]
        for k in range(1, count):
            copy(k, stats_in, me, {"dp": lax.rem(me + k, count)}).wait_send()

    summing = sum_stats()
    next(summing)

    def to_stage(number, source, kind, *at):
        spot = stage[kind].at[(core, *at)]
        return spot, pltpu.make_async_remote_copy(
            src_ref=source,
            dst_ref=spot,
            send_sem=core_send.at[number],
            recv_sem=core_recv.at[number],
            device_id={"section": 1 - core},
            device_id_type=pl.DeviceIdType.MESH,
        )

    spot, whole = to_stage(len(lanes), second_pre, "pre")
    whole_here = pltpu.make_async_copy(second_pre, spot, core_send.at[len(lanes)])

    @pl.when(core == 1)
    def _():
        whole_here.start()

    @pl.when(core == 0)
    def _():
        whole.start()

    moved = []
    started = []
    states = []
    for number, lane in enumerate(lanes):
        count = len(lane["buffers"])
        buffers, scratch = scratch[:count], scratch[count:]
        source = sources[lane["source"]]
        prefix = lane["prefix"]
        if isinstance(prefix, int):
            source = source.at[prefix]

        def part(at, source=source, prefix=prefix):
            if isinstance(prefix, tuple):
                return source.at[at, :, pl.ds(*prefix)]
            if prefix == "inner":
                return source.at[:, at]
            return source.at[at]

        axis, bits = lane["phases"][0]
        total, arrived = buffers[0], buffers[1:]
        rest = [bit for bit in bits[1:]]
        pending = []
        for choice in itertools.product((0, 1), repeat=len(rest)):
            values = dict(zip(rest, choice))
            slot = sum(value << i for i, value in enumerate(choice))
            far_at = place(axis, {**values, bits[0]: 1 - mine[axis, bits[0]]})
            here_at = place(axis, {**values, bits[0]: mine[axis, bits[0]]})
            copy = send(part(far_at), arrived[0].at[slot], (axis, bits[0]))
            pending.append((copy, slot))
            started.append(copy)
            states.append((number, part(here_at), slot, total))
        lane_state = {"total": total, "arrived": arrived, "pending": pending, "rest": rest}
        lane["state"] = lane_state
    locals_ = {}
    for at, (number, here, slot, total) in enumerate(states):
        copy = pltpu.make_async_copy(here, total.at[slot], local_sem.at[at])
        copy.start()
        locals_[number, slot] = copy
    longest = max(sum(len(bits) for _, bits in lane["phases"]) for lane in lanes)
    for step in range(1, longest + 1):
        if step == 2:
            next(summing)
        for number, lane in enumerate(lanes):
            state = lane["state"]
            sizes = [len(bits) for _, bits in lane["phases"]]
            if step > sum(sizes):
                continue
            if step <= sizes[0]:
                axis, bits = lane["phases"][0]
                resolved, rest = bits[:step], bits[step:]

                def slot_of(values):
                    found = 0
                    for i, bit in enumerate(bits[1:]):
                        found = found + values.get(bit, mine[axis, bit]) * (1 << i)
                    return found

                for copy, slot in state["pending"]:
                    copy.wait_recv()
                    if step == 1:
                        locals_[number, slot].wait()
                state["pending_next"] = []
                for choice in itertools.product((0, 1), repeat=len(rest)):
                    values = dict(zip(rest, choice))
                    got = sum(value << i for i, value in enumerate(choice))
                    add_slab(
                        state["total"].at[slot_of(values)], state["arrived"][step - 1].at[got]
                    )
                if rest:
                    following = rest[1:]
                    for choice in itertools.product((0, 1), repeat=len(following)):
                        values = dict(zip(following, choice))
                        got = sum(value << i for i, value in enumerate(choice))
                        values[rest[0]] = 1 - mine[axis, rest[0]]
                        copy = send(
                            state["total"].at[slot_of(values)],
                            state["arrived"][step].at[got],
                            (axis, rest[0]),
                        )
                        state["pending_next"].append((copy, got))
                        started.append(copy)
                final = state["total"].at[slot_of({})] if not rest else None
            else:
                axis, bits = lane["phases"][1]
                done = step - sizes[0]
                rest = bits[done:]
                final = state["final"]
                for copy, _ in state["pending"]:
                    copy.wait_recv()
                state["pending_next"] = []
                for choice in itertools.product((0, 1), repeat=len(rest)):
                    values = dict(zip(rest, choice))
                    got = sum(value << i for i, value in enumerate(choice))
                    at = place(axis, {bit: values.get(bit, mine[axis, bit]) for bit in bits})
                    add_slab(final.at[at], state["arrived"][step - 1].at[got])
                if not rest:
                    at = place(axis, {bit: mine[axis, bit] for bit in bits})
                    final = final.at[at]
            if final is not None and step >= sizes[0]:
                state["final"] = final
                if step == sum(sizes):
                    spot, copy = to_stage(number, final, *lane["target"])
                    moved.append((lane["layer"], copy))

                    @pl.when(core == lane["layer"])
                    def _(spot=spot, final=final):
                        spot[...] = final[...]

                    @pl.when(core != lane["layer"])
                    def _(copy=copy):
                        copy.start()
                elif step < sum(sizes):
                    axis, bits = lane["phases"][1]
                    done = step - sizes[0]
                    bit, following = bits[done], bits[done + 1 :]
                    for choice in itertools.product((0, 1), repeat=len(following)):
                        values = dict(zip(following, choice))
                        got = sum(value << i for i, value in enumerate(choice))
                        at = place(
                            axis,
                            {
                                b: values.get(b, 1 - mine[axis, b] if b == bit else mine[axis, b])
                                for b in bits
                            },
                        )
                        copy = send(final.at[at], state["arrived"][step].at[got], (axis, bit))
                        state["pending_next"].append((copy, got))
                        started.append(copy)
            state["pending"] = state["pending_next"]
    for _ in summing:
        pass

    @pl.when(core == 1)
    def _():
        whole.wait_recv()
        whole_here.wait()

    @pl.when(core == 0)
    def _():
        whole.wait_send()

    for layer, copy in moved:
        @pl.when(core == layer)
        def _(copy=copy):
            copy.wait_recv()

        @pl.when(core != layer)
        def _(copy=copy):
            copy.wait_send()

    pre, inner = stage["pre"], gate_out.shape[2]
    half = gate_out.shape[0] // 2
    rows = gate_out.shape[1]
    line = 16 if rows % 16 == 0 else rows

    def write(i, carry):
        at = pl.ds(pl.multiple_of(i * line, line), line)
        for c in range(2):
            for j in range(half):
                for kind, target in enumerate((gate_out, up_out)):
                    columns = pl.ds((kind * half + j) * inner, inner)
                    target[c * half + j, at] = pre[c, at, columns].astype(jnp.float32)
        return carry

    lax.fori_loop(0, rows // line, write, 0)
    rows = down_out.shape[1]
    line = 16 if rows % 16 == 0 else rows

    def write_down(i, carry):
        at = pl.ds(pl.multiple_of(i * line, line), line)
        for c in range(2):
            for j in range(half):
                down_out[c * half + j, at] = stage["down"][c, j, at].astype(jnp.float32)
        return carry

    lax.fori_loop(0, rows // line, write_down, 0)
    column = 0
    width = stage["qkv"].shape[2]
    for target in (query_out, key_out, value_out):
        done = 0
        while done < target.shape[1]:
            c, at = divmod(column, width)
            size = min(width - at, target.shape[1] - done)
            target[:, done : done + size] = stage["qkv"][c, :, at : at + size].astype(jnp.float32)
            done, column = done + size, column + size
    width = stage["out"].shape[2]
    for c in range(2):
        out_out[:, c * width : (c + 1) * width] = stage["out"][c].astype(jnp.float32)
    small_out[...] = stage["small"][0].astype(jnp.float32) + stage["small"][1].astype(jnp.float32)
    for copy in started:
        copy.wait_send()


def sum_scatter(arrays, lanes, second_pre, stats, inner, collective):
    plans, scratch, shapes, copies, locals_ = [], [], [], 0, 0
    sizes = {}
    for source, prefix, phases, layer, target in lanes:
        shape = arrays[source].shape
        if isinstance(prefix, int):
            shape = shape[1:]
        elif prefix == "inner":
            shape = (shape[1], shape[0], *shape[2:])
        elif prefix is not None:
            shape = (*shape[:-1], prefix[1])
        buffers = [(shape[0] // 2, *shape[1:])]
        for step in range(1, len(phases[0][1]) + 1):
            buffers.append((shape[0] >> step, *shape[1:]))
            copies += shape[0] >> step
        locals_ += shape[0] // 2
        if len(phases) > 1:
            for step in range(1, len(phases[1][1]) + 1):
                buffers.append((shape[1] >> step, *shape[2:]))
                copies += shape[1] >> step
        plans.append(
            {
                "source": source,
                "prefix": prefix,
                "phases": phases,
                "buffers": buffers,
                "layer": layer,
                "target": target,
            }
        )
        sizes.setdefault(target[0], shape[-2:])
        scratch += [pltpu.VMEM(buffer, jnp.bfloat16) for buffer in buffers]
    half = second_pre.shape[1] // (2 * inner)
    heads, kv = H * HD, KVH * HD
    shard = sizes["qkv"][0]
    shapes = [
        jax.ShapeDtypeStruct(shape, jnp.float32)
        for shape in (
            (2 * half, second_pre.shape[0], inner),
            (2 * half, second_pre.shape[0], inner),
            (2 * half, *sizes["down"]),
            (shard, heads),
            (shard, kv),
            (shard, kv),
            (shard, 2 * sizes["out"][1]),
            (shard, COLUMNS),
            stats.shape,
        )
    ]
    scratch += [
        pltpu.VMEM((2, *shape), jnp.bfloat16)
        for shape in (
            second_pre.shape,
            (half, *sizes["down"]),
            sizes["qkv"],
            sizes["out"],
            sizes["small"],
        )
    ]
    scratch += [
        pltpu.SemaphoreType.DMA((copies,)),
        pltpu.SemaphoreType.DMA((copies,)),
        pltpu.SemaphoreType.DMA((locals_,)),
    ]
    hops = lax.axis_size("dp") + 1
    scratch += [
        pltpu.VMEM((hops, *stats.shape), jnp.float32),
        pltpu.SemaphoreType.DMA((hops,)),
        pltpu.SemaphoreType.DMA((hops,)),
        pltpu.SemaphoreType.DMA((len(lanes) + 1,)),
        pltpu.SemaphoreType.DMA((len(lanes) + 1,)),
    ]
    return pl.pallas_call(
        functools.partial(sum_scatter_kernel, (plans, len(arrays), copies)),
        out_shape=shapes,
        in_specs=[pl.BlockSpec(memory_space=pl.ANY)] * (len(arrays) + 1)
        + [pl.BlockSpec(memory_space=pltpu.VMEM)],
        out_specs=[pl.BlockSpec(memory_space=pltpu.VMEM)] * len(shapes),
        scratch_shapes=scratch,
        compiler_params=pltpu.CompilerParams(
            collective_id=collective, has_side_effects=True, vmem_limit_bytes=60 * 2**20
        ),
    )(*arrays, second_pre, stats)


def bits_of(axis):
    return list(range(lax.axis_size(axis).bit_length() - 1))


def slice_of(start, size):
    return (slice(None), pl.ds(start, size))


def expert_lanes(first, inner):
    up, down = [("dp", bits_of("dp"))], [("dp", bits_of("dp")[::-1])]
    return [
        (first, (at * inner, inner), phases, 0, ("pre", *slice_of(at * inner, inner)))
        for at, phases in ((0, up), (2, down), (1, up), (3, down))
    ]


def down_lanes(first, layer):
    up, down = [("dp", bits_of("dp"))], [("dp", bits_of("dp")[::-1])]
    return [(first, 0, up, layer, ("down", 0)), (first, 1, down, layer, ("down", 1))]


def dense_lanes(first):
    up, down, deep = bits_of("dp"), bits_of("dp")[::-1], bits_of("expert")
    return [
        (first, "inner", [("expert", deep), ("dp", up)], 0, ("qkv",)),
        (first + 1, None, [("dp", down), ("expert", deep)], 0, ("out",)),
        (first + 2, None, [("dp", up), ("expert", deep)], 0, ("small",)),
    ]


def attention_forward(inputs, weights, segment_row):
    gain_attn, w_query, w_key, w_value, w_out, gain_moe = weights[:6]
    length = inputs.shape[0]
    cosine_table, sine_table = rotary_tables(length)
    inverse_one = lax.rsqrt(jnp.mean(inputs * inputs, axis=-1, keepdims=True) + EPSILON)
    normed_one = (inputs * inverse_one * gain_attn).astype(jnp.bfloat16)
    queries = rotate(
        matmul(normed_one, w_query).reshape(length, H, HD), cosine_table, sine_table
    ).astype(jnp.bfloat16)
    key_rows = rotate(
        matmul(normed_one, w_key).reshape(length, KVH, HD), cosine_table, sine_table
    ).astype(jnp.bfloat16)
    values = matmul(normed_one, w_value).astype(jnp.bfloat16).reshape(length, KVH, HD)
    scores = attention_scores(queries, key_rows, segment_row)
    highest = jnp.max(scores, axis=-1, keepdims=True)
    exponent = jnp.exp(scores - highest)
    denominator = jnp.sum(exponent, axis=-1, keepdims=True)
    weight = exponent / denominator
    attended = jnp.einsum(
        "kgqs,skd->qkgd", weight.astype(jnp.bfloat16), values, preferred_element_type=jnp.float32
    )
    attended = attended.reshape(length, H * HD).astype(jnp.bfloat16)
    hidden = inputs + matmul(attended, w_out)
    inverse_two = lax.rsqrt(jnp.mean(hidden * hidden, axis=-1, keepdims=True) + EPSILON)
    normed_two = (hidden * inverse_two * gain_moe).astype(jnp.bfloat16)
    state = (inverse_one, normed_one, queries, key_rows, values, weight, attended, hidden, inverse_two, normed_two)
    return state


MESH = pl.DeviceIdType.MESH
COLUMNS = 128
PARTS = 3


def move_rows(sources, held, pieces, sems, compute, z, n, others):
    row_send, row_recv, sum_send, sum_recv = sems
    barrier = pltpu.get_barrier_semaphore()
    for k in range(1, n):
        peer = lax.rem(z + k, n)
        pl.semaphore_signal(barrier, inc=1, device_id={"expert": peer}, device_id_type=MESH)
    for peer in others:
        pl.semaphore_signal(barrier, inc=1, device_id=peer, device_id_type=MESH)
    pl.semaphore_wait(barrier, n - 1 + len(others))

    def row_copy(kind, way, hop, source=None):
        step = 1 - 2 * way
        block = jnp.clip(z - step * hop, 0, n - 1)
        peer = jnp.clip(z + step, 0, n - 1)
        return pltpu.make_async_remote_copy(
            src_ref=held[kind].at[block] if source is None else source,
            dst_ref=held[kind].at[block],
            send_sem=row_send.at[kind, way, hop],
            recv_sem=row_recv.at[kind, way, hop],
            device_id={"expert": peer},
            device_id_type=MESH,
        )

    def sends(way, hop):
        step = 1 - 2 * way
        block, peer = z - step * hop, z + step
        return (block >= 0) & (block < n) & (peer >= 0) & (peer < n)

    def arrives(way, hop):
        block = z - (1 - 2 * way) * (hop + 1)
        return (block >= 0) & (block < n)

    def start(kind):
        for way in range(2):
            @pl.when(sends(way, 0))
            def _():
                row_copy(kind, way, 0, sources[kind]).start()

    def take(hop):
        for kind in range(len(held)):
            for way in range(2):
                @pl.when(arrives(way, hop))
                def _():
                    row_copy(kind, way, hop).wait_recv()

                @pl.when(sends(way, hop + 1) & (hop + 1 < n - 1))
                def _():
                    row_copy(kind, way, hop + 1).start()

    def behind(way):
        peer = z - (1 - 2 * way)
        return (peer >= 0) & (peer < n)

    def sum_copy(way, block, p):
        mine, arrived = pieces[p]
        return pltpu.make_async_remote_copy(
            src_ref=mine(block),
            dst_ref=arrived(way, block),
            send_sem=sum_send.at[block, p],
            recv_sem=sum_recv.at[way, block, p],
            device_id={"expert": jnp.clip(z + 1 - 2 * way, 0, n - 1)},
            device_id_type=MESH,
        )

    def sent(block, p):
        way = jnp.where(block > z, 0, 1)

        @pl.when((block != z) & jnp.logical_not(behind(way)))
        def _():
            sum_copy(way, block, p).start()

    def run():
        def both(hop):
            return (hop >= 0) & (z - 1 - hop >= 0) & (z + 1 + hop < n)

        def turn(k, carry):
            hop = lax.div(k + 1, 2) - 1
            block = z + (1 + hop) * (1 - 2 * lax.rem(k, 2))
            odd = lax.rem(k, 2) == 1

            @pl.when(odd & jnp.logical_not(both(hop - 1)))
            def _():
                take(hop)

            @pl.when(jnp.logical_not(odd) & both(hop) & (hop + 1 < n - 1))
            def _():
                take(hop + 1)

            @pl.when((block >= 0) & (block < n))
            def _():
                compute(block, sent)

            return carry

        lax.fori_loop(0, 2 * n - 1, turn, 0)

        first = jnp.where(2 * z < n, 0, 1)
        for way in (first, 1 - first):
            for k in range(1, n):
                block = z + (1 - 2 * way) * k

                @pl.when(behind(way) & (block >= 0) & (block < n))
                def _():
                    for p, (mine, arrived) in enumerate(pieces):
                        sum_copy(way, block, p).wait_recv()
                        own, other = mine(block), arrived(way, block)
                        own[...] = (
                            own[...].astype(jnp.float32) + other[...].astype(jnp.float32)
                        ).astype(jnp.bfloat16)
                        sum_copy(way, block, p).start()

    def collect(add):
        for way in range(2):
            @pl.when(behind(way))
            def _():
                for p, (_, arrived) in enumerate(pieces):
                    sum_copy(way, z, p).wait_recv()
                    add(p, arrived(way, z)[...].astype(jnp.float32))

    def finish():
        for kind in range(len(held)):
            for way in range(2):
                for hop in range(n - 1):
                    @pl.when(sends(way, hop))
                    def _():
                        row_copy(kind, way, hop).wait_send()
        for k in range(1, n):
            for p in range(len(pieces)):
                sum_copy(0, lax.rem(z + k, n), p).wait_send()

    return start, run, collect, finish


def row_pieces(sums, returned, parts):
    width = sums.shape[2] // parts

    def piece(p):
        at = pl.ds(p * width, width)
        return (
            lambda block: sums.at[block, :, at],
            lambda way, block: returned.at[way, block, :, at],
        )

    return [piece(p) for p in range(parts)]


def fetch_weights(layer, own, other, places, sem):
    count = places[0].shape[0]
    mine = lax.axis_index("section") == layer

    def copy(group, kind, e):
        return pltpu.make_async_copy(
            group[kind].at[e], places[kind].at[e], sem.at[kind * count + e]
        )

    for kind in range(len(places)):
        for e in range(count):
            @pl.when(mine)
            def _():
                copy(own, kind, e).start()

            @pl.when(jnp.logical_not(mine))
            def _():
                copy(other, kind, e).start()

    def wait():
        for kind in range(len(places)):
            for e in range(count):
                copy(own, kind, e).wait()

    return wait


def sigmoid_of(value):
    return 1.0 / (1.0 + jnp.exp(-value))


def column_of(block, column):
    here = lax.broadcasted_iota(jnp.int32, block.shape, 1) == column
    return jnp.sum(jnp.where(here, block, 0.0), axis=1, keepdims=True)


def experts_forward_kernel(
    layer, experts, x, mask, hidden, router, *refs
):
    own, other, refs = refs[:3], refs[3:6], refs[6:]
    own_dense, other_dense, refs = refs[:4], refs[4:8], refs[8:]
    out, rows, gates_all, gates, gate_keep, up_keep, gated, stats = refs[:8]
    placed, place_sem, refs = refs[8:12], refs[-1], refs[:8] + refs[12:-1]
    w_gate, w_up, w_down, sums, returned, mixed, total, stats_all = refs[8:16]
    weight_sem, *sems = refs[16:]
    n, held = rows.shape[0], w_gate.shape[0]
    z = lax.axis_index("expert")

    def compute(block, sent):
        picked = rows[block]
        gate_block = gates_all[block].astype(jnp.float32)

        def one(e, carry):
            gate_pre = jnp.dot(picked, w_gate[e], preferred_element_type=jnp.float32)
            up_pre = jnp.dot(picked, w_up[e], preferred_element_type=jnp.float32)
            gate_keep[e, block] = gate_pre.astype(jnp.bfloat16)
            up_keep[e, block] = up_pre.astype(jnp.bfloat16)
            active = gate_pre * sigmoid_of(gate_pre) * up_pre
            share = (column_of(gate_block, z * held + e) * active).astype(jnp.bfloat16)
            inner = share.shape[1]
            gated[block, :, pl.ds(pl.multiple_of(e * inner, inner), inner)] = share
            mixed[e] = share
            return carry

        lax.fori_loop(0, held, one, 0)
        width = out.shape[1] // PARTS
        for part in range(PARTS):
            at = pl.ds(part * width, width)
            result = jnp.zeros((out.shape[0], width), jnp.float32)
            for e in range(held):
                result += jnp.dot(mixed[e], w_down[e, :, at], preferred_element_type=jnp.float32)

            @pl.when(block == z)
            def _():
                total[:, at] = hidden[:, at] + result

            @pl.when(block != z)
            def _():
                sums[block, :, at] = result.astype(jnp.bfloat16)

            sent(block, part)

    own_gates = gates_all.at[z]
    start, run, collect, finish = move_rows(
        (x, own_gates, stats_all.at[z]),
        (rows, gates_all, stats_all),
        row_pieces(sums, returned, PARTS),
        sems,
        compute,
        z,
        n,
        [],
    )
    start(0)
    wait_weights = fetch_weights(layer, own, other, (w_gate, w_up, w_down), weight_sem)
    here = lax.axis_index("section") == 1 - layer

    def place_copy(group, i):
        return pltpu.make_async_copy(group[i], placed[i], place_sem.at[i])

    for i in range(4):
        @pl.when(here)
        def _():
            place_copy(own_dense, i).start()

        @pl.when(jnp.logical_not(here))
        def _():
            place_copy(other_dense, i).start()

    logits = jnp.dot(x[...], router[...], preferred_element_type=jnp.float32)
    chosen = mask[...] > 0
    highest = jnp.max(jnp.where(chosen, logits, MASKED), axis=1, keepdims=True)
    exponent = jnp.where(chosen, jnp.exp(logits - highest), 0.0)
    gates[...] = exponent / jnp.sum(exponent, axis=1, keepdims=True)
    own_gates[...] = gates[...].astype(jnp.bfloat16)
    start(1)
    real = lax.broadcasted_iota(jnp.int32, logits.shape, 1) < experts
    highest = jnp.max(jnp.where(real, logits, MASKED), axis=1, keepdims=True)
    exponent = jnp.where(real, jnp.exp(logits - highest), 0.0)
    chance = exponent / jnp.sum(exponent, axis=1, keepdims=True)
    line = lax.broadcasted_iota(jnp.int32, stats.shape, 0)
    stats_all[z] = jnp.where(
        line == 0,
        jnp.sum(chance, axis=0, keepdims=True),
        jnp.where(line == 1, jnp.sum(mask[...], axis=0, keepdims=True), 0.0),
    )
    start(2)
    rows[z] = x[...]
    wait_weights()
    run()
    stats[...] = jnp.sum(stats_all[...], axis=0)
    width = out.shape[1] // PARTS

    def add(p, value):
        total[:, p * width : (p + 1) * width] += value

    collect(add)
    out[...] = total[...].astype(jnp.bfloat16)
    finish()
    for i in range(4):
        place_copy(own_dense, i).wait()


def experts_backward_kernel(layer, grad, gates, gate_keep, up_keep, *refs):
    own, other, saved_rows, saved_gated, refs = refs[:3], refs[3:6], refs[6], refs[7], refs[8:]
    out, out_gates, rows_both, gated_both, grad_both, pre_both = refs[:6]
    w_gate, w_up, w_down, sums, sum_gates, returned, returned_gates, away, dots = refs[6:15]
    weight_sem, core_send, core_recv, core_local, *sems = refs[15:]
    n, held = gates.shape[0], w_gate.shape[0]
    half, inner = held // 2, w_gate.shape[2]
    core = lax.axis_index("section")
    z = lax.axis_index("expert")
    turned_dims = (((1,), (1,)), ((), ()))
    rows = grad_both.at[core]

    def to_core(number, source, target):
        return pltpu.make_async_remote_copy(
            src_ref=source,
            dst_ref=target,
            send_sem=core_send.at[number],
            recv_sem=core_recv.at[number],
            device_id={"section": 1 - core},
            device_id_type=MESH,
        )

    def block_copies(block):
        return (
            to_core(2 + block, rows.at[block], rows.at[block]),
            to_core(2 + n + block, away.at[block], pre_both.at[core, block]),
        )

    def columns(at):
        return pl.ds(pl.multiple_of(at * half * inner, half * inner), half * inner)

    def whole_copies():
        return (
            to_core(0, saved_rows, rows_both.at[core]),
            to_core(1, saved_gated.at[:, :, columns(1 - core)], gated_both.at[core]),
        )

    def local_copies():
        return (
            pltpu.make_async_copy(saved_rows, rows_both.at[core], core_local.at[0]),
            pltpu.make_async_copy(
                saved_gated.at[:, :, columns(core)], gated_both.at[core], core_local.at[1]
            ),
        )

    def compute(block, sent):
        picked = rows[block]
        gate_block = gates[block].astype(jnp.float32)
        dots[...] = jnp.zeros(dots.shape, jnp.float32)

        def one(e, place, j):
            raw = lax.dot_general(
                picked, w_down[e], turned_dims, preferred_element_type=jnp.float32
            )
            gate_pre = gate_keep[e, block].astype(jnp.float32)
            up_pre = up_keep[e, block].astype(jnp.float32)
            sigmoid = sigmoid_of(gate_pre)
            silu = gate_pre * sigmoid
            column = z * held + e
            dot = jnp.sum(raw * (silu * up_pre), axis=1, keepdims=True)
            here = lax.broadcasted_iota(jnp.int32, dots.shape, 1) == column
            dots[...] += jnp.where(here, dot, 0.0)
            active = column_of(gate_block, column) * raw
            place[:, pl.ds(pl.multiple_of(j * inner, inner), inner)] = (
                active * up_pre * sigmoid * (1.0 + gate_pre * (1.0 - sigmoid))
            ).astype(jnp.bfloat16)
            place[:, pl.ds(pl.multiple_of((half + j) * inner, inner), inner)] = (
                active * silu
            ).astype(jnp.bfloat16)

        def own_half(j, carry):
            one(core * half + j, pre_both.at[core, block], j)
            return carry

        def other_half(j, carry):
            one((1 - core) * half + j, away.at[block], j)
            return carry

        lax.fori_loop(0, half, other_half, 0)
        for copy in block_copies(block):
            copy.start()
        lax.fori_loop(0, half, own_half, 0)
        sum_gates[block] = dots[...].astype(jnp.bfloat16)

        @pl.when(block == z)
        def _():
            out_gates[...] = dots[...]

        sent(block, PARTS)
        width = out.shape[1] // PARTS
        for part in range(PARTS):
            at = pl.ds(part * width, width)
            result = jnp.zeros((out.shape[0], width), jnp.float32)
            for place, side in ((away.at[block], 1 - core), (pre_both.at[core, block], core)):
                for kind, right in enumerate((w_gate, w_up)):
                    for j in range(half):
                        left = place[:, pl.ds((kind * half + j) * inner, inner)]
                        result += lax.dot_general(
                            left,
                            right[side * half + j, at, :],
                            turned_dims,
                            preferred_element_type=jnp.float32,
                        )

            @pl.when(block == z)
            def _():
                out[:, at] = result

            @pl.when(block != z)
            def _():
                sums[block, :, at] = result.astype(jnp.bfloat16)

            sent(block, part)

    gate_piece = (lambda block: sum_gates.at[block], lambda way, block: returned_gates.at[way, block])
    start, run, collect, finish = move_rows(
        (grad,),
        (rows,),
        row_pieces(sums, returned, PARTS) + [gate_piece],
        sems,
        compute,
        z,
        n,
        [{"section": 1 - core}],
    )
    start(0)
    wait_weights = fetch_weights(layer, own, other, (w_gate, w_up, w_down), weight_sem)
    for copy in whole_copies() + local_copies():
        copy.start()
    rows[z] = grad[...]
    wait_weights()
    run()
    width = out.shape[1] // PARTS

    def add(p, value):
        if p == PARTS:
            out_gates[...] += value
        else:
            out[:, p * width : (p + 1) * width] += value

    collect(add)
    finish()
    for copy in local_copies():
        copy.wait()
    for copy in whole_copies():
        copy.wait()
    for block in range(n):
        for copy in block_copies(block):
            copy.wait()


def exchange_scratch(n, kinds_out, kinds_back):
    return [
        pltpu.SemaphoreType.DMA((kinds_out, 2, n)),
        pltpu.SemaphoreType.DMA((kinds_out, 2, n)),
        pltpu.SemaphoreType.DMA((n, kinds_back)),
        pltpu.SemaphoreType.DMA((2, n, kinds_back)),
    ]


def expert_call(kernel, operands, own, other, extra, shapes, scratch, collective, loose=0):
    vmem, free = pl.BlockSpec(memory_space=pltpu.VMEM), pl.BlockSpec(memory_space=pl.ANY)
    weights = [pltpu.VMEM(array.shape, jnp.bfloat16) for array in own]
    return pl.pallas_call(
        kernel,
        out_shape=shapes,
        in_specs=[vmem] * len(operands) + [free] * (6 + len(extra)),
        out_specs=[vmem] * (len(shapes) - loose) + [free] * loose,
        scratch_shapes=weights + scratch,
        compiler_params=pltpu.CompilerParams(
            collective_id=collective, has_side_effects=True, vmem_limit_bytes=50 * 2**20
        ),
        cost_estimate=pl.CostEstimate(
            flops=5 * 10**10, bytes_accessed=10**8, transcendentals=0
        ),
    )(*operands, *own, *other, *extra)


def experts_forward(
    layer, normed_two, mask, hidden, router, own, other, own_dense, other_dense, experts
):
    n, held = lax.axis_size("expert"), own[0].shape[0]
    length, width = normed_two.shape
    inner = own[0].shape[2]
    low, full = jnp.bfloat16, jnp.float32
    kept = jax.ShapeDtypeStruct((held, n, length, inner), low)
    shapes = [
        jax.ShapeDtypeStruct((length, width), low),
        jax.ShapeDtypeStruct((n, length, width), low),
        jax.ShapeDtypeStruct((n, length, COLUMNS), low),
        jax.ShapeDtypeStruct((length, COLUMNS), full),
        kept,
        kept,
        jax.ShapeDtypeStruct((n, length, held * inner), low),
        jax.ShapeDtypeStruct((8, COLUMNS), full),
    ] + [jax.ShapeDtypeStruct(array.shape, low) for array in own_dense]
    scratch = [
        pltpu.VMEM((n, length, width), low),
        pltpu.VMEM((2, n, length, width), low),
        pltpu.VMEM((held, length, inner), low),
        pltpu.VMEM((length, width), full),
        pltpu.VMEM((n, 8, COLUMNS), full),
        pltpu.SemaphoreType.DMA((3 * held,)),
    ] + exchange_scratch(n, 3, PARTS)
    scratch.append(pltpu.SemaphoreType.DMA((4,)))
    kernel = functools.partial(experts_forward_kernel, layer, experts)
    return expert_call(
        kernel,
        (normed_two, mask, hidden, router),
        own,
        other,
        (*own_dense, *other_dense),
        shapes,
        scratch,
        1 + layer,
        4,
    )


def experts_backward(layer, grad_low, gates, gate_keep, up_keep, rows, gated, own, other):
    held, n, length, inner = gate_keep.shape
    width = grad_low.shape[1]
    low, full = jnp.bfloat16, jnp.float32
    shapes = [
        jax.ShapeDtypeStruct((length, width), full),
        jax.ShapeDtypeStruct((length, COLUMNS), full),
        jax.ShapeDtypeStruct((2, n, length, width), low),
        jax.ShapeDtypeStruct((2, n, length, held // 2 * inner), low),
        jax.ShapeDtypeStruct((2, n, length, width), low),
        jax.ShapeDtypeStruct((2, n, length, held * inner), low),
    ]
    scratch = [
        pltpu.VMEM((n, length, width), low),
        pltpu.VMEM((n, length, COLUMNS), low),
        pltpu.VMEM((2, n, length, width), low),
        pltpu.VMEM((2, n, length, COLUMNS), low),
        pltpu.VMEM((n, length, held * inner), low),
        pltpu.VMEM((length, COLUMNS), full),
        pltpu.SemaphoreType.DMA((3 * held,)),
        pltpu.SemaphoreType.DMA((2 + 2 * n,)),
        pltpu.SemaphoreType.DMA((2 + 2 * n,)),
        pltpu.SemaphoreType.DMA((2,)),
    ] + exchange_scratch(n, 1, PARTS + 1)
    kernel = functools.partial(experts_backward_kernel, layer)
    return expert_call(
        kernel,
        (grad_low, gates, gate_keep, up_keep),
        own,
        other,
        (rows, gated),
        shapes,
        scratch,
        3 + layer,
    )


def attention_backward(grad_hidden, inputs, state, weights):
    gain_attn, w_query, w_key, w_value, w_out, gain_moe = weights[:6]
    (inverse_one, normed_one, queries, key_rows, values, weight, attended, hidden, inverse_two, normed_two) = state
    length = inputs.shape[0]
    grad_branch = grad_hidden.astype(jnp.bfloat16)
    grad_attended = jnp.einsum("td,cd->tc", grad_branch, w_out, preferred_element_type=jnp.float32)
    grad_attended = grad_attended.astype(jnp.bfloat16).reshape(length, KVH, H // KVH, HD)
    grad_weight = jnp.einsum(
        "qkgd,skd->kgqs", grad_attended, values, preferred_element_type=jnp.float32
    )
    grad_values = jnp.einsum(
        "kgqs,qkgd->skd",
        weight.astype(jnp.bfloat16),
        grad_attended,
        preferred_element_type=jnp.float32,
    )
    grad_values = grad_values.astype(jnp.bfloat16).reshape(length, KVH * HD)
    grad_scores = (
        weight * (grad_weight - jnp.sum(weight * grad_weight, axis=-1, keepdims=True))
    ).astype(jnp.bfloat16)
    score_scale = HD ** (-0.5)
    grouped = queries.reshape(length, KVH, H // KVH, HD)
    grad_queries = jnp.einsum(
        "kgqs,skd->qkgd", grad_scores, key_rows, preferred_element_type=jnp.float32
    )
    grad_queries = grad_queries.reshape(length, H, HD) * score_scale
    grad_keys = (
        jnp.einsum("kgqs,qkgd->skd", grad_scores, grouped, preferred_element_type=jnp.float32)
        * score_scale
    )
    cosine_table, sine_table = rotary_tables(length)
    grad_query_pre = (
        unrotate(grad_queries, cosine_table, sine_table)
        .reshape(length, H * HD)
        .astype(jnp.bfloat16)
    )
    grad_key_pre = (
        unrotate(grad_keys, cosine_table, sine_table).reshape(length, KVH * HD).astype(jnp.bfloat16)
    )
    grad_normed_one = (
        jnp.einsum("tq,cq->tc", grad_query_pre, w_query, preferred_element_type=jnp.float32)
        + jnp.einsum("tq,cq->tc", grad_key_pre, w_key, preferred_element_type=jnp.float32)
        + jnp.einsum("tq,cq->tc", grad_values, w_value, preferred_element_type=jnp.float32)
    )
    grad_norm_one, grad_gain_attn = norm_back(grad_normed_one, inputs, inverse_one, gain_attn)
    grad_inputs = grad_hidden + grad_norm_one
    grad_qkv = jnp.concatenate([grad_query_pre, grad_key_pre, grad_values], axis=1)
    return grad_inputs, grad_gain_attn, grad_qkv, grad_branch


def turned(left, right):
    return jnp.einsum("tc,tq->cq", left, right, preferred_element_type=jnp.float32)


def body(tokens, cotangent, segments, routes, *weight_arrays):
    core = lax.axis_index("section")
    first = core == 0
    experts = weight_arrays[6].shape[2]
    w_gate = weight_arrays[7]
    held = w_gate.shape[1]
    own = [array[0] for array in weight_arrays]
    other = [swapped(array) for array in own]
    weights = [
        [jnp.where(first, a, b) for a, b in zip(own[:7], other[:7])],
        [jnp.where(first, b, a) for a, b in zip(own[:7], other[:7])],
    ]
    inputs_low = lax.dynamic_slice_in_dim(tokens, core * SEQ, SEQ, 0)
    grad_low = lax.dynamic_slice_in_dim(cotangent, core * SEQ, SEQ, 0)
    segment_row = lax.dynamic_index_in_dim(segments, core, 0, keepdims=False)
    mine = lax.dynamic_slice_in_dim(routes[0], core * SEQ, SEQ, 0)
    got = swapped(lax.dynamic_slice_in_dim(routes[0], (1 - core) * SEQ, SEQ, 0))
    routes_here = jnp.stack([jnp.where(first, mine, got), jnp.where(first, got, mine)])
    masks = multi_hot(routes_here, COLUMNS)
    own_experts, other_experts = own[7:], other[7:]

    saved, outs, stats = [], [], []
    for s in range(2):
        inputs = inputs_low.astype(jnp.float32)
        state = attention_forward(inputs, weights[s], segment_row)
        hidden, normed_two = state[7], state[9]
        router = jnp.pad(weights[s][6], ((0, 0), (0, COLUMNS - experts)))
        inputs_low, *expert_state, stat, query, key, value, out = experts_forward(
            s,
            normed_two,
            masks[s],
            hidden,
            router,
            own_experts,
            other_experts,
            own[1:5],
            other[1:5],
            experts,
        )
        weights[1 - s][1:5] = [query, key, value, out]
        outs.append(inputs_low)
        stats.append(stat)
        saved.append((inputs, state, expert_state))

    grads = [None, None]
    input_grads = [None, None]
    for s in (1, 0):
        inputs, state, expert_state = saved[s]
        (inverse_one, normed_one, _, _, _, _, attended, hidden, inverse_two, normed_two) = state
        rows_all, gates_all, gates, gate_keep, up_keep, gated = expert_state
        gain_moe, w_router = weights[s][5], weights[s][6]
        grad_sum, grad_gates, rows_both, gated_both, grad_both, pre_both = experts_backward(
            s,
            grad_low,
            gates_all,
            gate_keep,
            up_keep,
            rows_all,
            gated,
            own_experts,
            other_experts,
        )
        inner = w_gate.shape[3]
        grad_gate_up = turned(
            rows_both.reshape(-1, D), pre_both.reshape(-1, held * inner)
        ).astype(jnp.bfloat16)
        if s == 1:
            grad_sum, grad_gate_up = lax.optimization_barrier((grad_sum, grad_gate_up))
            second_pre = lax.psum_scatter(grad_gate_up, "dp", scatter_dimension=0, tiled=True)
        else:
            grad_sum, second_pre = lax.optimization_barrier((grad_sum, second_pre))
        gates, grad_gates = gates[:, :experts], grad_gates[:, :experts]
        grad_chosen = gates * (grad_gates - jnp.sum(gates * grad_gates, axis=-1, keepdims=True))
        grad_logits = grad_chosen.astype(jnp.bfloat16)
        grad_normed_two = grad_sum + jnp.einsum(
            "te,de->td", grad_logits, w_router, preferred_element_type=jnp.float32
        )
        grad_norm_two, grad_gain_moe = norm_back(grad_normed_two, hidden, inverse_two, gain_moe)
        grad_hidden = grad_low.astype(jnp.float32) + grad_norm_two
        grad_inputs, grad_gain_attn, grad_qkv, grad_branch = attention_backward(
            grad_hidden, inputs, state, weights[s]
        )
        if s == 1:
            grad_inputs, gated_both = lax.optimization_barrier((grad_inputs, gated_both))
        grad_down = turned(
            gated_both.reshape(-1, held // 2 * inner), grad_both.reshape(-1, D)
        ).astype(jnp.bfloat16)

        def halves(array):
            width = array.shape[1] // 2
            return (
                lax.dynamic_slice_in_dim(array, core * width, width, 1),
                lax.dynamic_slice_in_dim(array, (1 - core) * width, width, 1),
            )
        qkv_keep, qkv_send = halves(grad_qkv)
        branch_keep, branch_send = halves(grad_branch)
        packed = swapped(jnp.concatenate([normed_one, attended, qkv_send, branch_send], axis=1))
        normed_got, attended_got = packed[:, :D], packed[:, D : 2 * D]
        qkv_got = packed[:, 2 * D : 2 * D + qkv_send.shape[1]]
        branch_got = packed[:, 2 * D + qkv_send.shape[1] :]
        grad_w_qkv = turned(
            jnp.concatenate([normed_one, normed_got]), jnp.concatenate([qkv_keep, qkv_got])
        ).astype(jnp.bfloat16)
        grad_w_out = turned(
            jnp.concatenate([attended, attended_got]), jnp.concatenate([branch_keep, branch_got])
        ).astype(jnp.bfloat16)
        grad_w_router = turned(normed_two, grad_logits)
        small = jnp.concatenate(
            [grad_gain_attn[:, None], grad_gain_moe[:, None], grad_w_router], axis=1
        ).astype(jnp.bfloat16)
        small = jnp.pad(small, ((0, 0), (0, COLUMNS - small.shape[1])))
        if s == 1:
            grad_inputs, grad_down, grad_w_qkv, grad_w_out = lax.optimization_barrier(
                (grad_inputs, grad_down, grad_w_qkv, grad_w_out)
            )
            second_out = lax.psum_scatter(grad_w_out, "dp", scatter_dimension=0, tiled=True)
            second_qkv = lax.psum_scatter(grad_w_qkv, "dp", scatter_dimension=0, tiled=True)
        grads[s] = (grad_gate_up, grad_down, grad_w_qkv, grad_w_out, small)
        input_grads[s] = grad_inputs
        grad_low = grad_inputs.astype(jnp.bfloat16)

    dp, deep = lax.axis_size("dp"), lax.axis_size("expert")
    half, inner = held // 2, w_gate.shape[3]
    grad_gate_up, grad_down, grad_w_qkv, grad_w_out, small = grads[0]
    arrays = [
        grad_gate_up.reshape(dp, D // dp, held * inner),
        grad_down.reshape(half, dp, inner // dp, D),
    ]
    lanes = expert_lanes(0, inner) + down_lanes(1, 0) + down_lanes(2, 1) + dense_lanes(3)
    arrays.append(grads[1][1].reshape(half, dp, inner // dp, D))
    for array in (grad_w_qkv, grad_w_out, small):
        arrays.append(array.reshape(dp, deep, array.shape[0] // (dp * deep), array.shape[1]))
    for array, kind in ((second_qkv, "qkv"), (second_out, "out")):
        lanes.append((len(arrays), None, [("expert", bits_of("expert"))], 1, (kind,)))
        arrays.append(array.reshape(deep, array.shape[0] // deep, array.shape[1]))
    lanes.append((len(arrays), None, dense_lanes(0)[2][2], 1, ("small",)))
    small = grads[1][4]
    arrays.append(small.reshape(dp, deep, small.shape[0] // (dp * deep), small.shape[1]))
    w_gate_grad, w_up_grad, w_down_grad, query, key, value, grad_w_out, small, stats = sum_scatter(
        arrays, lanes, second_pre, jnp.concatenate(stats, axis=0), inner, 0
    )
    stats = lax.dynamic_index_in_dim(stats.reshape(2, 8, COLUMNS), core, 0)
    token_total = SEQ * lax.axis_size(("section", "dp", "expert"))
    counts, chances = stats[:, 1, :experts], stats[:, 0, :experts]
    balance = experts * (counts / (token_total * TOPK) * chances / token_total)
    out_keep = jnp.where(first, outs[0], outs[1])
    out_got = swapped(jnp.where(first, outs[1], outs[0]))
    layer_out = jnp.where(
        first, jnp.concatenate([out_keep, out_got]), jnp.concatenate([out_got, out_keep])
    )
    low_one = input_grads[1].astype(jnp.bfloat16).astype(jnp.float32)
    grad_keep = jnp.where(first, input_grads[0], low_one)
    grad_got = swapped(jnp.where(first, low_one, input_grads[0]))
    input_grad = jnp.where(
        first, jnp.concatenate([grad_keep, grad_got]), jnp.concatenate([grad_got, grad_keep])
    )
    results = (
        layer_out,
        input_grad,
        small[:, 0],
        query,
        key,
        value,
        grad_w_out,
        small[:, 1],
        small[:, 2 : 2 + experts],
        w_gate_grad,
        w_up_grad,
        w_down_grad,
    )
    return tuple(result[None] for result in results) + (balance,)


def solution(mesh):
    return jax.shard_map(
        body,
        mesh=mesh,
        in_specs=(
            P(("dp", "expert"), None),
            P(("dp", "expert"), None),
            P(("dp", "expert"), None),
            P("section", ("dp", "expert"), None),
            P("section", None),
            P("section", None, None),
            P("section", None, None),
            P("section", None, None),
            P("section", None, None),
            P("section", None),
            P("section", None, None),
            P("section", "expert", None, None),
            P("section", "expert", None, None),
            P("section", "expert", None, None),
        ),
        out_specs=(
            P("section", ("dp", "expert"), None),
            P("section", ("dp", "expert"), None),
            P("section", ("dp", "expert")),
            P("section", ("dp", "expert"), None),
            P("section", ("dp", "expert"), None),
            P("section", ("dp", "expert"), None),
            P("section", ("dp", "expert"), None),
            P("section", ("dp", "expert")),
            P("section", ("dp", "expert"), None),
            P("section", "expert", "dp", None),
            P("section", "expert", "dp", None),
            P("section", "expert", "dp", None),
            P("section", None),
        ),
        check_vma=False,
    )
```

```python
import functools
import itertools
from types import SimpleNamespace

import jax
import jax.numpy as jnp
from jax import lax
from jax.experimental import pallas as pl
from jax.experimental.pallas import tpu as pltpu
from jax.sharding import PartitionSpec as P

D = 1536
H = 24
KVH = 8
HD = 64
TOPK = 8
SEQ = 96


EPSILON = 1e-05
THETA = 10000.0
MASKED = -1e30
COLUMNS = 128
GATE, UP, DOWN, QKV, OUT, SMALL = range(6)
CORE, GROUP, LINE = "section", "dp", "expert"
INNER = "inner"


def matmul(left_side, right_side):
    return jnp.dot(left_side, right_side, preferred_element_type=jnp.float32)


def rotary_tables(length):
    half_width = HD // 2
    position = jnp.arange(length, dtype=jnp.float32)[:, None]
    freq_rate = THETA ** (-jnp.arange(half_width, dtype=jnp.float32) / half_width)
    angles = position * freq_rate[None, :]
    return (jnp.cos(angles)[:, None, :], jnp.sin(angles)[:, None, :])


def rotate(tensor, cosine_table, sine_table):
    half_width = HD // 2
    first_half = tensor[..., :half_width]
    second_half = tensor[..., half_width:]
    return jnp.concatenate(
        [
            first_half * cosine_table - second_half * sine_table,
            second_half * cosine_table + first_half * sine_table,
        ],
        axis=-1,
    )


def unrotate(gradient, cosine_table, sine_table):
    half_width = HD // 2
    first_half = gradient[..., :half_width]
    second_half = gradient[..., half_width:]
    return jnp.concatenate(
        [
            first_half * cosine_table + second_half * sine_table,
            second_half * cosine_table - first_half * sine_table,
        ],
        axis=-1,
    )


def norm_back(grad_normed, tensor, inverse, gain_vector):
    scaled = grad_normed * gain_vector
    grad_gain = jnp.sum(grad_normed * tensor * inverse, axis=0)
    grad_tensor = inverse * scaled - tensor * inverse**3 * jnp.mean(
        scaled * tensor, axis=-1, keepdims=True
    )
    return (grad_tensor, grad_gain)


def attention_scores(queries, key_rows, segment_row):
    length = queries.shape[0]
    grouped = queries.reshape(length, KVH, H // KVH, HD)
    scores = jnp.einsum(
        "qkgd,skd->kgqs", grouped, key_rows, preferred_element_type=jnp.float32
    ) * HD ** (-0.5)
    position = jnp.arange(length)
    allowed = (position[None, :] <= position[:, None]) & (
        segment_row[:, None] == segment_row[None, :]
    )
    return jnp.where(allowed[None, None], scores, MASKED)


def multi_hot(route_rows, experts):
    columns = jnp.arange(experts, dtype=jnp.int32)
    return jnp.sum(
        (route_rows[..., None] == columns).astype(jnp.float32), axis=-2
    )


def swapped(array):
    return lax.ppermute(array, CORE, [(0, 1), (1, 0)])


def add_slab(total, arrived):
    *lead, rows, _ = total.shape
    step = 16 if rows % 16 == 0 else rows
    for where in itertools.product(*(range(n) for n in lead)):

        def add(i, carry):
            at = (*where, pl.ds(pl.multiple_of(i * step, step), step), slice(None))
            both = total[at].astype(jnp.float32) + arrived[at].astype(jnp.float32)
            total[at] = both.astype(jnp.bfloat16)
            return carry

        lax.fori_loop(0, rows // step, add, 0)


def sum_scatter_kernel(plan, *refs):
    lanes, ins, copies = plan
    sources = refs[:ins]
    second_pre, stats_in = refs[ins : ins + 2]
    stage, stats = refs[ins + 2 : ins + 8], refs[ins + 8]
    scratch = list(refs[ins + 9 :])
    send_sem, recv_sem, local_sem, stats_got, stats_send, stats_recv, core_send, core_recv = (
        scratch[-8:]
    )
    core = lax.axis_index(CORE)
    partners = []
    for lane in lanes:
        for axis, bits in lane.phases:
            partners += [(axis, bit) for bit in bits if (axis, bit) not in partners]
    partners.append((CORE, 0))
    index = {axis: lax.axis_index(axis) for axis, _ in partners}
    mine = {(axis, bit): (index[axis] >> bit) & 1 for axis, bit in partners}
    far = {key: index[key[0]] + (1 - 2 * mine[key]) * (1 << key[1]) for key in partners}
    barrier = pltpu.get_barrier_semaphore()
    peers = [{axis: far[axis, bit]} for axis, bit in partners if axis != GROUP]
    groups = lax.axis_size(GROUP)
    peers += [{GROUP: lax.rem(lax.axis_index(GROUP) + k, groups)} for k in range(1, groups)]
    for peer in peers:
        pl.semaphore_signal(
            barrier, inc=1, device_id=peer, device_id_type=pl.DeviceIdType.MESH
        )
    pl.semaphore_wait(barrier, len(peers))

    counter = itertools.count()

    def send(source, target, key):
        number = next(counter)
        copy = pltpu.make_async_remote_copy(
            src_ref=source,
            dst_ref=target,
            send_sem=send_sem.at[number],
            recv_sem=recv_sem.at[number],
            device_id={key[0]: far[key]},
            device_id_type=pl.DeviceIdType.MESH,
        )
        copy.start()
        return copy

    def place(axis, values):
        total = 0
        for bit, value in values.items():
            total = total + value * (1 << bit)
        return total

    def sum_stats():
        count = lax.axis_size(GROUP)
        me = lax.axis_index(GROUP)

        def copy(at, source, slot, target):
            return pltpu.make_async_remote_copy(
                src_ref=source,
                dst_ref=stats_got.at[slot],
                send_sem=stats_send.at[at],
                recv_sem=stats_recv.at[slot],
                device_id=target,
                device_id_type=pl.DeviceIdType.MESH,
            )

        for k in range(1, count):
            copy(k, stats_in, me, {GROUP: lax.rem(me + k, count)}).start()
        yield
        stats[...] = stats_in[...]
        for k in range(1, count):
            peer = lax.rem(me + k, count)
            copy(k, stats_in, peer, {GROUP: peer}).wait_recv()
            stats[...] += stats_got[peer]
        both = copy(0, stats, count, {CORE: far[CORE, 0]})
        both.start()
        yield
        both.wait()
        stats[...] += stats_got[count]
        for k in range(1, count):
            copy(k, stats_in, me, {GROUP: lax.rem(me + k, count)}).wait_send()

    summing = sum_stats()
    next(summing)

    def to_stage(number, source, kind, *at):
        spot = stage[kind].at[(core, *at)]
        return spot, pltpu.make_async_remote_copy(
            src_ref=source,
            dst_ref=spot,
            send_sem=core_send.at[number],
            recv_sem=core_recv.at[number],
            device_id={CORE: 1 - core},
            device_id_type=pl.DeviceIdType.MESH,
        )

    inner = stage[GATE].shape[3]
    wholes = []
    for number in range(second_pre.shape[1] // inner):
        kind, j = divmod(number, stage[GATE].shape[1])
        source = second_pre.at[:, pl.ds(number * inner, inner)]
        spot, copy = to_stage(len(lanes) + number, source, kind, j)
        wholes.append((copy, pltpu.make_async_copy(source, spot, core_send.at[len(lanes) + number])))
    for copy, here in wholes:
        @pl.when(core == 1)
        def _(here=here):
            here.start()

        @pl.when(core == 0)
        def _(copy=copy):
            copy.start()

    moved = []
    started = []
    states = []
    for number, lane in enumerate(lanes):
        count = len(lane.buffers)
        buffers, scratch = scratch[:count], scratch[count:]
        source = sources[lane.source]
        prefix = lane.prefix
        if isinstance(prefix, int):
            source = source.at[prefix]

        def part(at, source=source, prefix=prefix):
            if isinstance(prefix, tuple):
                return source.at[at, :, pl.ds(*prefix)]
            if prefix == INNER:
                return source.at[:, at]
            return source.at[at]

        axis, bits = lane.phases[0]
        total, arrived = buffers[0], buffers[1:]
        rest = [bit for bit in bits[1:]]
        pending = []
        for choice in itertools.product((0, 1), repeat=len(rest)):
            values = dict(zip(rest, choice))
            slot = sum(value << i for i, value in enumerate(choice))
            far_at = place(axis, {**values, bits[0]: 1 - mine[axis, bits[0]]})
            here_at = place(axis, {**values, bits[0]: mine[axis, bits[0]]})
            copy = send(part(far_at), arrived[0].at[slot], (axis, bits[0]))
            pending.append((copy, slot))
            started.append(copy)
            states.append((number, part(here_at), slot, total))
        lane_state = SimpleNamespace(total=total, arrived=arrived, pending=pending)
        lane.state = lane_state
    locals_ = {}
    for at, (number, here, slot, total) in enumerate(states):
        copy = pltpu.make_async_copy(here, total.at[slot], local_sem.at[at])
        copy.start()
        locals_[number, slot] = copy
    longest = max(sum(len(bits) for _, bits in lane.phases) for lane in lanes)
    for step in range(1, longest + 1):
        if step == 2:
            next(summing)
        for number, lane in enumerate(lanes):
            state = lane.state
            sizes = [len(bits) for _, bits in lane.phases]
            if step > sum(sizes):
                continue
            if step <= sizes[0]:
                axis, bits = lane.phases[0]
                resolved, rest = bits[:step], bits[step:]

                def slot_of(values):
                    found = 0
                    for i, bit in enumerate(bits[1:]):
                        found = found + values.get(bit, mine[axis, bit]) * (1 << i)
                    return found

                for copy, slot in state.pending:
                    copy.wait_recv()
                    if step == 1:
                        locals_[number, slot].wait()
                state.pending_next = []
                for choice in itertools.product((0, 1), repeat=len(rest)):
                    values = dict(zip(rest, choice))
                    got = sum(value << i for i, value in enumerate(choice))
                    add_slab(
                        state.total.at[slot_of(values)], state.arrived[step - 1].at[got]
                    )
                if rest:
                    following = rest[1:]
                    for choice in itertools.product((0, 1), repeat=len(following)):
                        values = dict(zip(following, choice))
                        got = sum(value << i for i, value in enumerate(choice))
                        values[rest[0]] = 1 - mine[axis, rest[0]]
                        copy = send(
                            state.total.at[slot_of(values)],
                            state.arrived[step].at[got],
                            (axis, rest[0]),
                        )
                        state.pending_next.append((copy, got))
                        started.append(copy)
                final = state.total.at[slot_of({})] if not rest else None
            else:
                axis, bits = lane.phases[1]
                done = step - sizes[0]
                rest = bits[done:]
                final = state.final
                for copy, _ in state.pending:
                    copy.wait_recv()
                state.pending_next = []
                for choice in itertools.product((0, 1), repeat=len(rest)):
                    values = dict(zip(rest, choice))
                    got = sum(value << i for i, value in enumerate(choice))
                    at = place(axis, {bit: values.get(bit, mine[axis, bit]) for bit in bits})
                    add_slab(final.at[at], state.arrived[step - 1].at[got])
                if not rest:
                    at = place(axis, {bit: mine[axis, bit] for bit in bits})
                    final = final.at[at]
            if final is not None and step >= sizes[0]:
                state.final = final
                if step == sum(sizes):
                    spot, copy = to_stage(number, final, *lane.target)
                    moved.append((lane.layer, copy))

                    @pl.when(core == lane.layer)
                    def _(spot=spot, final=final):
                        spot[...] = final[...]

                    @pl.when(core != lane.layer)
                    def _(copy=copy):
                        copy.start()
                elif step < sum(sizes):
                    axis, bits = lane.phases[1]
                    done = step - sizes[0]
                    bit, following = bits[done], bits[done + 1 :]
                    for choice in itertools.product((0, 1), repeat=len(following)):
                        values = dict(zip(following, choice))
                        got = sum(value << i for i, value in enumerate(choice))
                        at = place(
                            axis,
                            {
                                b: values.get(b, 1 - mine[axis, b] if b == bit else mine[axis, b])
                                for b in bits
                            },
                        )
                        copy = send(final.at[at], state.arrived[step].at[got], (axis, bit))
                        state.pending_next.append((copy, got))
                        started.append(copy)
            state.pending = state.pending_next
    for _ in summing:
        pass

    for copy, here in wholes:
        @pl.when(core == 1)
        def _(copy=copy, here=here):
            copy.wait_recv()
            here.wait()

        @pl.when(core == 0)
        def _(copy=copy):
            copy.wait_send()

    for layer, copy in moved:
        @pl.when(core == layer)
        def _(copy=copy):
            copy.wait_recv()

        @pl.when(core != layer)
        def _(copy=copy):
            copy.wait_send()

    for copy in started:
        copy.wait_send()


def sum_scatter(arrays, lanes, second_pre, stats, inner, collective):
    plans, scratch, shapes, copies, locals_ = [], [], [], 0, 0
    sizes = {}
    for source, prefix, phases, layer, target in lanes:
        shape = arrays[source].shape
        if isinstance(prefix, int):
            shape = shape[1:]
        elif prefix == INNER:
            shape = (shape[1], shape[0], *shape[2:])
        elif prefix is not None:
            shape = (*shape[:-1], prefix[1])
        buffers = [(shape[0] // 2, *shape[1:])]
        for step in range(1, len(phases[0][1]) + 1):
            buffers.append((shape[0] >> step, *shape[1:]))
            copies += shape[0] >> step
        locals_ += shape[0] // 2
        if len(phases) > 1:
            for step in range(1, len(phases[1][1]) + 1):
                buffers.append((shape[1] >> step, *shape[2:]))
                copies += shape[1] >> step
        plans.append(
            SimpleNamespace(
                source=source,
                prefix=prefix,
                phases=phases,
                buffers=buffers,
                layer=layer,
                target=target,
            )
        )
        sizes.setdefault(target[0], shape[-2:])
        scratch += [pltpu.VMEM(buffer, jnp.bfloat16) for buffer in buffers]
    half = second_pre.shape[1] // (2 * inner)
    experts_shape = (2, half, second_pre.shape[0], inner)
    shapes = [
        jax.ShapeDtypeStruct(shape, jnp.bfloat16)
        for shape in (
            experts_shape,
            experts_shape,
            (2, half, *sizes[DOWN]),
            (2, *sizes[QKV]),
            (2, *sizes[OUT]),
            (2, *sizes[SMALL]),
        )
    ] + [jax.ShapeDtypeStruct(stats.shape, jnp.float32)]
    scratch += [
        pltpu.SemaphoreType.DMA((copies,)),
        pltpu.SemaphoreType.DMA((copies,)),
        pltpu.SemaphoreType.DMA((locals_,)),
    ]
    hops = lax.axis_size(GROUP) + 1
    scratch += [
        pltpu.VMEM((hops, *stats.shape), jnp.float32),
        pltpu.SemaphoreType.DMA((hops,)),
        pltpu.SemaphoreType.DMA((hops,)),
        pltpu.SemaphoreType.DMA((len(lanes) + 2 * half,)),
        pltpu.SemaphoreType.DMA((len(lanes) + 2 * half,)),
    ]
    return pl.pallas_call(
        functools.partial(sum_scatter_kernel, (plans, len(arrays), copies)),
        out_shape=shapes,
        in_specs=[pl.BlockSpec(memory_space=pl.ANY)] * (len(arrays) + 1)
        + [pl.BlockSpec(memory_space=pltpu.VMEM)],
        out_specs=[pl.BlockSpec(memory_space=pltpu.VMEM)] * len(shapes),
        scratch_shapes=scratch,
        compiler_params=pltpu.CompilerParams(
            collective_id=collective, has_side_effects=True, vmem_limit_bytes=60 * 2**20
        ),
    )(*arrays, second_pre, stats)


def bits_of(axis):
    return list(range(lax.axis_size(axis).bit_length() - 1))


def expert_lanes(first, inner):
    up, down = [(GROUP, bits_of(GROUP))], [(GROUP, bits_of(GROUP)[::-1])]
    return [
        (first, ((2 * kind + j) * inner, inner), (up, down)[kind], 0, (kind, j))
        for j in range(2)
        for kind in (GATE, UP)
    ]


def down_lanes(first, layer):
    up, down = [(GROUP, bits_of(GROUP))], [(GROUP, bits_of(GROUP)[::-1])]
    return [(first, 0, up, layer, (DOWN, 0)), (first, 1, down, layer, (DOWN, 1))]


def dense_lanes(first):
    up, down, deep = bits_of(GROUP), bits_of(GROUP)[::-1], bits_of(LINE)
    return [
        (first, INNER, [(LINE, deep), (GROUP, up)], 0, (QKV,)),
        (first + 1, None, [(GROUP, down), (LINE, deep)], 0, (OUT,)),
        (first + 2, None, [(GROUP, up), (LINE, deep)], 0, (SMALL,)),
    ]


def attention_forward(inputs, weights, segment_row):
    gain_attn, w_query, w_key, w_value, w_out, gain_moe = weights[:6]
    length = inputs.shape[0]
    cosine_table, sine_table = rotary_tables(length)
    inverse_one = lax.rsqrt(jnp.mean(inputs * inputs, axis=-1, keepdims=True) + EPSILON)
    normed_one = (inputs * inverse_one * gain_attn).astype(jnp.bfloat16)
    queries = rotate(
        matmul(normed_one, w_query).reshape(length, H, HD), cosine_table, sine_table
    ).astype(jnp.bfloat16)
    key_rows = rotate(
        matmul(normed_one, w_key).reshape(length, KVH, HD), cosine_table, sine_table
    ).astype(jnp.bfloat16)
    values = matmul(normed_one, w_value).astype(jnp.bfloat16).reshape(length, KVH, HD)
    scores = attention_scores(queries, key_rows, segment_row)
    highest = jnp.max(scores, axis=-1, keepdims=True)
    exponent = jnp.exp(scores - highest)
    denominator = jnp.sum(exponent, axis=-1, keepdims=True)
    weight = exponent / denominator
    attended = jnp.einsum(
        "kgqs,skd->qkgd", weight.astype(jnp.bfloat16), values, preferred_element_type=jnp.float32
    )
    attended = attended.reshape(length, H * HD).astype(jnp.bfloat16)
    hidden = inputs + matmul(attended, w_out)
    inverse_two = lax.rsqrt(jnp.mean(hidden * hidden, axis=-1, keepdims=True) + EPSILON)
    normed_two = (hidden * inverse_two * gain_moe).astype(jnp.bfloat16)
    state = (inverse_one, normed_one, queries, key_rows, values, weight, attended, hidden, inverse_two, normed_two)
    return state


MESH = pl.DeviceIdType.MESH
PARTS = 3


def move_rows(sources, held, pieces, sems, compute, z, n, others):
    row_send, row_recv, sum_send, sum_recv = sems
    barrier = pltpu.get_barrier_semaphore()
    for k in range(1, n):
        peer = lax.rem(z + k, n)
        pl.semaphore_signal(barrier, inc=1, device_id={LINE: peer}, device_id_type=MESH)
    for peer in others:
        pl.semaphore_signal(barrier, inc=1, device_id=peer, device_id_type=MESH)
    pl.semaphore_wait(barrier, n - 1 + len(others))

    def row_copy(kind, way, hop, source=None):
        step = 1 - 2 * way
        block = jnp.clip(z - step * hop, 0, n - 1)
        peer = jnp.clip(z + step, 0, n - 1)
        return pltpu.make_async_remote_copy(
            src_ref=held[kind].at[block] if source is None else source,
            dst_ref=held[kind].at[block],
            send_sem=row_send.at[kind, way, hop],
            recv_sem=row_recv.at[kind, way, hop],
            device_id={LINE: peer},
            device_id_type=MESH,
        )

    def sends(way, hop):
        step = 1 - 2 * way
        block, peer = z - step * hop, z + step
        return (block >= 0) & (block < n) & (peer >= 0) & (peer < n)

    def arrives(way, hop):
        block = z - (1 - 2 * way) * (hop + 1)
        return (block >= 0) & (block < n)

    def start(kind):
        for way in range(2):
            @pl.when(sends(way, 0))
            def _():
                row_copy(kind, way, 0, sources[kind]).start()

    def take(hop):
        for kind in range(len(held)):
            for way in range(2):
                @pl.when(arrives(way, hop))
                def _():
                    row_copy(kind, way, hop).wait_recv()

                @pl.when(sends(way, hop + 1) & (hop + 1 < n - 1))
                def _():
                    row_copy(kind, way, hop + 1).start()

    def waits(way, block):
        peer, last = z - (1 - 2 * way), (n - 1) * (1 - way)
        return (peer >= 0) & (peer < n) & ((block != last) | (peer != n - 1 - last))

    def far_copy(p):
        mine, arrived = pieces[p]
        block, way = n - 1 - z, jnp.where(z == 0, 1, 0)
        return pltpu.make_async_remote_copy(
            src_ref=mine(block),
            dst_ref=arrived(way, block),
            send_sem=sum_send.at[block, p],
            recv_sem=sum_recv.at[way, block, p],
            device_id={LINE: block},
            device_id_type=MESH,
        )

    def sum_copy(way, block, p):
        mine, arrived = pieces[p]
        return pltpu.make_async_remote_copy(
            src_ref=mine(block),
            dst_ref=arrived(way, block),
            send_sem=sum_send.at[block, p],
            recv_sem=sum_recv.at[way, block, p],
            device_id={LINE: jnp.clip(z + 1 - 2 * way, 0, n - 1)},
            device_id_type=MESH,
        )

    def sent(block, p):
        way = jnp.where(block > z, 0, 1)
        far = ((z == 0) | (z == n - 1)) & (block == n - 1 - z)

        @pl.when(far)
        def _():
            far_copy(p).start()

        @pl.when((block != z) & jnp.logical_not(far) & jnp.logical_not(waits(way, block)))
        def _():
            sum_copy(way, block, p).start()

    def run():
        def both(hop):
            return (hop >= 0) & (z - 1 - hop >= 0) & (z + 1 + hop < n)

        def turn(k, carry):
            hop = lax.div(k + 1, 2) - 1
            block = z + (1 + hop) * (1 - 2 * lax.rem(k, 2))
            odd = lax.rem(k, 2) == 1

            @pl.when(odd & jnp.logical_not(both(hop - 1)))
            def _():
                take(hop)

            @pl.when(jnp.logical_not(odd) & both(hop) & (hop + 1 < n - 1))
            def _():
                take(hop + 1)

            @pl.when((block >= 0) & (block < n))
            def _():
                compute(block, sent)

            return carry

        lax.fori_loop(0, 2 * n - 1, turn, 0)

        first = jnp.where(2 * z < n, 0, 1)
        for way in (first, 1 - first):
            for k in range(1, n):
                block = z + (1 - 2 * way) * k

                @pl.when(waits(way, block) & (block >= 0) & (block < n))
                def _():
                    for p, (mine, arrived) in enumerate(pieces):
                        sum_copy(way, block, p).wait_recv()
                        own, other = mine(block), arrived(way, block)
                        own[...] = (
                            own[...].astype(jnp.float32) + other[...].astype(jnp.float32)
                        ).astype(jnp.bfloat16)
                        sum_copy(way, block, p).start()

    def collect(add):
        for way in range(2):
            for p, (_, arrived) in enumerate(pieces):
                sum_copy(way, z, p).wait_recv()
                add(p, arrived(way, z)[...].astype(jnp.float32))

    def finish():
        for kind in range(len(held)):
            for way in range(2):
                for hop in range(n - 1):
                    @pl.when(sends(way, hop))
                    def _():
                        row_copy(kind, way, hop).wait_send()
        for k in range(1, n):
            for p in range(len(pieces)):
                sum_copy(0, lax.rem(z + k, n), p).wait_send()

    return start, run, collect, finish


def row_pieces(sums, returned, parts):
    width = sums.shape[2] // parts

    def piece(p):
        at = pl.ds(p * width, width)
        return (
            lambda block: sums.at[block, :, at],
            lambda way, block: returned.at[way, block, :, at],
        )

    return [piece(p) for p in range(parts)]


def fetch_weights(layer, own, other, places, sem):
    count = places[0].shape[0]
    mine = lax.axis_index(CORE) == layer

    def copy(group, kind, e):
        return pltpu.make_async_copy(
            group[kind].at[e], places[kind].at[e], sem.at[kind * count + e]
        )

    for kind in range(len(places)):
        for e in range(count):
            @pl.when(mine)
            def _():
                copy(own, kind, e).start()

            @pl.when(jnp.logical_not(mine))
            def _():
                copy(other, kind, e).start()

    def wait():
        for kind in range(len(places)):
            for e in range(count):
                copy(own, kind, e).wait()

    return wait


def sigmoid_of(value):
    return 1.0 / (1.0 + jnp.exp(-value))


def column_of(block, column):
    here = lax.broadcasted_iota(jnp.int32, block.shape, 1) == column
    return jnp.sum(jnp.where(here, block, 0.0), axis=1, keepdims=True)


def experts_forward_kernel(
    layer, experts, x, mask, hidden, router, *refs
):
    own, other, refs = refs[:3], refs[3:6], refs[6:]
    own_dense, other_dense, refs = refs[:4], refs[4:8], refs[8:]
    out, rows, gates_all, gates, gate_keep, up_keep, gated, stats = refs[:8]
    placed, place_sem = refs[8:12], refs[-1]
    passing, refs = refs[-5:-1], refs[:8] + refs[12:-5]
    w_gate, w_up, w_down, sums, returned, mixed, total, stats_all = refs[8:16]
    weight_sem, *sems = refs[16:]
    n, held = rows.shape[0], w_gate.shape[0]
    z = lax.axis_index(LINE)

    def compute(block, sent):
        picked = rows[block]
        gate_block = gates_all[block].astype(jnp.float32)

        def one(e, carry):
            gate_pre = jnp.dot(picked, w_gate[e], preferred_element_type=jnp.float32)
            up_pre = jnp.dot(picked, w_up[e], preferred_element_type=jnp.float32)
            gate_keep[e, block] = gate_pre.astype(jnp.bfloat16)
            up_keep[e, block] = up_pre.astype(jnp.bfloat16)
            active = gate_pre * sigmoid_of(gate_pre) * up_pre
            share = (column_of(gate_block, z * held + e) * active).astype(jnp.bfloat16)
            inner = share.shape[1]
            gated[block, :, pl.ds(pl.multiple_of(e * inner, inner), inner)] = share
            mixed[e] = share
            return carry

        lax.fori_loop(0, held, one, 0)
        width = out.shape[1] // PARTS
        for part in range(PARTS):
            at = pl.ds(part * width, width)
            result = jnp.zeros((out.shape[0], width), jnp.float32)
            for e in range(held):
                result += jnp.dot(mixed[e], w_down[e, :, at], preferred_element_type=jnp.float32)

            @pl.when(block == z)
            def _():
                total[:, at] = hidden[:, at] + result

            @pl.when(block != z)
            def _():
                sums[block, :, at] = result.astype(jnp.bfloat16)

            sent(block, part)

    own_gates = gates_all.at[z]
    start, run, collect, finish = move_rows(
        (x, own_gates, stats_all.at[z]),
        (rows, gates_all, stats_all),
        row_pieces(sums, returned, PARTS),
        sems,
        compute,
        z,
        n,
        [],
    )
    start(0)
    wait_weights = fetch_weights(layer, own, other, (w_gate, w_up, w_down), weight_sem)
    here = lax.axis_index(CORE) == 1 - layer

    def place_copy(group, i):
        return pltpu.make_async_copy(group[i], passing[i], place_sem.at[0, i])

    def place_out(i):
        return pltpu.make_async_copy(passing[i], placed[i], place_sem.at[1, i])

    for i in range(4):
        @pl.when(here)
        def _():
            place_copy(own_dense, i).start()

        @pl.when(jnp.logical_not(here))
        def _():
            place_copy(other_dense, i).start()

    logits = jnp.dot(x[...], router[...], preferred_element_type=jnp.float32)
    chosen = mask[...] > 0
    highest = jnp.max(jnp.where(chosen, logits, MASKED), axis=1, keepdims=True)
    exponent = jnp.where(chosen, jnp.exp(logits - highest), 0.0)
    gates[...] = exponent / jnp.sum(exponent, axis=1, keepdims=True)
    own_gates[...] = gates[...].astype(jnp.bfloat16)
    start(1)
    real = lax.broadcasted_iota(jnp.int32, logits.shape, 1) < experts
    highest = jnp.max(jnp.where(real, logits, MASKED), axis=1, keepdims=True)
    exponent = jnp.where(real, jnp.exp(logits - highest), 0.0)
    chance = exponent / jnp.sum(exponent, axis=1, keepdims=True)
    line = lax.broadcasted_iota(jnp.int32, stats.shape, 0)
    stats_all[z] = jnp.where(
        line == 0,
        jnp.sum(chance, axis=0, keepdims=True),
        jnp.where(line == 1, jnp.sum(mask[...], axis=0, keepdims=True), 0.0),
    )
    start(2)
    rows[z] = x[...]
    wait_weights()
    run()
    for i in range(4):
        place_copy(own_dense, i).wait()
        place_out(i).start()
    stats[...] = jnp.sum(stats_all[...], axis=0)
    width = out.shape[1] // PARTS

    def add(p, value):
        total[:, p * width : (p + 1) * width] += value

    collect(add)
    out[...] = total[...].astype(jnp.bfloat16)
    finish()
    for i in range(4):
        place_out(i).wait()


def experts_backward_kernel(layer, grad, gates, gate_keep, up_keep, *refs):
    own, other, saved_rows, saved_gated, refs = refs[:3], refs[3:6], refs[6], refs[7], refs[8:]
    out, out_gates, rows_both, gated_both, grad_both, pre_both = refs[:6]
    w_gate, w_up, w_down, sums, sum_gates, returned, returned_gates, away, dots = refs[6:15]
    weight_sem, core_send, core_recv, core_local, *sems = refs[15:]
    n, held = gates.shape[0], w_gate.shape[0]
    half, inner = held // 2, w_gate.shape[2]
    core = lax.axis_index(CORE)
    z = lax.axis_index(LINE)
    turned_dims = (((1,), (1,)), ((), ()))
    rows = grad_both.at[core]

    def to_core(number, source, target):
        return pltpu.make_async_remote_copy(
            src_ref=source,
            dst_ref=target,
            send_sem=core_send.at[number],
            recv_sem=core_recv.at[number],
            device_id={CORE: 1 - core},
            device_id_type=MESH,
        )

    def block_copies(block):
        return (
            to_core(2 + block, rows.at[block], rows.at[block]),
            to_core(2 + n + block, away.at[block], pre_both.at[core, block]),
        )

    def columns(at):
        return pl.ds(pl.multiple_of(at * half * inner, half * inner), half * inner)

    def whole_copies():
        return (
            to_core(0, saved_rows, rows_both.at[core]),
            to_core(1, saved_gated.at[:, :, columns(1 - core)], gated_both.at[core]),
        )

    def local_copies():
        return (
            pltpu.make_async_copy(saved_rows, rows_both.at[core], core_local.at[0]),
            pltpu.make_async_copy(
                saved_gated.at[:, :, columns(core)], gated_both.at[core], core_local.at[1]
            ),
        )

    def compute(block, sent):
        picked = rows[block]
        gate_block = gates[block].astype(jnp.float32)
        dots[...] = jnp.zeros(dots.shape, jnp.float32)

        def one(e, place, j):
            raw = lax.dot_general(
                picked, w_down[e], turned_dims, preferred_element_type=jnp.float32
            )
            gate_pre = gate_keep[e, block].astype(jnp.float32)
            up_pre = up_keep[e, block].astype(jnp.float32)
            sigmoid = sigmoid_of(gate_pre)
            silu = gate_pre * sigmoid
            column = z * held + e
            dot = jnp.sum(raw * (silu * up_pre), axis=1, keepdims=True)
            here = lax.broadcasted_iota(jnp.int32, dots.shape, 1) == column
            dots[...] += jnp.where(here, dot, 0.0)
            active = column_of(gate_block, column) * raw
            place[:, pl.ds(pl.multiple_of(j * inner, inner), inner)] = (
                active * up_pre * sigmoid * (1.0 + gate_pre * (1.0 - sigmoid))
            ).astype(jnp.bfloat16)
            place[:, pl.ds(pl.multiple_of((half + j) * inner, inner), inner)] = (
                active * silu
            ).astype(jnp.bfloat16)

        def own_half(j, carry):
            one(core * half + j, pre_both.at[core, block], j)
            return carry

        def other_half(j, carry):
            one((1 - core) * half + j, away.at[block], j)
            return carry

        lax.fori_loop(0, half, other_half, 0)
        for copy in block_copies(block):
            copy.start()
        lax.fori_loop(0, half, own_half, 0)
        sum_gates[block] = dots[...].astype(jnp.bfloat16)

        @pl.when(block == z)
        def _():
            out_gates[...] = dots[...]

        sent(block, PARTS)
        width = out.shape[1] // PARTS
        for part in range(PARTS):
            at = pl.ds(part * width, width)
            result = jnp.zeros((out.shape[0], width), jnp.float32)
            for place, side in ((away.at[block], 1 - core), (pre_both.at[core, block], core)):
                for kind, right in enumerate((w_gate, w_up)):
                    for j in range(half):
                        left = place[:, pl.ds((kind * half + j) * inner, inner)]
                        result += lax.dot_general(
                            left,
                            right[side * half + j, at, :],
                            turned_dims,
                            preferred_element_type=jnp.float32,
                        )

            @pl.when(block == z)
            def _():
                out[:, at] = result

            @pl.when(block != z)
            def _():
                sums[block, :, at] = result.astype(jnp.bfloat16)

            sent(block, part)

    gate_piece = (lambda block: sum_gates.at[block], lambda way, block: returned_gates.at[way, block])
    start, run, collect, finish = move_rows(
        (grad,),
        (rows,),
        row_pieces(sums, returned, PARTS) + [gate_piece],
        sems,
        compute,
        z,
        n,
        [{CORE: 1 - core}],
    )
    start(0)
    wait_weights = fetch_weights(layer, own, other, (w_gate, w_up, w_down), weight_sem)
    for copy in whole_copies() + local_copies():
        copy.start()
    rows[z] = grad[...]
    wait_weights()
    run()
    width = out.shape[1] // PARTS

    def add(p, value):
        if p == PARTS:
            out_gates[...] += value
        else:
            out[:, p * width : (p + 1) * width] += value

    collect(add)
    finish()
    for copy in local_copies():
        copy.wait()
    for copy in whole_copies():
        copy.wait()
    for block in range(n):
        for copy in block_copies(block):
            copy.wait()


def exchange_scratch(n, kinds_out, kinds_back):
    return [
        pltpu.SemaphoreType.DMA((kinds_out, 2, n)),
        pltpu.SemaphoreType.DMA((kinds_out, 2, n)),
        pltpu.SemaphoreType.DMA((n, kinds_back)),
        pltpu.SemaphoreType.DMA((2, n, kinds_back)),
    ]


def expert_call(kernel, operands, own, other, extra, shapes, scratch, collective, loose=0):
    vmem, free = pl.BlockSpec(memory_space=pltpu.VMEM), pl.BlockSpec(memory_space=pl.ANY)
    weights = [pltpu.VMEM(array.shape, jnp.bfloat16) for array in own]
    return pl.pallas_call(
        kernel,
        out_shape=shapes,
        in_specs=[vmem] * len(operands) + [free] * (6 + len(extra)),
        out_specs=[vmem] * (len(shapes) - loose) + [free] * loose,
        scratch_shapes=weights + scratch,
        compiler_params=pltpu.CompilerParams(
            collective_id=collective, has_side_effects=True, vmem_limit_bytes=46 * 2**20
        ),
        cost_estimate=pl.CostEstimate(
            flops=5 * 10**10, bytes_accessed=10**8, transcendentals=0
        ),
    )(*operands, *own, *other, *extra)


def experts_forward(
    layer, normed_two, mask, hidden, router, own, other, own_dense, other_dense, experts
):
    n, held = lax.axis_size(LINE), own[0].shape[0]
    length, width = normed_two.shape
    inner = own[0].shape[2]
    low, full = jnp.bfloat16, jnp.float32
    kept = jax.ShapeDtypeStruct((held, n, length, inner), low)
    shapes = [
        jax.ShapeDtypeStruct((length, width), low),
        jax.ShapeDtypeStruct((n, length, width), low),
        jax.ShapeDtypeStruct((n, length, COLUMNS), low),
        jax.ShapeDtypeStruct((length, COLUMNS), full),
        kept,
        kept,
        jax.ShapeDtypeStruct((n, length, held * inner), low),
        jax.ShapeDtypeStruct((8, COLUMNS), full),
    ] + [jax.ShapeDtypeStruct(array.shape, low) for array in own_dense]
    scratch = [
        pltpu.VMEM((n, length, width), low),
        pltpu.VMEM((2, n, length, width), low),
        pltpu.VMEM((held, length, inner), low),
        pltpu.VMEM((length, width), full),
        pltpu.VMEM((n, 8, COLUMNS), full),
        pltpu.SemaphoreType.DMA((3 * held,)),
    ] + exchange_scratch(n, 3, PARTS)
    scratch += [pltpu.VMEM(array.shape, low) for array in own_dense]
    scratch.append(pltpu.SemaphoreType.DMA((2, 4)))
    kernel = functools.partial(experts_forward_kernel, layer, experts)
    return expert_call(
        kernel,
        (normed_two, mask, hidden, router),
        own,
        other,
        (*own_dense, *other_dense),
        shapes,
        scratch,
        1 + layer,
        4,
    )


def experts_backward(layer, grad_low, gates, gate_keep, up_keep, rows, gated, own, other):
    held, n, length, inner = gate_keep.shape
    width = grad_low.shape[1]
    low, full = jnp.bfloat16, jnp.float32
    shapes = [
        jax.ShapeDtypeStruct((length, width), full),
        jax.ShapeDtypeStruct((length, COLUMNS), full),
        jax.ShapeDtypeStruct((2, n, length, width), low),
        jax.ShapeDtypeStruct((2, n, length, held // 2 * inner), low),
        jax.ShapeDtypeStruct((2, n, length, width), low),
        jax.ShapeDtypeStruct((2, n, length, held * inner), low),
    ]
    scratch = [
        pltpu.VMEM((n, length, width), low),
        pltpu.VMEM((n, length, COLUMNS), low),
        pltpu.VMEM((2, n, length, width), low),
        pltpu.VMEM((2, n, length, COLUMNS), low),
        pltpu.VMEM((n, length, held * inner), low),
        pltpu.VMEM((length, COLUMNS), full),
        pltpu.SemaphoreType.DMA((3 * held,)),
        pltpu.SemaphoreType.DMA((2 + 2 * n,)),
        pltpu.SemaphoreType.DMA((2 + 2 * n,)),
        pltpu.SemaphoreType.DMA((2,)),
    ] + exchange_scratch(n, 1, PARTS + 1)
    kernel = functools.partial(experts_backward_kernel, layer)
    return expert_call(
        kernel,
        (grad_low, gates, gate_keep, up_keep),
        own,
        other,
        (rows, gated),
        shapes,
        scratch,
        3 + layer,
    )


def attention_backward(grad_hidden, inputs, state, weights):
    gain_attn, w_query, w_key, w_value, w_out, gain_moe = weights[:6]
    (inverse_one, normed_one, queries, key_rows, values, weight, attended, hidden, inverse_two, normed_two) = state
    length = inputs.shape[0]
    grad_branch = grad_hidden.astype(jnp.bfloat16)
    grad_attended = jnp.einsum("td,cd->tc", grad_branch, w_out, preferred_element_type=jnp.float32)
    grad_attended = grad_attended.astype(jnp.bfloat16).reshape(length, KVH, H // KVH, HD)
    grad_weight = jnp.einsum(
        "qkgd,skd->kgqs", grad_attended, values, preferred_element_type=jnp.float32
    )
    grad_values = jnp.einsum(
        "kgqs,qkgd->skd",
        weight.astype(jnp.bfloat16),
        grad_attended,
        preferred_element_type=jnp.float32,
    )
    grad_values = grad_values.astype(jnp.bfloat16).reshape(length, KVH * HD)
    grad_scores = (
        weight * (grad_weight - jnp.sum(weight * grad_weight, axis=-1, keepdims=True))
    ).astype(jnp.bfloat16)
    score_scale = HD ** (-0.5)
    grouped = queries.reshape(length, KVH, H // KVH, HD)
    grad_queries = jnp.einsum(
        "kgqs,skd->qkgd", grad_scores, key_rows, preferred_element_type=jnp.float32
    )
    grad_queries = grad_queries.reshape(length, H, HD) * score_scale
    grad_keys = (
        jnp.einsum("kgqs,qkgd->skd", grad_scores, grouped, preferred_element_type=jnp.float32)
        * score_scale
    )
    cosine_table, sine_table = rotary_tables(length)
    grad_query_pre = (
        unrotate(grad_queries, cosine_table, sine_table)
        .reshape(length, H * HD)
        .astype(jnp.bfloat16)
    )
    grad_key_pre = (
        unrotate(grad_keys, cosine_table, sine_table).reshape(length, KVH * HD).astype(jnp.bfloat16)
    )
    grad_normed_one = (
        jnp.einsum("tq,cq->tc", grad_query_pre, w_query, preferred_element_type=jnp.float32)
        + jnp.einsum("tq,cq->tc", grad_key_pre, w_key, preferred_element_type=jnp.float32)
        + jnp.einsum("tq,cq->tc", grad_values, w_value, preferred_element_type=jnp.float32)
    )
    grad_norm_one, grad_gain_attn = norm_back(grad_normed_one, inputs, inverse_one, gain_attn)
    grad_inputs = grad_hidden + grad_norm_one
    grad_qkv = jnp.concatenate([grad_query_pre, grad_key_pre, grad_values], axis=1)
    return grad_inputs, grad_gain_attn, grad_qkv, grad_branch


def turned(left, right):
    return jnp.einsum("tc,tq->cq", left, right, preferred_element_type=jnp.float32)


def body(tokens, cotangent, segments, routes, *weight_arrays):
    core = lax.axis_index(CORE)
    first = core == 0
    experts = weight_arrays[6].shape[2]
    w_gate = weight_arrays[7]
    held = w_gate.shape[1]
    own = [array[0] for array in weight_arrays]
    other = [swapped(array) for array in own]
    weights = [
        [jnp.where(first, a, b) for a, b in zip(own[:7], other[:7])],
        [jnp.where(first, b, a) for a, b in zip(own[:7], other[:7])],
    ]
    inputs_low = lax.dynamic_slice_in_dim(tokens, core * SEQ, SEQ, 0)
    grad_low = lax.dynamic_slice_in_dim(cotangent, core * SEQ, SEQ, 0)
    segment_row = lax.dynamic_index_in_dim(segments, core, 0, keepdims=False)
    mine = lax.dynamic_slice_in_dim(routes[0], core * SEQ, SEQ, 0)
    got = swapped(lax.dynamic_slice_in_dim(routes[0], (1 - core) * SEQ, SEQ, 0))
    routes_here = jnp.stack([jnp.where(first, mine, got), jnp.where(first, got, mine)])
    masks = multi_hot(routes_here, COLUMNS)
    own_experts, other_experts = own[7:], other[7:]

    saved, outs, stats = [], [], []
    for s in range(2):
        inputs = inputs_low.astype(jnp.float32)
        state = attention_forward(inputs, weights[s], segment_row)
        hidden, normed_two = state[7], state[9]
        router = jnp.pad(weights[s][6], ((0, 0), (0, COLUMNS - experts)))
        inputs_low, *expert_state, stat, query, key, value, out = experts_forward(
            s,
            normed_two,
            masks[s],
            hidden,
            router,
            own_experts,
            other_experts,
            own[1:5],
            other[1:5],
            experts,
        )
        weights[1 - s][1:5] = [query, key, value, out]
        outs.append(inputs_low)
        stats.append(stat)
        saved.append((inputs, state, expert_state))

    grads = [None, None]
    input_grads = [None, None]
    for s in (1, 0):
        inputs, state, expert_state = saved[s]
        (inverse_one, normed_one, _, _, _, _, attended, hidden, inverse_two, normed_two) = state
        rows_all, gates_all, gates, gate_keep, up_keep, gated = expert_state
        gain_moe, w_router = weights[s][5], weights[s][6]
        grad_sum, grad_gates, rows_both, gated_both, grad_both, pre_both = experts_backward(
            s,
            grad_low,
            gates_all,
            gate_keep,
            up_keep,
            rows_all,
            gated,
            own_experts,
            other_experts,
        )
        inner = w_gate.shape[3]
        grad_gate_up = turned(
            rows_both.reshape(-1, D), pre_both.reshape(-1, held * inner)
        ).astype(jnp.bfloat16)
        if s == 1:
            grad_sum, grad_gate_up = lax.optimization_barrier((grad_sum, grad_gate_up))
            second_pre = lax.psum_scatter(grad_gate_up, GROUP, scatter_dimension=0, tiled=True)
        else:
            grad_sum, second_pre = lax.optimization_barrier((grad_sum, second_pre))
        gates, grad_gates = gates[:, :experts], grad_gates[:, :experts]
        grad_chosen = gates * (grad_gates - jnp.sum(gates * grad_gates, axis=-1, keepdims=True))
        grad_logits = grad_chosen.astype(jnp.bfloat16)
        grad_normed_two = grad_sum + jnp.einsum(
            "te,de->td", grad_logits, w_router, preferred_element_type=jnp.float32
        )
        grad_norm_two, grad_gain_moe = norm_back(grad_normed_two, hidden, inverse_two, gain_moe)
        grad_hidden = grad_low.astype(jnp.float32) + grad_norm_two
        grad_inputs, grad_gain_attn, grad_qkv, grad_branch = attention_backward(
            grad_hidden, inputs, state, weights[s]
        )
        if s == 1:
            grad_inputs, gated_both = lax.optimization_barrier((grad_inputs, gated_both))
        grad_down = turned(
            gated_both.reshape(-1, held // 2 * inner), grad_both.reshape(-1, D)
        ).astype(jnp.bfloat16)

        def halves(array):
            width = array.shape[1] // 2
            return (
                lax.dynamic_slice_in_dim(array, core * width, width, 1),
                lax.dynamic_slice_in_dim(array, (1 - core) * width, width, 1),
            )
        qkv_keep, qkv_send = halves(grad_qkv)
        branch_keep, branch_send = halves(grad_branch)
        packed = swapped(jnp.concatenate([normed_one, attended, qkv_send, branch_send], axis=1))
        normed_got, attended_got = packed[:, :D], packed[:, D : 2 * D]
        qkv_got = packed[:, 2 * D : 2 * D + qkv_send.shape[1]]
        branch_got = packed[:, 2 * D + qkv_send.shape[1] :]
        grad_w_qkv = turned(
            jnp.concatenate([normed_one, normed_got]), jnp.concatenate([qkv_keep, qkv_got])
        ).astype(jnp.bfloat16)
        grad_w_out = turned(
            jnp.concatenate([attended, attended_got]), jnp.concatenate([branch_keep, branch_got])
        ).astype(jnp.bfloat16)
        grad_w_router = turned(normed_two, grad_logits)
        small = jnp.concatenate(
            [grad_gain_attn[:, None], grad_gain_moe[:, None], grad_w_router], axis=1
        ).astype(jnp.bfloat16)
        small = jnp.pad(small, ((0, 0), (0, COLUMNS - small.shape[1])))
        if s == 1:
            grad_inputs, grad_down, grad_w_qkv, grad_w_out = lax.optimization_barrier(
                (grad_inputs, grad_down, grad_w_qkv, grad_w_out)
            )
            dense = jnp.concatenate([grad_w_qkv, grad_w_out], axis=1)
            second_dense = lax.psum_scatter(dense, GROUP, scatter_dimension=0, tiled=True)
        grads[s] = (grad_gate_up, grad_down, grad_w_qkv, grad_w_out, small)
        input_grads[s] = grad_inputs
        grad_low = grad_inputs.astype(jnp.bfloat16)

    dp, deep = lax.axis_size(GROUP), lax.axis_size(LINE)
    half, inner = held // 2, w_gate.shape[3]
    grad_gate_up, grad_down, grad_w_qkv, grad_w_out, small = grads[0]
    arrays = [
        grad_gate_up.reshape(dp, D // dp, held * inner),
        grad_down.reshape(half, dp, inner // dp, D),
    ]
    lanes = expert_lanes(0, inner) + down_lanes(1, 0) + down_lanes(2, 1) + dense_lanes(3)
    arrays.append(grads[1][1].reshape(half, dp, inner // dp, D))
    for array in (grad_w_qkv, grad_w_out, small):
        arrays.append(array.reshape(dp, deep, array.shape[0] // (dp * deep), array.shape[1]))
    width = grad_w_qkv.shape[1]
    for array, kind in ((second_dense[:, :width], QKV), (second_dense[:, width:], OUT)):
        lanes.append((len(arrays), None, [(LINE, bits_of(LINE))], 1, (kind,)))
        arrays.append(array.reshape(deep, array.shape[0] // deep, array.shape[1]))
    lanes.append((len(arrays), None, dense_lanes(0)[2][2], 1, (SMALL,)))
    small = grads[1][4]
    arrays.append(small.reshape(dp, deep, small.shape[0] // (dp * deep), small.shape[1]))
    *grads, qkv, out, small, stats = sum_scatter(
        arrays, lanes, second_pre, jnp.concatenate(stats, axis=0), inner, 0
    )
    full = jnp.float32
    w_gate_grad, w_up_grad, w_down_grad = (
        grad.reshape(held, *grad.shape[2:]).astype(full) for grad in grads
    )
    qkv = jnp.concatenate([qkv[0], qkv[1]], axis=1).astype(full)
    grad_w_out = jnp.concatenate([out[0], out[1]], axis=1).astype(full)
    small = small[0].astype(full) + small[1].astype(full)
    heads, kv = H * HD, KVH * HD
    stats = lax.dynamic_index_in_dim(stats.reshape(2, 8, COLUMNS), core, 0)
    token_total = SEQ * lax.axis_size((CORE, GROUP, LINE))
    counts, chances = stats[:, 1, :experts], stats[:, 0, :experts]
    balance = experts * (counts / (token_total * TOPK) * chances / token_total)
    out_keep = jnp.where(first, outs[0], outs[1])
    out_got = swapped(jnp.where(first, outs[1], outs[0]))
    layer_out = jnp.where(
        first, jnp.concatenate([out_keep, out_got]), jnp.concatenate([out_got, out_keep])
    )
    low_one = input_grads[1].astype(jnp.bfloat16).astype(jnp.float32)
    grad_keep = jnp.where(first, input_grads[0], low_one)
    grad_got = swapped(jnp.where(first, low_one, input_grads[0]))
    input_grad = jnp.where(
        first, jnp.concatenate([grad_keep, grad_got]), jnp.concatenate([grad_got, grad_keep])
    )
    results = (
        layer_out,
        input_grad,
        small[:, 0],
        qkv[:, :heads],
        qkv[:, heads : heads + kv],
        qkv[:, heads + kv :],
        grad_w_out,
        small[:, 1],
        small[:, 2 : 2 + experts],
        w_gate_grad,
        w_up_grad,
        w_down_grad,
    )
    return tuple(result[None] for result in results) + (balance,)


def solution(mesh):
    return jax.shard_map(
        body,
        mesh=mesh,
        in_specs=(
            P((GROUP, LINE), None),
            P((GROUP, LINE), None),
            P((GROUP, LINE), None),
            P(CORE, (GROUP, LINE), None),
            P(CORE, None),
            P(CORE, None, None),
            P(CORE, None, None),
            P(CORE, None, None),
            P(CORE, None, None),
            P(CORE, None),
            P(CORE, None, None),
            P(CORE, LINE, None, None),
            P(CORE, LINE, None, None),
            P(CORE, LINE, None, None),
        ),
        out_specs=(
            P(CORE, (GROUP, LINE), None),
            P(CORE, (GROUP, LINE), None),
            P(CORE, (GROUP, LINE)),
            P(CORE, (GROUP, LINE), None),
            P(CORE, (GROUP, LINE), None),
            P(CORE, (GROUP, LINE), None),
            P(CORE, (GROUP, LINE), None),
            P(CORE, (GROUP, LINE)),
            P(CORE, (GROUP, LINE), None),
            P(CORE, LINE, GROUP, None),
            P(CORE, LINE, GROUP, None),
            P(CORE, LINE, GROUP, None),
            P(CORE, None),
        ),
        check_vma=False,
    )
```

```python
import functools
import itertools
from types import SimpleNamespace

import jax
import jax.numpy as jnp
from jax import lax
from jax.experimental import pallas as pl
from jax.experimental.pallas import tpu as pltpu
from jax.sharding import PartitionSpec as P

D = 1536
H = 24
KVH = 8
HD = 64
TOPK = 8
SEQ = 96


EPSILON = 1e-05
THETA = 10000.0
MASKED = -1e30
COLUMNS = 128
GATE, UP, DOWN, QKV, OUT, SMALL = range(6)
CORE, GROUP, LINE = "section", "dp", "expert"
INNER = "inner"


def matmul(left_side, right_side):
    return jnp.dot(left_side, right_side, preferred_element_type=jnp.float32)


def rotary_tables(length):
    half_width = HD // 2
    position = jnp.arange(length, dtype=jnp.float32)[:, None]
    freq_rate = THETA ** (-jnp.arange(half_width, dtype=jnp.float32) / half_width)
    angles = position * freq_rate[None, :]
    return (jnp.cos(angles)[:, None, :], jnp.sin(angles)[:, None, :])


def rotate(tensor, cosine_table, sine_table):
    half_width = HD // 2
    first_half = tensor[..., :half_width]
    second_half = tensor[..., half_width:]
    return jnp.concatenate(
        [
            first_half * cosine_table - second_half * sine_table,
            second_half * cosine_table + first_half * sine_table,
        ],
        axis=-1,
    )


def unrotate(gradient, cosine_table, sine_table):
    half_width = HD // 2
    first_half = gradient[..., :half_width]
    second_half = gradient[..., half_width:]
    return jnp.concatenate(
        [
            first_half * cosine_table + second_half * sine_table,
            second_half * cosine_table - first_half * sine_table,
        ],
        axis=-1,
    )


def norm_back(grad_normed, tensor, inverse, gain_vector):
    scaled = grad_normed * gain_vector
    grad_gain = jnp.sum(grad_normed * tensor * inverse, axis=0)
    grad_tensor = inverse * scaled - tensor * inverse**3 * jnp.mean(
        scaled * tensor, axis=-1, keepdims=True
    )
    return (grad_tensor, grad_gain)


def attention_scores(queries, key_rows, segment_row):
    length = queries.shape[0]
    grouped = queries.reshape(length, KVH, H // KVH, HD)
    scores = jnp.einsum(
        "qkgd,skd->kgqs", grouped, key_rows, preferred_element_type=jnp.float32
    ) * HD ** (-0.5)
    position = jnp.arange(length)
    allowed = (position[None, :] <= position[:, None]) & (
        segment_row[:, None] == segment_row[None, :]
    )
    return jnp.where(allowed[None, None], scores, MASKED)


def multi_hot(route_rows, experts):
    columns = jnp.arange(experts, dtype=jnp.int32)
    return jnp.sum(
        (route_rows[..., None] == columns).astype(jnp.float32), axis=-2
    )


def swapped(array):
    return lax.ppermute(array, CORE, [(0, 1), (1, 0)])


def add_slab(total, arrived):
    *lead, rows, _ = total.shape
    step = 16 if rows % 16 == 0 else rows
    for where in itertools.product(*(range(n) for n in lead)):

        def add(i, carry):
            at = (*where, pl.ds(pl.multiple_of(i * step, step), step), slice(None))
            both = total[at].astype(jnp.float32) + arrived[at].astype(jnp.float32)
            total[at] = both.astype(jnp.bfloat16)
            return carry

        lax.fori_loop(0, rows // step, add, 0)


def sum_scatter_kernel(plan, *refs):
    lanes, ins, copies = plan
    sources = refs[:ins]
    second_pre, second_down, stats_in = refs[ins : ins + 3]
    stage, stats = refs[ins + 3 : ins + 9], refs[ins + 9]
    scratch = list(refs[ins + 10 :])
    send_sem, recv_sem, local_sem, stats_got, stats_send, stats_recv, core_send, core_recv = (
        scratch[-8:]
    )
    core = lax.axis_index(CORE)
    partners = []
    for lane in lanes:
        for axis, bits in lane.phases:
            partners += [(axis, bit) for bit in bits if (axis, bit) not in partners]
    partners.append((CORE, 0))
    index = {axis: lax.axis_index(axis) for axis, _ in partners}
    mine = {(axis, bit): (index[axis] >> bit) & 1 for axis, bit in partners}
    far = {key: index[key[0]] + (1 - 2 * mine[key]) * (1 << key[1]) for key in partners}
    barrier = pltpu.get_barrier_semaphore()
    peers = [{axis: far[axis, bit]} for axis, bit in partners if axis != GROUP]
    groups = lax.axis_size(GROUP)
    peers += [{GROUP: lax.rem(lax.axis_index(GROUP) + k, groups)} for k in range(1, groups)]
    for peer in peers:
        pl.semaphore_signal(
            barrier, inc=1, device_id=peer, device_id_type=pl.DeviceIdType.MESH
        )
    pl.semaphore_wait(barrier, len(peers))

    counter = itertools.count()

    def send(source, target, key):
        number = next(counter)
        copy = pltpu.make_async_remote_copy(
            src_ref=source,
            dst_ref=target,
            send_sem=send_sem.at[number],
            recv_sem=recv_sem.at[number],
            device_id={key[0]: far[key]},
            device_id_type=pl.DeviceIdType.MESH,
        )
        copy.start()
        return copy

    def place(axis, values):
        total = 0
        for bit, value in values.items():
            total = total + value * (1 << bit)
        return total

    def sum_stats():
        count = lax.axis_size(GROUP)
        me = lax.axis_index(GROUP)

        def copy(at, source, slot, target):
            return pltpu.make_async_remote_copy(
                src_ref=source,
                dst_ref=stats_got.at[slot],
                send_sem=stats_send.at[at],
                recv_sem=stats_recv.at[slot],
                device_id=target,
                device_id_type=pl.DeviceIdType.MESH,
            )

        for k in range(1, count):
            copy(k, stats_in, me, {GROUP: lax.rem(me + k, count)}).start()
        yield
        stats[...] = stats_in[...]
        for k in range(1, count):
            peer = lax.rem(me + k, count)
            copy(k, stats_in, peer, {GROUP: peer}).wait_recv()
            stats[...] += stats_got[peer]
        both = copy(0, stats, count, {CORE: far[CORE, 0]})
        both.start()
        yield
        both.wait()
        stats[...] += stats_got[count]
        for k in range(1, count):
            copy(k, stats_in, me, {GROUP: lax.rem(me + k, count)}).wait_send()

    summing = sum_stats()
    next(summing)

    def to_stage(number, source, kind, *at):
        spot = stage[kind].at[(core, *at)]
        return spot, pltpu.make_async_remote_copy(
            src_ref=source,
            dst_ref=spot,
            send_sem=core_send.at[number],
            recv_sem=core_recv.at[number],
            device_id={CORE: 1 - core},
            device_id_type=pl.DeviceIdType.MESH,
        )

    inner = stage[GATE].shape[3]
    wholes = []
    half = stage[GATE].shape[1]
    for number in range(3 * half):
        kind, j = divmod(number, half)
        if kind == DOWN:
            source = second_down.at[j]
        else:
            source = second_pre.at[:, pl.ds(number * inner, inner)]
        spot, copy = to_stage(len(lanes) + number, source, kind, j)
        wholes.append((copy, pltpu.make_async_copy(source, spot, core_send.at[len(lanes) + number])))
    for copy, here in wholes:
        @pl.when(core == 1)
        def _(here=here):
            here.start()

        @pl.when(core == 0)
        def _(copy=copy):
            copy.start()

    moved = []
    started = []
    states = []
    for number, lane in enumerate(lanes):
        count = len(lane.buffers)
        buffers, scratch = scratch[:count], scratch[count:]
        source = sources[lane.source]
        prefix = lane.prefix
        if isinstance(prefix, int):
            source = source.at[prefix]

        def part(at, source=source, prefix=prefix):
            if isinstance(prefix, int):
                return source.at[at]
            inner, columns = prefix
            where = (slice(None), at) if inner else (at,)
            if columns is not None:
                where += (slice(None),) * (len(source.shape) - len(where) - 1) + (pl.ds(*columns),)
            return source.at[where]

        axis, bits = lane.phases[0]
        total, arrived = buffers[0], buffers[1:]
        rest = [bit for bit in bits[1:]]
        pending = []
        for choice in itertools.product((0, 1), repeat=len(rest)):
            values = dict(zip(rest, choice))
            slot = sum(value << i for i, value in enumerate(choice))
            far_at = place(axis, {**values, bits[0]: 1 - mine[axis, bits[0]]})
            here_at = place(axis, {**values, bits[0]: mine[axis, bits[0]]})
            copy = send(part(far_at), arrived[0].at[slot], (axis, bits[0]))
            pending.append((copy, slot))
            started.append(copy)
            states.append((number, part(here_at), slot, total))
        lane_state = SimpleNamespace(total=total, arrived=arrived, pending=pending)
        lane.state = lane_state
    locals_ = {}
    for at, (number, here, slot, total) in enumerate(states):
        copy = pltpu.make_async_copy(here, total.at[slot], local_sem.at[at])
        copy.start()
        locals_[number, slot] = copy
    short = [item for item in enumerate(lanes) if len(item[1].phases) == 1 and item[1].rows]
    long = [item for item in enumerate(lanes) if item not in short]
    turns = [(1, long), (1, short)]
    count = max(sum(len(bits) for _, bits in lane.phases) for lane in lanes)
    for step in range(2, count + 1):
        turns += [(2 * step - 2, long), (2 * step - 1, long), (step, short)]
    for at, (step, group) in enumerate(turns):
        if at == 2:
            next(summing)
        for number, lane in group:
            state = lane.state
            sizes = [len(bits) for _, bits in lane.phases]
            if step > sum(sizes):
                continue
            if step <= sizes[0]:
                axis, bits = lane.phases[0]
                resolved, rest = bits[:step], bits[step:]

                def slot_of(values):
                    found = 0
                    for i, bit in enumerate(bits[1:]):
                        found = found + values.get(bit, mine[axis, bit]) * (1 << i)
                    return found

                for copy, slot in state.pending:
                    copy.wait_recv()
                    if step == 1:
                        locals_[number, slot].wait()
                state.pending_next = []
                for choice in itertools.product((0, 1), repeat=len(rest)):
                    values = dict(zip(rest, choice))
                    got = sum(value << i for i, value in enumerate(choice))
                    add_slab(
                        state.total.at[slot_of(values)], state.arrived[step - 1].at[got]
                    )
                if rest:
                    following = rest[1:]
                    for choice in itertools.product((0, 1), repeat=len(following)):
                        values = dict(zip(following, choice))
                        got = sum(value << i for i, value in enumerate(choice))
                        values[rest[0]] = 1 - mine[axis, rest[0]]
                        copy = send(
                            state.total.at[slot_of(values)],
                            state.arrived[step].at[got],
                            (axis, rest[0]),
                        )
                        state.pending_next.append((copy, got))
                        started.append(copy)
                final = state.total.at[slot_of({})] if not rest else None
            else:
                axis, bits = lane.phases[1]
                done = step - sizes[0]
                rest = bits[done:]
                final = state.final
                for copy, _ in state.pending:
                    copy.wait_recv()
                state.pending_next = []
                for choice in itertools.product((0, 1), repeat=len(rest)):
                    values = dict(zip(rest, choice))
                    got = sum(value << i for i, value in enumerate(choice))
                    at = place(axis, {bit: values.get(bit, mine[axis, bit]) for bit in bits})
                    add_slab(final.at[at], state.arrived[step - 1].at[got])
                if not rest:
                    at = place(axis, {bit: mine[axis, bit] for bit in bits})
                    final = final.at[at]
            if final is not None and step >= sizes[0]:
                state.final = final
                if step == sum(sizes):
                    spot, copy = to_stage(number, final, *lane.target)
                    moved.append((lane.layer, copy))

                    @pl.when(core == lane.layer)
                    def _(spot=spot, final=final):
                        spot[...] = final[...]

                    @pl.when(core != lane.layer)
                    def _(copy=copy):
                        copy.start()
                elif step < sum(sizes):
                    axis, bits = lane.phases[1]
                    done = step - sizes[0]
                    bit, following = bits[done], bits[done + 1 :]
                    for choice in itertools.product((0, 1), repeat=len(following)):
                        values = dict(zip(following, choice))
                        got = sum(value << i for i, value in enumerate(choice))
                        at = place(
                            axis,
                            {
                                b: values.get(b, 1 - mine[axis, b] if b == bit else mine[axis, b])
                                for b in bits
                            },
                        )
                        copy = send(final.at[at], state.arrived[step].at[got], (axis, bit))
                        state.pending_next.append((copy, got))
                        started.append(copy)
            state.pending = state.pending_next
    for _ in summing:
        pass

    for copy, here in wholes:
        @pl.when(core == 1)
        def _(copy=copy, here=here):
            copy.wait_recv()
            here.wait()

        @pl.when(core == 0)
        def _(copy=copy):
            copy.wait_send()

    for layer, copy in moved:
        @pl.when(core == layer)
        def _(copy=copy):
            copy.wait_recv()

        @pl.when(core != layer)
        def _(copy=copy):
            copy.wait_send()

    for copy in started:
        copy.wait_send()


def sum_scatter(arrays, lanes, second_pre, second_down, stats, inner, collective):
    plans, scratch, shapes, copies, locals_ = [], [], [], 0, 0
    sizes = {}
    for source, prefix, phases, layer, target in lanes:
        shape = arrays[source].shape
        if isinstance(prefix, int):
            shape = shape[1:]
        else:
            if prefix[0]:
                shape = (shape[1], shape[0], *shape[2:])
            if prefix[1] is not None:
                shape = (*shape[:-1], prefix[1][1])
        buffers = [(shape[0] // 2, *shape[1:])]
        for step in range(1, len(phases[0][1]) + 1):
            buffers.append((shape[0] >> step, *shape[1:]))
            copies += shape[0] >> step
        locals_ += shape[0] // 2
        if len(phases) > 1:
            for step in range(1, len(phases[1][1]) + 1):
                buffers.append((shape[1] >> step, *shape[2:]))
                copies += shape[1] >> step
        plans.append(
            SimpleNamespace(
                source=source,
                prefix=prefix,
                phases=phases,
                buffers=buffers,
                rows=phases[0][0] == GROUP,
                layer=layer,
                target=target,
            )
        )
        width = sizes.get(target[0], (0, 0))[1] if len(target) > 2 else 0
        if layer == 0:
            sizes[target[0]] = (shape[-2], width + shape[-1])
        scratch += [pltpu.VMEM(buffer, jnp.bfloat16) for buffer in buffers]
    half = second_pre.shape[1] // (2 * inner)
    experts_shape = (2, half, second_pre.shape[0], inner)
    shapes = [
        jax.ShapeDtypeStruct(shape, jnp.bfloat16)
        for shape in (
            experts_shape,
            experts_shape,
            (2, half, *sizes[DOWN]),
            (2, *sizes[QKV]),
            (2, *sizes[OUT]),
            (2, *sizes[SMALL]),
        )
    ] + [jax.ShapeDtypeStruct(stats.shape, jnp.float32)]
    scratch += [
        pltpu.SemaphoreType.DMA((copies,)),
        pltpu.SemaphoreType.DMA((copies,)),
        pltpu.SemaphoreType.DMA((locals_,)),
    ]
    hops = lax.axis_size(GROUP) + 1
    scratch += [
        pltpu.VMEM((hops, *stats.shape), jnp.float32),
        pltpu.SemaphoreType.DMA((hops,)),
        pltpu.SemaphoreType.DMA((hops,)),
        pltpu.SemaphoreType.DMA((len(lanes) + 3 * half,)),
        pltpu.SemaphoreType.DMA((len(lanes) + 3 * half,)),
    ]
    return pl.pallas_call(
        functools.partial(sum_scatter_kernel, (plans, len(arrays), copies)),
        out_shape=shapes,
        in_specs=[pl.BlockSpec(memory_space=pl.ANY)] * (len(arrays) + 2)
        + [pl.BlockSpec(memory_space=pltpu.VMEM)],
        out_specs=[pl.BlockSpec(memory_space=pltpu.VMEM)] * len(shapes),
        scratch_shapes=scratch,
        compiler_params=pltpu.CompilerParams(
            collective_id=collective, has_side_effects=True, vmem_limit_bytes=60 * 2**20
        ),
    )(*arrays, second_pre, second_down, stats)


def bits_of(axis):
    return list(range(lax.axis_size(axis).bit_length() - 1))


def expert_lanes(first, inner):
    up, down = [(GROUP, bits_of(GROUP))], [(GROUP, bits_of(GROUP)[::-1])]
    return [
        (first, (False, ((2 * kind + j) * inner, inner)), (up, down)[kind], 0, (kind, j))
        for j in range(2)
        for kind in (GATE, UP)
    ]


def down_lanes(first, layer):
    up, down = [(GROUP, bits_of(GROUP))], [(GROUP, bits_of(GROUP)[::-1])]
    return [(first, 0, up, layer, (DOWN, 0)), (first, 1, down, layer, (DOWN, 1))]


def dense_lanes(first, width):
    up, down, deep = bits_of(GROUP), bits_of(GROUP)[::-1], bits_of(LINE)
    near = width // 4 // COLUMNS * COLUMNS
    away = width - near
    return [
        (
            first,
            (True, (0, away)),
            [(LINE, deep), (GROUP, up)],
            0,
            (QKV, slice(None), pl.ds(0, away)),
        ),
        (
            first,
            (False, (away, near)),
            [(GROUP, up), (LINE, deep)],
            0,
            (QKV, slice(None), pl.ds(away, near)),
        ),
        (first + 1, (False, None), [(GROUP, down), (LINE, deep)], 0, (OUT,)),
        small_lane(first + 2, 0),
    ]


def small_lane(first, layer):
    phases = [(GROUP, bits_of(GROUP)), (LINE, bits_of(LINE))]
    return (first, (False, None), phases, layer, (SMALL,))


def attention_forward(inputs, weights, segment_row):
    gain_attn, w_query, w_key, w_value, w_out, gain_moe = weights[:6]
    length = inputs.shape[0]
    cosine_table, sine_table = rotary_tables(length)
    inverse_one = lax.rsqrt(jnp.mean(inputs * inputs, axis=-1, keepdims=True) + EPSILON)
    normed_one = (inputs * inverse_one * gain_attn).astype(jnp.bfloat16)
    queries = rotate(
        matmul(normed_one, w_query).reshape(length, H, HD), cosine_table, sine_table
    ).astype(jnp.bfloat16)
    key_rows = rotate(
        matmul(normed_one, w_key).reshape(length, KVH, HD), cosine_table, sine_table
    ).astype(jnp.bfloat16)
    values = matmul(normed_one, w_value).astype(jnp.bfloat16).reshape(length, KVH, HD)
    scores = attention_scores(queries, key_rows, segment_row)
    highest = jnp.max(scores, axis=-1, keepdims=True)
    exponent = jnp.exp(scores - highest)
    denominator = jnp.sum(exponent, axis=-1, keepdims=True)
    weight = exponent / denominator
    attended = jnp.einsum(
        "kgqs,skd->qkgd", weight.astype(jnp.bfloat16), values, preferred_element_type=jnp.float32
    )
    attended = attended.reshape(length, H * HD).astype(jnp.bfloat16)
    hidden = inputs + matmul(attended, w_out)
    inverse_two = lax.rsqrt(jnp.mean(hidden * hidden, axis=-1, keepdims=True) + EPSILON)
    normed_two = (hidden * inverse_two * gain_moe).astype(jnp.bfloat16)
    state = (inverse_one, normed_one, queries, key_rows, values, weight, attended, hidden, inverse_two, normed_two)
    return state


MESH = pl.DeviceIdType.MESH
PARTS = 3


def move_rows(sources, held, pieces, sems, compute, z, n, others):
    row_send, row_recv, sum_send, sum_recv = sems
    barrier = pltpu.get_barrier_semaphore()
    for k in range(1, n):
        peer = lax.rem(z + k, n)
        pl.semaphore_signal(barrier, inc=1, device_id={LINE: peer}, device_id_type=MESH)
    for peer in others:
        pl.semaphore_signal(barrier, inc=1, device_id=peer, device_id_type=MESH)
    pl.semaphore_wait(barrier, n - 1 + len(others))

    def row_copy(kind, way, hop, source=None):
        step = 1 - 2 * way
        block = jnp.clip(z - step * hop, 0, n - 1)
        peer = jnp.clip(z + step, 0, n - 1)
        return pltpu.make_async_remote_copy(
            src_ref=held[kind].at[block] if source is None else source,
            dst_ref=held[kind].at[block],
            send_sem=row_send.at[kind, way, hop],
            recv_sem=row_recv.at[kind, way, hop],
            device_id={LINE: peer},
            device_id_type=MESH,
        )

    def sends(way, hop):
        step = 1 - 2 * way
        block, peer = z - step * hop, z + step
        return (block >= 0) & (block < n) & (peer >= 0) & (peer < n)

    def arrives(way, hop):
        block = z - (1 - 2 * way) * (hop + 1)
        return (block >= 0) & (block < n)

    def start(kind):
        for way in range(2):
            @pl.when(sends(way, 0))
            def _():
                row_copy(kind, way, 0, sources[kind]).start()

    def take(hop):
        for kind in range(len(held)):
            for way in range(2):
                @pl.when(arrives(way, hop))
                def _():
                    row_copy(kind, way, hop).wait_recv()

                @pl.when(sends(way, hop + 1) & (hop + 1 < n - 1))
                def _():
                    row_copy(kind, way, hop + 1).start()

    def waits(way, block):
        peer, last = z - (1 - 2 * way), (n - 1) * (1 - way)
        return (peer >= 0) & (peer < n) & ((block != last) | (peer != n - 1 - last))

    def far_copy(p):
        mine, arrived = pieces[p]
        block, way = n - 1 - z, jnp.where(z == 0, 1, 0)
        return pltpu.make_async_remote_copy(
            src_ref=mine(block),
            dst_ref=arrived(way, block),
            send_sem=sum_send.at[block, p],
            recv_sem=sum_recv.at[way, block, p],
            device_id={LINE: block},
            device_id_type=MESH,
        )

    def sum_copy(way, block, p):
        mine, arrived = pieces[p]
        return pltpu.make_async_remote_copy(
            src_ref=mine(block),
            dst_ref=arrived(way, block),
            send_sem=sum_send.at[block, p],
            recv_sem=sum_recv.at[way, block, p],
            device_id={LINE: jnp.clip(z + 1 - 2 * way, 0, n - 1)},
            device_id_type=MESH,
        )

    def sent(block, p):
        way = jnp.where(block > z, 0, 1)
        far = ((z == 0) | (z == n - 1)) & (block == n - 1 - z)

        @pl.when(far)
        def _():
            far_copy(p).start()

        @pl.when((block != z) & jnp.logical_not(far) & jnp.logical_not(waits(way, block)))
        def _():
            sum_copy(way, block, p).start()

    def run():
        def both(hop):
            return (hop >= 0) & (z - 1 - hop >= 0) & (z + 1 + hop < n)

        def turn(k, carry):
            hop = lax.div(k + 1, 2) - 1
            block = z + (1 + hop) * (1 - 2 * lax.rem(k, 2))
            odd = lax.rem(k, 2) == 1

            @pl.when(odd & jnp.logical_not(both(hop - 1)))
            def _():
                take(hop)

            @pl.when(jnp.logical_not(odd) & both(hop) & (hop + 1 < n - 1))
            def _():
                take(hop + 1)

            @pl.when((block >= 0) & (block < n))
            def _():
                compute(block, sent)

            return carry

        lax.fori_loop(0, 2 * n - 1, turn, 0)

        first = jnp.where(2 * z < n, 0, 1)
        for way in (first, 1 - first):
            for k in range(1, n):
                block = z + (1 - 2 * way) * k

                @pl.when(waits(way, block) & (block >= 0) & (block < n))
                def _():
                    for p, (mine, arrived) in enumerate(pieces):
                        sum_copy(way, block, p).wait_recv()
                        own, other = mine(block), arrived(way, block)
                        own[...] = (
                            own[...].astype(jnp.float32) + other[...].astype(jnp.float32)
                        ).astype(jnp.bfloat16)
                        sum_copy(way, block, p).start()

    def collect(add):
        for way in range(2):
            for p, (_, arrived) in enumerate(pieces):
                sum_copy(way, z, p).wait_recv()
                add(p, arrived(way, z)[...].astype(jnp.float32))

    def finish():
        for kind in range(len(held)):
            for way in range(2):
                for hop in range(n - 1):
                    @pl.when(sends(way, hop))
                    def _():
                        row_copy(kind, way, hop).wait_send()
        for k in range(1, n):
            for p in range(len(pieces)):
                sum_copy(0, lax.rem(z + k, n), p).wait_send()

    return start, run, collect, finish


def row_pieces(sums, returned, parts):
    width = sums.shape[2] // parts

    def piece(p):
        at = pl.ds(p * width, width)
        return (
            lambda block: sums.at[block, :, at],
            lambda way, block: returned.at[way, block, :, at],
        )

    return [piece(p) for p in range(parts)]


def fetch_weights(layer, own, other, places, sem):
    count = places[0].shape[0]
    mine = lax.axis_index(CORE) == layer

    def copy(group, kind, e):
        return pltpu.make_async_copy(
            group[kind].at[e], places[kind].at[e], sem.at[kind * count + e]
        )

    for kind in range(len(places)):
        for e in range(count):
            @pl.when(mine)
            def _():
                copy(own, kind, e).start()

            @pl.when(jnp.logical_not(mine))
            def _():
                copy(other, kind, e).start()

    def wait():
        for kind in range(len(places)):
            for e in range(count):
                copy(own, kind, e).wait()

    return wait


def sigmoid_of(value):
    return 1.0 / (1.0 + jnp.exp(-value))


def column_of(block, column):
    here = lax.broadcasted_iota(jnp.int32, block.shape, 1) == column
    return jnp.sum(jnp.where(here, block, 0.0), axis=1, keepdims=True)


def experts_forward_kernel(
    layer, experts, x, mask, hidden, router, *refs
):
    own, other, refs = refs[:3], refs[3:6], refs[6:]
    own_dense, other_dense, refs = refs[:4], refs[4:8], refs[8:]
    out, rows, gates_all, gates, gate_keep, up_keep, gated, stats = refs[:8]
    placed, place_sem = refs[8:12], refs[-1]
    passing, refs = refs[-5:-1], refs[:8] + refs[12:-5]
    w_gate, w_up, w_down, sums, returned, mixed, total, stats_all = refs[8:16]
    weight_sem, *sems = refs[16:]
    n, held = rows.shape[0], w_gate.shape[0]
    z = lax.axis_index(LINE)

    def compute(block, sent):
        picked = rows[block]
        gate_block = gates_all[block].astype(jnp.float32)

        def one(e, carry):
            gate_pre = jnp.dot(picked, w_gate[e], preferred_element_type=jnp.float32)
            up_pre = jnp.dot(picked, w_up[e], preferred_element_type=jnp.float32)
            gate_keep[e, block] = gate_pre.astype(jnp.bfloat16)
            up_keep[e, block] = up_pre.astype(jnp.bfloat16)
            active = gate_pre * sigmoid_of(gate_pre) * up_pre
            share = (column_of(gate_block, z * held + e) * active).astype(jnp.bfloat16)
            inner = share.shape[1]
            gated[block, :, pl.ds(pl.multiple_of(e * inner, inner), inner)] = share
            mixed[e] = share
            return carry

        lax.fori_loop(0, held, one, 0)
        width = out.shape[1] // PARTS
        for part in range(PARTS):
            at = pl.ds(part * width, width)
            result = jnp.zeros((out.shape[0], width), jnp.float32)
            for e in range(held):
                result += jnp.dot(mixed[e], w_down[e, :, at], preferred_element_type=jnp.float32)

            @pl.when(block == z)
            def _():
                total[:, at] = hidden[:, at] + result

            @pl.when(block != z)
            def _():
                sums[block, :, at] = result.astype(jnp.bfloat16)

            sent(block, part)

    own_gates = gates_all.at[z]
    start, run, collect, finish = move_rows(
        (x, own_gates, stats_all.at[z]),
        (rows, gates_all, stats_all),
        row_pieces(sums, returned, PARTS),
        sems,
        compute,
        z,
        n,
        [],
    )
    start(0)
    wait_weights = fetch_weights(layer, own, other, (w_gate, w_up, w_down), weight_sem)
    here = lax.axis_index(CORE) == 1 - layer

    def place_copy(group, i):
        return pltpu.make_async_copy(group[i], passing[i], place_sem.at[0, i])

    def place_out(i):
        return pltpu.make_async_copy(passing[i], placed[i], place_sem.at[1, i])

    logits = jnp.dot(x[...], router[...], preferred_element_type=jnp.float32)
    chosen = mask[...] > 0
    highest = jnp.max(jnp.where(chosen, logits, MASKED), axis=1, keepdims=True)
    exponent = jnp.where(chosen, jnp.exp(logits - highest), 0.0)
    gates[...] = exponent / jnp.sum(exponent, axis=1, keepdims=True)
    own_gates[...] = gates[...].astype(jnp.bfloat16)
    start(1)
    real = lax.broadcasted_iota(jnp.int32, logits.shape, 1) < experts
    highest = jnp.max(jnp.where(real, logits, MASKED), axis=1, keepdims=True)
    exponent = jnp.where(real, jnp.exp(logits - highest), 0.0)
    chance = exponent / jnp.sum(exponent, axis=1, keepdims=True)
    line = lax.broadcasted_iota(jnp.int32, stats.shape, 0)
    stats_all[z] = jnp.where(
        line == 0,
        jnp.sum(chance, axis=0, keepdims=True),
        jnp.where(line == 1, jnp.sum(mask[...], axis=0, keepdims=True), 0.0),
    )
    start(2)
    rows[z] = x[...]
    wait_weights()
    for i in range(4):
        @pl.when(here)
        def _():
            place_copy(own_dense, i).start()

        @pl.when(jnp.logical_not(here))
        def _():
            place_copy(other_dense, i).start()

    run()
    for i in range(4):
        place_copy(own_dense, i).wait()
        place_out(i).start()
    stats[...] = jnp.sum(stats_all[...], axis=0)
    width = out.shape[1] // PARTS

    def add(p, value):
        total[:, p * width : (p + 1) * width] += value

    collect(add)
    out[...] = total[...].astype(jnp.bfloat16)
    finish()
    for i in range(4):
        place_out(i).wait()


def experts_backward_kernel(layer, grad, gates, gate_keep, up_keep, *refs):
    own, other, saved_rows, saved_gated, refs = refs[:3], refs[3:6], refs[6], refs[7], refs[8:]
    carried = layer == 0
    if carried:
        extra, refs = refs[0], refs[1:]
        extra_sum, refs = refs[6], refs[:6] + refs[7:]
        landed, extra_send, extra_recv = refs[-3:]
        refs = refs[:-3]
    out, out_gates, rows_both, gated_both, grad_both, pre_both = refs[:6]
    w_gate, w_up, w_down, sums, sum_gates, returned, returned_gates, away, dots = refs[6:15]
    weight_sem, core_send, core_recv, core_local, *sems = refs[15:]
    n, held = gates.shape[0], w_gate.shape[0]
    half, inner = held // 2, w_gate.shape[2]
    core = lax.axis_index(CORE)
    z = lax.axis_index(LINE)
    turned_dims = (((1,), (1,)), ((), ()))
    rows = grad_both.at[core]

    def to_core(number, source, target):
        return pltpu.make_async_remote_copy(
            src_ref=source,
            dst_ref=target,
            send_sem=core_send.at[number],
            recv_sem=core_recv.at[number],
            device_id={CORE: 1 - core},
            device_id_type=MESH,
        )

    def block_copies(block):
        return (
            to_core(2 + block, rows.at[block], rows.at[block]),
            to_core(2 + n + block, away.at[block], pre_both.at[core, block]),
        )

    def columns(at):
        return pl.ds(pl.multiple_of(at * half * inner, half * inner), half * inner)

    def whole_copies():
        return (
            to_core(0, saved_rows, rows_both.at[core]),
            to_core(1, saved_gated.at[:, :, columns(1 - core)], gated_both.at[core]),
        )

    def local_copies():
        return (
            pltpu.make_async_copy(saved_rows, rows_both.at[core], core_local.at[0]),
            pltpu.make_async_copy(
                saved_gated.at[:, :, columns(core)], gated_both.at[core], core_local.at[1]
            ),
        )

    me, count = lax.axis_index(GROUP), lax.axis_size(GROUP)
    peers = [lax.rem(me + k, count) for k in range(1, count)] if carried else []

    def extra_copy(k, peer, slot):
        return pltpu.make_async_remote_copy(
            src_ref=extra.at[:, peer],
            dst_ref=landed.at[slot],
            send_sem=extra_send.at[k],
            recv_sem=extra_recv.at[slot],
            device_id={GROUP: peer},
            device_id_type=MESH,
        )

    def compute(block, sent):
        picked = rows[block]
        gate_block = gates[block].astype(jnp.float32)
        dots[...] = jnp.zeros(dots.shape, jnp.float32)

        def one(e, place, j):
            raw = lax.dot_general(
                picked, w_down[e], turned_dims, preferred_element_type=jnp.float32
            )
            gate_pre = gate_keep[e, block].astype(jnp.float32)
            up_pre = up_keep[e, block].astype(jnp.float32)
            sigmoid = sigmoid_of(gate_pre)
            silu = gate_pre * sigmoid
            column = z * held + e
            dot = jnp.sum(raw * (silu * up_pre), axis=1, keepdims=True)
            here = lax.broadcasted_iota(jnp.int32, dots.shape, 1) == column
            dots[...] += jnp.where(here, dot, 0.0)
            active = column_of(gate_block, column) * raw
            place[:, pl.ds(pl.multiple_of(j * inner, inner), inner)] = (
                active * up_pre * sigmoid * (1.0 + gate_pre * (1.0 - sigmoid))
            ).astype(jnp.bfloat16)
            place[:, pl.ds(pl.multiple_of((half + j) * inner, inner), inner)] = (
                active * silu
            ).astype(jnp.bfloat16)

        def own_half(j, carry):
            one(core * half + j, pre_both.at[core, block], j)
            return carry

        def other_half(j, carry):
            one((1 - core) * half + j, away.at[block], j)
            return carry

        lax.fori_loop(0, half, other_half, 0)
        for copy in block_copies(block):
            copy.start()
        lax.fori_loop(0, half, own_half, 0)
        sum_gates[block] = dots[...].astype(jnp.bfloat16)

        @pl.when(block == z)
        def _():
            out_gates[...] = dots[...]

        sent(block, PARTS)
        width = out.shape[1] // PARTS
        for part in range(PARTS):
            at = pl.ds(part * width, width)
            result = jnp.zeros((out.shape[0], width), jnp.float32)
            for place, side in ((away.at[block], 1 - core), (pre_both.at[core, block], core)):
                for kind, right in enumerate((w_gate, w_up)):
                    for j in range(half):
                        left = place[:, pl.ds((kind * half + j) * inner, inner)]
                        result += lax.dot_general(
                            left,
                            right[side * half + j, at, :],
                            turned_dims,
                            preferred_element_type=jnp.float32,
                        )

            @pl.when(block == z)
            def _():
                out[:, at] = result

            @pl.when(block != z)
            def _():
                sums[block, :, at] = result.astype(jnp.bfloat16)

            sent(block, part)

    gate_piece = (lambda block: sum_gates.at[block], lambda way, block: returned_gates.at[way, block])
    start, run, collect, finish = move_rows(
        (grad,),
        (rows,),
        row_pieces(sums, returned, PARTS) + [gate_piece],
        sems,
        compute,
        z,
        n,
        [{CORE: 1 - core}] + [{GROUP: peer} for peer in peers],
    )
    start(0)
    for k, peer in enumerate(peers):
        extra_copy(k, peer, me).start()
    if carried:
        mine = pltpu.make_async_copy(extra.at[:, me], landed.at[me], extra_send.at[len(peers)])
        mine.start()
    wait_weights = fetch_weights(layer, own, other, (w_gate, w_up, w_down), weight_sem)
    for copy in whole_copies() + local_copies():
        copy.start()
    rows[z] = grad[...]
    wait_weights()
    run()
    width = out.shape[1] // PARTS

    def add(p, value):
        if p == PARTS:
            out_gates[...] += value
        else:
            out[:, p * width : (p + 1) * width] += value

    if carried:
        mine.wait()
        for k, peer in enumerate(peers):
            extra_copy(k, peer, peer).wait_recv()
        half, rows_each = extra_sum.shape[:2]
        step = 16 if rows_each % 16 == 0 else rows_each

        def add_up(i, carry):
            at = pl.ds(pl.multiple_of(i * step, step), step)
            for j in range(half):
                value = landed[0, j, at].astype(jnp.float32)
                for k in range(1, count):
                    value += landed[k, j, at].astype(jnp.float32)
                extra_sum[j, at] = value.astype(jnp.bfloat16)
            return carry

        lax.fori_loop(0, rows_each // step, add_up, 0)
    collect(add)
    finish()
    for k, peer in enumerate(peers):
        extra_copy(k, peer, me).wait_send()
    for copy in local_copies():
        copy.wait()
    for copy in whole_copies():
        copy.wait()
    for block in range(n):
        for copy in block_copies(block):
            copy.wait()


def exchange_scratch(n, kinds_out, kinds_back):
    return [
        pltpu.SemaphoreType.DMA((kinds_out, 2, n)),
        pltpu.SemaphoreType.DMA((kinds_out, 2, n)),
        pltpu.SemaphoreType.DMA((n, kinds_back)),
        pltpu.SemaphoreType.DMA((2, n, kinds_back)),
    ]


def expert_call(kernel, operands, own, other, extra, shapes, scratch, collective, loose=0):
    vmem, free = pl.BlockSpec(memory_space=pltpu.VMEM), pl.BlockSpec(memory_space=pl.ANY)
    weights = [pltpu.VMEM(array.shape, jnp.bfloat16) for array in own]
    return pl.pallas_call(
        kernel,
        out_shape=shapes,
        in_specs=[vmem] * len(operands) + [free] * (6 + len(extra)),
        out_specs=[vmem] * (len(shapes) - loose) + [free] * loose,
        scratch_shapes=weights + scratch,
        compiler_params=pltpu.CompilerParams(
            collective_id=collective, has_side_effects=True, vmem_limit_bytes=46 * 2**20
        ),
        cost_estimate=pl.CostEstimate(
            flops=5 * 10**10, bytes_accessed=10**8, transcendentals=0
        ),
    )(*operands, *own, *other, *extra)


def experts_forward(
    layer, normed_two, mask, hidden, router, own, other, own_dense, other_dense, experts
):
    n, held = lax.axis_size(LINE), own[0].shape[0]
    length, width = normed_two.shape
    inner = own[0].shape[2]
    low, full = jnp.bfloat16, jnp.float32
    kept = jax.ShapeDtypeStruct((held, n, length, inner), low)
    shapes = [
        jax.ShapeDtypeStruct((length, width), low),
        jax.ShapeDtypeStruct((n, length, width), low),
        jax.ShapeDtypeStruct((n, length, COLUMNS), low),
        jax.ShapeDtypeStruct((length, COLUMNS), full),
        kept,
        kept,
        jax.ShapeDtypeStruct((n, length, held * inner), low),
        jax.ShapeDtypeStruct((8, COLUMNS), full),
    ] + [jax.ShapeDtypeStruct(array.shape, low) for array in own_dense]
    scratch = [
        pltpu.VMEM((n, length, width), low),
        pltpu.VMEM((2, n, length, width), low),
        pltpu.VMEM((held, length, inner), low),
        pltpu.VMEM((length, width), full),
        pltpu.VMEM((n, 8, COLUMNS), full),
        pltpu.SemaphoreType.DMA((3 * held,)),
    ] + exchange_scratch(n, 3, PARTS)
    scratch += [pltpu.VMEM(array.shape, low) for array in own_dense]
    scratch.append(pltpu.SemaphoreType.DMA((2, 4)))
    kernel = functools.partial(experts_forward_kernel, layer, experts)
    return expert_call(
        kernel,
        (normed_two, mask, hidden, router),
        own,
        other,
        (*own_dense, *other_dense),
        shapes,
        scratch,
        1 + layer,
        4,
    )


def experts_backward(layer, grad_low, gates, gate_keep, up_keep, rows, gated, own, other, extra):
    held, n, length, inner = gate_keep.shape
    width = grad_low.shape[1]
    low, full = jnp.bfloat16, jnp.float32
    shapes = [
        jax.ShapeDtypeStruct((length, width), full),
        jax.ShapeDtypeStruct((length, COLUMNS), full),
        jax.ShapeDtypeStruct((2, n, length, width), low),
        jax.ShapeDtypeStruct((2, n, length, held // 2 * inner), low),
        jax.ShapeDtypeStruct((2, n, length, width), low),
        jax.ShapeDtypeStruct((2, n, length, held * inner), low),
    ]
    scratch = [
        pltpu.VMEM((n, length, width), low),
        pltpu.VMEM((n, length, COLUMNS), low),
        pltpu.VMEM((2, n, length, width), low),
        pltpu.VMEM((2, n, length, COLUMNS), low),
        pltpu.VMEM((n, length, held * inner), low),
        pltpu.VMEM((length, COLUMNS), full),
        pltpu.SemaphoreType.DMA((3 * held,)),
        pltpu.SemaphoreType.DMA((2 + 2 * n,)),
        pltpu.SemaphoreType.DMA((2 + 2 * n,)),
        pltpu.SemaphoreType.DMA((2,)),
    ] + exchange_scratch(n, 1, PARTS + 1)
    if layer == 0:
        half, count, *block = extra.shape
        shapes.append(jax.ShapeDtypeStruct((half, *block), low))
        scratch += [
            pltpu.VMEM((count, half, *block), low),
            pltpu.SemaphoreType.DMA((count,)),
            pltpu.SemaphoreType.DMA((count,)),
        ]
    kernel = functools.partial(experts_backward_kernel, layer)
    return expert_call(
        kernel,
        (grad_low, gates, gate_keep, up_keep),
        own,
        other,
        (rows, gated) if extra is None else (rows, gated, extra),
        shapes,
        scratch,
        3 + layer,
    )


def attention_backward(grad_hidden, inputs, state, weights):
    gain_attn, w_query, w_key, w_value, w_out, gain_moe = weights[:6]
    (inverse_one, normed_one, queries, key_rows, values, weight, attended, hidden, inverse_two, normed_two) = state
    length = inputs.shape[0]
    grad_branch = grad_hidden.astype(jnp.bfloat16)
    grad_attended = jnp.einsum("td,cd->tc", grad_branch, w_out, preferred_element_type=jnp.float32)
    grad_attended = grad_attended.astype(jnp.bfloat16).reshape(length, KVH, H // KVH, HD)
    grad_weight = jnp.einsum(
        "qkgd,skd->kgqs", grad_attended, values, preferred_element_type=jnp.float32
    )
    grad_values = jnp.einsum(
        "kgqs,qkgd->skd",
        weight.astype(jnp.bfloat16),
        grad_attended,
        preferred_element_type=jnp.float32,
    )
    grad_values = grad_values.astype(jnp.bfloat16).reshape(length, KVH * HD)
    grad_scores = (
        weight * (grad_weight - jnp.sum(weight * grad_weight, axis=-1, keepdims=True))
    ).astype(jnp.bfloat16)
    score_scale = HD ** (-0.5)
    grouped = queries.reshape(length, KVH, H // KVH, HD)
    grad_queries = jnp.einsum(
        "kgqs,skd->qkgd", grad_scores, key_rows, preferred_element_type=jnp.float32
    )
    grad_queries = grad_queries.reshape(length, H, HD) * score_scale
    grad_keys = (
        jnp.einsum("kgqs,qkgd->skd", grad_scores, grouped, preferred_element_type=jnp.float32)
        * score_scale
    )
    cosine_table, sine_table = rotary_tables(length)
    grad_query_pre = (
        unrotate(grad_queries, cosine_table, sine_table)
        .reshape(length, H * HD)
        .astype(jnp.bfloat16)
    )
    grad_key_pre = (
        unrotate(grad_keys, cosine_table, sine_table).reshape(length, KVH * HD).astype(jnp.bfloat16)
    )
    grad_normed_one = (
        jnp.einsum("tq,cq->tc", grad_query_pre, w_query, preferred_element_type=jnp.float32)
        + jnp.einsum("tq,cq->tc", grad_key_pre, w_key, preferred_element_type=jnp.float32)
        + jnp.einsum("tq,cq->tc", grad_values, w_value, preferred_element_type=jnp.float32)
    )
    grad_norm_one, grad_gain_attn = norm_back(grad_normed_one, inputs, inverse_one, gain_attn)
    grad_inputs = grad_hidden + grad_norm_one
    grad_qkv = jnp.concatenate([grad_query_pre, grad_key_pre, grad_values], axis=1)
    return grad_inputs, grad_gain_attn, grad_qkv, grad_branch


def turned(left, right):
    return jnp.einsum("tc,tq->cq", left, right, preferred_element_type=jnp.float32)


def body(tokens, cotangent, segments, routes, *weight_arrays):
    core = lax.axis_index(CORE)
    first = core == 0
    experts = weight_arrays[6].shape[2]
    w_gate = weight_arrays[7]
    held = w_gate.shape[1]
    own = [array[0] for array in weight_arrays]
    other = [swapped(array) for array in own]
    weights = [
        [jnp.where(first, a, b) for a, b in zip(own[:7], other[:7])],
        [jnp.where(first, b, a) for a, b in zip(own[:7], other[:7])],
    ]
    inputs_low = lax.dynamic_slice_in_dim(tokens, core * SEQ, SEQ, 0)
    grad_low = lax.dynamic_slice_in_dim(cotangent, core * SEQ, SEQ, 0)
    segment_row = lax.dynamic_index_in_dim(segments, core, 0, keepdims=False)
    mine = lax.dynamic_slice_in_dim(routes[0], core * SEQ, SEQ, 0)
    got = swapped(lax.dynamic_slice_in_dim(routes[0], (1 - core) * SEQ, SEQ, 0))
    routes_here = jnp.stack([jnp.where(first, mine, got), jnp.where(first, got, mine)])
    masks = multi_hot(routes_here, COLUMNS)
    own_experts, other_experts = own[7:], other[7:]

    saved, outs, stats = [], [], []
    for s in range(2):
        inputs = inputs_low.astype(jnp.float32)
        state = attention_forward(inputs, weights[s], segment_row)
        hidden, normed_two = state[7], state[9]
        both_cores = [jnp.concatenate([a, swapped(a)]) for a in (state[1], state[6])]
        router = jnp.pad(weights[s][6], ((0, 0), (0, COLUMNS - experts)))
        inputs_low, *expert_state, stat, query, key, value, out = experts_forward(
            s,
            normed_two,
            masks[s],
            hidden,
            router,
            own_experts,
            other_experts,
            own[1:5],
            other[1:5],
            experts,
        )
        weights[1 - s][1:5] = [query, key, value, out]
        outs.append(inputs_low)
        stats.append(stat)
        saved.append((inputs, state, expert_state, both_cores))

    dp, deep = lax.axis_size(GROUP), lax.axis_size(LINE)
    grads = [None, None]
    input_grads = [None, None]
    for s in (1, 0):
        inputs, state, expert_state, both_cores = saved[s]
        (inverse_one, normed_one, _, _, _, _, attended, hidden, inverse_two, normed_two) = state
        rows_all, gates_all, gates, gate_keep, up_keep, gated = expert_state
        gain_moe, w_router = weights[s][5], weights[s][6]
        grad_sum, grad_gates, rows_both, gated_both, grad_both, pre_both, *sums = experts_backward(
            s,
            grad_low,
            gates_all,
            gate_keep,
            up_keep,
            rows_all,
            gated,
            own_experts,
            other_experts,
            None if s == 1 else grads[1][1].reshape(held // 2, dp, -1, D),
        )
        if s == 0:
            (second_down,) = sums
        inner = w_gate.shape[3]
        grad_gate_up = turned(
            rows_both.reshape(-1, D), pre_both.reshape(-1, held * inner)
        ).astype(jnp.bfloat16)
        if s == 1:
            grad_sum, grad_gate_up = lax.optimization_barrier((grad_sum, grad_gate_up))
            second_pre = lax.psum_scatter(grad_gate_up, GROUP, scatter_dimension=0, tiled=True)
        else:
            grad_sum, second_pre = lax.optimization_barrier((grad_sum, second_pre))
        gates, grad_gates = gates[:, :experts], grad_gates[:, :experts]
        grad_chosen = gates * (grad_gates - jnp.sum(gates * grad_gates, axis=-1, keepdims=True))
        grad_logits = grad_chosen.astype(jnp.bfloat16)
        grad_normed_two = grad_sum + jnp.einsum(
            "te,de->td", grad_logits, w_router, preferred_element_type=jnp.float32
        )
        grad_norm_two, grad_gain_moe = norm_back(grad_normed_two, hidden, inverse_two, gain_moe)
        grad_hidden = grad_low.astype(jnp.float32) + grad_norm_two
        grad_inputs, grad_gain_attn, grad_qkv, grad_branch = attention_backward(
            grad_hidden, inputs, state, weights[s]
        )
        if s == 1:
            grad_inputs, gated_both = lax.optimization_barrier((grad_inputs, gated_both))
        grad_down = turned(
            gated_both.reshape(-1, held // 2 * inner), grad_both.reshape(-1, D)
        ).astype(jnp.bfloat16)

        def halves(array):
            width = array.shape[1] // 2
            return (
                lax.dynamic_slice_in_dim(array, core * width, width, 1),
                lax.dynamic_slice_in_dim(array, (1 - core) * width, width, 1),
            )
        qkv_keep, qkv_send = halves(grad_qkv)
        branch_keep, branch_send = halves(grad_branch)
        grad_w_qkv = turned(
            both_cores[0], jnp.concatenate([qkv_keep, swapped(qkv_send)])
        ).astype(jnp.bfloat16)
        grad_w_out = turned(
            both_cores[1], jnp.concatenate([branch_keep, swapped(branch_send)])
        ).astype(jnp.bfloat16)
        grad_w_router = turned(normed_two, grad_logits)
        small = jnp.concatenate(
            [grad_gain_attn[:, None], grad_gain_moe[:, None], grad_w_router], axis=1
        ).astype(jnp.bfloat16)
        small = jnp.pad(small, ((0, 0), (0, COLUMNS - small.shape[1])))
        if s == 1:
            grad_inputs, grad_down, grad_w_qkv, grad_w_out = lax.optimization_barrier(
                (grad_inputs, grad_down, grad_w_qkv, grad_w_out)
            )
            dense = jnp.concatenate([grad_w_qkv, grad_w_out], axis=1)
            second_dense = lax.psum_scatter(dense, GROUP, scatter_dimension=0, tiled=True)
        grads[s] = (grad_gate_up, grad_down, grad_w_qkv, grad_w_out, small)
        input_grads[s] = grad_inputs
        grad_low = grad_inputs.astype(jnp.bfloat16)

    dp, deep = lax.axis_size(GROUP), lax.axis_size(LINE)
    half, inner = held // 2, w_gate.shape[3]
    grad_gate_up, grad_down, grad_w_qkv, grad_w_out, small = grads[0]
    arrays = [
        grad_gate_up.reshape(dp, D // dp, held * inner),
        grad_down.reshape(half, dp, inner // dp, D),
    ]
    lanes = dense_lanes(2, grad_w_qkv.shape[1])
    for array in (grad_w_qkv, grad_w_out, small):
        arrays.append(array.reshape(dp, deep, array.shape[0] // (dp * deep), array.shape[1]))
    width = grad_w_qkv.shape[1]
    whole = second_dense.shape[1]
    for columns, kind in (((0, width), QKV), ((width, whole - width), OUT)):
        start, size = columns
        target = (kind, slice(None), pl.ds(start - (start // width) * width, size))
        lanes.append((len(arrays), (False, columns), [(LINE, bits_of(LINE))], 1, target))
    arrays.append(second_dense.reshape(deep, second_dense.shape[0] // deep, whole))
    lanes.append(small_lane(len(arrays), 1))
    lanes += expert_lanes(0, inner) + down_lanes(1, 0)
    small = grads[1][4]
    arrays.append(small.reshape(dp, deep, small.shape[0] // (dp * deep), small.shape[1]))
    *grads, qkv, out, small, stats = sum_scatter(
        arrays, lanes, second_pre, second_down, jnp.concatenate(stats, axis=0), inner, 0
    )
    full = jnp.float32
    w_gate_grad, w_up_grad, w_down_grad = (
        grad.reshape(held, *grad.shape[2:]).astype(full) for grad in grads
    )
    qkv = jnp.concatenate([qkv[0], qkv[1]], axis=1).astype(full)
    grad_w_out = jnp.concatenate([out[0], out[1]], axis=1).astype(full)
    small = small[0].astype(full) + small[1].astype(full)
    heads, kv = H * HD, KVH * HD
    stats = lax.dynamic_index_in_dim(stats.reshape(2, 8, COLUMNS), core, 0)
    token_total = SEQ * lax.axis_size((CORE, GROUP, LINE))
    counts, chances = stats[:, 1, :experts], stats[:, 0, :experts]
    balance = experts * (counts / (token_total * TOPK) * chances / token_total)
    out_keep = jnp.where(first, outs[0], outs[1])
    out_got = swapped(jnp.where(first, outs[1], outs[0]))
    layer_out = jnp.where(
        first, jnp.concatenate([out_keep, out_got]), jnp.concatenate([out_got, out_keep])
    )
    low_one = input_grads[1].astype(jnp.bfloat16).astype(jnp.float32)
    grad_keep = jnp.where(first, input_grads[0], low_one)
    grad_got = swapped(jnp.where(first, low_one, input_grads[0]))
    input_grad = jnp.where(
        first, jnp.concatenate([grad_keep, grad_got]), jnp.concatenate([grad_got, grad_keep])
    )
    results = (
        layer_out,
        input_grad,
        small[:, 0],
        qkv[:, :heads],
        qkv[:, heads : heads + kv],
        qkv[:, heads + kv :],
        grad_w_out,
        small[:, 1],
        small[:, 2 : 2 + experts],
        w_gate_grad,
        w_up_grad,
        w_down_grad,
    )
    return tuple(result[None] for result in results) + (balance,)


def solution(mesh):
    return jax.shard_map(
        body,
        mesh=mesh,
        in_specs=(
            P((GROUP, LINE), None),
            P((GROUP, LINE), None),
            P((GROUP, LINE), None),
            P(CORE, (GROUP, LINE), None),
            P(CORE, None),
            P(CORE, None, None),
            P(CORE, None, None),
            P(CORE, None, None),
            P(CORE, None, None),
            P(CORE, None),
            P(CORE, None, None),
            P(CORE, LINE, None, None),
            P(CORE, LINE, None, None),
            P(CORE, LINE, None, None),
        ),
        out_specs=(
            P(CORE, (GROUP, LINE), None),
            P(CORE, (GROUP, LINE), None),
            P(CORE, (GROUP, LINE)),
            P(CORE, (GROUP, LINE), None),
            P(CORE, (GROUP, LINE), None),
            P(CORE, (GROUP, LINE), None),
            P(CORE, (GROUP, LINE), None),
            P(CORE, (GROUP, LINE)),
            P(CORE, (GROUP, LINE), None),
            P(CORE, LINE, GROUP, None),
            P(CORE, LINE, GROUP, None),
            P(CORE, LINE, GROUP, None),
            P(CORE, None),
        ),
        check_vma=False,
    )
```

```python
import functools
import itertools
from types import SimpleNamespace

import jax
import jax.numpy as jnp
from jax import lax
from jax.experimental import pallas as pl
from jax.experimental.pallas import tpu as pltpu
from jax.sharding import PartitionSpec as P

D = 1536
H = 24
KVH = 8
HD = 64
TOPK = 8
SEQ = 96


EPSILON = 1e-05
THETA = 10000.0
MASKED = -1e30
COLUMNS = 128
GATE, UP, DOWN, QKV, OUT, SMALL = range(6)
CORE, GROUP, LINE = "section", "dp", "expert"
INNER = "inner"


def matmul(left_side, right_side):
    return jnp.dot(left_side, right_side, preferred_element_type=jnp.float32)


def rotary_tables(length):
    half_width = HD // 2
    position = jnp.arange(length, dtype=jnp.float32)[:, None]
    freq_rate = THETA ** (-jnp.arange(half_width, dtype=jnp.float32) / half_width)
    angles = position * freq_rate[None, :]
    return (jnp.cos(angles)[:, None, :], jnp.sin(angles)[:, None, :])


def rotate(tensor, cosine_table, sine_table):
    half_width = HD // 2
    first_half = tensor[..., :half_width]
    second_half = tensor[..., half_width:]
    return jnp.concatenate(
        [
            first_half * cosine_table - second_half * sine_table,
            second_half * cosine_table + first_half * sine_table,
        ],
        axis=-1,
    )


def unrotate(gradient, cosine_table, sine_table):
    half_width = HD // 2
    first_half = gradient[..., :half_width]
    second_half = gradient[..., half_width:]
    return jnp.concatenate(
        [
            first_half * cosine_table + second_half * sine_table,
            second_half * cosine_table - first_half * sine_table,
        ],
        axis=-1,
    )


def norm_back(grad_normed, tensor, inverse, gain_vector):
    scaled = grad_normed * gain_vector
    grad_gain = jnp.sum(grad_normed * tensor * inverse, axis=0)
    grad_tensor = inverse * scaled - tensor * inverse**3 * jnp.mean(
        scaled * tensor, axis=-1, keepdims=True
    )
    return (grad_tensor, grad_gain)


def attention_scores(queries, key_rows, segment_row):
    length = queries.shape[0]
    grouped = queries.reshape(length, KVH, H // KVH, HD)
    scores = jnp.einsum(
        "qkgd,skd->kgqs", grouped, key_rows, preferred_element_type=jnp.float32
    ) * HD ** (-0.5)
    position = jnp.arange(length)
    allowed = (position[None, :] <= position[:, None]) & (
        segment_row[:, None] == segment_row[None, :]
    )
    return jnp.where(allowed[None, None], scores, MASKED)


def multi_hot(route_rows, experts):
    columns = jnp.arange(experts, dtype=jnp.int32)
    return jnp.sum(
        (route_rows[..., None] == columns).astype(jnp.float32), axis=-2
    )


def swapped(array):
    return lax.ppermute(array, CORE, [(0, 1), (1, 0)])


def add_slab(total, arrived):
    *lead, rows, _ = total.shape
    step = 16 if rows % 16 == 0 else rows
    for where in itertools.product(*(range(n) for n in lead)):

        def add(i, carry):
            at = (*where, pl.ds(pl.multiple_of(i * step, step), step), slice(None))
            both = total[at].astype(jnp.float32) + arrived[at].astype(jnp.float32)
            total[at] = both.astype(jnp.bfloat16)
            return carry

        lax.fori_loop(0, rows // step, add, 0)


def sum_scatter_kernel(plan, *refs):
    lanes, ins, copies = plan
    sources = refs[:ins]
    second_pre, second_down, stats_in = refs[ins : ins + 3]
    stage, stats = refs[ins + 3 : ins + 9], refs[ins + 9]
    scratch = list(refs[ins + 10 :])
    send_sem, recv_sem, local_sem, stats_got, stats_send, stats_recv, core_send, core_recv = (
        scratch[-8:]
    )
    core = lax.axis_index(CORE)
    partners = []
    for lane in lanes:
        for axis, bits in lane.phases:
            partners += [(axis, bit) for bit in bits if (axis, bit) not in partners]
    partners.append((CORE, 0))
    index = {axis: lax.axis_index(axis) for axis, _ in partners}
    mine = {(axis, bit): (index[axis] >> bit) & 1 for axis, bit in partners}
    far = {key: index[key[0]] + (1 - 2 * mine[key]) * (1 << key[1]) for key in partners}
    barrier = pltpu.get_barrier_semaphore()
    peers = [{axis: far[axis, bit]} for axis, bit in partners if axis != GROUP]
    groups = lax.axis_size(GROUP)
    peers += [{GROUP: lax.rem(lax.axis_index(GROUP) + k, groups)} for k in range(1, groups)]
    for peer in peers:
        pl.semaphore_signal(
            barrier, inc=1, device_id=peer, device_id_type=pl.DeviceIdType.MESH
        )
    pl.semaphore_wait(barrier, len(peers))

    counter = itertools.count()

    def send(source, target, key):
        number = next(counter)
        copy = pltpu.make_async_remote_copy(
            src_ref=source,
            dst_ref=target,
            send_sem=send_sem.at[number],
            recv_sem=recv_sem.at[number],
            device_id={key[0]: far[key]},
            device_id_type=pl.DeviceIdType.MESH,
        )
        copy.start()
        return copy

    def place(axis, values):
        total = 0
        for bit, value in values.items():
            total = total + value * (1 << bit)
        return total

    def sum_stats():
        count = lax.axis_size(GROUP)
        me = lax.axis_index(GROUP)

        def copy(at, source, slot, target):
            return pltpu.make_async_remote_copy(
                src_ref=source,
                dst_ref=stats_got.at[slot],
                send_sem=stats_send.at[at],
                recv_sem=stats_recv.at[slot],
                device_id=target,
                device_id_type=pl.DeviceIdType.MESH,
            )

        for k in range(1, count):
            copy(k, stats_in, me, {GROUP: lax.rem(me + k, count)}).start()
        yield
        stats[...] = stats_in[...]
        for k in range(1, count):
            peer = lax.rem(me + k, count)
            copy(k, stats_in, peer, {GROUP: peer}).wait_recv()
            stats[...] += stats_got[peer]
        both = copy(0, stats, count, {CORE: far[CORE, 0]})
        both.start()
        yield
        both.wait()
        stats[...] += stats_got[count]
        for k in range(1, count):
            copy(k, stats_in, me, {GROUP: lax.rem(me + k, count)}).wait_send()

    summing = sum_stats()
    next(summing)

    def to_stage(number, source, kind, *at):
        spot = stage[kind].at[(core, *at)]
        return spot, pltpu.make_async_remote_copy(
            src_ref=source,
            dst_ref=spot,
            send_sem=core_send.at[number],
            recv_sem=core_recv.at[number],
            device_id={CORE: 1 - core},
            device_id_type=pl.DeviceIdType.MESH,
        )

    inner = stage[GATE].shape[3]
    wholes = []
    half = stage[GATE].shape[1]
    for number in range(3 * half):
        kind, j = divmod(number, half)
        if kind == DOWN:
            source = second_down.at[j]
        else:
            source = second_pre.at[:, pl.ds(number * inner, inner)]
        spot, copy = to_stage(len(lanes) + number, source, kind, j)
        wholes.append((copy, pltpu.make_async_copy(source, spot, core_send.at[len(lanes) + number])))
    for copy, here in wholes:
        @pl.when(core == 1)
        def _(here=here):
            here.start()

        @pl.when(core == 0)
        def _(copy=copy):
            copy.start()

    moved = []
    started = []
    states = []
    for number, lane in enumerate(lanes):
        count = len(lane.buffers)
        buffers, scratch = scratch[:count], scratch[count:]
        source = sources[lane.source]
        prefix = lane.prefix
        if isinstance(prefix, int):
            source = source.at[prefix]

        def part(at, source=source, prefix=prefix):
            if isinstance(prefix, int):
                return source.at[at]
            inner, columns = prefix
            where = (slice(None), at) if inner else (at,)
            if columns is not None:
                where += (slice(None),) * (len(source.shape) - len(where) - 1) + (pl.ds(*columns),)
            return source.at[where]

        axis, bits = lane.phases[0]
        total, arrived = buffers[0], buffers[1:]
        rest = [bit for bit in bits[1:]]
        pending = []
        for choice in itertools.product((0, 1), repeat=len(rest)):
            values = dict(zip(rest, choice))
            slot = sum(value << i for i, value in enumerate(choice))
            far_at = place(axis, {**values, bits[0]: 1 - mine[axis, bits[0]]})
            here_at = place(axis, {**values, bits[0]: mine[axis, bits[0]]})
            copy = send(part(far_at), arrived[0].at[slot], (axis, bits[0]))
            pending.append((copy, slot))
            started.append(copy)
            states.append((number, part(here_at), slot, total))
        lane_state = SimpleNamespace(total=total, arrived=arrived, pending=pending)
        lane.state = lane_state
    locals_ = {}
    for at, (number, here, slot, total) in enumerate(states):
        copy = pltpu.make_async_copy(here, total.at[slot], local_sem.at[at])
        copy.start()
        locals_[number, slot] = copy
    short = [item for item in enumerate(lanes) if len(item[1].phases) == 1 and item[1].rows]
    long = [item for item in enumerate(lanes) if item not in short]
    turns = [(1, long), (1, short)]
    count = max(sum(len(bits) for _, bits in lane.phases) for lane in lanes)
    for step in range(2, count + 1):
        turns += [(2 * step - 2, long), (2 * step - 1, long), (step, short)]
    for at, (step, group) in enumerate(turns):
        if at == 2:
            next(summing)
        for number, lane in group:
            state = lane.state
            sizes = [len(bits) for _, bits in lane.phases]
            if step > sum(sizes):
                continue
            if step <= sizes[0]:
                axis, bits = lane.phases[0]
                resolved, rest = bits[:step], bits[step:]

                def slot_of(values):
                    found = 0
                    for i, bit in enumerate(bits[1:]):
                        found = found + values.get(bit, mine[axis, bit]) * (1 << i)
                    return found

                for copy, slot in state.pending:
                    copy.wait_recv()
                    if step == 1:
                        locals_[number, slot].wait()
                state.pending_next = []
                for choice in itertools.product((0, 1), repeat=len(rest)):
                    values = dict(zip(rest, choice))
                    got = sum(value << i for i, value in enumerate(choice))
                    add_slab(
                        state.total.at[slot_of(values)], state.arrived[step - 1].at[got]
                    )
                if rest:
                    following = rest[1:]
                    for choice in itertools.product((0, 1), repeat=len(following)):
                        values = dict(zip(following, choice))
                        got = sum(value << i for i, value in enumerate(choice))
                        values[rest[0]] = 1 - mine[axis, rest[0]]
                        copy = send(
                            state.total.at[slot_of(values)],
                            state.arrived[step].at[got],
                            (axis, rest[0]),
                        )
                        state.pending_next.append((copy, got))
                        started.append(copy)
                final = state.total.at[slot_of({})] if not rest else None
            else:
                axis, bits = lane.phases[1]
                done = step - sizes[0]
                rest = bits[done:]
                final = state.final
                for copy, _ in state.pending:
                    copy.wait_recv()
                state.pending_next = []
                for choice in itertools.product((0, 1), repeat=len(rest)):
                    values = dict(zip(rest, choice))
                    got = sum(value << i for i, value in enumerate(choice))
                    at = place(axis, {bit: values.get(bit, mine[axis, bit]) for bit in bits})
                    add_slab(final.at[at], state.arrived[step - 1].at[got])
                if not rest:
                    at = place(axis, {bit: mine[axis, bit] for bit in bits})
                    final = final.at[at]
            if final is not None and step >= sizes[0]:
                state.final = final
                if step == sum(sizes):
                    spot, copy = to_stage(number, final, *lane.target)
                    moved.append((lane.layer, copy))

                    @pl.when(core == lane.layer)
                    def _(spot=spot, final=final):
                        spot[...] = final[...]

                    @pl.when(core != lane.layer)
                    def _(copy=copy):
                        copy.start()
                elif step < sum(sizes):
                    axis, bits = lane.phases[1]
                    done = step - sizes[0]
                    bit, following = bits[done], bits[done + 1 :]
                    for choice in itertools.product((0, 1), repeat=len(following)):
                        values = dict(zip(following, choice))
                        got = sum(value << i for i, value in enumerate(choice))
                        at = place(
                            axis,
                            {
                                b: values.get(b, 1 - mine[axis, b] if b == bit else mine[axis, b])
                                for b in bits
                            },
                        )
                        copy = send(final.at[at], state.arrived[step].at[got], (axis, bit))
                        state.pending_next.append((copy, got))
                        started.append(copy)
            state.pending = state.pending_next
    for _ in summing:
        pass

    for copy, here in wholes:
        @pl.when(core == 1)
        def _(copy=copy, here=here):
            copy.wait_recv()
            here.wait()

        @pl.when(core == 0)
        def _(copy=copy):
            copy.wait_send()

    for layer, copy in moved:
        @pl.when(core == layer)
        def _(copy=copy):
            copy.wait_recv()

        @pl.when(core != layer)
        def _(copy=copy):
            copy.wait_send()

    for copy in started:
        copy.wait_send()


def sum_scatter(arrays, lanes, second_pre, second_down, stats, inner, collective):
    plans, scratch, shapes, copies, locals_ = [], [], [], 0, 0
    sizes = {}
    for source, prefix, phases, layer, target in lanes:
        shape = arrays[source].shape
        if isinstance(prefix, int):
            shape = shape[1:]
        else:
            if prefix[0]:
                shape = (shape[1], shape[0], *shape[2:])
            if prefix[1] is not None:
                shape = (*shape[:-1], prefix[1][1])
        buffers = [(shape[0] // 2, *shape[1:])]
        for step in range(1, len(phases[0][1]) + 1):
            buffers.append((shape[0] >> step, *shape[1:]))
            copies += shape[0] >> step
        locals_ += shape[0] // 2
        if len(phases) > 1:
            for step in range(1, len(phases[1][1]) + 1):
                buffers.append((shape[1] >> step, *shape[2:]))
                copies += shape[1] >> step
        plans.append(
            SimpleNamespace(
                source=source,
                prefix=prefix,
                phases=phases,
                buffers=buffers,
                rows=phases[0][0] == GROUP,
                layer=layer,
                target=target,
            )
        )
        width = sizes.get(target[0], (0, 0))[1] if len(target) > 2 else 0
        if layer == 0:
            sizes[target[0]] = (shape[-2], width + shape[-1])
        scratch += [pltpu.VMEM(buffer, jnp.bfloat16) for buffer in buffers]
    half = second_pre.shape[1] // (2 * inner)
    experts_shape = (2, half, second_pre.shape[0], inner)
    shapes = [
        jax.ShapeDtypeStruct(shape, jnp.bfloat16)
        for shape in (
            experts_shape,
            experts_shape,
            (2, half, *sizes[DOWN]),
            (2, *sizes[QKV]),
            (2, *sizes[OUT]),
            (2, *sizes[SMALL]),
        )
    ] + [jax.ShapeDtypeStruct(stats.shape, jnp.float32)]
    scratch += [
        pltpu.SemaphoreType.DMA((copies,)),
        pltpu.SemaphoreType.DMA((copies,)),
        pltpu.SemaphoreType.DMA((locals_,)),
    ]
    hops = lax.axis_size(GROUP) + 1
    scratch += [
        pltpu.VMEM((hops, *stats.shape), jnp.float32),
        pltpu.SemaphoreType.DMA((hops,)),
        pltpu.SemaphoreType.DMA((hops,)),
        pltpu.SemaphoreType.DMA((len(lanes) + 3 * half,)),
        pltpu.SemaphoreType.DMA((len(lanes) + 3 * half,)),
    ]
    return pl.pallas_call(
        functools.partial(sum_scatter_kernel, (plans, len(arrays), copies)),
        out_shape=shapes,
        in_specs=[pl.BlockSpec(memory_space=pl.ANY)] * (len(arrays) + 2)
        + [pl.BlockSpec(memory_space=pltpu.VMEM)],
        out_specs=[pl.BlockSpec(memory_space=pltpu.VMEM)] * len(shapes),
        scratch_shapes=scratch,
        compiler_params=pltpu.CompilerParams(
            collective_id=collective, has_side_effects=True, vmem_limit_bytes=60 * 2**20
        ),
    )(*arrays, second_pre, second_down, stats)


def bits_of(axis):
    return list(range(lax.axis_size(axis).bit_length() - 1))


def expert_lanes(first, inner):
    up, down = [(GROUP, bits_of(GROUP))], [(GROUP, bits_of(GROUP)[::-1])]
    return [
        (first, (False, ((2 * kind + j) * inner, inner)), (up, down)[kind], 0, (kind, j))
        for j in range(2)
        for kind in (GATE, UP)
    ]


def down_lanes(first, layer):
    up, down = [(GROUP, bits_of(GROUP))], [(GROUP, bits_of(GROUP)[::-1])]
    return [(first, 0, up, layer, (DOWN, 0)), (first, 1, down, layer, (DOWN, 1))]


def dense_lanes(first, width):
    up, down, deep = bits_of(GROUP), bits_of(GROUP)[::-1], bits_of(LINE)
    near = width * 2 // 5 // COLUMNS * COLUMNS
    away = width - near
    return [
        (
            first,
            (True, (0, away)),
            [(LINE, deep), (GROUP, up)],
            0,
            (QKV, slice(None), pl.ds(0, away)),
        ),
        (
            first,
            (False, (away, near)),
            [(GROUP, up), (LINE, deep)],
            0,
            (QKV, slice(None), pl.ds(away, near)),
        ),
        (first + 1, (False, None), [(GROUP, down), (LINE, deep)], 0, (OUT,)),
        small_lane(first + 2, 0),
    ]


def small_lane(first, layer):
    phases = [(GROUP, bits_of(GROUP)), (LINE, bits_of(LINE))]
    return (first, (False, None), phases, layer, (SMALL,))


def attention_forward(inputs, weights, segment_row):
    gain_attn, w_query, w_key, w_value, w_out, gain_moe = weights[:6]
    length = inputs.shape[0]
    cosine_table, sine_table = rotary_tables(length)
    inverse_one = lax.rsqrt(jnp.mean(inputs * inputs, axis=-1, keepdims=True) + EPSILON)
    normed_one = (inputs * inverse_one * gain_attn).astype(jnp.bfloat16)
    queries = rotate(
        matmul(normed_one, w_query).reshape(length, H, HD), cosine_table, sine_table
    ).astype(jnp.bfloat16)
    key_rows = rotate(
        matmul(normed_one, w_key).reshape(length, KVH, HD), cosine_table, sine_table
    ).astype(jnp.bfloat16)
    values = matmul(normed_one, w_value).astype(jnp.bfloat16).reshape(length, KVH, HD)
    scores = attention_scores(queries, key_rows, segment_row)
    highest = jnp.max(scores, axis=-1, keepdims=True)
    exponent = jnp.exp(scores - highest)
    denominator = jnp.sum(exponent, axis=-1, keepdims=True)
    weight = exponent / denominator
    attended = jnp.einsum(
        "kgqs,skd->qkgd", weight.astype(jnp.bfloat16), values, preferred_element_type=jnp.float32
    )
    attended = attended.reshape(length, H * HD).astype(jnp.bfloat16)
    hidden = inputs + matmul(attended, w_out)
    inverse_two = lax.rsqrt(jnp.mean(hidden * hidden, axis=-1, keepdims=True) + EPSILON)
    normed_two = (hidden * inverse_two * gain_moe).astype(jnp.bfloat16)
    state = (inverse_one, normed_one, queries, key_rows, values, weight, attended, hidden, inverse_two, normed_two)
    return state


MESH = pl.DeviceIdType.MESH
PARTS = 3


def move_rows(sources, held, pieces, sems, compute, z, n, others):
    row_send, row_recv, sum_send, sum_recv = sems
    barrier = pltpu.get_barrier_semaphore()
    for k in range(1, n):
        peer = lax.rem(z + k, n)
        pl.semaphore_signal(barrier, inc=1, device_id={LINE: peer}, device_id_type=MESH)
    for peer in others:
        pl.semaphore_signal(barrier, inc=1, device_id=peer, device_id_type=MESH)
    pl.semaphore_wait(barrier, n - 1 + len(others))

    def row_copy(kind, way, hop, source=None):
        step = 1 - 2 * way
        block = jnp.clip(z - step * hop, 0, n - 1)
        peer = jnp.clip(z + step, 0, n - 1)
        return pltpu.make_async_remote_copy(
            src_ref=held[kind].at[block] if source is None else source,
            dst_ref=held[kind].at[block],
            send_sem=row_send.at[kind, way, hop],
            recv_sem=row_recv.at[kind, way, hop],
            device_id={LINE: peer},
            device_id_type=MESH,
        )

    def sends(way, hop):
        step = 1 - 2 * way
        block, peer = z - step * hop, z + step
        return (block >= 0) & (block < n) & (peer >= 0) & (peer < n)

    def arrives(way, hop):
        block = z - (1 - 2 * way) * (hop + 1)
        return (block >= 0) & (block < n)

    def start(kind):
        for way in range(2):
            @pl.when(sends(way, 0))
            def _():
                row_copy(kind, way, 0, sources[kind]).start()

    def take(hop):
        for kind in range(len(held)):
            for way in range(2):
                @pl.when(arrives(way, hop))
                def _():
                    row_copy(kind, way, hop).wait_recv()

                @pl.when(sends(way, hop + 1) & (hop + 1 < n - 1))
                def _():
                    row_copy(kind, way, hop + 1).start()

    def waits(way, block):
        peer, last = z - (1 - 2 * way), (n - 1) * (1 - way)
        return (peer >= 0) & (peer < n) & ((block != last) | (peer != n - 1 - last))

    def far_copy(p):
        mine, arrived = pieces[p]
        block, way = n - 1 - z, jnp.where(z == 0, 1, 0)
        return pltpu.make_async_remote_copy(
            src_ref=mine(block),
            dst_ref=arrived(way, block),
            send_sem=sum_send.at[block, p],
            recv_sem=sum_recv.at[way, block, p],
            device_id={LINE: block},
            device_id_type=MESH,
        )

    def sum_copy(way, block, p):
        mine, arrived = pieces[p]
        return pltpu.make_async_remote_copy(
            src_ref=mine(block),
            dst_ref=arrived(way, block),
            send_sem=sum_send.at[block, p],
            recv_sem=sum_recv.at[way, block, p],
            device_id={LINE: jnp.clip(z + 1 - 2 * way, 0, n - 1)},
            device_id_type=MESH,
        )

    def sent(block, p):
        way = jnp.where(block > z, 0, 1)
        far = ((z == 0) | (z == n - 1)) & (block == n - 1 - z)

        @pl.when(far)
        def _():
            far_copy(p).start()

        @pl.when((block != z) & jnp.logical_not(far) & jnp.logical_not(waits(way, block)))
        def _():
            sum_copy(way, block, p).start()

    def run():
        def both(hop):
            return (hop >= 0) & (z - 1 - hop >= 0) & (z + 1 + hop < n)

        def turn(k, carry):
            hop = lax.div(k + 1, 2) - 1
            block = z + (1 + hop) * (1 - 2 * lax.rem(k, 2))
            odd = lax.rem(k, 2) == 1

            @pl.when(odd & jnp.logical_not(both(hop - 1)))
            def _():
                take(hop)

            @pl.when(jnp.logical_not(odd) & both(hop) & (hop + 1 < n - 1))
            def _():
                take(hop + 1)

            @pl.when((block >= 0) & (block < n))
            def _():
                compute(block, sent)

            return carry

        lax.fori_loop(0, 2 * n - 1, turn, 0)

        first = jnp.where(2 * z < n, 0, 1)
        for way in (first, 1 - first):
            for k in range(1, n):
                block = z + (1 - 2 * way) * k

                @pl.when(waits(way, block) & (block >= 0) & (block < n))
                def _():
                    for p, (mine, arrived) in enumerate(pieces):
                        sum_copy(way, block, p).wait_recv()
                        own, other = mine(block), arrived(way, block)
                        own[...] = (
                            own[...].astype(jnp.float32) + other[...].astype(jnp.float32)
                        ).astype(jnp.bfloat16)
                        sum_copy(way, block, p).start()

    def collect(add):
        for way in range(2):
            for p, (_, arrived) in enumerate(pieces):
                sum_copy(way, z, p).wait_recv()
                add(p, arrived(way, z)[...].astype(jnp.float32))

    def finish():
        for kind in range(len(held)):
            for way in range(2):
                for hop in range(n - 1):
                    @pl.when(sends(way, hop))
                    def _():
                        row_copy(kind, way, hop).wait_send()
        for k in range(1, n):
            for p in range(len(pieces)):
                sum_copy(0, lax.rem(z + k, n), p).wait_send()

    return start, run, collect, finish


def row_pieces(sums, returned, parts):
    width = sums.shape[2] // parts

    def piece(p):
        at = pl.ds(p * width, width)
        return (
            lambda block: sums.at[block, :, at],
            lambda way, block: returned.at[way, block, :, at],
        )

    return [piece(p) for p in range(parts)]


def fetch_weights(layer, own, other, places, sem):
    count = places[0].shape[0]
    mine = lax.axis_index(CORE) == layer

    def copy(group, kind, e):
        return pltpu.make_async_copy(
            group[kind].at[e], places[kind].at[e], sem.at[kind * count + e]
        )

    for kind in range(len(places)):
        for e in range(count):
            @pl.when(mine)
            def _():
                copy(own, kind, e).start()

            @pl.when(jnp.logical_not(mine))
            def _():
                copy(other, kind, e).start()

    def wait():
        for kind in range(len(places)):
            for e in range(count):
                copy(own, kind, e).wait()

    return wait


def sigmoid_of(value):
    return 1.0 / (1.0 + jnp.exp(-value))


def column_of(block, column):
    here = lax.broadcasted_iota(jnp.int32, block.shape, 1) == column
    return jnp.sum(jnp.where(here, block, 0.0), axis=1, keepdims=True)


def experts_forward_kernel(
    layer, experts, x, mask, hidden, router, *refs
):
    own, other, refs = refs[:3], refs[3:6], refs[6:]
    own_dense, other_dense, refs = refs[:4], refs[4:8], refs[8:]
    out, rows, gates_all, gates, gate_keep, up_keep, gated, stats = refs[:8]
    placed, place_sem = refs[8:12], refs[-1]
    passing, refs = refs[-5:-1], refs[:8] + refs[12:-5]
    w_gate, w_up, w_down, sums, returned, mixed, total, stats_all = refs[8:16]
    weight_sem, *sems = refs[16:]
    n, held = rows.shape[0], w_gate.shape[0]
    z = lax.axis_index(LINE)

    def compute(block, sent):
        picked = rows[block]
        gate_block = gates_all[block].astype(jnp.float32)

        def one(e, carry):
            gate_pre = jnp.dot(picked, w_gate[e], preferred_element_type=jnp.float32)
            up_pre = jnp.dot(picked, w_up[e], preferred_element_type=jnp.float32)
            gate_keep[e, block] = gate_pre.astype(jnp.bfloat16)
            up_keep[e, block] = up_pre.astype(jnp.bfloat16)
            active = gate_pre * sigmoid_of(gate_pre) * up_pre
            share = (column_of(gate_block, z * held + e) * active).astype(jnp.bfloat16)
            inner = share.shape[1]
            gated[block, :, pl.ds(pl.multiple_of(e * inner, inner), inner)] = share
            mixed[e] = share
            return carry

        lax.fori_loop(0, held, one, 0)
        width = out.shape[1] // PARTS
        for part in range(PARTS):
            at = pl.ds(part * width, width)
            result = jnp.zeros((out.shape[0], width), jnp.float32)
            for e in range(held):
                result += jnp.dot(mixed[e], w_down[e, :, at], preferred_element_type=jnp.float32)

            @pl.when(block == z)
            def _():
                total[:, at] = hidden[:, at] + result

            @pl.when(block != z)
            def _():
                sums[block, :, at] = result.astype(jnp.bfloat16)

            sent(block, part)

    own_gates = gates_all.at[z]
    start, run, collect, finish = move_rows(
        (x, own_gates, stats_all.at[z]),
        (rows, gates_all, stats_all),
        row_pieces(sums, returned, PARTS),
        sems,
        compute,
        z,
        n,
        [],
    )
    start(0)
    wait_weights = fetch_weights(layer, own, other, (w_gate, w_up, w_down), weight_sem)
    here = lax.axis_index(CORE) == 1 - layer

    def place_copy(group, i):
        return pltpu.make_async_copy(group[i], passing[i], place_sem.at[0, i])

    def place_out(i):
        return pltpu.make_async_copy(passing[i], placed[i], place_sem.at[1, i])

    logits = jnp.dot(x[...], router[...], preferred_element_type=jnp.float32)
    chosen = mask[...] > 0
    highest = jnp.max(jnp.where(chosen, logits, MASKED), axis=1, keepdims=True)
    exponent = jnp.where(chosen, jnp.exp(logits - highest), 0.0)
    gates[...] = exponent / jnp.sum(exponent, axis=1, keepdims=True)
    own_gates[...] = gates[...].astype(jnp.bfloat16)
    start(1)
    real = lax.broadcasted_iota(jnp.int32, logits.shape, 1) < experts
    highest = jnp.max(jnp.where(real, logits, MASKED), axis=1, keepdims=True)
    exponent = jnp.where(real, jnp.exp(logits - highest), 0.0)
    chance = exponent / jnp.sum(exponent, axis=1, keepdims=True)
    line = lax.broadcasted_iota(jnp.int32, stats.shape, 0)
    stats_all[z] = jnp.where(
        line == 0,
        jnp.sum(chance, axis=0, keepdims=True),
        jnp.where(line == 1, jnp.sum(mask[...], axis=0, keepdims=True), 0.0),
    )
    start(2)
    rows[z] = x[...]
    wait_weights()
    for i in range(4):
        @pl.when(here)
        def _():
            place_copy(own_dense, i).start()

        @pl.when(jnp.logical_not(here))
        def _():
            place_copy(other_dense, i).start()

    run()
    for i in range(4):
        place_copy(own_dense, i).wait()
        place_out(i).start()
    stats[...] = jnp.sum(stats_all[...], axis=0)
    width = out.shape[1] // PARTS

    def add(p, value):
        total[:, p * width : (p + 1) * width] += value

    collect(add)
    out[...] = total[...].astype(jnp.bfloat16)
    finish()
    for i in range(4):
        place_out(i).wait()


def experts_backward_kernel(layer, grad, gates, gate_keep, up_keep, *refs):
    own, other, saved_rows, saved_gated, refs = refs[:3], refs[3:6], refs[6], refs[7], refs[8:]
    carried = layer == 0
    if carried:
        extra, refs = refs[0], refs[1:]
        extra_sum, refs = refs[6], refs[:6] + refs[7:]
        landed, extra_send, extra_recv = refs[-3:]
        refs = refs[:-3]
    out, out_gates, rows_both, gated_both, grad_both, pre_both = refs[:6]
    w_gate, w_up, w_down, sums, sum_gates, returned, returned_gates, away, dots = refs[6:15]
    weight_sem, core_send, core_recv, core_local, *sems = refs[15:]
    n, held = gates.shape[0], w_gate.shape[0]
    half, inner = held // 2, w_gate.shape[2]
    core = lax.axis_index(CORE)
    z = lax.axis_index(LINE)
    turned_dims = (((1,), (1,)), ((), ()))
    rows = grad_both.at[core]

    def to_core(number, source, target):
        return pltpu.make_async_remote_copy(
            src_ref=source,
            dst_ref=target,
            send_sem=core_send.at[number],
            recv_sem=core_recv.at[number],
            device_id={CORE: 1 - core},
            device_id_type=MESH,
        )

    def block_copies(block):
        return (
            to_core(2 + block, rows.at[block], rows.at[block]),
            to_core(2 + n + block, away.at[block], pre_both.at[core, block]),
        )

    def columns(at):
        return pl.ds(pl.multiple_of(at * half * inner, half * inner), half * inner)

    def whole_copies():
        return (
            to_core(0, saved_rows, rows_both.at[core]),
            to_core(1, saved_gated.at[:, :, columns(1 - core)], gated_both.at[core]),
        )

    def local_copies():
        return (
            pltpu.make_async_copy(saved_rows, rows_both.at[core], core_local.at[0]),
            pltpu.make_async_copy(
                saved_gated.at[:, :, columns(core)], gated_both.at[core], core_local.at[1]
            ),
        )

    me, count = lax.axis_index(GROUP), lax.axis_size(GROUP)
    peers = [lax.rem(me + k, count) for k in range(1, count)] if carried else []

    def extra_copy(k, peer, slot):
        return pltpu.make_async_remote_copy(
            src_ref=extra.at[:, peer],
            dst_ref=landed.at[slot],
            send_sem=extra_send.at[k],
            recv_sem=extra_recv.at[slot],
            device_id={GROUP: peer},
            device_id_type=MESH,
        )

    def compute(block, sent):
        picked = rows[block]
        gate_block = gates[block].astype(jnp.float32)
        dots[...] = jnp.zeros(dots.shape, jnp.float32)

        def one(e, place, j):
            raw = lax.dot_general(
                picked, w_down[e], turned_dims, preferred_element_type=jnp.float32
            )
            gate_pre = gate_keep[e, block].astype(jnp.float32)
            up_pre = up_keep[e, block].astype(jnp.float32)
            sigmoid = sigmoid_of(gate_pre)
            silu = gate_pre * sigmoid
            column = z * held + e
            dot = jnp.sum(raw * (silu * up_pre), axis=1, keepdims=True)
            here = lax.broadcasted_iota(jnp.int32, dots.shape, 1) == column
            dots[...] += jnp.where(here, dot, 0.0)
            active = column_of(gate_block, column) * raw
            place[:, pl.ds(pl.multiple_of(j * inner, inner), inner)] = (
                active * up_pre * sigmoid * (1.0 + gate_pre * (1.0 - sigmoid))
            ).astype(jnp.bfloat16)
            place[:, pl.ds(pl.multiple_of((half + j) * inner, inner), inner)] = (
                active * silu
            ).astype(jnp.bfloat16)

        def own_half(j, carry):
            one(core * half + j, pre_both.at[core, block], j)
            return carry

        def other_half(j, carry):
            one((1 - core) * half + j, away.at[block], j)
            return carry

        lax.fori_loop(0, half, other_half, 0)
        for copy in block_copies(block):
            copy.start()
        lax.fori_loop(0, half, own_half, 0)
        sum_gates[block] = dots[...].astype(jnp.bfloat16)

        @pl.when(block == z)
        def _():
            out_gates[...] = dots[...]

        sent(block, PARTS)
        width = out.shape[1] // PARTS
        for part in range(PARTS):
            at = pl.ds(part * width, width)
            result = jnp.zeros((out.shape[0], width), jnp.float32)
            for place, side in ((away.at[block], 1 - core), (pre_both.at[core, block], core)):
                for kind, right in enumerate((w_gate, w_up)):
                    for j in range(half):
                        left = place[:, pl.ds((kind * half + j) * inner, inner)]
                        result += lax.dot_general(
                            left,
                            right[side * half + j, at, :],
                            turned_dims,
                            preferred_element_type=jnp.float32,
                        )

            @pl.when(block == z)
            def _():
                out[:, at] = result

            @pl.when(block != z)
            def _():
                sums[block, :, at] = result.astype(jnp.bfloat16)

            sent(block, part)

    gate_piece = (lambda block: sum_gates.at[block], lambda way, block: returned_gates.at[way, block])
    start, run, collect, finish = move_rows(
        (grad,),
        (rows,),
        row_pieces(sums, returned, PARTS) + [gate_piece],
        sems,
        compute,
        z,
        n,
        [{CORE: 1 - core}] + [{GROUP: peer} for peer in peers],
    )
    start(0)
    for k, peer in enumerate(peers):
        extra_copy(k, peer, me).start()
    if carried:
        mine = pltpu.make_async_copy(extra.at[:, me], landed.at[me], extra_send.at[len(peers)])
        mine.start()
    wait_weights = fetch_weights(layer, own, other, (w_gate, w_up, w_down), weight_sem)
    for copy in whole_copies() + local_copies():
        copy.start()
    rows[z] = grad[...]
    wait_weights()
    run()
    width = out.shape[1] // PARTS

    def add(p, value):
        if p == PARTS:
            out_gates[...] += value
        else:
            out[:, p * width : (p + 1) * width] += value

    if carried:
        mine.wait()
        for k, peer in enumerate(peers):
            extra_copy(k, peer, peer).wait_recv()
        half, rows_each = extra_sum.shape[:2]
        step = 16 if rows_each % 16 == 0 else rows_each

        def add_up(i, carry):
            at = pl.ds(pl.multiple_of(i * step, step), step)
            for j in range(half):
                value = landed[0, j, at].astype(jnp.float32)
                for k in range(1, count):
                    value += landed[k, j, at].astype(jnp.float32)
                extra_sum[j, at] = value.astype(jnp.bfloat16)
            return carry

        lax.fori_loop(0, rows_each // step, add_up, 0)
    collect(add)
    finish()
    for k, peer in enumerate(peers):
        extra_copy(k, peer, me).wait_send()
    for copy in local_copies():
        copy.wait()
    for copy in whole_copies():
        copy.wait()
    for block in range(n):
        for copy in block_copies(block):
            copy.wait()


def exchange_scratch(n, kinds_out, kinds_back):
    return [
        pltpu.SemaphoreType.DMA((kinds_out, 2, n)),
        pltpu.SemaphoreType.DMA((kinds_out, 2, n)),
        pltpu.SemaphoreType.DMA((n, kinds_back)),
        pltpu.SemaphoreType.DMA((2, n, kinds_back)),
    ]


def expert_call(kernel, operands, own, other, extra, shapes, scratch, collective, loose=0):
    vmem, free = pl.BlockSpec(memory_space=pltpu.VMEM), pl.BlockSpec(memory_space=pl.ANY)
    weights = [pltpu.VMEM(array.shape, jnp.bfloat16) for array in own]
    return pl.pallas_call(
        kernel,
        out_shape=shapes,
        in_specs=[vmem] * len(operands) + [free] * (6 + len(extra)),
        out_specs=[vmem] * (len(shapes) - loose) + [free] * loose,
        scratch_shapes=weights + scratch,
        compiler_params=pltpu.CompilerParams(
            collective_id=collective, has_side_effects=True, vmem_limit_bytes=46 * 2**20
        ),
        cost_estimate=pl.CostEstimate(
            flops=10**10, bytes_accessed=10**7, transcendentals=0
        ),
    )(*operands, *own, *other, *extra)


def experts_forward(
    layer, normed_two, mask, hidden, router, own, other, own_dense, other_dense, experts
):
    n, held = lax.axis_size(LINE), own[0].shape[0]
    length, width = normed_two.shape
    inner = own[0].shape[2]
    low, full = jnp.bfloat16, jnp.float32
    kept = jax.ShapeDtypeStruct((held, n, length, inner), low)
    shapes = [
        jax.ShapeDtypeStruct((length, width), low),
        jax.ShapeDtypeStruct((n, length, width), low),
        jax.ShapeDtypeStruct((n, length, COLUMNS), low),
        jax.ShapeDtypeStruct((length, COLUMNS), full),
        kept,
        kept,
        jax.ShapeDtypeStruct((n, length, held * inner), low),
        jax.ShapeDtypeStruct((8, COLUMNS), full),
    ] + [jax.ShapeDtypeStruct(array.shape, low) for array in own_dense]
    scratch = [
        pltpu.VMEM((n, length, width), low),
        pltpu.VMEM((2, n, length, width), low),
        pltpu.VMEM((held, length, inner), low),
        pltpu.VMEM((length, width), full),
        pltpu.VMEM((n, 8, COLUMNS), full),
        pltpu.SemaphoreType.DMA((3 * held,)),
    ] + exchange_scratch(n, 3, PARTS)
    scratch += [pltpu.VMEM(array.shape, low) for array in own_dense]
    scratch.append(pltpu.SemaphoreType.DMA((2, 4)))
    kernel = functools.partial(experts_forward_kernel, layer, experts)
    return expert_call(
        kernel,
        (normed_two, mask, hidden, router),
        own,
        other,
        (*own_dense, *other_dense),
        shapes,
        scratch,
        1 + layer,
        4,
    )


def experts_backward(layer, grad_low, gates, gate_keep, up_keep, rows, gated, own, other, extra):
    held, n, length, inner = gate_keep.shape
    width = grad_low.shape[1]
    low, full = jnp.bfloat16, jnp.float32
    shapes = [
        jax.ShapeDtypeStruct((length, width), full),
        jax.ShapeDtypeStruct((length, COLUMNS), full),
        jax.ShapeDtypeStruct((2, n, length, width), low),
        jax.ShapeDtypeStruct((2, n, length, held // 2 * inner), low),
        jax.ShapeDtypeStruct((2, n, length, width), low),
        jax.ShapeDtypeStruct((2, n, length, held * inner), low),
    ]
    scratch = [
        pltpu.VMEM((n, length, width), low),
        pltpu.VMEM((n, length, COLUMNS), low),
        pltpu.VMEM((2, n, length, width), low),
        pltpu.VMEM((2, n, length, COLUMNS), low),
        pltpu.VMEM((n, length, held * inner), low),
        pltpu.VMEM((length, COLUMNS), full),
        pltpu.SemaphoreType.DMA((3 * held,)),
        pltpu.SemaphoreType.DMA((2 + 2 * n,)),
        pltpu.SemaphoreType.DMA((2 + 2 * n,)),
        pltpu.SemaphoreType.DMA((2,)),
    ] + exchange_scratch(n, 1, PARTS + 1)
    if layer == 0:
        half, count, *block = extra.shape
        shapes.append(jax.ShapeDtypeStruct((half, *block), low))
        scratch += [
            pltpu.VMEM((count, half, *block), low),
            pltpu.SemaphoreType.DMA((count,)),
            pltpu.SemaphoreType.DMA((count,)),
        ]
    kernel = functools.partial(experts_backward_kernel, layer)
    return expert_call(
        kernel,
        (grad_low, gates, gate_keep, up_keep),
        own,
        other,
        (rows, gated) if extra is None else (rows, gated, extra),
        shapes,
        scratch,
        3 + layer,
    )


def attention_backward(grad_hidden, inputs, state, weights):
    gain_attn, w_query, w_key, w_value, w_out, gain_moe = weights[:6]
    (inverse_one, normed_one, queries, key_rows, values, weight, attended, hidden, inverse_two, normed_two) = state
    length = inputs.shape[0]
    grad_branch = grad_hidden.astype(jnp.bfloat16)
    grad_attended = jnp.einsum("td,cd->tc", grad_branch, w_out, preferred_element_type=jnp.float32)
    grad_attended = grad_attended.astype(jnp.bfloat16).reshape(length, KVH, H // KVH, HD)
    grad_weight = jnp.einsum(
        "qkgd,skd->kgqs", grad_attended, values, preferred_element_type=jnp.float32
    )
    grad_values = jnp.einsum(
        "kgqs,qkgd->skd",
        weight.astype(jnp.bfloat16),
        grad_attended,
        preferred_element_type=jnp.float32,
    )
    grad_values = grad_values.astype(jnp.bfloat16).reshape(length, KVH * HD)
    grad_scores = (
        weight * (grad_weight - jnp.sum(weight * grad_weight, axis=-1, keepdims=True))
    ).astype(jnp.bfloat16)
    score_scale = HD ** (-0.5)
    grouped = queries.reshape(length, KVH, H // KVH, HD)
    grad_queries = jnp.einsum(
        "kgqs,skd->qkgd", grad_scores, key_rows, preferred_element_type=jnp.float32
    )
    grad_queries = grad_queries.reshape(length, H, HD) * score_scale
    grad_keys = (
        jnp.einsum("kgqs,qkgd->skd", grad_scores, grouped, preferred_element_type=jnp.float32)
        * score_scale
    )
    cosine_table, sine_table = rotary_tables(length)
    grad_query_pre = (
        unrotate(grad_queries, cosine_table, sine_table)
        .reshape(length, H * HD)
        .astype(jnp.bfloat16)
    )
    grad_key_pre = (
        unrotate(grad_keys, cosine_table, sine_table).reshape(length, KVH * HD).astype(jnp.bfloat16)
    )
    grad_normed_one = (
        jnp.einsum("tq,cq->tc", grad_query_pre, w_query, preferred_element_type=jnp.float32)
        + jnp.einsum("tq,cq->tc", grad_key_pre, w_key, preferred_element_type=jnp.float32)
        + jnp.einsum("tq,cq->tc", grad_values, w_value, preferred_element_type=jnp.float32)
    )
    grad_norm_one, grad_gain_attn = norm_back(grad_normed_one, inputs, inverse_one, gain_attn)
    grad_inputs = grad_hidden + grad_norm_one
    grad_qkv = jnp.concatenate([grad_query_pre, grad_key_pre, grad_values], axis=1)
    return grad_inputs, grad_gain_attn, grad_qkv, grad_branch


class Halving:
    def __init__(self, array, order):
        self.order, self.left = list(order), sorted(order, reverse=True)
        count = len(self.left)
        self.array = array.reshape(*(2,) * count, array.shape[0] >> count, array.shape[1])

    def split(self):
        bit = self.order[0]
        mine = (lax.axis_index(GROUP) >> bit) & 1
        at = self.left.index(bit)
        self.keep, self.away = (
            lax.dynamic_index_in_dim(self.array, side, at, keepdims=False)
            for side in (mine, 1 - mine)
        )

    def send(self):
        bit = self.order.pop(0)
        self.left.remove(bit)
        count = lax.axis_size(GROUP)
        pairs = [(i, i ^ (1 << bit)) for i in range(count)]
        self.got = lax.ppermute(self.away, GROUP, pairs)

    def add(self):
        total = self.keep.astype(jnp.float32) + self.got.astype(jnp.float32)
        self.array = total.astype(jnp.bfloat16)


def turned(left, right):
    return jnp.einsum("tc,tq->cq", left, right, preferred_element_type=jnp.float32)


def body(tokens, cotangent, segments, routes, *weight_arrays):
    core = lax.axis_index(CORE)
    first = core == 0
    experts = weight_arrays[6].shape[2]
    w_gate = weight_arrays[7]
    held = w_gate.shape[1]
    own = [array[0] for array in weight_arrays]
    other = [swapped(array) for array in own]
    weights = [
        [jnp.where(first, a, b) for a, b in zip(own[:7], other[:7])],
        [jnp.where(first, b, a) for a, b in zip(own[:7], other[:7])],
    ]
    inputs_low = lax.dynamic_slice_in_dim(tokens, core * SEQ, SEQ, 0)
    grad_low = lax.dynamic_slice_in_dim(cotangent, core * SEQ, SEQ, 0)
    segment_row = lax.dynamic_index_in_dim(segments, core, 0, keepdims=False)
    mine = lax.dynamic_slice_in_dim(routes[0], core * SEQ, SEQ, 0)
    got = swapped(lax.dynamic_slice_in_dim(routes[0], (1 - core) * SEQ, SEQ, 0))
    routes_here = jnp.stack([jnp.where(first, mine, got), jnp.where(first, got, mine)])
    masks = multi_hot(routes_here, COLUMNS)
    own_experts, other_experts = own[7:], other[7:]

    saved, outs, stats = [], [], []
    for s in range(2):
        inputs = inputs_low.astype(jnp.float32)
        state = attention_forward(inputs, weights[s], segment_row)
        hidden, normed_two = state[7], state[9]
        both_cores = [jnp.concatenate([a, swapped(a)]) for a in (state[1], state[6])]
        router = jnp.pad(weights[s][6], ((0, 0), (0, COLUMNS - experts)))
        inputs_low, *expert_state, stat, query, key, value, out = experts_forward(
            s,
            normed_two,
            masks[s],
            hidden,
            router,
            own_experts,
            other_experts,
            own[1:5],
            other[1:5],
            experts,
        )
        weights[1 - s][1:5] = [query, key, value, out]
        outs.append(inputs_low)
        stats.append(stat)
        saved.append((inputs, state, expert_state, both_cores))

    dp, deep = lax.axis_size(GROUP), lax.axis_size(LINE)
    grads = [None, None]
    input_grads = [None, None]
    for s in (1, 0):
        inputs, state, expert_state, both_cores = saved[s]
        (inverse_one, normed_one, _, _, _, _, attended, hidden, inverse_two, normed_two) = state
        rows_all, gates_all, gates, gate_keep, up_keep, gated = expert_state
        gain_moe, w_router = weights[s][5], weights[s][6]
        grad_sum, grad_gates, rows_both, gated_both, grad_both, pre_both, *sums = experts_backward(
            s,
            grad_low,
            gates_all,
            gate_keep,
            up_keep,
            rows_all,
            gated,
            own_experts,
            other_experts,
            None if s == 1 else grads[1][1].reshape(held // 2, dp, -1, D),
        )
        if s == 0:
            (second_down,) = sums
            for part in second:
                part.add()
            while second[0].order:
                for part in second:
                    part.split()
                grad_sum, *away = lax.optimization_barrier(
                    (grad_sum, *(part.away for part in second))
                )
                for part, value in zip(second, away):
                    part.away = value
                    part.send()
                if second[0].order:
                    for part in second:
                        part.add()
        inner = w_gate.shape[3]
        grad_gate_up = turned(
            rows_both.reshape(-1, D), pre_both.reshape(-1, held * inner)
        ).astype(jnp.bfloat16)
        if s == 1:
            grad_sum, grad_gate_up = lax.optimization_barrier((grad_sum, grad_gate_up))
            second_pre = lax.psum_scatter(grad_gate_up, GROUP, scatter_dimension=0, tiled=True)
        else:
            grad_sum, second_pre = lax.optimization_barrier((grad_sum, second_pre))
        gates, grad_gates = gates[:, :experts], grad_gates[:, :experts]
        grad_chosen = gates * (grad_gates - jnp.sum(gates * grad_gates, axis=-1, keepdims=True))
        grad_logits = grad_chosen.astype(jnp.bfloat16)
        grad_normed_two = grad_sum + jnp.einsum(
            "te,de->td", grad_logits, w_router, preferred_element_type=jnp.float32
        )
        grad_norm_two, grad_gain_moe = norm_back(grad_normed_two, hidden, inverse_two, gain_moe)
        grad_hidden = grad_low.astype(jnp.float32) + grad_norm_two
        grad_inputs, grad_gain_attn, grad_qkv, grad_branch = attention_backward(
            grad_hidden, inputs, state, weights[s]
        )
        if s == 1:
            grad_inputs, gated_both = lax.optimization_barrier((grad_inputs, gated_both))
        grad_down = turned(
            gated_both.reshape(-1, held // 2 * inner), grad_both.reshape(-1, D)
        ).astype(jnp.bfloat16)

        def halves(array):
            width = array.shape[1] // 2
            return (
                lax.dynamic_slice_in_dim(array, core * width, width, 1),
                lax.dynamic_slice_in_dim(array, (1 - core) * width, width, 1),
            )
        qkv_keep, qkv_send = halves(grad_qkv)
        branch_keep, branch_send = halves(grad_branch)
        grad_w_qkv = turned(
            both_cores[0], jnp.concatenate([qkv_keep, swapped(qkv_send)])
        ).astype(jnp.bfloat16)
        grad_w_out = turned(
            both_cores[1], jnp.concatenate([branch_keep, swapped(branch_send)])
        ).astype(jnp.bfloat16)
        grad_w_router = turned(normed_two, grad_logits)
        small = jnp.concatenate(
            [grad_gain_attn[:, None], grad_gain_moe[:, None], grad_w_router], axis=1
        ).astype(jnp.bfloat16)
        small = jnp.pad(small, ((0, 0), (0, COLUMNS - small.shape[1])))
        if s == 1:
            bits = bits_of(GROUP)
            second = [Halving(grad_w_qkv, bits), Halving(grad_w_out, bits[::-1])]
            for part in second:
                part.split()
            grad_inputs, grad_down, *away = lax.optimization_barrier(
                (grad_inputs, grad_down, *(part.away for part in second))
            )
            for part, value in zip(second, away):
                part.away = value
                part.send()
        grads[s] = (grad_gate_up, grad_down, grad_w_qkv, grad_w_out, small)
        input_grads[s] = grad_inputs
        grad_low = grad_inputs.astype(jnp.bfloat16)

    dp, deep = lax.axis_size(GROUP), lax.axis_size(LINE)
    half, inner = held // 2, w_gate.shape[3]
    grad_gate_up, grad_down, grad_w_qkv, grad_w_out, small = grads[0]
    arrays = [
        grad_gate_up.reshape(dp, D // dp, held * inner),
        grad_down.reshape(half, dp, inner // dp, D),
    ]
    lanes = dense_lanes(2, grad_w_qkv.shape[1])
    for array in (grad_w_qkv, grad_w_out, small):
        arrays.append(array.reshape(dp, deep, array.shape[0] // (dp * deep), array.shape[1]))
    for part, kind in zip(second, (QKV, OUT)):
        grad_w_qkv, part.keep = lax.optimization_barrier((grad_w_qkv, part.keep))
        part.add()
        lanes.append((len(arrays), (False, None), [(LINE, bits_of(LINE))], 1, (kind,)))
        rows, columns = part.array.shape
        arrays.append(part.array.reshape(deep, rows // deep, columns))
    lanes.append(small_lane(len(arrays), 1))
    lanes += expert_lanes(0, inner) + down_lanes(1, 0)
    small = grads[1][4]
    arrays.append(small.reshape(dp, deep, small.shape[0] // (dp * deep), small.shape[1]))
    out_keep = jnp.where(first, outs[0], outs[1])
    out_got = swapped(jnp.where(first, outs[1], outs[0]))
    layer_out = jnp.where(
        first, jnp.concatenate([out_keep, out_got]), jnp.concatenate([out_got, out_keep])
    )
    low_one = input_grads[1].astype(jnp.bfloat16).astype(jnp.float32)
    grad_keep = jnp.where(first, input_grads[0], low_one)
    grad_got = swapped(jnp.where(first, low_one, input_grads[0]))
    input_grad = jnp.where(
        first, jnp.concatenate([grad_keep, grad_got]), jnp.concatenate([grad_got, grad_keep])
    )
    stats = jnp.concatenate(stats, axis=0)
    stats, layer_out, input_grad = lax.optimization_barrier((stats, layer_out, input_grad))
    *grads, qkv, out, small, stats = sum_scatter(
        arrays, lanes, second_pre, second_down, stats, inner, 0
    )
    full = jnp.float32
    w_gate_grad, w_up_grad, w_down_grad = (
        grad.reshape(held, *grad.shape[2:]).astype(full) for grad in grads
    )
    qkv = jnp.concatenate([qkv[0], qkv[1]], axis=1).astype(full)
    grad_w_out = jnp.concatenate([out[0], out[1]], axis=1).astype(full)
    small = small[0].astype(full) + small[1].astype(full)
    heads, kv = H * HD, KVH * HD
    stats = lax.dynamic_index_in_dim(stats.reshape(2, 8, COLUMNS), core, 0)
    token_total = SEQ * lax.axis_size((CORE, GROUP, LINE))
    counts, chances = stats[:, 1, :experts], stats[:, 0, :experts]
    balance = experts * (counts / (token_total * TOPK) * chances / token_total)
    results = (
        layer_out,
        input_grad,
        small[:, 0],
        qkv[:, :heads],
        qkv[:, heads : heads + kv],
        qkv[:, heads + kv :],
        grad_w_out,
        small[:, 1],
        small[:, 2 : 2 + experts],
        w_gate_grad,
        w_up_grad,
        w_down_grad,
    )
    return tuple(result[None] for result in results) + (balance,)


def solution(mesh):
    return jax.shard_map(
        body,
        mesh=mesh,
        in_specs=(
            P((GROUP, LINE), None),
            P((GROUP, LINE), None),
            P((GROUP, LINE), None),
            P(CORE, (GROUP, LINE), None),
            P(CORE, None),
            P(CORE, None, None),
            P(CORE, None, None),
            P(CORE, None, None),
            P(CORE, None, None),
            P(CORE, None),
            P(CORE, None, None),
            P(CORE, LINE, None, None),
            P(CORE, LINE, None, None),
            P(CORE, LINE, None, None),
        ),
        out_specs=(
            P(CORE, (GROUP, LINE), None),
            P(CORE, (GROUP, LINE), None),
            P(CORE, (GROUP, LINE)),
            P(CORE, (GROUP, LINE), None),
            P(CORE, (GROUP, LINE), None),
            P(CORE, (GROUP, LINE), None),
            P(CORE, (GROUP, LINE), None),
            P(CORE, (GROUP, LINE)),
            P(CORE, (GROUP, LINE), None),
            P(CORE, LINE, GROUP, None),
            P(CORE, LINE, GROUP, None),
            P(CORE, LINE, GROUP, None),
            P(CORE, None),
        ),
        check_vma=False,
    )
```

```python
import functools
import itertools
from types import SimpleNamespace

import jax
import jax.numpy as jnp
from jax import lax
from jax.experimental import pallas as pl
from jax.experimental.pallas import tpu as pltpu
from jax.sharding import PartitionSpec as P

D = 1536
H = 24
KVH = 8
HD = 64
TOPK = 8
SEQ = 96


EPSILON = 1e-05
THETA = 10000.0
MASKED = -1e30
COLUMNS = 128
GATE, UP, DOWN, QKV, OUT, SMALL = range(6)
CORE, GROUP, LINE = "section", "dp", "expert"
INNER = "inner"


def matmul(left_side, right_side):
    return jnp.dot(left_side, right_side, preferred_element_type=jnp.float32)


def rotary_tables(length):
    half_width = HD // 2
    position = jnp.arange(length, dtype=jnp.float32)[:, None]
    freq_rate = THETA ** (-jnp.arange(half_width, dtype=jnp.float32) / half_width)
    angles = position * freq_rate[None, :]
    return (jnp.cos(angles)[:, None, :], jnp.sin(angles)[:, None, :])


def rotate(tensor, cosine_table, sine_table):
    half_width = HD // 2
    first_half = tensor[..., :half_width]
    second_half = tensor[..., half_width:]
    return jnp.concatenate(
        [
            first_half * cosine_table - second_half * sine_table,
            second_half * cosine_table + first_half * sine_table,
        ],
        axis=-1,
    )


def unrotate(gradient, cosine_table, sine_table):
    half_width = HD // 2
    first_half = gradient[..., :half_width]
    second_half = gradient[..., half_width:]
    return jnp.concatenate(
        [
            first_half * cosine_table + second_half * sine_table,
            second_half * cosine_table - first_half * sine_table,
        ],
        axis=-1,
    )


def norm_back(grad_normed, tensor, inverse, gain_vector):
    scaled = grad_normed * gain_vector
    grad_gain = jnp.sum(grad_normed * tensor * inverse, axis=0)
    grad_tensor = inverse * scaled - tensor * inverse**3 * jnp.mean(
        scaled * tensor, axis=-1, keepdims=True
    )
    return (grad_tensor, grad_gain)


def attention_scores(queries, key_rows, segment_row):
    length = queries.shape[0]
    grouped = queries.reshape(length, KVH, H // KVH, HD)
    scores = jnp.einsum(
        "qkgd,skd->kgqs", grouped, key_rows, preferred_element_type=jnp.float32
    ) * HD ** (-0.5)
    position = jnp.arange(length)
    allowed = (position[None, :] <= position[:, None]) & (
        segment_row[:, None] == segment_row[None, :]
    )
    return jnp.where(allowed[None, None], scores, MASKED)


def multi_hot(route_rows, experts):
    columns = jnp.arange(experts, dtype=jnp.int32)
    return jnp.sum(
        (route_rows[..., None] == columns).astype(jnp.float32), axis=-2
    )


def swapped(array):
    return lax.ppermute(array, CORE, [(0, 1), (1, 0)])


def add_slab(total, arrived):
    *lead, rows, _ = total.shape
    step = 16 if rows % 16 == 0 else rows
    for where in itertools.product(*(range(n) for n in lead)):

        def add(i, carry):
            at = (*where, pl.ds(pl.multiple_of(i * step, step), step), slice(None))
            both = total[at].astype(jnp.float32) + arrived[at].astype(jnp.float32)
            total[at] = both.astype(jnp.bfloat16)
            return carry

        lax.fori_loop(0, rows // step, add, 0)


def sum_scatter_kernel(plan, *refs):
    lanes, ins, copies = plan
    sources = refs[:ins]
    second_pre, second_down, stats_in = refs[ins : ins + 3]
    stage, stats = refs[ins + 3 : ins + 9], refs[ins + 9]
    scratch = list(refs[ins + 10 :])
    send_sem, recv_sem, local_sem, stats_got, stats_send, stats_recv, core_send, core_recv = (
        scratch[-8:]
    )
    core = lax.axis_index(CORE)
    partners = []
    for lane in lanes:
        for axis, bits in lane.phases:
            partners += [(axis, bit) for bit in bits if (axis, bit) not in partners]
    partners.append((CORE, 0))
    index = {axis: lax.axis_index(axis) for axis, _ in partners}
    mine = {(axis, bit): (index[axis] >> bit) & 1 for axis, bit in partners}
    far = {key: index[key[0]] + (1 - 2 * mine[key]) * (1 << key[1]) for key in partners}
    barrier = pltpu.get_barrier_semaphore()
    peers = [{axis: far[axis, bit]} for axis, bit in partners if axis != GROUP]
    groups = lax.axis_size(GROUP)
    peers += [{GROUP: lax.rem(lax.axis_index(GROUP) + k, groups)} for k in range(1, groups)]
    for peer in peers:
        pl.semaphore_signal(
            barrier, inc=1, device_id=peer, device_id_type=pl.DeviceIdType.MESH
        )
    pl.semaphore_wait(barrier, len(peers))

    counter = itertools.count()

    def send(source, target, key):
        number = next(counter)
        copy = pltpu.make_async_remote_copy(
            src_ref=source,
            dst_ref=target,
            send_sem=send_sem.at[number],
            recv_sem=recv_sem.at[number],
            device_id={key[0]: far[key]},
            device_id_type=pl.DeviceIdType.MESH,
        )
        copy.start()
        return copy

    def place(axis, values):
        total = 0
        for bit, value in values.items():
            total = total + value * (1 << bit)
        return total

    def sum_stats():
        count = lax.axis_size(GROUP)
        me = lax.axis_index(GROUP)

        def copy(at, source, slot, target):
            return pltpu.make_async_remote_copy(
                src_ref=source,
                dst_ref=stats_got.at[slot],
                send_sem=stats_send.at[at],
                recv_sem=stats_recv.at[slot],
                device_id=target,
                device_id_type=pl.DeviceIdType.MESH,
            )

        for k in range(1, count):
            copy(k, stats_in, me, {GROUP: lax.rem(me + k, count)}).start()
        yield
        stats[...] = stats_in[...]
        for k in range(1, count):
            peer = lax.rem(me + k, count)
            copy(k, stats_in, peer, {GROUP: peer}).wait_recv()
            stats[...] += stats_got[peer]
        both = copy(0, stats, count, {CORE: far[CORE, 0]})
        both.start()
        yield
        both.wait()
        stats[...] += stats_got[count]
        for k in range(1, count):
            copy(k, stats_in, me, {GROUP: lax.rem(me + k, count)}).wait_send()

    summing = sum_stats()
    next(summing)

    def to_stage(number, source, kind, *at):
        spot = stage[kind].at[(core, *at)]
        return spot, pltpu.make_async_remote_copy(
            src_ref=source,
            dst_ref=spot,
            send_sem=core_send.at[number],
            recv_sem=core_recv.at[number],
            device_id={CORE: 1 - core},
            device_id_type=pl.DeviceIdType.MESH,
        )

    inner = stage[GATE].shape[3]
    wholes = []
    half = stage[GATE].shape[1]
    for number in range(3 * half):
        kind, j = divmod(number, half)
        if kind == DOWN:
            source = second_down.at[j]
        else:
            source = second_pre.at[:, pl.ds(number * inner, inner)]
        spot, copy = to_stage(len(lanes) + number, source, kind, j)
        wholes.append((copy, pltpu.make_async_copy(source, spot, core_send.at[len(lanes) + number])))
    for copy, here in wholes:
        @pl.when(core == 1)
        def _(here=here):
            here.start()

        @pl.when(core == 0)
        def _(copy=copy):
            copy.start()

    moved = []
    started = []
    states = []
    for number, lane in enumerate(lanes):
        count = len(lane.buffers)
        buffers, scratch = scratch[:count], scratch[count:]
        source = sources[lane.source]
        prefix = lane.prefix
        if isinstance(prefix, int):
            source = source.at[prefix]

        def part(at, source=source, prefix=prefix):
            if isinstance(prefix, int):
                return source.at[at]
            inner, columns = prefix
            where = (slice(None), at) if inner else (at,)
            if columns is not None:
                where += (slice(None),) * (len(source.shape) - len(where) - 1) + (pl.ds(*columns),)
            return source.at[where]

        axis, bits = lane.phases[0]
        total, arrived = buffers[0], buffers[1:]
        rest = [bit for bit in bits[1:]]
        pending = []
        for choice in itertools.product((0, 1), repeat=len(rest)):
            values = dict(zip(rest, choice))
            slot = sum(value << i for i, value in enumerate(choice))
            far_at = place(axis, {**values, bits[0]: 1 - mine[axis, bits[0]]})
            here_at = place(axis, {**values, bits[0]: mine[axis, bits[0]]})
            copy = send(part(far_at), arrived[0].at[slot], (axis, bits[0]))
            pending.append((copy, slot))
            started.append(copy)
            states.append((number, part(here_at), slot, total))
        lane_state = SimpleNamespace(total=total, arrived=arrived, pending=pending)
        lane.state = lane_state
    locals_ = {}
    for at, (number, here, slot, total) in enumerate(states):
        copy = pltpu.make_async_copy(here, total.at[slot], local_sem.at[at])
        copy.start()
        locals_[number, slot] = copy
    short = [item for item in enumerate(lanes) if len(item[1].phases) == 1 and item[1].rows]
    long = [item for item in enumerate(lanes) if item not in short]
    turns = [(1, long), (1, short)]
    count = max(sum(len(bits) for _, bits in lane.phases) for lane in lanes)
    for step in range(2, count + 1):
        turns += [(2 * step - 2, long), (2 * step - 1, long), (step, short)]
    for at, (step, group) in enumerate(turns):
        if at == 2:
            next(summing)
        for number, lane in group:
            state = lane.state
            sizes = [len(bits) for _, bits in lane.phases]
            if step > sum(sizes):
                continue
            if step <= sizes[0]:
                axis, bits = lane.phases[0]
                resolved, rest = bits[:step], bits[step:]

                def slot_of(values):
                    found = 0
                    for i, bit in enumerate(bits[1:]):
                        found = found + values.get(bit, mine[axis, bit]) * (1 << i)
                    return found

                for copy, slot in state.pending:
                    copy.wait_recv()
                    if step == 1:
                        locals_[number, slot].wait()
                state.pending_next = []
                for choice in itertools.product((0, 1), repeat=len(rest)):
                    values = dict(zip(rest, choice))
                    got = sum(value << i for i, value in enumerate(choice))
                    add_slab(
                        state.total.at[slot_of(values)], state.arrived[step - 1].at[got]
                    )
                if rest:
                    following = rest[1:]
                    for choice in itertools.product((0, 1), repeat=len(following)):
                        values = dict(zip(following, choice))
                        got = sum(value << i for i, value in enumerate(choice))
                        values[rest[0]] = 1 - mine[axis, rest[0]]
                        copy = send(
                            state.total.at[slot_of(values)],
                            state.arrived[step].at[got],
                            (axis, rest[0]),
                        )
                        state.pending_next.append((copy, got))
                        started.append(copy)
                final = state.total.at[slot_of({})] if not rest else None
            else:
                axis, bits = lane.phases[1]
                done = step - sizes[0]
                rest = bits[done:]
                final = state.final
                for copy, _ in state.pending:
                    copy.wait_recv()
                state.pending_next = []
                for choice in itertools.product((0, 1), repeat=len(rest)):
                    values = dict(zip(rest, choice))
                    got = sum(value << i for i, value in enumerate(choice))
                    at = place(axis, {bit: values.get(bit, mine[axis, bit]) for bit in bits})
                    add_slab(final.at[at], state.arrived[step - 1].at[got])
                if not rest:
                    at = place(axis, {bit: mine[axis, bit] for bit in bits})
                    final = final.at[at]
            if final is not None and step >= sizes[0]:
                state.final = final
                if step == sum(sizes):
                    spot, copy = to_stage(number, final, *lane.target)
                    moved.append((lane.layer, copy))

                    @pl.when(core == lane.layer)
                    def _(spot=spot, final=final):
                        spot[...] = final[...]

                    @pl.when(core != lane.layer)
                    def _(copy=copy):
                        copy.start()
                elif step < sum(sizes):
                    axis, bits = lane.phases[1]
                    done = step - sizes[0]
                    bit, following = bits[done], bits[done + 1 :]
                    for choice in itertools.product((0, 1), repeat=len(following)):
                        values = dict(zip(following, choice))
                        got = sum(value << i for i, value in enumerate(choice))
                        at = place(
                            axis,
                            {
                                b: values.get(b, 1 - mine[axis, b] if b == bit else mine[axis, b])
                                for b in bits
                            },
                        )
                        copy = send(final.at[at], state.arrived[step].at[got], (axis, bit))
                        state.pending_next.append((copy, got))
                        started.append(copy)
            state.pending = state.pending_next
    for _ in summing:
        pass

    for copy, here in wholes:
        @pl.when(core == 1)
        def _(copy=copy, here=here):
            copy.wait_recv()
            here.wait()

        @pl.when(core == 0)
        def _(copy=copy):
            copy.wait_send()

    for layer, copy in moved:
        @pl.when(core == layer)
        def _(copy=copy):
            copy.wait_recv()

        @pl.when(core != layer)
        def _(copy=copy):
            copy.wait_send()

    for copy in started:
        copy.wait_send()


def sum_scatter(arrays, lanes, second_pre, second_down, stats, inner, collective):
    plans, scratch, shapes, copies, locals_ = [], [], [], 0, 0
    sizes = {}
    for source, prefix, phases, layer, target in lanes:
        shape = arrays[source].shape
        if isinstance(prefix, int):
            shape = shape[1:]
        else:
            if prefix[0]:
                shape = (shape[1], shape[0], *shape[2:])
            if prefix[1] is not None:
                shape = (*shape[:-1], prefix[1][1])
        buffers = [(shape[0] // 2, *shape[1:])]
        for step in range(1, len(phases[0][1]) + 1):
            buffers.append((shape[0] >> step, *shape[1:]))
            copies += shape[0] >> step
        locals_ += shape[0] // 2
        if len(phases) > 1:
            for step in range(1, len(phases[1][1]) + 1):
                buffers.append((shape[1] >> step, *shape[2:]))
                copies += shape[1] >> step
        plans.append(
            SimpleNamespace(
                source=source,
                prefix=prefix,
                phases=phases,
                buffers=buffers,
                rows=phases[0][0] == GROUP,
                layer=layer,
                target=target,
            )
        )
        width = sizes.get(target[0], (0, 0))[1] if len(target) > 2 else 0
        if layer == 0:
            sizes[target[0]] = (shape[-2], width + shape[-1])
        scratch += [pltpu.VMEM(buffer, jnp.bfloat16) for buffer in buffers]
    half = second_pre.shape[1] // (2 * inner)
    experts_shape = (2, half, second_pre.shape[0], inner)
    shapes = [
        jax.ShapeDtypeStruct(shape, jnp.bfloat16)
        for shape in (
            experts_shape,
            experts_shape,
            (2, half, *sizes[DOWN]),
            (2, *sizes[QKV]),
            (2, *sizes[OUT]),
            (2, *sizes[SMALL]),
        )
    ] + [jax.ShapeDtypeStruct(stats.shape, jnp.float32)]
    scratch += [
        pltpu.SemaphoreType.DMA((copies,)),
        pltpu.SemaphoreType.DMA((copies,)),
        pltpu.SemaphoreType.DMA((locals_,)),
    ]
    hops = lax.axis_size(GROUP) + 1
    scratch += [
        pltpu.VMEM((hops, *stats.shape), jnp.float32),
        pltpu.SemaphoreType.DMA((hops,)),
        pltpu.SemaphoreType.DMA((hops,)),
        pltpu.SemaphoreType.DMA((len(lanes) + 3 * half,)),
        pltpu.SemaphoreType.DMA((len(lanes) + 3 * half,)),
    ]
    return pl.pallas_call(
        functools.partial(sum_scatter_kernel, (plans, len(arrays), copies)),
        out_shape=shapes,
        in_specs=[pl.BlockSpec(memory_space=pl.ANY)] * (len(arrays) + 2)
        + [pl.BlockSpec(memory_space=pltpu.VMEM)],
        out_specs=[pl.BlockSpec(memory_space=pltpu.VMEM)] * len(shapes),
        scratch_shapes=scratch,
        compiler_params=pltpu.CompilerParams(
            collective_id=collective, has_side_effects=True, vmem_limit_bytes=60 * 2**20
        ),
    )(*arrays, second_pre, second_down, stats)


def bits_of(axis):
    return list(range(lax.axis_size(axis).bit_length() - 1))


def expert_lanes(first, inner):
    up, down = [(GROUP, bits_of(GROUP))], [(GROUP, bits_of(GROUP)[::-1])]
    return [
        (first, (False, ((2 * kind + j) * inner, inner)), (up, down)[kind], 0, (kind, j))
        for j in range(2)
        for kind in (GATE, UP)
    ]


def down_lanes(first, layer):
    up, down = [(GROUP, bits_of(GROUP))], [(GROUP, bits_of(GROUP)[::-1])]
    return [(first, 0, up, layer, (DOWN, 0)), (first, 1, down, layer, (DOWN, 1))]


def dense_lanes(first, width):
    up, down, deep = bits_of(GROUP), bits_of(GROUP)[::-1], bits_of(LINE)
    near = width // 4 // COLUMNS * COLUMNS
    away = width - near
    return [
        (
            first,
            (True, (0, away)),
            [(LINE, deep), (GROUP, up)],
            0,
            (QKV, slice(None), pl.ds(0, away)),
        ),
        (
            first,
            (False, (away, near)),
            [(GROUP, up), (LINE, deep)],
            0,
            (QKV, slice(None), pl.ds(away, near)),
        ),
        (first + 1, (False, None), [(GROUP, down), (LINE, deep)], 0, (OUT,)),
        small_lane(first + 2, 0),
    ]


def small_lane(first, layer):
    phases = [(GROUP, bits_of(GROUP)), (LINE, bits_of(LINE))]
    return (first, (False, None), phases, layer, (SMALL,))


def attention_forward(inputs, weights, segment_row):
    gain_attn, w_query, w_key, w_value, w_out, gain_moe = weights[:6]
    length = inputs.shape[0]
    cosine_table, sine_table = rotary_tables(length)
    inverse_one = lax.rsqrt(jnp.mean(inputs * inputs, axis=-1, keepdims=True) + EPSILON)
    normed_one = (inputs * inverse_one * gain_attn).astype(jnp.bfloat16)
    queries = rotate(
        matmul(normed_one, w_query).reshape(length, H, HD), cosine_table, sine_table
    ).astype(jnp.bfloat16)
    key_rows = rotate(
        matmul(normed_one, w_key).reshape(length, KVH, HD), cosine_table, sine_table
    ).astype(jnp.bfloat16)
    values = matmul(normed_one, w_value).astype(jnp.bfloat16).reshape(length, KVH, HD)
    scores = attention_scores(queries, key_rows, segment_row)
    highest = jnp.max(scores, axis=-1, keepdims=True)
    exponent = jnp.exp(scores - highest)
    denominator = jnp.sum(exponent, axis=-1, keepdims=True)
    weight = exponent / denominator
    attended = jnp.einsum(
        "kgqs,skd->qkgd", weight.astype(jnp.bfloat16), values, preferred_element_type=jnp.float32
    )
    attended = attended.reshape(length, H * HD).astype(jnp.bfloat16)
    hidden = inputs + matmul(attended, w_out)
    inverse_two = lax.rsqrt(jnp.mean(hidden * hidden, axis=-1, keepdims=True) + EPSILON)
    normed_two = (hidden * inverse_two * gain_moe).astype(jnp.bfloat16)
    state = (inverse_one, normed_one, queries, key_rows, values, weight, attended, hidden, inverse_two, normed_two)
    return state


MESH = pl.DeviceIdType.MESH
PARTS = 3


def move_rows(sources, held, pieces, sems, compute, z, n, others):
    row_send, row_recv, sum_send, sum_recv = sems
    barrier = pltpu.get_barrier_semaphore()
    for k in range(1, n):
        peer = lax.rem(z + k, n)
        pl.semaphore_signal(barrier, inc=1, device_id={LINE: peer}, device_id_type=MESH)
    for peer in others:
        pl.semaphore_signal(barrier, inc=1, device_id=peer, device_id_type=MESH)
    pl.semaphore_wait(barrier, n - 1 + len(others))

    def row_copy(kind, way, hop, source=None):
        step = 1 - 2 * way
        block = jnp.clip(z - step * hop, 0, n - 1)
        peer = jnp.clip(z + step, 0, n - 1)
        return pltpu.make_async_remote_copy(
            src_ref=held[kind].at[block] if source is None else source,
            dst_ref=held[kind].at[block],
            send_sem=row_send.at[kind, way, hop],
            recv_sem=row_recv.at[kind, way, hop],
            device_id={LINE: peer},
            device_id_type=MESH,
        )

    def sends(way, hop):
        step = 1 - 2 * way
        block, peer = z - step * hop, z + step
        return (block >= 0) & (block < n) & (peer >= 0) & (peer < n)

    def arrives(way, hop):
        block = z - (1 - 2 * way) * (hop + 1)
        return (block >= 0) & (block < n)

    def start(kind):
        for way in range(2):
            @pl.when(sends(way, 0))
            def _():
                row_copy(kind, way, 0, sources[kind]).start()

    def take(hop):
        for kind in range(len(held)):
            for way in range(2):
                @pl.when(arrives(way, hop))
                def _():
                    row_copy(kind, way, hop).wait_recv()

                @pl.when(sends(way, hop + 1) & (hop + 1 < n - 1))
                def _():
                    row_copy(kind, way, hop + 1).start()

    def waits(way, block):
        peer, last = z - (1 - 2 * way), (n - 1) * (1 - way)
        return (peer >= 0) & (peer < n) & ((block != last) | (peer != n - 1 - last))

    def far_copy(p):
        mine, arrived = pieces[p]
        block, way = n - 1 - z, jnp.where(z == 0, 1, 0)
        return pltpu.make_async_remote_copy(
            src_ref=mine(block),
            dst_ref=arrived(way, block),
            send_sem=sum_send.at[block, p],
            recv_sem=sum_recv.at[way, block, p],
            device_id={LINE: block},
            device_id_type=MESH,
        )

    def sum_copy(way, block, p):
        mine, arrived = pieces[p]
        return pltpu.make_async_remote_copy(
            src_ref=mine(block),
            dst_ref=arrived(way, block),
            send_sem=sum_send.at[block, p],
            recv_sem=sum_recv.at[way, block, p],
            device_id={LINE: jnp.clip(z + 1 - 2 * way, 0, n - 1)},
            device_id_type=MESH,
        )

    def sent(block, p):
        way = jnp.where(block > z, 0, 1)
        far = ((z == 0) | (z == n - 1)) & (block == n - 1 - z)

        @pl.when(far)
        def _():
            far_copy(p).start()

        @pl.when((block != z) & jnp.logical_not(far) & jnp.logical_not(waits(way, block)))
        def _():
            sum_copy(way, block, p).start()

    def run():
        def both(hop):
            return (hop >= 0) & (z - 1 - hop >= 0) & (z + 1 + hop < n)

        def turn(k, carry):
            hop = lax.div(k + 1, 2) - 1
            block = z + (1 + hop) * (1 - 2 * lax.rem(k, 2))
            odd = lax.rem(k, 2) == 1

            @pl.when(odd & jnp.logical_not(both(hop - 1)))
            def _():
                take(hop)

            @pl.when(jnp.logical_not(odd) & both(hop) & (hop + 1 < n - 1))
            def _():
                take(hop + 1)

            @pl.when((block >= 0) & (block < n))
            def _():
                compute(block, sent)

            return carry

        def far_first(k, carry):
            block = z + (n - 1 - lax.div(k, 2)) * (1 - 2 * lax.rem(k, 2))

            @pl.when((block >= 0) & (block < n))
            def _():
                compute(block, sent)

            return carry

        lax.fori_loop(0, 2 * n - 1, turn if held else far_first, 0)

        first = jnp.where(2 * z < n, 0, 1)
        for way in (first, 1 - first):
            for k in range(1, n):
                block = z + (1 - 2 * way) * k

                @pl.when(waits(way, block) & (block >= 0) & (block < n))
                def _():
                    for p, (mine, arrived) in enumerate(pieces):
                        sum_copy(way, block, p).wait_recv()
                        own, other = mine(block), arrived(way, block)
                        own[...] = (
                            own[...].astype(jnp.float32) + other[...].astype(jnp.float32)
                        ).astype(jnp.bfloat16)
                        sum_copy(way, block, p).start()

    def collect(add):
        for way in range(2):
            for p, (_, arrived) in enumerate(pieces):
                sum_copy(way, z, p).wait_recv()
                add(p, arrived(way, z)[...].astype(jnp.float32))

    def finish():
        for kind in range(len(held)):
            for way in range(2):
                for hop in range(n - 1):
                    @pl.when(sends(way, hop))
                    def _():
                        row_copy(kind, way, hop).wait_send()
        for k in range(1, n):
            for p in range(len(pieces)):
                sum_copy(0, lax.rem(z + k, n), p).wait_send()

    return start, run, collect, finish


def row_pieces(sums, returned, parts):
    width = sums.shape[2] // parts

    def piece(p):
        at = pl.ds(p * width, width)
        return (
            lambda block: sums.at[block, :, at],
            lambda way, block: returned.at[way, block, :, at],
        )

    return [piece(p) for p in range(parts)]


def fetch_weights(layer, own, other, places, sem):
    count = places[0].shape[0]
    mine = lax.axis_index(CORE) == layer

    def copy(group, kind, e):
        return pltpu.make_async_copy(
            group[kind].at[e], places[kind].at[e], sem.at[kind * count + e]
        )

    for kind in range(len(places)):
        for e in range(count):
            @pl.when(mine)
            def _():
                copy(own, kind, e).start()

            @pl.when(jnp.logical_not(mine))
            def _():
                copy(other, kind, e).start()

    def wait():
        for kind in range(len(places)):
            for e in range(count):
                copy(own, kind, e).wait()

    return wait


def sigmoid_of(value):
    return 1.0 / (1.0 + jnp.exp(-value))


def column_of(block, column):
    here = lax.broadcasted_iota(jnp.int32, block.shape, 1) == column
    return jnp.sum(jnp.where(here, block, 0.0), axis=1, keepdims=True)


def experts_forward_kernel(
    layer, experts, x, mask, hidden, router, *refs
):
    own, other, refs = refs[:3], refs[3:6], refs[6:]
    own_dense, other_dense, refs = refs[:4], refs[4:8], refs[8:]
    out, rows, gates_all, gates, gate_keep, up_keep, gated, stats = refs[:8]
    placed, place_sem = refs[8:12], refs[-1]
    passing, refs = refs[-5:-1], refs[:8] + refs[12:-5]
    w_gate, w_up, w_down, sums, returned, mixed, total, stats_all = refs[8:16]
    weight_sem, *sems = refs[16:]
    n, held = rows.shape[0], w_gate.shape[0]
    z = lax.axis_index(LINE)

    def compute(block, sent):
        picked = rows[block]
        gate_block = gates_all[block].astype(jnp.float32)

        def one(e, carry):
            gate_pre = jnp.dot(picked, w_gate[e], preferred_element_type=jnp.float32)
            up_pre = jnp.dot(picked, w_up[e], preferred_element_type=jnp.float32)
            gate_keep[e, block] = gate_pre.astype(jnp.bfloat16)
            up_keep[e, block] = up_pre.astype(jnp.bfloat16)
            active = gate_pre * sigmoid_of(gate_pre) * up_pre
            share = (column_of(gate_block, z * held + e) * active).astype(jnp.bfloat16)
            inner = share.shape[1]
            gated[block, :, pl.ds(pl.multiple_of(e * inner, inner), inner)] = share
            mixed[e] = share
            return carry

        lax.fori_loop(0, held, one, 0)
        width = out.shape[1] // PARTS
        for part in range(PARTS):
            at = pl.ds(part * width, width)
            result = jnp.zeros((out.shape[0], width), jnp.float32)
            for e in range(held):
                result += jnp.dot(mixed[e], w_down[e, :, at], preferred_element_type=jnp.float32)

            @pl.when(block == z)
            def _():
                total[:, at] = hidden[:, at] + result

            @pl.when(block != z)
            def _():
                sums[block, :, at] = result.astype(jnp.bfloat16)

            sent(block, part)

    own_gates = gates_all.at[z]
    start, run, collect, finish = move_rows(
        (x, own_gates, stats_all.at[z]),
        (rows, gates_all, stats_all),
        row_pieces(sums, returned, PARTS),
        sems,
        compute,
        z,
        n,
        [],
    )
    start(0)
    wait_weights = fetch_weights(layer, own, other, (w_gate, w_up, w_down), weight_sem)
    here = lax.axis_index(CORE) == 1 - layer

    def place_copy(group, i):
        return pltpu.make_async_copy(group[i], passing[i], place_sem.at[0, i])

    def place_out(i):
        return pltpu.make_async_copy(passing[i], placed[i], place_sem.at[1, i])

    logits = jnp.dot(x[...], router[...], preferred_element_type=jnp.float32)
    chosen = mask[...] > 0
    highest = jnp.max(jnp.where(chosen, logits, MASKED), axis=1, keepdims=True)
    exponent = jnp.where(chosen, jnp.exp(logits - highest), 0.0)
    gates[...] = exponent / jnp.sum(exponent, axis=1, keepdims=True)
    own_gates[...] = gates[...].astype(jnp.bfloat16)
    start(1)
    real = lax.broadcasted_iota(jnp.int32, logits.shape, 1) < experts
    highest = jnp.max(jnp.where(real, logits, MASKED), axis=1, keepdims=True)
    exponent = jnp.where(real, jnp.exp(logits - highest), 0.0)
    chance = exponent / jnp.sum(exponent, axis=1, keepdims=True)
    line = lax.broadcasted_iota(jnp.int32, stats.shape, 0)
    stats_all[z] = jnp.where(
        line == 0,
        jnp.sum(chance, axis=0, keepdims=True),
        jnp.where(line == 1, jnp.sum(mask[...], axis=0, keepdims=True), 0.0),
    )
    start(2)
    rows[z] = x[...]
    wait_weights()
    for i in range(4):
        @pl.when(here)
        def _():
            place_copy(own_dense, i).start()

        @pl.when(jnp.logical_not(here))
        def _():
            place_copy(other_dense, i).start()

    run()
    for i in range(4):
        place_copy(own_dense, i).wait()
        place_out(i).start()
    stats[...] = jnp.sum(stats_all[...], axis=0)
    width = out.shape[1] // PARTS

    def add(p, value):
        total[:, p * width : (p + 1) * width] += value

    collect(add)
    out[...] = total[...].astype(jnp.bfloat16)
    finish()
    for i in range(4):
        place_out(i).wait()


def experts_backward_kernel(layer, grad, gates, gate_keep, up_keep, *refs):
    own, other, saved_rows, saved_gated, refs = refs[:3], refs[3:6], refs[6], refs[7], refs[8:]
    carried = layer == 0
    if carried:
        extra, refs = refs[0], refs[1:]
        extra_sum, refs = refs[6], refs[:6] + refs[7:]
        landed, extra_send, extra_recv = refs[-3:]
        refs = refs[:-3]
    out, out_gates, rows_both, gated_both, grad_both, pre_both = refs[:6]
    w_gate, w_up, w_down, sums, sum_gates, returned, returned_gates, away, dots = refs[6:15]
    weight_sem, core_send, core_recv, core_local, *sems = refs[15:]
    n, held = gates.shape[0], w_gate.shape[0]
    half, inner = held // 2, w_gate.shape[2]
    core = lax.axis_index(CORE)
    z = lax.axis_index(LINE)
    turned_dims = (((1,), (1,)), ((), ()))
    gathered = layer == 1
    rows = grad if gathered else grad_both.at[core]

    def to_core(number, source, target):
        return pltpu.make_async_remote_copy(
            src_ref=source,
            dst_ref=target,
            send_sem=core_send.at[number],
            recv_sem=core_recv.at[number],
            device_id={CORE: 1 - core},
            device_id_type=MESH,
        )

    def block_copies(block):
        away_copy = to_core(2 + n + block, away.at[block], pre_both.at[core, block])
        if gathered:
            return (away_copy,)
        return (to_core(2 + block, rows.at[block], rows.at[block]), away_copy)

    def columns(at):
        return pl.ds(pl.multiple_of(at * half * inner, half * inner), half * inner)

    def whole_copies():
        copies = (
            to_core(0, saved_rows, rows_both.at[core]),
            to_core(1, saved_gated.at[:, :, columns(1 - core)], gated_both.at[core]),
        )
        return copies + ((to_core(2, grad, grad_both.at[core]),) if gathered else ())

    def local_copies():
        copies = (
            pltpu.make_async_copy(saved_rows, rows_both.at[core], core_local.at[0]),
            pltpu.make_async_copy(
                saved_gated.at[:, :, columns(core)], gated_both.at[core], core_local.at[1]
            ),
        )
        if gathered:
            copies += (pltpu.make_async_copy(grad, grad_both.at[core], core_local.at[2]),)
        return copies

    me, count = lax.axis_index(GROUP), lax.axis_size(GROUP)
    peers = [lax.rem(me + k, count) for k in range(1, count)] if carried else []

    def extra_copy(k, peer, slot):
        return pltpu.make_async_remote_copy(
            src_ref=extra.at[:, peer],
            dst_ref=landed.at[slot],
            send_sem=extra_send.at[k],
            recv_sem=extra_recv.at[slot],
            device_id={GROUP: peer},
            device_id_type=MESH,
        )

    def compute(block, sent):
        picked = rows[block]
        gate_block = gates[block].astype(jnp.float32)
        dots[...] = jnp.zeros(dots.shape, jnp.float32)

        def one(e, place, j):
            raw = lax.dot_general(
                picked, w_down[e], turned_dims, preferred_element_type=jnp.float32
            )
            gate_pre = gate_keep[e, block].astype(jnp.float32)
            up_pre = up_keep[e, block].astype(jnp.float32)
            sigmoid = sigmoid_of(gate_pre)
            silu = gate_pre * sigmoid
            column = z * held + e
            dot = jnp.sum(raw * (silu * up_pre), axis=1, keepdims=True)
            here = lax.broadcasted_iota(jnp.int32, dots.shape, 1) == column
            dots[...] += jnp.where(here, dot, 0.0)
            active = column_of(gate_block, column) * raw
            place[:, pl.ds(pl.multiple_of(j * inner, inner), inner)] = (
                active * up_pre * sigmoid * (1.0 + gate_pre * (1.0 - sigmoid))
            ).astype(jnp.bfloat16)
            place[:, pl.ds(pl.multiple_of((half + j) * inner, inner), inner)] = (
                active * silu
            ).astype(jnp.bfloat16)

        def own_half(j, carry):
            one(core * half + j, pre_both.at[core, block], j)
            return carry

        def other_half(j, carry):
            one((1 - core) * half + j, away.at[block], j)
            return carry

        lax.fori_loop(0, half, other_half, 0)
        for copy in block_copies(block):
            copy.start()
        lax.fori_loop(0, half, own_half, 0)
        sum_gates[block] = dots[...].astype(jnp.bfloat16)

        @pl.when(block == z)
        def _():
            out_gates[...] = dots[...]

        sent(block, PARTS)
        width = out.shape[1] // PARTS
        for part in range(PARTS):
            at = pl.ds(part * width, width)
            result = jnp.zeros((out.shape[0], width), jnp.float32)
            for place, side in ((away.at[block], 1 - core), (pre_both.at[core, block], core)):
                for kind, right in enumerate((w_gate, w_up)):
                    for j in range(half):
                        left = place[:, pl.ds((kind * half + j) * inner, inner)]
                        result += lax.dot_general(
                            left,
                            right[side * half + j, at, :],
                            turned_dims,
                            preferred_element_type=jnp.float32,
                        )

            @pl.when(block == z)
            def _():
                out[:, at] = result

            @pl.when(block != z)
            def _():
                sums[block, :, at] = result.astype(jnp.bfloat16)

            sent(block, part)

    gate_piece = (lambda block: sum_gates.at[block], lambda way, block: returned_gates.at[way, block])
    start, run, collect, finish = move_rows(
        () if gathered else (grad,),
        () if gathered else (rows,),
        row_pieces(sums, returned, PARTS) + [gate_piece],
        sems,
        compute,
        z,
        n,
        [{CORE: 1 - core}] + [{GROUP: peer} for peer in peers],
    )
    if not gathered:
        start(0)
    for k, peer in enumerate(peers):
        extra_copy(k, peer, me).start()
    if carried:
        mine = pltpu.make_async_copy(extra.at[:, me], landed.at[me], extra_send.at[len(peers)])
        mine.start()
    wait_weights = fetch_weights(layer, own, other, (w_gate, w_up, w_down), weight_sem)
    for copy in whole_copies() + local_copies():
        copy.start()
    if not gathered:
        rows[z] = grad[...]
    wait_weights()
    run()
    width = out.shape[1] // PARTS

    def add(p, value):
        if p == PARTS:
            out_gates[...] += value
        else:
            out[:, p * width : (p + 1) * width] += value

    if carried:
        mine.wait()
        for k, peer in enumerate(peers):
            extra_copy(k, peer, peer).wait_recv()
        half, rows_each = extra_sum.shape[:2]
        step = 16 if rows_each % 16 == 0 else rows_each

        def add_up(i, carry):
            at = pl.ds(pl.multiple_of(i * step, step), step)
            for j in range(half):
                value = landed[0, j, at].astype(jnp.float32)
                for k in range(1, count):
                    value += landed[k, j, at].astype(jnp.float32)
                extra_sum[j, at] = value.astype(jnp.bfloat16)
            return carry

        lax.fori_loop(0, rows_each // step, add_up, 0)
    collect(add)
    finish()
    for k, peer in enumerate(peers):
        extra_copy(k, peer, me).wait_send()
    for copy in local_copies():
        copy.wait()
    for copy in whole_copies():
        copy.wait()
    for block in range(n):
        for copy in block_copies(block):
            copy.wait()


def exchange_scratch(n, kinds_out, kinds_back):
    return [
        pltpu.SemaphoreType.DMA((kinds_out, 2, n)),
        pltpu.SemaphoreType.DMA((kinds_out, 2, n)),
        pltpu.SemaphoreType.DMA((n, kinds_back)),
        pltpu.SemaphoreType.DMA((2, n, kinds_back)),
    ]


def expert_call(kernel, operands, own, other, extra, shapes, scratch, collective, loose=0):
    vmem, free = pl.BlockSpec(memory_space=pltpu.VMEM), pl.BlockSpec(memory_space=pl.ANY)
    weights = [pltpu.VMEM(array.shape, jnp.bfloat16) for array in own]
    return pl.pallas_call(
        kernel,
        out_shape=shapes,
        in_specs=[vmem] * len(operands) + [free] * (6 + len(extra)),
        out_specs=[vmem] * (len(shapes) - loose) + [free] * loose,
        scratch_shapes=weights + scratch,
        compiler_params=pltpu.CompilerParams(
            collective_id=collective, has_side_effects=True, vmem_limit_bytes=46 * 2**20
        ),
        cost_estimate=pl.CostEstimate(
            flops=5 * 10**10, bytes_accessed=10**8, transcendentals=0
        ),
    )(*operands, *own, *other, *extra)


def experts_forward(
    layer, normed_two, mask, hidden, router, own, other, own_dense, other_dense, experts
):
    n, held = lax.axis_size(LINE), own[0].shape[0]
    length, width = normed_two.shape
    inner = own[0].shape[2]
    low, full = jnp.bfloat16, jnp.float32
    kept = jax.ShapeDtypeStruct((held, n, length, inner), low)
    shapes = [
        jax.ShapeDtypeStruct((length, width), low),
        jax.ShapeDtypeStruct((n, length, width), low),
        jax.ShapeDtypeStruct((n, length, COLUMNS), low),
        jax.ShapeDtypeStruct((length, COLUMNS), full),
        kept,
        kept,
        jax.ShapeDtypeStruct((n, length, held * inner), low),
        jax.ShapeDtypeStruct((8, COLUMNS), full),
    ] + [jax.ShapeDtypeStruct(array.shape, low) for array in own_dense]
    scratch = [
        pltpu.VMEM((n, length, width), low),
        pltpu.VMEM((2, n, length, width), low),
        pltpu.VMEM((held, length, inner), low),
        pltpu.VMEM((length, width), full),
        pltpu.VMEM((n, 8, COLUMNS), full),
        pltpu.SemaphoreType.DMA((3 * held,)),
    ] + exchange_scratch(n, 3, PARTS)
    scratch += [pltpu.VMEM(array.shape, low) for array in own_dense]
    scratch.append(pltpu.SemaphoreType.DMA((2, 4)))
    kernel = functools.partial(experts_forward_kernel, layer, experts)
    return expert_call(
        kernel,
        (normed_two, mask, hidden, router),
        own,
        other,
        (*own_dense, *other_dense),
        shapes,
        scratch,
        1 + layer,
        4,
    )


def experts_backward(layer, grad_low, gates, gate_keep, up_keep, rows, gated, own, other, extra):
    held, n, length, inner = gate_keep.shape
    width = grad_low.shape[-1]
    low, full = jnp.bfloat16, jnp.float32
    shapes = [
        jax.ShapeDtypeStruct((length, width), full),
        jax.ShapeDtypeStruct((length, COLUMNS), full),
        jax.ShapeDtypeStruct((2, n, length, width), low),
        jax.ShapeDtypeStruct((2, n, length, held // 2 * inner), low),
        jax.ShapeDtypeStruct((2, n, length, width), low),
        jax.ShapeDtypeStruct((2, n, length, held * inner), low),
    ]
    scratch = [
        pltpu.VMEM((n, length, width), low),
        pltpu.VMEM((n, length, COLUMNS), low),
        pltpu.VMEM((2, n, length, width), low),
        pltpu.VMEM((2, n, length, COLUMNS), low),
        pltpu.VMEM((n, length, held * inner), low),
        pltpu.VMEM((length, COLUMNS), full),
        pltpu.SemaphoreType.DMA((3 * held,)),
        pltpu.SemaphoreType.DMA((2 + 2 * n,)),
        pltpu.SemaphoreType.DMA((2 + 2 * n,)),
        pltpu.SemaphoreType.DMA((3,)),
    ] + exchange_scratch(n, 1, PARTS + 1)
    if layer == 0:
        half, count, *block = extra.shape
        shapes.append(jax.ShapeDtypeStruct((half, *block), low))
        scratch += [
            pltpu.VMEM((count, half, *block), low),
            pltpu.SemaphoreType.DMA((count,)),
            pltpu.SemaphoreType.DMA((count,)),
        ]
    kernel = functools.partial(experts_backward_kernel, layer)
    return expert_call(
        kernel,
        (grad_low, gates, gate_keep, up_keep),
        own,
        other,
        (rows, gated) if extra is None else (rows, gated, extra),
        shapes,
        scratch,
        3 + layer,
    )


def attention_backward(grad_hidden, inputs, state, weights):
    gain_attn, w_query, w_key, w_value, w_out, gain_moe = weights[:6]
    (inverse_one, normed_one, queries, key_rows, values, weight, attended, hidden, inverse_two, normed_two) = state
    length = inputs.shape[0]
    grad_branch = grad_hidden.astype(jnp.bfloat16)
    grad_attended = jnp.einsum("td,cd->tc", grad_branch, w_out, preferred_element_type=jnp.float32)
    grad_attended = grad_attended.astype(jnp.bfloat16).reshape(length, KVH, H // KVH, HD)
    grad_weight = jnp.einsum(
        "qkgd,skd->kgqs", grad_attended, values, preferred_element_type=jnp.float32
    )
    grad_values = jnp.einsum(
        "kgqs,qkgd->skd",
        weight.astype(jnp.bfloat16),
        grad_attended,
        preferred_element_type=jnp.float32,
    )
    grad_values = grad_values.astype(jnp.bfloat16).reshape(length, KVH * HD)
    grad_scores = (
        weight * (grad_weight - jnp.sum(weight * grad_weight, axis=-1, keepdims=True))
    ).astype(jnp.bfloat16)
    score_scale = HD ** (-0.5)
    grouped = queries.reshape(length, KVH, H // KVH, HD)
    grad_queries = jnp.einsum(
        "kgqs,skd->qkgd", grad_scores, key_rows, preferred_element_type=jnp.float32
    )
    grad_queries = grad_queries.reshape(length, H, HD) * score_scale
    grad_keys = (
        jnp.einsum("kgqs,qkgd->skd", grad_scores, grouped, preferred_element_type=jnp.float32)
        * score_scale
    )
    cosine_table, sine_table = rotary_tables(length)
    grad_query_pre = (
        unrotate(grad_queries, cosine_table, sine_table)
        .reshape(length, H * HD)
        .astype(jnp.bfloat16)
    )
    grad_key_pre = (
        unrotate(grad_keys, cosine_table, sine_table).reshape(length, KVH * HD).astype(jnp.bfloat16)
    )
    grad_normed_one = (
        jnp.einsum("tq,cq->tc", grad_query_pre, w_query, preferred_element_type=jnp.float32)
        + jnp.einsum("tq,cq->tc", grad_key_pre, w_key, preferred_element_type=jnp.float32)
        + jnp.einsum("tq,cq->tc", grad_values, w_value, preferred_element_type=jnp.float32)
    )
    grad_norm_one, grad_gain_attn = norm_back(grad_normed_one, inputs, inverse_one, gain_attn)
    grad_inputs = grad_hidden + grad_norm_one
    grad_qkv = jnp.concatenate([grad_query_pre, grad_key_pre, grad_values], axis=1)
    return grad_inputs, grad_gain_attn, grad_qkv, grad_branch


def turned(left, right):
    return jnp.einsum("tc,tq->cq", left, right, preferred_element_type=jnp.float32)


def body(tokens, cotangent, segments, routes, *weight_arrays):
    core = lax.axis_index(CORE)
    first = core == 0
    experts = weight_arrays[6].shape[2]
    w_gate = weight_arrays[7]
    held = w_gate.shape[1]
    own = [array[0] for array in weight_arrays]
    other = [swapped(array) for array in own]
    weights = [
        [jnp.where(first, a, b) for a, b in zip(own[:7], other[:7])],
        [jnp.where(first, b, a) for a, b in zip(own[:7], other[:7])],
    ]
    inputs_low = lax.dynamic_slice_in_dim(tokens, core * SEQ, SEQ, 0)
    grad_low = lax.dynamic_slice_in_dim(cotangent, core * SEQ, SEQ, 0)
    cotangent_all = lax.all_gather(grad_low, LINE, axis=0)
    segment_row = lax.dynamic_index_in_dim(segments, core, 0, keepdims=False)
    mine = lax.dynamic_slice_in_dim(routes[0], core * SEQ, SEQ, 0)
    got = swapped(lax.dynamic_slice_in_dim(routes[0], (1 - core) * SEQ, SEQ, 0))
    routes_here = jnp.stack([jnp.where(first, mine, got), jnp.where(first, got, mine)])
    masks = multi_hot(routes_here, COLUMNS)
    own_experts, other_experts = own[7:], other[7:]

    saved, outs, stats = [], [], []
    for s in range(2):
        inputs = inputs_low.astype(jnp.float32)
        state = attention_forward(inputs, weights[s], segment_row)
        hidden, normed_two = state[7], state[9]
        both_cores = [jnp.concatenate([a, swapped(a)]) for a in (state[1], state[6])]
        router = jnp.pad(weights[s][6], ((0, 0), (0, COLUMNS - experts)))
        inputs_low, *expert_state, stat, query, key, value, out = experts_forward(
            s,
            normed_two,
            masks[s],
            hidden,
            router,
            own_experts,
            other_experts,
            own[1:5],
            other[1:5],
            experts,
        )
        weights[1 - s][1:5] = [query, key, value, out]
        outs.append(inputs_low)
        stats.append(stat)
        saved.append((inputs, state, expert_state, both_cores))

    dp, deep = lax.axis_size(GROUP), lax.axis_size(LINE)
    grads = [None, None]
    input_grads = [None, None]
    for s in (1, 0):
        inputs, state, expert_state, both_cores = saved[s]
        (inverse_one, normed_one, _, _, _, _, attended, hidden, inverse_two, normed_two) = state
        rows_all, gates_all, gates, gate_keep, up_keep, gated = expert_state
        gain_moe, w_router = weights[s][5], weights[s][6]
        grad_sum, grad_gates, rows_both, gated_both, grad_both, pre_both, *sums = experts_backward(
            s,
            cotangent_all if s == 1 else grad_low,
            gates_all,
            gate_keep,
            up_keep,
            rows_all,
            gated,
            own_experts,
            other_experts,
            None if s == 1 else grads[1][1].reshape(held // 2, dp, -1, D),
        )
        if s == 0:
            (second_down,) = sums
        inner = w_gate.shape[3]
        grad_gate_up = turned(
            rows_both.reshape(-1, D), pre_both.reshape(-1, held * inner)
        ).astype(jnp.bfloat16)
        if s == 1:
            grad_sum, grad_gate_up = lax.optimization_barrier((grad_sum, grad_gate_up))
            second_pre = lax.psum_scatter(grad_gate_up, GROUP, scatter_dimension=0, tiled=True)
        else:
            grad_sum, second_pre = lax.optimization_barrier((grad_sum, second_pre))
        gates, grad_gates = gates[:, :experts], grad_gates[:, :experts]
        grad_chosen = gates * (grad_gates - jnp.sum(gates * grad_gates, axis=-1, keepdims=True))
        grad_logits = grad_chosen.astype(jnp.bfloat16)
        grad_normed_two = grad_sum + jnp.einsum(
            "te,de->td", grad_logits, w_router, preferred_element_type=jnp.float32
        )
        grad_norm_two, grad_gain_moe = norm_back(grad_normed_two, hidden, inverse_two, gain_moe)
        grad_hidden = grad_low.astype(jnp.float32) + grad_norm_two
        grad_inputs, grad_gain_attn, grad_qkv, grad_branch = attention_backward(
            grad_hidden, inputs, state, weights[s]
        )
        if s == 1:
            grad_inputs, gated_both = lax.optimization_barrier((grad_inputs, gated_both))
        grad_down = turned(
            gated_both.reshape(-1, held // 2 * inner), grad_both.reshape(-1, D)
        ).astype(jnp.bfloat16)

        def halves(array):
            width = array.shape[1] // 2
            return (
                lax.dynamic_slice_in_dim(array, core * width, width, 1),
                lax.dynamic_slice_in_dim(array, (1 - core) * width, width, 1),
            )
        qkv_keep, qkv_send = halves(grad_qkv)
        branch_keep, branch_send = halves(grad_branch)
        grad_w_qkv = turned(
            both_cores[0], jnp.concatenate([qkv_keep, swapped(qkv_send)])
        ).astype(jnp.bfloat16)
        grad_w_out = turned(
            both_cores[1], jnp.concatenate([branch_keep, swapped(branch_send)])
        ).astype(jnp.bfloat16)
        grad_w_router = turned(normed_two, grad_logits)
        small = jnp.concatenate(
            [grad_gain_attn[:, None], grad_gain_moe[:, None], grad_w_router], axis=1
        ).astype(jnp.bfloat16)
        small = jnp.pad(small, ((0, 0), (0, COLUMNS - small.shape[1])))
        if s == 1:
            grad_inputs, grad_down, grad_w_qkv, grad_w_out = lax.optimization_barrier(
                (grad_inputs, grad_down, grad_w_qkv, grad_w_out)
            )
            dense = jnp.concatenate([grad_w_qkv, grad_w_out], axis=1)
            second_dense = lax.psum_scatter(dense, GROUP, scatter_dimension=0, tiled=True)
        grads[s] = (grad_gate_up, grad_down, grad_w_qkv, grad_w_out, small)
        input_grads[s] = grad_inputs
        grad_low = grad_inputs.astype(jnp.bfloat16)

    dp, deep = lax.axis_size(GROUP), lax.axis_size(LINE)
    half, inner = held // 2, w_gate.shape[3]
    grad_gate_up, grad_down, grad_w_qkv, grad_w_out, small = grads[0]
    arrays = [
        grad_gate_up.reshape(dp, D // dp, held * inner),
        grad_down.reshape(half, dp, inner // dp, D),
    ]
    lanes = dense_lanes(2, grad_w_qkv.shape[1])
    for array in (grad_w_qkv, grad_w_out, small):
        arrays.append(array.reshape(dp, deep, array.shape[0] // (dp * deep), array.shape[1]))
    width = grad_w_qkv.shape[1]
    whole = second_dense.shape[1]
    for columns, kind in (((0, width), QKV), ((width, whole - width), OUT)):
        start, size = columns
        target = (kind, slice(None), pl.ds(start - (start // width) * width, size))
        lanes.append((len(arrays), (False, columns), [(LINE, bits_of(LINE))], 1, target))
    arrays.append(second_dense.reshape(deep, second_dense.shape[0] // deep, whole))
    lanes.append(small_lane(len(arrays), 1))
    lanes += expert_lanes(0, inner) + down_lanes(1, 0)
    small = grads[1][4]
    arrays.append(small.reshape(dp, deep, small.shape[0] // (dp * deep), small.shape[1]))
    out_keep = jnp.where(first, outs[0], outs[1])
    out_got = swapped(jnp.where(first, outs[1], outs[0]))
    layer_out = jnp.where(
        first, jnp.concatenate([out_keep, out_got]), jnp.concatenate([out_got, out_keep])
    )
    low_one = input_grads[1].astype(jnp.bfloat16).astype(jnp.float32)
    grad_keep = jnp.where(first, input_grads[0], low_one)
    grad_got = swapped(jnp.where(first, low_one, input_grads[0]))
    input_grad = jnp.where(
        first, jnp.concatenate([grad_keep, grad_got]), jnp.concatenate([grad_got, grad_keep])
    )
    stats = jnp.concatenate(stats, axis=0)
    stats, layer_out, input_grad = lax.optimization_barrier((stats, layer_out, input_grad))
    *grads, qkv, out, small, stats = sum_scatter(
        arrays, lanes, second_pre, second_down, stats, inner, 0
    )
    full = jnp.float32
    w_gate_grad, w_up_grad, w_down_grad = (
        grad.reshape(held, *grad.shape[2:]).astype(full) for grad in grads
    )
    qkv = jnp.concatenate([qkv[0], qkv[1]], axis=1).astype(full)
    grad_w_out = jnp.concatenate([out[0], out[1]], axis=1).astype(full)
    small = small[0].astype(full) + small[1].astype(full)
    heads, kv = H * HD, KVH * HD
    stats = lax.dynamic_index_in_dim(stats.reshape(2, 8, COLUMNS), core, 0)
    token_total = SEQ * lax.axis_size((CORE, GROUP, LINE))
    counts, chances = stats[:, 1, :experts], stats[:, 0, :experts]
    balance = experts * (counts / (token_total * TOPK) * chances / token_total)
    results = (
        layer_out,
        input_grad,
        small[:, 0],
        qkv[:, :heads],
        qkv[:, heads : heads + kv],
        qkv[:, heads + kv :],
        grad_w_out,
        small[:, 1],
        small[:, 2 : 2 + experts],
        w_gate_grad,
        w_up_grad,
        w_down_grad,
    )
    return tuple(result[None] for result in results) + (balance,)


def solution(mesh):
    return jax.shard_map(
        body,
        mesh=mesh,
        in_specs=(
            P((GROUP, LINE), None),
            P((GROUP, LINE), None),
            P((GROUP, LINE), None),
            P(CORE, (GROUP, LINE), None),
            P(CORE, None),
            P(CORE, None, None),
            P(CORE, None, None),
            P(CORE, None, None),
            P(CORE, None, None),
            P(CORE, None),
            P(CORE, None, None),
            P(CORE, LINE, None, None),
            P(CORE, LINE, None, None),
            P(CORE, LINE, None, None),
        ),
        out_specs=(
            P(CORE, (GROUP, LINE), None),
            P(CORE, (GROUP, LINE), None),
            P(CORE, (GROUP, LINE)),
            P(CORE, (GROUP, LINE), None),
            P(CORE, (GROUP, LINE), None),
            P(CORE, (GROUP, LINE), None),
            P(CORE, (GROUP, LINE), None),
            P(CORE, (GROUP, LINE)),
            P(CORE, (GROUP, LINE), None),
            P(CORE, LINE, GROUP, None),
            P(CORE, LINE, GROUP, None),
            P(CORE, LINE, GROUP, None),
            P(CORE, None),
        ),
        check_vma=False,
    )
```

```python
import functools
import itertools
from types import SimpleNamespace

import jax
import jax.numpy as jnp
from jax import lax
from jax.experimental import pallas as pl
from jax.experimental.pallas import tpu as pltpu
from jax.sharding import PartitionSpec as P

D = 1536
H = 24
KVH = 8
HD = 64
TOPK = 8
SEQ = 96


EPSILON = 1e-05
THETA = 10000.0
MASKED = -1e30
COLUMNS = 128
GATE, UP, DOWN, QKV, OUT, SMALL = range(6)
CORE, GROUP, LINE = "section", "dp", "expert"
INNER = "inner"


def matmul(left_side, right_side):
    return jnp.dot(left_side, right_side, preferred_element_type=jnp.float32)


def rotary_tables(length):
    half_width = HD // 2
    position = jnp.arange(length, dtype=jnp.float32)[:, None]
    freq_rate = THETA ** (-jnp.arange(half_width, dtype=jnp.float32) / half_width)
    angles = position * freq_rate[None, :]
    return (jnp.cos(angles)[:, None, :], jnp.sin(angles)[:, None, :])


def rotate(tensor, cosine_table, sine_table):
    half_width = HD // 2
    first_half = tensor[..., :half_width]
    second_half = tensor[..., half_width:]
    return jnp.concatenate(
        [
            first_half * cosine_table - second_half * sine_table,
            second_half * cosine_table + first_half * sine_table,
        ],
        axis=-1,
    )


def unrotate(gradient, cosine_table, sine_table):
    half_width = HD // 2
    first_half = gradient[..., :half_width]
    second_half = gradient[..., half_width:]
    return jnp.concatenate(
        [
            first_half * cosine_table + second_half * sine_table,
            second_half * cosine_table - first_half * sine_table,
        ],
        axis=-1,
    )


def norm_back(grad_normed, tensor, inverse, gain_vector):
    scaled = grad_normed * gain_vector
    grad_gain = jnp.sum(grad_normed * tensor * inverse, axis=0)
    grad_tensor = inverse * scaled - tensor * inverse**3 * jnp.mean(
        scaled * tensor, axis=-1, keepdims=True
    )
    return (grad_tensor, grad_gain)


def attention_scores(queries, key_rows, segment_row):
    length = queries.shape[0]
    grouped = queries.reshape(length, KVH, H // KVH, HD)
    scores = jnp.einsum(
        "qkgd,skd->kgqs", grouped, key_rows, preferred_element_type=jnp.float32
    ) * HD ** (-0.5)
    position = jnp.arange(length)
    allowed = (position[None, :] <= position[:, None]) & (
        segment_row[:, None] == segment_row[None, :]
    )
    return jnp.where(allowed[None, None], scores, MASKED)


def multi_hot(route_rows, experts):
    columns = jnp.arange(experts, dtype=jnp.int32)
    return jnp.sum(
        (route_rows[..., None] == columns).astype(jnp.float32), axis=-2
    )


def swapped(array):
    return lax.ppermute(array, CORE, [(0, 1), (1, 0)])


def add_slab(total, arrived):
    *lead, rows, _ = total.shape
    step = 16 if rows % 16 == 0 else rows
    for where in itertools.product(*(range(n) for n in lead)):

        def add(i, carry):
            at = (*where, pl.ds(pl.multiple_of(i * step, step), step), slice(None))
            both = total[at].astype(jnp.float32) + arrived[at].astype(jnp.float32)
            total[at] = both.astype(jnp.bfloat16)
            return carry

        lax.fori_loop(0, rows // step, add, 0)


def sum_scatter_kernel(plan, *refs):
    lanes, ins, copies = plan
    sources = refs[:ins]
    second_pre, second_down, stats_in = refs[ins : ins + 3]
    stage, stats = refs[ins + 3 : ins + 9], refs[ins + 9]
    scratch = list(refs[ins + 10 :])
    send_sem, recv_sem, local_sem, stats_got, stats_send, stats_recv, core_send, core_recv = (
        scratch[-8:]
    )
    core = lax.axis_index(CORE)
    partners = []
    for lane in lanes:
        for axis, bits in lane.phases:
            partners += [(axis, bit) for bit in bits if (axis, bit) not in partners]
    partners.append((CORE, 0))
    index = {axis: lax.axis_index(axis) for axis, _ in partners}
    mine = {(axis, bit): (index[axis] >> bit) & 1 for axis, bit in partners}
    far = {key: index[key[0]] + (1 - 2 * mine[key]) * (1 << key[1]) for key in partners}
    barrier = pltpu.get_barrier_semaphore()
    peers = [{axis: far[axis, bit]} for axis, bit in partners if axis != GROUP]
    groups = lax.axis_size(GROUP)
    peers += [{GROUP: lax.rem(lax.axis_index(GROUP) + k, groups)} for k in range(1, groups)]
    for peer in peers:
        pl.semaphore_signal(
            barrier, inc=1, device_id=peer, device_id_type=pl.DeviceIdType.MESH
        )
    pl.semaphore_wait(barrier, len(peers))

    counter = itertools.count()

    def send(source, target, key):
        number = next(counter)
        copy = pltpu.make_async_remote_copy(
            src_ref=source,
            dst_ref=target,
            send_sem=send_sem.at[number],
            recv_sem=recv_sem.at[number],
            device_id={key[0]: far[key]},
            device_id_type=pl.DeviceIdType.MESH,
        )
        copy.start()
        return copy

    def place(axis, values):
        total = 0
        for bit, value in values.items():
            total = total + value * (1 << bit)
        return total

    def sum_stats():
        count = lax.axis_size(GROUP)
        me = lax.axis_index(GROUP)

        def copy(at, source, slot, target):
            return pltpu.make_async_remote_copy(
                src_ref=source,
                dst_ref=stats_got.at[slot],
                send_sem=stats_send.at[at],
                recv_sem=stats_recv.at[slot],
                device_id=target,
                device_id_type=pl.DeviceIdType.MESH,
            )

        for k in range(1, count):
            copy(k, stats_in, me, {GROUP: lax.rem(me + k, count)}).start()
        yield
        stats[...] = stats_in[...]
        for k in range(1, count):
            peer = lax.rem(me + k, count)
            copy(k, stats_in, peer, {GROUP: peer}).wait_recv()
            stats[...] += stats_got[peer]
        both = copy(0, stats, count, {CORE: far[CORE, 0]})
        both.start()
        yield
        both.wait()
        stats[...] += stats_got[count]
        for k in range(1, count):
            copy(k, stats_in, me, {GROUP: lax.rem(me + k, count)}).wait_send()

    summing = sum_stats()
    next(summing)

    def to_stage(number, source, kind, *at):
        spot = stage[kind].at[(core, *at)]
        return spot, pltpu.make_async_remote_copy(
            src_ref=source,
            dst_ref=spot,
            send_sem=core_send.at[number],
            recv_sem=core_recv.at[number],
            device_id={CORE: 1 - core},
            device_id_type=pl.DeviceIdType.MESH,
        )

    inner = stage[GATE].shape[3]
    wholes = []
    half = stage[GATE].shape[1]
    for number in range(3 * half):
        kind, j = divmod(number, half)
        if kind == DOWN:
            source = second_down.at[j]
        else:
            source = second_pre.at[:, pl.ds(number * inner, inner)]
        spot, copy = to_stage(len(lanes) + number, source, kind, j)
        wholes.append((copy, pltpu.make_async_copy(source, spot, core_send.at[len(lanes) + number])))
    for copy, here in wholes:
        @pl.when(core == 1)
        def _(here=here):
            here.start()

        @pl.when(core == 0)
        def _(copy=copy):
            copy.start()

    moved = []
    started = []
    states = []
    for number, lane in enumerate(lanes):
        count = len(lane.buffers)
        buffers, scratch = scratch[:count], scratch[count:]
        source = sources[lane.source]
        prefix = lane.prefix
        if isinstance(prefix, int):
            source = source.at[prefix]

        def part(at, source=source, prefix=prefix):
            if isinstance(prefix, int):
                return source.at[at]
            inner, columns = prefix
            where = (slice(None), at) if inner else (at,)
            if columns is not None:
                where += (slice(None),) * (len(source.shape) - len(where) - 1) + (pl.ds(*columns),)
            return source.at[where]

        axis, bits = lane.phases[0]
        total, arrived = buffers[0], buffers[1:]
        rest = [bit for bit in bits[1:]]
        pending = []
        for choice in itertools.product((0, 1), repeat=len(rest)):
            values = dict(zip(rest, choice))
            slot = sum(value << i for i, value in enumerate(choice))
            far_at = place(axis, {**values, bits[0]: 1 - mine[axis, bits[0]]})
            here_at = place(axis, {**values, bits[0]: mine[axis, bits[0]]})
            copy = send(part(far_at), arrived[0].at[slot], (axis, bits[0]))
            pending.append((copy, slot))
            started.append(copy)
            states.append((number, part(here_at), slot, total))
        lane_state = SimpleNamespace(total=total, arrived=arrived, pending=pending)
        lane.state = lane_state
    locals_ = {}
    for at, (number, here, slot, total) in enumerate(states):
        copy = pltpu.make_async_copy(here, total.at[slot], local_sem.at[at])
        copy.start()
        locals_[number, slot] = copy
    short = [item for item in enumerate(lanes) if len(item[1].phases) == 1 and item[1].rows]
    long = [item for item in enumerate(lanes) if item not in short]
    turns = [(1, long), (1, short)]
    count = max(sum(len(bits) for _, bits in lane.phases) for lane in lanes)
    for step in range(2, count + 1):
        turns += [(2 * step - 2, long), (2 * step - 1, long), (step, short)]
    for at, (step, group) in enumerate(turns):
        if at == 2:
            next(summing)
        for number, lane in group:
            state = lane.state
            sizes = [len(bits) for _, bits in lane.phases]
            if step > sum(sizes):
                continue
            if step <= sizes[0]:
                axis, bits = lane.phases[0]
                resolved, rest = bits[:step], bits[step:]

                def slot_of(values):
                    found = 0
                    for i, bit in enumerate(bits[1:]):
                        found = found + values.get(bit, mine[axis, bit]) * (1 << i)
                    return found

                for copy, slot in state.pending:
                    copy.wait_recv()
                    if step == 1:
                        locals_[number, slot].wait()
                state.pending_next = []
                for choice in itertools.product((0, 1), repeat=len(rest)):
                    values = dict(zip(rest, choice))
                    got = sum(value << i for i, value in enumerate(choice))
                    add_slab(
                        state.total.at[slot_of(values)], state.arrived[step - 1].at[got]
                    )
                if rest:
                    following = rest[1:]
                    for choice in itertools.product((0, 1), repeat=len(following)):
                        values = dict(zip(following, choice))
                        got = sum(value << i for i, value in enumerate(choice))
                        values[rest[0]] = 1 - mine[axis, rest[0]]
                        copy = send(
                            state.total.at[slot_of(values)],
                            state.arrived[step].at[got],
                            (axis, rest[0]),
                        )
                        state.pending_next.append((copy, got))
                        started.append(copy)
                final = state.total.at[slot_of({})] if not rest else None
            else:
                axis, bits = lane.phases[1]
                done = step - sizes[0]
                rest = bits[done:]
                final = state.final
                for copy, _ in state.pending:
                    copy.wait_recv()
                state.pending_next = []
                for choice in itertools.product((0, 1), repeat=len(rest)):
                    values = dict(zip(rest, choice))
                    got = sum(value << i for i, value in enumerate(choice))
                    at = place(axis, {bit: values.get(bit, mine[axis, bit]) for bit in bits})
                    add_slab(final.at[at], state.arrived[step - 1].at[got])
                if not rest:
                    at = place(axis, {bit: mine[axis, bit] for bit in bits})
                    final = final.at[at]
            if final is not None and step >= sizes[0]:
                state.final = final
                if step == sum(sizes):
                    spot, copy = to_stage(number, final, *lane.target)
                    moved.append((lane.layer, copy))

                    @pl.when(core == lane.layer)
                    def _(spot=spot, final=final):
                        spot[...] = final[...]

                    @pl.when(core != lane.layer)
                    def _(copy=copy):
                        copy.start()
                elif step < sum(sizes):
                    axis, bits = lane.phases[1]
                    done = step - sizes[0]
                    bit, following = bits[done], bits[done + 1 :]
                    for choice in itertools.product((0, 1), repeat=len(following)):
                        values = dict(zip(following, choice))
                        got = sum(value << i for i, value in enumerate(choice))
                        at = place(
                            axis,
                            {
                                b: values.get(b, 1 - mine[axis, b] if b == bit else mine[axis, b])
                                for b in bits
                            },
                        )
                        copy = send(final.at[at], state.arrived[step].at[got], (axis, bit))
                        state.pending_next.append((copy, got))
                        started.append(copy)
            state.pending = state.pending_next
    for _ in summing:
        pass

    for copy, here in wholes:
        @pl.when(core == 1)
        def _(copy=copy, here=here):
            copy.wait_recv()
            here.wait()

        @pl.when(core == 0)
        def _(copy=copy):
            copy.wait_send()

    for layer, copy in moved:
        @pl.when(core == layer)
        def _(copy=copy):
            copy.wait_recv()

        @pl.when(core != layer)
        def _(copy=copy):
            copy.wait_send()

    for copy in started:
        copy.wait_send()


def sum_scatter(arrays, lanes, second_pre, second_down, stats, inner, collective):
    plans, scratch, shapes, copies, locals_ = [], [], [], 0, 0
    sizes = {}
    for source, prefix, phases, layer, target in lanes:
        shape = arrays[source].shape
        if isinstance(prefix, int):
            shape = shape[1:]
        else:
            if prefix[0]:
                shape = (shape[1], shape[0], *shape[2:])
            if prefix[1] is not None:
                shape = (*shape[:-1], prefix[1][1])
        buffers = [(shape[0] // 2, *shape[1:])]
        for step in range(1, len(phases[0][1]) + 1):
            buffers.append((shape[0] >> step, *shape[1:]))
            copies += shape[0] >> step
        locals_ += shape[0] // 2
        if len(phases) > 1:
            for step in range(1, len(phases[1][1]) + 1):
                buffers.append((shape[1] >> step, *shape[2:]))
                copies += shape[1] >> step
        plans.append(
            SimpleNamespace(
                source=source,
                prefix=prefix,
                phases=phases,
                buffers=buffers,
                rows=phases[0][0] == GROUP,
                layer=layer,
                target=target,
            )
        )
        width = sizes.get(target[0], (0, 0))[1] if len(target) > 2 else 0
        if layer == 0:
            sizes[target[0]] = (shape[-2], width + shape[-1])
        scratch += [pltpu.VMEM(buffer, jnp.bfloat16) for buffer in buffers]
    half = second_pre.shape[1] // (2 * inner)
    experts_shape = (2, half, second_pre.shape[0], inner)
    shapes = [
        jax.ShapeDtypeStruct(shape, jnp.bfloat16)
        for shape in (
            experts_shape,
            experts_shape,
            (2, half, *sizes[DOWN]),
            (2, *sizes[QKV]),
            (2, *sizes[OUT]),
            (2, *sizes[SMALL]),
        )
    ] + [jax.ShapeDtypeStruct(stats.shape, jnp.float32)]
    scratch += [
        pltpu.SemaphoreType.DMA((copies,)),
        pltpu.SemaphoreType.DMA((copies,)),
        pltpu.SemaphoreType.DMA((locals_,)),
    ]
    hops = lax.axis_size(GROUP) + 1
    scratch += [
        pltpu.VMEM((hops, *stats.shape), jnp.float32),
        pltpu.SemaphoreType.DMA((hops,)),
        pltpu.SemaphoreType.DMA((hops,)),
        pltpu.SemaphoreType.DMA((len(lanes) + 3 * half,)),
        pltpu.SemaphoreType.DMA((len(lanes) + 3 * half,)),
    ]
    return pl.pallas_call(
        functools.partial(sum_scatter_kernel, (plans, len(arrays), copies)),
        out_shape=shapes,
        in_specs=[pl.BlockSpec(memory_space=pl.ANY)] * (len(arrays) + 2)
        + [pl.BlockSpec(memory_space=pltpu.VMEM)],
        out_specs=[pl.BlockSpec(memory_space=pltpu.VMEM)] * len(shapes),
        scratch_shapes=scratch,
        compiler_params=pltpu.CompilerParams(
            collective_id=collective, has_side_effects=True, vmem_limit_bytes=60 * 2**20
        ),
    )(*arrays, second_pre, second_down, stats)


def bits_of(axis):
    return list(range(lax.axis_size(axis).bit_length() - 1))


def expert_lanes(first, inner):
    up, down = [(GROUP, bits_of(GROUP))], [(GROUP, bits_of(GROUP)[::-1])]
    return [
        (first, (False, ((2 * kind + j) * inner, inner)), (up, down)[kind], 0, (kind, j))
        for j in range(2)
        for kind in (GATE, UP)
    ]


def down_lanes(first, layer):
    up, down = [(GROUP, bits_of(GROUP))], [(GROUP, bits_of(GROUP)[::-1])]
    return [(first, 0, up, layer, (DOWN, 0)), (first, 1, down, layer, (DOWN, 1))]


def dense_lanes(first, width):
    up, down, deep = bits_of(GROUP), bits_of(GROUP)[::-1], bits_of(LINE)
    near = width // 4 // COLUMNS * COLUMNS
    away = width - near
    return [
        (
            first,
            (True, (0, away)),
            [(LINE, deep), (GROUP, up)],
            0,
            (QKV, slice(None), pl.ds(0, away)),
        ),
        (
            first,
            (False, (away, near)),
            [(GROUP, up), (LINE, deep)],
            0,
            (QKV, slice(None), pl.ds(away, near)),
        ),
        (first + 1, (False, None), [(GROUP, down), (LINE, deep)], 0, (OUT,)),
        small_lane(first + 2, 0),
    ]


def small_lane(first, layer):
    phases = [(GROUP, bits_of(GROUP)), (LINE, bits_of(LINE))]
    return (first, (False, None), phases, layer, (SMALL,))


def attention_forward(inputs, weights, segment_row):
    gain_attn, w_query, w_key, w_value, w_out, gain_moe = weights[:6]
    length = inputs.shape[0]
    cosine_table, sine_table = rotary_tables(length)
    inverse_one = lax.rsqrt(jnp.mean(inputs * inputs, axis=-1, keepdims=True) + EPSILON)
    normed_one = (inputs * inverse_one * gain_attn).astype(jnp.bfloat16)
    queries = rotate(
        matmul(normed_one, w_query).reshape(length, H, HD), cosine_table, sine_table
    ).astype(jnp.bfloat16)
    key_rows = rotate(
        matmul(normed_one, w_key).reshape(length, KVH, HD), cosine_table, sine_table
    ).astype(jnp.bfloat16)
    values = matmul(normed_one, w_value).astype(jnp.bfloat16).reshape(length, KVH, HD)
    scores = attention_scores(queries, key_rows, segment_row)
    highest = jnp.max(scores, axis=-1, keepdims=True)
    exponent = jnp.exp(scores - highest)
    denominator = jnp.sum(exponent, axis=-1, keepdims=True)
    weight = exponent / denominator
    attended = jnp.einsum(
        "kgqs,skd->qkgd", weight.astype(jnp.bfloat16), values, preferred_element_type=jnp.float32
    )
    attended = attended.reshape(length, H * HD).astype(jnp.bfloat16)
    hidden = inputs + matmul(attended, w_out)
    inverse_two = lax.rsqrt(jnp.mean(hidden * hidden, axis=-1, keepdims=True) + EPSILON)
    normed_two = (hidden * inverse_two * gain_moe).astype(jnp.bfloat16)
    state = (inverse_one, normed_one, queries, key_rows, values, weight, attended, hidden, inverse_two, normed_two)
    return state


MESH = pl.DeviceIdType.MESH
PARTS = 3


def move_rows(sources, held, pieces, sems, compute, z, n, others):
    row_send, row_recv, sum_send, sum_recv = sems
    barrier = pltpu.get_barrier_semaphore()
    for k in range(1, n):
        peer = lax.rem(z + k, n)
        pl.semaphore_signal(barrier, inc=1, device_id={LINE: peer}, device_id_type=MESH)
    for peer in others:
        pl.semaphore_signal(barrier, inc=1, device_id=peer, device_id_type=MESH)
    pl.semaphore_wait(barrier, n - 1 + len(others))

    def row_copy(kind, way, hop, source=None):
        step = 1 - 2 * way
        block = jnp.clip(z - step * hop, 0, n - 1)
        peer = jnp.clip(z + step, 0, n - 1)
        return pltpu.make_async_remote_copy(
            src_ref=held[kind].at[block] if source is None else source,
            dst_ref=held[kind].at[block],
            send_sem=row_send.at[kind, way, hop],
            recv_sem=row_recv.at[kind, way, hop],
            device_id={LINE: peer},
            device_id_type=MESH,
        )

    def sends(way, hop):
        step = 1 - 2 * way
        block, peer = z - step * hop, z + step
        return (block >= 0) & (block < n) & (peer >= 0) & (peer < n)

    def arrives(way, hop):
        block = z - (1 - 2 * way) * (hop + 1)
        return (block >= 0) & (block < n)

    def start(kind):
        for way in range(2):
            @pl.when(sends(way, 0))
            def _():
                row_copy(kind, way, 0, sources[kind]).start()

    def take(hop):
        for kind in range(len(held)):
            for way in range(2):
                @pl.when(arrives(way, hop))
                def _():
                    row_copy(kind, way, hop).wait_recv()

                @pl.when(sends(way, hop + 1) & (hop + 1 < n - 1))
                def _():
                    row_copy(kind, way, hop + 1).start()

    def waits(way, block):
        peer, last = z - (1 - 2 * way), (n - 1) * (1 - way)
        return (peer >= 0) & (peer < n) & ((block != last) | (peer != n - 1 - last))

    def far_copy(p):
        mine, arrived = pieces[p]
        block, way = n - 1 - z, jnp.where(z == 0, 1, 0)
        return pltpu.make_async_remote_copy(
            src_ref=mine(block),
            dst_ref=arrived(way, block),
            send_sem=sum_send.at[block, p],
            recv_sem=sum_recv.at[way, block, p],
            device_id={LINE: block},
            device_id_type=MESH,
        )

    def sum_copy(way, block, p):
        mine, arrived = pieces[p]
        return pltpu.make_async_remote_copy(
            src_ref=mine(block),
            dst_ref=arrived(way, block),
            send_sem=sum_send.at[block, p],
            recv_sem=sum_recv.at[way, block, p],
            device_id={LINE: jnp.clip(z + 1 - 2 * way, 0, n - 1)},
            device_id_type=MESH,
        )

    def sent(block, p):
        way = jnp.where(block > z, 0, 1)
        far = ((z == 0) | (z == n - 1)) & (block == n - 1 - z)

        @pl.when(far)
        def _():
            far_copy(p).start()

        @pl.when((block != z) & jnp.logical_not(far) & jnp.logical_not(waits(way, block)))
        def _():
            sum_copy(way, block, p).start()

    def run():
        def both(hop):
            return (hop >= 0) & (z - 1 - hop >= 0) & (z + 1 + hop < n)

        def turn(k, carry):
            hop = lax.div(k + 1, 2) - 1
            block = z + (1 + hop) * (1 - 2 * lax.rem(k, 2))
            odd = lax.rem(k, 2) == 1

            @pl.when(odd & jnp.logical_not(both(hop - 1)))
            def _():
                take(hop)

            @pl.when(jnp.logical_not(odd) & both(hop) & (hop + 1 < n - 1))
            def _():
                take(hop + 1)

            @pl.when((block >= 0) & (block < n))
            def _():
                compute(block, sent)

            return carry

        def far_first(k, carry):
            block = z + (n - 1 - lax.div(k, 2)) * (1 - 2 * lax.rem(k, 2))

            @pl.when((block >= 0) & (block < n))
            def _():
                compute(block, sent)

            return carry

        lax.fori_loop(0, 2 * n - 1, turn if held else far_first, 0)

        first = jnp.where(2 * z < n, 0, 1)
        for way in (first, 1 - first):
            for k in range(1, n):
                block = z + (1 - 2 * way) * k

                @pl.when(waits(way, block) & (block >= 0) & (block < n))
                def _():
                    for p, (mine, arrived) in enumerate(pieces):
                        sum_copy(way, block, p).wait_recv()
                        own, other = mine(block), arrived(way, block)
                        own[...] = (
                            own[...].astype(jnp.float32) + other[...].astype(jnp.float32)
                        ).astype(jnp.bfloat16)
                        sum_copy(way, block, p).start()

    def collect(add):
        for way in range(2):
            for p, (_, arrived) in enumerate(pieces):
                sum_copy(way, z, p).wait_recv()
                add(p, arrived(way, z)[...].astype(jnp.float32))

    def finish():
        for kind in range(len(held)):
            for way in range(2):
                for hop in range(n - 1):
                    @pl.when(sends(way, hop))
                    def _():
                        row_copy(kind, way, hop).wait_send()
        for k in range(1, n):
            for p in range(len(pieces)):
                sum_copy(0, lax.rem(z + k, n), p).wait_send()

    return start, run, collect, finish


def row_pieces(sums, returned, parts):
    width = sums.shape[2] // parts

    def piece(p):
        at = pl.ds(p * width, width)
        return (
            lambda block: sums.at[block, :, at],
            lambda way, block: returned.at[way, block, :, at],
        )

    return [piece(p) for p in range(parts)]


def fetch_weights(layer, own, other, places, sem):
    count = places[0].shape[0]
    mine = lax.axis_index(CORE) == layer

    def copy(group, kind, e):
        return pltpu.make_async_copy(
            group[kind].at[e], places[kind].at[e], sem.at[kind * count + e]
        )

    for kind in range(len(places)):
        for e in range(count):
            @pl.when(mine)
            def _():
                copy(own, kind, e).start()

            @pl.when(jnp.logical_not(mine))
            def _():
                copy(other, kind, e).start()

    def wait():
        for kind in range(len(places)):
            for e in range(count):
                copy(own, kind, e).wait()

    return wait


def sigmoid_of(value):
    return 1.0 / (1.0 + jnp.exp(-value))


def column_of(block, column):
    here = lax.broadcasted_iota(jnp.int32, block.shape, 1) == column
    return jnp.sum(jnp.where(here, block, 0.0), axis=1, keepdims=True)


def experts_forward_kernel(
    layer, experts, x, mask, hidden, router, *refs
):
    own, other, refs = refs[:3], refs[3:6], refs[6:]
    own_dense, other_dense, refs = refs[:4], refs[4:8], refs[8:]
    out, rows, gates_all, gates, stats, gate_out, up_out, gated_out = refs[:8]
    placed, place_sem, keep_sem = refs[8:12], refs[-2], refs[-1]
    passing, (gate_keep, up_keep, gated) = refs[-9:-5], refs[-5:-2]
    refs = refs[:8] + refs[12:-9]
    w_gate, w_up, w_down, sums, returned, mixed, total, stats_all = refs[8:16]
    weight_sem, *sems = refs[16:]
    n, held = rows.shape[0], w_gate.shape[0]
    z = lax.axis_index(LINE)

    def keep_copies(block):
        pairs = (
            (gate_keep.at[:, block], gate_out.at[:, block]),
            (up_keep.at[:, block], up_out.at[:, block]),
            (gated.at[block], gated_out.at[block]),
        )
        return [
            pltpu.make_async_copy(source, target, keep_sem.at[i, block])
            for i, (source, target) in enumerate(pairs)
        ]

    def compute(block, sent):
        picked = rows[block]
        gate_block = gates_all[block].astype(jnp.float32)

        def one(e, carry):
            gate_pre = jnp.dot(picked, w_gate[e], preferred_element_type=jnp.float32)
            up_pre = jnp.dot(picked, w_up[e], preferred_element_type=jnp.float32)
            gate_keep[e, block] = gate_pre.astype(jnp.bfloat16)
            up_keep[e, block] = up_pre.astype(jnp.bfloat16)
            active = gate_pre * sigmoid_of(gate_pre) * up_pre
            share = (column_of(gate_block, z * held + e) * active).astype(jnp.bfloat16)
            inner = share.shape[1]
            gated[block, :, pl.ds(pl.multiple_of(e * inner, inner), inner)] = share
            mixed[e] = share
            return carry

        lax.fori_loop(0, held, one, 0)
        for copy in keep_copies(block):
            copy.start()
        width = out.shape[1] // PARTS
        for part in range(PARTS):
            at = pl.ds(part * width, width)
            result = jnp.zeros((out.shape[0], width), jnp.float32)
            for e in range(held):
                result += jnp.dot(mixed[e], w_down[e, :, at], preferred_element_type=jnp.float32)

            @pl.when(block == z)
            def _():
                total[:, at] = hidden[:, at] + result

            @pl.when(block != z)
            def _():
                sums[block, :, at] = result.astype(jnp.bfloat16)

            sent(block, part)

    own_gates = gates_all.at[z]
    start, run, collect, finish = move_rows(
        (x, own_gates, stats_all.at[z]),
        (rows, gates_all, stats_all),
        row_pieces(sums, returned, PARTS),
        sems,
        compute,
        z,
        n,
        [],
    )
    start(0)
    wait_weights = fetch_weights(layer, own, other, (w_gate, w_up, w_down), weight_sem)
    here = lax.axis_index(CORE) == 1 - layer

    def place_copy(group, i):
        return pltpu.make_async_copy(group[i], passing[i], place_sem.at[0, i])

    def place_out(i):
        return pltpu.make_async_copy(passing[i], placed[i], place_sem.at[1, i])

    logits = jnp.dot(x[...], router[...], preferred_element_type=jnp.float32)
    chosen = mask[...] > 0
    highest = jnp.max(jnp.where(chosen, logits, MASKED), axis=1, keepdims=True)
    exponent = jnp.where(chosen, jnp.exp(logits - highest), 0.0)
    gates[...] = exponent / jnp.sum(exponent, axis=1, keepdims=True)
    own_gates[...] = gates[...].astype(jnp.bfloat16)
    start(1)
    real = lax.broadcasted_iota(jnp.int32, logits.shape, 1) < experts
    highest = jnp.max(jnp.where(real, logits, MASKED), axis=1, keepdims=True)
    exponent = jnp.where(real, jnp.exp(logits - highest), 0.0)
    chance = exponent / jnp.sum(exponent, axis=1, keepdims=True)
    line = lax.broadcasted_iota(jnp.int32, stats.shape, 0)
    stats_all[z] = jnp.where(
        line == 0,
        jnp.sum(chance, axis=0, keepdims=True),
        jnp.where(line == 1, jnp.sum(mask[...], axis=0, keepdims=True), 0.0),
    )
    start(2)
    rows[z] = x[...]
    wait_weights()
    for i in range(4):
        @pl.when(here)
        def _():
            place_copy(own_dense, i).start()

        @pl.when(jnp.logical_not(here))
        def _():
            place_copy(other_dense, i).start()

    run()
    for i in range(4):
        place_copy(own_dense, i).wait()
        place_out(i).start()
    stats[...] = jnp.sum(stats_all[...], axis=0)
    width = out.shape[1] // PARTS

    def add(p, value):
        total[:, p * width : (p + 1) * width] += value

    collect(add)
    out[...] = total[...].astype(jnp.bfloat16)
    finish()
    for i in range(4):
        place_out(i).wait()
    for block in range(n):
        for copy in keep_copies(block):
            copy.wait()


def experts_backward_kernel(layer, grad, gates, *refs):
    own, other, saved_rows, saved_gated, refs = refs[:3], refs[3:6], refs[6], refs[7], refs[8:]
    kept, refs = refs[:2], refs[2:]
    keep_places, keep_sem, refs = refs[-3:-1], refs[-1], refs[:-3]
    gate_keep, up_keep = keep_places
    carried = layer == 0
    if carried:
        extra, refs = refs[0], refs[1:]
        extra_sum, refs = refs[6], refs[:6] + refs[7:]
        landed, extra_send, extra_recv = refs[-3:]
        refs = refs[:-3]
    out, out_gates, rows_both, gated_both, grad_both, pre_both = refs[:6]
    w_gate, w_up, w_down, sums, sum_gates, returned, returned_gates, away, dots = refs[6:15]
    weight_sem, core_send, core_recv, core_local, *sems = refs[15:]
    n, held = gates.shape[0], w_gate.shape[0]
    half, inner = held // 2, w_gate.shape[2]
    core = lax.axis_index(CORE)
    z = lax.axis_index(LINE)
    turned_dims = (((1,), (1,)), ((), ()))
    gathered = layer == 1
    rows = grad if gathered else grad_both.at[core]

    def to_core(number, source, target):
        return pltpu.make_async_remote_copy(
            src_ref=source,
            dst_ref=target,
            send_sem=core_send.at[number],
            recv_sem=core_recv.at[number],
            device_id={CORE: 1 - core},
            device_id_type=MESH,
        )

    def block_copies(block):
        away_copy = to_core(2 + n + block, away.at[block], pre_both.at[core, block])
        if gathered:
            return (away_copy,)
        return (to_core(2 + block, rows.at[block], rows.at[block]), away_copy)

    def columns(at):
        return pl.ds(pl.multiple_of(at * half * inner, half * inner), half * inner)

    def whole_copies():
        copies = (
            to_core(0, saved_rows, rows_both.at[core]),
            to_core(1, saved_gated.at[:, :, columns(1 - core)], gated_both.at[core]),
        )
        return copies + ((to_core(2, grad, grad_both.at[core]),) if gathered else ())

    def local_copies():
        copies = (
            pltpu.make_async_copy(saved_rows, rows_both.at[core], core_local.at[0]),
            pltpu.make_async_copy(
                saved_gated.at[:, :, columns(core)], gated_both.at[core], core_local.at[1]
            ),
        )
        if gathered:
            copies += (pltpu.make_async_copy(grad, grad_both.at[core], core_local.at[2]),)
        return copies

    me, count = lax.axis_index(GROUP), lax.axis_size(GROUP)
    peers = [lax.rem(me + k, count) for k in range(1, count)] if carried else []

    def extra_copy(k, peer, slot):
        return pltpu.make_async_remote_copy(
            src_ref=extra.at[:, peer],
            dst_ref=landed.at[slot],
            send_sem=extra_send.at[k],
            recv_sem=extra_recv.at[slot],
            device_id={GROUP: peer},
            device_id_type=MESH,
        )

    def compute(block, sent):
        picked = rows[block]
        gate_block = gates[block].astype(jnp.float32)
        dots[...] = jnp.zeros(dots.shape, jnp.float32)

        def one(e, place, j):
            raw = lax.dot_general(
                picked, w_down[e], turned_dims, preferred_element_type=jnp.float32
            )
            gate_pre = gate_keep[e, block].astype(jnp.float32)
            up_pre = up_keep[e, block].astype(jnp.float32)
            sigmoid = sigmoid_of(gate_pre)
            silu = gate_pre * sigmoid
            column = z * held + e
            dot = jnp.sum(raw * (silu * up_pre), axis=1, keepdims=True)
            here = lax.broadcasted_iota(jnp.int32, dots.shape, 1) == column
            dots[...] += jnp.where(here, dot, 0.0)
            active = column_of(gate_block, column) * raw
            place[:, pl.ds(pl.multiple_of(j * inner, inner), inner)] = (
                active * up_pre * sigmoid * (1.0 + gate_pre * (1.0 - sigmoid))
            ).astype(jnp.bfloat16)
            place[:, pl.ds(pl.multiple_of((half + j) * inner, inner), inner)] = (
                active * silu
            ).astype(jnp.bfloat16)

        def own_half(j, carry):
            one(core * half + j, pre_both.at[core, block], j)
            return carry

        def other_half(j, carry):
            one((1 - core) * half + j, away.at[block], j)
            return carry

        lax.fori_loop(0, half, other_half, 0)
        for copy in block_copies(block):
            copy.start()
        lax.fori_loop(0, half, own_half, 0)
        sum_gates[block] = dots[...].astype(jnp.bfloat16)

        @pl.when(block == z)
        def _():
            out_gates[...] = dots[...]

        sent(block, PARTS)
        width = out.shape[1] // PARTS
        for part in range(PARTS):
            at = pl.ds(part * width, width)
            result = jnp.zeros((out.shape[0], width), jnp.float32)
            for place, side in ((away.at[block], 1 - core), (pre_both.at[core, block], core)):
                for kind, right in enumerate((w_gate, w_up)):
                    for j in range(half):
                        left = place[:, pl.ds((kind * half + j) * inner, inner)]
                        result += lax.dot_general(
                            left,
                            right[side * half + j, at, :],
                            turned_dims,
                            preferred_element_type=jnp.float32,
                        )

            @pl.when(block == z)
            def _():
                out[:, at] = result

            @pl.when(block != z)
            def _():
                sums[block, :, at] = result.astype(jnp.bfloat16)

            sent(block, part)

    gate_piece = (lambda block: sum_gates.at[block], lambda way, block: returned_gates.at[way, block])
    start, run, collect, finish = move_rows(
        () if gathered else (grad,),
        () if gathered else (rows,),
        row_pieces(sums, returned, PARTS) + [gate_piece],
        sems,
        compute,
        z,
        n,
        [{CORE: 1 - core}] + [{GROUP: peer} for peer in peers],
    )
    if not gathered:
        start(0)
    for k, peer in enumerate(peers):
        extra_copy(k, peer, me).start()
    if carried:
        mine = pltpu.make_async_copy(extra.at[:, me], landed.at[me], extra_send.at[len(peers)])
        mine.start()
    wait_weights = fetch_weights(layer, own, other, (w_gate, w_up, w_down), weight_sem)
    keep_copies = [
        pltpu.make_async_copy(kept[i], keep_places[i], keep_sem.at[i]) for i in range(2)
    ]
    for copy in keep_copies:
        copy.start()
    for copy in whole_copies() + local_copies():
        copy.start()
    if not gathered:
        rows[z] = grad[...]
    for copy in keep_copies:
        copy.wait()
    wait_weights()
    run()
    width = out.shape[1] // PARTS

    def add(p, value):
        if p == PARTS:
            out_gates[...] += value
        else:
            out[:, p * width : (p + 1) * width] += value

    if carried:
        mine.wait()
        for k, peer in enumerate(peers):
            extra_copy(k, peer, peer).wait_recv()
        half, rows_each = extra_sum.shape[:2]
        step = 16 if rows_each % 16 == 0 else rows_each

        def add_up(i, carry):
            at = pl.ds(pl.multiple_of(i * step, step), step)
            for j in range(half):
                value = landed[0, j, at].astype(jnp.float32)
                for k in range(1, count):
                    value += landed[k, j, at].astype(jnp.float32)
                extra_sum[j, at] = value.astype(jnp.bfloat16)
            return carry

        lax.fori_loop(0, rows_each // step, add_up, 0)
    collect(add)
    finish()
    for k, peer in enumerate(peers):
        extra_copy(k, peer, me).wait_send()
    for copy in local_copies():
        copy.wait()
    for copy in whole_copies():
        copy.wait()
    for block in range(n):
        for copy in block_copies(block):
            copy.wait()


def exchange_scratch(n, kinds_out, kinds_back):
    return [
        pltpu.SemaphoreType.DMA((kinds_out, 2, n)),
        pltpu.SemaphoreType.DMA((kinds_out, 2, n)),
        pltpu.SemaphoreType.DMA((n, kinds_back)),
        pltpu.SemaphoreType.DMA((2, n, kinds_back)),
    ]


def expert_call(kernel, operands, own, other, extra, shapes, scratch, collective, loose=0):
    vmem, free = pl.BlockSpec(memory_space=pltpu.VMEM), pl.BlockSpec(memory_space=pl.ANY)
    weights = [pltpu.VMEM(array.shape, jnp.bfloat16) for array in own]
    return pl.pallas_call(
        kernel,
        out_shape=shapes,
        in_specs=[vmem] * len(operands) + [free] * (6 + len(extra)),
        out_specs=[vmem] * (len(shapes) - loose) + [free] * loose,
        scratch_shapes=weights + scratch,
        compiler_params=pltpu.CompilerParams(
            collective_id=collective, has_side_effects=True, vmem_limit_bytes=46 * 2**20
        ),
        cost_estimate=pl.CostEstimate(
            flops=5 * 10**10, bytes_accessed=10**8, transcendentals=0
        ),
    )(*operands, *own, *other, *extra)


def experts_forward(
    layer, normed_two, mask, hidden, router, own, other, own_dense, other_dense, experts
):
    n, held = lax.axis_size(LINE), own[0].shape[0]
    length, width = normed_two.shape
    inner = own[0].shape[2]
    low, full = jnp.bfloat16, jnp.float32
    kept = jax.ShapeDtypeStruct((held, n, length, inner), low)
    shapes = [
        jax.ShapeDtypeStruct((length, width), low),
        jax.ShapeDtypeStruct((n, length, width), low),
        jax.ShapeDtypeStruct((n, length, COLUMNS), low),
        jax.ShapeDtypeStruct((length, COLUMNS), full),
        jax.ShapeDtypeStruct((8, COLUMNS), full),
        kept,
        kept,
        jax.ShapeDtypeStruct((n, length, held * inner), low),
    ] + [jax.ShapeDtypeStruct(array.shape, low) for array in own_dense]
    scratch = [
        pltpu.VMEM((n, length, width), low),
        pltpu.VMEM((2, n, length, width), low),
        pltpu.VMEM((held, length, inner), low),
        pltpu.VMEM((length, width), full),
        pltpu.VMEM((n, 8, COLUMNS), full),
        pltpu.SemaphoreType.DMA((3 * held,)),
    ] + exchange_scratch(n, 3, PARTS)
    scratch += [pltpu.VMEM(array.shape, low) for array in own_dense]
    scratch += [pltpu.VMEM(shape.shape, low) for shape in shapes[5:8]]
    scratch.append(pltpu.SemaphoreType.DMA((2, 4)))
    scratch.append(pltpu.SemaphoreType.DMA((3, n)))
    kernel = functools.partial(experts_forward_kernel, layer, experts)
    return expert_call(
        kernel,
        (normed_two, mask, hidden, router),
        own,
        other,
        (*own_dense, *other_dense),
        shapes,
        scratch,
        1 + layer,
        7,
    )


def experts_backward(layer, grad_low, gates, gate_keep, up_keep, rows, gated, own, other, extra):
    held, n, length, inner = gate_keep.shape
    width = grad_low.shape[-1]
    low, full = jnp.bfloat16, jnp.float32
    shapes = [
        jax.ShapeDtypeStruct((length, width), full),
        jax.ShapeDtypeStruct((length, COLUMNS), full),
        jax.ShapeDtypeStruct((2, n, length, width), low),
        jax.ShapeDtypeStruct((2, n, length, held // 2 * inner), low),
        jax.ShapeDtypeStruct((2, n, length, width), low),
        jax.ShapeDtypeStruct((2, n, length, held * inner), low),
    ]
    scratch = [
        pltpu.VMEM((n, length, width), low),
        pltpu.VMEM((n, length, COLUMNS), low),
        pltpu.VMEM((2, n, length, width), low),
        pltpu.VMEM((2, n, length, COLUMNS), low),
        pltpu.VMEM((n, length, held * inner), low),
        pltpu.VMEM((length, COLUMNS), full),
        pltpu.SemaphoreType.DMA((3 * held,)),
        pltpu.SemaphoreType.DMA((2 + 2 * n,)),
        pltpu.SemaphoreType.DMA((2 + 2 * n,)),
        pltpu.SemaphoreType.DMA((3,)),
    ] + exchange_scratch(n, 1, PARTS + 1)
    if layer == 0:
        half, count, *block = extra.shape
        shapes.append(jax.ShapeDtypeStruct((half, *block), low))
        scratch += [
            pltpu.VMEM((count, half, *block), low),
            pltpu.SemaphoreType.DMA((count,)),
            pltpu.SemaphoreType.DMA((count,)),
        ]
    scratch += [pltpu.VMEM(gate_keep.shape, low)] * 2 + [pltpu.SemaphoreType.DMA((2,))]
    kernel = functools.partial(experts_backward_kernel, layer)
    return expert_call(
        kernel,
        (grad_low, gates),
        own,
        other,
        (rows, gated, gate_keep, up_keep) + (() if extra is None else (extra,)),
        shapes,
        scratch,
        3 + layer,
    )


def attention_backward(grad_hidden, inputs, state, weights):
    gain_attn, w_query, w_key, w_value, w_out, gain_moe = weights[:6]
    (inverse_one, normed_one, queries, key_rows, values, weight, attended, hidden, inverse_two, normed_two) = state
    length = inputs.shape[0]
    grad_branch = grad_hidden.astype(jnp.bfloat16)
    grad_attended = jnp.einsum("td,cd->tc", grad_branch, w_out, preferred_element_type=jnp.float32)
    grad_attended = grad_attended.astype(jnp.bfloat16).reshape(length, KVH, H // KVH, HD)
    grad_weight = jnp.einsum(
        "qkgd,skd->kgqs", grad_attended, values, preferred_element_type=jnp.float32
    )
    grad_values = jnp.einsum(
        "kgqs,qkgd->skd",
        weight.astype(jnp.bfloat16),
        grad_attended,
        preferred_element_type=jnp.float32,
    )
    grad_values = grad_values.astype(jnp.bfloat16).reshape(length, KVH * HD)
    grad_scores = (
        weight * (grad_weight - jnp.sum(weight * grad_weight, axis=-1, keepdims=True))
    ).astype(jnp.bfloat16)
    score_scale = HD ** (-0.5)
    grouped = queries.reshape(length, KVH, H // KVH, HD)
    grad_queries = jnp.einsum(
        "kgqs,skd->qkgd", grad_scores, key_rows, preferred_element_type=jnp.float32
    )
    grad_queries = grad_queries.reshape(length, H, HD) * score_scale
    grad_keys = (
        jnp.einsum("kgqs,qkgd->skd", grad_scores, grouped, preferred_element_type=jnp.float32)
        * score_scale
    )
    cosine_table, sine_table = rotary_tables(length)
    grad_query_pre = (
        unrotate(grad_queries, cosine_table, sine_table)
        .reshape(length, H * HD)
        .astype(jnp.bfloat16)
    )
    grad_key_pre = (
        unrotate(grad_keys, cosine_table, sine_table).reshape(length, KVH * HD).astype(jnp.bfloat16)
    )
    grad_normed_one = (
        jnp.einsum("tq,cq->tc", grad_query_pre, w_query, preferred_element_type=jnp.float32)
        + jnp.einsum("tq,cq->tc", grad_key_pre, w_key, preferred_element_type=jnp.float32)
        + jnp.einsum("tq,cq->tc", grad_values, w_value, preferred_element_type=jnp.float32)
    )
    grad_norm_one, grad_gain_attn = norm_back(grad_normed_one, inputs, inverse_one, gain_attn)
    grad_inputs = grad_hidden + grad_norm_one
    grad_qkv = jnp.concatenate([grad_query_pre, grad_key_pre, grad_values], axis=1)
    return grad_inputs, grad_gain_attn, grad_qkv, grad_branch


def turned(left, right):
    return jnp.einsum("tc,tq->cq", left, right, preferred_element_type=jnp.float32)


def body(tokens, cotangent, segments, routes, *weight_arrays):
    core = lax.axis_index(CORE)
    first = core == 0
    experts = weight_arrays[6].shape[2]
    w_gate = weight_arrays[7]
    held = w_gate.shape[1]
    own = [array[0] for array in weight_arrays]
    other = [swapped(array) for array in own]
    weights = [
        [jnp.where(first, a, b) for a, b in zip(own[:7], other[:7])],
        [jnp.where(first, b, a) for a, b in zip(own[:7], other[:7])],
    ]
    inputs_low = lax.dynamic_slice_in_dim(tokens, core * SEQ, SEQ, 0)
    grad_low = lax.dynamic_slice_in_dim(cotangent, core * SEQ, SEQ, 0)
    cotangent_all = lax.all_gather(grad_low, LINE, axis=0)
    segment_row = lax.dynamic_index_in_dim(segments, core, 0, keepdims=False)
    mine = lax.dynamic_slice_in_dim(routes[0], core * SEQ, SEQ, 0)
    got = swapped(lax.dynamic_slice_in_dim(routes[0], (1 - core) * SEQ, SEQ, 0))
    routes_here = jnp.stack([jnp.where(first, mine, got), jnp.where(first, got, mine)])
    masks = multi_hot(routes_here, COLUMNS)
    own_experts, other_experts = own[7:], other[7:]

    saved, outs, stats = [], [], []
    for s in range(2):
        inputs = inputs_low.astype(jnp.float32)
        state = attention_forward(inputs, weights[s], segment_row)
        hidden, normed_two = state[7], state[9]
        if s == 0:
            normed_two, cotangent_all = lax.optimization_barrier((normed_two, cotangent_all))
        both_cores = [jnp.concatenate([a, swapped(a)]) for a in (state[1], state[6])]
        router = jnp.pad(weights[s][6], ((0, 0), (0, COLUMNS - experts)))
        inputs_low, rows, gates_all, gates, stat, *kept, query, key, value, out = experts_forward(
            s,
            normed_two,
            masks[s],
            hidden,
            router,
            own_experts,
            other_experts,
            own[1:5],
            other[1:5],
            experts,
        )
        weights[1 - s][1:5] = [query, key, value, out]
        outs.append(inputs_low)
        stats.append(stat)
        expert_state = (rows, gates_all, gates, *kept)
        saved.append((inputs, state, expert_state, both_cores))

    dp, deep = lax.axis_size(GROUP), lax.axis_size(LINE)
    grads = [None, None]
    input_grads = [None, None]
    for s in (1, 0):
        inputs, state, expert_state, both_cores = saved[s]
        (inverse_one, normed_one, _, _, _, _, attended, hidden, inverse_two, normed_two) = state
        rows_all, gates_all, gates, gate_keep, up_keep, gated = expert_state
        gain_moe, w_router = weights[s][5], weights[s][6]
        grad_sum, grad_gates, rows_both, gated_both, grad_both, pre_both, *sums = experts_backward(
            s,
            cotangent_all if s == 1 else grad_low,
            gates_all,
            gate_keep,
            up_keep,
            rows_all,
            gated,
            own_experts,
            other_experts,
            None if s == 1 else grads[1][1].reshape(held // 2, dp, -1, D),
        )
        if s == 0:
            (second_down,) = sums
        inner = w_gate.shape[3]
        grad_gate_up = turned(
            rows_both.reshape(-1, D), pre_both.reshape(-1, held * inner)
        ).astype(jnp.bfloat16)
        if s == 1:
            grad_sum, grad_gate_up = lax.optimization_barrier((grad_sum, grad_gate_up))
            second_pre = lax.psum_scatter(grad_gate_up, GROUP, scatter_dimension=0, tiled=True)
        else:
            grad_sum, second_pre = lax.optimization_barrier((grad_sum, second_pre))
        gates, grad_gates = gates[:, :experts], grad_gates[:, :experts]
        grad_chosen = gates * (grad_gates - jnp.sum(gates * grad_gates, axis=-1, keepdims=True))
        grad_logits = grad_chosen.astype(jnp.bfloat16)
        grad_normed_two = grad_sum + jnp.einsum(
            "te,de->td", grad_logits, w_router, preferred_element_type=jnp.float32
        )
        grad_norm_two, grad_gain_moe = norm_back(grad_normed_two, hidden, inverse_two, gain_moe)
        grad_hidden = grad_low.astype(jnp.float32) + grad_norm_two
        grad_inputs, grad_gain_attn, grad_qkv, grad_branch = attention_backward(
            grad_hidden, inputs, state, weights[s]
        )
        if s == 1:
            grad_inputs, gated_both = lax.optimization_barrier((grad_inputs, gated_both))
        grad_down = turned(
            gated_both.reshape(-1, held // 2 * inner), grad_both.reshape(-1, D)
        ).astype(jnp.bfloat16)

        def halves(array):
            width = array.shape[1] // 2
            return (
                lax.dynamic_slice_in_dim(array, core * width, width, 1),
                lax.dynamic_slice_in_dim(array, (1 - core) * width, width, 1),
            )
        qkv_keep, qkv_send = halves(grad_qkv)
        branch_keep, branch_send = halves(grad_branch)
        grad_w_qkv = turned(
            both_cores[0], jnp.concatenate([qkv_keep, swapped(qkv_send)])
        ).astype(jnp.bfloat16)
        grad_w_out = turned(
            both_cores[1], jnp.concatenate([branch_keep, swapped(branch_send)])
        ).astype(jnp.bfloat16)
        grad_w_router = turned(normed_two, grad_logits)
        small = jnp.concatenate(
            [grad_gain_attn[:, None], grad_gain_moe[:, None], grad_w_router], axis=1
        ).astype(jnp.bfloat16)
        small = jnp.pad(small, ((0, 0), (0, COLUMNS - small.shape[1])))
        if s == 1:
            grad_inputs, grad_down, grad_w_qkv, grad_w_out = lax.optimization_barrier(
                (grad_inputs, grad_down, grad_w_qkv, grad_w_out)
            )
            dense = jnp.concatenate([grad_w_qkv, grad_w_out], axis=1)
            second_dense = lax.psum_scatter(dense, GROUP, scatter_dimension=0, tiled=True)
        grads[s] = (grad_gate_up, grad_down, grad_w_qkv, grad_w_out, small)
        input_grads[s] = grad_inputs
        grad_low = grad_inputs.astype(jnp.bfloat16)

    dp, deep = lax.axis_size(GROUP), lax.axis_size(LINE)
    half, inner = held // 2, w_gate.shape[3]
    grad_gate_up, grad_down, grad_w_qkv, grad_w_out, small = grads[0]
    arrays = [
        grad_gate_up.reshape(dp, D // dp, held * inner),
        grad_down.reshape(half, dp, inner // dp, D),
    ]
    lanes = dense_lanes(2, grad_w_qkv.shape[1])
    for array in (grad_w_qkv, grad_w_out, small):
        arrays.append(array.reshape(dp, deep, array.shape[0] // (dp * deep), array.shape[1]))
    width = grad_w_qkv.shape[1]
    whole = second_dense.shape[1]
    for columns, kind in (((0, width), QKV), ((width, whole - width), OUT)):
        start, size = columns
        target = (kind, slice(None), pl.ds(start - (start // width) * width, size))
        lanes.append((len(arrays), (False, columns), [(LINE, bits_of(LINE))], 1, target))
    arrays.append(second_dense.reshape(deep, second_dense.shape[0] // deep, whole))
    lanes.append(small_lane(len(arrays), 1))
    lanes += expert_lanes(0, inner) + down_lanes(1, 0)
    small = grads[1][4]
    arrays.append(small.reshape(dp, deep, small.shape[0] // (dp * deep), small.shape[1]))
    out_keep = jnp.where(first, outs[0], outs[1])
    out_got = swapped(jnp.where(first, outs[1], outs[0]))
    layer_out = jnp.where(
        first, jnp.concatenate([out_keep, out_got]), jnp.concatenate([out_got, out_keep])
    )
    low_one = input_grads[1].astype(jnp.bfloat16).astype(jnp.float32)
    grad_keep = jnp.where(first, input_grads[0], low_one)
    grad_got = swapped(jnp.where(first, low_one, input_grads[0]))
    input_grad = jnp.where(
        first, jnp.concatenate([grad_keep, grad_got]), jnp.concatenate([grad_got, grad_keep])
    )
    stats = jnp.concatenate(stats, axis=0)
    stats, layer_out, input_grad = lax.optimization_barrier((stats, layer_out, input_grad))
    *grads, qkv, out, small, stats = sum_scatter(
        arrays, lanes, second_pre, second_down, stats, inner, 0
    )
    full = jnp.float32
    w_gate_grad, w_up_grad, w_down_grad = (
        grad.reshape(held, *grad.shape[2:]).astype(full) for grad in grads
    )
    qkv = jnp.concatenate([qkv[0], qkv[1]], axis=1).astype(full)
    grad_w_out = jnp.concatenate([out[0], out[1]], axis=1).astype(full)
    small = small[0].astype(full) + small[1].astype(full)
    heads, kv = H * HD, KVH * HD
    stats = lax.dynamic_index_in_dim(stats.reshape(2, 8, COLUMNS), core, 0)
    token_total = SEQ * lax.axis_size((CORE, GROUP, LINE))
    counts, chances = stats[:, 1, :experts], stats[:, 0, :experts]
    balance = experts * (counts / (token_total * TOPK) * chances / token_total)
    results = (
        layer_out,
        input_grad,
        small[:, 0],
        qkv[:, :heads],
        qkv[:, heads : heads + kv],
        qkv[:, heads + kv :],
        grad_w_out,
        small[:, 1],
        small[:, 2 : 2 + experts],
        w_gate_grad,
        w_up_grad,
        w_down_grad,
    )
    return tuple(result[None] for result in results) + (balance,)


def solution(mesh):
    return jax.shard_map(
        body,
        mesh=mesh,
        in_specs=(
            P((GROUP, LINE), None),
            P((GROUP, LINE), None),
            P((GROUP, LINE), None),
            P(CORE, (GROUP, LINE), None),
            P(CORE, None),
            P(CORE, None, None),
            P(CORE, None, None),
            P(CORE, None, None),
            P(CORE, None, None),
            P(CORE, None),
            P(CORE, None, None),
            P(CORE, LINE, None, None),
            P(CORE, LINE, None, None),
            P(CORE, LINE, None, None),
        ),
        out_specs=(
            P(CORE, (GROUP, LINE), None),
            P(CORE, (GROUP, LINE), None),
            P(CORE, (GROUP, LINE)),
            P(CORE, (GROUP, LINE), None),
            P(CORE, (GROUP, LINE), None),
            P(CORE, (GROUP, LINE), None),
            P(CORE, (GROUP, LINE), None),
            P(CORE, (GROUP, LINE)),
            P(CORE, (GROUP, LINE), None),
            P(CORE, LINE, GROUP, None),
            P(CORE, LINE, GROUP, None),
            P(CORE, LINE, GROUP, None),
            P(CORE, None),
        ),
        check_vma=False,
    )
```

```python
import functools
import itertools
from types import SimpleNamespace

import jax
import jax.numpy as jnp
from jax import lax
from jax.experimental import pallas as pl
from jax.experimental.pallas import tpu as pltpu
from jax.sharding import PartitionSpec as P

D = 1536
H = 24
KVH = 8
HD = 64
TOPK = 8
SEQ = 96


EPSILON = 1e-05
THETA = 10000.0
MASKED = -1e30
COLUMNS = 128
GATE, UP, DOWN, QKV, OUT, SMALL = range(6)
CORE, GROUP, LINE = "section", "dp", "expert"
INNER = "inner"


def matmul(left_side, right_side):
    return jnp.dot(left_side, right_side, preferred_element_type=jnp.float32)


def rotary_tables(length):
    half_width = HD // 2
    position = jnp.arange(length, dtype=jnp.float32)[:, None]
    freq_rate = THETA ** (-jnp.arange(half_width, dtype=jnp.float32) / half_width)
    angles = position * freq_rate[None, :]
    return (jnp.cos(angles)[:, None, :], jnp.sin(angles)[:, None, :])


def rotate(tensor, cosine_table, sine_table):
    half_width = HD // 2
    first_half = tensor[..., :half_width]
    second_half = tensor[..., half_width:]
    return jnp.concatenate(
        [
            first_half * cosine_table - second_half * sine_table,
            second_half * cosine_table + first_half * sine_table,
        ],
        axis=-1,
    )


def unrotate(gradient, cosine_table, sine_table):
    half_width = HD // 2
    first_half = gradient[..., :half_width]
    second_half = gradient[..., half_width:]
    return jnp.concatenate(
        [
            first_half * cosine_table + second_half * sine_table,
            second_half * cosine_table - first_half * sine_table,
        ],
        axis=-1,
    )


def norm_back(grad_normed, tensor, inverse, gain_vector):
    scaled = grad_normed * gain_vector
    grad_gain = jnp.sum(grad_normed * tensor * inverse, axis=0)
    grad_tensor = inverse * scaled - tensor * inverse**3 * jnp.mean(
        scaled * tensor, axis=-1, keepdims=True
    )
    return (grad_tensor, grad_gain)


def attention_scores(queries, key_rows, segment_row):
    length = queries.shape[0]
    grouped = queries.reshape(length, KVH, H // KVH, HD)
    scores = jnp.einsum(
        "qkgd,skd->kgqs", grouped, key_rows, preferred_element_type=jnp.float32
    ) * HD ** (-0.5)
    position = jnp.arange(length)
    allowed = (position[None, :] <= position[:, None]) & (
        segment_row[:, None] == segment_row[None, :]
    )
    return jnp.where(allowed[None, None], scores, MASKED)


def multi_hot(route_rows, experts):
    columns = jnp.arange(experts, dtype=jnp.int32)
    return jnp.sum(
        (route_rows[..., None] == columns).astype(jnp.float32), axis=-2
    )


def swapped(array):
    return lax.ppermute(array, CORE, [(0, 1), (1, 0)])


def add_slab(total, arrived):
    *lead, rows, _ = total.shape
    step = 16 if rows % 16 == 0 else rows
    for where in itertools.product(*(range(n) for n in lead)):

        def add(i, carry):
            at = (*where, pl.ds(pl.multiple_of(i * step, step), step), slice(None))
            both = total[at].astype(jnp.float32) + arrived[at].astype(jnp.float32)
            total[at] = both.astype(jnp.bfloat16)
            return carry

        lax.fori_loop(0, rows // step, add, 0)


def sum_scatter_kernel(plan, *refs):
    lanes, ins, copies = plan
    sources = refs[:ins]
    second_pre, second_down, stats_in = refs[ins : ins + 3]
    stage, stats = refs[ins + 3 : ins + 9], refs[ins + 9]
    scratch = list(refs[ins + 10 :])
    send_sem, recv_sem, local_sem, stats_got, stats_send, stats_recv, core_send, core_recv = (
        scratch[-8:]
    )
    core = lax.axis_index(CORE)
    partners = []
    for lane in lanes:
        for axis, bits in lane.phases:
            partners += [(axis, bit) for bit in bits if (axis, bit) not in partners]
    partners.append((CORE, 0))
    index = {axis: lax.axis_index(axis) for axis, _ in partners}
    mine = {(axis, bit): (index[axis] >> bit) & 1 for axis, bit in partners}
    far = {key: index[key[0]] + (1 - 2 * mine[key]) * (1 << key[1]) for key in partners}
    barrier = pltpu.get_barrier_semaphore()
    peers = [{axis: far[axis, bit]} for axis, bit in partners if axis != GROUP]
    groups = lax.axis_size(GROUP)
    peers += [{GROUP: lax.rem(lax.axis_index(GROUP) + k, groups)} for k in range(1, groups)]
    for peer in peers:
        pl.semaphore_signal(
            barrier, inc=1, device_id=peer, device_id_type=pl.DeviceIdType.MESH
        )
    pl.semaphore_wait(barrier, len(peers))

    counter = itertools.count()

    def send(source, target, key):
        number = next(counter)
        copy = pltpu.make_async_remote_copy(
            src_ref=source,
            dst_ref=target,
            send_sem=send_sem.at[number],
            recv_sem=recv_sem.at[number],
            device_id={key[0]: far[key]},
            device_id_type=pl.DeviceIdType.MESH,
        )
        copy.start()
        return copy

    def place(axis, values):
        total = 0
        for bit, value in values.items():
            total = total + value * (1 << bit)
        return total

    def sum_stats():
        count = lax.axis_size(GROUP)
        me = lax.axis_index(GROUP)

        def copy(at, source, slot, target):
            return pltpu.make_async_remote_copy(
                src_ref=source,
                dst_ref=stats_got.at[slot],
                send_sem=stats_send.at[at],
                recv_sem=stats_recv.at[slot],
                device_id=target,
                device_id_type=pl.DeviceIdType.MESH,
            )

        for k in range(1, count):
            copy(k, stats_in, me, {GROUP: lax.rem(me + k, count)}).start()
        yield
        stats[...] = stats_in[...]
        for k in range(1, count):
            peer = lax.rem(me + k, count)
            copy(k, stats_in, peer, {GROUP: peer}).wait_recv()
            stats[...] += stats_got[peer]
        both = copy(0, stats, count, {CORE: far[CORE, 0]})
        both.start()
        yield
        both.wait()
        stats[...] += stats_got[count]
        for k in range(1, count):
            copy(k, stats_in, me, {GROUP: lax.rem(me + k, count)}).wait_send()

    summing = sum_stats()
    next(summing)

    def to_stage(number, source, kind, *at):
        spot = stage[kind].at[(core, *at)]
        return spot, pltpu.make_async_remote_copy(
            src_ref=source,
            dst_ref=spot,
            send_sem=core_send.at[number],
            recv_sem=core_recv.at[number],
            device_id={CORE: 1 - core},
            device_id_type=pl.DeviceIdType.MESH,
        )

    inner = stage[GATE].shape[3]
    wholes = []
    half = stage[GATE].shape[1]
    for number in range(3 * half):
        kind, j = divmod(number, half)
        if kind == DOWN:
            source = second_down.at[j]
        else:
            source = second_pre.at[:, pl.ds(number * inner, inner)]
        spot, copy = to_stage(len(lanes) + number, source, kind, j)
        wholes.append((copy, pltpu.make_async_copy(source, spot, core_send.at[len(lanes) + number])))
    for copy, here in wholes:
        @pl.when(core == 1)
        def _(here=here):
            here.start()

        @pl.when(core == 0)
        def _(copy=copy):
            copy.start()

    moved = []
    started = []
    states = []
    for number, lane in enumerate(lanes):
        count = len(lane.buffers)
        buffers, scratch = scratch[:count], scratch[count:]
        source = sources[lane.source]
        prefix = lane.prefix
        if isinstance(prefix, int):
            source = source.at[prefix]

        def part(at, source=source, prefix=prefix):
            if isinstance(prefix, int):
                return source.at[at]
            inner, columns = prefix
            where = (slice(None), at) if inner else (at,)
            if columns is not None:
                where += (slice(None),) * (len(source.shape) - len(where) - 1) + (pl.ds(*columns),)
            return source.at[where]

        axis, bits = lane.phases[0]
        total, arrived = buffers[0], buffers[1:]
        rest = [bit for bit in bits[1:]]
        pending = []
        for choice in itertools.product((0, 1), repeat=len(rest)):
            values = dict(zip(rest, choice))
            slot = sum(value << i for i, value in enumerate(choice))
            far_at = place(axis, {**values, bits[0]: 1 - mine[axis, bits[0]]})
            here_at = place(axis, {**values, bits[0]: mine[axis, bits[0]]})
            copy = send(part(far_at), arrived[0].at[slot], (axis, bits[0]))
            pending.append((copy, slot))
            started.append(copy)
            states.append((number, part(here_at), slot, total))
        lane_state = SimpleNamespace(total=total, arrived=arrived, pending=pending)
        lane.state = lane_state
    locals_ = {}
    for at, (number, here, slot, total) in enumerate(states):
        copy = pltpu.make_async_copy(here, total.at[slot], local_sem.at[at])
        copy.start()
        locals_[number, slot] = copy
    short = [item for item in enumerate(lanes) if len(item[1].phases) == 1 and item[1].rows]
    long = [item for item in enumerate(lanes) if item not in short]
    turns = [(1, long), (1, short)]
    count = max(sum(len(bits) for _, bits in lane.phases) for lane in lanes)
    for step in range(2, count + 1):
        turns += [(2 * step - 2, long), (2 * step - 1, long), (step, short)]
    for at, (step, group) in enumerate(turns):
        if at == 2:
            next(summing)
        for number, lane in group:
            state = lane.state
            sizes = [len(bits) for _, bits in lane.phases]
            if step > sum(sizes):
                continue
            if step <= sizes[0]:
                axis, bits = lane.phases[0]
                resolved, rest = bits[:step], bits[step:]

                def slot_of(values):
                    found = 0
                    for i, bit in enumerate(bits[1:]):
                        found = found + values.get(bit, mine[axis, bit]) * (1 << i)
                    return found

                for copy, slot in state.pending:
                    copy.wait_recv()
                    if step == 1:
                        locals_[number, slot].wait()
                state.pending_next = []
                for choice in itertools.product((0, 1), repeat=len(rest)):
                    values = dict(zip(rest, choice))
                    got = sum(value << i for i, value in enumerate(choice))
                    add_slab(
                        state.total.at[slot_of(values)], state.arrived[step - 1].at[got]
                    )
                if rest:
                    following = rest[1:]
                    for choice in itertools.product((0, 1), repeat=len(following)):
                        values = dict(zip(following, choice))
                        got = sum(value << i for i, value in enumerate(choice))
                        values[rest[0]] = 1 - mine[axis, rest[0]]
                        copy = send(
                            state.total.at[slot_of(values)],
                            state.arrived[step].at[got],
                            (axis, rest[0]),
                        )
                        state.pending_next.append((copy, got))
                        started.append(copy)
                final = state.total.at[slot_of({})] if not rest else None
            else:
                axis, bits = lane.phases[1]
                done = step - sizes[0]
                rest = bits[done:]
                final = state.final
                for copy, _ in state.pending:
                    copy.wait_recv()
                state.pending_next = []
                for choice in itertools.product((0, 1), repeat=len(rest)):
                    values = dict(zip(rest, choice))
                    got = sum(value << i for i, value in enumerate(choice))
                    at = place(axis, {bit: values.get(bit, mine[axis, bit]) for bit in bits})
                    add_slab(final.at[at], state.arrived[step - 1].at[got])
                if not rest:
                    at = place(axis, {bit: mine[axis, bit] for bit in bits})
                    final = final.at[at]
            if final is not None and step >= sizes[0]:
                state.final = final
                if step == sum(sizes):
                    spot, copy = to_stage(number, final, *lane.target)
                    moved.append((lane.layer, copy))

                    @pl.when(core == lane.layer)
                    def _(spot=spot, final=final):
                        spot[...] = final[...]

                    @pl.when(core != lane.layer)
                    def _(copy=copy):
                        copy.start()
                elif step < sum(sizes):
                    axis, bits = lane.phases[1]
                    done = step - sizes[0]
                    bit, following = bits[done], bits[done + 1 :]
                    for choice in itertools.product((0, 1), repeat=len(following)):
                        values = dict(zip(following, choice))
                        got = sum(value << i for i, value in enumerate(choice))
                        at = place(
                            axis,
                            {
                                b: values.get(b, 1 - mine[axis, b] if b == bit else mine[axis, b])
                                for b in bits
                            },
                        )
                        copy = send(final.at[at], state.arrived[step].at[got], (axis, bit))
                        state.pending_next.append((copy, got))
                        started.append(copy)
            state.pending = state.pending_next
    for _ in summing:
        pass

    for copy, here in wholes:
        @pl.when(core == 1)
        def _(copy=copy, here=here):
            copy.wait_recv()
            here.wait()

        @pl.when(core == 0)
        def _(copy=copy):
            copy.wait_send()

    for layer, copy in moved:
        @pl.when(core == layer)
        def _(copy=copy):
            copy.wait_recv()

        @pl.when(core != layer)
        def _(copy=copy):
            copy.wait_send()

    for copy in started:
        copy.wait_send()


def sum_scatter(arrays, lanes, second_pre, second_down, stats, inner, collective):
    plans, scratch, shapes, copies, locals_ = [], [], [], 0, 0
    sizes = {}
    for source, prefix, phases, layer, target in lanes:
        shape = arrays[source].shape
        if isinstance(prefix, int):
            shape = shape[1:]
        else:
            if prefix[0]:
                shape = (shape[1], shape[0], *shape[2:])
            if prefix[1] is not None:
                shape = (*shape[:-1], prefix[1][1])
        buffers = [(shape[0] // 2, *shape[1:])]
        for step in range(1, len(phases[0][1]) + 1):
            buffers.append((shape[0] >> step, *shape[1:]))
            copies += shape[0] >> step
        locals_ += shape[0] // 2
        if len(phases) > 1:
            for step in range(1, len(phases[1][1]) + 1):
                buffers.append((shape[1] >> step, *shape[2:]))
                copies += shape[1] >> step
        plans.append(
            SimpleNamespace(
                source=source,
                prefix=prefix,
                phases=phases,
                buffers=buffers,
                rows=phases[0][0] == GROUP,
                layer=layer,
                target=target,
            )
        )
        width = sizes.get(target[0], (0, 0))[1] if len(target) > 2 else 0
        if layer == 0:
            sizes[target[0]] = (shape[-2], width + shape[-1])
        scratch += [pltpu.VMEM(buffer, jnp.bfloat16) for buffer in buffers]
    half = second_pre.shape[1] // (2 * inner)
    experts_shape = (2, half, second_pre.shape[0], inner)
    shapes = [
        jax.ShapeDtypeStruct(shape, jnp.bfloat16)
        for shape in (
            experts_shape,
            experts_shape,
            (2, half, *sizes[DOWN]),
            (2, *sizes[QKV]),
            (2, *sizes[OUT]),
            (2, *sizes[SMALL]),
        )
    ] + [jax.ShapeDtypeStruct(stats.shape, jnp.float32)]
    scratch += [
        pltpu.SemaphoreType.DMA((copies,)),
        pltpu.SemaphoreType.DMA((copies,)),
        pltpu.SemaphoreType.DMA((locals_,)),
    ]
    hops = lax.axis_size(GROUP) + 1
    scratch += [
        pltpu.VMEM((hops, *stats.shape), jnp.float32),
        pltpu.SemaphoreType.DMA((hops,)),
        pltpu.SemaphoreType.DMA((hops,)),
        pltpu.SemaphoreType.DMA((len(lanes) + 3 * half,)),
        pltpu.SemaphoreType.DMA((len(lanes) + 3 * half,)),
    ]
    return pl.pallas_call(
        functools.partial(sum_scatter_kernel, (plans, len(arrays), copies)),
        out_shape=shapes,
        in_specs=[pl.BlockSpec(memory_space=pl.ANY)] * (len(arrays) + 2)
        + [pl.BlockSpec(memory_space=pltpu.VMEM)],
        out_specs=[pl.BlockSpec(memory_space=pltpu.VMEM)] * len(shapes),
        scratch_shapes=scratch,
        compiler_params=pltpu.CompilerParams(
            collective_id=collective, has_side_effects=True, vmem_limit_bytes=60 * 2**20
        ),
    )(*arrays, second_pre, second_down, stats)


def bits_of(axis):
    return list(range(lax.axis_size(axis).bit_length() - 1))


def expert_lanes(first, inner):
    up, down = [(GROUP, bits_of(GROUP))], [(GROUP, bits_of(GROUP)[::-1])]
    return [
        (first, (False, ((2 * kind + j) * inner, inner)), (up, down)[kind], 0, (kind, j))
        for j in range(2)
        for kind in (GATE, UP)
    ]


def down_lanes(first, layer):
    up, down = [(GROUP, bits_of(GROUP))], [(GROUP, bits_of(GROUP)[::-1])]
    return [(first, 0, up, layer, (DOWN, 0)), (first, 1, down, layer, (DOWN, 1))]


def dense_lanes(first, width):
    up, down, deep = bits_of(GROUP), bits_of(GROUP)[::-1], bits_of(LINE)
    near = width // 4 // COLUMNS * COLUMNS
    away = width - near
    return [
        (
            first,
            (True, (0, away)),
            [(LINE, deep), (GROUP, up)],
            0,
            (QKV, slice(None), pl.ds(0, away)),
        ),
        (
            first,
            (False, (away, near)),
            [(GROUP, up), (LINE, deep)],
            0,
            (QKV, slice(None), pl.ds(away, near)),
        ),
        (first + 1, (False, None), [(GROUP, down), (LINE, deep)], 0, (OUT,)),
        small_lane(first + 2, 0),
    ]


def small_lane(first, layer):
    phases = [(GROUP, bits_of(GROUP)), (LINE, bits_of(LINE))]
    return (first, (False, None), phases, layer, (SMALL,))


def attention_forward(inputs, weights, segment_row):
    gain_attn, w_query, w_key, w_value, w_out, gain_moe = weights[:6]
    length = inputs.shape[0]
    cosine_table, sine_table = rotary_tables(length)
    inverse_one = lax.rsqrt(jnp.mean(inputs * inputs, axis=-1, keepdims=True) + EPSILON)
    normed_one = (inputs * inverse_one * gain_attn).astype(jnp.bfloat16)
    queries = rotate(
        matmul(normed_one, w_query).reshape(length, H, HD), cosine_table, sine_table
    ).astype(jnp.bfloat16)
    key_rows = rotate(
        matmul(normed_one, w_key).reshape(length, KVH, HD), cosine_table, sine_table
    ).astype(jnp.bfloat16)
    values = matmul(normed_one, w_value).astype(jnp.bfloat16).reshape(length, KVH, HD)
    scores = attention_scores(queries, key_rows, segment_row)
    highest = jnp.max(scores, axis=-1, keepdims=True)
    exponent = jnp.exp(scores - highest)
    denominator = jnp.sum(exponent, axis=-1, keepdims=True)
    weight = exponent / denominator
    attended = jnp.einsum(
        "kgqs,skd->qkgd", weight.astype(jnp.bfloat16), values, preferred_element_type=jnp.float32
    )
    attended = attended.reshape(length, H * HD).astype(jnp.bfloat16)
    hidden = inputs + matmul(attended, w_out)
    inverse_two = lax.rsqrt(jnp.mean(hidden * hidden, axis=-1, keepdims=True) + EPSILON)
    normed_two = (hidden * inverse_two * gain_moe).astype(jnp.bfloat16)
    state = (inverse_one, normed_one, queries, key_rows, values, weight, attended, hidden, inverse_two, normed_two)
    return state


MESH = pl.DeviceIdType.MESH
PARTS = 3


def move_rows(sources, held, pieces, sems, compute, z, n, others):
    row_send, row_recv, sum_send, sum_recv = sems
    barrier = pltpu.get_barrier_semaphore()
    for k in range(1, n):
        peer = lax.rem(z + k, n)
        pl.semaphore_signal(barrier, inc=1, device_id={LINE: peer}, device_id_type=MESH)
    for peer in others:
        pl.semaphore_signal(barrier, inc=1, device_id=peer, device_id_type=MESH)
    pl.semaphore_wait(barrier, n - 1 + len(others))

    def row_copy(kind, way, hop, source=None):
        step = 1 - 2 * way
        block = jnp.clip(z - step * hop, 0, n - 1)
        peer = jnp.clip(z + step, 0, n - 1)
        return pltpu.make_async_remote_copy(
            src_ref=held[kind].at[block] if source is None else source,
            dst_ref=held[kind].at[block],
            send_sem=row_send.at[kind, way, hop],
            recv_sem=row_recv.at[kind, way, hop],
            device_id={LINE: peer},
            device_id_type=MESH,
        )

    def sends(way, hop):
        step = 1 - 2 * way
        block, peer = z - step * hop, z + step
        return (block >= 0) & (block < n) & (peer >= 0) & (peer < n)

    def arrives(way, hop):
        block = z - (1 - 2 * way) * (hop + 1)
        return (block >= 0) & (block < n)

    def start(kind):
        for way in range(2):
            @pl.when(sends(way, 0))
            def _():
                row_copy(kind, way, 0, sources[kind]).start()

    def take(hop):
        for kind in range(len(held)):
            for way in range(2):
                @pl.when(arrives(way, hop))
                def _():
                    row_copy(kind, way, hop).wait_recv()

                @pl.when(sends(way, hop + 1) & (hop + 1 < n - 1))
                def _():
                    row_copy(kind, way, hop + 1).start()

    def waits(way, block):
        peer, last = z - (1 - 2 * way), (n - 1) * (1 - way)
        return (peer >= 0) & (peer < n) & ((block != last) | (peer != n - 1 - last))

    def far_copy(p):
        mine, arrived = pieces[p]
        block, way = n - 1 - z, jnp.where(z == 0, 1, 0)
        return pltpu.make_async_remote_copy(
            src_ref=mine(block),
            dst_ref=arrived(way, block),
            send_sem=sum_send.at[block, p],
            recv_sem=sum_recv.at[way, block, p],
            device_id={LINE: block},
            device_id_type=MESH,
        )

    def sum_copy(way, block, p):
        mine, arrived = pieces[p]
        return pltpu.make_async_remote_copy(
            src_ref=mine(block),
            dst_ref=arrived(way, block),
            send_sem=sum_send.at[block, p],
            recv_sem=sum_recv.at[way, block, p],
            device_id={LINE: jnp.clip(z + 1 - 2 * way, 0, n - 1)},
            device_id_type=MESH,
        )

    def sent(block, p):
        way = jnp.where(block > z, 0, 1)
        far = ((z == 0) | (z == n - 1)) & (block == n - 1 - z)

        @pl.when(far)
        def _():
            far_copy(p).start()

        @pl.when((block != z) & jnp.logical_not(far) & jnp.logical_not(waits(way, block)))
        def _():
            sum_copy(way, block, p).start()

    def between(block):
        if held:
            @pl.when(block == z)
            def _():
                take(0)

    def run():
        def both(hop):
            return (hop >= 0) & (z - 1 - hop >= 0) & (z + 1 + hop < n)

        def turn(k, carry):
            hop = lax.div(k + 1, 2) - 1
            block = z + (1 + hop) * (1 - 2 * lax.rem(k, 2))
            odd = lax.rem(k, 2) == 1

            @pl.when(odd & (hop > 0) & jnp.logical_not(both(hop - 1)))
            def _():
                take(hop)

            @pl.when(jnp.logical_not(odd) & both(hop) & (hop + 1 < n - 1))
            def _():
                take(hop + 1)

            @pl.when((block >= 0) & (block < n))
            def _():
                compute(block, sent, between)

            return carry

        def far_first(k, carry):
            block = z + (n - 1 - lax.div(k, 2)) * (1 - 2 * lax.rem(k, 2))

            @pl.when((block >= 0) & (block < n))
            def _():
                compute(block, sent, between)

            return carry

        if held:
            lax.fori_loop(0, 2 * n - 1, turn, 0)
        else:
            lax.fori_loop(0, 2 * n - 2, far_first, 0)

        first = jnp.where(2 * z < n, 0, 1)
        for way in (first, 1 - first):
            for k in range(1, n):
                block = z + (1 - 2 * way) * k

                @pl.when(waits(way, block) & (block >= 0) & (block < n))
                def _():
                    for p, (mine, arrived) in enumerate(pieces):
                        sum_copy(way, block, p).wait_recv()
                        own, other = mine(block), arrived(way, block)
                        own[...] = (
                            own[...].astype(jnp.float32) + other[...].astype(jnp.float32)
                        ).astype(jnp.bfloat16)
                        sum_copy(way, block, p).start()

        if not held:
            compute(z, sent, between)

    def collect(add):
        for way in range(2):
            for p, (_, arrived) in enumerate(pieces):
                sum_copy(way, z, p).wait_recv()
                add(p, arrived(way, z)[...].astype(jnp.float32))

    def finish():
        for kind in range(len(held)):
            for way in range(2):
                for hop in range(n - 1):
                    @pl.when(sends(way, hop))
                    def _():
                        row_copy(kind, way, hop).wait_send()
        for k in range(1, n):
            for p in range(len(pieces)):
                sum_copy(0, lax.rem(z + k, n), p).wait_send()

    return start, run, collect, finish


def row_pieces(sums, returned, parts):
    width = sums.shape[2] // parts

    def piece(p):
        at = pl.ds(p * width, width)
        return (
            lambda block: sums.at[block, :, at],
            lambda way, block: returned.at[way, block, :, at],
        )

    return [piece(p) for p in range(parts)]


def fetch_weights(layer, own, other, places, sem):
    count = places[0].shape[0]
    mine = lax.axis_index(CORE) == layer

    def copy(group, kind, e):
        return pltpu.make_async_copy(
            group[kind].at[e], places[kind].at[e], sem.at[kind * count + e]
        )

    for kind in range(len(places)):
        for e in range(count):
            @pl.when(mine)
            def _():
                copy(own, kind, e).start()

            @pl.when(jnp.logical_not(mine))
            def _():
                copy(other, kind, e).start()

    def wait():
        for kind in range(len(places)):
            for e in range(count):
                copy(own, kind, e).wait()

    return wait


def sigmoid_of(value):
    return 1.0 / (1.0 + jnp.exp(-value))


def column_of(block, column):
    here = lax.broadcasted_iota(jnp.int32, block.shape, 1) == column
    return jnp.sum(jnp.where(here, block, 0.0), axis=1, keepdims=True)


def experts_forward_kernel(
    layer, experts, x, mask, hidden, router, *refs
):
    own, other, refs = refs[:3], refs[3:6], refs[6:]
    own_dense, other_dense, refs = refs[:4], refs[4:8], refs[8:]
    out, rows, gates_all, gates, stats, gate_out, up_out, gated_out = refs[:8]
    placed, place_sem, keep_sem = refs[8:12], refs[-2], refs[-1]
    passing, (gate_keep, up_keep, gated) = refs[-9:-5], refs[-5:-2]
    refs = refs[:8] + refs[12:-9]
    w_gate, w_up, w_down, sums, returned, mixed, total, stats_all = refs[8:16]
    weight_sem, *sems = refs[16:]
    n, held = rows.shape[0], w_gate.shape[0]
    z = lax.axis_index(LINE)

    def keep_copies(block):
        pairs = (
            (gate_keep.at[:, block], gate_out.at[:, block]),
            (up_keep.at[:, block], up_out.at[:, block]),
            (gated.at[block], gated_out.at[block]),
        )
        return [
            pltpu.make_async_copy(source, target, keep_sem.at[i, block])
            for i, (source, target) in enumerate(pairs)
        ]

    def compute(block, sent, between):
        picked = rows[block]
        gate_block = gates_all[block].astype(jnp.float32)

        def one(e, carry):
            gate_pre = jnp.dot(picked, w_gate[e], preferred_element_type=jnp.float32)
            up_pre = jnp.dot(picked, w_up[e], preferred_element_type=jnp.float32)
            gate_keep[e, block] = gate_pre.astype(jnp.bfloat16)
            up_keep[e, block] = up_pre.astype(jnp.bfloat16)
            active = gate_pre * sigmoid_of(gate_pre) * up_pre
            share = (column_of(gate_block, z * held + e) * active).astype(jnp.bfloat16)
            inner = share.shape[1]
            gated[block, :, pl.ds(pl.multiple_of(e * inner, inner), inner)] = share
            mixed[e] = share
            return carry

        lax.fori_loop(0, held, one, 0)
        between(block)
        for copy in keep_copies(block):
            copy.start()
        width = out.shape[1] // PARTS
        for part in range(PARTS):
            at = pl.ds(part * width, width)
            result = jnp.zeros((out.shape[0], width), jnp.float32)
            for e in range(held):
                result += jnp.dot(mixed[e], w_down[e, :, at], preferred_element_type=jnp.float32)

            @pl.when(block == z)
            def _():
                total[:, at] = hidden[:, at] + result

            @pl.when(block != z)
            def _():
                sums[block, :, at] = result.astype(jnp.bfloat16)

            sent(block, part)

    own_gates = gates_all.at[z]
    start, run, collect, finish = move_rows(
        (x, own_gates, stats_all.at[z]),
        (rows, gates_all, stats_all),
        row_pieces(sums, returned, PARTS),
        sems,
        compute,
        z,
        n,
        [],
    )
    start(0)
    wait_weights = fetch_weights(layer, own, other, (w_gate, w_up, w_down), weight_sem)
    here = lax.axis_index(CORE) == 1 - layer

    def place_copy(group, i):
        return pltpu.make_async_copy(group[i], passing[i], place_sem.at[0, i])

    def place_out(i):
        return pltpu.make_async_copy(passing[i], placed[i], place_sem.at[1, i])

    logits = jnp.dot(x[...], router[...], preferred_element_type=jnp.float32)
    chosen = mask[...] > 0
    highest = jnp.max(jnp.where(chosen, logits, MASKED), axis=1, keepdims=True)
    exponent = jnp.where(chosen, jnp.exp(logits - highest), 0.0)
    gates[...] = exponent / jnp.sum(exponent, axis=1, keepdims=True)
    own_gates[...] = gates[...].astype(jnp.bfloat16)
    start(1)
    real = lax.broadcasted_iota(jnp.int32, logits.shape, 1) < experts
    highest = jnp.max(jnp.where(real, logits, MASKED), axis=1, keepdims=True)
    exponent = jnp.where(real, jnp.exp(logits - highest), 0.0)
    chance = exponent / jnp.sum(exponent, axis=1, keepdims=True)
    line = lax.broadcasted_iota(jnp.int32, stats.shape, 0)
    stats_all[z] = jnp.where(
        line == 0,
        jnp.sum(chance, axis=0, keepdims=True),
        jnp.where(line == 1, jnp.sum(mask[...], axis=0, keepdims=True), 0.0),
    )
    start(2)
    rows[z] = x[...]
    wait_weights()
    for i in range(4):
        @pl.when(here)
        def _():
            place_copy(own_dense, i).start()

        @pl.when(jnp.logical_not(here))
        def _():
            place_copy(other_dense, i).start()

    run()
    for i in range(4):
        place_copy(own_dense, i).wait()
        place_out(i).start()
    stats[...] = jnp.sum(stats_all[...], axis=0)
    width = out.shape[1] // PARTS

    def add(p, value):
        total[:, p * width : (p + 1) * width] += value

    collect(add)
    out[...] = total[...].astype(jnp.bfloat16)
    finish()
    for i in range(4):
        place_out(i).wait()
    for block in range(n):
        for copy in keep_copies(block):
            copy.wait()


def experts_backward_kernel(layer, grad, gates, *refs):
    own, other, saved_rows, saved_gated, refs = refs[:3], refs[3:6], refs[6], refs[7], refs[8:]
    kept, refs = refs[:2], refs[2:]
    keep_places, keep_sem, refs = refs[-3:-1], refs[-1], refs[:-3]
    gate_keep, up_keep = keep_places
    carried = layer == 0
    if carried:
        extra, refs = refs[0], refs[1:]
        extra_sum, refs = refs[6], refs[:6] + refs[7:]
        landed, extra_send, extra_recv = refs[-3:]
        refs = refs[:-3]
    out, out_gates, rows_both, gated_both, grad_both, pre_both = refs[:6]
    w_gate, w_up, w_down, sums, sum_gates, returned, returned_gates, away, dots = refs[6:15]
    weight_sem, core_send, core_recv, core_local, *sems = refs[15:]
    n, held = gates.shape[0], w_gate.shape[0]
    half, inner = held // 2, w_gate.shape[2]
    core = lax.axis_index(CORE)
    z = lax.axis_index(LINE)
    turned_dims = (((1,), (1,)), ((), ()))
    gathered = layer == 1
    rows = grad if gathered else grad_both.at[core]

    def to_core(number, source, target):
        return pltpu.make_async_remote_copy(
            src_ref=source,
            dst_ref=target,
            send_sem=core_send.at[number],
            recv_sem=core_recv.at[number],
            device_id={CORE: 1 - core},
            device_id_type=MESH,
        )

    def block_copies(block):
        away_copy = to_core(2 + n + block, away.at[block], pre_both.at[core, block])
        if gathered:
            return (away_copy,)
        return (to_core(2 + block, rows.at[block], rows.at[block]), away_copy)

    def columns(at):
        return pl.ds(pl.multiple_of(at * half * inner, half * inner), half * inner)

    def whole_copies():
        copies = (
            to_core(0, saved_rows, rows_both.at[core]),
            to_core(1, saved_gated.at[:, :, columns(1 - core)], gated_both.at[core]),
        )
        return copies + ((to_core(2, grad, grad_both.at[core]),) if gathered else ())

    def local_copies():
        copies = (
            pltpu.make_async_copy(saved_rows, rows_both.at[core], core_local.at[0]),
            pltpu.make_async_copy(
                saved_gated.at[:, :, columns(core)], gated_both.at[core], core_local.at[1]
            ),
        )
        if gathered:
            copies += (pltpu.make_async_copy(grad, grad_both.at[core], core_local.at[2]),)
        return copies

    me, count = lax.axis_index(GROUP), lax.axis_size(GROUP)
    peers = [lax.rem(me + k, count) for k in range(1, count)] if carried else []

    def extra_copy(k, peer, slot):
        return pltpu.make_async_remote_copy(
            src_ref=extra.at[:, peer],
            dst_ref=landed.at[slot],
            send_sem=extra_send.at[k],
            recv_sem=extra_recv.at[slot],
            device_id={GROUP: peer},
            device_id_type=MESH,
        )

    def compute(block, sent, between):
        picked = rows[block]
        gate_block = gates[block].astype(jnp.float32)
        dots[...] = jnp.zeros(dots.shape, jnp.float32)

        def one(e, place, j):
            raw = lax.dot_general(
                picked, w_down[e], turned_dims, preferred_element_type=jnp.float32
            )
            gate_pre = gate_keep[e, block].astype(jnp.float32)
            up_pre = up_keep[e, block].astype(jnp.float32)
            sigmoid = sigmoid_of(gate_pre)
            silu = gate_pre * sigmoid
            column = z * held + e
            dot = jnp.sum(raw * (silu * up_pre), axis=1, keepdims=True)
            here = lax.broadcasted_iota(jnp.int32, dots.shape, 1) == column
            dots[...] += jnp.where(here, dot, 0.0)
            active = column_of(gate_block, column) * raw
            place[:, pl.ds(pl.multiple_of(j * inner, inner), inner)] = (
                active * up_pre * sigmoid * (1.0 + gate_pre * (1.0 - sigmoid))
            ).astype(jnp.bfloat16)
            place[:, pl.ds(pl.multiple_of((half + j) * inner, inner), inner)] = (
                active * silu
            ).astype(jnp.bfloat16)

        def own_half(j, carry):
            one(core * half + j, pre_both.at[core, block], j)
            return carry

        def other_half(j, carry):
            one((1 - core) * half + j, away.at[block], j)
            return carry

        lax.fori_loop(0, half, other_half, 0)
        for copy in block_copies(block):
            copy.start()
        lax.fori_loop(0, half, own_half, 0)
        between(block)
        sum_gates[block] = dots[...].astype(jnp.bfloat16)

        @pl.when(block == z)
        def _():
            out_gates[...] = dots[...]

        sent(block, PARTS)
        width = out.shape[1] // PARTS
        for part in range(PARTS):
            at = pl.ds(part * width, width)
            result = jnp.zeros((out.shape[0], width), jnp.float32)
            for place, side in ((away.at[block], 1 - core), (pre_both.at[core, block], core)):
                for kind, right in enumerate((w_gate, w_up)):
                    for j in range(half):
                        left = place[:, pl.ds((kind * half + j) * inner, inner)]
                        result += lax.dot_general(
                            left,
                            right[side * half + j, at, :],
                            turned_dims,
                            preferred_element_type=jnp.float32,
                        )

            @pl.when(block == z)
            def _():
                out[:, at] = result

            @pl.when(block != z)
            def _():
                sums[block, :, at] = result.astype(jnp.bfloat16)

            sent(block, part)

    gate_piece = (lambda block: sum_gates.at[block], lambda way, block: returned_gates.at[way, block])
    start, run, collect, finish = move_rows(
        () if gathered else (grad,),
        () if gathered else (rows,),
        row_pieces(sums, returned, PARTS) + [gate_piece],
        sems,
        compute,
        z,
        n,
        [{CORE: 1 - core}] + [{GROUP: peer} for peer in peers],
    )
    if not gathered:
        start(0)
    for k, peer in enumerate(peers):
        extra_copy(k, peer, me).start()
    if carried:
        mine = pltpu.make_async_copy(extra.at[:, me], landed.at[me], extra_send.at[len(peers)])
        mine.start()
    wait_weights = fetch_weights(layer, own, other, (w_gate, w_up, w_down), weight_sem)
    keep_copies = [
        pltpu.make_async_copy(kept[i], keep_places[i], keep_sem.at[i]) for i in range(2)
    ]
    for copy in keep_copies:
        copy.start()
    for copy in whole_copies() + local_copies():
        copy.start()
    if not gathered:
        rows[z] = grad[...]
    for copy in keep_copies:
        copy.wait()
    wait_weights()
    run()
    width = out.shape[1] // PARTS

    def add(p, value):
        if p == PARTS:
            out_gates[...] += value
        else:
            out[:, p * width : (p + 1) * width] += value

    if carried:
        mine.wait()
        for k, peer in enumerate(peers):
            extra_copy(k, peer, peer).wait_recv()
        half, rows_each = extra_sum.shape[:2]
        step = 16 if rows_each % 16 == 0 else rows_each

        def add_up(i, carry):
            at = pl.ds(pl.multiple_of(i * step, step), step)
            for j in range(half):
                value = landed[0, j, at].astype(jnp.float32)
                for k in range(1, count):
                    value += landed[k, j, at].astype(jnp.float32)
                extra_sum[j, at] = value.astype(jnp.bfloat16)
            return carry

        lax.fori_loop(0, rows_each // step, add_up, 0)
    collect(add)
    finish()
    for k, peer in enumerate(peers):
        extra_copy(k, peer, me).wait_send()
    for copy in local_copies():
        copy.wait()
    for copy in whole_copies():
        copy.wait()
    for block in range(n):
        for copy in block_copies(block):
            copy.wait()


def exchange_scratch(n, kinds_out, kinds_back):
    return [
        pltpu.SemaphoreType.DMA((kinds_out, 2, n)),
        pltpu.SemaphoreType.DMA((kinds_out, 2, n)),
        pltpu.SemaphoreType.DMA((n, kinds_back)),
        pltpu.SemaphoreType.DMA((2, n, kinds_back)),
    ]


def expert_call(kernel, operands, own, other, extra, shapes, scratch, collective, loose=0):
    vmem, free = pl.BlockSpec(memory_space=pltpu.VMEM), pl.BlockSpec(memory_space=pl.ANY)
    weights = [pltpu.VMEM(array.shape, jnp.bfloat16) for array in own]
    return pl.pallas_call(
        kernel,
        out_shape=shapes,
        in_specs=[vmem] * len(operands) + [free] * (6 + len(extra)),
        out_specs=[vmem] * (len(shapes) - loose) + [free] * loose,
        scratch_shapes=weights + scratch,
        compiler_params=pltpu.CompilerParams(
            collective_id=collective, has_side_effects=True, vmem_limit_bytes=46 * 2**20
        ),
        cost_estimate=pl.CostEstimate(
            flops=5 * 10**10, bytes_accessed=10**8, transcendentals=0
        ),
    )(*operands, *own, *other, *extra)


def experts_forward(
    layer, normed_two, mask, hidden, router, own, other, own_dense, other_dense, experts
):
    n, held = lax.axis_size(LINE), own[0].shape[0]
    length, width = normed_two.shape
    inner = own[0].shape[2]
    low, full = jnp.bfloat16, jnp.float32
    kept = jax.ShapeDtypeStruct((held, n, length, inner), low)
    shapes = [
        jax.ShapeDtypeStruct((length, width), low),
        jax.ShapeDtypeStruct((n, length, width), low),
        jax.ShapeDtypeStruct((n, length, COLUMNS), low),
        jax.ShapeDtypeStruct((length, COLUMNS), full),
        jax.ShapeDtypeStruct((8, COLUMNS), full),
        kept,
        kept,
        jax.ShapeDtypeStruct((n, length, held * inner), low),
    ] + [jax.ShapeDtypeStruct(array.shape, low) for array in own_dense]
    scratch = [
        pltpu.VMEM((n, length, width), low),
        pltpu.VMEM((2, n, length, width), low),
        pltpu.VMEM((held, length, inner), low),
        pltpu.VMEM((length, width), full),
        pltpu.VMEM((n, 8, COLUMNS), full),
        pltpu.SemaphoreType.DMA((3 * held,)),
    ] + exchange_scratch(n, 3, PARTS)
    scratch += [pltpu.VMEM(array.shape, low) for array in own_dense]
    scratch += [pltpu.VMEM(shape.shape, low) for shape in shapes[5:8]]
    scratch.append(pltpu.SemaphoreType.DMA((2, 4)))
    scratch.append(pltpu.SemaphoreType.DMA((3, n)))
    kernel = functools.partial(experts_forward_kernel, layer, experts)
    return expert_call(
        kernel,
        (normed_two, mask, hidden, router),
        own,
        other,
        (*own_dense, *other_dense),
        shapes,
        scratch,
        1 + layer,
        7,
    )


def experts_backward(layer, grad_low, gates, gate_keep, up_keep, rows, gated, own, other, extra):
    held, n, length, inner = gate_keep.shape
    width = grad_low.shape[-1]
    low, full = jnp.bfloat16, jnp.float32
    shapes = [
        jax.ShapeDtypeStruct((length, width), full),
        jax.ShapeDtypeStruct((length, COLUMNS), full),
        jax.ShapeDtypeStruct((2, n, length, width), low),
        jax.ShapeDtypeStruct((2, n, length, held // 2 * inner), low),
        jax.ShapeDtypeStruct((2, n, length, width), low),
        jax.ShapeDtypeStruct((2, n, length, held * inner), low),
    ]
    scratch = [
        pltpu.VMEM((n, length, width), low),
        pltpu.VMEM((n, length, COLUMNS), low),
        pltpu.VMEM((2, n, length, width), low),
        pltpu.VMEM((2, n, length, COLUMNS), low),
        pltpu.VMEM((n, length, held * inner), low),
        pltpu.VMEM((length, COLUMNS), full),
        pltpu.SemaphoreType.DMA((3 * held,)),
        pltpu.SemaphoreType.DMA((2 + 2 * n,)),
        pltpu.SemaphoreType.DMA((2 + 2 * n,)),
        pltpu.SemaphoreType.DMA((3,)),
    ] + exchange_scratch(n, 1, PARTS + 1)
    if layer == 0:
        half, count, *block = extra.shape
        shapes.append(jax.ShapeDtypeStruct((half, *block), low))
        scratch += [
            pltpu.VMEM((count, half, *block), low),
            pltpu.SemaphoreType.DMA((count,)),
            pltpu.SemaphoreType.DMA((count,)),
        ]
    scratch += [pltpu.VMEM(gate_keep.shape, low)] * 2 + [pltpu.SemaphoreType.DMA((2,))]
    kernel = functools.partial(experts_backward_kernel, layer)
    return expert_call(
        kernel,
        (grad_low, gates),
        own,
        other,
        (rows, gated, gate_keep, up_keep) + (() if extra is None else (extra,)),
        shapes,
        scratch,
        3 + layer,
    )


def attention_backward(grad_hidden, inputs, state, weights):
    gain_attn, w_query, w_key, w_value, w_out, gain_moe = weights[:6]
    (inverse_one, normed_one, queries, key_rows, values, weight, attended, hidden, inverse_two, normed_two) = state
    length = inputs.shape[0]
    grad_branch = grad_hidden.astype(jnp.bfloat16)
    grad_attended = jnp.einsum("td,cd->tc", grad_branch, w_out, preferred_element_type=jnp.float32)
    grad_attended = grad_attended.astype(jnp.bfloat16).reshape(length, KVH, H // KVH, HD)
    grad_weight = jnp.einsum(
        "qkgd,skd->kgqs", grad_attended, values, preferred_element_type=jnp.float32
    )
    grad_values = jnp.einsum(
        "kgqs,qkgd->skd",
        weight.astype(jnp.bfloat16),
        grad_attended,
        preferred_element_type=jnp.float32,
    )
    grad_values = grad_values.astype(jnp.bfloat16).reshape(length, KVH * HD)
    grad_scores = (
        weight * (grad_weight - jnp.sum(weight * grad_weight, axis=-1, keepdims=True))
    ).astype(jnp.bfloat16)
    score_scale = HD ** (-0.5)
    grouped = queries.reshape(length, KVH, H // KVH, HD)
    grad_queries = jnp.einsum(
        "kgqs,skd->qkgd", grad_scores, key_rows, preferred_element_type=jnp.float32
    )
    grad_queries = grad_queries.reshape(length, H, HD) * score_scale
    grad_keys = (
        jnp.einsum("kgqs,qkgd->skd", grad_scores, grouped, preferred_element_type=jnp.float32)
        * score_scale
    )
    cosine_table, sine_table = rotary_tables(length)
    grad_query_pre = (
        unrotate(grad_queries, cosine_table, sine_table)
        .reshape(length, H * HD)
        .astype(jnp.bfloat16)
    )
    grad_key_pre = (
        unrotate(grad_keys, cosine_table, sine_table).reshape(length, KVH * HD).astype(jnp.bfloat16)
    )
    grad_normed_one = (
        jnp.einsum("tq,cq->tc", grad_query_pre, w_query, preferred_element_type=jnp.float32)
        + jnp.einsum("tq,cq->tc", grad_key_pre, w_key, preferred_element_type=jnp.float32)
        + jnp.einsum("tq,cq->tc", grad_values, w_value, preferred_element_type=jnp.float32)
    )
    grad_norm_one, grad_gain_attn = norm_back(grad_normed_one, inputs, inverse_one, gain_attn)
    grad_inputs = grad_hidden + grad_norm_one
    grad_qkv = jnp.concatenate([grad_query_pre, grad_key_pre, grad_values], axis=1)
    return grad_inputs, grad_gain_attn, grad_qkv, grad_branch


def turned(left, right):
    return jnp.einsum("tc,tq->cq", left, right, preferred_element_type=jnp.float32)


def body(tokens, cotangent, segments, routes, *weight_arrays):
    core = lax.axis_index(CORE)
    first = core == 0
    experts = weight_arrays[6].shape[2]
    w_gate = weight_arrays[7]
    held = w_gate.shape[1]
    own = [array[0] for array in weight_arrays]
    other = [swapped(array) for array in own]
    weights = [
        [jnp.where(first, a, b) for a, b in zip(own[:7], other[:7])],
        [jnp.where(first, b, a) for a, b in zip(own[:7], other[:7])],
    ]
    inputs_low = lax.dynamic_slice_in_dim(tokens, core * SEQ, SEQ, 0)
    grad_low = lax.dynamic_slice_in_dim(cotangent, core * SEQ, SEQ, 0)
    cotangent_all = lax.all_gather(grad_low, LINE, axis=0)
    segment_row = lax.dynamic_index_in_dim(segments, core, 0, keepdims=False)
    mine = lax.dynamic_slice_in_dim(routes[0], core * SEQ, SEQ, 0)
    got = swapped(lax.dynamic_slice_in_dim(routes[0], (1 - core) * SEQ, SEQ, 0))
    routes_here = jnp.stack([jnp.where(first, mine, got), jnp.where(first, got, mine)])
    masks = multi_hot(routes_here, COLUMNS)
    own_experts, other_experts = own[7:], other[7:]

    saved, outs, stats = [], [], []
    for s in range(2):
        inputs = inputs_low.astype(jnp.float32)
        state = attention_forward(inputs, weights[s], segment_row)
        hidden, normed_two = state[7], state[9]
        if s == 0:
            normed_two, cotangent_all = lax.optimization_barrier((normed_two, cotangent_all))
        both_cores = [jnp.concatenate([a, swapped(a)]) for a in (state[1], state[6])]
        router = jnp.pad(weights[s][6], ((0, 0), (0, COLUMNS - experts)))
        inputs_low, rows, gates_all, gates, stat, *kept, query, key, value, out = experts_forward(
            s,
            normed_two,
            masks[s],
            hidden,
            router,
            own_experts,
            other_experts,
            own[1:5],
            other[1:5],
            experts,
        )
        weights[1 - s][1:5] = [query, key, value, out]
        outs.append(inputs_low)
        stats.append(stat)
        expert_state = (rows, gates_all, gates, *kept)
        saved.append((inputs, state, expert_state, both_cores))

    dp, deep = lax.axis_size(GROUP), lax.axis_size(LINE)
    grads = [None, None]
    input_grads = [None, None]
    for s in (1, 0):
        inputs, state, expert_state, both_cores = saved[s]
        (inverse_one, normed_one, _, _, _, _, attended, hidden, inverse_two, normed_two) = state
        rows_all, gates_all, gates, gate_keep, up_keep, gated = expert_state
        gain_moe, w_router = weights[s][5], weights[s][6]
        grad_sum, grad_gates, rows_both, gated_both, grad_both, pre_both, *sums = experts_backward(
            s,
            cotangent_all if s == 1 else grad_low,
            gates_all,
            gate_keep,
            up_keep,
            rows_all,
            gated,
            own_experts,
            other_experts,
            None if s == 1 else grads[1][1].reshape(held // 2, dp, -1, D),
        )
        if s == 0:
            (second_down,) = sums
        inner = w_gate.shape[3]
        grad_gate_up = turned(
            rows_both.reshape(-1, D), pre_both.reshape(-1, held * inner)
        ).astype(jnp.bfloat16)
        if s == 1:
            grad_sum, grad_gate_up = lax.optimization_barrier((grad_sum, grad_gate_up))
            second_pre = lax.psum_scatter(grad_gate_up, GROUP, scatter_dimension=0, tiled=True)
        else:
            grad_sum, second_pre = lax.optimization_barrier((grad_sum, second_pre))
        gates, grad_gates = gates[:, :experts], grad_gates[:, :experts]
        grad_chosen = gates * (grad_gates - jnp.sum(gates * grad_gates, axis=-1, keepdims=True))
        grad_logits = grad_chosen.astype(jnp.bfloat16)
        grad_normed_two = grad_sum + jnp.einsum(
            "te,de->td", grad_logits, w_router, preferred_element_type=jnp.float32
        )
        grad_norm_two, grad_gain_moe = norm_back(grad_normed_two, hidden, inverse_two, gain_moe)
        grad_hidden = grad_low.astype(jnp.float32) + grad_norm_two
        grad_inputs, grad_gain_attn, grad_qkv, grad_branch = attention_backward(
            grad_hidden, inputs, state, weights[s]
        )
        if s == 1:
            grad_inputs, gated_both = lax.optimization_barrier((grad_inputs, gated_both))
        grad_down = turned(
            gated_both.reshape(-1, held // 2 * inner), grad_both.reshape(-1, D)
        ).astype(jnp.bfloat16)

        def halves(array):
            width = array.shape[1] // 2
            return (
                lax.dynamic_slice_in_dim(array, core * width, width, 1),
                lax.dynamic_slice_in_dim(array, (1 - core) * width, width, 1),
            )
        qkv_keep, qkv_send = halves(grad_qkv)
        branch_keep, branch_send = halves(grad_branch)
        grad_w_qkv = turned(
            both_cores[0], jnp.concatenate([qkv_keep, swapped(qkv_send)])
        ).astype(jnp.bfloat16)
        grad_w_out = turned(
            both_cores[1], jnp.concatenate([branch_keep, swapped(branch_send)])
        ).astype(jnp.bfloat16)
        grad_w_router = turned(normed_two, grad_logits)
        small = jnp.concatenate(
            [grad_gain_attn[:, None], grad_gain_moe[:, None], grad_w_router], axis=1
        ).astype(jnp.bfloat16)
        small = jnp.pad(small, ((0, 0), (0, COLUMNS - small.shape[1])))
        if s == 1:
            grad_inputs, grad_down, grad_w_qkv, grad_w_out = lax.optimization_barrier(
                (grad_inputs, grad_down, grad_w_qkv, grad_w_out)
            )
            dense = jnp.concatenate([grad_w_qkv, grad_w_out], axis=1)
            second_dense = lax.psum_scatter(dense, GROUP, scatter_dimension=0, tiled=True)
        grads[s] = (grad_gate_up, grad_down, grad_w_qkv, grad_w_out, small)
        input_grads[s] = grad_inputs
        grad_low = grad_inputs.astype(jnp.bfloat16)

    dp, deep = lax.axis_size(GROUP), lax.axis_size(LINE)
    half, inner = held // 2, w_gate.shape[3]
    grad_gate_up, grad_down, grad_w_qkv, grad_w_out, small = grads[0]
    arrays = [
        grad_gate_up.reshape(dp, D // dp, held * inner),
        grad_down.reshape(half, dp, inner // dp, D),
    ]
    lanes = dense_lanes(2, grad_w_qkv.shape[1])
    for array in (grad_w_qkv, grad_w_out, small):
        arrays.append(array.reshape(dp, deep, array.shape[0] // (dp * deep), array.shape[1]))
    width = grad_w_qkv.shape[1]
    whole = second_dense.shape[1]
    for columns, kind in (((0, width), QKV), ((width, whole - width), OUT)):
        start, size = columns
        target = (kind, slice(None), pl.ds(start - (start // width) * width, size))
        lanes.append((len(arrays), (False, columns), [(LINE, bits_of(LINE))], 1, target))
    arrays.append(second_dense.reshape(deep, second_dense.shape[0] // deep, whole))
    lanes.append(small_lane(len(arrays), 1))
    lanes += expert_lanes(0, inner) + down_lanes(1, 0)
    small = grads[1][4]
    arrays.append(small.reshape(dp, deep, small.shape[0] // (dp * deep), small.shape[1]))
    out_keep = jnp.where(first, outs[0], outs[1])
    out_got = swapped(jnp.where(first, outs[1], outs[0]))
    layer_out = jnp.where(
        first, jnp.concatenate([out_keep, out_got]), jnp.concatenate([out_got, out_keep])
    )
    low_one = input_grads[1].astype(jnp.bfloat16).astype(jnp.float32)
    grad_keep = jnp.where(first, input_grads[0], low_one)
    grad_got = swapped(jnp.where(first, low_one, input_grads[0]))
    input_grad = jnp.where(
        first, jnp.concatenate([grad_keep, grad_got]), jnp.concatenate([grad_got, grad_keep])
    )
    stats = jnp.concatenate(stats, axis=0)
    stats, layer_out, input_grad = lax.optimization_barrier((stats, layer_out, input_grad))
    *grads, qkv, out, small, stats = sum_scatter(
        arrays, lanes, second_pre, second_down, stats, inner, 0
    )
    full = jnp.float32
    w_gate_grad, w_up_grad, w_down_grad = (
        grad.reshape(held, *grad.shape[2:]).astype(full) for grad in grads
    )
    qkv = jnp.concatenate([qkv[0], qkv[1]], axis=1).astype(full)
    grad_w_out = jnp.concatenate([out[0], out[1]], axis=1).astype(full)
    small = small[0].astype(full) + small[1].astype(full)
    heads, kv = H * HD, KVH * HD
    stats = lax.dynamic_index_in_dim(stats.reshape(2, 8, COLUMNS), core, 0)
    token_total = SEQ * lax.axis_size((CORE, GROUP, LINE))
    counts, chances = stats[:, 1, :experts], stats[:, 0, :experts]
    balance = experts * (counts / (token_total * TOPK) * chances / token_total)
    results = (
        layer_out,
        input_grad,
        small[:, 0],
        qkv[:, :heads],
        qkv[:, heads : heads + kv],
        qkv[:, heads + kv :],
        grad_w_out,
        small[:, 1],
        small[:, 2 : 2 + experts],
        w_gate_grad,
        w_up_grad,
        w_down_grad,
    )
    return tuple(result[None] for result in results) + (balance,)


def solution(mesh):
    return jax.shard_map(
        body,
        mesh=mesh,
        in_specs=(
            P((GROUP, LINE), None),
            P((GROUP, LINE), None),
            P((GROUP, LINE), None),
            P(CORE, (GROUP, LINE), None),
            P(CORE, None),
            P(CORE, None, None),
            P(CORE, None, None),
            P(CORE, None, None),
            P(CORE, None, None),
            P(CORE, None),
            P(CORE, None, None),
            P(CORE, LINE, None, None),
            P(CORE, LINE, None, None),
            P(CORE, LINE, None, None),
        ),
        out_specs=(
            P(CORE, (GROUP, LINE), None),
            P(CORE, (GROUP, LINE), None),
            P(CORE, (GROUP, LINE)),
            P(CORE, (GROUP, LINE), None),
            P(CORE, (GROUP, LINE), None),
            P(CORE, (GROUP, LINE), None),
            P(CORE, (GROUP, LINE), None),
            P(CORE, (GROUP, LINE)),
            P(CORE, (GROUP, LINE), None),
            P(CORE, LINE, GROUP, None),
            P(CORE, LINE, GROUP, None),
            P(CORE, LINE, GROUP, None),
            P(CORE, None),
        ),
        check_vma=False,
    )
```

```python
import functools
import itertools
from types import SimpleNamespace

import jax
import jax.numpy as jnp
from jax import lax
from jax.experimental import pallas as pl
from jax.experimental.pallas import tpu as pltpu
from jax.sharding import PartitionSpec as P

D = 1536
H = 24
KVH = 8
HD = 64
TOPK = 8
SEQ = 96


EPSILON = 1e-05
THETA = 10000.0
MASKED = -1e30
COLUMNS = 128
GATE, UP, DOWN, QKV, OUT, SMALL = range(6)
CORE, GROUP, LINE = "section", "dp", "expert"
INNER = "inner"


def matmul(left_side, right_side):
    return jnp.dot(left_side, right_side, preferred_element_type=jnp.float32)


def rotary_tables(length):
    half_width = HD // 2
    position = jnp.arange(length, dtype=jnp.float32)[:, None]
    freq_rate = THETA ** (-jnp.arange(half_width, dtype=jnp.float32) / half_width)
    angles = position * freq_rate[None, :]
    return (jnp.cos(angles)[:, None, :], jnp.sin(angles)[:, None, :])


def rotate(tensor, cosine_table, sine_table):
    half_width = HD // 2
    first_half = tensor[..., :half_width]
    second_half = tensor[..., half_width:]
    return jnp.concatenate(
        [
            first_half * cosine_table - second_half * sine_table,
            second_half * cosine_table + first_half * sine_table,
        ],
        axis=-1,
    )


def unrotate(gradient, cosine_table, sine_table):
    half_width = HD // 2
    first_half = gradient[..., :half_width]
    second_half = gradient[..., half_width:]
    return jnp.concatenate(
        [
            first_half * cosine_table + second_half * sine_table,
            second_half * cosine_table - first_half * sine_table,
        ],
        axis=-1,
    )


def norm_back(grad_normed, tensor, inverse, gain_vector):
    scaled = grad_normed * gain_vector
    grad_gain = jnp.sum(grad_normed * tensor * inverse, axis=0)
    grad_tensor = inverse * scaled - tensor * inverse**3 * jnp.mean(
        scaled * tensor, axis=-1, keepdims=True
    )
    return (grad_tensor, grad_gain)


def attention_scores(queries, key_rows, segment_row):
    length = queries.shape[0]
    grouped = queries.reshape(length, KVH, H // KVH, HD)
    scores = jnp.einsum(
        "qkgd,skd->kgqs", grouped, key_rows, preferred_element_type=jnp.float32
    ) * HD ** (-0.5)
    position = jnp.arange(length)
    allowed = (position[None, :] <= position[:, None]) & (
        segment_row[:, None] == segment_row[None, :]
    )
    return jnp.where(allowed[None, None], scores, MASKED)


def multi_hot(route_rows, experts):
    columns = jnp.arange(experts, dtype=jnp.int32)
    return jnp.sum(
        (route_rows[..., None] == columns).astype(jnp.float32), axis=-2
    )


def swapped(array):
    return lax.ppermute(array, CORE, [(0, 1), (1, 0)])


def add_slab(total, arrived):
    *lead, rows, _ = total.shape
    step = 16 if rows % 16 == 0 else rows
    for where in itertools.product(*(range(n) for n in lead)):

        def add(i, carry):
            at = (*where, pl.ds(pl.multiple_of(i * step, step), step), slice(None))
            both = total[at].astype(jnp.float32) + arrived[at].astype(jnp.float32)
            total[at] = both.astype(jnp.bfloat16)
            return carry

        lax.fori_loop(0, rows // step, add, 0)


def sum_scatter_kernel(plan, *refs):
    lanes, ins, copies = plan
    sources = refs[:ins]
    second_pre, stats_in = refs[ins : ins + 2]
    stage, stats = refs[ins + 2 : ins + 8], refs[ins + 8]
    scratch = list(refs[ins + 9 :])
    send_sem, recv_sem, local_sem, stats_got, stats_send, stats_recv, core_send, core_recv = (
        scratch[-8:]
    )
    core = lax.axis_index(CORE)
    partners = []
    for lane in lanes:
        for axis, bits in lane.phases:
            partners += [(axis, bit) for bit in bits if (axis, bit) not in partners]
    partners.append((CORE, 0))
    index = {axis: lax.axis_index(axis) for axis, _ in partners}
    mine = {(axis, bit): (index[axis] >> bit) & 1 for axis, bit in partners}
    far = {key: index[key[0]] + (1 - 2 * mine[key]) * (1 << key[1]) for key in partners}
    barrier = pltpu.get_barrier_semaphore()
    peers = [{axis: far[axis, bit]} for axis, bit in partners if axis != GROUP]
    groups = lax.axis_size(GROUP)
    peers += [{GROUP: lax.rem(lax.axis_index(GROUP) + k, groups)} for k in range(1, groups)]
    for peer in peers:
        pl.semaphore_signal(
            barrier, inc=1, device_id=peer, device_id_type=pl.DeviceIdType.MESH
        )
    pl.semaphore_wait(barrier, len(peers))

    counter = itertools.count()

    def send(source, target, key):
        number = next(counter)
        copy = pltpu.make_async_remote_copy(
            src_ref=source,
            dst_ref=target,
            send_sem=send_sem.at[number],
            recv_sem=recv_sem.at[number],
            device_id={key[0]: far[key]},
            device_id_type=pl.DeviceIdType.MESH,
        )
        copy.start()
        return copy

    def place(axis, values):
        total = 0
        for bit, value in values.items():
            total = total + value * (1 << bit)
        return total

    def sum_stats():
        count = lax.axis_size(GROUP)
        me = lax.axis_index(GROUP)

        def copy(at, source, slot, target):
            return pltpu.make_async_remote_copy(
                src_ref=source,
                dst_ref=stats_got.at[slot],
                send_sem=stats_send.at[at],
                recv_sem=stats_recv.at[slot],
                device_id=target,
                device_id_type=pl.DeviceIdType.MESH,
            )

        for k in range(1, count):
            copy(k, stats_in, me, {GROUP: lax.rem(me + k, count)}).start()
        yield
        stats[...] = stats_in[...]
        for k in range(1, count):
            peer = lax.rem(me + k, count)
            copy(k, stats_in, peer, {GROUP: peer}).wait_recv()
            stats[...] += stats_got[peer]
        both = copy(0, stats, count, {CORE: far[CORE, 0]})
        both.start()
        yield
        both.wait()
        stats[...] += stats_got[count]
        for k in range(1, count):
            copy(k, stats_in, me, {GROUP: lax.rem(me + k, count)}).wait_send()

    summing = sum_stats()
    next(summing)

    def to_stage(number, source, kind, *at):
        spot = stage[kind].at[(core, *at)]
        return spot, pltpu.make_async_remote_copy(
            src_ref=source,
            dst_ref=spot,
            send_sem=core_send.at[number],
            recv_sem=core_recv.at[number],
            device_id={CORE: 1 - core},
            device_id_type=pl.DeviceIdType.MESH,
        )

    inner = stage[GATE].shape[3]
    wholes = []
    half = stage[GATE].shape[1]
    for number in range(2 * half):
        kind, j = divmod(number, half)
        source = second_pre.at[:, pl.ds(number * inner, inner)]
        spot, copy = to_stage(len(lanes) + number, source, kind, j)
        wholes.append((copy, pltpu.make_async_copy(source, spot, core_send.at[len(lanes) + number])))
    for copy, here in wholes:
        @pl.when(core == 1)
        def _(here=here):
            here.start()

        @pl.when(core == 0)
        def _(copy=copy):
            copy.start()

    moved = []
    started = []
    states = []
    for number, lane in enumerate(lanes):
        count = len(lane.buffers)
        buffers, scratch = scratch[:count], scratch[count:]
        source = sources[lane.source]
        prefix = lane.prefix
        if isinstance(prefix, int):
            source = source.at[prefix]

        def part(at, source=source, prefix=prefix):
            if isinstance(prefix, int):
                return source.at[at]
            inner, columns = prefix
            where = (slice(None), at) if inner else (at,)
            if columns is not None:
                where += (slice(None),) * (len(source.shape) - len(where) - 1) + (pl.ds(*columns),)
            return source.at[where]

        axis, bits = lane.phases[0]
        total, arrived = buffers[0], buffers[1:]
        rest = [bit for bit in bits[1:]]
        pending = []
        for choice in itertools.product((0, 1), repeat=len(rest)):
            values = dict(zip(rest, choice))
            slot = sum(value << i for i, value in enumerate(choice))
            far_at = place(axis, {**values, bits[0]: 1 - mine[axis, bits[0]]})
            here_at = place(axis, {**values, bits[0]: mine[axis, bits[0]]})
            copy = send(part(far_at), arrived[0].at[slot], (axis, bits[0]))
            pending.append((copy, slot))
            started.append(copy)
            states.append((number, part(here_at), slot, total))
        lane_state = SimpleNamespace(total=total, arrived=arrived, pending=pending)
        lane.state = lane_state
    locals_ = {}
    for at, (number, here, slot, total) in enumerate(states):
        copy = pltpu.make_async_copy(here, total.at[slot], local_sem.at[at])
        copy.start()
        locals_[number, slot] = copy
    short = [item for item in enumerate(lanes) if len(item[1].phases) == 1 and item[1].rows]
    long = [item for item in enumerate(lanes) if item not in short]
    turns = [(1, long), (1, short)]
    count = max(sum(len(bits) for _, bits in lane.phases) for lane in lanes)
    for step in range(2, count + 1):
        turns += [(2 * step - 2, long), (2 * step - 1, long), (step, short)]
    for at, (step, group) in enumerate(turns):
        if at == 2:
            next(summing)
        for number, lane in group:
            state = lane.state
            sizes = [len(bits) for _, bits in lane.phases]
            if step > sum(sizes):
                continue
            if step <= sizes[0]:
                axis, bits = lane.phases[0]
                resolved, rest = bits[:step], bits[step:]

                def slot_of(values):
                    found = 0
                    for i, bit in enumerate(bits[1:]):
                        found = found + values.get(bit, mine[axis, bit]) * (1 << i)
                    return found

                for copy, slot in state.pending:
                    copy.wait_recv()
                    if step == 1:
                        locals_[number, slot].wait()
                state.pending_next = []
                for choice in itertools.product((0, 1), repeat=len(rest)):
                    values = dict(zip(rest, choice))
                    got = sum(value << i for i, value in enumerate(choice))
                    add_slab(
                        state.total.at[slot_of(values)], state.arrived[step - 1].at[got]
                    )
                if rest:
                    following = rest[1:]
                    for choice in itertools.product((0, 1), repeat=len(following)):
                        values = dict(zip(following, choice))
                        got = sum(value << i for i, value in enumerate(choice))
                        values[rest[0]] = 1 - mine[axis, rest[0]]
                        copy = send(
                            state.total.at[slot_of(values)],
                            state.arrived[step].at[got],
                            (axis, rest[0]),
                        )
                        state.pending_next.append((copy, got))
                        started.append(copy)
                final = state.total.at[slot_of({})] if not rest else None
            else:
                axis, bits = lane.phases[1]
                done = step - sizes[0]
                rest = bits[done:]
                final = state.final
                for copy, _ in state.pending:
                    copy.wait_recv()
                state.pending_next = []
                for choice in itertools.product((0, 1), repeat=len(rest)):
                    values = dict(zip(rest, choice))
                    got = sum(value << i for i, value in enumerate(choice))
                    at = place(axis, {bit: values.get(bit, mine[axis, bit]) for bit in bits})
                    add_slab(final.at[at], state.arrived[step - 1].at[got])
                if not rest:
                    at = place(axis, {bit: mine[axis, bit] for bit in bits})
                    final = final.at[at]
            if final is not None and step >= sizes[0]:
                state.final = final
                if step == sum(sizes):
                    spot, copy = to_stage(number, final, *lane.target)
                    moved.append((lane.layer, copy))

                    @pl.when(core == lane.layer)
                    def _(spot=spot, final=final):
                        spot[...] = final[...]

                    @pl.when(core != lane.layer)
                    def _(copy=copy):
                        copy.start()
                elif step < sum(sizes):
                    axis, bits = lane.phases[1]
                    done = step - sizes[0]
                    bit, following = bits[done], bits[done + 1 :]
                    for choice in itertools.product((0, 1), repeat=len(following)):
                        values = dict(zip(following, choice))
                        got = sum(value << i for i, value in enumerate(choice))
                        at = place(
                            axis,
                            {
                                b: values.get(b, 1 - mine[axis, b] if b == bit else mine[axis, b])
                                for b in bits
                            },
                        )
                        copy = send(final.at[at], state.arrived[step].at[got], (axis, bit))
                        state.pending_next.append((copy, got))
                        started.append(copy)
            state.pending = state.pending_next
    for _ in summing:
        pass

    for copy, here in wholes:
        @pl.when(core == 1)
        def _(copy=copy, here=here):
            copy.wait_recv()
            here.wait()

        @pl.when(core == 0)
        def _(copy=copy):
            copy.wait_send()

    for layer, copy in moved:
        @pl.when(core == layer)
        def _(copy=copy):
            copy.wait_recv()

        @pl.when(core != layer)
        def _(copy=copy):
            copy.wait_send()

    for copy in started:
        copy.wait_send()


def sum_scatter(arrays, lanes, second_pre, stats, inner, collective):
    plans, scratch, shapes, copies, locals_ = [], [], [], 0, 0
    sizes = {}
    for source, prefix, phases, layer, target in lanes:
        shape = arrays[source].shape
        if isinstance(prefix, int):
            shape = shape[1:]
        else:
            if prefix[0]:
                shape = (shape[1], shape[0], *shape[2:])
            if prefix[1] is not None:
                shape = (*shape[:-1], prefix[1][1])
        buffers = [(shape[0] // 2, *shape[1:])]
        for step in range(1, len(phases[0][1]) + 1):
            buffers.append((shape[0] >> step, *shape[1:]))
            copies += shape[0] >> step
        locals_ += shape[0] // 2
        if len(phases) > 1:
            for step in range(1, len(phases[1][1]) + 1):
                buffers.append((shape[1] >> step, *shape[2:]))
                copies += shape[1] >> step
        plans.append(
            SimpleNamespace(
                source=source,
                prefix=prefix,
                phases=phases,
                buffers=buffers,
                rows=phases[0][0] == GROUP,
                layer=layer,
                target=target,
            )
        )
        width = sizes.get(target[0], (0, 0))[1] if len(target) > 2 else 0
        if layer == 0:
            sizes[target[0]] = (shape[-2], width + shape[-1])
        scratch += [pltpu.VMEM(buffer, jnp.bfloat16) for buffer in buffers]
    half = second_pre.shape[1] // (2 * inner)
    experts_shape = (2, half, second_pre.shape[0], inner)
    shapes = [
        jax.ShapeDtypeStruct(shape, jnp.bfloat16)
        for shape in (
            experts_shape,
            experts_shape,
            (2, half, *sizes[DOWN]),
            (2, *sizes[QKV]),
            (2, *sizes[OUT]),
            (2, *sizes[SMALL]),
        )
    ] + [jax.ShapeDtypeStruct(stats.shape, jnp.float32)]
    scratch += [
        pltpu.SemaphoreType.DMA((copies,)),
        pltpu.SemaphoreType.DMA((copies,)),
        pltpu.SemaphoreType.DMA((locals_,)),
    ]
    hops = lax.axis_size(GROUP) + 1
    scratch += [
        pltpu.VMEM((hops, *stats.shape), jnp.float32),
        pltpu.SemaphoreType.DMA((hops,)),
        pltpu.SemaphoreType.DMA((hops,)),
        pltpu.SemaphoreType.DMA((len(lanes) + 2 * half,)),
        pltpu.SemaphoreType.DMA((len(lanes) + 2 * half,)),
    ]
    return pl.pallas_call(
        functools.partial(sum_scatter_kernel, (plans, len(arrays), copies)),
        out_shape=shapes,
        in_specs=[pl.BlockSpec(memory_space=pl.ANY)] * (len(arrays) + 1)
        + [pl.BlockSpec(memory_space=pltpu.VMEM)],
        out_specs=[pl.BlockSpec(memory_space=pltpu.VMEM)] * len(shapes),
        scratch_shapes=scratch,
        compiler_params=pltpu.CompilerParams(
            collective_id=collective, has_side_effects=True, vmem_limit_bytes=60 * 2**20
        ),
    )(*arrays, second_pre, stats)


def bits_of(axis):
    return list(range(lax.axis_size(axis).bit_length() - 1))


def expert_lanes(first, inner):
    up, down = [(GROUP, bits_of(GROUP))], [(GROUP, bits_of(GROUP)[::-1])]
    return [
        (first, (False, ((2 * kind + j) * inner, inner)), (up, down)[kind], 0, (kind, j))
        for j in range(2)
        for kind in (GATE, UP)
    ]


def down_lanes(first, layer):
    up, down = [(GROUP, bits_of(GROUP))], [(GROUP, bits_of(GROUP)[::-1])]
    return [(first, 0, up, layer, (DOWN, 0)), (first, 1, down, layer, (DOWN, 1))]


def dense_lanes(first, width):
    up, down, deep = bits_of(GROUP), bits_of(GROUP)[::-1], bits_of(LINE)
    near = width // 8 // COLUMNS * COLUMNS
    away = width - near
    return [
        (
            first,
            (True, (0, away)),
            [(LINE, deep), (GROUP, up)],
            0,
            (QKV, slice(None), pl.ds(0, away)),
        ),
        (
            first,
            (False, (away, near)),
            [(GROUP, up), (LINE, deep)],
            0,
            (QKV, slice(None), pl.ds(away, near)),
        ),
        (first + 1, (False, None), [(GROUP, down), (LINE, deep)], 0, (OUT,)),
        small_lane(first + 2, 0),
    ]


def small_lane(first, layer):
    phases = [(GROUP, bits_of(GROUP)), (LINE, bits_of(LINE))]
    return (first, (False, None), phases, layer, (SMALL,))


def attention_forward(inputs, weights, segment_row):
    gain_attn, w_query, w_key, w_value, w_out, gain_moe = weights[:6]
    length = inputs.shape[0]
    cosine_table, sine_table = rotary_tables(length)
    inverse_one = lax.rsqrt(jnp.mean(inputs * inputs, axis=-1, keepdims=True) + EPSILON)
    normed_one = (inputs * inverse_one * gain_attn).astype(jnp.bfloat16)
    queries = rotate(
        matmul(normed_one, w_query).reshape(length, H, HD), cosine_table, sine_table
    ).astype(jnp.bfloat16)
    key_rows = rotate(
        matmul(normed_one, w_key).reshape(length, KVH, HD), cosine_table, sine_table
    ).astype(jnp.bfloat16)
    values = matmul(normed_one, w_value).astype(jnp.bfloat16).reshape(length, KVH, HD)
    scores = attention_scores(queries, key_rows, segment_row)
    highest = jnp.max(scores, axis=-1, keepdims=True)
    exponent = jnp.exp(scores - highest)
    denominator = jnp.sum(exponent, axis=-1, keepdims=True)
    weight = exponent / denominator
    attended = jnp.einsum(
        "kgqs,skd->qkgd", weight.astype(jnp.bfloat16), values, preferred_element_type=jnp.float32
    )
    attended = attended.reshape(length, H * HD).astype(jnp.bfloat16)
    hidden = inputs + matmul(attended, w_out)
    inverse_two = lax.rsqrt(jnp.mean(hidden * hidden, axis=-1, keepdims=True) + EPSILON)
    normed_two = (hidden * inverse_two * gain_moe).astype(jnp.bfloat16)
    state = (inverse_one, normed_one, queries, key_rows, values, weight, attended, hidden, inverse_two, normed_two)
    return state


MESH = pl.DeviceIdType.MESH
PARTS = 3


def move_rows(sources, held, pieces, sems, compute, z, n, others):
    row_send, row_recv, sum_send, sum_recv = sems
    barrier = pltpu.get_barrier_semaphore()
    for k in range(1, n):
        peer = lax.rem(z + k, n)
        pl.semaphore_signal(barrier, inc=1, device_id={LINE: peer}, device_id_type=MESH)
    for peer in others:
        pl.semaphore_signal(barrier, inc=1, device_id=peer, device_id_type=MESH)
    pl.semaphore_wait(barrier, n - 1 + len(others))

    def row_copy(kind, way, hop, source=None):
        step = 1 - 2 * way
        block = jnp.clip(z - step * hop, 0, n - 1)
        peer = jnp.clip(z + step, 0, n - 1)
        return pltpu.make_async_remote_copy(
            src_ref=held[kind].at[block] if source is None else source,
            dst_ref=held[kind].at[block],
            send_sem=row_send.at[kind, way, hop],
            recv_sem=row_recv.at[kind, way, hop],
            device_id={LINE: peer},
            device_id_type=MESH,
        )

    def sends(way, hop):
        step = 1 - 2 * way
        block, peer = z - step * hop, z + step
        return (block >= 0) & (block < n) & (peer >= 0) & (peer < n)

    def arrives(way, hop):
        block = z - (1 - 2 * way) * (hop + 1)
        return (block >= 0) & (block < n)

    def start(kind):
        for way in range(2):
            @pl.when(sends(way, 0))
            def _():
                row_copy(kind, way, 0, sources[kind]).start()

    def take(hop):
        for kind in range(len(held)):
            for way in range(2):
                @pl.when(arrives(way, hop))
                def _():
                    row_copy(kind, way, hop).wait_recv()

                @pl.when(sends(way, hop + 1) & (hop + 1 < n - 1))
                def _():
                    row_copy(kind, way, hop + 1).start()

    def waits(way, block):
        peer, last = z - (1 - 2 * way), (n - 1) * (1 - way)
        return (peer >= 0) & (peer < n) & ((block != last) | (peer != n - 1 - last))

    def far_copy(p):
        mine, arrived = pieces[p]
        block, way = n - 1 - z, jnp.where(z == 0, 1, 0)
        return pltpu.make_async_remote_copy(
            src_ref=mine(block),
            dst_ref=arrived(way, block),
            send_sem=sum_send.at[block, p],
            recv_sem=sum_recv.at[way, block, p],
            device_id={LINE: block},
            device_id_type=MESH,
        )

    def sum_copy(way, block, p):
        mine, arrived = pieces[p]
        return pltpu.make_async_remote_copy(
            src_ref=mine(block),
            dst_ref=arrived(way, block),
            send_sem=sum_send.at[block, p],
            recv_sem=sum_recv.at[way, block, p],
            device_id={LINE: jnp.clip(z + 1 - 2 * way, 0, n - 1)},
            device_id_type=MESH,
        )

    def sent(block, p):
        way = jnp.where(block > z, 0, 1)
        far = ((z == 0) | (z == n - 1)) & (block == n - 1 - z)

        @pl.when(far)
        def _():
            far_copy(p).start()

        @pl.when((block != z) & jnp.logical_not(far) & jnp.logical_not(waits(way, block)))
        def _():
            sum_copy(way, block, p).start()

    def between(block):
        if held:
            @pl.when(block == z)
            def _():
                take(0)

    def run():
        def both(hop):
            return (hop >= 0) & (z - 1 - hop >= 0) & (z + 1 + hop < n)

        def turn(k, carry):
            hop = lax.div(k + 1, 2) - 1
            block = z + (1 + hop) * (1 - 2 * lax.rem(k, 2))
            odd = lax.rem(k, 2) == 1

            @pl.when(odd & (hop > 0) & jnp.logical_not(both(hop - 1)))
            def _():
                take(hop)

            @pl.when(jnp.logical_not(odd) & both(hop) & (hop + 1 < n - 1))
            def _():
                take(hop + 1)

            @pl.when((block >= 0) & (block < n))
            def _():
                compute(block, sent, between)

            return carry

        def far_first(k, carry):
            block = z + (n - 1 - lax.div(k, 2)) * (1 - 2 * lax.rem(k, 2))

            @pl.when((block >= 0) & (block < n))
            def _():
                compute(block, sent, between)

            return carry

        if held:
            lax.fori_loop(0, 2 * n - 1, turn, 0)
        else:
            lax.fori_loop(0, 2 * n - 2, far_first, 0)

        first = jnp.where(2 * z < n, 0, 1)
        for way in (first, 1 - first):
            for k in range(1, n):
                block = z + (1 - 2 * way) * k

                @pl.when(waits(way, block) & (block >= 0) & (block < n))
                def _():
                    for p, (mine, arrived) in enumerate(pieces):
                        sum_copy(way, block, p).wait_recv()
                        own, other = mine(block), arrived(way, block)
                        own[...] = (
                            own[...].astype(jnp.float32) + other[...].astype(jnp.float32)
                        ).astype(jnp.bfloat16)
                        sum_copy(way, block, p).start()

        if not held:
            compute(z, sent, between)

    def collect(add):
        for way in range(2):
            for p, (_, arrived) in enumerate(pieces):
                sum_copy(way, z, p).wait_recv()
                add(p, arrived(way, z)[...].astype(jnp.float32))

    def finish():
        for kind in range(len(held)):
            for way in range(2):
                for hop in range(n - 1):
                    @pl.when(sends(way, hop))
                    def _():
                        row_copy(kind, way, hop).wait_send()
        for k in range(1, n):
            for p in range(len(pieces)):
                sum_copy(0, lax.rem(z + k, n), p).wait_send()

    return start, run, collect, finish


def row_pieces(sums, returned, parts):
    width = sums.shape[2] // parts

    def piece(p):
        at = pl.ds(p * width, width)
        return (
            lambda block: sums.at[block, :, at],
            lambda way, block: returned.at[way, block, :, at],
        )

    return [piece(p) for p in range(parts)]


def fetch_weights(layer, own, other, places, sem):
    count = places[0].shape[0]
    mine = lax.axis_index(CORE) == layer

    def copy(group, kind, e):
        return pltpu.make_async_copy(
            group[kind].at[e], places[kind].at[e], sem.at[kind * count + e]
        )

    for kind in range(len(places)):
        for e in range(count):
            @pl.when(mine)
            def _():
                copy(own, kind, e).start()

            @pl.when(jnp.logical_not(mine))
            def _():
                copy(other, kind, e).start()

    def wait():
        for kind in range(len(places)):
            for e in range(count):
                copy(own, kind, e).wait()

    return wait


def sigmoid_of(value):
    return 1.0 / (1.0 + jnp.exp(-value))


def column_of(block, column):
    here = lax.broadcasted_iota(jnp.int32, block.shape, 1) == column
    return jnp.sum(jnp.where(here, block, 0.0), axis=1, keepdims=True)


def experts_forward_kernel(
    layer, experts, x, mask, hidden, router, *refs
):
    own, other, refs = refs[:3], refs[3:6], refs[6:]
    own_dense, other_dense, refs = refs[:4], refs[4:8], refs[8:]
    out, rows, gates_all, gates, stats, gate_out, up_out, gated_out = refs[:8]
    placed, place_sem, keep_sem = refs[8:12], refs[-2], refs[-1]
    passing, (gate_keep, up_keep, gated) = refs[-9:-5], refs[-5:-2]
    refs = refs[:8] + refs[12:-9]
    w_gate, w_up, w_down, sums, returned, mixed, total, stats_all = refs[8:16]
    weight_sem, *sems = refs[16:]
    n, held = rows.shape[0], w_gate.shape[0]
    z = lax.axis_index(LINE)

    def keep_copies(block):
        pairs = (
            (gate_keep.at[:, block], gate_out.at[:, block]),
            (up_keep.at[:, block], up_out.at[:, block]),
            (gated.at[block], gated_out.at[block]),
        )
        return [
            pltpu.make_async_copy(source, target, keep_sem.at[i, block])
            for i, (source, target) in enumerate(pairs)
        ]

    def compute(block, sent, between):
        picked = rows[block]
        gate_block = gates_all[block].astype(jnp.float32)

        def one(e, carry):
            gate_pre = jnp.dot(picked, w_gate[e], preferred_element_type=jnp.float32)
            up_pre = jnp.dot(picked, w_up[e], preferred_element_type=jnp.float32)
            gate_keep[e, block] = gate_pre.astype(jnp.bfloat16)
            up_keep[e, block] = up_pre.astype(jnp.bfloat16)
            active = gate_pre * sigmoid_of(gate_pre) * up_pre
            share = (column_of(gate_block, z * held + e) * active).astype(jnp.bfloat16)
            inner = share.shape[1]
            gated[block, :, pl.ds(pl.multiple_of(e * inner, inner), inner)] = share
            mixed[e] = share
            return carry

        lax.fori_loop(0, held, one, 0)
        between(block)
        for copy in keep_copies(block):
            copy.start()
        width = out.shape[1] // PARTS
        for part in range(PARTS):
            at = pl.ds(part * width, width)
            result = jnp.zeros((out.shape[0], width), jnp.float32)
            for e in range(held):
                result += jnp.dot(mixed[e], w_down[e, :, at], preferred_element_type=jnp.float32)

            @pl.when(block == z)
            def _():
                total[:, at] = hidden[:, at] + result

            @pl.when(block != z)
            def _():
                sums[block, :, at] = result.astype(jnp.bfloat16)

            sent(block, part)

    own_gates = gates_all.at[z]
    start, run, collect, finish = move_rows(
        (x, own_gates, stats_all.at[z]),
        (rows, gates_all, stats_all),
        row_pieces(sums, returned, PARTS),
        sems,
        compute,
        z,
        n,
        [],
    )
    start(0)
    wait_weights = fetch_weights(layer, own, other, (w_gate, w_up, w_down), weight_sem)
    here = lax.axis_index(CORE) == 1 - layer

    def place_copy(group, i):
        return pltpu.make_async_copy(group[i], passing[i], place_sem.at[0, i])

    def place_out(i):
        return pltpu.make_async_copy(passing[i], placed[i], place_sem.at[1, i])

    logits = jnp.dot(x[...], router[...], preferred_element_type=jnp.float32)
    chosen = mask[...] > 0
    highest = jnp.max(jnp.where(chosen, logits, MASKED), axis=1, keepdims=True)
    exponent = jnp.where(chosen, jnp.exp(logits - highest), 0.0)
    gates[...] = exponent / jnp.sum(exponent, axis=1, keepdims=True)
    own_gates[...] = gates[...].astype(jnp.bfloat16)
    start(1)
    real = lax.broadcasted_iota(jnp.int32, logits.shape, 1) < experts
    highest = jnp.max(jnp.where(real, logits, MASKED), axis=1, keepdims=True)
    exponent = jnp.where(real, jnp.exp(logits - highest), 0.0)
    chance = exponent / jnp.sum(exponent, axis=1, keepdims=True)
    line = lax.broadcasted_iota(jnp.int32, stats.shape, 0)
    stats_all[z] = jnp.where(
        line == 0,
        jnp.sum(chance, axis=0, keepdims=True),
        jnp.where(line == 1, jnp.sum(mask[...], axis=0, keepdims=True), 0.0),
    )
    start(2)
    rows[z] = x[...]
    wait_weights()
    for i in range(4):
        @pl.when(here)
        def _():
            place_copy(own_dense, i).start()

        @pl.when(jnp.logical_not(here))
        def _():
            place_copy(other_dense, i).start()

    run()
    for i in range(4):
        place_copy(own_dense, i).wait()
        place_out(i).start()
    stats[...] = jnp.sum(stats_all[...], axis=0)
    width = out.shape[1] // PARTS

    def add(p, value):
        total[:, p * width : (p + 1) * width] += value

    collect(add)
    out[...] = total[...].astype(jnp.bfloat16)
    finish()
    for i in range(4):
        place_out(i).wait()
    for block in range(n):
        for copy in keep_copies(block):
            copy.wait()


def experts_backward_kernel(layer, grad, gates, *refs):
    own, other, saved_rows, saved_gated, refs = refs[:3], refs[3:6], refs[6], refs[7], refs[8:]
    kept, refs = refs[:2], refs[2:]
    keep_places, keep_sem, refs = refs[-3:-1], refs[-1], refs[:-3]
    gate_keep, up_keep = keep_places
    out, out_gates, rows_both, gated_both, grad_both, pre_both = refs[:6]
    w_gate, w_up, w_down, sums, sum_gates, returned, returned_gates, away, dots = refs[6:15]
    weight_sem, core_send, core_recv, core_local, *sems = refs[15:]
    n, held = gates.shape[0], w_gate.shape[0]
    half, inner = held // 2, w_gate.shape[2]
    core = lax.axis_index(CORE)
    z = lax.axis_index(LINE)
    turned_dims = (((1,), (1,)), ((), ()))
    gathered = layer == 1
    rows = grad if gathered else grad_both.at[core]

    def to_core(number, source, target):
        return pltpu.make_async_remote_copy(
            src_ref=source,
            dst_ref=target,
            send_sem=core_send.at[number],
            recv_sem=core_recv.at[number],
            device_id={CORE: 1 - core},
            device_id_type=MESH,
        )

    def block_copies(block):
        away_copy = to_core(2 + n + block, away.at[block], pre_both.at[core, block])
        if gathered:
            return (away_copy,)
        return (to_core(2 + block, rows.at[block], rows.at[block]), away_copy)

    def columns(at):
        return pl.ds(pl.multiple_of(at * half * inner, half * inner), half * inner)

    def whole_copies():
        copies = (
            to_core(0, saved_rows, rows_both.at[core]),
            to_core(1, saved_gated.at[:, :, columns(1 - core)], gated_both.at[core]),
        )
        return copies + ((to_core(2, grad, grad_both.at[core]),) if gathered else ())

    def local_copies():
        copies = (
            pltpu.make_async_copy(saved_rows, rows_both.at[core], core_local.at[0]),
            pltpu.make_async_copy(
                saved_gated.at[:, :, columns(core)], gated_both.at[core], core_local.at[1]
            ),
        )
        if gathered:
            copies += (pltpu.make_async_copy(grad, grad_both.at[core], core_local.at[2]),)
        return copies

    def compute(block, sent, between):
        picked = rows[block]
        gate_block = gates[block].astype(jnp.float32)
        dots[...] = jnp.zeros(dots.shape, jnp.float32)

        def one(e, place, j):
            raw = lax.dot_general(
                picked, w_down[e], turned_dims, preferred_element_type=jnp.float32
            )
            gate_pre = gate_keep[e, block].astype(jnp.float32)
            up_pre = up_keep[e, block].astype(jnp.float32)
            sigmoid = sigmoid_of(gate_pre)
            silu = gate_pre * sigmoid
            column = z * held + e
            dot = jnp.sum(raw * (silu * up_pre), axis=1, keepdims=True)
            here = lax.broadcasted_iota(jnp.int32, dots.shape, 1) == column
            dots[...] += jnp.where(here, dot, 0.0)
            active = column_of(gate_block, column) * raw
            place[:, pl.ds(pl.multiple_of(j * inner, inner), inner)] = (
                active * up_pre * sigmoid * (1.0 + gate_pre * (1.0 - sigmoid))
            ).astype(jnp.bfloat16)
            place[:, pl.ds(pl.multiple_of((half + j) * inner, inner), inner)] = (
                active * silu
            ).astype(jnp.bfloat16)

        def own_half(j, carry):
            one(core * half + j, pre_both.at[core, block], j)
            return carry

        def other_half(j, carry):
            one((1 - core) * half + j, away.at[block], j)
            return carry

        lax.fori_loop(0, half, other_half, 0)
        for copy in block_copies(block):
            copy.start()
        lax.fori_loop(0, half, own_half, 0)
        between(block)
        sum_gates[block] = dots[...].astype(jnp.bfloat16)

        @pl.when(block == z)
        def _():
            out_gates[...] = dots[...]

        sent(block, PARTS)
        width = out.shape[1] // PARTS
        for part in range(PARTS):
            at = pl.ds(part * width, width)
            result = jnp.zeros((out.shape[0], width), jnp.float32)
            for place, side in ((away.at[block], 1 - core), (pre_both.at[core, block], core)):
                for kind, right in enumerate((w_gate, w_up)):
                    for j in range(half):
                        left = place[:, pl.ds((kind * half + j) * inner, inner)]
                        result += lax.dot_general(
                            left,
                            right[side * half + j, at, :],
                            turned_dims,
                            preferred_element_type=jnp.float32,
                        )

            @pl.when(block == z)
            def _():
                out[:, at] = result

            @pl.when(block != z)
            def _():
                sums[block, :, at] = result.astype(jnp.bfloat16)

            sent(block, part)

    gate_piece = (lambda block: sum_gates.at[block], lambda way, block: returned_gates.at[way, block])
    start, run, collect, finish = move_rows(
        () if gathered else (grad,),
        () if gathered else (rows,),
        row_pieces(sums, returned, PARTS) + [gate_piece],
        sems,
        compute,
        z,
        n,
        [{CORE: 1 - core}],
    )
    if not gathered:
        start(0)
    wait_weights = fetch_weights(layer, own, other, (w_gate, w_up, w_down), weight_sem)
    keep_copies = [
        pltpu.make_async_copy(kept[i], keep_places[i], keep_sem.at[i]) for i in range(2)
    ]
    for copy in keep_copies:
        copy.start()
    for copy in whole_copies() + local_copies():
        copy.start()
    if not gathered:
        rows[z] = grad[...]
    for copy in keep_copies:
        copy.wait()
    wait_weights()
    run()
    width = out.shape[1] // PARTS

    def add(p, value):
        if p == PARTS:
            out_gates[...] += value
        else:
            out[:, p * width : (p + 1) * width] += value

    collect(add)
    finish()
    for copy in local_copies():
        copy.wait()
    for copy in whole_copies():
        copy.wait()
    for block in range(n):
        for copy in block_copies(block):
            copy.wait()


def exchange_scratch(n, kinds_out, kinds_back):
    return [
        pltpu.SemaphoreType.DMA((kinds_out, 2, n)),
        pltpu.SemaphoreType.DMA((kinds_out, 2, n)),
        pltpu.SemaphoreType.DMA((n, kinds_back)),
        pltpu.SemaphoreType.DMA((2, n, kinds_back)),
    ]


def expert_call(kernel, operands, own, other, extra, shapes, scratch, collective, loose=0):
    vmem, free = pl.BlockSpec(memory_space=pltpu.VMEM), pl.BlockSpec(memory_space=pl.ANY)
    weights = [pltpu.VMEM(array.shape, jnp.bfloat16) for array in own]
    return pl.pallas_call(
        kernel,
        out_shape=shapes,
        in_specs=[vmem] * len(operands) + [free] * (6 + len(extra)),
        out_specs=[vmem] * (len(shapes) - loose) + [free] * loose,
        scratch_shapes=weights + scratch,
        compiler_params=pltpu.CompilerParams(
            collective_id=collective, has_side_effects=True, vmem_limit_bytes=46 * 2**20
        ),
        cost_estimate=pl.CostEstimate(
            flops=5 * 10**10, bytes_accessed=10**8, transcendentals=0
        ),
    )(*operands, *own, *other, *extra)


def experts_forward(
    layer, normed_two, mask, hidden, router, own, other, own_dense, other_dense, experts
):
    n, held = lax.axis_size(LINE), own[0].shape[0]
    length, width = normed_two.shape
    inner = own[0].shape[2]
    low, full = jnp.bfloat16, jnp.float32
    kept = jax.ShapeDtypeStruct((held, n, length, inner), low)
    shapes = [
        jax.ShapeDtypeStruct((length, width), low),
        jax.ShapeDtypeStruct((n, length, width), low),
        jax.ShapeDtypeStruct((n, length, COLUMNS), low),
        jax.ShapeDtypeStruct((length, COLUMNS), full),
        jax.ShapeDtypeStruct((8, COLUMNS), full),
        kept,
        kept,
        jax.ShapeDtypeStruct((n, length, held * inner), low),
    ] + [jax.ShapeDtypeStruct(array.shape, low) for array in own_dense]
    scratch = [
        pltpu.VMEM((n, length, width), low),
        pltpu.VMEM((2, n, length, width), low),
        pltpu.VMEM((held, length, inner), low),
        pltpu.VMEM((length, width), full),
        pltpu.VMEM((n, 8, COLUMNS), full),
        pltpu.SemaphoreType.DMA((3 * held,)),
    ] + exchange_scratch(n, 3, PARTS)
    scratch += [pltpu.VMEM(array.shape, low) for array in own_dense]
    scratch += [pltpu.VMEM(shape.shape, low) for shape in shapes[5:8]]
    scratch.append(pltpu.SemaphoreType.DMA((2, 4)))
    scratch.append(pltpu.SemaphoreType.DMA((3, n)))
    kernel = functools.partial(experts_forward_kernel, layer, experts)
    return expert_call(
        kernel,
        (normed_two, mask, hidden, router),
        own,
        other,
        (*own_dense, *other_dense),
        shapes,
        scratch,
        1 + layer,
        7,
    )


def experts_backward(layer, grad_low, gates, gate_keep, up_keep, rows, gated, own, other):
    held, n, length, inner = gate_keep.shape
    width = grad_low.shape[-1]
    low, full = jnp.bfloat16, jnp.float32
    shapes = [
        jax.ShapeDtypeStruct((length, width), full),
        jax.ShapeDtypeStruct((length, COLUMNS), full),
        jax.ShapeDtypeStruct((2, n, length, width), low),
        jax.ShapeDtypeStruct((2, n, length, held // 2 * inner), low),
        jax.ShapeDtypeStruct((2, n, length, width), low),
        jax.ShapeDtypeStruct((2, n, length, held * inner), low),
    ]
    scratch = [
        pltpu.VMEM((n, length, width), low),
        pltpu.VMEM((n, length, COLUMNS), low),
        pltpu.VMEM((2, n, length, width), low),
        pltpu.VMEM((2, n, length, COLUMNS), low),
        pltpu.VMEM((n, length, held * inner), low),
        pltpu.VMEM((length, COLUMNS), full),
        pltpu.SemaphoreType.DMA((3 * held,)),
        pltpu.SemaphoreType.DMA((2 + 2 * n,)),
        pltpu.SemaphoreType.DMA((2 + 2 * n,)),
        pltpu.SemaphoreType.DMA((3,)),
    ] + exchange_scratch(n, 1, PARTS + 1)
    scratch += [pltpu.VMEM(gate_keep.shape, low)] * 2 + [pltpu.SemaphoreType.DMA((2,))]
    kernel = functools.partial(experts_backward_kernel, layer)
    return expert_call(
        kernel,
        (grad_low, gates),
        own,
        other,
        (rows, gated, gate_keep, up_keep),
        shapes,
        scratch,
        3 + layer,
    )


def attention_backward(grad_hidden, inputs, state, weights):
    gain_attn, w_query, w_key, w_value, w_out, gain_moe = weights[:6]
    (inverse_one, normed_one, queries, key_rows, values, weight, attended, hidden, inverse_two, normed_two) = state
    length = inputs.shape[0]
    grad_branch = grad_hidden.astype(jnp.bfloat16)
    grad_attended = jnp.einsum("td,cd->tc", grad_branch, w_out, preferred_element_type=jnp.float32)
    grad_attended = grad_attended.astype(jnp.bfloat16).reshape(length, KVH, H // KVH, HD)
    grad_weight = jnp.einsum(
        "qkgd,skd->kgqs", grad_attended, values, preferred_element_type=jnp.float32
    )
    grad_values = jnp.einsum(
        "kgqs,qkgd->skd",
        weight.astype(jnp.bfloat16),
        grad_attended,
        preferred_element_type=jnp.float32,
    )
    grad_values = grad_values.astype(jnp.bfloat16).reshape(length, KVH * HD)
    grad_scores = (
        weight * (grad_weight - jnp.sum(weight * grad_weight, axis=-1, keepdims=True))
    ).astype(jnp.bfloat16)
    score_scale = HD ** (-0.5)
    grouped = queries.reshape(length, KVH, H // KVH, HD)
    grad_queries = jnp.einsum(
        "kgqs,skd->qkgd", grad_scores, key_rows, preferred_element_type=jnp.float32
    )
    grad_queries = grad_queries.reshape(length, H, HD) * score_scale
    grad_keys = (
        jnp.einsum("kgqs,qkgd->skd", grad_scores, grouped, preferred_element_type=jnp.float32)
        * score_scale
    )
    cosine_table, sine_table = rotary_tables(length)
    grad_query_pre = (
        unrotate(grad_queries, cosine_table, sine_table)
        .reshape(length, H * HD)
        .astype(jnp.bfloat16)
    )
    grad_key_pre = (
        unrotate(grad_keys, cosine_table, sine_table).reshape(length, KVH * HD).astype(jnp.bfloat16)
    )
    grad_normed_one = (
        jnp.einsum("tq,cq->tc", grad_query_pre, w_query, preferred_element_type=jnp.float32)
        + jnp.einsum("tq,cq->tc", grad_key_pre, w_key, preferred_element_type=jnp.float32)
        + jnp.einsum("tq,cq->tc", grad_values, w_value, preferred_element_type=jnp.float32)
    )
    grad_norm_one, grad_gain_attn = norm_back(grad_normed_one, inputs, inverse_one, gain_attn)
    grad_inputs = grad_hidden + grad_norm_one
    grad_qkv = jnp.concatenate([grad_query_pre, grad_key_pre, grad_values], axis=1)
    return grad_inputs, grad_gain_attn, grad_qkv, grad_branch


def turned(left, right):
    return jnp.einsum("tc,tq->cq", left, right, preferred_element_type=jnp.float32)


def body(tokens, cotangent, segments, routes, *weight_arrays):
    core = lax.axis_index(CORE)
    first = core == 0
    experts = weight_arrays[6].shape[2]
    w_gate = weight_arrays[7]
    held = w_gate.shape[1]
    own = [array[0] for array in weight_arrays]
    other = [swapped(array) for array in own]
    weights = [
        [jnp.where(first, a, b) for a, b in zip(own[:7], other[:7])],
        [jnp.where(first, b, a) for a, b in zip(own[:7], other[:7])],
    ]
    inputs_low = lax.dynamic_slice_in_dim(tokens, core * SEQ, SEQ, 0)
    grad_low = lax.dynamic_slice_in_dim(cotangent, core * SEQ, SEQ, 0)
    cotangent_all = lax.all_gather(grad_low, LINE, axis=0)
    segment_row = lax.dynamic_index_in_dim(segments, core, 0, keepdims=False)
    mine = lax.dynamic_slice_in_dim(routes[0], core * SEQ, SEQ, 0)
    got = swapped(lax.dynamic_slice_in_dim(routes[0], (1 - core) * SEQ, SEQ, 0))
    routes_here = jnp.stack([jnp.where(first, mine, got), jnp.where(first, got, mine)])
    masks = multi_hot(routes_here, COLUMNS)
    own_experts, other_experts = own[7:], other[7:]

    saved, outs, stats = [], [], []
    for s in range(2):
        inputs = inputs_low.astype(jnp.float32)
        state = attention_forward(inputs, weights[s], segment_row)
        hidden, normed_two = state[7], state[9]
        if s == 0:
            normed_two, cotangent_all = lax.optimization_barrier((normed_two, cotangent_all))
        both_cores = [jnp.concatenate([a, swapped(a)]) for a in (state[1], state[6])]
        router = jnp.pad(weights[s][6], ((0, 0), (0, COLUMNS - experts)))
        inputs_low, rows, gates_all, gates, stat, *kept, query, key, value, out = experts_forward(
            s,
            normed_two,
            masks[s],
            hidden,
            router,
            own_experts,
            other_experts,
            own[1:5],
            other[1:5],
            experts,
        )
        weights[1 - s][1:5] = [query, key, value, out]
        outs.append(inputs_low)
        stats.append(stat)
        expert_state = (rows, gates_all, gates, *kept)
        saved.append((inputs, state, expert_state, both_cores))

    dp, deep = lax.axis_size(GROUP), lax.axis_size(LINE)
    grads = [None, None]
    input_grads = [None, None]
    for s in (1, 0):
        inputs, state, expert_state, both_cores = saved[s]
        (inverse_one, normed_one, _, _, _, _, attended, hidden, inverse_two, normed_two) = state
        rows_all, gates_all, gates, gate_keep, up_keep, gated = expert_state
        gain_moe, w_router = weights[s][5], weights[s][6]
        grad_sum, grad_gates, rows_both, gated_both, grad_both, pre_both = experts_backward(
            s,
            cotangent_all if s == 1 else grad_low,
            gates_all,
            gate_keep,
            up_keep,
            rows_all,
            gated,
            own_experts,
            other_experts,
        )
        inner = w_gate.shape[3]
        grad_gate_up = turned(
            rows_both.reshape(-1, D), pre_both.reshape(-1, held * inner)
        ).astype(jnp.bfloat16)
        if s == 1:
            grad_sum, grad_gate_up = lax.optimization_barrier((grad_sum, grad_gate_up))
            second_pre = lax.psum_scatter(grad_gate_up, GROUP, scatter_dimension=0, tiled=True)
        else:
            grad_sum, second_pre = lax.optimization_barrier((grad_sum, second_pre))
        gates, grad_gates = gates[:, :experts], grad_gates[:, :experts]
        grad_chosen = gates * (grad_gates - jnp.sum(gates * grad_gates, axis=-1, keepdims=True))
        grad_logits = grad_chosen.astype(jnp.bfloat16)
        grad_normed_two = grad_sum + jnp.einsum(
            "te,de->td", grad_logits, w_router, preferred_element_type=jnp.float32
        )
        grad_norm_two, grad_gain_moe = norm_back(grad_normed_two, hidden, inverse_two, gain_moe)
        grad_hidden = grad_low.astype(jnp.float32) + grad_norm_two
        grad_inputs, grad_gain_attn, grad_qkv, grad_branch = attention_backward(
            grad_hidden, inputs, state, weights[s]
        )
        if s == 1:
            grad_inputs, gated_both = lax.optimization_barrier((grad_inputs, gated_both))
        grad_down = turned(
            gated_both.reshape(-1, held // 2 * inner), grad_both.reshape(-1, D)
        ).astype(jnp.bfloat16)

        def halves(array):
            width = array.shape[1] // 2
            return (
                lax.dynamic_slice_in_dim(array, core * width, width, 1),
                lax.dynamic_slice_in_dim(array, (1 - core) * width, width, 1),
            )
        qkv_keep, qkv_send = halves(grad_qkv)
        branch_keep, branch_send = halves(grad_branch)
        grad_w_qkv = turned(
            both_cores[0], jnp.concatenate([qkv_keep, swapped(qkv_send)])
        ).astype(jnp.bfloat16)
        grad_w_out = turned(
            both_cores[1], jnp.concatenate([branch_keep, swapped(branch_send)])
        ).astype(jnp.bfloat16)
        grad_w_router = turned(normed_two, grad_logits)
        small = jnp.concatenate(
            [grad_gain_attn[:, None], grad_gain_moe[:, None], grad_w_router], axis=1
        ).astype(jnp.bfloat16)
        small = jnp.pad(small, ((0, 0), (0, COLUMNS - small.shape[1])))
        if s == 1:
            grad_inputs, grad_down, grad_w_qkv, grad_w_out = lax.optimization_barrier(
                (grad_inputs, grad_down, grad_w_qkv, grad_w_out)
            )
            dense = jnp.concatenate([grad_w_qkv, grad_w_out], axis=1)
            second_dense = lax.psum_scatter(dense, GROUP, scatter_dimension=0, tiled=True)
        grads[s] = (grad_gate_up, grad_down, grad_w_qkv, grad_w_out, small)
        input_grads[s] = grad_inputs
        grad_low = grad_inputs.astype(jnp.bfloat16)

    dp, deep = lax.axis_size(GROUP), lax.axis_size(LINE)
    half, inner = held // 2, w_gate.shape[3]
    grad_gate_up, grad_down, grad_w_qkv, grad_w_out, small = grads[0]
    arrays = [
        grad_gate_up.reshape(dp, D // dp, held * inner),
        grad_down.reshape(half, dp, inner // dp, D),
    ]
    lanes = dense_lanes(2, grad_w_qkv.shape[1])
    for array in (grad_w_qkv, grad_w_out, small):
        arrays.append(array.reshape(dp, deep, array.shape[0] // (dp * deep), array.shape[1]))
    width = grad_w_qkv.shape[1]
    whole = second_dense.shape[1]
    for columns, kind in (((0, width), QKV), ((width, whole - width), OUT)):
        start, size = columns
        target = (kind, slice(None), pl.ds(start - (start // width) * width, size))
        lanes.append((len(arrays), (False, columns), [(LINE, bits_of(LINE))], 1, target))
    arrays.append(second_dense.reshape(deep, second_dense.shape[0] // deep, whole))
    lanes.append(small_lane(len(arrays), 1))
    lanes += expert_lanes(0, inner) + down_lanes(1, 0) + down_lanes(len(arrays) + 1, 1)
    small = grads[1][4]
    arrays.append(small.reshape(dp, deep, small.shape[0] // (dp * deep), small.shape[1]))
    arrays.append(grads[1][1].reshape(half, dp, inner // dp, D))
    out_keep = jnp.where(first, outs[0], outs[1])
    out_got = swapped(jnp.where(first, outs[1], outs[0]))
    layer_out = jnp.where(
        first, jnp.concatenate([out_keep, out_got]), jnp.concatenate([out_got, out_keep])
    )
    low_one = input_grads[1].astype(jnp.bfloat16).astype(jnp.float32)
    grad_keep = jnp.where(first, input_grads[0], low_one)
    grad_got = swapped(jnp.where(first, low_one, input_grads[0]))
    input_grad = jnp.where(
        first, jnp.concatenate([grad_keep, grad_got]), jnp.concatenate([grad_got, grad_keep])
    )
    stats = jnp.concatenate(stats, axis=0)
    stats, layer_out, input_grad = lax.optimization_barrier((stats, layer_out, input_grad))
    *grads, qkv, out, small, stats = sum_scatter(
        arrays, lanes, second_pre, stats, inner, 0
    )
    full = jnp.float32
    w_gate_grad, w_up_grad, w_down_grad = (
        grad.reshape(held, *grad.shape[2:]).astype(full) for grad in grads
    )
    qkv = jnp.concatenate([qkv[0], qkv[1]], axis=1).astype(full)
    grad_w_out = jnp.concatenate([out[0], out[1]], axis=1).astype(full)
    small = small[0].astype(full) + small[1].astype(full)
    heads, kv = H * HD, KVH * HD
    stats = lax.dynamic_index_in_dim(stats.reshape(2, 8, COLUMNS), core, 0)
    token_total = SEQ * lax.axis_size((CORE, GROUP, LINE))
    counts, chances = stats[:, 1, :experts], stats[:, 0, :experts]
    balance = experts * (counts / (token_total * TOPK) * chances / token_total)
    results = (
        layer_out,
        input_grad,
        small[:, 0],
        qkv[:, :heads],
        qkv[:, heads : heads + kv],
        qkv[:, heads + kv :],
        grad_w_out,
        small[:, 1],
        small[:, 2 : 2 + experts],
        w_gate_grad,
        w_up_grad,
        w_down_grad,
    )
    return tuple(result[None] for result in results) + (balance,)


def solution(mesh):
    return jax.shard_map(
        body,
        mesh=mesh,
        in_specs=(
            P((GROUP, LINE), None),
            P((GROUP, LINE), None),
            P((GROUP, LINE), None),
            P(CORE, (GROUP, LINE), None),
            P(CORE, None),
            P(CORE, None, None),
            P(CORE, None, None),
            P(CORE, None, None),
            P(CORE, None, None),
            P(CORE, None),
            P(CORE, None, None),
            P(CORE, LINE, None, None),
            P(CORE, LINE, None, None),
            P(CORE, LINE, None, None),
        ),
        out_specs=(
            P(CORE, (GROUP, LINE), None),
            P(CORE, (GROUP, LINE), None),
            P(CORE, (GROUP, LINE)),
            P(CORE, (GROUP, LINE), None),
            P(CORE, (GROUP, LINE), None),
            P(CORE, (GROUP, LINE), None),
            P(CORE, (GROUP, LINE), None),
            P(CORE, (GROUP, LINE)),
            P(CORE, (GROUP, LINE), None),
            P(CORE, LINE, GROUP, None),
            P(CORE, LINE, GROUP, None),
            P(CORE, LINE, GROUP, None),
            P(CORE, None),
        ),
        check_vma=False,
    )
```

```python
import functools
import itertools
from types import SimpleNamespace

import jax
import jax.numpy as jnp
from jax import lax
from jax.experimental import pallas as pl
from jax.experimental.pallas import tpu as pltpu
from jax.sharding import PartitionSpec as P

D = 1536
H = 24
KVH = 8
HD = 64
TOPK = 8
SEQ = 96


EPSILON = 1e-05
THETA = 10000.0
MASKED = -1e30
COLUMNS = 128
GATE, UP, DOWN, QKV, OUT, SMALL = range(6)
CORE, GROUP, LINE = "section", "dp", "expert"
INNER = "inner"


def matmul(left_side, right_side):
    return jnp.dot(left_side, right_side, preferred_element_type=jnp.float32)


def rotary_tables(length):
    half_width = HD // 2
    position = jnp.arange(length, dtype=jnp.float32)[:, None]
    freq_rate = THETA ** (-jnp.arange(half_width, dtype=jnp.float32) / half_width)
    angles = position * freq_rate[None, :]
    return (jnp.cos(angles)[:, None, :], jnp.sin(angles)[:, None, :])


def rotate(tensor, cosine_table, sine_table):
    half_width = HD // 2
    first_half = tensor[..., :half_width]
    second_half = tensor[..., half_width:]
    return jnp.concatenate(
        [
            first_half * cosine_table - second_half * sine_table,
            second_half * cosine_table + first_half * sine_table,
        ],
        axis=-1,
    )


def unrotate(gradient, cosine_table, sine_table):
    half_width = HD // 2
    first_half = gradient[..., :half_width]
    second_half = gradient[..., half_width:]
    return jnp.concatenate(
        [
            first_half * cosine_table + second_half * sine_table,
            second_half * cosine_table - first_half * sine_table,
        ],
        axis=-1,
    )


def norm_back(grad_normed, tensor, inverse, gain_vector):
    scaled = grad_normed * gain_vector
    grad_gain = jnp.sum(grad_normed * tensor * inverse, axis=0)
    grad_tensor = inverse * scaled - tensor * inverse**3 * jnp.mean(
        scaled * tensor, axis=-1, keepdims=True
    )
    return (grad_tensor, grad_gain)


def attention_scores(queries, key_rows, segment_row):
    length = queries.shape[0]
    grouped = queries.reshape(length, KVH, H // KVH, HD)
    scores = jnp.einsum(
        "qkgd,skd->kgqs", grouped, key_rows, preferred_element_type=jnp.float32
    ) * HD ** (-0.5)
    position = jnp.arange(length)
    allowed = (position[None, :] <= position[:, None]) & (
        segment_row[:, None] == segment_row[None, :]
    )
    return jnp.where(allowed[None, None], scores, MASKED)


def multi_hot(route_rows, experts):
    columns = jnp.arange(experts, dtype=jnp.int32)
    return jnp.sum(
        (route_rows[..., None] == columns).astype(jnp.float32), axis=-2
    )


def swapped(array):
    return lax.ppermute(array, CORE, [(0, 1), (1, 0)])


def add_slab(total, arrived):
    *lead, rows, _ = total.shape
    step = 16 if rows % 16 == 0 else rows
    for where in itertools.product(*(range(n) for n in lead)):

        def add(i, carry):
            at = (*where, pl.ds(pl.multiple_of(i * step, step), step), slice(None))
            both = total[at].astype(jnp.float32) + arrived[at].astype(jnp.float32)
            total[at] = both.astype(jnp.bfloat16)
            return carry

        lax.fori_loop(0, rows // step, add, 0)


def sum_scatter_kernel(plan, *refs):
    lanes, ins, copies = plan
    sources = refs[:ins]
    second_pre, stats_in = refs[ins : ins + 2]
    stage, stats = refs[ins + 2 : ins + 8], refs[ins + 8]
    scratch = list(refs[ins + 9 :])
    send_sem, recv_sem, local_sem, stats_got, stats_send, stats_recv, core_send, core_recv = (
        scratch[-8:]
    )
    core = lax.axis_index(CORE)
    partners = []
    for lane in lanes:
        for axis, bits in lane.phases:
            partners += [(axis, bit) for bit in bits if (axis, bit) not in partners]
    partners.append((CORE, 0))
    index = {axis: lax.axis_index(axis) for axis, _ in partners}
    mine = {(axis, bit): (index[axis] >> bit) & 1 for axis, bit in partners}
    far = {key: index[key[0]] + (1 - 2 * mine[key]) * (1 << key[1]) for key in partners}
    barrier = pltpu.get_barrier_semaphore()
    peers = [{axis: far[axis, bit]} for axis, bit in partners if axis != GROUP]
    groups = lax.axis_size(GROUP)
    peers += [{GROUP: lax.rem(lax.axis_index(GROUP) + k, groups)} for k in range(1, groups)]
    for peer in peers:
        pl.semaphore_signal(
            barrier, inc=1, device_id=peer, device_id_type=pl.DeviceIdType.MESH
        )
    pl.semaphore_wait(barrier, len(peers))

    counter = itertools.count()

    def send(source, target, key):
        number = next(counter)
        copy = pltpu.make_async_remote_copy(
            src_ref=source,
            dst_ref=target,
            send_sem=send_sem.at[number],
            recv_sem=recv_sem.at[number],
            device_id={key[0]: far[key]},
            device_id_type=pl.DeviceIdType.MESH,
        )
        copy.start()
        return copy

    def place(axis, values):
        total = 0
        for bit, value in values.items():
            total = total + value * (1 << bit)
        return total

    def sum_stats():
        count = lax.axis_size(GROUP)
        me = lax.axis_index(GROUP)

        def copy(at, source, slot, target):
            return pltpu.make_async_remote_copy(
                src_ref=source,
                dst_ref=stats_got.at[slot],
                send_sem=stats_send.at[at],
                recv_sem=stats_recv.at[slot],
                device_id=target,
                device_id_type=pl.DeviceIdType.MESH,
            )

        for k in range(1, count):
            copy(k, stats_in, me, {GROUP: lax.rem(me + k, count)}).start()
        yield
        stats[...] = stats_in[...]
        for k in range(1, count):
            peer = lax.rem(me + k, count)
            copy(k, stats_in, peer, {GROUP: peer}).wait_recv()
            stats[...] += stats_got[peer]
        both = copy(0, stats, count, {CORE: far[CORE, 0]})
        both.start()
        yield
        both.wait()
        stats[...] += stats_got[count]
        for k in range(1, count):
            copy(k, stats_in, me, {GROUP: lax.rem(me + k, count)}).wait_send()

    summing = sum_stats()
    next(summing)

    def to_stage(number, source, kind, *at):
        spot = stage[kind].at[(core, *at)]
        return spot, pltpu.make_async_remote_copy(
            src_ref=source,
            dst_ref=spot,
            send_sem=core_send.at[number],
            recv_sem=core_recv.at[number],
            device_id={CORE: 1 - core},
            device_id_type=pl.DeviceIdType.MESH,
        )

    inner = stage[GATE].shape[3]
    wholes = []
    half = stage[GATE].shape[1]
    for number in range(2 * half):
        kind, j = divmod(number, half)
        source = second_pre.at[:, pl.ds(number * inner, inner)]
        spot, copy = to_stage(len(lanes) + number, source, kind, j)
        wholes.append((copy, pltpu.make_async_copy(source, spot, core_send.at[len(lanes) + number])))
    for copy, here in wholes:
        @pl.when(core == 1)
        def _(here=here):
            here.start()

        @pl.when(core == 0)
        def _(copy=copy):
            copy.start()

    moved = []
    started = []
    states = []
    for number, lane in enumerate(lanes):
        count = len(lane.buffers)
        buffers, scratch = scratch[:count], scratch[count:]
        source = sources[lane.source]
        prefix = lane.prefix
        if isinstance(prefix, int):
            source = source.at[prefix]

        def part(at, source=source, prefix=prefix):
            if isinstance(prefix, int):
                return source.at[at]
            inner, columns = prefix
            where = (slice(None), at) if inner else (at,)
            if columns is not None:
                where += (slice(None),) * (len(source.shape) - len(where) - 1) + (pl.ds(*columns),)
            return source.at[where]

        axis, bits = lane.phases[0]
        total, arrived = buffers[0], buffers[1:]
        rest = [bit for bit in bits[1:]]
        pending = []
        for choice in itertools.product((0, 1), repeat=len(rest)):
            values = dict(zip(rest, choice))
            slot = sum(value << i for i, value in enumerate(choice))
            far_at = place(axis, {**values, bits[0]: 1 - mine[axis, bits[0]]})
            here_at = place(axis, {**values, bits[0]: mine[axis, bits[0]]})
            copy = send(part(far_at), arrived[0].at[slot], (axis, bits[0]))
            pending.append((copy, slot))
            started.append(copy)
            states.append((number, part(here_at), slot, total))
        lane_state = SimpleNamespace(total=total, arrived=arrived, pending=pending)
        lane.state = lane_state
    locals_ = {}
    for at, (number, here, slot, total) in enumerate(states):
        copy = pltpu.make_async_copy(here, total.at[slot], local_sem.at[at])
        copy.start()
        locals_[number, slot] = copy
    short = [item for item in enumerate(lanes) if len(item[1].phases) == 1 and item[1].rows]
    long = [item for item in enumerate(lanes) if item not in short]
    turns = [(1, long), (1, short)]
    count = max(sum(len(bits) for _, bits in lane.phases) for lane in lanes)
    for step in range(2, count + 1):
        turns += [(2 * step - 2, long), (2 * step - 1, long), (step, short)]
    for at, (step, group) in enumerate(turns):
        if at == 2:
            next(summing)
        for number, lane in group:
            state = lane.state
            sizes = [len(bits) for _, bits in lane.phases]
            if step > sum(sizes):
                continue
            if step <= sizes[0]:
                axis, bits = lane.phases[0]
                resolved, rest = bits[:step], bits[step:]

                def slot_of(values):
                    found = 0
                    for i, bit in enumerate(bits[1:]):
                        found = found + values.get(bit, mine[axis, bit]) * (1 << i)
                    return found

                for copy, slot in state.pending:
                    copy.wait_recv()
                    if step == 1:
                        locals_[number, slot].wait()
                state.pending_next = []
                for choice in itertools.product((0, 1), repeat=len(rest)):
                    values = dict(zip(rest, choice))
                    got = sum(value << i for i, value in enumerate(choice))
                    add_slab(
                        state.total.at[slot_of(values)], state.arrived[step - 1].at[got]
                    )
                if rest:
                    following = rest[1:]
                    for choice in itertools.product((0, 1), repeat=len(following)):
                        values = dict(zip(following, choice))
                        got = sum(value << i for i, value in enumerate(choice))
                        values[rest[0]] = 1 - mine[axis, rest[0]]
                        copy = send(
                            state.total.at[slot_of(values)],
                            state.arrived[step].at[got],
                            (axis, rest[0]),
                        )
                        state.pending_next.append((copy, got))
                        started.append(copy)
                final = state.total.at[slot_of({})] if not rest else None
            else:
                axis, bits = lane.phases[1]
                done = step - sizes[0]
                rest = bits[done:]
                final = state.final
                for copy, _ in state.pending:
                    copy.wait_recv()
                state.pending_next = []
                for choice in itertools.product((0, 1), repeat=len(rest)):
                    values = dict(zip(rest, choice))
                    got = sum(value << i for i, value in enumerate(choice))
                    at = place(axis, {bit: values.get(bit, mine[axis, bit]) for bit in bits})
                    add_slab(final.at[at], state.arrived[step - 1].at[got])
                if not rest:
                    at = place(axis, {bit: mine[axis, bit] for bit in bits})
                    final = final.at[at]
            if final is not None and step >= sizes[0]:
                state.final = final
                if step == sum(sizes):
                    spot, copy = to_stage(number, final, *lane.target)
                    moved.append((lane.layer, copy))

                    @pl.when(core == lane.layer)
                    def _(spot=spot, final=final):
                        spot[...] = final[...]

                    @pl.when(core != lane.layer)
                    def _(copy=copy):
                        copy.start()
                elif step < sum(sizes):
                    axis, bits = lane.phases[1]
                    done = step - sizes[0]
                    bit, following = bits[done], bits[done + 1 :]
                    for choice in itertools.product((0, 1), repeat=len(following)):
                        values = dict(zip(following, choice))
                        got = sum(value << i for i, value in enumerate(choice))
                        at = place(
                            axis,
                            {
                                b: values.get(b, 1 - mine[axis, b] if b == bit else mine[axis, b])
                                for b in bits
                            },
                        )
                        copy = send(final.at[at], state.arrived[step].at[got], (axis, bit))
                        state.pending_next.append((copy, got))
                        started.append(copy)
            state.pending = state.pending_next
    for _ in summing:
        pass

    for copy, here in wholes:
        @pl.when(core == 1)
        def _(copy=copy, here=here):
            copy.wait_recv()
            here.wait()

        @pl.when(core == 0)
        def _(copy=copy):
            copy.wait_send()

    for layer, copy in moved:
        @pl.when(core == layer)
        def _(copy=copy):
            copy.wait_recv()

        @pl.when(core != layer)
        def _(copy=copy):
            copy.wait_send()

    for copy in started:
        copy.wait_send()


def sum_scatter(arrays, lanes, second_pre, stats, inner, collective):
    plans, scratch, shapes, copies, locals_ = [], [], [], 0, 0
    sizes = {}
    for source, prefix, phases, layer, target in lanes:
        shape = arrays[source].shape
        if isinstance(prefix, int):
            shape = shape[1:]
        else:
            if prefix[0]:
                shape = (shape[1], shape[0], *shape[2:])
            if prefix[1] is not None:
                shape = (*shape[:-1], prefix[1][1])
        buffers = [(shape[0] // 2, *shape[1:])]
        for step in range(1, len(phases[0][1]) + 1):
            buffers.append((shape[0] >> step, *shape[1:]))
            copies += shape[0] >> step
        locals_ += shape[0] // 2
        if len(phases) > 1:
            for step in range(1, len(phases[1][1]) + 1):
                buffers.append((shape[1] >> step, *shape[2:]))
                copies += shape[1] >> step
        plans.append(
            SimpleNamespace(
                source=source,
                prefix=prefix,
                phases=phases,
                buffers=buffers,
                rows=phases[0][0] == GROUP,
                layer=layer,
                target=target,
            )
        )
        width = sizes.get(target[0], (0, 0))[1] if len(target) > 2 else 0
        if layer == 0:
            sizes[target[0]] = (shape[-2], width + shape[-1])
        scratch += [pltpu.VMEM(buffer, jnp.bfloat16) for buffer in buffers]
    half = second_pre.shape[1] // (2 * inner)
    experts_shape = (2, half, second_pre.shape[0], inner)
    shapes = [
        jax.ShapeDtypeStruct(shape, jnp.bfloat16)
        for shape in (
            experts_shape,
            experts_shape,
            (2, half, *sizes[DOWN]),
            (2, *sizes[QKV]),
            (2, *sizes[OUT]),
            (2, *sizes[SMALL]),
        )
    ] + [jax.ShapeDtypeStruct(stats.shape, jnp.float32)]
    scratch += [
        pltpu.SemaphoreType.DMA((copies,)),
        pltpu.SemaphoreType.DMA((copies,)),
        pltpu.SemaphoreType.DMA((locals_,)),
    ]
    hops = lax.axis_size(GROUP) + 1
    scratch += [
        pltpu.VMEM((hops, *stats.shape), jnp.float32),
        pltpu.SemaphoreType.DMA((hops,)),
        pltpu.SemaphoreType.DMA((hops,)),
        pltpu.SemaphoreType.DMA((len(lanes) + 2 * half,)),
        pltpu.SemaphoreType.DMA((len(lanes) + 2 * half,)),
    ]
    return pl.pallas_call(
        functools.partial(sum_scatter_kernel, (plans, len(arrays), copies)),
        out_shape=shapes,
        in_specs=[pl.BlockSpec(memory_space=pl.ANY)] * (len(arrays) + 1)
        + [pl.BlockSpec(memory_space=pltpu.VMEM)],
        out_specs=[pl.BlockSpec(memory_space=pltpu.VMEM)] * len(shapes),
        scratch_shapes=scratch,
        compiler_params=pltpu.CompilerParams(
            collective_id=collective, has_side_effects=True, vmem_limit_bytes=60 * 2**20
        ),
    )(*arrays, second_pre, stats)


def bits_of(axis):
    return list(range(lax.axis_size(axis).bit_length() - 1))


def expert_lanes(first, inner):
    up, down = [(GROUP, bits_of(GROUP))], [(GROUP, bits_of(GROUP)[::-1])]
    return [
        (first, (False, ((2 * kind + j) * inner, inner)), (up, down)[kind], 0, (kind, j))
        for j in range(2)
        for kind in (GATE, UP)
    ]


def down_lanes(first, layer):
    up, down = [(GROUP, bits_of(GROUP))], [(GROUP, bits_of(GROUP)[::-1])]
    return [(first, 0, up, layer, (DOWN, 0)), (first, 1, down, layer, (DOWN, 1))]


def dense_lanes(first):
    up, down, deep = bits_of(GROUP), bits_of(GROUP)[::-1], bits_of(LINE)
    return [
        (first, (True, None), [(LINE, deep), (GROUP, up)], 0, (QKV,)),
        (first + 1, (False, None), [(GROUP, down), (LINE, deep)], 0, (OUT,)),
        small_lane(first + 2, 0),
    ]


def small_lane(first, layer):
    phases = [(GROUP, bits_of(GROUP)), (LINE, bits_of(LINE))]
    return (first, (False, None), phases, layer, (SMALL,))


def attention_forward(inputs, weights, segment_row):
    gain_attn, w_query, w_key, w_value, w_out, gain_moe = weights[:6]
    length = inputs.shape[0]
    cosine_table, sine_table = rotary_tables(length)
    inverse_one = lax.rsqrt(jnp.mean(inputs * inputs, axis=-1, keepdims=True) + EPSILON)
    normed_one = (inputs * inverse_one * gain_attn).astype(jnp.bfloat16)
    queries = rotate(
        matmul(normed_one, w_query).reshape(length, H, HD), cosine_table, sine_table
    ).astype(jnp.bfloat16)
    key_rows = rotate(
        matmul(normed_one, w_key).reshape(length, KVH, HD), cosine_table, sine_table
    ).astype(jnp.bfloat16)
    values = matmul(normed_one, w_value).astype(jnp.bfloat16).reshape(length, KVH, HD)
    scores = attention_scores(queries, key_rows, segment_row)
    highest = jnp.max(scores, axis=-1, keepdims=True)
    exponent = jnp.exp(scores - highest)
    denominator = jnp.sum(exponent, axis=-1, keepdims=True)
    weight = exponent / denominator
    attended = jnp.einsum(
        "kgqs,skd->qkgd", weight.astype(jnp.bfloat16), values, preferred_element_type=jnp.float32
    )
    attended = attended.reshape(length, H * HD).astype(jnp.bfloat16)
    hidden = inputs + matmul(attended, w_out)
    inverse_two = lax.rsqrt(jnp.mean(hidden * hidden, axis=-1, keepdims=True) + EPSILON)
    normed_two = (hidden * inverse_two * gain_moe).astype(jnp.bfloat16)
    state = (inverse_one, normed_one, queries, key_rows, values, weight, attended, hidden, inverse_two, normed_two)
    return state


MESH = pl.DeviceIdType.MESH
PARTS = 3


def move_rows(sources, held, pieces, sems, compute, z, n, others):
    row_send, row_recv, sum_send, sum_recv = sems
    barrier = pltpu.get_barrier_semaphore()
    for k in range(1, n):
        peer = lax.rem(z + k, n)
        pl.semaphore_signal(barrier, inc=1, device_id={LINE: peer}, device_id_type=MESH)
    for peer in others:
        pl.semaphore_signal(barrier, inc=1, device_id=peer, device_id_type=MESH)
    pl.semaphore_wait(barrier, n - 1 + len(others))

    def row_copy(kind, way, hop, source=None):
        step = 1 - 2 * way
        block = jnp.clip(z - step * hop, 0, n - 1)
        peer = jnp.clip(z + step, 0, n - 1)
        return pltpu.make_async_remote_copy(
            src_ref=held[kind].at[block] if source is None else source,
            dst_ref=held[kind].at[block],
            send_sem=row_send.at[kind, way, hop],
            recv_sem=row_recv.at[kind, way, hop],
            device_id={LINE: peer},
            device_id_type=MESH,
        )

    def sends(way, hop):
        step = 1 - 2 * way
        block, peer = z - step * hop, z + step
        return (block >= 0) & (block < n) & (peer >= 0) & (peer < n)

    def arrives(way, hop):
        block = z - (1 - 2 * way) * (hop + 1)
        return (block >= 0) & (block < n)

    def start(kind):
        for way in range(2):
            @pl.when(sends(way, 0))
            def _():
                row_copy(kind, way, 0, sources[kind]).start()

    def take(hop):
        for kind in range(len(held)):
            for way in range(2):
                @pl.when(arrives(way, hop))
                def _():
                    row_copy(kind, way, hop).wait_recv()

                @pl.when(sends(way, hop + 1) & (hop + 1 < n - 1))
                def _():
                    row_copy(kind, way, hop + 1).start()

    def waits(way, block):
        peer, last = z - (1 - 2 * way), (n - 1) * (1 - way)
        return (peer >= 0) & (peer < n) & ((block != last) | (peer != n - 1 - last))

    def far_copy(p):
        mine, arrived = pieces[p]
        block, way = n - 1 - z, jnp.where(z == 0, 1, 0)
        return pltpu.make_async_remote_copy(
            src_ref=mine(block),
            dst_ref=arrived(way, block),
            send_sem=sum_send.at[block, p],
            recv_sem=sum_recv.at[way, block, p],
            device_id={LINE: block},
            device_id_type=MESH,
        )

    def sum_copy(way, block, p):
        mine, arrived = pieces[p]
        return pltpu.make_async_remote_copy(
            src_ref=mine(block),
            dst_ref=arrived(way, block),
            send_sem=sum_send.at[block, p],
            recv_sem=sum_recv.at[way, block, p],
            device_id={LINE: jnp.clip(z + 1 - 2 * way, 0, n - 1)},
            device_id_type=MESH,
        )

    def sent(block, p):
        way = jnp.where(block > z, 0, 1)
        far = ((z == 0) | (z == n - 1)) & (block == n - 1 - z)

        @pl.when(far)
        def _():
            far_copy(p).start()

        @pl.when((block != z) & jnp.logical_not(far) & jnp.logical_not(waits(way, block)))
        def _():
            sum_copy(way, block, p).start()

    def between(block):
        if held:
            @pl.when(block == z)
            def _():
                take(0)

    def run():
        def both(hop):
            return (hop >= 0) & (z - 1 - hop >= 0) & (z + 1 + hop < n)

        def turn(k, carry):
            hop = lax.div(k + 1, 2) - 1
            block = z + (1 + hop) * (1 - 2 * lax.rem(k, 2))
            odd = lax.rem(k, 2) == 1

            @pl.when(odd & (hop > 0) & jnp.logical_not(both(hop - 1)))
            def _():
                take(hop)

            @pl.when(jnp.logical_not(odd) & both(hop) & (hop + 1 < n - 1))
            def _():
                take(hop + 1)

            @pl.when((block >= 0) & (block < n))
            def _():
                compute(block, sent, between)

            return carry

        def far_first(k, carry):
            block = z + (n - 1 - lax.div(k, 2)) * (1 - 2 * lax.rem(k, 2))

            @pl.when((block >= 0) & (block < n))
            def _():
                compute(block, sent, between)

            return carry

        if held:
            lax.fori_loop(0, 2 * n - 1, turn, 0)
        else:
            lax.fori_loop(0, 2 * n - 2, far_first, 0)

        first = jnp.where(2 * z < n, 0, 1)
        for way in (first, 1 - first):
            for k in range(1, n):
                block = z + (1 - 2 * way) * k

                @pl.when(waits(way, block) & (block >= 0) & (block < n))
                def _():
                    for p, (mine, arrived) in enumerate(pieces):
                        sum_copy(way, block, p).wait_recv()
                        own, other = mine(block), arrived(way, block)
                        own[...] = (
                            own[...].astype(jnp.float32) + other[...].astype(jnp.float32)
                        ).astype(jnp.bfloat16)
                        sum_copy(way, block, p).start()

        if not held:
            compute(z, sent, between)

    def collect(add):
        for way in range(2):
            for p, (_, arrived) in enumerate(pieces):
                sum_copy(way, z, p).wait_recv()
                add(p, arrived(way, z)[...].astype(jnp.float32))

    def finish():
        for kind in range(len(held)):
            for way in range(2):
                for hop in range(n - 1):
                    @pl.when(sends(way, hop))
                    def _():
                        row_copy(kind, way, hop).wait_send()
        for k in range(1, n):
            for p in range(len(pieces)):
                sum_copy(0, lax.rem(z + k, n), p).wait_send()

    return start, run, collect, finish


def row_pieces(sums, returned, parts):
    width = sums.shape[2] // parts

    def piece(p):
        at = pl.ds(p * width, width)
        return (
            lambda block: sums.at[block, :, at],
            lambda way, block: returned.at[way, block, :, at],
        )

    return [piece(p) for p in range(parts)]


def fetch_weights(layer, own, other, places, sem):
    count = places[0].shape[0]
    mine = lax.axis_index(CORE) == layer

    def copy(group, kind, e):
        return pltpu.make_async_copy(
            group[kind].at[e], places[kind].at[e], sem.at[kind * count + e]
        )

    for kind in range(len(places)):
        for e in range(count):
            @pl.when(mine)
            def _():
                copy(own, kind, e).start()

            @pl.when(jnp.logical_not(mine))
            def _():
                copy(other, kind, e).start()

    def wait():
        for kind in range(len(places)):
            for e in range(count):
                copy(own, kind, e).wait()

    return wait


def sigmoid_of(value):
    return 1.0 / (1.0 + jnp.exp(-value))


def column_of(block, column):
    here = lax.broadcasted_iota(jnp.int32, block.shape, 1) == column
    return jnp.sum(jnp.where(here, block, 0.0), axis=1, keepdims=True)


def experts_forward_kernel(
    layer, experts, x, mask, hidden, router, *refs
):
    own, other, refs = refs[:3], refs[3:6], refs[6:]
    own_dense, other_dense, refs = refs[:4], refs[4:8], refs[8:]
    out, rows, gates_all, gates, stats, gate_out, up_out, gated_out = refs[:8]
    placed, place_sem, keep_sem = refs[8:12], refs[-2], refs[-1]
    passing, (gate_keep, up_keep, gated) = refs[-9:-5], refs[-5:-2]
    refs = refs[:8] + refs[12:-9]
    w_gate, w_up, w_down, sums, returned, mixed, total, stats_all = refs[8:16]
    weight_sem, *sems = refs[16:]
    n, held = rows.shape[0], w_gate.shape[0]
    z = lax.axis_index(LINE)

    def keep_copies(block):
        pairs = (
            (gate_keep.at[:, block], gate_out.at[:, block]),
            (up_keep.at[:, block], up_out.at[:, block]),
            (gated.at[block], gated_out.at[block]),
        )
        return [
            pltpu.make_async_copy(source, target, keep_sem.at[i, block])
            for i, (source, target) in enumerate(pairs)
        ]

    def compute(block, sent, between):
        picked = rows[block]
        gate_block = gates_all[block].astype(jnp.float32)

        def one(e, carry):
            gate_pre = jnp.dot(picked, w_gate[e], preferred_element_type=jnp.float32)
            up_pre = jnp.dot(picked, w_up[e], preferred_element_type=jnp.float32)
            gate_keep[e, block] = gate_pre.astype(jnp.bfloat16)
            up_keep[e, block] = up_pre.astype(jnp.bfloat16)
            active = gate_pre * sigmoid_of(gate_pre) * up_pre
            share = (column_of(gate_block, z * held + e) * active).astype(jnp.bfloat16)
            inner = share.shape[1]
            gated[block, :, pl.ds(pl.multiple_of(e * inner, inner), inner)] = share
            mixed[e] = share
            return carry

        lax.fori_loop(0, held, one, 0)
        between(block)
        for copy in keep_copies(block):
            copy.start()
        width = out.shape[1] // PARTS
        for part in range(PARTS):
            at = pl.ds(part * width, width)
            result = jnp.zeros((out.shape[0], width), jnp.float32)
            for e in range(held):
                result += jnp.dot(mixed[e], w_down[e, :, at], preferred_element_type=jnp.float32)

            @pl.when(block == z)
            def _():
                total[:, at] = hidden[:, at] + result

            @pl.when(block != z)
            def _():
                sums[block, :, at] = result.astype(jnp.bfloat16)

            sent(block, part)

    own_gates = gates_all.at[z]
    start, run, collect, finish = move_rows(
        (x, own_gates, stats_all.at[z]),
        (rows, gates_all, stats_all),
        row_pieces(sums, returned, PARTS),
        sems,
        compute,
        z,
        n,
        [],
    )
    start(0)
    wait_weights = fetch_weights(layer, own, other, (w_gate, w_up, w_down), weight_sem)
    here = lax.axis_index(CORE) == 1 - layer

    def place_copy(group, i):
        return pltpu.make_async_copy(group[i], passing[i], place_sem.at[0, i])

    def place_out(i):
        return pltpu.make_async_copy(passing[i], placed[i], place_sem.at[1, i])

    logits = jnp.dot(x[...], router[...], preferred_element_type=jnp.float32)
    chosen = mask[...] > 0
    highest = jnp.max(jnp.where(chosen, logits, MASKED), axis=1, keepdims=True)
    exponent = jnp.where(chosen, jnp.exp(logits - highest), 0.0)
    gates[...] = exponent / jnp.sum(exponent, axis=1, keepdims=True)
    own_gates[...] = gates[...].astype(jnp.bfloat16)
    start(1)
    real = lax.broadcasted_iota(jnp.int32, logits.shape, 1) < experts
    highest = jnp.max(jnp.where(real, logits, MASKED), axis=1, keepdims=True)
    exponent = jnp.where(real, jnp.exp(logits - highest), 0.0)
    chance = exponent / jnp.sum(exponent, axis=1, keepdims=True)
    line = lax.broadcasted_iota(jnp.int32, stats.shape, 0)
    stats_all[z] = jnp.where(
        line == 0,
        jnp.sum(chance, axis=0, keepdims=True),
        jnp.where(line == 1, jnp.sum(mask[...], axis=0, keepdims=True), 0.0),
    )
    start(2)
    rows[z] = x[...]
    wait_weights()
    for i in range(4):
        @pl.when(here)
        def _():
            place_copy(own_dense, i).start()

        @pl.when(jnp.logical_not(here))
        def _():
            place_copy(other_dense, i).start()

    run()
    for i in range(4):
        place_copy(own_dense, i).wait()
        place_out(i).start()
    stats[...] = jnp.sum(stats_all[...], axis=0)
    width = out.shape[1] // PARTS

    def add(p, value):
        total[:, p * width : (p + 1) * width] += value

    collect(add)
    out[...] = total[...].astype(jnp.bfloat16)
    finish()
    for i in range(4):
        place_out(i).wait()
    for block in range(n):
        for copy in keep_copies(block):
            copy.wait()


def experts_backward_kernel(layer, grad, gates, *refs):
    own, other, saved_rows, saved_gated, refs = refs[:3], refs[3:6], refs[6], refs[7], refs[8:]
    kept, refs = refs[:2], refs[2:]
    keep_places, keep_sem, refs = refs[-3:-1], refs[-1], refs[:-3]
    gate_keep, up_keep = keep_places
    out, out_gates, rows_both, gated_both, grad_both, pre_both = refs[:6]
    w_gate, w_up, w_down, sums, sum_gates, returned, returned_gates, away, dots = refs[6:15]
    weight_sem, core_send, core_recv, core_local, *sems = refs[15:]
    n, held = gates.shape[0], w_gate.shape[0]
    half, inner = held // 2, w_gate.shape[2]
    core = lax.axis_index(CORE)
    z = lax.axis_index(LINE)
    turned_dims = (((1,), (1,)), ((), ()))
    gathered = layer == 1
    rows = grad if gathered else grad_both.at[core]

    def to_core(number, source, target):
        return pltpu.make_async_remote_copy(
            src_ref=source,
            dst_ref=target,
            send_sem=core_send.at[number],
            recv_sem=core_recv.at[number],
            device_id={CORE: 1 - core},
            device_id_type=MESH,
        )

    def block_copies(block):
        away_copy = to_core(2 + n + block, away.at[block], pre_both.at[core, block])
        if gathered:
            return (away_copy,)
        return (to_core(2 + block, rows.at[block], rows.at[block]), away_copy)

    def columns(at):
        return pl.ds(pl.multiple_of(at * half * inner, half * inner), half * inner)

    def whole_copies():
        copies = (
            to_core(0, saved_rows, rows_both.at[core]),
            to_core(1, saved_gated.at[:, :, columns(1 - core)], gated_both.at[core]),
        )
        return copies + ((to_core(2, grad, grad_both.at[core]),) if gathered else ())

    def local_copies():
        copies = (
            pltpu.make_async_copy(saved_rows, rows_both.at[core], core_local.at[0]),
            pltpu.make_async_copy(
                saved_gated.at[:, :, columns(core)], gated_both.at[core], core_local.at[1]
            ),
        )
        if gathered:
            copies += (pltpu.make_async_copy(grad, grad_both.at[core], core_local.at[2]),)
        return copies

    def compute(block, sent, between):
        picked = rows[block]
        gate_block = gates[block].astype(jnp.float32)
        dots[...] = jnp.zeros(dots.shape, jnp.float32)

        def one(e, place, j):
            raw = lax.dot_general(
                picked, w_down[e], turned_dims, preferred_element_type=jnp.float32
            )
            gate_pre = gate_keep[e, block].astype(jnp.float32)
            up_pre = up_keep[e, block].astype(jnp.float32)
            sigmoid = sigmoid_of(gate_pre)
            silu = gate_pre * sigmoid
            column = z * held + e
            dot = jnp.sum(raw * (silu * up_pre), axis=1, keepdims=True)
            here = lax.broadcasted_iota(jnp.int32, dots.shape, 1) == column
            dots[...] += jnp.where(here, dot, 0.0)
            active = column_of(gate_block, column) * raw
            place[:, pl.ds(pl.multiple_of(j * inner, inner), inner)] = (
                active * up_pre * sigmoid * (1.0 + gate_pre * (1.0 - sigmoid))
            ).astype(jnp.bfloat16)
            place[:, pl.ds(pl.multiple_of((half + j) * inner, inner), inner)] = (
                active * silu
            ).astype(jnp.bfloat16)

        def own_half(j, carry):
            one(core * half + j, pre_both.at[core, block], j)
            return carry

        def other_half(j, carry):
            one((1 - core) * half + j, away.at[block], j)
            return carry

        lax.fori_loop(0, half, other_half, 0)
        for copy in block_copies(block):
            copy.start()
        lax.fori_loop(0, half, own_half, 0)
        between(block)
        sum_gates[block] = dots[...].astype(jnp.bfloat16)

        @pl.when(block == z)
        def _():
            out_gates[...] = dots[...]

        sent(block, PARTS)
        width = out.shape[1] // PARTS
        for part in range(PARTS):
            at = pl.ds(part * width, width)
            result = jnp.zeros((out.shape[0], width), jnp.float32)
            for place, side in ((away.at[block], 1 - core), (pre_both.at[core, block], core)):
                for kind, right in enumerate((w_gate, w_up)):
                    for j in range(half):
                        left = place[:, pl.ds((kind * half + j) * inner, inner)]
                        result += lax.dot_general(
                            left,
                            right[side * half + j, at, :],
                            turned_dims,
                            preferred_element_type=jnp.float32,
                        )

            @pl.when(block == z)
            def _():
                out[:, at] = result

            @pl.when(block != z)
            def _():
                sums[block, :, at] = result.astype(jnp.bfloat16)

            sent(block, part)

    gate_piece = (lambda block: sum_gates.at[block], lambda way, block: returned_gates.at[way, block])
    start, run, collect, finish = move_rows(
        () if gathered else (grad,),
        () if gathered else (rows,),
        row_pieces(sums, returned, PARTS) + [gate_piece],
        sems,
        compute,
        z,
        n,
        [{CORE: 1 - core}],
    )
    if not gathered:
        start(0)
    wait_weights = fetch_weights(layer, own, other, (w_gate, w_up, w_down), weight_sem)
    keep_copies = [
        pltpu.make_async_copy(kept[i], keep_places[i], keep_sem.at[i]) for i in range(2)
    ]
    for copy in keep_copies:
        copy.start()
    for copy in whole_copies() + local_copies():
        copy.start()
    if not gathered:
        rows[z] = grad[...]
    for copy in keep_copies:
        copy.wait()
    wait_weights()
    run()
    width = out.shape[1] // PARTS

    def add(p, value):
        if p == PARTS:
            out_gates[...] += value
        else:
            out[:, p * width : (p + 1) * width] += value

    collect(add)
    finish()
    for copy in local_copies():
        copy.wait()
    for copy in whole_copies():
        copy.wait()
    for block in range(n):
        for copy in block_copies(block):
            copy.wait()


def exchange_scratch(n, kinds_out, kinds_back):
    return [
        pltpu.SemaphoreType.DMA((kinds_out, 2, n)),
        pltpu.SemaphoreType.DMA((kinds_out, 2, n)),
        pltpu.SemaphoreType.DMA((n, kinds_back)),
        pltpu.SemaphoreType.DMA((2, n, kinds_back)),
    ]


def expert_call(kernel, operands, own, other, extra, shapes, scratch, collective, loose=0):
    vmem, free = pl.BlockSpec(memory_space=pltpu.VMEM), pl.BlockSpec(memory_space=pl.ANY)
    weights = [pltpu.VMEM(array.shape, jnp.bfloat16) for array in own]
    return pl.pallas_call(
        kernel,
        out_shape=shapes,
        in_specs=[vmem] * len(operands) + [free] * (6 + len(extra)),
        out_specs=[vmem] * (len(shapes) - loose) + [free] * loose,
        scratch_shapes=weights + scratch,
        compiler_params=pltpu.CompilerParams(
            collective_id=collective, has_side_effects=True, vmem_limit_bytes=46 * 2**20
        ),
        cost_estimate=pl.CostEstimate(
            flops=5 * 10**10, bytes_accessed=10**8, transcendentals=0
        ),
    )(*operands, *own, *other, *extra)


def experts_forward(
    layer, normed_two, mask, hidden, router, own, other, own_dense, other_dense, experts
):
    n, held = lax.axis_size(LINE), own[0].shape[0]
    length, width = normed_two.shape
    inner = own[0].shape[2]
    low, full = jnp.bfloat16, jnp.float32
    kept = jax.ShapeDtypeStruct((held, n, length, inner), low)
    shapes = [
        jax.ShapeDtypeStruct((length, width), low),
        jax.ShapeDtypeStruct((n, length, width), low),
        jax.ShapeDtypeStruct((n, length, COLUMNS), low),
        jax.ShapeDtypeStruct((length, COLUMNS), full),
        jax.ShapeDtypeStruct((8, COLUMNS), full),
        kept,
        kept,
        jax.ShapeDtypeStruct((n, length, held * inner), low),
    ] + [jax.ShapeDtypeStruct(array.shape, low) for array in own_dense]
    scratch = [
        pltpu.VMEM((n, length, width), low),
        pltpu.VMEM((2, n, length, width), low),
        pltpu.VMEM((held, length, inner), low),
        pltpu.VMEM((length, width), full),
        pltpu.VMEM((n, 8, COLUMNS), full),
        pltpu.SemaphoreType.DMA((3 * held,)),
    ] + exchange_scratch(n, 3, PARTS)
    scratch += [pltpu.VMEM(array.shape, low) for array in own_dense]
    scratch += [pltpu.VMEM(shape.shape, low) for shape in shapes[5:8]]
    scratch.append(pltpu.SemaphoreType.DMA((2, 4)))
    scratch.append(pltpu.SemaphoreType.DMA((3, n)))
    kernel = functools.partial(experts_forward_kernel, layer, experts)
    return expert_call(
        kernel,
        (normed_two, mask, hidden, router),
        own,
        other,
        (*own_dense, *other_dense),
        shapes,
        scratch,
        1 + layer,
        7,
    )


def experts_backward(layer, grad_low, gates, gate_keep, up_keep, rows, gated, own, other):
    held, n, length, inner = gate_keep.shape
    width = grad_low.shape[-1]
    low, full = jnp.bfloat16, jnp.float32
    shapes = [
        jax.ShapeDtypeStruct((length, width), full),
        jax.ShapeDtypeStruct((length, COLUMNS), full),
        jax.ShapeDtypeStruct((2, n, length, width), low),
        jax.ShapeDtypeStruct((2, n, length, held // 2 * inner), low),
        jax.ShapeDtypeStruct((2, n, length, width), low),
        jax.ShapeDtypeStruct((2, n, length, held * inner), low),
    ]
    scratch = [
        pltpu.VMEM((n, length, width), low),
        pltpu.VMEM((n, length, COLUMNS), low),
        pltpu.VMEM((2, n, length, width), low),
        pltpu.VMEM((2, n, length, COLUMNS), low),
        pltpu.VMEM((n, length, held * inner), low),
        pltpu.VMEM((length, COLUMNS), full),
        pltpu.SemaphoreType.DMA((3 * held,)),
        pltpu.SemaphoreType.DMA((2 + 2 * n,)),
        pltpu.SemaphoreType.DMA((2 + 2 * n,)),
        pltpu.SemaphoreType.DMA((3,)),
    ] + exchange_scratch(n, 1, PARTS + 1)
    scratch += [pltpu.VMEM(gate_keep.shape, low)] * 2 + [pltpu.SemaphoreType.DMA((2,))]
    kernel = functools.partial(experts_backward_kernel, layer)
    return expert_call(
        kernel,
        (grad_low, gates),
        own,
        other,
        (rows, gated, gate_keep, up_keep),
        shapes,
        scratch,
        3 + layer,
    )


def attention_backward(grad_hidden, inputs, state, weights):
    gain_attn, w_query, w_key, w_value, w_out, gain_moe = weights[:6]
    (inverse_one, normed_one, queries, key_rows, values, weight, attended, hidden, inverse_two, normed_two) = state
    length = inputs.shape[0]
    grad_branch = grad_hidden.astype(jnp.bfloat16)
    grad_attended = jnp.einsum("td,cd->tc", grad_branch, w_out, preferred_element_type=jnp.float32)
    grad_attended = grad_attended.astype(jnp.bfloat16).reshape(length, KVH, H // KVH, HD)
    grad_weight = jnp.einsum(
        "qkgd,skd->kgqs", grad_attended, values, preferred_element_type=jnp.float32
    )
    grad_values = jnp.einsum(
        "kgqs,qkgd->skd",
        weight.astype(jnp.bfloat16),
        grad_attended,
        preferred_element_type=jnp.float32,
    )
    grad_values = grad_values.astype(jnp.bfloat16).reshape(length, KVH * HD)
    grad_scores = (
        weight * (grad_weight - jnp.sum(weight * grad_weight, axis=-1, keepdims=True))
    ).astype(jnp.bfloat16)
    score_scale = HD ** (-0.5)
    grouped = queries.reshape(length, KVH, H // KVH, HD)
    grad_queries = jnp.einsum(
        "kgqs,skd->qkgd", grad_scores, key_rows, preferred_element_type=jnp.float32
    )
    grad_queries = grad_queries.reshape(length, H, HD) * score_scale
    grad_keys = (
        jnp.einsum("kgqs,qkgd->skd", grad_scores, grouped, preferred_element_type=jnp.float32)
        * score_scale
    )
    cosine_table, sine_table = rotary_tables(length)
    grad_query_pre = (
        unrotate(grad_queries, cosine_table, sine_table)
        .reshape(length, H * HD)
        .astype(jnp.bfloat16)
    )
    grad_key_pre = (
        unrotate(grad_keys, cosine_table, sine_table).reshape(length, KVH * HD).astype(jnp.bfloat16)
    )
    grad_normed_one = (
        jnp.einsum("tq,cq->tc", grad_query_pre, w_query, preferred_element_type=jnp.float32)
        + jnp.einsum("tq,cq->tc", grad_key_pre, w_key, preferred_element_type=jnp.float32)
        + jnp.einsum("tq,cq->tc", grad_values, w_value, preferred_element_type=jnp.float32)
    )
    grad_norm_one, grad_gain_attn = norm_back(grad_normed_one, inputs, inverse_one, gain_attn)
    grad_inputs = grad_hidden + grad_norm_one
    grad_qkv = jnp.concatenate([grad_query_pre, grad_key_pre, grad_values], axis=1)
    return grad_inputs, grad_gain_attn, grad_qkv, grad_branch


def turned(left, right):
    return jnp.einsum("tc,tq->cq", left, right, preferred_element_type=jnp.float32)


def body(tokens, cotangent, segments, routes, *weight_arrays):
    core = lax.axis_index(CORE)
    first = core == 0
    experts = weight_arrays[6].shape[2]
    w_gate = weight_arrays[7]
    held = w_gate.shape[1]
    own = [array[0] for array in weight_arrays]
    other = [swapped(array) for array in own]
    weights = [
        [jnp.where(first, a, b) for a, b in zip(own[:7], other[:7])],
        [jnp.where(first, b, a) for a, b in zip(own[:7], other[:7])],
    ]
    inputs_low = lax.dynamic_slice_in_dim(tokens, core * SEQ, SEQ, 0)
    grad_low = lax.dynamic_slice_in_dim(cotangent, core * SEQ, SEQ, 0)
    cotangent_all = lax.all_gather(grad_low, LINE, axis=0)
    segment_row = lax.dynamic_index_in_dim(segments, core, 0, keepdims=False)
    mine = lax.dynamic_slice_in_dim(routes[0], core * SEQ, SEQ, 0)
    got = swapped(lax.dynamic_slice_in_dim(routes[0], (1 - core) * SEQ, SEQ, 0))
    routes_here = jnp.stack([jnp.where(first, mine, got), jnp.where(first, got, mine)])
    masks = multi_hot(routes_here, COLUMNS)
    own_experts, other_experts = own[7:], other[7:]

    saved, outs, stats = [], [], []
    for s in range(2):
        inputs = inputs_low.astype(jnp.float32)
        state = attention_forward(inputs, weights[s], segment_row)
        hidden, normed_two = state[7], state[9]
        if s == 0:
            normed_two, cotangent_all = lax.optimization_barrier((normed_two, cotangent_all))
        both_cores = [jnp.concatenate([a, swapped(a)]) for a in (state[1], state[6])]
        router = jnp.pad(weights[s][6], ((0, 0), (0, COLUMNS - experts)))
        inputs_low, rows, gates_all, gates, stat, *kept, query, key, value, out = experts_forward(
            s,
            normed_two,
            masks[s],
            hidden,
            router,
            own_experts,
            other_experts,
            own[1:5],
            other[1:5],
            experts,
        )
        weights[1 - s][1:5] = [query, key, value, out]
        outs.append(inputs_low)
        stats.append(stat)
        expert_state = (rows, gates_all, gates, *kept)
        saved.append((inputs, state, expert_state, both_cores))

    dp, deep = lax.axis_size(GROUP), lax.axis_size(LINE)
    grads = [None, None]
    input_grads = [None, None]
    for s in (1, 0):
        inputs, state, expert_state, both_cores = saved[s]
        (inverse_one, normed_one, _, _, _, _, attended, hidden, inverse_two, normed_two) = state
        rows_all, gates_all, gates, gate_keep, up_keep, gated = expert_state
        gain_moe, w_router = weights[s][5], weights[s][6]
        grad_sum, grad_gates, rows_both, gated_both, grad_both, pre_both = experts_backward(
            s,
            cotangent_all if s == 1 else grad_low,
            gates_all,
            gate_keep,
            up_keep,
            rows_all,
            gated,
            own_experts,
            other_experts,
        )
        inner = w_gate.shape[3]
        grad_gate_up = turned(
            rows_both.reshape(-1, D), pre_both.reshape(-1, held * inner)
        ).astype(jnp.bfloat16)
        if s == 1:
            grad_sum, grad_gate_up = lax.optimization_barrier((grad_sum, grad_gate_up))
            second_pre = lax.psum_scatter(grad_gate_up, GROUP, scatter_dimension=0, tiled=True)
        else:
            grad_sum, second_pre = lax.optimization_barrier((grad_sum, second_pre))
        gates, grad_gates = gates[:, :experts], grad_gates[:, :experts]
        grad_chosen = gates * (grad_gates - jnp.sum(gates * grad_gates, axis=-1, keepdims=True))
        grad_logits = grad_chosen.astype(jnp.bfloat16)
        grad_normed_two = grad_sum + jnp.einsum(
            "te,de->td", grad_logits, w_router, preferred_element_type=jnp.float32
        )
        grad_norm_two, grad_gain_moe = norm_back(grad_normed_two, hidden, inverse_two, gain_moe)
        grad_hidden = grad_low.astype(jnp.float32) + grad_norm_two
        grad_inputs, grad_gain_attn, grad_qkv, grad_branch = attention_backward(
            grad_hidden, inputs, state, weights[s]
        )
        if s == 1:
            grad_inputs, gated_both = lax.optimization_barrier((grad_inputs, gated_both))
        grad_down = turned(
            gated_both.reshape(-1, held // 2 * inner), grad_both.reshape(-1, D)
        ).astype(jnp.bfloat16)

        def halves(array):
            width = array.shape[1] // 2
            return (
                lax.dynamic_slice_in_dim(array, core * width, width, 1),
                lax.dynamic_slice_in_dim(array, (1 - core) * width, width, 1),
            )
        qkv_keep, qkv_send = halves(grad_qkv)
        branch_keep, branch_send = halves(grad_branch)
        grad_w_qkv = turned(
            both_cores[0], jnp.concatenate([qkv_keep, swapped(qkv_send)])
        ).astype(jnp.bfloat16)
        grad_w_out = turned(
            both_cores[1], jnp.concatenate([branch_keep, swapped(branch_send)])
        ).astype(jnp.bfloat16)
        grad_w_router = turned(normed_two, grad_logits)
        small = jnp.concatenate(
            [grad_gain_attn[:, None], grad_gain_moe[:, None], grad_w_router], axis=1
        ).astype(jnp.bfloat16)
        small = jnp.pad(small, ((0, 0), (0, COLUMNS - small.shape[1])))
        if s == 1:
            grad_inputs, grad_down, grad_w_qkv, grad_w_out = lax.optimization_barrier(
                (grad_inputs, grad_down, grad_w_qkv, grad_w_out)
            )
            dense = jnp.concatenate([grad_w_qkv, grad_w_out], axis=1)
            second_dense = lax.psum_scatter(dense, GROUP, scatter_dimension=0, tiled=True)
        grads[s] = (grad_gate_up, grad_down, grad_w_qkv, grad_w_out, small)
        input_grads[s] = grad_inputs
        grad_low = grad_inputs.astype(jnp.bfloat16)

    dp, deep = lax.axis_size(GROUP), lax.axis_size(LINE)
    half, inner = held // 2, w_gate.shape[3]
    grad_gate_up, grad_down, grad_w_qkv, grad_w_out, small = grads[0]
    arrays = [
        grad_gate_up.reshape(dp, D // dp, held * inner),
        grad_down.reshape(half, dp, inner // dp, D),
    ]
    lanes = dense_lanes(2)
    for array in (grad_w_qkv, grad_w_out, small):
        arrays.append(array.reshape(dp, deep, array.shape[0] // (dp * deep), array.shape[1]))
    width = grad_w_qkv.shape[1]
    whole = second_dense.shape[1]
    for columns, kind in (((0, width), QKV), ((width, whole - width), OUT)):
        start, size = columns
        target = (kind, slice(None), pl.ds(start - (start // width) * width, size))
        lanes.append((len(arrays), (False, columns), [(LINE, bits_of(LINE))], 1, target))
    arrays.append(second_dense.reshape(deep, second_dense.shape[0] // deep, whole))
    lanes.append(small_lane(len(arrays), 1))
    lanes += expert_lanes(0, inner) + down_lanes(1, 0) + down_lanes(len(arrays) + 1, 1)
    small = grads[1][4]
    arrays.append(small.reshape(dp, deep, small.shape[0] // (dp * deep), small.shape[1]))
    arrays.append(grads[1][1].reshape(half, dp, inner // dp, D))
    out_keep = jnp.where(first, outs[0], outs[1])
    out_got = swapped(jnp.where(first, outs[1], outs[0]))
    layer_out = jnp.where(
        first, jnp.concatenate([out_keep, out_got]), jnp.concatenate([out_got, out_keep])
    )
    low_one = input_grads[1].astype(jnp.bfloat16).astype(jnp.float32)
    grad_keep = jnp.where(first, input_grads[0], low_one)
    grad_got = swapped(jnp.where(first, low_one, input_grads[0]))
    input_grad = jnp.where(
        first, jnp.concatenate([grad_keep, grad_got]), jnp.concatenate([grad_got, grad_keep])
    )
    stats = jnp.concatenate(stats, axis=0)
    stats, layer_out, input_grad = lax.optimization_barrier((stats, layer_out, input_grad))
    *grads, qkv, out, small, stats = sum_scatter(
        arrays, lanes, second_pre, stats, inner, 0
    )
    full = jnp.float32
    w_gate_grad, w_up_grad, w_down_grad = (
        grad.reshape(held, *grad.shape[2:]).astype(full) for grad in grads
    )
    qkv = jnp.concatenate([qkv[0], qkv[1]], axis=1).astype(full)
    grad_w_out = jnp.concatenate([out[0], out[1]], axis=1).astype(full)
    small = small[0].astype(full) + small[1].astype(full)
    heads, kv = H * HD, KVH * HD
    stats = lax.dynamic_index_in_dim(stats.reshape(2, 8, COLUMNS), core, 0)
    token_total = SEQ * lax.axis_size((CORE, GROUP, LINE))
    counts, chances = stats[:, 1, :experts], stats[:, 0, :experts]
    balance = experts * (counts / (token_total * TOPK) * chances / token_total)
    results = (
        layer_out,
        input_grad,
        small[:, 0],
        qkv[:, :heads],
        qkv[:, heads : heads + kv],
        qkv[:, heads + kv :],
        grad_w_out,
        small[:, 1],
        small[:, 2 : 2 + experts],
        w_gate_grad,
        w_up_grad,
        w_down_grad,
    )
    return tuple(result[None] for result in results) + (balance,)


def solution(mesh):
    return jax.shard_map(
        body,
        mesh=mesh,
        in_specs=(
            P((GROUP, LINE), None),
            P((GROUP, LINE), None),
            P((GROUP, LINE), None),
            P(CORE, (GROUP, LINE), None),
            P(CORE, None),
            P(CORE, None, None),
            P(CORE, None, None),
            P(CORE, None, None),
            P(CORE, None, None),
            P(CORE, None),
            P(CORE, None, None),
            P(CORE, LINE, None, None),
            P(CORE, LINE, None, None),
            P(CORE, LINE, None, None),
        ),
        out_specs=(
            P(CORE, (GROUP, LINE), None),
            P(CORE, (GROUP, LINE), None),
            P(CORE, (GROUP, LINE)),
            P(CORE, (GROUP, LINE), None),
            P(CORE, (GROUP, LINE), None),
            P(CORE, (GROUP, LINE), None),
            P(CORE, (GROUP, LINE), None),
            P(CORE, (GROUP, LINE)),
            P(CORE, (GROUP, LINE), None),
            P(CORE, LINE, GROUP, None),
            P(CORE, LINE, GROUP, None),
            P(CORE, LINE, GROUP, None),
            P(CORE, None),
        ),
        check_vma=False,
    )
```

```python
import functools
import itertools
from types import SimpleNamespace

import jax
import jax.numpy as jnp
from jax import lax
from jax.experimental import pallas as pl
from jax.experimental.pallas import tpu as pltpu
from jax.sharding import PartitionSpec as P

D = 1536
H = 24
KVH = 8
HD = 64
TOPK = 8
SEQ = 96


EPSILON = 1e-05
THETA = 10000.0
MASKED = -1e30
COLUMNS = 128
GATE, UP, DOWN, QKV, OUT, SMALL = range(6)
CORE, GROUP, LINE = "section", "dp", "expert"
INNER = "inner"


def matmul(left_side, right_side):
    return jnp.dot(left_side, right_side, preferred_element_type=jnp.float32)


def rotary_tables(length):
    half_width = HD // 2
    position = jnp.arange(length, dtype=jnp.float32)[:, None]
    freq_rate = THETA ** (-jnp.arange(half_width, dtype=jnp.float32) / half_width)
    angles = position * freq_rate[None, :]
    return (jnp.cos(angles)[:, None, :], jnp.sin(angles)[:, None, :])


def rotate(tensor, cosine_table, sine_table):
    half_width = HD // 2
    first_half = tensor[..., :half_width]
    second_half = tensor[..., half_width:]
    return jnp.concatenate(
        [
            first_half * cosine_table - second_half * sine_table,
            second_half * cosine_table + first_half * sine_table,
        ],
        axis=-1,
    )


def unrotate(gradient, cosine_table, sine_table):
    half_width = HD // 2
    first_half = gradient[..., :half_width]
    second_half = gradient[..., half_width:]
    return jnp.concatenate(
        [
            first_half * cosine_table + second_half * sine_table,
            second_half * cosine_table - first_half * sine_table,
        ],
        axis=-1,
    )


def norm_back(grad_normed, tensor, inverse, gain_vector):
    scaled = grad_normed * gain_vector
    grad_gain = jnp.sum(grad_normed * tensor * inverse, axis=0)
    grad_tensor = inverse * scaled - tensor * inverse**3 * jnp.mean(
        scaled * tensor, axis=-1, keepdims=True
    )
    return (grad_tensor, grad_gain)


def attention_scores(queries, key_rows, segment_row):
    length = queries.shape[0]
    grouped = queries.reshape(length, KVH, H // KVH, HD)
    scores = jnp.einsum(
        "qkgd,skd->kgqs", grouped, key_rows, preferred_element_type=jnp.float32
    ) * HD ** (-0.5)
    position = jnp.arange(length)
    allowed = (position[None, :] <= position[:, None]) & (
        segment_row[:, None] == segment_row[None, :]
    )
    return jnp.where(allowed[None, None], scores, MASKED)


def multi_hot(route_rows, experts):
    columns = jnp.arange(experts, dtype=jnp.int32)
    return jnp.sum(
        (route_rows[..., None] == columns).astype(jnp.float32), axis=-2
    )


def swapped(array):
    return lax.ppermute(array, CORE, [(0, 1), (1, 0)])


def add_slab(total, arrived):
    *lead, rows, _ = total.shape
    step = 16 if rows % 16 == 0 else rows
    for where in itertools.product(*(range(n) for n in lead)):

        def add(i, carry):
            at = (*where, pl.ds(pl.multiple_of(i * step, step), step), slice(None))
            both = total[at].astype(jnp.float32) + arrived[at].astype(jnp.float32)
            total[at] = both.astype(jnp.bfloat16)
            return carry

        lax.fori_loop(0, rows // step, add, 0)


def sum_scatter_kernel(plan, *refs):
    lanes, ins, copies = plan
    sources = refs[:ins]
    second_pre, stats_in = refs[ins : ins + 2]
    stage, stats = refs[ins + 2 : ins + 8], refs[ins + 8]
    scratch = list(refs[ins + 9 :])
    send_sem, recv_sem, local_sem, stats_got, stats_send, stats_recv, core_send, core_recv = (
        scratch[-8:]
    )
    core = lax.axis_index(CORE)
    partners = []
    for lane in lanes:
        for axis, bits in lane.phases:
            partners += [(axis, bit) for bit in bits if (axis, bit) not in partners]
    partners.append((CORE, 0))
    index = {axis: lax.axis_index(axis) for axis, _ in partners}
    mine = {(axis, bit): (index[axis] >> bit) & 1 for axis, bit in partners}
    far = {key: index[key[0]] + (1 - 2 * mine[key]) * (1 << key[1]) for key in partners}
    barrier = pltpu.get_barrier_semaphore()
    peers = [{axis: far[axis, bit]} for axis, bit in partners if axis != GROUP]
    groups = lax.axis_size(GROUP)
    peers += [{GROUP: lax.rem(lax.axis_index(GROUP) + k, groups)} for k in range(1, groups)]
    for peer in peers:
        pl.semaphore_signal(
            barrier, inc=1, device_id=peer, device_id_type=pl.DeviceIdType.MESH
        )
    pl.semaphore_wait(barrier, len(peers))

    counter = itertools.count()

    def send(source, target, key):
        number = next(counter)
        copy = pltpu.make_async_remote_copy(
            src_ref=source,
            dst_ref=target,
            send_sem=send_sem.at[number],
            recv_sem=recv_sem.at[number],
            device_id={key[0]: far[key]},
            device_id_type=pl.DeviceIdType.MESH,
        )
        copy.start()
        return copy

    def place(axis, values):
        total = 0
        for bit, value in values.items():
            total = total + value * (1 << bit)
        return total

    def sum_stats():
        count = lax.axis_size(GROUP)
        me = lax.axis_index(GROUP)

        def copy(at, source, slot, target):
            return pltpu.make_async_remote_copy(
                src_ref=source,
                dst_ref=stats_got.at[slot],
                send_sem=stats_send.at[at],
                recv_sem=stats_recv.at[slot],
                device_id=target,
                device_id_type=pl.DeviceIdType.MESH,
            )

        for k in range(1, count):
            copy(k, stats_in, me, {GROUP: lax.rem(me + k, count)}).start()
        yield
        stats[...] = stats_in[...]
        for k in range(1, count):
            peer = lax.rem(me + k, count)
            copy(k, stats_in, peer, {GROUP: peer}).wait_recv()
            stats[...] += stats_got[peer]
        both = copy(0, stats, count, {CORE: far[CORE, 0]})
        both.start()
        yield
        both.wait()
        stats[...] += stats_got[count]
        for k in range(1, count):
            copy(k, stats_in, me, {GROUP: lax.rem(me + k, count)}).wait_send()

    summing = sum_stats()
    next(summing)

    def to_stage(number, source, kind, *at):
        spot = stage[kind].at[(core, *at)]
        return spot, pltpu.make_async_remote_copy(
            src_ref=source,
            dst_ref=spot,
            send_sem=core_send.at[number],
            recv_sem=core_recv.at[number],
            device_id={CORE: 1 - core},
            device_id_type=pl.DeviceIdType.MESH,
        )

    inner = stage[GATE].shape[3]
    wholes = []
    half = stage[GATE].shape[1]
    for number in range(2 * half):
        kind, j = divmod(number, half)
        source = second_pre.at[:, pl.ds(number * inner, inner)]
        spot, copy = to_stage(len(lanes) + number, source, kind, j)
        wholes.append((copy, pltpu.make_async_copy(source, spot, core_send.at[len(lanes) + number])))
    for copy, here in wholes:
        @pl.when(core == 1)
        def _(here=here):
            here.start()

        @pl.when(core == 0)
        def _(copy=copy):
            copy.start()

    moved = []
    started = []
    states = []
    for number, lane in enumerate(lanes):
        count = len(lane.buffers)
        buffers, scratch = scratch[:count], scratch[count:]
        source = sources[lane.source]
        prefix = lane.prefix
        if isinstance(prefix, int):
            source = source.at[prefix]

        def part(at, source=source, prefix=prefix):
            if isinstance(prefix, int):
                return source.at[at]
            inner, columns = prefix
            where = (slice(None), at) if inner else (at,)
            if columns is not None:
                where += (slice(None),) * (len(source.shape) - len(where) - 1) + (pl.ds(*columns),)
            return source.at[where]

        axis, bits = lane.phases[0]
        total, arrived = buffers[0], buffers[1:]
        rest = [bit for bit in bits[1:]]
        pending = []
        for choice in itertools.product((0, 1), repeat=len(rest)):
            values = dict(zip(rest, choice))
            slot = sum(value << i for i, value in enumerate(choice))
            far_at = place(axis, {**values, bits[0]: 1 - mine[axis, bits[0]]})
            here_at = place(axis, {**values, bits[0]: mine[axis, bits[0]]})
            copy = send(part(far_at), arrived[0].at[slot], (axis, bits[0]))
            pending.append((copy, slot))
            started.append(copy)
            states.append((number, part(here_at), slot, total))
        lane_state = SimpleNamespace(total=total, arrived=arrived, pending=pending)
        lane.state = lane_state
    locals_ = {}
    for at, (number, here, slot, total) in enumerate(states):
        copy = pltpu.make_async_copy(here, total.at[slot], local_sem.at[at])
        copy.start()
        locals_[number, slot] = copy
    short = [item for item in enumerate(lanes) if len(item[1].phases) == 1 and item[1].rows]
    long = [item for item in enumerate(lanes) if item not in short]
    turns = [(1, long), (1, short)]
    count = max(sum(len(bits) for _, bits in lane.phases) for lane in lanes)
    for step in range(2, count + 1):
        turns += [(2 * step - 2, long), (2 * step - 1, long), (step, short)]
    for at, (step, group) in enumerate(turns):
        if at == 2:
            next(summing)
        for number, lane in group:
            state = lane.state
            sizes = [len(bits) for _, bits in lane.phases]
            if step > sum(sizes):
                continue
            if step <= sizes[0]:
                axis, bits = lane.phases[0]
                resolved, rest = bits[:step], bits[step:]

                def slot_of(values):
                    found = 0
                    for i, bit in enumerate(bits[1:]):
                        found = found + values.get(bit, mine[axis, bit]) * (1 << i)
                    return found

                for copy, slot in state.pending:
                    copy.wait_recv()
                    if step == 1:
                        locals_[number, slot].wait()
                state.pending_next = []
                for choice in itertools.product((0, 1), repeat=len(rest)):
                    values = dict(zip(rest, choice))
                    got = sum(value << i for i, value in enumerate(choice))
                    add_slab(
                        state.total.at[slot_of(values)], state.arrived[step - 1].at[got]
                    )
                if rest:
                    following = rest[1:]
                    for choice in itertools.product((0, 1), repeat=len(following)):
                        values = dict(zip(following, choice))
                        got = sum(value << i for i, value in enumerate(choice))
                        values[rest[0]] = 1 - mine[axis, rest[0]]
                        copy = send(
                            state.total.at[slot_of(values)],
                            state.arrived[step].at[got],
                            (axis, rest[0]),
                        )
                        state.pending_next.append((copy, got))
                        started.append(copy)
                final = state.total.at[slot_of({})] if not rest else None
            else:
                axis, bits = lane.phases[1]
                done = step - sizes[0]
                rest = bits[done:]
                final = state.final
                for copy, _ in state.pending:
                    copy.wait_recv()
                state.pending_next = []
                for choice in itertools.product((0, 1), repeat=len(rest)):
                    values = dict(zip(rest, choice))
                    got = sum(value << i for i, value in enumerate(choice))
                    at = place(axis, {bit: values.get(bit, mine[axis, bit]) for bit in bits})
                    add_slab(final.at[at], state.arrived[step - 1].at[got])
                if not rest:
                    at = place(axis, {bit: mine[axis, bit] for bit in bits})
                    final = final.at[at]
            if final is not None and step >= sizes[0]:
                state.final = final
                if step == sum(sizes):
                    spot, copy = to_stage(number, final, *lane.target)
                    moved.append((lane.layer, copy))

                    @pl.when(core == lane.layer)
                    def _(spot=spot, final=final):
                        spot[...] = final[...]

                    @pl.when(core != lane.layer)
                    def _(copy=copy):
                        copy.start()
                elif step < sum(sizes):
                    axis, bits = lane.phases[1]
                    done = step - sizes[0]
                    bit, following = bits[done], bits[done + 1 :]
                    for choice in itertools.product((0, 1), repeat=len(following)):
                        values = dict(zip(following, choice))
                        got = sum(value << i for i, value in enumerate(choice))
                        at = place(
                            axis,
                            {
                                b: values.get(b, 1 - mine[axis, b] if b == bit else mine[axis, b])
                                for b in bits
                            },
                        )
                        copy = send(final.at[at], state.arrived[step].at[got], (axis, bit))
                        state.pending_next.append((copy, got))
                        started.append(copy)
            state.pending = state.pending_next
    for _ in summing:
        pass

    for copy, here in wholes:
        @pl.when(core == 1)
        def _(copy=copy, here=here):
            copy.wait_recv()
            here.wait()

        @pl.when(core == 0)
        def _(copy=copy):
            copy.wait_send()

    for layer, copy in moved:
        @pl.when(core == layer)
        def _(copy=copy):
            copy.wait_recv()

        @pl.when(core != layer)
        def _(copy=copy):
            copy.wait_send()

    for copy in started:
        copy.wait_send()


def sum_scatter(arrays, lanes, second_pre, stats, inner, collective):
    plans, scratch, shapes, copies, locals_ = [], [], [], 0, 0
    sizes = {}
    for source, prefix, phases, layer, target in lanes:
        shape = arrays[source].shape
        if isinstance(prefix, int):
            shape = shape[1:]
        else:
            if prefix[0]:
                shape = (shape[1], shape[0], *shape[2:])
            if prefix[1] is not None:
                shape = (*shape[:-1], prefix[1][1])
        buffers = [(shape[0] // 2, *shape[1:])]
        for step in range(1, len(phases[0][1]) + 1):
            buffers.append((shape[0] >> step, *shape[1:]))
            copies += shape[0] >> step
        locals_ += shape[0] // 2
        if len(phases) > 1:
            for step in range(1, len(phases[1][1]) + 1):
                buffers.append((shape[1] >> step, *shape[2:]))
                copies += shape[1] >> step
        plans.append(
            SimpleNamespace(
                source=source,
                prefix=prefix,
                phases=phases,
                buffers=buffers,
                rows=phases[0][0] == GROUP,
                layer=layer,
                target=target,
            )
        )
        width = sizes.get(target[0], (0, 0))[1] if len(target) > 2 else 0
        if layer == 0:
            sizes[target[0]] = (shape[-2], width + shape[-1])
        scratch += [pltpu.VMEM(buffer, jnp.bfloat16) for buffer in buffers]
    half = second_pre.shape[1] // (2 * inner)
    experts_shape = (2, half, second_pre.shape[0], inner)
    shapes = [
        jax.ShapeDtypeStruct(shape, jnp.bfloat16)
        for shape in (
            experts_shape,
            experts_shape,
            (2, half, *sizes[DOWN]),
            (2, *sizes[QKV]),
            (2, *sizes[OUT]),
            (2, *sizes[SMALL]),
        )
    ] + [jax.ShapeDtypeStruct(stats.shape, jnp.float32)]
    scratch += [
        pltpu.SemaphoreType.DMA((copies,)),
        pltpu.SemaphoreType.DMA((copies,)),
        pltpu.SemaphoreType.DMA((locals_,)),
    ]
    hops = lax.axis_size(GROUP) + 1
    scratch += [
        pltpu.VMEM((hops, *stats.shape), jnp.float32),
        pltpu.SemaphoreType.DMA((hops,)),
        pltpu.SemaphoreType.DMA((hops,)),
        pltpu.SemaphoreType.DMA((len(lanes) + 2 * half,)),
        pltpu.SemaphoreType.DMA((len(lanes) + 2 * half,)),
    ]
    return pl.pallas_call(
        functools.partial(sum_scatter_kernel, (plans, len(arrays), copies)),
        out_shape=shapes,
        in_specs=[pl.BlockSpec(memory_space=pl.ANY)] * (len(arrays) + 1)
        + [pl.BlockSpec(memory_space=pltpu.VMEM)],
        out_specs=[pl.BlockSpec(memory_space=pltpu.VMEM)] * len(shapes),
        scratch_shapes=scratch,
        compiler_params=pltpu.CompilerParams(
            collective_id=collective, has_side_effects=True, vmem_limit_bytes=60 * 2**20
        ),
    )(*arrays, second_pre, stats)


def bits_of(axis):
    return list(range(lax.axis_size(axis).bit_length() - 1))


def expert_lanes(first, inner):
    up, down = [(GROUP, bits_of(GROUP))], [(GROUP, bits_of(GROUP)[::-1])]
    return [
        (first, (False, ((2 * kind + j) * inner, inner)), (up, down)[kind], 0, (kind, j))
        for j in range(2)
        for kind in (GATE, UP)
    ]


def down_lanes(first, layer):
    up, down = [(GROUP, bits_of(GROUP))], [(GROUP, bits_of(GROUP)[::-1])]
    return [(first, 0, up, layer, (DOWN, 0)), (first, 1, down, layer, (DOWN, 1))]


def dense_lanes(first, half):
    up, down, deep = bits_of(GROUP), bits_of(GROUP)[::-1], bits_of(LINE)
    return [
        (first, (True, None), [(LINE, deep), (GROUP, up)], 0, (QKV,)),
        *(
            (
                first + 1,
                (False, (at, half)),
                [(GROUP, order), (LINE, deep)],
                0,
                (OUT, slice(None), pl.ds(at, half)),
            )
            for at, order in ((0, up), (half, down))
        ),
        small_lane(first + 2, 0),
    ]


def small_lane(first, layer):
    phases = [(GROUP, bits_of(GROUP)), (LINE, bits_of(LINE))]
    return (first, (False, None), phases, layer, (SMALL,))


def attention_forward(inputs, weights, segment_row):
    gain_attn, w_query, w_key, w_value, w_out, gain_moe = weights[:6]
    length = inputs.shape[0]
    cosine_table, sine_table = rotary_tables(length)
    inverse_one = lax.rsqrt(jnp.mean(inputs * inputs, axis=-1, keepdims=True) + EPSILON)
    normed_one = (inputs * inverse_one * gain_attn).astype(jnp.bfloat16)
    queries = rotate(
        matmul(normed_one, w_query).reshape(length, H, HD), cosine_table, sine_table
    ).astype(jnp.bfloat16)
    key_rows = rotate(
        matmul(normed_one, w_key).reshape(length, KVH, HD), cosine_table, sine_table
    ).astype(jnp.bfloat16)
    values = matmul(normed_one, w_value).astype(jnp.bfloat16).reshape(length, KVH, HD)
    scores = attention_scores(queries, key_rows, segment_row)
    highest = jnp.max(scores, axis=-1, keepdims=True)
    exponent = jnp.exp(scores - highest)
    denominator = jnp.sum(exponent, axis=-1, keepdims=True)
    weight = exponent / denominator
    attended = jnp.einsum(
        "kgqs,skd->qkgd", weight.astype(jnp.bfloat16), values, preferred_element_type=jnp.float32
    )
    attended = attended.reshape(length, H * HD).astype(jnp.bfloat16)
    hidden = inputs + matmul(attended, w_out)
    inverse_two = lax.rsqrt(jnp.mean(hidden * hidden, axis=-1, keepdims=True) + EPSILON)
    normed_two = (hidden * inverse_two * gain_moe).astype(jnp.bfloat16)
    state = (inverse_one, normed_one, queries, key_rows, values, weight, attended, hidden, inverse_two, normed_two)
    return state


MESH = pl.DeviceIdType.MESH
PARTS = 3


def move_rows(sources, held, pieces, sems, compute, z, n, others):
    row_send, row_recv, sum_send, sum_recv = sems
    barrier = pltpu.get_barrier_semaphore()
    for k in range(1, n):
        peer = lax.rem(z + k, n)
        pl.semaphore_signal(barrier, inc=1, device_id={LINE: peer}, device_id_type=MESH)
    for peer in others:
        pl.semaphore_signal(barrier, inc=1, device_id=peer, device_id_type=MESH)
    pl.semaphore_wait(barrier, n - 1 + len(others))

    def row_copy(kind, way, hop, source=None):
        step = 1 - 2 * way
        block = jnp.clip(z - step * hop, 0, n - 1)
        peer = jnp.clip(z + step, 0, n - 1)
        return pltpu.make_async_remote_copy(
            src_ref=held[kind].at[block] if source is None else source,
            dst_ref=held[kind].at[block],
            send_sem=row_send.at[kind, way, hop],
            recv_sem=row_recv.at[kind, way, hop],
            device_id={LINE: peer},
            device_id_type=MESH,
        )

    def sends(way, hop):
        step = 1 - 2 * way
        block, peer = z - step * hop, z + step
        return (block >= 0) & (block < n) & (peer >= 0) & (peer < n)

    def arrives(way, hop):
        block = z - (1 - 2 * way) * (hop + 1)
        return (block >= 0) & (block < n)

    def start(kind):
        for way in range(2):
            @pl.when(sends(way, 0))
            def _():
                row_copy(kind, way, 0, sources[kind]).start()

    def take(hop):
        for kind in range(len(held)):
            for way in range(2):
                @pl.when(arrives(way, hop))
                def _():
                    row_copy(kind, way, hop).wait_recv()

                @pl.when(sends(way, hop + 1) & (hop + 1 < n - 1))
                def _():
                    row_copy(kind, way, hop + 1).start()

    def waits(way, block):
        peer, last = z - (1 - 2 * way), (n - 1) * (1 - way)
        return (peer >= 0) & (peer < n) & ((block != last) | (peer != n - 1 - last))

    def far_copy(p):
        mine, arrived = pieces[p]
        block, way = n - 1 - z, jnp.where(z == 0, 1, 0)
        return pltpu.make_async_remote_copy(
            src_ref=mine(block),
            dst_ref=arrived(way, block),
            send_sem=sum_send.at[block, p],
            recv_sem=sum_recv.at[way, block, p],
            device_id={LINE: block},
            device_id_type=MESH,
        )

    def sum_copy(way, block, p):
        mine, arrived = pieces[p]
        return pltpu.make_async_remote_copy(
            src_ref=mine(block),
            dst_ref=arrived(way, block),
            send_sem=sum_send.at[block, p],
            recv_sem=sum_recv.at[way, block, p],
            device_id={LINE: jnp.clip(z + 1 - 2 * way, 0, n - 1)},
            device_id_type=MESH,
        )

    def sent(block, p):
        way = jnp.where(block > z, 0, 1)
        far = ((z == 0) | (z == n - 1)) & (block == n - 1 - z)

        @pl.when(far)
        def _():
            far_copy(p).start()

        @pl.when((block != z) & jnp.logical_not(far) & jnp.logical_not(waits(way, block)))
        def _():
            sum_copy(way, block, p).start()

    def between(block):
        if held:
            @pl.when(block == z)
            def _():
                take(0)

    def run():
        def both(hop):
            return (hop >= 0) & (z - 1 - hop >= 0) & (z + 1 + hop < n)

        def turn(k, carry):
            hop = lax.div(k + 1, 2) - 1
            block = z + (1 + hop) * (1 - 2 * lax.rem(k, 2))
            odd = lax.rem(k, 2) == 1

            @pl.when(odd & (hop > 0) & jnp.logical_not(both(hop - 1)))
            def _():
                take(hop)

            @pl.when(jnp.logical_not(odd) & both(hop) & (hop + 1 < n - 1))
            def _():
                take(hop + 1)

            @pl.when((block >= 0) & (block < n))
            def _():
                compute(block, sent, between)

            return carry

        def far_first(k, carry):
            block = z + (n - 1 - lax.div(k, 2)) * (1 - 2 * lax.rem(k, 2))

            @pl.when((block >= 0) & (block < n))
            def _():
                compute(block, sent, between)

            return carry

        if held:
            lax.fori_loop(0, 2 * n - 1, turn, 0)
        else:
            lax.fori_loop(0, 2 * n - 2, far_first, 0)

        first = jnp.where(2 * z < n, 0, 1)
        for way in (first, 1 - first):
            for k in range(1, n):
                block = z + (1 - 2 * way) * k

                @pl.when(waits(way, block) & (block >= 0) & (block < n))
                def _():
                    for p, (mine, arrived) in enumerate(pieces):
                        sum_copy(way, block, p).wait_recv()
                        own, other = mine(block), arrived(way, block)
                        own[...] = (
                            own[...].astype(jnp.float32) + other[...].astype(jnp.float32)
                        ).astype(jnp.bfloat16)
                        sum_copy(way, block, p).start()

        if not held:
            compute(z, sent, between)

    def collect(add):
        for way in range(2):
            for p, (_, arrived) in enumerate(pieces):
                sum_copy(way, z, p).wait_recv()
                add(p, arrived(way, z)[...].astype(jnp.float32))

    def finish():
        for kind in range(len(held)):
            for way in range(2):
                for hop in range(n - 1):
                    @pl.when(sends(way, hop))
                    def _():
                        row_copy(kind, way, hop).wait_send()
        for k in range(1, n):
            for p in range(len(pieces)):
                sum_copy(0, lax.rem(z + k, n), p).wait_send()

    return start, run, collect, finish


def row_pieces(sums, returned, parts):
    width = sums.shape[2] // parts

    def piece(p):
        at = pl.ds(p * width, width)
        return (
            lambda block: sums.at[block, :, at],
            lambda way, block: returned.at[way, block, :, at],
        )

    return [piece(p) for p in range(parts)]


def fetch_weights(layer, own, other, places, sem):
    count = places[0].shape[0]
    mine = lax.axis_index(CORE) == layer

    def copy(group, kind, e):
        return pltpu.make_async_copy(
            group[kind].at[e], places[kind].at[e], sem.at[kind * count + e]
        )

    for kind in range(len(places)):
        for e in range(count):
            @pl.when(mine)
            def _():
                copy(own, kind, e).start()

            @pl.when(jnp.logical_not(mine))
            def _():
                copy(other, kind, e).start()

    def wait():
        for kind in range(len(places)):
            for e in range(count):
                copy(own, kind, e).wait()

    return wait


def sigmoid_of(value):
    return 1.0 / (1.0 + jnp.exp(-value))


def column_of(block, column):
    here = lax.broadcasted_iota(jnp.int32, block.shape, 1) == column
    return jnp.sum(jnp.where(here, block, 0.0), axis=1, keepdims=True)


def experts_forward_kernel(
    layer, experts, x, mask, hidden, router, *refs
):
    own, other, refs = refs[:3], refs[3:6], refs[6:]
    own_dense, other_dense, refs = refs[:4], refs[4:8], refs[8:]
    out, rows, gates_all, gates, stats, gate_out, up_out, gated_out = refs[:8]
    placed, place_sem, keep_sem = refs[8:12], refs[-2], refs[-1]
    passing, (gate_keep, up_keep, gated) = refs[-9:-5], refs[-5:-2]
    refs = refs[:8] + refs[12:-9]
    w_gate, w_up, w_down, sums, returned, mixed, total, stats_all = refs[8:16]
    weight_sem, *sems = refs[16:]
    n, held = rows.shape[0], w_gate.shape[0]
    z = lax.axis_index(LINE)

    def keep_copies(block):
        pairs = (
            (gate_keep.at[:, block], gate_out.at[:, block]),
            (up_keep.at[:, block], up_out.at[:, block]),
            (gated.at[block], gated_out.at[block]),
        )
        return [
            pltpu.make_async_copy(source, target, keep_sem.at[i, block])
            for i, (source, target) in enumerate(pairs)
        ]

    def compute(block, sent, between):
        picked = rows[block]
        gate_block = gates_all[block].astype(jnp.float32)

        def one(e, carry):
            gate_pre = jnp.dot(picked, w_gate[e], preferred_element_type=jnp.float32)
            up_pre = jnp.dot(picked, w_up[e], preferred_element_type=jnp.float32)
            gate_keep[e, block] = gate_pre.astype(jnp.bfloat16)
            up_keep[e, block] = up_pre.astype(jnp.bfloat16)
            active = gate_pre * sigmoid_of(gate_pre) * up_pre
            share = (column_of(gate_block, z * held + e) * active).astype(jnp.bfloat16)
            inner = share.shape[1]
            gated[block, :, pl.ds(pl.multiple_of(e * inner, inner), inner)] = share
            mixed[e] = share
            return carry

        lax.fori_loop(0, held, one, 0)
        between(block)
        for copy in keep_copies(block):
            copy.start()
        width = out.shape[1] // PARTS
        for part in range(PARTS):
            at = pl.ds(part * width, width)
            result = jnp.zeros((out.shape[0], width), jnp.float32)
            for e in range(held):
                result += jnp.dot(mixed[e], w_down[e, :, at], preferred_element_type=jnp.float32)

            @pl.when(block == z)
            def _():
                total[:, at] = hidden[:, at] + result

            @pl.when(block != z)
            def _():
                sums[block, :, at] = result.astype(jnp.bfloat16)

            sent(block, part)

    own_gates = gates_all.at[z]
    start, run, collect, finish = move_rows(
        (x, own_gates, stats_all.at[z]),
        (rows, gates_all, stats_all),
        row_pieces(sums, returned, PARTS),
        sems,
        compute,
        z,
        n,
        [],
    )
    start(0)
    wait_weights = fetch_weights(layer, own, other, (w_gate, w_up, w_down), weight_sem)
    here = lax.axis_index(CORE) == 1 - layer

    def place_copy(group, i):
        return pltpu.make_async_copy(group[i], passing[i], place_sem.at[0, i])

    def place_out(i):
        return pltpu.make_async_copy(passing[i], placed[i], place_sem.at[1, i])

    logits = jnp.dot(x[...], router[...], preferred_element_type=jnp.float32)
    chosen = mask[...] > 0
    highest = jnp.max(jnp.where(chosen, logits, MASKED), axis=1, keepdims=True)
    exponent = jnp.where(chosen, jnp.exp(logits - highest), 0.0)
    gates[...] = exponent / jnp.sum(exponent, axis=1, keepdims=True)
    own_gates[...] = gates[...].astype(jnp.bfloat16)
    start(1)
    real = lax.broadcasted_iota(jnp.int32, logits.shape, 1) < experts
    highest = jnp.max(jnp.where(real, logits, MASKED), axis=1, keepdims=True)
    exponent = jnp.where(real, jnp.exp(logits - highest), 0.0)
    chance = exponent / jnp.sum(exponent, axis=1, keepdims=True)
    line = lax.broadcasted_iota(jnp.int32, stats.shape, 0)
    stats_all[z] = jnp.where(
        line == 0,
        jnp.sum(chance, axis=0, keepdims=True),
        jnp.where(line == 1, jnp.sum(mask[...], axis=0, keepdims=True), 0.0),
    )
    start(2)
    rows[z] = x[...]
    wait_weights()
    for i in range(4):
        @pl.when(here)
        def _():
            place_copy(own_dense, i).start()

        @pl.when(jnp.logical_not(here))
        def _():
            place_copy(other_dense, i).start()

    run()
    for i in range(4):
        place_copy(own_dense, i).wait()
        place_out(i).start()
    stats[...] = jnp.sum(stats_all[...], axis=0)
    width = out.shape[1] // PARTS

    def add(p, value):
        total[:, p * width : (p + 1) * width] += value

    collect(add)
    out[...] = total[...].astype(jnp.bfloat16)
    finish()
    for i in range(4):
        place_out(i).wait()
    for block in range(n):
        for copy in keep_copies(block):
            copy.wait()


def experts_backward_kernel(layer, grad, gates, *refs):
    own, other, saved_rows, saved_gated, refs = refs[:3], refs[3:6], refs[6], refs[7], refs[8:]
    kept, refs = refs[:2], refs[2:]
    keep_places, keep_sem, refs = refs[-3:-1], refs[-1], refs[:-3]
    gate_keep, up_keep = keep_places
    out, out_gates, rows_both, gated_both, grad_both, pre_both = refs[:6]
    w_gate, w_up, w_down, sums, sum_gates, returned, returned_gates, away, dots = refs[6:15]
    weight_sem, core_send, core_recv, core_local, *sems = refs[15:]
    n, held = gates.shape[0], w_gate.shape[0]
    half, inner = held // 2, w_gate.shape[2]
    core = lax.axis_index(CORE)
    z = lax.axis_index(LINE)
    turned_dims = (((1,), (1,)), ((), ()))
    gathered = layer == 1
    rows = grad if gathered else grad_both.at[core]

    def to_core(number, source, target):
        return pltpu.make_async_remote_copy(
            src_ref=source,
            dst_ref=target,
            send_sem=core_send.at[number],
            recv_sem=core_recv.at[number],
            device_id={CORE: 1 - core},
            device_id_type=MESH,
        )

    def block_copies(block):
        away_copy = to_core(2 + n + block, away.at[block], pre_both.at[core, block])
        if gathered:
            return (away_copy,)
        return (to_core(2 + block, rows.at[block], rows.at[block]), away_copy)

    def columns(at):
        return pl.ds(pl.multiple_of(at * half * inner, half * inner), half * inner)

    def whole_copies():
        copies = (
            to_core(0, saved_rows, rows_both.at[core]),
            to_core(1, saved_gated.at[:, :, columns(1 - core)], gated_both.at[core]),
        )
        return copies + ((to_core(2, grad, grad_both.at[core]),) if gathered else ())

    def local_copies():
        copies = (
            pltpu.make_async_copy(saved_rows, rows_both.at[core], core_local.at[0]),
            pltpu.make_async_copy(
                saved_gated.at[:, :, columns(core)], gated_both.at[core], core_local.at[1]
            ),
        )
        if gathered:
            copies += (pltpu.make_async_copy(grad, grad_both.at[core], core_local.at[2]),)
        return copies

    def compute(block, sent, between):
        picked = rows[block]
        gate_block = gates[block].astype(jnp.float32)
        dots[...] = jnp.zeros(dots.shape, jnp.float32)

        def one(e, place, j):
            raw = lax.dot_general(
                picked, w_down[e], turned_dims, preferred_element_type=jnp.float32
            )
            gate_pre = gate_keep[e, block].astype(jnp.float32)
            up_pre = up_keep[e, block].astype(jnp.float32)
            sigmoid = sigmoid_of(gate_pre)
            silu = gate_pre * sigmoid
            column = z * held + e
            dot = jnp.sum(raw * (silu * up_pre), axis=1, keepdims=True)
            here = lax.broadcasted_iota(jnp.int32, dots.shape, 1) == column
            dots[...] += jnp.where(here, dot, 0.0)
            active = column_of(gate_block, column) * raw
            place[:, pl.ds(pl.multiple_of(j * inner, inner), inner)] = (
                active * up_pre * sigmoid * (1.0 + gate_pre * (1.0 - sigmoid))
            ).astype(jnp.bfloat16)
            place[:, pl.ds(pl.multiple_of((half + j) * inner, inner), inner)] = (
                active * silu
            ).astype(jnp.bfloat16)

        def own_half(j, carry):
            one(core * half + j, pre_both.at[core, block], j)
            return carry

        def other_half(j, carry):
            one((1 - core) * half + j, away.at[block], j)
            return carry

        lax.fori_loop(0, half, other_half, 0)
        for copy in block_copies(block):
            copy.start()
        lax.fori_loop(0, half, own_half, 0)
        between(block)
        sum_gates[block] = dots[...].astype(jnp.bfloat16)

        @pl.when(block == z)
        def _():
            out_gates[...] = dots[...]

        sent(block, PARTS)
        width = out.shape[1] // PARTS
        for part in range(PARTS):
            at = pl.ds(part * width, width)
            result = jnp.zeros((out.shape[0], width), jnp.float32)
            for place, side in ((away.at[block], 1 - core), (pre_both.at[core, block], core)):
                for kind, right in enumerate((w_gate, w_up)):
                    for j in range(half):
                        left = place[:, pl.ds((kind * half + j) * inner, inner)]
                        result += lax.dot_general(
                            left,
                            right[side * half + j, at, :],
                            turned_dims,
                            preferred_element_type=jnp.float32,
                        )

            @pl.when(block == z)
            def _():
                out[:, at] = result

            @pl.when(block != z)
            def _():
                sums[block, :, at] = result.astype(jnp.bfloat16)

            sent(block, part)

    gate_piece = (lambda block: sum_gates.at[block], lambda way, block: returned_gates.at[way, block])
    start, run, collect, finish = move_rows(
        () if gathered else (grad,),
        () if gathered else (rows,),
        row_pieces(sums, returned, PARTS) + [gate_piece],
        sems,
        compute,
        z,
        n,
        [{CORE: 1 - core}],
    )
    if not gathered:
        start(0)
    wait_weights = fetch_weights(layer, own, other, (w_gate, w_up, w_down), weight_sem)
    keep_copies = [
        pltpu.make_async_copy(kept[i], keep_places[i], keep_sem.at[i]) for i in range(2)
    ]
    for copy in keep_copies:
        copy.start()
    for copy in whole_copies() + local_copies():
        copy.start()
    if not gathered:
        rows[z] = grad[...]
    for copy in keep_copies:
        copy.wait()
    wait_weights()
    run()
    width = out.shape[1] // PARTS

    def add(p, value):
        if p == PARTS:
            out_gates[...] += value
        else:
            out[:, p * width : (p + 1) * width] += value

    collect(add)
    finish()
    for copy in local_copies():
        copy.wait()
    for copy in whole_copies():
        copy.wait()
    for block in range(n):
        for copy in block_copies(block):
            copy.wait()


def exchange_scratch(n, kinds_out, kinds_back):
    return [
        pltpu.SemaphoreType.DMA((kinds_out, 2, n)),
        pltpu.SemaphoreType.DMA((kinds_out, 2, n)),
        pltpu.SemaphoreType.DMA((n, kinds_back)),
        pltpu.SemaphoreType.DMA((2, n, kinds_back)),
    ]


def expert_call(kernel, operands, own, other, extra, shapes, scratch, collective, loose=0):
    vmem, free = pl.BlockSpec(memory_space=pltpu.VMEM), pl.BlockSpec(memory_space=pl.ANY)
    weights = [pltpu.VMEM(array.shape, jnp.bfloat16) for array in own]
    return pl.pallas_call(
        kernel,
        out_shape=shapes,
        in_specs=[vmem] * len(operands) + [free] * (6 + len(extra)),
        out_specs=[vmem] * (len(shapes) - loose) + [free] * loose,
        scratch_shapes=weights + scratch,
        compiler_params=pltpu.CompilerParams(
            collective_id=collective, has_side_effects=True, vmem_limit_bytes=46 * 2**20
        ),
        cost_estimate=pl.CostEstimate(
            flops=5 * 10**10, bytes_accessed=10**8, transcendentals=0
        ),
    )(*operands, *own, *other, *extra)


def experts_forward(
    layer, normed_two, mask, hidden, router, own, other, own_dense, other_dense, experts
):
    n, held = lax.axis_size(LINE), own[0].shape[0]
    length, width = normed_two.shape
    inner = own[0].shape[2]
    low, full = jnp.bfloat16, jnp.float32
    kept = jax.ShapeDtypeStruct((held, n, length, inner), low)
    shapes = [
        jax.ShapeDtypeStruct((length, width), low),
        jax.ShapeDtypeStruct((n, length, width), low),
        jax.ShapeDtypeStruct((n, length, COLUMNS), low),
        jax.ShapeDtypeStruct((length, COLUMNS), full),
        jax.ShapeDtypeStruct((8, COLUMNS), full),
        kept,
        kept,
        jax.ShapeDtypeStruct((n, length, held * inner), low),
    ] + [jax.ShapeDtypeStruct(array.shape, low) for array in own_dense]
    scratch = [
        pltpu.VMEM((n, length, width), low),
        pltpu.VMEM((2, n, length, width), low),
        pltpu.VMEM((held, length, inner), low),
        pltpu.VMEM((length, width), full),
        pltpu.VMEM((n, 8, COLUMNS), full),
        pltpu.SemaphoreType.DMA((3 * held,)),
    ] + exchange_scratch(n, 3, PARTS)
    scratch += [pltpu.VMEM(array.shape, low) for array in own_dense]
    scratch += [pltpu.VMEM(shape.shape, low) for shape in shapes[5:8]]
    scratch.append(pltpu.SemaphoreType.DMA((2, 4)))
    scratch.append(pltpu.SemaphoreType.DMA((3, n)))
    kernel = functools.partial(experts_forward_kernel, layer, experts)
    return expert_call(
        kernel,
        (normed_two, mask, hidden, router),
        own,
        other,
        (*own_dense, *other_dense),
        shapes,
        scratch,
        1 + layer,
        7,
    )


def experts_backward(layer, grad_low, gates, gate_keep, up_keep, rows, gated, own, other):
    held, n, length, inner = gate_keep.shape
    width = grad_low.shape[-1]
    low, full = jnp.bfloat16, jnp.float32
    shapes = [
        jax.ShapeDtypeStruct((length, width), full),
        jax.ShapeDtypeStruct((length, COLUMNS), full),
        jax.ShapeDtypeStruct((2, n, length, width), low),
        jax.ShapeDtypeStruct((2, n, length, held // 2 * inner), low),
        jax.ShapeDtypeStruct((2, n, length, width), low),
        jax.ShapeDtypeStruct((2, n, length, held * inner), low),
    ]
    scratch = [
        pltpu.VMEM((n, length, width), low),
        pltpu.VMEM((n, length, COLUMNS), low),
        pltpu.VMEM((2, n, length, width), low),
        pltpu.VMEM((2, n, length, COLUMNS), low),
        pltpu.VMEM((n, length, held * inner), low),
        pltpu.VMEM((length, COLUMNS), full),
        pltpu.SemaphoreType.DMA((3 * held,)),
        pltpu.SemaphoreType.DMA((2 + 2 * n,)),
        pltpu.SemaphoreType.DMA((2 + 2 * n,)),
        pltpu.SemaphoreType.DMA((3,)),
    ] + exchange_scratch(n, 1, PARTS + 1)
    scratch += [pltpu.VMEM(gate_keep.shape, low)] * 2 + [pltpu.SemaphoreType.DMA((2,))]
    kernel = functools.partial(experts_backward_kernel, layer)
    return expert_call(
        kernel,
        (grad_low, gates),
        own,
        other,
        (rows, gated, gate_keep, up_keep),
        shapes,
        scratch,
        3 + layer,
    )


def attention_backward(grad_hidden, inputs, state, weights):
    gain_attn, w_query, w_key, w_value, w_out, gain_moe = weights[:6]
    (inverse_one, normed_one, queries, key_rows, values, weight, attended, hidden, inverse_two, normed_two) = state
    length = inputs.shape[0]
    grad_branch = grad_hidden.astype(jnp.bfloat16)
    grad_attended = jnp.einsum("td,cd->tc", grad_branch, w_out, preferred_element_type=jnp.float32)
    grad_attended = grad_attended.astype(jnp.bfloat16).reshape(length, KVH, H // KVH, HD)
    grad_weight = jnp.einsum(
        "qkgd,skd->kgqs", grad_attended, values, preferred_element_type=jnp.float32
    )
    grad_values = jnp.einsum(
        "kgqs,qkgd->skd",
        weight.astype(jnp.bfloat16),
        grad_attended,
        preferred_element_type=jnp.float32,
    )
    grad_values = grad_values.astype(jnp.bfloat16).reshape(length, KVH * HD)
    grad_scores = (
        weight * (grad_weight - jnp.sum(weight * grad_weight, axis=-1, keepdims=True))
    ).astype(jnp.bfloat16)
    score_scale = HD ** (-0.5)
    grouped = queries.reshape(length, KVH, H // KVH, HD)
    grad_queries = jnp.einsum(
        "kgqs,skd->qkgd", grad_scores, key_rows, preferred_element_type=jnp.float32
    )
    grad_queries = grad_queries.reshape(length, H, HD) * score_scale
    grad_keys = (
        jnp.einsum("kgqs,qkgd->skd", grad_scores, grouped, preferred_element_type=jnp.float32)
        * score_scale
    )
    cosine_table, sine_table = rotary_tables(length)
    grad_query_pre = (
        unrotate(grad_queries, cosine_table, sine_table)
        .reshape(length, H * HD)
        .astype(jnp.bfloat16)
    )
    grad_key_pre = (
        unrotate(grad_keys, cosine_table, sine_table).reshape(length, KVH * HD).astype(jnp.bfloat16)
    )
    grad_normed_one = (
        jnp.einsum("tq,cq->tc", grad_query_pre, w_query, preferred_element_type=jnp.float32)
        + jnp.einsum("tq,cq->tc", grad_key_pre, w_key, preferred_element_type=jnp.float32)
        + jnp.einsum("tq,cq->tc", grad_values, w_value, preferred_element_type=jnp.float32)
    )
    grad_norm_one, grad_gain_attn = norm_back(grad_normed_one, inputs, inverse_one, gain_attn)
    grad_inputs = grad_hidden + grad_norm_one
    grad_qkv = jnp.concatenate([grad_query_pre, grad_key_pre, grad_values], axis=1)
    return grad_inputs, grad_gain_attn, grad_qkv, grad_branch


def turned(left, right):
    return jnp.einsum("tc,tq->cq", left, right, preferred_element_type=jnp.float32)


def body(tokens, cotangent, segments, routes, *weight_arrays):
    core = lax.axis_index(CORE)
    first = core == 0
    experts = weight_arrays[6].shape[2]
    w_gate = weight_arrays[7]
    held = w_gate.shape[1]
    own = [array[0] for array in weight_arrays]
    other = [swapped(array) for array in own]
    weights = [
        [jnp.where(first, a, b) for a, b in zip(own[:7], other[:7])],
        [jnp.where(first, b, a) for a, b in zip(own[:7], other[:7])],
    ]
    inputs_low = lax.dynamic_slice_in_dim(tokens, core * SEQ, SEQ, 0)
    grad_low = lax.dynamic_slice_in_dim(cotangent, core * SEQ, SEQ, 0)
    cotangent_all = lax.all_gather(grad_low, LINE, axis=0)
    segment_row = lax.dynamic_index_in_dim(segments, core, 0, keepdims=False)
    mine = lax.dynamic_slice_in_dim(routes[0], core * SEQ, SEQ, 0)
    got = swapped(lax.dynamic_slice_in_dim(routes[0], (1 - core) * SEQ, SEQ, 0))
    routes_here = jnp.stack([jnp.where(first, mine, got), jnp.where(first, got, mine)])
    masks = multi_hot(routes_here, COLUMNS)
    own_experts, other_experts = own[7:], other[7:]

    saved, outs, stats = [], [], []
    for s in range(2):
        inputs = inputs_low.astype(jnp.float32)
        state = attention_forward(inputs, weights[s], segment_row)
        hidden, normed_two = state[7], state[9]
        if s == 0:
            normed_two, cotangent_all = lax.optimization_barrier((normed_two, cotangent_all))
        both_cores = [jnp.concatenate([a, swapped(a)]) for a in (state[1], state[6])]
        router = jnp.pad(weights[s][6], ((0, 0), (0, COLUMNS - experts)))
        inputs_low, rows, gates_all, gates, stat, *kept, query, key, value, out = experts_forward(
            s,
            normed_two,
            masks[s],
            hidden,
            router,
            own_experts,
            other_experts,
            own[1:5],
            other[1:5],
            experts,
        )
        weights[1 - s][1:5] = [query, key, value, out]
        outs.append(inputs_low)
        stats.append(stat)
        expert_state = (rows, gates_all, gates, *kept)
        saved.append((inputs, state, expert_state, both_cores))

    dp, deep = lax.axis_size(GROUP), lax.axis_size(LINE)
    grads = [None, None]
    input_grads = [None, None]
    for s in (1, 0):
        inputs, state, expert_state, both_cores = saved[s]
        (inverse_one, normed_one, _, _, _, _, attended, hidden, inverse_two, normed_two) = state
        rows_all, gates_all, gates, gate_keep, up_keep, gated = expert_state
        gain_moe, w_router = weights[s][5], weights[s][6]
        grad_sum, grad_gates, rows_both, gated_both, grad_both, pre_both = experts_backward(
            s,
            cotangent_all if s == 1 else grad_low,
            gates_all,
            gate_keep,
            up_keep,
            rows_all,
            gated,
            own_experts,
            other_experts,
        )
        inner = w_gate.shape[3]
        grad_gate_up = turned(
            rows_both.reshape(-1, D), pre_both.reshape(-1, held * inner)
        ).astype(jnp.bfloat16)
        if s == 1:
            grad_sum, grad_gate_up = lax.optimization_barrier((grad_sum, grad_gate_up))
            second_pre = lax.psum_scatter(grad_gate_up, GROUP, scatter_dimension=0, tiled=True)
        else:
            grad_sum, second_pre = lax.optimization_barrier((grad_sum, second_pre))
        gates, grad_gates = gates[:, :experts], grad_gates[:, :experts]
        grad_chosen = gates * (grad_gates - jnp.sum(gates * grad_gates, axis=-1, keepdims=True))
        grad_logits = grad_chosen.astype(jnp.bfloat16)
        grad_normed_two = grad_sum + jnp.einsum(
            "te,de->td", grad_logits, w_router, preferred_element_type=jnp.float32
        )
        grad_norm_two, grad_gain_moe = norm_back(grad_normed_two, hidden, inverse_two, gain_moe)
        grad_hidden = grad_low.astype(jnp.float32) + grad_norm_two
        grad_inputs, grad_gain_attn, grad_qkv, grad_branch = attention_backward(
            grad_hidden, inputs, state, weights[s]
        )
        if s == 1:
            grad_inputs, gated_both = lax.optimization_barrier((grad_inputs, gated_both))
        grad_down = turned(
            gated_both.reshape(-1, held // 2 * inner), grad_both.reshape(-1, D)
        ).astype(jnp.bfloat16)

        def halves(array):
            width = array.shape[1] // 2
            return (
                lax.dynamic_slice_in_dim(array, core * width, width, 1),
                lax.dynamic_slice_in_dim(array, (1 - core) * width, width, 1),
            )
        qkv_keep, qkv_send = halves(grad_qkv)
        branch_keep, branch_send = halves(grad_branch)
        grad_w_qkv = turned(
            both_cores[0], jnp.concatenate([qkv_keep, swapped(qkv_send)])
        ).astype(jnp.bfloat16)
        grad_w_out = turned(
            both_cores[1], jnp.concatenate([branch_keep, swapped(branch_send)])
        ).astype(jnp.bfloat16)
        grad_w_router = turned(normed_two, grad_logits)
        small = jnp.concatenate(
            [grad_gain_attn[:, None], grad_gain_moe[:, None], grad_w_router], axis=1
        ).astype(jnp.bfloat16)
        small = jnp.pad(small, ((0, 0), (0, COLUMNS - small.shape[1])))
        if s == 1:
            grad_inputs, grad_down, grad_w_qkv, grad_w_out = lax.optimization_barrier(
                (grad_inputs, grad_down, grad_w_qkv, grad_w_out)
            )
            dense = jnp.concatenate([grad_w_qkv, grad_w_out], axis=1)
            second_dense = lax.psum_scatter(dense, GROUP, scatter_dimension=0, tiled=True)
        grads[s] = (grad_gate_up, grad_down, grad_w_qkv, grad_w_out, small)
        input_grads[s] = grad_inputs
        grad_low = grad_inputs.astype(jnp.bfloat16)

    dp, deep = lax.axis_size(GROUP), lax.axis_size(LINE)
    half, inner = held // 2, w_gate.shape[3]
    grad_gate_up, grad_down, grad_w_qkv, grad_w_out, small = grads[0]
    arrays = [
        grad_gate_up.reshape(dp, D // dp, held * inner),
        grad_down.reshape(half, dp, inner // dp, D),
    ]
    lanes = dense_lanes(2, grad_w_out.shape[1] // 2)
    for array in (grad_w_qkv, grad_w_out, small):
        arrays.append(array.reshape(dp, deep, array.shape[0] // (dp * deep), array.shape[1]))
    width = grad_w_qkv.shape[1]
    whole = second_dense.shape[1]
    for columns, kind in (((0, width), QKV), ((width, whole - width), OUT)):
        start, size = columns
        target = (kind, slice(None), pl.ds(start - (start // width) * width, size))
        lanes.append((len(arrays), (False, columns), [(LINE, bits_of(LINE))], 1, target))
    arrays.append(second_dense.reshape(deep, second_dense.shape[0] // deep, whole))
    lanes.append(small_lane(len(arrays), 1))
    lanes += expert_lanes(0, inner) + down_lanes(1, 0) + down_lanes(len(arrays) + 1, 1)
    small = grads[1][4]
    arrays.append(small.reshape(dp, deep, small.shape[0] // (dp * deep), small.shape[1]))
    arrays.append(grads[1][1].reshape(half, dp, inner // dp, D))
    out_keep = jnp.where(first, outs[0], outs[1])
    out_got = swapped(jnp.where(first, outs[1], outs[0]))
    layer_out = jnp.where(
        first, jnp.concatenate([out_keep, out_got]), jnp.concatenate([out_got, out_keep])
    )
    low_one = input_grads[1].astype(jnp.bfloat16).astype(jnp.float32)
    grad_keep = jnp.where(first, input_grads[0], low_one)
    grad_got = swapped(jnp.where(first, low_one, input_grads[0]))
    input_grad = jnp.where(
        first, jnp.concatenate([grad_keep, grad_got]), jnp.concatenate([grad_got, grad_keep])
    )
    stats = jnp.concatenate(stats, axis=0)
    stats, layer_out, input_grad = lax.optimization_barrier((stats, layer_out, input_grad))
    *grads, qkv, out, small, stats = sum_scatter(
        arrays, lanes, second_pre, stats, inner, 0
    )
    full = jnp.float32
    w_gate_grad, w_up_grad, w_down_grad = (
        grad.reshape(held, *grad.shape[2:]).astype(full) for grad in grads
    )
    qkv = jnp.concatenate([qkv[0], qkv[1]], axis=1).astype(full)
    grad_w_out = jnp.concatenate([out[0], out[1]], axis=1).astype(full)
    small = small[0].astype(full) + small[1].astype(full)
    heads, kv = H * HD, KVH * HD
    stats = lax.dynamic_index_in_dim(stats.reshape(2, 8, COLUMNS), core, 0)
    token_total = SEQ * lax.axis_size((CORE, GROUP, LINE))
    counts, chances = stats[:, 1, :experts], stats[:, 0, :experts]
    balance = experts * (counts / (token_total * TOPK) * chances / token_total)
    results = (
        layer_out,
        input_grad,
        small[:, 0],
        qkv[:, :heads],
        qkv[:, heads : heads + kv],
        qkv[:, heads + kv :],
        grad_w_out,
        small[:, 1],
        small[:, 2 : 2 + experts],
        w_gate_grad,
        w_up_grad,
        w_down_grad,
    )
    return tuple(result[None] for result in results) + (balance,)


def solution(mesh):
    return jax.shard_map(
        body,
        mesh=mesh,
        in_specs=(
            P((GROUP, LINE), None),
            P((GROUP, LINE), None),
            P((GROUP, LINE), None),
            P(CORE, (GROUP, LINE), None),
            P(CORE, None),
            P(CORE, None, None),
            P(CORE, None, None),
            P(CORE, None, None),
            P(CORE, None, None),
            P(CORE, None),
            P(CORE, None, None),
            P(CORE, LINE, None, None),
            P(CORE, LINE, None, None),
            P(CORE, LINE, None, None),
        ),
        out_specs=(
            P(CORE, (GROUP, LINE), None),
            P(CORE, (GROUP, LINE), None),
            P(CORE, (GROUP, LINE)),
            P(CORE, (GROUP, LINE), None),
            P(CORE, (GROUP, LINE), None),
            P(CORE, (GROUP, LINE), None),
            P(CORE, (GROUP, LINE), None),
            P(CORE, (GROUP, LINE)),
            P(CORE, (GROUP, LINE), None),
            P(CORE, LINE, GROUP, None),
            P(CORE, LINE, GROUP, None),
            P(CORE, LINE, GROUP, None),
            P(CORE, None),
        ),
        check_vma=False,
    )
```
